128 devices in a mesh: dp: 4 (over y), row: 2 (over core), col: 16 (over z, x).
Axes of the slice: x: 4, y: 4, z: 4, core: 2. Of those that a mesh axis runs over, the one named last changes fastest.
Arguments:
- hidden_in: bfloat16 [32768, 1024], P(('dp', 'col', 'row')), may hold values from -6 to 6
- cotangent: bfloat16 [32768, 1024], P(('dp', 'col', 'row')), may hold values from -6 to 6
- lengths: int32 [64], P(('dp', 'col')), may hold values from 288 to 512, as said below
- routes: int32 [32768, 8], P(('dp', 'col', 'row')), may hold values from 0 to 31, all different within a row
- priority: int32 [128, 2048], P(('dp', 'col', 'row')), may hold values from 0 to 2047, each once within a row
- attn_gain: float32 [1024], replicated, may hold values from 0.5 to 1.5
- query_weight: bfloat16 [1024, 1024], P(('row', 'col')), may hold values from -0.1875 to 0.1875
- key_weight: bfloat16 [1024, 512], P(('row', 'col')), may hold values from -0.1875 to 0.1875
- value_weight: bfloat16 [1024, 512], P(('row', 'col')), may hold values from -0.1875 to 0.1875
- output_weight: bfloat16 [1024, 1024], P(('row', 'col')), may hold values from -1.5 to 1.5
- moe_gain: float32 [1024], replicated, may hold values from 0.5 to 1.5
- router: bfloat16 [1024, 32], replicated, may hold values from -0.09375 to 0.09375
- gate_weight: bfloat16 [32, 1024, 512], P(('row', 'col')), may hold values from -0.1875 to 0.1875
- up_weight: bfloat16 [32, 1024, 512], P(('row', 'col')), may hold values from -0.1875 to 0.1875
- down_weight: bfloat16 [32, 512, 1024], P(('row', 'col')), may hold values from -1 to 1
Outputs:
- hidden_out: bfloat16 [32768, 1024], P(('dp', 'col', 'row'))
- hidden_grad: float32 [32768, 1024], P(('dp', 'col', 'row'))
- attn_gain_grad: float32 [1024], replicated
- query_grad: float32 [1024, 1024], P(('row', 'col'))
- key_grad: float32 [1024, 512], P(('row', 'col'))
- value_grad: float32 [1024, 512], P(('row', 'col'))
- output_grad: float32 [1024, 1024], P(('row', 'col'))
- moe_gain_grad: float32 [1024], replicated
- router_grad: float32 [1024, 32], replicated
- gate_grad: float32 [32, 1024, 512], P(('row', 'col'))
- up_grad: float32 [32, 1024, 512], P(('row', 'col'))
- down_grad: float32 [32, 512, 1024], P(('row', 'col'))
The draws below stay inside these ranges and needn't reach their ends.
Inputs may be any that keep to these rules, and one draw needn't show every extreme that they name: `lengths`: every sequence holds more than 256 used tokens; some sequence is full and some has the least length. `routes`: each row names 8 different experts. `priority`: each row holds every rank once.
All inputs are finite; a program needn't handle non-finite values.
Results may differ from the reference program's by a relative error of at most 0.025.
Values may be sent and summed in bfloat16 or wider, within the bound.
A program may use at most 192 MiB of HBM per device.

```python
import jax
import jax.numpy as jnp
from jax import lax

D = 1024
HEADS = 16
HEAD = 64
KV_HEADS = 8
EXPERTS = 32
FFE = 512
TOP = 8
TOK_DEV = 256
LEN = 512
TOKENS = 32768
CAP = 64


def draw_lengths(key, part):
    key = jax.random.fold_in(key, 11)
    seq_count = TOKENS // LEN
    lowest = TOK_DEV + TOK_DEV // 8
    sampled = jax.random.randint(jax.random.fold_in(key, 1), (seq_count,), lowest, LEN + 1)
    picks = jax.random.permutation(jax.random.fold_in(key, 2), seq_count)
    position_ids = jnp.arange(seq_count)
    sampled = jnp.where(position_ids == picks[0], LEN, sampled)
    sampled = jnp.where(position_ids == picks[1], lowest, sampled)
    return sampled.astype(jnp.int32)


def steps_of(own_key, dims, split, least, top_value):
    level = 1.0
    for dim, blocks in split:
        draws = jax.random.uniform(jax.random.fold_in(jax.random.fold_in(own_key, 6), dim), (blocks,), jnp.float32, least / len(split), top_value / len(split))
        level = level * jnp.repeat(jnp.exp(draws), dims[dim] // blocks).reshape((-1,) + (1,) * (len(dims) - 1 - dim))
    return level


def different_ones(stream_key, rows, number_of, top, lift):
    order = jax.random.permutation(jax.random.fold_in(stream_key, 1), number_of)
    pull = order
    for power in range(3):
        pull = pull * pull // number_of
    pull = pull * lift // number_of
    tickets = jax.random.randint(jax.random.fold_in(stream_key, 2), (rows, number_of), 0, 4096) + pull
    holders = jax.random.permutation(jax.random.fold_in(stream_key, 3), rows)[jnp.arange(number_of) % rows]
    tickets = jnp.where(jnp.arange(rows)[:, None] == holders[None, :], 1 << 14, tickets)
    score = tickets * number_of + jnp.arange(number_of)
    return lax.top_k(score.astype(jnp.int32), top)[1].astype(jnp.int32)


def centred(rng, dims, deviation, most, shards=(), held_as=jnp.bfloat16):
    drawn = jax.random.normal(rng, dims, jnp.float32) * deviation
    if len(shards) > 0:
        drawn = steps_of(rng, dims, shards, -0.22, 0.18) * drawn
    return jnp.clip(drawn, min=-most, max=most).astype(held_as)


def setup_inputs(seed: int = 0) -> dict:
    key_list = jax.random.split(jax.random.key(seed), 16)
    hidden_in = centred(key_list[0], (TOKENS, D), 1.0, 6.0, ((0, 128),))
    cotangent = centred(key_list[1], (TOKENS, D), 1.0, 6.0, ((0, 128),))
    lengths = draw_lengths(jax.random.fold_in(key_list[15], 71), 0)
    routes = different_ones(key_list[3], TOKENS, EXPERTS, TOP, 2048)
    priority = jax.vmap(lambda own: jax.random.permutation(own, TOK_DEV * TOP))(jax.random.split(key_list[4], (TOKENS // TOK_DEV))).reshape((TOKENS // TOK_DEV, TOK_DEV * TOP)).astype(jnp.int32)
    attn_gain = jnp.clip(1.0 + 0.1 * jax.random.normal(key_list[5], (D,), jnp.float32), 0.5, 1.5)
    query_weight = centred(key_list[6], (D, D), D ** -0.5, 0.1875, ((0, 32),))
    key_weight = centred(key_list[7], (D, KV_HEADS * HEAD), D ** -0.5, 0.1875, ((0, 32),))
    value_weight = centred(key_list[8], (D, KV_HEADS * HEAD), D ** -0.5, 0.1875, ((0, 32),))
    output_weight = centred(key_list[9], (D, D), (D // 64) ** -0.5, 1.5, ((0, 32),))
    moe_gain = jnp.clip(1.0 + 0.1 * jax.random.normal(key_list[10], (D,), jnp.float32), 0.5, 1.5)
    router = centred(key_list[11], (D, EXPERTS), (4 * D) ** -0.5, 0.09375)
    gate_weight = centred(key_list[12], (EXPERTS, D, FFE), D ** -0.5, 0.1875, ((0, 32),))
    up_weight = centred(key_list[13], (EXPERTS, D, FFE), D ** -0.5, 0.1875, ((0, 32),))
    down_weight = centred(key_list[14], (EXPERTS, FFE, D), (FFE // 16) ** -0.5, 1.0, ((0, 32),))
    return dict(hidden_in=hidden_in, cotangent=cotangent, lengths=lengths, routes=routes, priority=priority, attn_gain=attn_gain, query_weight=query_weight, key_weight=key_weight, value_weight=value_weight, output_weight=output_weight, moe_gain=moe_gain, router=router, gate_weight=gate_weight, up_weight=up_weight, down_weight=down_weight)


epsilon = 1e-05
rotary_base = 10000.0
highest = lax.Precision.HIGHEST

@jax.custom_vjp
def low(v):
    return lax.optimization_barrier(v.astype(jnp.bfloat16)).astype(jnp.float32)

@jax.custom_vjp
def low_back(v):
    return v

def low_keep(v):
    return (low(v), None)

def low_pass(kept, grad):
    return (grad,)

def back_keep(v):
    return (v, None)

def back_low(kept, grad):
    return (low(grad),)
low.defvjp(low_keep, low_pass)
low_back.defvjp(back_keep, back_low)

def rms_norm(values, gain_vec):
    scale_rows = lax.rsqrt(lax.optimization_barrier(jnp.mean(values * values, axis=-1, keepdims=True)) + epsilon)
    return values * scale_rows * gain_vec

def rotary(values, positions, sign):
    half_dim = values.shape[-1] // 2
    frequency = rotary_base ** (-jnp.arange(half_dim, dtype=jnp.float32) / half_dim)
    angles = positions.astype(jnp.float32)[:, None] * frequency[None, :]
    cosine = jnp.cos(angles)[:, None, :]
    sine_table = jnp.sin(angles)[:, None, :] * sign
    first_half = values[..., :half_dim]
    second_half = values[..., half_dim:]
    return jnp.concatenate([first_half * cosine - second_half * sine_table, second_half * cosine + first_half * sine_table], axis=-1)

def attend(pieces):
    queries, key_rows, values, length = pieces
    seq_len = queries.shape[0]
    grouped = queries.reshape(seq_len, KV_HEADS, HEADS // KV_HEADS, HEAD)
    scores = low_back(jnp.einsum('tkgd,jkd->kgtj', grouped, key_rows, precision=highest) * HEAD ** (-0.5))
    usable = jnp.arange(seq_len) < length
    scores = jnp.where(usable[None, None, None, :], scores, -1000000000.0)
    top_score = lax.optimization_barrier(jnp.max(scores, axis=-1, keepdims=True))
    weights = jnp.exp(scores - top_score)
    attn_probs = weights / lax.optimization_barrier(jnp.sum(weights, axis=-1, keepdims=True))
    mixed_rows = jnp.einsum('kgtj,jkd->tkgd', low(attn_probs), values, precision=highest)
    return mixed_rows.reshape(seq_len, HEADS * HEAD)

def expert_rows(pieces):
    slot_rows, gate_w, up_w, down_w = pieces
    gate_pre = low_back(jnp.dot(slot_rows, gate_w, precision=highest))
    up_pre = low_back(jnp.dot(slot_rows, up_w, precision=highest))
    active = low(low_back(jax.nn.silu(gate_pre) * up_pre))
    return low(low_back(jnp.dot(active, down_w, precision=highest)))

def assign_slots(routes, priority, live_rows):
    blocks = priority.shape[0]
    pair_span = priority.shape[1]
    expert_ids = routes.reshape(blocks, pair_span)
    live_pairs = jnp.broadcast_to(live_rows.reshape(blocks, pair_span // TOP, 1), (blocks, pair_span // TOP, TOP)).reshape(blocks, pair_span)

    def one_block(pieces):
        block_ids, block_live, block_rank = pieces
        sequence = jnp.argsort(block_rank).astype(jnp.int32)
        onehot = ((block_ids[:, None] == jnp.arange(EXPERTS, dtype=jnp.int32)[None, :]) & block_live[:, None]).astype(jnp.int32)
        ordered = onehot[sequence]
        earlier = jnp.cumsum(ordered, axis=0) - ordered
        slot_ordered = lax.optimization_barrier(jnp.sum(earlier * ordered, axis=1)).astype(jnp.int32)
        return jnp.zeros(pair_span, jnp.int32).at[sequence].set(slot_ordered)
    slot_ids = lax.map(one_block, (expert_ids, live_pairs, priority))
    kept_pairs = live_pairs & (slot_ids < CAP)
    return (expert_ids, slot_ids, kept_pairs)

def reference(hidden_in, cotangent, lengths, routes, priority, attn_gain, query_weight, key_weight, value_weight, output_weight, moe_gain, router, gate_weight, up_weight, down_weight):
    tokens = hidden_in.shape[0]
    seq_count = lengths.shape[0]
    seq_len = tokens // seq_count
    blocks = priority.shape[0]
    positions = jnp.arange(tokens, dtype=jnp.int32) % seq_len
    live_rows = positions < jnp.repeat(lengths, seq_len)
    expert_ids, slot_ids, kept_pairs = assign_slots(routes, priority, live_rows)
    expert_span = blocks * CAP
    block_index = jnp.arange(blocks, dtype=jnp.int32)[:, None]
    dest_slot = jnp.where(kept_pairs, expert_ids * expert_span + block_index * CAP + slot_ids, EXPERTS * expert_span).reshape(-1).astype(jnp.int32)
    pair_total = tokens * TOP
    source = jnp.full((EXPERTS * expert_span + 1,), pair_total, jnp.int32).at[dest_slot].set(jnp.arange(pair_total, dtype=jnp.int32))[:-1]
    source_token = jnp.where(source < pair_total, source // TOP, tokens).astype(jnp.int32)
    live_float = live_rows.astype(jnp.float32)

    def forward(inputs, gain_one, w_query, w_key, w_value, w_out, gain_two, w_router, w_gate, w_up, w_down):
        normed = low(rms_norm(inputs, gain_one))
        query_pre = low_back(jnp.dot(normed, w_query, precision=highest)).reshape(tokens, HEADS, HEAD)
        key_pre = low_back(jnp.dot(normed, w_key, precision=highest)).reshape(tokens, KV_HEADS, HEAD)
        queries = low(rotary(query_pre, positions, 1.0))
        key_rows = low(rotary(key_pre, positions, 1.0))
        values = low(low_back(jnp.dot(normed, w_value, precision=highest))).reshape(tokens, KV_HEADS, HEAD)
        mixed_rows = lax.map(jax.checkpoint(attend), (queries.reshape(seq_count, seq_len, HEADS, HEAD), key_rows.reshape(seq_count, seq_len, KV_HEADS, HEAD), values.reshape(seq_count, seq_len, KV_HEADS, HEAD), lengths))
        mixed_rows = low(low_back(mixed_rows.reshape(tokens, HEADS * HEAD)))
        branch = low_back(jnp.dot(mixed_rows, w_out, precision=highest))
        middle = inputs + branch
        routed = low(rms_norm(middle, gain_two))
        logits = jnp.dot(routed, w_router, precision=highest)
        picked = jnp.take_along_axis(logits, routes, axis=1)
        picked_top = lax.optimization_barrier(jnp.max(picked, axis=1, keepdims=True))
        picked_exp = jnp.exp(picked - picked_top)
        gate_values = picked_exp / lax.optimization_barrier(jnp.sum(picked_exp, axis=1, keepdims=True))
        padded = jnp.concatenate([routed, jnp.zeros((1, D), routed.dtype)], axis=0)
        buffers = low_back(padded[source_token]).reshape(EXPERTS, expert_span, D)
        results = lax.map(jax.checkpoint(expert_rows), (buffers, w_gate, w_up, w_down))
        results = jnp.concatenate([results.reshape(EXPERTS * expert_span, D), jnp.zeros((1, D), results.dtype)], axis=0)
        returned = results[dest_slot].reshape(tokens, TOP, D)
        mixture = jnp.einsum('tj,tjd->td', gate_values, returned, precision=highest)
        return (middle + mixture) * live_float[:, None].astype(middle.dtype)
    result, pullback = jax.vjp(forward, hidden_in.astype(jnp.float32), attn_gain.astype(jnp.float32), query_weight.astype(jnp.float32), key_weight.astype(jnp.float32), value_weight.astype(jnp.float32), output_weight.astype(jnp.float32), moe_gain.astype(jnp.float32), router.astype(jnp.float32), gate_weight.astype(jnp.float32), up_weight.astype(jnp.float32), down_weight.astype(jnp.float32))
    gradients = pullback(cotangent.astype(jnp.float32))
    return (result.astype(jnp.bfloat16), gradients[0], gradients[1], gradients[2], gradients[3], gradients[4], gradients[5], gradients[6], gradients[7], gradients[8], gradients[9], gradients[10])
```

```python
import functools

import jax
import jax.numpy as jnp
from jax import lax
from jax.experimental import pallas as pl
from jax.experimental.pallas import tpu as pltpu
from jax.sharding import PartitionSpec as P

D = 1024
HEADS = 16
HEAD = 64
KV_HEADS = 8
EXPERTS = 32
TOP = 8
CAP = 64


epsilon = 1e-05
rotary_base = 10000.0


def cut_along(array, dim, length):
    dims = array.shape
    tiles = array.reshape(*dims[:dim], length, dims[dim] // length, *dims[dim + 1 :])
    return jnp.moveaxis(tiles, dim, 0)


def joined_along(tiles, dim):
    tiles = jnp.moveaxis(tiles, 0, dim)
    dims = tiles.shape
    return tiles.reshape(*dims[:dim], dims[dim] * dims[dim + 1], *dims[dim + 2 :])


def exchange_both(array, axis, axes, splits, concats):
    sizes = [lax.axis_size(a) for a in axes]
    tiles = cut_along(array, splits[0], sizes[0])
    tiles = jnp.moveaxis(cut_along(tiles, splits[1] + 1, sizes[1]), 0, 1)
    inside = tiles.shape[2:]
    tiles = tiles.reshape(-1, *inside)
    tiles = lax.all_to_all(tiles, axis, split_axis=0, concat_axis=0, tiled=True)
    tiles = joined_along(tiles.reshape(*sizes, *inside), concats[0] + 1)
    return joined_along(tiles, concats[1])


def sent_together(arrays, axis, dim, along):
    widths = [a.shape[along] for a in arrays]
    both = jnp.concatenate(arrays, axis=along)
    whole = lax.all_gather(both, axis, axis=dim, tiled=True)
    return tuple(jnp.split(whole, [sum(widths[:k]) for k in range(1, len(widths))], axis=along))


def summed_on_arrival(array, axis, dim):
    tiles = cut_along(array, dim, lax.axis_size(axis))
    arrived = lax.all_to_all(tiles, axis, split_axis=0, concat_axis=0, tiled=True)
    return arrived.astype(jnp.float32).sum(axis=0)


def in_one_piece(arrays, axis, dim, along):
    widths = [a.shape[along] for a in arrays]
    both = jnp.concatenate(arrays, axis=along)
    whole = summed_on_arrival(both, axis, dim)
    return tuple(jnp.split(whole, [sum(widths[:k]) for k in range(1, len(widths))], axis=along))


def padded_to(lines, length):
    spare = -lines.shape[0] % length
    if not spare:
        return lines
    return jnp.concatenate([lines, jnp.zeros((spare, *lines.shape[1:]), lines.dtype)])


def sum_in_two_steps(array, axis):
    lines = array.reshape(-1, *array.shape[1:][-1:])
    padded = padded_to(lines, lax.axis_size(axis))
    own = lax.psum_scatter(padded, axis, scatter_dimension=0, tiled=True)
    whole = lax.all_gather(own, axis, axis=0, tiled=True)
    return whole[: len(lines)].reshape(array.shape)


def rms_scale(values):
    return lax.rsqrt(jnp.mean(values * values, axis=-1, keepdims=True) + epsilon)


def norm_back(grad_rows, normed_rows, scale_rows, gain_vec):
    scaled = grad_rows * gain_vec
    inner_sum = jnp.mean(scaled * normed_rows, axis=-1, keepdims=True)
    return (
        scale_rows * (scaled - normed_rows * inner_sum),
        jnp.sum(grad_rows * normed_rows, axis=0),
    )


def rotary(values, positions, sign):
    half_dim = values.shape[-1] // 2
    frequency = rotary_base ** (-jnp.arange(half_dim, dtype=jnp.float32) / half_dim)
    angles = positions.astype(jnp.float32)[:, None] * frequency[None, :]
    cosine = jnp.cos(angles)[:, None, :]
    sine_table = jnp.sin(angles)[:, None, :] * sign
    first_half = values[..., :half_dim]
    second_half = values[..., half_dim:]
    return jnp.concatenate(
        [
            first_half * cosine - second_half * sine_table,
            second_half * cosine + first_half * sine_table,
        ],
        axis=-1,
    )


def send_rows(outgoing, row_total, col_total):
    per_device = outgoing.shape[0] // (row_total * col_total)
    cap_rows = outgoing.shape[1]
    width = outgoing.shape[2]
    shaped = outgoing.reshape(row_total, col_total, per_device, 1, 1, cap_rows, width)
    moved = exchange_both(shaped, ("row", "col"), ("row", "col"), (0, 1), (3, 4))
    return moved.reshape(per_device, row_total * col_total * cap_rows, width)


def return_rows(produced, row_total, col_total):
    per_device = produced.shape[0]
    width = produced.shape[2]
    cap_rows = produced.shape[1] // (row_total * col_total)
    shaped = produced.reshape(1, 1, per_device, row_total, col_total, cap_rows, width)
    moved = exchange_both(shaped, ("row", "col"), ("row", "col"), (3, 4), (0, 1))
    return moved.reshape(row_total * col_total * per_device, cap_rows, width)


MESH = pl.DeviceIdType.MESH
GROUP = 32
CHUNKS = 8
SPAN = GROUP // CHUNKS


def place():
    col = lax.axis_index("col")
    return lax.axis_index("dp"), lax.axis_index("row"), lax.rem(col, 4), col // 4


def shifted(k, sign):
    y, r, x, z = place()
    chunk, i = k // SPAN, lax.rem(k, SPAN)
    dr, dx, dz = chunk // 4, i, lax.rem(i + lax.rem(chunk, 4), 4)
    row = lax.rem(r + dr, 2)
    col = lax.rem(z + sign * dz + 4, 4) * 4 + lax.rem(x + sign * dx + 4, 4)
    return (y, row, col), row * 16 + col


def eye(n):
    return lax.broadcasted_iota(jnp.int32, (n, n), 0) == lax.broadcasted_iota(
        jnp.int32, (n, n), 1
    )


def as_row(column):
    return jnp.sum(jnp.where(eye(column.shape[0]), column, 0.0), axis=0, keepdims=True)


def as_column(row_vec):
    return jnp.sum(jnp.where(eye(row_vec.shape[1]), row_vec, 0.0), axis=1, keepdims=True)


def dot(a, b, dims):
    return lax.dot_general(a, b, (dims, ((), ())), preferred_element_type=jnp.float32)


def plane_barrier():
    barrier = pltpu.get_barrier_semaphore()

    @pl.loop(1, GROUP)
    def _(k):
        device, _ = shifted(k, 1)
        pl.semaphore_signal(barrier, inc=1, device_id=device, device_id_type=MESH)

    pl.semaphore_wait(barrier, GROUP - 1)


def expert_kernel(
    routed_ref,
    pos_ref,
    gates_ref,
    grads_ref,
    wg_ref,
    wu_ref,
    wd_ref,
    rg_ref,
    gdot_ref,
    prod_ref,
    dg_ref,
    du_ref,
    dd_ref,
    onehot,
    outgoing,
    arrived,
    going_back,
    come_back,
    gate_out,
    gate_in,
    dot_out,
    dot_in,
    active,
    weighted,
    pre_grads,
    send_sem,
    recv_sem,
    gsend_sem,
    grecv_sem,
):
    plane_barrier()

    def copies(k, out, into, small_out, small_into, sign, base):
        device, _ = shifted(k, sign)
        return (
            pltpu.make_async_remote_copy(
                src_ref=out.at[k],
                dst_ref=into.at[k],
                send_sem=send_sem.at[base + k],
                recv_sem=recv_sem.at[base + k],
                device_id=device,
                device_id_type=MESH,
            ),
            pltpu.make_async_remote_copy(
                src_ref=small_out.at[k],
                dst_ref=small_into.at[k],
                send_sem=gsend_sem.at[base + k],
                recv_sem=grecv_sem.at[base + k],
                device_id=device,
                device_id_type=MESH,
            ),
        )

    def there(k):
        return copies(k, outgoing, arrived, gate_out, gate_in, 1, 0)

    def back(k):
        return copies(k, going_back, come_back, dot_out, dot_in, -1, GROUP)

    slot_iota = lax.broadcasted_iota(jnp.int32, (CAP, routed_ref.shape[0]), 0)

    @pl.loop(0, CHUNKS)
    def _(c):
        parts = []
        for i in range(SPAN):
            k = c * SPAN + i
            _, expert = shifted(k, 1)
            chosen = slot_iota == pos_ref[pl.ds(expert, 1), :]
            gate_col = jnp.sum(
                jnp.where(chosen, gates_ref[pl.ds(expert, 1), :], 0.0), axis=1, keepdims=True
            )
            gate_out[k, 0:1, 0:CAP] = as_row(gate_col)
            parts.append(chosen.astype(jnp.float32).astype(jnp.bfloat16))
        chosen = jnp.concatenate(parts, axis=0)
        onehot[pl.ds(c * SPAN * CAP, SPAN * CAP), :] = chosen
        rows = dot(chosen, routed_ref[...], ((1,), (0,))).astype(jnp.bfloat16)
        for i in range(SPAN):
            k = c * SPAN + i
            outgoing[k] = rows[i * CAP : (i + 1) * CAP]

            @pl.when(k != 0)
            def _():
                for copy in there(k):
                    copy.start()

    arrived[0] = outgoing[0]
    gate_in[0] = gate_out[0]

    @pl.loop(0, CHUNKS)
    def _(c):
        for i in range(SPAN):
            k = c * SPAN + i

            @pl.when(k != 0)
            def _():
                for copy in there(k):
                    copy.wait_recv()

        span = pl.ds(c * SPAN * CAP, SPAN * CAP)
        rows, gate_cols, grads = [], [], []
        for i in range(SPAN):
            k = c * SPAN + i
            _, source = shifted(k, -1)
            rows.append(arrived[k])
            gate_cols.append(as_column(gate_in[k, 0:1, 0:CAP]))
            grads.append(grads_ref[source])
        rows = jnp.concatenate(rows, axis=0)
        gate_cols = jnp.concatenate(gate_cols, axis=0)
        grads = jnp.concatenate(grads, axis=0).astype(jnp.float32)
        gate_pre = dot(rows, wg_ref[...], ((1,), (0,)))
        up_pre = dot(rows, wu_ref[...], ((1,), (0,)))
        gate_sig = jax.nn.sigmoid(gate_pre)
        gate_act = gate_pre * gate_sig
        act = (gate_act * up_pre).astype(jnp.bfloat16)
        active[span, :] = act
        produced = dot(act, wd_ref[...], ((1,), (0,))).astype(jnp.bfloat16)
        dots = jnp.sum(produced.astype(jnp.float32) * grads, axis=1, keepdims=True)
        produced_grad = (gate_cols * grads).astype(jnp.bfloat16)
        weighted[span, :] = produced_grad
        act_grad = dot(produced_grad, wd_ref[...], ((1,), (1,))).astype(jnp.bfloat16)
        act_grad = act_grad.astype(jnp.float32)
        gate_grad = (
            act_grad * up_pre * gate_sig * (1.0 + gate_pre * (1.0 - gate_sig))
        ).astype(jnp.bfloat16)
        up_grad = (act_grad * gate_act).astype(jnp.bfloat16)
        pre_grads[span, 0:512] = gate_grad
        pre_grads[span, 512:1024] = up_grad
        row_grads = dot(gate_grad, wg_ref[...], ((1,), (1,)))
        row_grads = row_grads + dot(up_grad, wu_ref[...], ((1,), (1,)))
        row_grads = row_grads.astype(jnp.bfloat16)
        for i in range(SPAN):
            k = c * SPAN + i
            _, source = shifted(k, -1)
            part = slice(i * CAP, (i + 1) * CAP)
            prod_ref[source] = produced[part]
            going_back[k] = row_grads[part]
            dot_out[k, 0:1, 0:CAP] = as_row(dots[part])

            @pl.when(k != 0)
            def _():
                for copy in back(k):
                    copy.start()

    come_back[0] = going_back[0]
    dot_in[0] = dot_out[0]

    @pl.loop(0, 4)
    def _(n):
        span = pl.ds(pl.multiple_of(n * 256, 256), 256)
        part = dot(arrived[:, :, span].reshape(GROUP * CAP, 256), pre_grads[...], ((0,), (0,)))
        dg_ref[span, :] = part[:, 0:512].astype(jnp.bfloat16)
        du_ref[span, :] = part[:, 512:1024].astype(jnp.bfloat16)

    @pl.loop(0, 2)
    def _(n):
        span = pl.ds(pl.multiple_of(n * 256, 256), 256)
        dd_ref[span, :] = dot(active[:, span], weighted[...], ((0,), (0,))).astype(jnp.bfloat16)

    rg_ref[...] = jnp.zeros_like(rg_ref)

    @pl.loop(0, CHUNKS)
    def _(c):
        for i in range(SPAN):
            k = c * SPAN + i

            @pl.when(k != 0)
            def _():
                for copy in back(k):
                    copy.wait_recv()

        span = pl.ds(c * SPAN * CAP, SPAN * CAP)
        chosen = onehot[span, :]
        rows = come_back[pl.ds(c * SPAN, SPAN)].reshape(SPAN * CAP, D)
        rg_ref[...] += dot(chosen, rows, ((0,), (0,)))
        for i in range(SPAN):
            k = c * SPAN + i
            _, expert = shifted(k, 1)
            dots = as_column(dot_in[k, 0:1, 0:CAP])
            mask = chosen[i * CAP : (i + 1) * CAP].astype(jnp.float32)
            gdot_ref[pl.ds(expert, 1), :] = jnp.sum(mask * dots, axis=0, keepdims=True)

    @pl.loop(1, GROUP)
    def _(k):
        for copy in there(k):
            copy.wait_send()
        for copy in back(k):
            copy.wait_send()


def experts(routed, pos, gates, grads, wg, wu, wd):
    tokens = routed.shape[0]
    rows = GROUP * CAP
    f32, bf16 = jnp.float32, jnp.bfloat16
    vmem = pl.BlockSpec(memory_space=pltpu.VMEM)
    block = pltpu.VMEM((GROUP, CAP, D), bf16)
    small = pltpu.VMEM((GROUP, 8, 128), f32)
    return pl.pallas_call(
        expert_kernel,
        out_shape=(
            jax.ShapeDtypeStruct((tokens, D), f32),
            jax.ShapeDtypeStruct((EXPERTS, tokens), f32),
            jax.ShapeDtypeStruct((GROUP, CAP, D), bf16),
            jax.ShapeDtypeStruct(wg.shape, bf16),
            jax.ShapeDtypeStruct(wu.shape, bf16),
            jax.ShapeDtypeStruct(wd.shape, bf16),
        ),
        in_specs=[vmem] * 7,
        out_specs=[vmem] * 6,
        scratch_shapes=[
            pltpu.VMEM((rows, tokens), bf16),
            block,
            block,
            block,
            block,
            small,
            small,
            small,
            small,
            pltpu.VMEM((rows, 512), bf16),
            pltpu.VMEM((rows, D), bf16),
            pltpu.VMEM((rows, 1024), bf16),
            pltpu.SemaphoreType.DMA((2 * GROUP,)),
            pltpu.SemaphoreType.DMA((2 * GROUP,)),
            pltpu.SemaphoreType.DMA((2 * GROUP,)),
            pltpu.SemaphoreType.DMA((2 * GROUP,)),
        ],
        compiler_params=pltpu.CompilerParams(
            collective_id=1, has_side_effects=True, vmem_limit_bytes=58 << 20
        ),
        name="experts",
    )(routed, pos, gates, grads, wg, wu, wd)


def on_device(
    hidden_in,
    cotangent,
    lengths,
    routes,
    priority,
    attn_gain,
    query_weight,
    key_weight,
    value_weight,
    output_weight,
    moe_gain,
    router,
    gate_weight,
    up_weight,
    down_weight,
):
    row_total = lax.axis_size("row")
    col_total = lax.axis_size("col")
    tok_count = hidden_in.shape[0]
    seq_len = row_total * tok_count
    groups = HEADS // KV_HEADS
    kv_width = KV_HEADS * HEAD
    score_scale = HEAD ** (-0.5)
    positions = lax.axis_index("row") * tok_count + jnp.arange(tok_count, dtype=jnp.int32)
    seq_length = lengths[0]
    live_rows = positions < seq_length
    live_float = live_rows.astype(jnp.float32)[:, None]
    key_live = jnp.arange(seq_len) < seq_length
    expert_ids = jnp.arange(EXPERTS, dtype=jnp.int32)
    chosen = routes[:, :, None] == expert_ids[None, None, :]
    routed_to = jnp.any(chosen, axis=1)
    ranks = jnp.sum(jnp.where(chosen, priority.reshape(tok_count, TOP, 1), 0), axis=1)
    ranks = jnp.where(routed_to & live_rows[:, None], ranks, 1 << 20)
    ranks_et = ranks.T
    slots_et = jnp.sum((ranks_et[:, :, None] > ranks_et[:, None, :]).astype(jnp.int32), axis=2)
    pos_et = jnp.where((ranks_et < (1 << 20)) & (slots_et < CAP), slots_et, -1)
    onehot = (pos_et[:, None, :] == jnp.arange(CAP, dtype=jnp.int32)[None, :, None]).astype(
        jnp.bfloat16
    )
    onehot = onehot.reshape(EXPERTS * CAP, tok_count)
    outgoing_grad = jnp.dot(onehot, cotangent, preferred_element_type=jnp.float32)
    outgoing_grad = outgoing_grad.astype(jnp.bfloat16).reshape(EXPERTS, CAP, D)
    arrived_grad = lax.all_to_all(
        outgoing_grad, ("row", "col"), split_axis=0, concat_axis=0, tiled=True
    )
    grad_out = cotangent.astype(jnp.float32) * live_float
    inputs = hidden_in.astype(jnp.float32)
    scale_one = rms_scale(inputs)
    normed_one = inputs * scale_one
    normed = (normed_one * attn_gain).astype(jnp.bfloat16)
    w_query, w_key, w_value, w_out = sent_together(
        (query_weight, key_weight, value_weight, output_weight), ("row", "col"), 0, 1
    )
    query_pre = jnp.dot(normed, w_query, preferred_element_type=jnp.float32).reshape(
        tok_count, HEADS, HEAD
    )
    key_pre = jnp.dot(normed, w_key, preferred_element_type=jnp.float32).reshape(
        tok_count, KV_HEADS, HEAD
    )
    queries = (
        rotary(query_pre, positions, 1.0)
        .astype(jnp.bfloat16)
        .reshape(tok_count, KV_HEADS, groups, HEAD)
    )
    key_rows = rotary(key_pre, positions, 1.0).astype(jnp.bfloat16)
    values = (
        jnp.dot(normed, w_value, preferred_element_type=jnp.float32)
        .astype(jnp.bfloat16)
        .reshape(tok_count, KV_HEADS, HEAD)
    )
    all_keys, all_values = sent_together((key_rows, values), "row", 0, 1)

    def masked_scores():
        raw_scores = (
            jnp.einsum("tkgd,jkd->kgtj", queries, all_keys, preferred_element_type=jnp.float32)
            * score_scale
        )
        return jnp.where(key_live[None, None, None, :], raw_scores, -1000000000.0)

    scores = masked_scores()
    top_score = jnp.max(scores, axis=-1, keepdims=True)
    weights = jnp.exp(scores - top_score)
    totals = jnp.sum(weights, axis=-1, keepdims=True)
    log_total = top_score + jnp.log(totals)
    attn_probs = (weights / totals).astype(jnp.bfloat16)
    mixed_rows = jnp.einsum(
        "kgtj,jkd->tkgd", attn_probs, all_values, preferred_element_type=jnp.float32
    )
    mixed_rows = mixed_rows.reshape(tok_count, D).astype(jnp.bfloat16)
    middle = inputs + jnp.dot(mixed_rows, w_out, preferred_element_type=jnp.float32)
    scale_two = rms_scale(middle)
    normed_two = middle * scale_two
    routed = (normed_two * moe_gain).astype(jnp.bfloat16)
    logits = jnp.dot(routed, router, preferred_element_type=jnp.float32)
    picked = jnp.where(routed_to, logits, -jnp.inf)
    picked_exp = jnp.exp(picked - jnp.max(picked, axis=1, keepdims=True))
    gates_te = picked_exp / jnp.sum(picked_exp, axis=1, keepdims=True)
    returned_rows, gate_dot_et, produced, gate_local, up_local, down_local = experts(
        routed, pos_et, gates_te.T, arrived_grad, gate_weight[0], up_weight[0], down_weight[0]
    )
    returned = lax.all_to_all(produced, ("row", "col"), split_axis=0, concat_axis=0, tiled=True)
    gate_dot = gate_dot_et.T
    picked_grad = gates_te * (
        gate_dot - jnp.sum(gates_te * gate_dot, axis=1, keepdims=True)
    )
    logit_grad = picked_grad
    router_local = jnp.dot(
        routed.astype(jnp.float32).T, logit_grad, precision=lax.Precision.HIGHEST
    )
    routed_grad = jnp.dot(logit_grad, router.astype(jnp.float32).T, precision=lax.Precision.HIGHEST)
    routed_grad = routed_grad + returned_rows
    middle_norm_grad, moe_gain_local = norm_back(routed_grad, normed_two, scale_two, moe_gain)
    middle_grad = grad_out + middle_norm_grad
    branch_grad = middle_grad.astype(jnp.bfloat16)
    mixed_grad = jnp.einsum("te,de->td", branch_grad, w_out, preferred_element_type=jnp.float32)
    mixed_grad = mixed_grad.astype(jnp.bfloat16).reshape(tok_count, KV_HEADS, groups, HEAD)
    probs_again = jnp.exp(masked_scores() - log_total)
    prob_grad = jnp.einsum(
        "tkgd,jkd->kgtj", mixed_grad, all_values, preferred_element_type=jnp.float32
    )
    value_part = jnp.einsum(
        "kgtj,tkgd->jkd",
        probs_again.astype(jnp.bfloat16),
        mixed_grad,
        preferred_element_type=jnp.float32,
    )
    inner_sum = jnp.sum(probs_again * prob_grad, axis=-1, keepdims=True)
    score_grad = (probs_again * (prob_grad - inner_sum)).astype(jnp.bfloat16)
    query_rot_grad = (
        jnp.einsum("kgtj,jkd->tkgd", score_grad, all_keys, preferred_element_type=jnp.float32)
        * score_scale
    )
    key_part = (
        jnp.einsum("kgtj,tkgd->jkd", score_grad, queries, preferred_element_type=jnp.float32)
        * score_scale
    )
    key_sum, value_sum = in_one_piece(
        (key_part.astype(jnp.bfloat16), value_part.astype(jnp.bfloat16)), "row", 0, 1
    )
    query_pre_grad = (
        rotary(query_rot_grad.reshape(tok_count, HEADS, HEAD), positions, -1.0)
        .reshape(tok_count, D)
        .astype(jnp.bfloat16)
    )
    key_pre_grad = (
        rotary(key_sum, positions, -1.0).reshape(tok_count, kv_width).astype(jnp.bfloat16)
    )
    value_pre_grad = value_sum.reshape(tok_count, kv_width).astype(jnp.bfloat16)
    normed_grad = jnp.einsum(
        "tc,dc->td", query_pre_grad, w_query, preferred_element_type=jnp.float32
    )
    normed_grad = normed_grad + jnp.einsum(
        "tc,dc->td", key_pre_grad, w_key, preferred_element_type=jnp.float32
    )
    normed_grad = normed_grad + jnp.einsum(
        "tc,dc->td", value_pre_grad, w_value, preferred_element_type=jnp.float32
    )
    input_norm_grad, attn_gain_local = norm_back(normed_grad, normed_one, scale_one, attn_gain)
    hidden_grad = middle_grad + input_norm_grad
    qkv_grad = jnp.concatenate([query_pre_grad, key_pre_grad, value_pre_grad], axis=1)
    grad_part = lax.psum_scatter(
        jnp.concatenate(
            [
                jnp.einsum("tr,tc->rc", normed, qkv_grad, preferred_element_type=jnp.float32),
                jnp.einsum(
                    "tr,tc->rc", mixed_rows, branch_grad, preferred_element_type=jnp.float32
                ),
            ],
            axis=1,
        ).astype(jnp.bfloat16),
        ("row", "col"),
        scatter_dimension=0,
        tiled=True,
    )
    grad_shard, gate_sum, up_sum, down_sum = (
        sum_in_two_steps(grad_part, "dp").astype(jnp.float32),
        sum_in_two_steps(gate_local.astype(jnp.bfloat16), "dp").astype(jnp.float32),
        sum_in_two_steps(up_local.astype(jnp.bfloat16), "dp").astype(jnp.float32),
        sum_in_two_steps(down_local.astype(jnp.bfloat16), "dp").astype(jnp.float32),
    )
    attn_gain_sum, moe_gain_sum, router_sum = lax.psum(
        (attn_gain_local, moe_gain_local, router_local), ("dp", "row", "col")
    )
    gate_rows = jnp.sum(
        jnp.where(onehot.reshape(EXPERTS, CAP, tok_count) > 0, gates_te.T[:, None, :], 0.0),
        axis=2,
    )
    weighted = (returned.astype(jnp.float32) * gate_rows[:, :, None]).reshape(EXPERTS * CAP, D)
    high = weighted.astype(jnp.bfloat16)
    rest = (weighted - high.astype(jnp.float32)).astype(jnp.bfloat16)
    mixture = jnp.einsum("st,sd->td", onehot, high, preferred_element_type=jnp.float32)
    mixture = mixture + jnp.einsum("st,sd->td", onehot, rest, preferred_element_type=jnp.float32)
    hidden_out = ((middle + mixture) * live_float).astype(jnp.bfloat16)
    query_grad = grad_shard[:, :D]
    key_grad = grad_shard[:, D : D + kv_width]
    value_grad = grad_shard[:, D + kv_width : D + 2 * kv_width]
    output_grad = grad_shard[:, D + 2 * kv_width :]
    return (
        hidden_out,
        hidden_grad,
        attn_gain_sum,
        query_grad,
        key_grad,
        value_grad,
        output_grad,
        moe_gain_sum,
        router_sum,
        gate_sum[None],
        up_sum[None],
        down_sum[None],
    )


def solution(mesh):
    return jax.shard_map(
        on_device,
        mesh=mesh,
        in_specs=(
            P(("dp", "col", "row"), None),
            P(("dp", "col", "row"), None),
            P(("dp", "col")),
            P(("dp", "col", "row"), None),
            P(("dp", "col", "row"), None),
            P(),
            P(("row", "col"), None),
            P(("row", "col"), None),
            P(("row", "col"), None),
            P(("row", "col"), None),
            P(),
            P(),
            P(("row", "col"), None, None),
            P(("row", "col"), None, None),
            P(("row", "col"), None, None),
        ),
        out_specs=(
            P(("dp", "col", "row"), None),
            P(("dp", "col", "row"), None),
            P(),
            P(("row", "col"), None),
            P(("row", "col"), None),
            P(("row", "col"), None),
            P(("row", "col"), None),
            P(),
            P(),
            P(("row", "col"), None, None),
            P(("row", "col"), None, None),
            P(("row", "col"), None, None),
        ),
        check_vma=False,
    )
```

```python
import functools

import jax
import jax.numpy as jnp
from jax import lax
from jax.experimental import pallas as pl
from jax.experimental.pallas import tpu as pltpu
from jax.sharding import PartitionSpec as P

D = 1024
HEADS = 16
HEAD = 64
KV_HEADS = 8
EXPERTS = 32
TOP = 8
CAP = 64


epsilon = 1e-05
rotary_base = 10000.0


def sent_together(arrays, axis, dim, along):
    widths = [a.shape[along] for a in arrays]
    both = jnp.concatenate(arrays, axis=along)
    whole = lax.all_gather(both, axis, axis=dim, tiled=True)
    return tuple(jnp.split(whole, [sum(widths[:k]) for k in range(1, len(widths))], axis=along))


def rms_scale(values):
    return lax.rsqrt(jnp.mean(values * values, axis=-1, keepdims=True) + epsilon)


def rotary(values, positions, sign):
    half_dim = values.shape[-1] // 2
    frequency = rotary_base ** (-jnp.arange(half_dim, dtype=jnp.float32) / half_dim)
    angles = positions.astype(jnp.float32)[:, None] * frequency[None, :]
    cosine = jnp.cos(angles)[:, None, :]
    sine_table = jnp.sin(angles)[:, None, :] * sign
    first_half = values[..., :half_dim]
    second_half = values[..., half_dim:]
    return jnp.concatenate(
        [
            first_half * cosine - second_half * sine_table,
            second_half * cosine + first_half * sine_table,
        ],
        axis=-1,
    )


MESH = pl.DeviceIdType.MESH
GROUP = 32
CHUNKS = 8
SPAN = GROUP // CHUNKS


def place():
    col = lax.axis_index("col")
    return lax.axis_index("dp"), lax.axis_index("row"), lax.rem(col, 4), col // 4


def shifted(k, sign):
    y, r, x, z = place()
    chunk, i = k // SPAN, lax.rem(k, SPAN)
    dr, dx, dz = chunk // 4, i, lax.rem(i + lax.rem(chunk, 4), 4)
    row = lax.rem(r + dr, 2)
    col = lax.rem(z + sign * dz + 4, 4) * 4 + lax.rem(x + sign * dx + 4, 4)
    return (y, row, col), row * 16 + col


def eye(n):
    return lax.broadcasted_iota(jnp.int32, (n, n), 0) == lax.broadcasted_iota(
        jnp.int32, (n, n), 1
    )


def as_row(column):
    return jnp.sum(jnp.where(eye(column.shape[0]), column, 0.0), axis=0, keepdims=True)


def as_column(row_vec):
    return jnp.sum(jnp.where(eye(row_vec.shape[1]), row_vec, 0.0), axis=1, keepdims=True)


def dot(a, b, dims):
    return lax.dot_general(a, b, (dims, ((), ())), preferred_element_type=jnp.float32)


def plane_barrier():
    barrier = pltpu.get_barrier_semaphore()

    @pl.loop(1, GROUP)
    def _(k):
        device, _ = shifted(k, 1)
        pl.semaphore_signal(barrier, inc=1, device_id=device, device_id_type=MESH)

    pl.semaphore_wait(barrier, GROUP - 1)


def expert_kernel(
    routed_ref,
    pos_ref,
    gates_ref,
    grads_ref,
    wg_ref,
    wu_ref,
    wd_ref,
    rg_ref,
    gdot_ref,
    prod_ref,
    dg_ref,
    du_ref,
    dd_ref,
    onehot,
    outgoing,
    arrived,
    going_back,
    come_back,
    gate_out,
    gate_in,
    dot_out,
    dot_in,
    active,
    weighted,
    pre_grads,
    send_sem,
    recv_sem,
    gsend_sem,
    grecv_sem,
):
    plane_barrier()

    def copies(k, out, into, small_out, small_into, sign, base):
        device, _ = shifted(k, sign)
        return (
            pltpu.make_async_remote_copy(
                src_ref=out.at[k],
                dst_ref=into.at[k],
                send_sem=send_sem.at[base + k],
                recv_sem=recv_sem.at[base + k],
                device_id=device,
                device_id_type=MESH,
            ),
            pltpu.make_async_remote_copy(
                src_ref=small_out.at[k],
                dst_ref=small_into.at[k],
                send_sem=gsend_sem.at[base + k],
                recv_sem=grecv_sem.at[base + k],
                device_id=device,
                device_id_type=MESH,
            ),
        )

    def there(k):
        return copies(k, outgoing, arrived, gate_out, gate_in, 1, 0)

    def back(k):
        return copies(k, going_back, come_back, dot_out, dot_in, -1, GROUP)

    slot_iota = lax.broadcasted_iota(jnp.int32, (CAP, routed_ref.shape[0]), 0)

    @pl.loop(0, CHUNKS)
    def _(c):
        parts = []
        for i in range(SPAN):
            k = c * SPAN + i
            _, expert = shifted(k, 1)
            chosen = slot_iota == pos_ref[pl.ds(expert, 1), :]
            gate_col = jnp.sum(
                jnp.where(chosen, gates_ref[pl.ds(expert, 1), :], 0.0), axis=1, keepdims=True
            )
            gate_out[k, 0:1, 0:CAP] = as_row(gate_col)
            parts.append(chosen.astype(jnp.float32).astype(jnp.bfloat16))
        chosen = jnp.concatenate(parts, axis=0)
        onehot[pl.ds(c * SPAN * CAP, SPAN * CAP), :] = chosen
        rows = dot(chosen, routed_ref[...], ((1,), (0,))).astype(jnp.bfloat16)
        for i in range(SPAN):
            k = c * SPAN + i
            outgoing[k] = rows[i * CAP : (i + 1) * CAP]

            @pl.when(k != 0)
            def _():
                for copy in there(k):
                    copy.start()

    arrived[0] = outgoing[0]
    gate_in[0] = gate_out[0]

    @pl.loop(0, CHUNKS)
    def _(c):
        for i in range(SPAN):
            k = c * SPAN + i

            @pl.when(k != 0)
            def _():
                for copy in there(k):
                    copy.wait_recv()

        span = pl.ds(c * SPAN * CAP, SPAN * CAP)
        rows, gate_cols, grads = [], [], []
        for i in range(SPAN):
            k = c * SPAN + i
            _, source = shifted(k, -1)
            rows.append(arrived[k])
            gate_cols.append(as_column(gate_in[k, 0:1, 0:CAP]))
            grads.append(grads_ref[source])
        rows = jnp.concatenate(rows, axis=0)
        gate_cols = jnp.concatenate(gate_cols, axis=0)
        grads = jnp.concatenate(grads, axis=0).astype(jnp.float32)
        gate_pre = dot(rows, wg_ref[...], ((1,), (0,)))
        up_pre = dot(rows, wu_ref[...], ((1,), (0,)))
        gate_sig = jax.nn.sigmoid(gate_pre)
        gate_act = gate_pre * gate_sig
        act = (gate_act * up_pre).astype(jnp.bfloat16)
        active[span, :] = act
        produced = dot(act, wd_ref[...], ((1,), (0,))).astype(jnp.bfloat16)
        dots = jnp.sum(produced.astype(jnp.float32) * grads, axis=1, keepdims=True)
        produced_grad = (gate_cols * grads).astype(jnp.bfloat16)
        weighted[span, :] = produced_grad
        act_grad = dot(produced_grad, wd_ref[...], ((1,), (1,))).astype(jnp.bfloat16)
        act_grad = act_grad.astype(jnp.float32)
        gate_grad = (
            act_grad * up_pre * gate_sig * (1.0 + gate_pre * (1.0 - gate_sig))
        ).astype(jnp.bfloat16)
        up_grad = (act_grad * gate_act).astype(jnp.bfloat16)
        pre_grads[span, 0:512] = gate_grad
        pre_grads[span, 512:1024] = up_grad
        row_grads = dot(gate_grad, wg_ref[...], ((1,), (1,)))
        row_grads = row_grads + dot(up_grad, wu_ref[...], ((1,), (1,)))
        row_grads = row_grads.astype(jnp.bfloat16)
        for i in range(SPAN):
            k = c * SPAN + i
            _, source = shifted(k, -1)
            part = slice(i * CAP, (i + 1) * CAP)
            prod_ref[k] = produced[part]
            going_back[k] = row_grads[part]
            dot_out[k, 0:1, 0:CAP] = as_row(dots[part])

            @pl.when(k != 0)
            def _():
                for copy in back(k):
                    copy.start()

    come_back[0] = going_back[0]
    dot_in[0] = dot_out[0]

    @pl.loop(0, 4)
    def _(n):
        span = pl.ds(pl.multiple_of(n * 256, 256), 256)
        part = dot(arrived[:, :, span].reshape(GROUP * CAP, 256), pre_grads[...], ((0,), (0,)))
        dg_ref[span, :] = part[:, 0:512].astype(jnp.bfloat16)
        du_ref[span, :] = part[:, 512:1024].astype(jnp.bfloat16)

    @pl.loop(0, 2)
    def _(n):
        span = pl.ds(pl.multiple_of(n * 256, 256), 256)
        dd_ref[span, :] = dot(active[:, span], weighted[...], ((0,), (0,))).astype(jnp.bfloat16)

    rg_ref[...] = jnp.zeros_like(rg_ref)

    @pl.loop(0, CHUNKS)
    def _(c):
        for i in range(SPAN):
            k = c * SPAN + i

            @pl.when(k != 0)
            def _():
                for copy in back(k):
                    copy.wait_recv()

        span = pl.ds(c * SPAN * CAP, SPAN * CAP)
        chosen = onehot[span, :]
        rows = come_back[pl.ds(c * SPAN, SPAN)].reshape(SPAN * CAP, D)
        rg_ref[...] += dot(chosen, rows, ((0,), (0,)))
        for i in range(SPAN):
            k = c * SPAN + i
            _, expert = shifted(k, 1)
            dots = as_column(dot_in[k, 0:1, 0:CAP])
            mask = chosen[i * CAP : (i + 1) * CAP].astype(jnp.float32)
            gdot_ref[pl.ds(expert, 1), :] = jnp.sum(mask * dots, axis=0, keepdims=True)

    @pl.loop(1, GROUP)
    def _(k):
        for copy in there(k):
            copy.wait_send()
        for copy in back(k):
            copy.wait_send()


def experts(routed, pos, gates, grads, wg, wu, wd):
    tokens = routed.shape[0]
    rows = GROUP * CAP
    f32, bf16 = jnp.float32, jnp.bfloat16
    vmem = pl.BlockSpec(memory_space=pltpu.VMEM)
    block = pltpu.VMEM((GROUP, CAP, D), bf16)
    small = pltpu.VMEM((GROUP, 8, 128), f32)
    return pl.pallas_call(
        expert_kernel,
        out_shape=(
            jax.ShapeDtypeStruct((tokens, D), f32),
            jax.ShapeDtypeStruct((EXPERTS, tokens), f32),
            jax.ShapeDtypeStruct((GROUP, CAP, D), bf16),
            jax.ShapeDtypeStruct(wg.shape, bf16),
            jax.ShapeDtypeStruct(wu.shape, bf16),
            jax.ShapeDtypeStruct(wd.shape, bf16),
        ),
        in_specs=[vmem] * 7,
        out_specs=[vmem] * 6,
        scratch_shapes=[
            pltpu.VMEM((rows, tokens), bf16),
            block,
            block,
            block,
            block,
            small,
            small,
            small,
            small,
            pltpu.VMEM((rows, 512), bf16),
            pltpu.VMEM((rows, D), bf16),
            pltpu.VMEM((rows, 1024), bf16),
            pltpu.SemaphoreType.DMA((2 * GROUP,)),
            pltpu.SemaphoreType.DMA((2 * GROUP,)),
            pltpu.SemaphoreType.DMA((2 * GROUP,)),
            pltpu.SemaphoreType.DMA((2 * GROUP,)),
        ],
        compiler_params=pltpu.CompilerParams(
            collective_id=1, has_side_effects=True, vmem_limit_bytes=58 << 20
        ),
        name="experts",
    )(routed, pos, gates, grads, wg, wu, wd)


PLANES = 4
CHIPS = 16
HALF = D // 2
NEG = -1000000000.0


def chip_shift(q, sign):
    y, r, x, z = place()
    dx, dz = lax.rem(q, 4), lax.rem(lax.rem(q, 4) + q // 4, 4)
    col = lax.rem(z + sign * dz + 4, 4) * 4 + lax.rem(x + sign * dx + 4, 4)
    return (y, r, col), col


def plane_shift(n):
    y, r, x, z = place()
    other = lax.rem(y + n, PLANES)
    return (other, r, z * 4 + x), other


def split_two(values):
    high = values.astype(jnp.bfloat16)
    return high, (values - high.astype(jnp.float32)).astype(jnp.bfloat16)


def turned_back(rows, cosine, sine):
    first, second = rows[0:32], rows[32:64]
    return jnp.concatenate(
        [first * cosine + second * sine, second * cosine - first * sine], axis=0
    )


def remote(src, dst, send_sem, recv_sem, device):
    return pltpu.make_async_remote_copy(
        src_ref=src,
        dst_ref=dst,
        send_sem=send_sem,
        recv_sem=recv_sem,
        device_id=device,
        device_id_type=MESH,
    )


def finish_kernel(
    length_ref,
    prod_ref,
    pos_ref,
    gates_ref,
    rg_ref,
    gdot_ref,
    dg_ref,
    du_ref,
    dd_ref,
    routed_ref,
    router_ref,
    middle_ref,
    cot_ref,
    hidden_ref,
    again_ref,
    mgain_ref,
    normed_ref,
    mixed_ref,
    w_ref,
    q_ref,
    k_ref,
    v_ref,
    lse_ref,
    cos_ref,
    sin_ref,
    hout_ref,
    hgrad_ref,
    again_out,
    mgain_out,
    router_out,
    own_out,
    gsum_ref,
    usum_ref,
    dsum_ref,
    back,
    y_in,
    branch_own,
    branch_sib,
    normed_sib,
    mixed_sib,
    mg_t,
    grad_t,
    grad_sib,
    kv_own,
    kv_out,
    kv_in,
    weight_part,
    weight_in,
    y_out,
    y_parts,
    small_out,
    small_in,
    small_y,
    small_y_in,
    gain_out,
    gain_in,
    gain_y,
    gain_y_in,
    router_all,
    c_send,
    c_recv,
    y1_send,
    y1_recv,
    y2_send,
    y2_recv,
    sib_send,
    sib_recv,
    rs_send,
    rs_recv,
    ys_send,
    ys_recv,
    sm_send,
    sm_recv,
):
    y, r, x, z = place()
    me = r * 16 + z * 4 + x
    sibling = (y, 1 - r, z * 4 + x)
    tokens = routed_ref.shape[0]
    f32, bf16 = jnp.float32, jnp.bfloat16

    barrier = pltpu.get_barrier_semaphore()

    @pl.loop(1, GROUP)
    def _(k):
        device, _ = shifted(k, 1)
        pl.semaphore_signal(barrier, inc=1, device_id=device, device_id_type=MESH)

    for n in range(1, PLANES):
        device, _ = plane_shift(n)
        pl.semaphore_signal(barrier, inc=1, device_id=device, device_id_type=MESH)
    pl.semaphore_wait(barrier, GROUP - 1 + PLANES - 1)

    def result(k):
        device, _ = shifted(k, -1)
        return remote(prod_ref.at[k], back.at[k], c_send.at[k], c_recv.at[k], device)

    parts = ((dg_ref, gsum_ref, 256), (du_ref, usum_ref, 256), (dd_ref, dsum_ref, 128))

    def quarter(j, n):
        device, other = plane_shift(n)
        source, _, rows = parts[j]
        at = 3 * j + n - 1
        return remote(
            source.at[pl.ds(other * rows, rows)],
            y_in[j].at[n - 1],
            y1_send.at[at],
            y1_recv.at[at],
            device,
        )

    def summed_quarter(j, n):
        device, _ = plane_shift(n)
        _, total, rows = parts[j]
        at = 3 * j + n - 1
        mine = total.at[pl.ds(y * rows, rows)]
        return remote(mine, mine, y2_send.at[at], y2_recv.at[at], device)

    half = pl.ds(pl.multiple_of((1 - r) * HALF, HALF), HALF)
    sib_normed = remote(normed_ref.at[:, half], normed_sib, sib_send.at[0], sib_recv.at[0], sibling)
    sib_mixed = remote(mixed_ref.at[:, half], mixed_sib, sib_send.at[1], sib_recv.at[1], sibling)
    sib_branch = remote(branch_own, branch_sib, sib_send.at[2], sib_recv.at[2], sibling)
    sib_kv = remote(kv_out, kv_in, sib_send.at[3], sib_recv.at[3], sibling)
    sib_query = remote(
        grad_t.at[pl.ds(0, D)], grad_sib.at[pl.ds(0, D)], sib_send.at[4], sib_recv.at[4], sibling
    )
    sib_keyval = remote(
        grad_t.at[pl.ds(D, D)], grad_sib.at[pl.ds(D, D)], sib_send.at[5], sib_recv.at[5], sibling
    )

    sib_mixed.start()
    sib_normed.start()
    for n in range(1, PLANES):
        for j in range(3):
            quarter(j, n).start()

    @pl.loop(1, GROUP)
    def _(k):
        result(k).start()

    back[0] = prod_ref[0]

    gates = gates_ref[...]
    gdot = gdot_ref[...]
    logit_grad = gates * (gdot - jnp.sum(gates * gdot, axis=0, keepdims=True))
    high, rest = split_two(logit_grad)
    router_part = dot(high, routed_ref[...], ((1,), (0,)))
    router_part = router_part + dot(rest, routed_ref[...], ((1,), (0,)))
    routed_grad = dot(high, router_ref[...], ((0,), (0,)))
    routed_grad = routed_grad + dot(rest, router_ref[...], ((0,), (0,)))
    routed_grad = routed_grad + rg_ref[...]
    live = (
        r * tokens + lax.broadcasted_iota(jnp.int32, (tokens, 1), 0) < length_ref[0]
    ).astype(f32)
    middle = middle_ref[...]
    scale = lax.rsqrt(jnp.mean(middle * middle, axis=1, keepdims=True) + epsilon)
    rows = middle * scale
    moe_part = jnp.sum(routed_grad * rows, axis=0, keepdims=True)
    scaled = routed_grad * mgain_ref[...]
    inner = jnp.mean(scaled * rows, axis=1, keepdims=True)
    middle_grad = cot_ref[...].astype(f32) * live + scale * (scaled - rows * inner)
    hgrad_ref[...] = middle_grad
    branch_own[...] = middle_grad.astype(bf16)
    sib_branch.start()
    for j in range(8):
        part = slice(128 * j, 128 * j + 128)
        small_out[:, j, :] = router_part[:, part]
        small_out[:, 8 + j, :] = jnp.broadcast_to(moe_part[:, part], (GROUP, 128))

    def small(k):
        device, other = shifted(k, 1)
        return remote(small_out.at[other], small_in.at[me], sm_send.at[k], sm_recv.at[k], device)

    @pl.loop(1, GROUP)
    def _(k):
        small(k).start()

    small_in[me] = small_out[me]

    mg_t[...] = dot(w_ref[:, 2 * D : 3 * D], branch_own[...], ((1,), (1,))).astype(bf16)

    sib_mixed.wait_recv()
    sib_branch.wait_recv()
    mine = pl.ds(pl.multiple_of(r * HALF, HALF), HALF)

    def rows_part(q, at, first, width):
        device, other = chip_shift(q, 1)
        _, own = chip_shift(0, 1)
        return remote(
            weight_part.at[pl.ds(other * 32, 32), pl.ds(first, width)],
            weight_in.at[own, :, pl.ds(first, width)],
            rs_send.at[at * CHIPS + q],
            rs_recv.at[at * CHIPS + q],
            device,
        )

    pieces = ((2 * D, D), (0, D), (D, D))

    def send_part(at, left_own, left_sib, right_own, right_sib, contract):
        first, width = pieces[at]
        total = dot(left_own, right_own, ((0,), (contract,)))
        total = total + dot(left_sib, right_sib, ((0,), (contract,)))
        weight_part[:, first : first + width] = total.astype(bf16)

        @pl.loop(1, CHIPS)
        def _(q):
            rows_part(q, at, first, width).start()

        _, own = chip_shift(0, 1)
        weight_in[own, :, first : first + width] = weight_part[
            pl.ds(own * 32, 32), first : first + width
        ]

    def sum_part(at):
        first, width = pieces[at]

        @pl.loop(1, CHIPS)
        def _(q):
            rows_part(q, at, first, width).wait_recv()

        total = weight_in[0, :, first : first + width].astype(f32)
        for s in range(1, CHIPS):
            total = total + weight_in[s, :, first : first + width].astype(f32)
        y_out[:, first : first + width] = total.astype(bf16)
        y_parts[y, :, first : first + width] = total.astype(bf16)
        for n in range(1, PLANES):
            across(at, n).start()

    def across(at, n):
        first, width = pieces[at]
        device, _ = plane_shift(n)
        return remote(
            y_out.at[:, pl.ds(first, width)],
            y_parts.at[y, :, pl.ds(first, width)],
            ys_send.at[at * 3 + n - 1],
            ys_recv.at[at * 3 + n - 1],
            device,
        )

    send_part(0, mixed_ref[:, mine], mixed_sib[...], branch_own[...], branch_sib[...], 0)

    key_live = lax.broadcasted_iota(jnp.int32, (2 * tokens, 1), 0) < length_ref[0]
    score_scale = HEAD ** (-0.5)
    cosine, sine = cos_ref[...], sin_ref[...]

    def key_head(g):
        head = pl.ds(pl.multiple_of(g * HEAD, HEAD), HEAD)
        keys, values = k_ref[head, :], v_ref[head, :]
        key_sum, value_sum = None, None
        for j in range(2):
            at = pl.ds(pl.multiple_of((2 * g + j) * HEAD, HEAD), HEAD)
            query, mixed_grad = q_ref[at, :], mg_t[at, :]
            scores = dot(keys, query, ((0,), (0,))) * score_scale
            scores = jnp.where(key_live, scores, NEG)
            probs = jnp.exp(scores - lse_ref[pl.ds(2 * g + j, 1), :])
            prob_grad = dot(values, mixed_grad, ((0,), (0,)))
            value_part = dot(mixed_grad, probs.astype(bf16), ((1,), (1,)))
            inner = jnp.sum(probs * prob_grad, axis=0, keepdims=True)
            score_grad = (probs * (prob_grad - inner)).astype(bf16)
            key_part = dot(query, score_grad, ((1,), (1,)))
            query_grad = dot(keys, score_grad, ((1,), (0,))) * score_scale
            grad_t[at, :] = turned_back(query_grad, cosine, sine).astype(bf16)
            key_sum = key_part if key_sum is None else key_sum + key_part
            value_sum = value_part if value_sum is None else value_sum + value_part
        key_sum = key_sum * score_scale
        low = pl.ds(pl.multiple_of(g * HEAD, HEAD), HEAD)
        high = pl.ds(pl.multiple_of(HALF + g * HEAD, HEAD), HEAD)
        first = r == 0
        kv_own[low, :] = jnp.where(first, key_sum[:, :tokens], key_sum[:, tokens:])
        kv_own[high, :] = jnp.where(first, value_sum[:, :tokens], value_sum[:, tokens:])
        kv_out[low, :] = jnp.where(first, key_sum[:, tokens:], key_sum[:, :tokens]).astype(bf16)
        kv_out[high, :] = jnp.where(first, value_sum[:, tokens:], value_sum[:, :tokens]).astype(bf16)

    pl.loop(0, 4)(key_head)

    for j in range(3):
        source, total, rows_of = parts[j]
        mine_y = pl.ds(y * rows_of, rows_of)
        acc = source[mine_y, :].astype(f32)
        for n in range(1, PLANES):
            quarter(j, n).wait_recv()
        for n in range(1, PLANES):
            acc = acc + y_in[j][n - 1].astype(f32)
        total[mine_y, :] = acc.astype(bf16)
        for n in range(1, PLANES):
            summed_quarter(j, n).start()

    @pl.loop(1, GROUP)
    def _(k):
        small(k).wait_recv()

    def small_across(n):
        device, _ = plane_shift(n)
        return remote(
            small_y, small_y_in.at[y], sm_send.at[GROUP + n], sm_recv.at[GROUP + n], device
        )

    small_y[...] = jnp.sum(small_in[...], axis=0)
    small_y_in[y] = small_y[...]
    for n in range(1, PLANES):
        small_across(n).start()

    pl.loop(4, 8)(key_head)

    sib_kv.start()
    sib_query.start()

    for n in range(1, PLANES):
        small_across(n).wait_recv()
    totals = small_y_in[0] + small_y_in[1] + small_y_in[2] + small_y_in[3]
    mgain_out[...] = totals[8:16]
    router_all[me] = totals[0:8]

    def router_row(k):
        device, _ = shifted(k, 1)
        at = 2 * GROUP + k
        return remote(
            router_all.at[me], router_all.at[me], sm_send.at[at], sm_recv.at[at], device
        )

    @pl.loop(1, GROUP)
    def _(k):
        router_row(k).start()

    sib_normed.wait_recv()
    sib_query.wait_recv()
    send_part(1, normed_ref[:, mine], normed_sib[...], grad_t[0:D, :], grad_sib[0:D, :], 1)
    sib_kv.wait_recv()

    @pl.loop(0, 8)
    def _(g):
        low = pl.ds(pl.multiple_of(g * HEAD, HEAD), HEAD)
        total = kv_own[low, :] + kv_in[low, :].astype(f32)
        to = pl.ds(pl.multiple_of(D + g * HEAD, HEAD), HEAD)
        grad_t[to, :] = turned_back(total, cosine, sine).astype(bf16)

    grad_t[D + HALF : 2 * D, :] = (
        kv_own[HALF:D, :] + kv_in[HALF:D, :].astype(f32)
    ).astype(bf16)
    sib_keyval.start()
    normed_grad = dot(grad_t[0:D, :], w_ref[:, 0:D], ((0,), (1,)))
    sib_keyval.wait_recv()
    send_part(2, normed_ref[:, mine], normed_sib[...], grad_t[D:, :], grad_sib[D:, :], 1)
    normed_grad = normed_grad + dot(grad_t[D:, :], w_ref[:, D : 2 * D], ((0,), (1,)))

    inputs = hidden_ref[...].astype(f32)
    scale = lax.rsqrt(jnp.mean(inputs * inputs, axis=1, keepdims=True) + epsilon)
    rows = inputs * scale
    attn_part = jnp.sum(normed_grad * rows, axis=0, keepdims=True)
    for j in range(8):
        gain_out[j : j + 1, :] = attn_part[:, 128 * j : 128 * j + 128]

    def gain(k):
        device, _ = shifted(k, 1)
        at = 3 * GROUP + k
        return remote(gain_out, gain_in.at[me], sm_send.at[at], sm_recv.at[at], device)

    @pl.loop(1, GROUP)
    def _(k):
        gain(k).start()

    gain_in[me] = gain_out[...]
    scaled = normed_grad * again_ref[...]
    inner = jnp.mean(scaled * rows, axis=1, keepdims=True)
    hgrad_ref[...] += scale * (scaled - rows * inner)

    slot_iota = lax.broadcasted_iota(jnp.int32, (CAP, tokens), 0)

    def mix(c, total):
        chosen = []
        for i in range(SPAN):
            k = c * SPAN + i

            @pl.when(k != 0)
            def _():
                result(k).wait_recv()

            _, expert = shifted(k, 1)
            picked = slot_iota == pos_ref[pl.ds(expert, 1), :]
            chosen.append(jnp.where(picked, gates_ref[pl.ds(expert, 1), :], 0.0))
        high, rest = split_two(jnp.concatenate(chosen, axis=0))
        rows = back[pl.ds(c * SPAN, SPAN)].reshape(SPAN * CAP, D)
        total = total + dot(high, rows, ((0,), (0,)))
        return total + dot(rest, rows, ((0,), (0,)))

    mixture = lax.fori_loop(0, CHUNKS, mix, jnp.zeros((tokens, D), f32))
    hout_ref[...] = ((middle_ref[...] + mixture) * live).astype(bf16)

    for at in range(3):
        sum_part(at)

    @pl.loop(1, GROUP)
    def _(k):
        gain(k).wait_recv()

    gain_y[...] = jnp.sum(gain_in[...], axis=0)
    gain_y_in[y] = gain_y[...]

    def gain_across(n):
        device, _ = plane_shift(n)
        at = 4 * GROUP + n
        return remote(gain_y, gain_y_in.at[y], sm_send.at[at], sm_recv.at[at], device)

    for n in range(1, PLANES):
        gain_across(n).start()
    for at in range(3):
        for n in range(1, PLANES):
            across(at, n).wait_recv()
    own_out[...] = (y_parts[0].astype(f32) + y_parts[1].astype(f32)) + (
        y_parts[2].astype(f32) + y_parts[3].astype(f32)
    )
    for n in range(1, PLANES):
        gain_across(n).wait_recv()
    again_out[...] = (gain_y_in[0] + gain_y_in[1]) + (gain_y_in[2] + gain_y_in[3])

    @pl.loop(1, GROUP)
    def _(k):
        router_row(k).wait_recv()

    router_out[...] = router_all[...]

    @pl.loop(1, GROUP)
    def _(k):
        result(k).wait_send()
        small(k).wait_send()
        router_row(k).wait_send()
        gain(k).wait_send()

    for at in range(3):
        first, width = pieces[at]

        @pl.loop(1, CHIPS)
        def _(q):
            rows_part(q, at, first, width).wait_send()

    for n in range(1, PLANES):
        for j in range(3):
            quarter(j, n).wait_send()
            summed_quarter(j, n).wait()
            across(j, n).wait_send()
        small_across(n).wait_send()
        gain_across(n).wait_send()
    for copy in (sib_normed, sib_mixed, sib_branch, sib_kv, sib_query, sib_keyval):
        copy.wait_send()


def finish(length, *arrays):
    (prod, pos, gates, rg, gdot, dg, du, dd, routed) = arrays[:9]
    tokens = routed.shape[0]
    f32, bf16 = jnp.float32, jnp.bfloat16
    vmem = pl.BlockSpec(memory_space=pltpu.VMEM)
    shape = jax.ShapeDtypeStruct
    sems = pltpu.SemaphoreType.DMA
    scratch = [
        pltpu.VMEM((GROUP, CAP, D), bf16),
        [
            pltpu.VMEM((3, 256, 512), bf16),
            pltpu.VMEM((3, 256, 512), bf16),
            pltpu.VMEM((3, 128, 1024), bf16),
        ],
        pltpu.VMEM((tokens, D), bf16),
        pltpu.VMEM((tokens, D), bf16),
        pltpu.VMEM((tokens, HALF), bf16),
        pltpu.VMEM((tokens, HALF), bf16),
        pltpu.VMEM((D, tokens), bf16),
        pltpu.VMEM((2 * D, tokens), bf16),
        pltpu.VMEM((2 * D, tokens), bf16),
        pltpu.VMEM((D, tokens), f32),
        pltpu.VMEM((D, tokens), bf16),
        pltpu.VMEM((D, tokens), bf16),
        pltpu.VMEM((HALF, 3 * D), bf16),
        pltpu.VMEM((CHIPS, 32, 3 * D), bf16),
        pltpu.VMEM((32, 3 * D), bf16),
        pltpu.VMEM((PLANES, 32, 3 * D), bf16),
        pltpu.VMEM((GROUP, 16, 128), f32),
        pltpu.VMEM((GROUP, 16, 128), f32),
        pltpu.VMEM((16, 128), f32),
        pltpu.VMEM((PLANES, 16, 128), f32),
        pltpu.VMEM((8, 128), f32),
        pltpu.VMEM((GROUP, 8, 128), f32),
        pltpu.VMEM((8, 128), f32),
        pltpu.VMEM((PLANES, 8, 128), f32),
        pltpu.VMEM((GROUP, 8, 128), f32),
    ]
    for count in (GROUP, 9, 9, 6, 3 * CHIPS, 9, 5 * GROUP):
        scratch += [sems((count,)), sems((count,))]
    return pl.pallas_call(
        finish_kernel,
        out_shape=(
            shape((tokens, D), bf16),
            shape((tokens, D), f32),
            shape((8, 128), f32),
            shape((8, 128), f32),
            shape((GROUP, 8, 128), f32),
            shape((32, 3 * D), f32),
            shape(dg.shape, bf16),
            shape(du.shape, bf16),
            shape(dd.shape, bf16),
        ),
        in_specs=[pl.BlockSpec(memory_space=pltpu.SMEM)] + [vmem] * len(arrays),
        out_specs=[vmem] * 9,
        scratch_shapes=scratch,
        compiler_params=pltpu.CompilerParams(
            collective_id=2, has_side_effects=True, vmem_limit_bytes=60 << 20
        ),
        name="finish",
    )(length, *arrays)


def on_device(
    hidden_in,
    cotangent,
    lengths,
    routes,
    priority,
    attn_gain,
    query_weight,
    key_weight,
    value_weight,
    output_weight,
    moe_gain,
    router,
    gate_weight,
    up_weight,
    down_weight,
):
    row_total = lax.axis_size("row")
    tok_count = hidden_in.shape[0]
    seq_len = row_total * tok_count
    groups = HEADS // KV_HEADS
    kv_width = KV_HEADS * HEAD
    score_scale = HEAD ** (-0.5)
    positions = lax.axis_index("row") * tok_count + jnp.arange(tok_count, dtype=jnp.int32)
    seq_length = lengths[0]
    live_rows = positions < seq_length
    live_float = live_rows.astype(jnp.float32)[:, None]
    key_live = jnp.arange(seq_len) < seq_length
    expert_ids = jnp.arange(EXPERTS, dtype=jnp.int32)
    chosen = routes[:, :, None] == expert_ids[None, None, :]
    routed_to = jnp.any(chosen, axis=1)
    ranks = jnp.sum(jnp.where(chosen, priority.reshape(tok_count, TOP, 1), 0), axis=1)
    ranks = jnp.where(routed_to & live_rows[:, None], ranks, 1 << 20)
    ranks_et = ranks.T
    slots_et = jnp.sum((ranks_et[:, :, None] > ranks_et[:, None, :]).astype(jnp.int32), axis=2)
    pos_et = jnp.where((ranks_et < (1 << 20)) & (slots_et < CAP), slots_et, -1)
    onehot = (pos_et[:, None, :] == jnp.arange(CAP, dtype=jnp.int32)[None, :, None]).astype(
        jnp.bfloat16
    )
    onehot = onehot.reshape(EXPERTS * CAP, tok_count)
    outgoing_grad = jnp.dot(onehot, cotangent, preferred_element_type=jnp.float32)
    outgoing_grad = outgoing_grad.astype(jnp.bfloat16).reshape(EXPERTS, CAP, D)
    arrived_grad = lax.all_to_all(
        outgoing_grad, ("row", "col"), split_axis=0, concat_axis=0, tiled=True
    )
    inputs = hidden_in.astype(jnp.float32)
    scale_one = rms_scale(inputs)
    normed_one = inputs * scale_one
    normed = (normed_one * attn_gain).astype(jnp.bfloat16)
    w_query, w_key, w_value, w_out = sent_together(
        (query_weight, key_weight, value_weight, output_weight), ("row", "col"), 0, 1
    )
    query_pre = jnp.dot(normed, w_query, preferred_element_type=jnp.float32).reshape(
        tok_count, HEADS, HEAD
    )
    key_pre = jnp.dot(normed, w_key, preferred_element_type=jnp.float32).reshape(
        tok_count, KV_HEADS, HEAD
    )
    queries = (
        rotary(query_pre, positions, 1.0)
        .astype(jnp.bfloat16)
        .reshape(tok_count, KV_HEADS, groups, HEAD)
    )
    key_rows = rotary(key_pre, positions, 1.0).astype(jnp.bfloat16)
    values = (
        jnp.dot(normed, w_value, preferred_element_type=jnp.float32)
        .astype(jnp.bfloat16)
        .reshape(tok_count, KV_HEADS, HEAD)
    )
    all_keys, all_values = sent_together((key_rows, values), "row", 0, 1)

    def masked_scores():
        raw_scores = (
            jnp.einsum("tkgd,jkd->kgtj", queries, all_keys, preferred_element_type=jnp.float32)
            * score_scale
        )
        return jnp.where(key_live[None, None, None, :], raw_scores, -1000000000.0)

    scores = masked_scores()
    top_score = jnp.max(scores, axis=-1, keepdims=True)
    weights = jnp.exp(scores - top_score)
    totals = jnp.sum(weights, axis=-1, keepdims=True)
    log_total = top_score + jnp.log(totals)
    attn_probs = (weights / totals).astype(jnp.bfloat16)
    mixed_rows = jnp.einsum(
        "kgtj,jkd->tkgd", attn_probs, all_values, preferred_element_type=jnp.float32
    )
    mixed_rows = mixed_rows.reshape(tok_count, D).astype(jnp.bfloat16)
    middle = inputs + jnp.dot(mixed_rows, w_out, preferred_element_type=jnp.float32)
    scale_two = rms_scale(middle)
    normed_two = middle * scale_two
    routed = (normed_two * moe_gain).astype(jnp.bfloat16)
    logits = jnp.dot(routed, router, preferred_element_type=jnp.float32)
    picked = jnp.where(routed_to, logits, -jnp.inf)
    picked_exp = jnp.exp(picked - jnp.max(picked, axis=1, keepdims=True))
    gates_te = picked_exp / jnp.sum(picked_exp, axis=1, keepdims=True)
    gates_et = gates_te.T
    returned_rows, gate_dot_et, produced, gate_local, up_local, down_local = experts(
        routed, pos_et, gates_et, arrived_grad, gate_weight[0], up_weight[0], down_weight[0]
    )
    half_dim = HEAD // 2
    frequency = rotary_base ** (-jnp.arange(half_dim, dtype=jnp.float32) / half_dim)
    angles = frequency[:, None] * positions.astype(jnp.float32)[None, :]
    (
        hidden_out,
        hidden_grad,
        attn_gain_sum,
        moe_gain_sum,
        router_sum,
        own_rows,
        gate_sum,
        up_sum,
        down_sum,
    ) = finish(
        lengths,
        produced,
        pos_et,
        gates_et,
        returned_rows,
        gate_dot_et,
        gate_local,
        up_local,
        down_local,
        routed,
        router.T,
        middle,
        cotangent,
        hidden_in,
        attn_gain[None],
        moe_gain[None],
        normed,
        mixed_rows,
        jnp.concatenate([w_query, w_key, w_value, w_out], axis=1),
        queries.reshape(tok_count, D).T,
        all_keys.reshape(seq_len, kv_width).T,
        all_values.reshape(seq_len, kv_width).T,
        log_total.reshape(HEADS, tok_count),
        jnp.cos(angles),
        jnp.sin(angles),
    )
    return (
        hidden_out,
        hidden_grad,
        attn_gain_sum.reshape(D),
        own_rows[:, :D],
        own_rows[:, D : D + kv_width],
        own_rows[:, D + kv_width : 2 * D],
        own_rows[:, 2 * D :],
        moe_gain_sum.reshape(D),
        router_sum.reshape(EXPERTS, D).T,
        gate_sum.astype(jnp.float32)[None],
        up_sum.astype(jnp.float32)[None],
        down_sum.astype(jnp.float32)[None],
    )


def solution(mesh):
    return jax.shard_map(
        on_device,
        mesh=mesh,
        in_specs=(
            P(("dp", "col", "row"), None),
            P(("dp", "col", "row"), None),
            P(("dp", "col")),
            P(("dp", "col", "row"), None),
            P(("dp", "col", "row"), None),
            P(),
            P(("row", "col"), None),
            P(("row", "col"), None),
            P(("row", "col"), None),
            P(("row", "col"), None),
            P(),
            P(),
            P(("row", "col"), None, None),
            P(("row", "col"), None, None),
            P(("row", "col"), None, None),
        ),
        out_specs=(
            P(("dp", "col", "row"), None),
            P(("dp", "col", "row"), None),
            P(),
            P(("row", "col"), None),
            P(("row", "col"), None),
            P(("row", "col"), None),
            P(("row", "col"), None),
            P(),
            P(),
            P(("row", "col"), None, None),
            P(("row", "col"), None, None),
            P(("row", "col"), None, None),
        ),
        check_vma=False,
    )
```

```python
import jax
import jax.numpy as jnp
from jax import lax
from jax.experimental import pallas as pl
from jax.experimental.pallas import tpu as pltpu
from jax.sharding import PartitionSpec as P

D = 1024
HEADS = 16
HEAD = 64
KV_HEADS = 8
EXPERTS = 32
TOP = 8
CAP = 64


epsilon = 1e-05
rotary_base = 10000.0


MESH = pl.DeviceIdType.MESH
GROUP = 32
PLANES = 4
CHIPS = 16
HALF = D // 2
TOKENS = 256
NEG = -1000000000.0


def place():
    col = lax.axis_index("col")
    return lax.axis_index("dp"), lax.axis_index("row"), lax.rem(col, 4), col // 4


def moved(dx, dz, core):
    y, r, x, z = place()
    col = lax.rem(z + dz + 4, 4) * 4 + lax.rem(x + dx + 4, 4)
    return (y, core, col), core * CHIPS + col


def plane_shift(n):
    y, r, x, z = place()
    other = lax.rem(y + n, PLANES)
    return (other, r, z * 4 + x), other


def step_of(k, sign):
    y, r, x, z = place()
    return moved(sign * lax.rem(k, 4), sign * lax.rem(k // 4, 4), lax.rem(r + k // CHIPS, 2))


def remote(src, dst, send_sem, recv_sem, device):
    return pltpu.make_async_remote_copy(
        src_ref=src,
        dst_ref=dst,
        send_sem=send_sem,
        recv_sem=recv_sem,
        device_id=device,
        device_id_type=MESH,
    )


def meet(plane, planes):
    barrier = pltpu.get_barrier_semaphore()
    y, r, x, z = place()

    def greet(device):
        pl.semaphore_signal(barrier, inc=1, device_id=device, device_id_type=MESH)

    if plane:

        @pl.loop(1, GROUP)
        def _(k):
            greet(step_of(k, 1)[0])

        count = GROUP - 1
    else:
        for core in range(2):

            @pl.loop(1, 4)
            def _(d):
                greet(moved(d, 0, core)[0])
                greet(moved(0, d, core)[0])

        greet(moved(0, 0, 1 - r)[0])
        count = 13
    if planes:
        for n in range(1, PLANES):
            greet(plane_shift(n)[0])
        count += PLANES - 1
    pl.semaphore_wait(barrier, count)


def eye(n):
    return lax.broadcasted_iota(jnp.int32, (n, n), 0) == lax.broadcasted_iota(
        jnp.int32, (n, n), 1
    )


def as_row(column):
    return jnp.sum(jnp.where(eye(column.shape[0]), column, 0.0), axis=0, keepdims=True)


def as_column(row_vec):
    return jnp.sum(jnp.where(eye(row_vec.shape[1]), row_vec, 0.0), axis=1, keepdims=True)


def dot(a, b, dims):
    return lax.dot_general(a, b, (dims, ((), ())), preferred_element_type=jnp.float32)


def split_two(values):
    high = values.astype(jnp.bfloat16)
    return high, (values - high.astype(jnp.float32)).astype(jnp.bfloat16)


def picks(positions):
    slots = lax.broadcasted_iota(jnp.int32, (CAP, positions.shape[1]), 0)
    return slots == positions


def as_hot(mask):
    return mask.astype(jnp.float32).astype(jnp.bfloat16)


LEFT = pl.ds(0, HALF)
RIGHT = pl.ds(HALF, HALF)


def spread(d, source, tok_z, tok_x, send_sem, recv_sem):
    y, r, x, z = place()
    return (
        remote(
            source.at[:, LEFT], tok_z.at[d], send_sem.at[d], recv_sem.at[d], moved(0, d, r)[0]
        ),
        remote(
            source.at[:, RIGHT],
            tok_x.at[d],
            send_sem.at[4 + d],
            recv_sem.at[4 + d],
            moved(d, 0, r)[0],
        ),
    )


def slot_copies(out, into, core, there, dz, dx, send_sem, recv_sem, sign):
    y, r, x, z = place()
    at = there * CHIPS + dz * 4 + dx
    to = core * CHIPS + dz * 4 + dx
    return (
        lambda: remote(
            out.at[there, dz, dx, :, LEFT],
            into.at[core, dz, dx, :, LEFT],
            send_sem.at[at],
            recv_sem.at[to],
            moved(sign * dx, 0, there)[0],
        ),
        lambda: remote(
            out.at[there, dz, dx, :, RIGHT],
            into.at[core, dz, dx, :, RIGHT],
            send_sem.at[GROUP + at],
            recv_sem.at[GROUP + to],
            moved(0, sign * dz, there)[0],
        ),
    )


def is_local(core, offset):
    y, r, x, z = place()
    return (core == r) & (offset == 0)


def send_slots(out, into, there, dz, dx, send_sem, recv_sem, sign):
    y, r, x, z = place()
    left, right = slot_copies(out, into, r, there, dz, dx, send_sem, recv_sem, sign)

    @pl.when(jnp.logical_not(is_local(there, dx)))
    def _():
        left().start()

    @pl.when(is_local(there, dx))
    def _():
        into[r, dz, dx, :, 0:HALF] = out[there, dz, dx, :, 0:HALF]

    @pl.when(jnp.logical_not(is_local(there, dz)))
    def _():
        right().start()

    @pl.when(is_local(there, dz))
    def _():
        into[r, dz, dx, :, HALF:D] = out[there, dz, dx, :, HALF:D]


def slots_arrived(out, into, core, dz, dx, send_sem, recv_sem, left=True, right=True):
    copies = slot_copies(out, into, core, core, dz, dx, send_sem, recv_sem, 1)
    for copy, offset, wanted in zip(copies, (dx, dz), (left, right)):
        if wanted:

            @pl.when(jnp.logical_not(is_local(core, offset)))
            def _():
                copy().wait_recv()


def slots_sent(out, into, send_sem, recv_sem):
    @pl.loop(0, GROUP)
    def _(k):
        there, dz, dx = k // CHIPS, lax.rem(k // 4, 4), lax.rem(k, 4)
        copies = slot_copies(out, into, there, there, dz, dx, send_sem, recv_sem, 1)
        for copy, offset in zip(copies, (dx, dz)):

            @pl.when(jnp.logical_not(is_local(there, offset)))
            def _():
                copy().wait_send()


def line_rows(line, d, axis):
    y, r, x, z = place()
    own = x if axis == 0 else z
    return [
        line[d, pl.ds(core * 4 + lax.rem(own + i, 4), 1), :] for core in range(2) for i in range(4)
    ]


def line_hot(line, d, axis):
    return as_hot(jnp.concatenate([picks(p) for p in line_rows(line, d, axis)], axis=0))


def add_up(mid, line, d, axis):
    if axis == 0:
        rows = mid[:, d, :, :, 0:HALF]
    else:
        rows = mid[:, :, d, :, HALF:D]
    return dot(line_hot(line, d, axis), rows.reshape(8 * CAP, HALF), ((0,), (0,))).astype(
        jnp.bfloat16
    )


def part_copies(d, out, into, send_sem, recv_sem):
    y, r, x, z = place()
    return (
        lambda: remote(
            out.at[d, :, LEFT],
            into.at[d, :, LEFT],
            send_sem.at[d],
            recv_sem.at[d],
            moved(0, -d, r)[0],
        ),
        lambda: remote(
            out.at[d, :, RIGHT],
            into.at[d, :, RIGHT],
            send_sem.at[4 + d],
            recv_sem.at[4 + d],
            moved(-d, 0, r)[0],
        ),
    )


def fold_parts(out, into, mid, slots, slot_send, slot_recv, posz_ref, posx_ref, send_sem, recv_sem):
    @pl.loop(0, 4)
    def _(d):
        for core in range(2):
            for i in range(4):
                slots_arrived(slots, mid, core, d, i, slot_send, slot_recv, right=False)
        left = add_up(mid, posz_ref, d, 0)

        @pl.when(d == 0)
        def _():
            into[0, :, 0:HALF] = left

        @pl.when(d != 0)
        def _():
            out[d, :, 0:HALF] = left
            part_copies(d, out, into, send_sem, recv_sem)[0]().start()

        for core in range(2):
            for i in range(4):
                slots_arrived(slots, mid, core, i, d, slot_send, slot_recv, left=False)
        right = add_up(mid, posx_ref, d, 1)

        @pl.when(d == 0)
        def _():
            into[0, :, HALF:D] = right

        @pl.when(d != 0)
        def _():
            out[d, :, HALF:D] = right
            part_copies(d, out, into, send_sem, recv_sem)[1]().start()


def parts_arrived(out, into, send_sem, recv_sem):
    @pl.loop(1, 4)
    def _(d):
        for copy in part_copies(d, out, into, send_sem, recv_sem):
            copy().wait_recv()


def parts_sent(out, into, send_sem, recv_sem):
    @pl.loop(1, 4)
    def _(d):
        for copy in part_copies(d, out, into, send_sem, recv_sem):
            copy().wait_send()


def front_kernel(
    length_ref,
    hidden_ref,
    cot_ref,
    routes_ref,
    prio_ref,
    again_ref,
    mgain_ref,
    wq_ref,
    wk_ref,
    wv_ref,
    wo_ref,
    router_ref,
    cos_ref,
    sin_ref,
    w_ref,
    normed_ref,
    q_ref,
    k_ref,
    v_ref,
    lse_ref,
    mixed_ref,
    middle_ref,
    routed_ref,
    gates_ref,
    pos_ref,
    posz_ref,
    posx_ref,
    grads_ref,
    mixed_t,
    posz_out,
    posx_out,
    tok_z,
    tok_x,
    outgoing,
    w_send,
    w_recv,
    core_send,
    core_recv,
    kv_send,
    kv_recv,
    first_send,
    first_recv,
    slot_send,
    slot_recv,
    pos_send,
    pos_recv,
):
    y, r, x, z = place()
    f32, bf16 = jnp.float32, jnp.bfloat16
    sibling = moved(0, 0, 1 - r)[0]
    meet(False, False)

    w_ref[r, z, x, :, 0:D] = wq_ref[...]
    w_ref[r, z, x, :, D : D + HALF] = wk_ref[...]
    w_ref[r, z, x, :, D + HALF : 2 * D] = wv_ref[...]
    w_ref[r, z, x, :, 2 * D : 3 * D] = wo_ref[...]
    front, rear = pl.ds(0, D + HALF), pl.ds(D + HALF, D + HALF)

    def line_step(d):
        mine_q, mine_o = w_ref.at[r, z, x, :, front], w_ref.at[r, z, x, :, rear]
        return (
            remote(mine_q, mine_q, w_send.at[d], w_recv.at[d], moved(0, d, r)[0]),
            remote(mine_o, mine_o, w_send.at[4 + d], w_recv.at[4 + d], moved(d, 0, r)[0]),
        )

    def cross_step(e, d):
        at = 8 + 4 * e + d
        from_z = w_ref.at[r, lax.rem(z - e + 4, 4), x, :, front]
        from_x = w_ref.at[r, z, lax.rem(x - e + 4, 4), :, rear]
        return (
            remote(from_z, from_z, w_send.at[at], w_recv.at[at], moved(d, 0, r)[0]),
            remote(from_x, from_x, w_send.at[16 + at], w_recv.at[16 + at], moved(0, d, r)[0]),
        )

    def core_step(d):
        from_x = w_ref.at[r, :, lax.rem(x - d + 4, 4), :, front]
        from_z = w_ref.at[r, lax.rem(z - d + 4, 4), :, :, rear]
        return (
            remote(from_x, from_x, core_send.at[d], core_recv.at[d], sibling),
            remote(from_z, from_z, core_send.at[4 + d], core_recv.at[4 + d], sibling),
        )

    @pl.loop(1, 4)
    def _(d):
        for copy in line_step(d):
            copy.start()

    @pl.loop(1, 4)
    def _(d):
        for copy in cross_step(0, d):
            copy.start()

    tokens = hidden_ref.shape[0]
    experts_iota = lax.broadcasted_iota(jnp.int32, (EXPERTS, tokens), 0)
    live = r * tokens + lax.broadcasted_iota(jnp.int32, (1, tokens), 1) < length_ref[0]
    routed_to = jnp.zeros((EXPERTS, tokens), f32)
    ranks = jnp.zeros((EXPERTS, tokens), f32)
    for j in range(TOP):
        match = experts_iota == routes_ref[j : j + 1, :]
        routed_to = jnp.where(match, 1.0, routed_to)
        ranks = jnp.where(match, prio_ref[j : j + 1, :].astype(f32), ranks)
    far = float(1 << 20)
    ranks = jnp.where((routed_to > 0.0) & live, ranks, far)
    ranks_t = ranks.T
    rows = []
    for e in range(EXPERTS):
        earlier = ranks_t[:, e : e + 1] < ranks[e : e + 1, :]
        rows.append(jnp.sum(earlier.astype(f32), axis=0, keepdims=True))
    slots = jnp.concatenate(rows, axis=0)
    pos = jnp.where((ranks < far) & (slots < CAP), slots, -1.0).astype(jnp.int32)
    pos_ref[...] = pos
    for core in range(2):
        for i in range(4):
            at = core * CHIPS + 4 * i
            posz_out[i, 4 * core : 4 * core + 4, :] = pos[at : at + 4, :]
            for j in range(4):
                posx_out[j, 4 * core + i : 4 * core + i + 1, :] = pos[at + j : at + j + 1, :]
    posz_ref[0] = posz_out[z]
    posx_ref[0] = posx_out[x]
    tok_z[0] = cot_ref[:, 0:HALF]
    tok_x[0] = cot_ref[:, HALF:D]

    def pos_step(d):
        to_z, to_x = lax.rem(z + d, 4), lax.rem(x + d, 4)
        return (
            remote(
                posz_out.at[to_z],
                posz_ref.at[d],
                pos_send.at[d],
                pos_recv.at[d],
                moved(0, d, r)[0],
            ),
            remote(
                posx_out.at[to_x],
                posx_ref.at[d],
                pos_send.at[4 + d],
                pos_recv.at[4 + d],
                moved(d, 0, r)[0],
            ),
        )

    @pl.loop(1, 4)
    def _(d):
        for copy in pos_step(d):
            copy.start()

    @pl.loop(1, 4)
    def _(e):
        for copy in line_step(e):
            copy.wait_recv()

        @pl.loop(1, 4)
        def _(d):
            for copy in cross_step(e, d):
                copy.start()

    for copy in core_step(0):
        copy.start()

    inputs = hidden_ref[...].astype(f32)
    scale = lax.rsqrt(jnp.mean(inputs * inputs, axis=1, keepdims=True) + epsilon)
    normed_ref[...] = (inputs * scale * again_ref[...]).astype(bf16)

    @pl.loop(1, 4)
    def _(d):
        @pl.loop(0, 4)
        def _(e):
            for copy in cross_step(e, d):
                copy.wait_recv()

        for copy in core_step(d):
            copy.start()

    @pl.loop(1, 4)
    def _(d):
        for copy in spread(d, cot_ref, tok_z, tok_x, first_send, first_recv):
            copy.start()

    @pl.loop(0, 4)
    def _(d):
        for copy in core_step(d):
            copy.wait_recv()

    cosine, sine = cos_ref[...], sin_ref[...]
    here = pl.ds(pl.multiple_of(r * tokens, tokens), tokens)

    def projected(first):
        weight = w_ref[:, :, :, :, first : first + HALF].reshape(D, HALF)
        return dot(normed_ref[...], weight, ((1,), (0,))).T

    def turned(rows):
        parts = []
        for h in range(rows.shape[0] // HEAD):
            first, second = rows[HEAD * h : HEAD * h + 32], rows[HEAD * h + 32 : HEAD * h + HEAD]
            parts += [first * cosine - second * sine, second * cosine + first * sine]
        return jnp.concatenate(parts, axis=0).astype(bf16)

    key_copy = remote(
        k_ref.at[:, here], k_ref.at[:, here], kv_send.at[0], kv_recv.at[0], sibling
    )
    value_copy = remote(
        v_ref.at[:, here], v_ref.at[:, here], kv_send.at[1], kv_recv.at[1], sibling
    )
    k_ref[:, here] = turned(projected(D))
    key_copy.start()
    v_ref[:, here] = projected(D + HALF).astype(bf16)
    value_copy.start()
    q_ref[0:HALF, :] = turned(projected(0))
    q_ref[HALF:D, :] = turned(projected(HALF))

    @pl.loop(1, 4)
    def _(d):
        for copy in spread(d, cot_ref, tok_z, tok_x, first_send, first_recv):
            copy.wait_recv()
        for copy in pos_step(d):
            copy.wait_recv()

    @pl.loop(0, 4)
    def _(d):
        left = dot(line_hot(posz_ref, d, 0), tok_z[d], ((1,), (0,))).astype(bf16)
        right = dot(line_hot(posx_ref, d, 1), tok_x[d], ((1,), (0,))).astype(bf16)
        for core in range(2):
            for i in range(4):
                part = slice((core * 4 + i) * CAP, (core * 4 + i + 1) * CAP)
                outgoing[core, d, i, :, 0:HALF] = left[part]
                outgoing[core, i, d, :, HALF:D] = right[part]

    @pl.loop(0, CHIPS)
    def _(k):
        dx = lax.rem(k, 4)
        dz = lax.rem(dx + k // 4, 4)
        for core in range(2):
            send_slots(outgoing, grads_ref, core, dz, dx, slot_send, slot_recv, 1)

    key_copy.wait_recv()
    value_copy.wait_recv()

    key_live = lax.broadcasted_iota(jnp.int32, (2 * tokens, 1), 0) < length_ref[0]
    score_scale = HEAD ** (-0.5)

    @pl.loop(0, KV_HEADS)
    def _(g):
        head = pl.ds(pl.multiple_of(g * HEAD, HEAD), HEAD)
        keys, values = k_ref[head, :], v_ref[head, :]
        for j in range(2):
            at = pl.ds(pl.multiple_of((2 * g + j) * HEAD, HEAD), HEAD)
            scores = dot(keys, q_ref[at, :], ((0,), (0,))) * score_scale
            scores = jnp.where(key_live, scores, NEG)
            top = jnp.max(scores, axis=0, keepdims=True)
            weights = jnp.exp(scores - top)
            total = jnp.sum(weights, axis=0, keepdims=True)
            lse_ref[pl.ds(2 * g + j, 1), :] = top + jnp.log(total)
            probs = (weights * (1.0 / total)).astype(bf16)
            mixed_t[at, :] = dot(values, probs, ((1,), (0,))).astype(bf16)

    mixed_ref[...] = mixed_t[...].T
    w_out = w_ref[:, :, :, :, 2 * D : 3 * D].reshape(D, D)
    middle = hidden_ref[...].astype(f32) + dot(mixed_ref[...], w_out, ((1,), (0,)))
    middle_ref[...] = middle
    scale = lax.rsqrt(jnp.mean(middle * middle, axis=1, keepdims=True) + epsilon)
    routed_ref[...] = (middle * scale * mgain_ref[...]).astype(bf16)
    logits = dot(router_ref[...], routed_ref[...], ((1,), (1,)))
    logits = jnp.where(routed_to > 0.0, logits, -jnp.inf)
    picked = jnp.exp(logits - jnp.max(logits, axis=0, keepdims=True))
    gates_ref[...] = picked / jnp.sum(picked, axis=0, keepdims=True)

    @pl.loop(0, GROUP)
    def _(k):
        slots_arrived(
            outgoing,
            grads_ref,
            k // CHIPS,
            lax.rem(k // 4, 4),
            lax.rem(k, 4),
            slot_send,
            slot_recv,
        )

    slots_sent(outgoing, grads_ref, slot_send, slot_recv)

    @pl.loop(1, 4)
    def _(d):
        for copies in (
            line_step(d),
            core_step(d),
            pos_step(d),
            spread(d, cot_ref, tok_z, tok_x, first_send, first_recv),
        ):
            for copy in copies:
                copy.wait_send()

        @pl.loop(0, 4)
        def _(e):
            for copy in cross_step(e, d):
                copy.wait_send()

    for copy in core_step(0):
        copy.wait_send()
    key_copy.wait_send()
    value_copy.wait_send()


def front(length, *arrays):
    f32, bf16, i32 = jnp.float32, jnp.bfloat16, jnp.int32
    vmem = pl.BlockSpec(memory_space=pltpu.VMEM)
    shape = jax.ShapeDtypeStruct
    out_shape = (
        shape((2, 4, 4, 32, 3 * D), bf16),
        shape((TOKENS, D), bf16),
        shape((D, TOKENS), bf16),
        shape((HALF, 2 * TOKENS), bf16),
        shape((HALF, 2 * TOKENS), bf16),
        shape((HEADS, TOKENS), f32),
        shape((TOKENS, D), bf16),
        shape((TOKENS, D), f32),
        shape((TOKENS, D), bf16),
        shape((EXPERTS, TOKENS), f32),
        shape((EXPERTS, TOKENS), i32),
        shape((4, 8, TOKENS), i32),
        shape((4, 8, TOKENS), i32),
        shape((2, 4, 4, CAP, D), bf16),
    )
    scratch = [
        pltpu.VMEM((D, TOKENS), bf16),
        pltpu.VMEM((4, 8, TOKENS), i32),
        pltpu.VMEM((4, 8, TOKENS), i32),
        pltpu.VMEM((4, TOKENS, HALF), bf16),
        pltpu.VMEM((4, TOKENS, HALF), bf16),
        pltpu.VMEM((2, 4, 4, CAP, D), bf16),
    ]
    for count in (40, 8, 2, 8, 2 * GROUP, 8):
        scratch += [pltpu.SemaphoreType.DMA((count,))] * 2
    return pl.pallas_call(
        front_kernel,
        out_shape=out_shape,
        in_specs=[pl.BlockSpec(memory_space=pltpu.SMEM)] + [vmem] * len(arrays),
        out_specs=[vmem] * len(out_shape),
        scratch_shapes=scratch,
        compiler_params=pltpu.CompilerParams(
            collective_id=3, has_side_effects=True, vmem_limit_bytes=60 << 20
        ),
        name="front",
    )(length, *arrays)


def expert_kernel(
    routed_ref,
    pos_ref,
    posz_ref,
    posx_ref,
    gates_ref,
    grads_ref,
    wg_ref,
    wu_ref,
    wd_ref,
    rg_ref,
    gdot_ref,
    prod_ref,
    dg_ref,
    du_ref,
    dd_ref,
    tok_z,
    tok_x,
    outgoing,
    arrived,
    going_back,
    mid,
    parts_out,
    parts_in,
    gate_out,
    gate_in,
    dot_out,
    dot_in,
    active,
    weighted,
    pre_grads,
    first_send,
    first_recv,
    slot_send,
    slot_recv,
    back_send,
    back_recv,
    part_send,
    part_recv,
    small_send,
    small_recv,
):
    y, r, x, z = place()
    f32, bf16 = jnp.float32, jnp.bfloat16
    meet(True, False)

    @pl.loop(1, 4)
    def _(d):
        for copy in spread(d, routed_ref, tok_z, tok_x, first_send, first_recv):
            copy.start()

    tok_z[0] = routed_ref[:, 0:HALF]
    tok_x[0] = routed_ref[:, HALF:D]

    def small(k, out, into, sign, base, arriving=False):
        there, dz, dx = k // CHIPS, lax.rem(k // 4, 4), lax.rem(k, 4)
        slot = k if arriving else r * CHIPS + lax.rem(k, CHIPS)
        return remote(
            out.at[k],
            into.at[slot],
            small_send.at[base + k],
            small_recv.at[base + slot],
            moved(sign * dx, sign * dz, there)[0],
        )

    def own_slot(k):
        return k == r * CHIPS

    @pl.loop(0, GROUP)
    def _(k):
        there, dz, dx = k // CHIPS, lax.rem(k // 4, 4), lax.rem(k, 4)
        _, expert = moved(dx, dz, there)
        chosen = picks(pos_ref[pl.ds(expert, 1), :])
        gate_col = jnp.sum(
            jnp.where(chosen, gates_ref[pl.ds(expert, 1), :], 0.0), axis=1, keepdims=True
        )
        gate_out[k, 0:1, 0:CAP] = as_row(gate_col)

        @pl.when(own_slot(k))
        def _():
            gate_in[k] = gate_out[k]

        @pl.when(jnp.logical_not(own_slot(k)))
        def _():
            small(k, gate_out, gate_in, 1, 0).start()

    @pl.loop(1, 4)
    def _(d):
        for copy in spread(d, routed_ref, tok_z, tok_x, first_send, first_recv):
            copy.wait_recv()

    @pl.loop(0, 4)
    def _(g):
        for dx in range(4):
            dz = lax.rem(dx + g, 4)
            left_rows, right_rows = [], []
            for core in range(2):
                at_x = core * 4 + lax.rem(x + dx, 4)
                at_z = core * 4 + lax.rem(z + dz, 4)
                left_rows.append(picks(posz_ref[dz, pl.ds(at_x, 1), :]))
                right_rows.append(picks(posx_ref[dx, pl.ds(at_z, 1), :]))
            left = dot(as_hot(jnp.concatenate(left_rows, axis=0)), tok_z[dz], ((1,), (0,)))
            right = dot(as_hot(jnp.concatenate(right_rows, axis=0)), tok_x[dx], ((1,), (0,)))
            for core in range(2):
                part = slice(core * CAP, core * CAP + CAP)
                outgoing[core, dz, dx, :, 0:HALF] = left[part].astype(bf16)
                outgoing[core, dz, dx, :, HALF:D] = right[part].astype(bf16)
                send_slots(outgoing, arrived, core, dz, dx, slot_send, slot_recv, 1)

    @pl.loop(0, 8)
    def _(c):
        g, core = c // 2, lax.rem(c, 2)
        rows, gate_cols, grads = [], [], []
        for dx in range(4):
            dz = lax.rem(dx + g, 4)
            k = core * CHIPS + dz * 4 + dx
            slots_arrived(outgoing, arrived, core, dz, dx, slot_send, slot_recv)

            @pl.when(jnp.logical_not(own_slot(k)))
            def _():
                small(k, gate_out, gate_in, 1, 0, True).wait_recv()

            rows.append(arrived[core, dz, dx])
            gate_cols.append(as_column(gate_in[k, 0:1, 0:CAP]))
            grads.append(grads_ref[core, dz, dx])
        rows = jnp.concatenate(rows, axis=0)
        gate_cols = jnp.concatenate(gate_cols, axis=0)
        grads = jnp.concatenate(grads, axis=0).astype(f32)
        gate_pre = dot(rows, wg_ref[...], ((1,), (0,)))
        up_pre = dot(rows, wu_ref[...], ((1,), (0,)))
        gate_sig = jax.nn.sigmoid(gate_pre)
        gate_act = gate_pre * gate_sig
        act = (gate_act * up_pre).astype(bf16)
        produced = dot(act, wd_ref[...], ((1,), (0,))).astype(bf16).astype(f32)
        dots = jnp.sum(produced * grads, axis=1, keepdims=True)
        produced_grad = (gate_cols * grads).astype(bf16)
        act_grad = dot(produced_grad, wd_ref[...], ((1,), (1,))).astype(bf16).astype(f32)
        gate_grad = (
            act_grad * up_pre * gate_sig * (1.0 + gate_pre * (1.0 - gate_sig))
        ).astype(bf16)
        up_grad = (act_grad * gate_act).astype(bf16)
        row_grads = dot(gate_grad, wg_ref[...], ((1,), (1,)))
        row_grads = (row_grads + dot(up_grad, wu_ref[...], ((1,), (1,)))).astype(bf16)
        produced = (produced * gate_cols).astype(bf16)
        for dx in range(4):
            dz = lax.rem(dx + g, 4)
            k = core * CHIPS + dz * 4 + dx
            part = slice(dx * CAP, dx * CAP + CAP)
            going_back[core, dz, dx] = row_grads[part]
            send_slots(going_back, mid, core, dz, dx, back_send, back_recv, -1)
            dot_out[k, 0:1, 0:CAP] = as_row(dots[part])

            @pl.when(own_slot(k))
            def _():
                dot_in[k] = dot_out[k]

            @pl.when(jnp.logical_not(own_slot(k)))
            def _():
                small(k, dot_out, dot_in, -1, GROUP).start()

            prod_ref[core, dz, dx] = produced[part]
            active[core, dz, dx] = act[part]
            weighted[core, dz, dx] = produced_grad[part]
            pre_grads[core, dz, dx, :, 0:HALF] = gate_grad[part]
            pre_grads[core, dz, dx, :, HALF:D] = up_grad[part]

    all_rows = GROUP * CAP

    @pl.loop(0, 2)
    def _(n):
        span = pl.ds(pl.multiple_of(n * 256, 256), 256)
        left = active[:, :, :, :, span].reshape(all_rows, 256)
        right = weighted[...].reshape(all_rows, D)
        dd_ref[span, :] = dot(left, right, ((0,), (0,))).astype(bf16)

    fold_parts(
        parts_out,
        parts_in,
        mid,
        going_back,
        back_send,
        back_recv,
        posz_ref,
        posx_ref,
        part_send,
        part_recv,
    )

    @pl.loop(0, 4)
    def _(n):
        span = pl.ds(pl.multiple_of(n * 256, 256), 256)
        left = arrived[:, :, :, :, span].reshape(all_rows, 256)
        part = dot(left, pre_grads[...].reshape(all_rows, D), ((0,), (0,)))
        dg_ref[span, :] = part[:, 0:HALF].astype(bf16)
        du_ref[span, :] = part[:, HALF:D].astype(bf16)

    @pl.loop(0, GROUP)
    def _(k):
        @pl.when(jnp.logical_not(own_slot(k)))
        def _():
            small(k, dot_out, dot_in, -1, GROUP, True).wait_recv()

        there, dz, dx = k // CHIPS, lax.rem(k // 4, 4), lax.rem(k, 4)
        _, expert = moved(dx, dz, there)
        at = pl.ds(expert, 1)
        dots = as_column(dot_in[k, 0:1, 0:CAP])
        gdot_ref[at, :] = jnp.sum(
            jnp.where(picks(pos_ref[at, :]), dots, 0.0), axis=0, keepdims=True
        )

    parts_arrived(parts_out, parts_in, part_send, part_recv)
    rg_ref[...] = (parts_in[0].astype(f32) + parts_in[1].astype(f32)) + (
        parts_in[2].astype(f32) + parts_in[3].astype(f32)
    )
    slots_sent(outgoing, arrived, slot_send, slot_recv)
    slots_sent(going_back, mid, back_send, back_recv)
    parts_sent(parts_out, parts_in, part_send, part_recv)

    @pl.loop(1, 4)
    def _(d):
        for copy in spread(d, routed_ref, tok_z, tok_x, first_send, first_recv):
            copy.wait_send()

    @pl.loop(0, GROUP)
    def _(k):
        @pl.when(jnp.logical_not(own_slot(k)))
        def _():
            small(k, gate_out, gate_in, 1, 0).wait_send()
            small(k, dot_out, dot_in, -1, GROUP).wait_send()


def experts(*arrays):
    f32, bf16 = jnp.float32, jnp.bfloat16
    wg, wu, wd = arrays[-3:]
    vmem = pl.BlockSpec(memory_space=pltpu.VMEM)
    shape = jax.ShapeDtypeStruct
    block = pltpu.VMEM((2, 4, 4, CAP, D), bf16)
    narrow = pltpu.VMEM((2, 4, 4, CAP, HALF), bf16)
    line = pltpu.VMEM((4, TOKENS, HALF), bf16)
    wide = pltpu.VMEM((4, TOKENS, D), bf16)
    little = pltpu.VMEM((GROUP, 8, 128), f32)
    scratch = [line, line, block, block, block, block, wide, wide]
    scratch += [little] * 4 + [narrow, block, block]
    for count in (8, 2 * GROUP, 2 * GROUP, 8, 2 * GROUP):
        scratch += [pltpu.SemaphoreType.DMA((count,))] * 2
    out_shape = (
        shape((TOKENS, D), f32),
        shape((EXPERTS, TOKENS), f32),
        shape((2, 4, 4, CAP, D), bf16),
        shape(wg.shape, bf16),
        shape(wu.shape, bf16),
        shape(wd.shape, bf16),
    )
    return pl.pallas_call(
        expert_kernel,
        out_shape=out_shape,
        in_specs=[vmem] * len(arrays),
        out_specs=[vmem] * len(out_shape),
        scratch_shapes=scratch,
        compiler_params=pltpu.CompilerParams(
            collective_id=1, has_side_effects=True, vmem_limit_bytes=60 << 20
        ),
        name="experts",
    )(*arrays)


def chip_shift(q, sign):
    y, r, x, z = place()
    dx, dz = lax.rem(q, 4), lax.rem(lax.rem(q, 4) + q // 4, 4)
    col = lax.rem(z + sign * dz + 4, 4) * 4 + lax.rem(x + sign * dx + 4, 4)
    return (y, r, col), col


def turned_back(rows, cosine, sine):
    first, second = rows[0:32], rows[32:64]
    return jnp.concatenate(
        [first * cosine + second * sine, second * cosine - first * sine], axis=0
    )


def finish_kernel(
    length_ref,
    prod_ref,
    posz_ref,
    posx_ref,
    gates_ref,
    rg_ref,
    gdot_ref,
    dg_ref,
    du_ref,
    dd_ref,
    routed_ref,
    router_ref,
    middle_ref,
    cot_ref,
    hidden_ref,
    again_ref,
    mgain_ref,
    normed_ref,
    mixed_ref,
    w_ref,
    q_ref,
    k_ref,
    v_ref,
    lse_ref,
    cos_ref,
    sin_ref,
    hout_ref,
    hgrad_ref,
    again_out,
    mgain_out,
    router_out,
    own_out,
    gsum_ref,
    usum_ref,
    dsum_ref,
    mid,
    parts_out,
    parts_in,
    y_in,
    branch_own,
    branch_sib,
    normed_sib,
    mixed_sib,
    mg_t,
    grad_t,
    grad_sib,
    kv_own,
    kv_out,
    kv_in,
    weight_part,
    weight_in,
    y_out,
    y_parts,
    small_out,
    small_in,
    small_y,
    small_y_in,
    gain_out,
    gain_in,
    gain_y,
    gain_y_in,
    router_all,
    c_send,
    c_recv,
    part_send,
    part_recv,
    y1_send,
    y1_recv,
    y2_send,
    y2_recv,
    sib_send,
    sib_recv,
    rs_send,
    rs_recv,
    ys_send,
    ys_recv,
    sm_send,
    sm_recv,
):
    y, r, x, z = place()
    me = r * 16 + z * 4 + x
    sibling = (y, 1 - r, z * 4 + x)
    tokens = routed_ref.shape[0]
    f32, bf16 = jnp.float32, jnp.bfloat16

    meet(True, True)

    parts = ((dg_ref, gsum_ref, 256), (du_ref, usum_ref, 256), (dd_ref, dsum_ref, 128))

    def quarter(j, n):
        device, other = plane_shift(n)
        source, _, rows = parts[j]
        at = 3 * j + n - 1
        return remote(
            source.at[pl.ds(other * rows, rows)],
            y_in[j].at[n - 1],
            y1_send.at[at],
            y1_recv.at[at],
            device,
        )

    def summed_quarter(j, n):
        device, _ = plane_shift(n)
        _, total, rows = parts[j]
        at = 3 * j + n - 1
        mine = total.at[pl.ds(y * rows, rows)]
        return remote(mine, mine, y2_send.at[at], y2_recv.at[at], device)

    def weight(first, width):
        return w_ref[:, :, :, :, first : first + width].reshape(D, width)

    half = pl.ds(pl.multiple_of((1 - r) * HALF, HALF), HALF)
    sib_normed = remote(normed_ref.at[:, half], normed_sib, sib_send.at[0], sib_recv.at[0], sibling)
    sib_mixed = remote(mixed_ref.at[:, half], mixed_sib, sib_send.at[1], sib_recv.at[1], sibling)
    sib_branch = remote(branch_own, branch_sib, sib_send.at[2], sib_recv.at[2], sibling)
    sib_kv = remote(kv_out, kv_in, sib_send.at[3], sib_recv.at[3], sibling)
    sib_query = remote(
        grad_t.at[pl.ds(0, D)], grad_sib.at[pl.ds(0, D)], sib_send.at[4], sib_recv.at[4], sibling
    )
    sib_keyval = remote(
        grad_t.at[pl.ds(D, D)], grad_sib.at[pl.ds(D, D)], sib_send.at[5], sib_recv.at[5], sibling
    )

    sib_mixed.start()
    sib_normed.start()
    for n in range(1, PLANES):
        for j in range(3):
            quarter(j, n).start()

    @pl.loop(0, CHIPS)
    def _(k):
        dx = lax.rem(k, 4)
        dz = lax.rem(dx + k // 4, 4)
        for core in range(2):
            send_slots(prod_ref, mid, core, dz, dx, c_send, c_recv, -1)

    gates = gates_ref[...]
    gdot = gdot_ref[...]
    logit_grad = gates * (gdot - jnp.sum(gates * gdot, axis=0, keepdims=True))
    high, rest = split_two(logit_grad)
    router_part = dot(high, routed_ref[...], ((1,), (0,)))
    router_part = router_part + dot(rest, routed_ref[...], ((1,), (0,)))
    routed_grad = dot(high, router_ref[...], ((0,), (0,)))
    routed_grad = routed_grad + dot(rest, router_ref[...], ((0,), (0,)))
    routed_grad = routed_grad + rg_ref[...]
    live = (
        r * tokens + lax.broadcasted_iota(jnp.int32, (tokens, 1), 0) < length_ref[0]
    ).astype(f32)
    middle = middle_ref[...]
    scale = lax.rsqrt(jnp.mean(middle * middle, axis=1, keepdims=True) + epsilon)
    rows = middle * scale
    moe_part = jnp.sum(routed_grad * rows, axis=0, keepdims=True)
    scaled = routed_grad * mgain_ref[...]
    inner = jnp.mean(scaled * rows, axis=1, keepdims=True)
    middle_grad = cot_ref[...].astype(f32) * live + scale * (scaled - rows * inner)
    hgrad_ref[...] = middle_grad
    branch_own[...] = middle_grad.astype(bf16)
    sib_branch.start()
    for j in range(8):
        part = slice(128 * j, 128 * j + 128)
        small_out[:, j, :] = router_part[:, part]
        small_out[:, 8 + j, :] = jnp.broadcast_to(moe_part[:, part], (GROUP, 128))

    def small(k):
        device, other = step_of(k, 1)
        return remote(small_out.at[other], small_in.at[me], sm_send.at[k], sm_recv.at[k], device)

    @pl.loop(1, GROUP)
    def _(k):
        small(k).start()

    small_in[me] = small_out[me]

    mg_t[...] = dot(weight(2 * D, D), branch_own[...], ((1,), (1,))).astype(bf16)

    sib_mixed.wait_recv()
    sib_branch.wait_recv()
    mine = pl.ds(pl.multiple_of(r * HALF, HALF), HALF)

    def rows_part(q, at, first, width):
        device, other = chip_shift(q, 1)
        _, own = chip_shift(0, 1)
        return remote(
            weight_part.at[pl.ds(other * 32, 32), pl.ds(first, width)],
            weight_in.at[own, :, pl.ds(first, width)],
            rs_send.at[at * CHIPS + q],
            rs_recv.at[at * CHIPS + q],
            device,
        )

    pieces = ((2 * D, D), (0, D), (D, D))

    def send_part(at, left_own, left_sib, right_own, right_sib, contract):
        first, width = pieces[at]
        total = dot(left_own, right_own, ((0,), (contract,)))
        total = total + dot(left_sib, right_sib, ((0,), (contract,)))
        weight_part[:, first : first + width] = total.astype(bf16)

        @pl.loop(1, CHIPS)
        def _(q):
            rows_part(q, at, first, width).start()

        _, own = chip_shift(0, 1)
        weight_in[own, :, first : first + width] = weight_part[
            pl.ds(own * 32, 32), first : first + width
        ]

    def sum_part(at):
        first, width = pieces[at]

        @pl.loop(1, CHIPS)
        def _(q):
            rows_part(q, at, first, width).wait_recv()

        total = weight_in[0, :, first : first + width].astype(f32)
        for s in range(1, CHIPS):
            total = total + weight_in[s, :, first : first + width].astype(f32)
        y_out[:, first : first + width] = total.astype(bf16)
        y_parts[y, :, first : first + width] = total.astype(bf16)
        for n in range(1, PLANES):
            across(at, n).start()

    def across(at, n):
        first, width = pieces[at]
        device, _ = plane_shift(n)
        return remote(
            y_out.at[:, pl.ds(first, width)],
            y_parts.at[y, :, pl.ds(first, width)],
            ys_send.at[at * 3 + n - 1],
            ys_recv.at[at * 3 + n - 1],
            device,
        )

    send_part(0, mixed_ref[:, mine], mixed_sib[...], branch_own[...], branch_sib[...], 0)

    key_live = lax.broadcasted_iota(jnp.int32, (2 * tokens, 1), 0) < length_ref[0]
    score_scale = HEAD ** (-0.5)
    cosine, sine = cos_ref[...], sin_ref[...]

    def key_head(g):
        head = pl.ds(pl.multiple_of(g * HEAD, HEAD), HEAD)
        keys, values = k_ref[head, :], v_ref[head, :]
        key_sum, value_sum = None, None
        for j in range(2):
            at = pl.ds(pl.multiple_of((2 * g + j) * HEAD, HEAD), HEAD)
            query, mixed_grad = q_ref[at, :], mg_t[at, :]
            scores = dot(keys, query, ((0,), (0,))) * score_scale
            scores = jnp.where(key_live, scores, NEG)
            probs = jnp.exp(scores - lse_ref[pl.ds(2 * g + j, 1), :])
            prob_grad = dot(values, mixed_grad, ((0,), (0,)))
            value_part = dot(mixed_grad, probs.astype(bf16), ((1,), (1,)))
            inner = jnp.sum(probs * prob_grad, axis=0, keepdims=True)
            score_grad = (probs * (prob_grad - inner)).astype(bf16)
            key_part = dot(query, score_grad, ((1,), (1,)))
            query_grad = dot(keys, score_grad, ((1,), (0,))) * score_scale
            grad_t[at, :] = turned_back(query_grad, cosine, sine).astype(bf16)
            key_sum = key_part if key_sum is None else key_sum + key_part
            value_sum = value_part if value_sum is None else value_sum + value_part
        key_sum = key_sum * score_scale
        low = pl.ds(pl.multiple_of(g * HEAD, HEAD), HEAD)
        high = pl.ds(pl.multiple_of(HALF + g * HEAD, HEAD), HEAD)
        first = r == 0
        kv_own[low, :] = jnp.where(first, key_sum[:, :tokens], key_sum[:, tokens:])
        kv_own[high, :] = jnp.where(first, value_sum[:, :tokens], value_sum[:, tokens:])
        kv_out[low, :] = jnp.where(first, key_sum[:, tokens:], key_sum[:, :tokens]).astype(bf16)
        kv_out[high, :] = jnp.where(first, value_sum[:, tokens:], value_sum[:, :tokens]).astype(bf16)

    pl.loop(0, 4)(key_head)

    for j in range(3):
        source, total, rows_of = parts[j]
        mine_y = pl.ds(y * rows_of, rows_of)
        acc = source[mine_y, :].astype(f32)
        for n in range(1, PLANES):
            quarter(j, n).wait_recv()
        for n in range(1, PLANES):
            acc = acc + y_in[j][n - 1].astype(f32)
        total[mine_y, :] = acc.astype(bf16)
        for n in range(1, PLANES):
            summed_quarter(j, n).start()

    @pl.loop(1, GROUP)
    def _(k):
        small(k).wait_recv()

    def small_across(n):
        device, _ = plane_shift(n)
        return remote(
            small_y, small_y_in.at[y], sm_send.at[GROUP + n], sm_recv.at[GROUP + n], device
        )

    small_y[...] = jnp.sum(small_in[...], axis=0)
    small_y_in[y] = small_y[...]
    for n in range(1, PLANES):
        small_across(n).start()

    fold_parts(
        parts_out,
        parts_in,
        mid,
        prod_ref,
        c_send,
        c_recv,
        posz_ref,
        posx_ref,
        part_send,
        part_recv,
    )
    pl.loop(4, 8)(key_head)

    sib_kv.start()
    sib_query.start()

    for n in range(1, PLANES):
        small_across(n).wait_recv()
    totals = small_y_in[0] + small_y_in[1] + small_y_in[2] + small_y_in[3]
    mgain_out[...] = totals[8:16]
    router_all[me] = totals[0:8]

    def router_row(k):
        device, _ = step_of(k, 1)
        at = 2 * GROUP + k
        return remote(
            router_all.at[me], router_all.at[me], sm_send.at[at], sm_recv.at[at], device
        )

    @pl.loop(1, GROUP)
    def _(k):
        router_row(k).start()

    sib_normed.wait_recv()
    sib_query.wait_recv()
    send_part(1, normed_ref[:, mine], normed_sib[...], grad_t[0:D, :], grad_sib[0:D, :], 1)
    sib_kv.wait_recv()

    @pl.loop(0, 8)
    def _(g):
        low = pl.ds(pl.multiple_of(g * HEAD, HEAD), HEAD)
        total = kv_own[low, :] + kv_in[low, :].astype(f32)
        to = pl.ds(pl.multiple_of(D + g * HEAD, HEAD), HEAD)
        grad_t[to, :] = turned_back(total, cosine, sine).astype(bf16)

    grad_t[D + HALF : 2 * D, :] = (
        kv_own[HALF:D, :] + kv_in[HALF:D, :].astype(f32)
    ).astype(bf16)
    sib_keyval.start()
    normed_grad = dot(grad_t[0:D, :], weight(0, D), ((0,), (1,)))
    sib_keyval.wait_recv()
    send_part(2, normed_ref[:, mine], normed_sib[...], grad_t[D:, :], grad_sib[D:, :], 1)
    normed_grad = normed_grad + dot(grad_t[D:, :], weight(D, D), ((0,), (1,)))

    inputs = hidden_ref[...].astype(f32)
    scale = lax.rsqrt(jnp.mean(inputs * inputs, axis=1, keepdims=True) + epsilon)
    rows = inputs * scale
    attn_part = jnp.sum(normed_grad * rows, axis=0, keepdims=True)
    for j in range(8):
        gain_out[j : j + 1, :] = attn_part[:, 128 * j : 128 * j + 128]

    def gain(k):
        device, _ = step_of(k, 1)
        at = 3 * GROUP + k
        return remote(gain_out, gain_in.at[me], sm_send.at[at], sm_recv.at[at], device)

    @pl.loop(1, GROUP)
    def _(k):
        gain(k).start()

    gain_in[me] = gain_out[...]
    scaled = normed_grad * again_ref[...]
    inner = jnp.mean(scaled * rows, axis=1, keepdims=True)
    hgrad_ref[...] += scale * (scaled - rows * inner)

    parts_arrived(parts_out, parts_in, part_send, part_recv)
    mixture = (parts_in[0].astype(f32) + parts_in[1].astype(f32)) + (
        parts_in[2].astype(f32) + parts_in[3].astype(f32)
    )
    hout_ref[...] = ((middle_ref[...] + mixture) * live).astype(bf16)

    for at in range(3):
        sum_part(at)

    @pl.loop(1, GROUP)
    def _(k):
        gain(k).wait_recv()

    gain_y[...] = jnp.sum(gain_in[...], axis=0)
    gain_y_in[y] = gain_y[...]

    def gain_across(n):
        device, _ = plane_shift(n)
        at = 4 * GROUP + n
        return remote(gain_y, gain_y_in.at[y], sm_send.at[at], sm_recv.at[at], device)

    for n in range(1, PLANES):
        gain_across(n).start()
    for at in range(3):
        for n in range(1, PLANES):
            across(at, n).wait_recv()
    own_out[...] = (y_parts[0].astype(f32) + y_parts[1].astype(f32)) + (
        y_parts[2].astype(f32) + y_parts[3].astype(f32)
    )
    for n in range(1, PLANES):
        gain_across(n).wait_recv()
    again_out[...] = (gain_y_in[0] + gain_y_in[1]) + (gain_y_in[2] + gain_y_in[3])

    @pl.loop(1, GROUP)
    def _(k):
        router_row(k).wait_recv()

    router_out[...] = router_all[...]

    slots_sent(prod_ref, mid, c_send, c_recv)
    parts_sent(parts_out, parts_in, part_send, part_recv)

    @pl.loop(1, GROUP)
    def _(k):
        small(k).wait_send()
        router_row(k).wait_send()
        gain(k).wait_send()

    for at in range(3):
        first, width = pieces[at]

        @pl.loop(1, CHIPS)
        def _(q):
            rows_part(q, at, first, width).wait_send()

    for n in range(1, PLANES):
        for j in range(3):
            quarter(j, n).wait_send()
            summed_quarter(j, n).wait()
            across(j, n).wait_send()
        small_across(n).wait_send()
        gain_across(n).wait_send()
    for copy in (sib_normed, sib_mixed, sib_branch, sib_kv, sib_query, sib_keyval):
        copy.wait_send()


def finish(length, *arrays):
    dg, du, dd = arrays[6:9]
    tokens = TOKENS
    f32, bf16 = jnp.float32, jnp.bfloat16
    vmem = pl.BlockSpec(memory_space=pltpu.VMEM)
    shape = jax.ShapeDtypeStruct
    sems = pltpu.SemaphoreType.DMA
    scratch = [
        pltpu.VMEM((2, 4, 4, CAP, D), bf16),
        pltpu.VMEM((4, tokens, D), bf16),
        pltpu.VMEM((4, tokens, D), bf16),
        [
            pltpu.VMEM((3, 256, 512), bf16),
            pltpu.VMEM((3, 256, 512), bf16),
            pltpu.VMEM((3, 128, 1024), bf16),
        ],
        pltpu.VMEM((tokens, D), bf16),
        pltpu.VMEM((tokens, D), bf16),
        pltpu.VMEM((tokens, HALF), bf16),
        pltpu.VMEM((tokens, HALF), bf16),
        pltpu.VMEM((D, tokens), bf16),
        pltpu.VMEM((2 * D, tokens), bf16),
        pltpu.VMEM((2 * D, tokens), bf16),
        pltpu.VMEM((D, tokens), f32),
        pltpu.VMEM((D, tokens), bf16),
        pltpu.VMEM((D, tokens), bf16),
        pltpu.VMEM((HALF, 3 * D), bf16),
        pltpu.VMEM((CHIPS, 32, 3 * D), bf16),
        pltpu.VMEM((32, 3 * D), bf16),
        pltpu.VMEM((PLANES, 32, 3 * D), bf16),
        pltpu.VMEM((GROUP, 16, 128), f32),
        pltpu.VMEM((GROUP, 16, 128), f32),
        pltpu.VMEM((16, 128), f32),
        pltpu.VMEM((PLANES, 16, 128), f32),
        pltpu.VMEM((8, 128), f32),
        pltpu.VMEM((GROUP, 8, 128), f32),
        pltpu.VMEM((8, 128), f32),
        pltpu.VMEM((PLANES, 8, 128), f32),
        pltpu.VMEM((GROUP, 8, 128), f32),
    ]
    for count in (2 * GROUP, 8, 9, 9, 6, 3 * CHIPS, 9, 5 * GROUP):
        scratch += [sems((count,)), sems((count,))]
    return pl.pallas_call(
        finish_kernel,
        out_shape=(
            shape((tokens, D), bf16),
            shape((tokens, D), f32),
            shape((8, 128), f32),
            shape((8, 128), f32),
            shape((GROUP, 8, 128), f32),
            shape((32, 3 * D), f32),
            shape(dg.shape, bf16),
            shape(du.shape, bf16),
            shape(dd.shape, bf16),
        ),
        in_specs=[pl.BlockSpec(memory_space=pltpu.SMEM)] + [vmem] * len(arrays),
        out_specs=[vmem] * 9,
        scratch_shapes=scratch,
        compiler_params=pltpu.CompilerParams(
            collective_id=2, has_side_effects=True, vmem_limit_bytes=60 << 20
        ),
        name="finish",
    )(length, *arrays)


def on_device(
    hidden_in,
    cotangent,
    lengths,
    routes,
    priority,
    attn_gain,
    query_weight,
    key_weight,
    value_weight,
    output_weight,
    moe_gain,
    router,
    gate_weight,
    up_weight,
    down_weight,
):
    tok_count = hidden_in.shape[0]
    kv_width = KV_HEADS * HEAD
    positions = lax.axis_index("row") * tok_count + jnp.arange(tok_count, dtype=jnp.int32)
    half_dim = HEAD // 2
    frequency = rotary_base ** (-jnp.arange(half_dim, dtype=jnp.float32) / half_dim)
    angles = frequency[:, None] * positions.astype(jnp.float32)[None, :]
    cosine, sine = jnp.cos(angles), jnp.sin(angles)
    router_t = router.T
    (
        weights,
        normed,
        queries,
        keys,
        values,
        log_total,
        mixed_rows,
        middle,
        routed,
        gates,
        pos,
        posz,
        posx,
        arrived_grad,
    ) = front(
        lengths,
        hidden_in,
        cotangent,
        routes.T,
        priority.reshape(tok_count, TOP).T,
        attn_gain[None],
        moe_gain[None],
        query_weight,
        key_weight,
        value_weight,
        output_weight,
        router_t,
        cosine,
        sine,
    )
    returned_rows, gate_dot, produced, gate_local, up_local, down_local = experts(
        routed,
        pos,
        posz,
        posx,
        gates,
        arrived_grad,
        gate_weight[0],
        up_weight[0],
        down_weight[0],
    )
    (
        hidden_out,
        hidden_grad,
        attn_gain_sum,
        moe_gain_sum,
        router_sum,
        own_rows,
        gate_sum,
        up_sum,
        down_sum,
    ) = finish(
        lengths,
        produced,
        posz,
        posx,
        gates,
        returned_rows,
        gate_dot,
        gate_local,
        up_local,
        down_local,
        routed,
        router_t,
        middle,
        cotangent,
        hidden_in,
        attn_gain[None],
        moe_gain[None],
        normed,
        mixed_rows,
        weights,
        queries,
        keys,
        values,
        log_total,
        cosine,
        sine,
    )
    return (
        hidden_out,
        hidden_grad,
        attn_gain_sum.reshape(D),
        own_rows[:, :D],
        own_rows[:, D : D + kv_width],
        own_rows[:, D + kv_width : 2 * D],
        own_rows[:, 2 * D :],
        moe_gain_sum.reshape(D),
        router_sum.reshape(EXPERTS, D).T,
        gate_sum.astype(jnp.float32)[None],
        up_sum.astype(jnp.float32)[None],
        down_sum.astype(jnp.float32)[None],
    )


def solution(mesh):
    return jax.shard_map(
        on_device,
        mesh=mesh,
        in_specs=(
            P(("dp", "col", "row"), None),
            P(("dp", "col", "row"), None),
            P(("dp", "col")),
            P(("dp", "col", "row"), None),
            P(("dp", "col", "row"), None),
            P(),
            P(("row", "col"), None),
            P(("row", "col"), None),
            P(("row", "col"), None),
            P(("row", "col"), None),
            P(),
            P(),
            P(("row", "col"), None, None),
            P(("row", "col"), None, None),
            P(("row", "col"), None, None),
        ),
        out_specs=(
            P(("dp", "col", "row"), None),
            P(("dp", "col", "row"), None),
            P(),
            P(("row", "col"), None),
            P(("row", "col"), None),
            P(("row", "col"), None),
            P(("row", "col"), None),
            P(),
            P(),
            P(("row", "col"), None, None),
            P(("row", "col"), None, None),
            P(("row", "col"), None, None),
        ),
        check_vma=False,
    )
```

```python
import jax
import jax.numpy as jnp
from jax import lax
from jax.experimental import pallas as pl
from jax.experimental.pallas import tpu as pltpu
from jax.sharding import PartitionSpec as P

D = 1024
HEADS = 16
HEAD = 64
KV_HEADS = 8
EXPERTS = 32
TOP = 8
CAP = 64


epsilon = 1e-05
rotary_base = 10000.0


MESH = pl.DeviceIdType.MESH
GROUP = 32
PLANES = 4
CHIPS = 16
HALF = D // 2
TOKENS = 256
NEG = -1000000000.0


def place():
    col = lax.axis_index("col")
    return lax.axis_index("dp"), lax.axis_index("row"), lax.rem(col, 4), col // 4


def moved(dx, dz, core):
    y, r, x, z = place()
    col = lax.rem(z + dz + 4, 4) * 4 + lax.rem(x + dx + 4, 4)
    return (y, core, col), core * CHIPS + col


def plane_shift(n):
    y, r, x, z = place()
    other = lax.rem(y + n, PLANES)
    return (other, r, z * 4 + x), other


def step_of(k, sign):
    y, r, x, z = place()
    return moved(sign * lax.rem(k, 4), sign * lax.rem(k // 4, 4), lax.rem(r + k // CHIPS, 2))


def remote(src, dst, send_sem, recv_sem, device):
    return pltpu.make_async_remote_copy(
        src_ref=src,
        dst_ref=dst,
        send_sem=send_sem,
        recv_sem=recv_sem,
        device_id=device,
        device_id_type=MESH,
    )


def meet(plane, planes):
    barrier = pltpu.get_barrier_semaphore()
    y, r, x, z = place()

    def greet(device):
        pl.semaphore_signal(barrier, inc=1, device_id=device, device_id_type=MESH)

    if plane:

        @pl.loop(1, GROUP)
        def _(k):
            greet(step_of(k, 1)[0])

        count = GROUP - 1
    else:
        for core in range(2):

            @pl.loop(1, 4)
            def _(d):
                greet(moved(d, 0, core)[0])
                greet(moved(0, d, core)[0])

        greet(moved(0, 0, 1 - r)[0])
        count = 13
    if planes:
        for n in range(1, PLANES):
            greet(plane_shift(n)[0])
        count += PLANES - 1
    pl.semaphore_wait(barrier, count)


def eye(n):
    return lax.broadcasted_iota(jnp.int32, (n, n), 0) == lax.broadcasted_iota(
        jnp.int32, (n, n), 1
    )


def as_row(column):
    return jnp.sum(jnp.where(eye(column.shape[0]), column, 0.0), axis=0, keepdims=True)


def as_column(row_vec):
    return jnp.sum(jnp.where(eye(row_vec.shape[1]), row_vec, 0.0), axis=1, keepdims=True)


def dot(a, b, dims):
    return lax.dot_general(a, b, (dims, ((), ())), preferred_element_type=jnp.float32)


def split_two(values):
    high = values.astype(jnp.bfloat16)
    return high, (values - high.astype(jnp.float32)).astype(jnp.bfloat16)


def picks(positions):
    slots = lax.broadcasted_iota(jnp.int32, (CAP, positions.shape[1]), 0)
    return slots == positions


def as_hot(mask):
    return mask.astype(jnp.float32).astype(jnp.bfloat16)


LEFT = pl.ds(0, HALF)
RIGHT = pl.ds(HALF, HALF)


def spread(d, source, tok_z, tok_x, send_sem, recv_sem):
    y, r, x, z = place()
    return (
        remote(
            source.at[:, LEFT], tok_z.at[d], send_sem.at[d], recv_sem.at[d], moved(0, d, r)[0]
        ),
        remote(
            source.at[:, RIGHT],
            tok_x.at[d],
            send_sem.at[4 + d],
            recv_sem.at[4 + d],
            moved(d, 0, r)[0],
        ),
    )


def slot_copies(out, into, core, there, dz, dx, send_sem, recv_sem, sign):
    y, r, x, z = place()
    at = there * CHIPS + dz * 4 + dx
    to = core * CHIPS + dz * 4 + dx
    return (
        lambda: remote(
            out.at[there, dz, dx, :, LEFT],
            into.at[core, dz, dx, :, LEFT],
            send_sem.at[at],
            recv_sem.at[to],
            moved(sign * dx, 0, there)[0],
        ),
        lambda: remote(
            out.at[there, dz, dx, :, RIGHT],
            into.at[core, dz, dx, :, RIGHT],
            send_sem.at[GROUP + at],
            recv_sem.at[GROUP + to],
            moved(0, sign * dz, there)[0],
        ),
    )


def is_local(core, offset):
    y, r, x, z = place()
    return (core == r) & (offset == 0)


def send_slots(out, into, there, dz, dx, send_sem, recv_sem, sign, local_sem=None):
    y, r, x, z = place()

    def keep(cols):
        source, target = out.at[there, dz, dx, :, cols], into.at[r, dz, dx, :, cols]
        if local_sem is None:
            target[...] = source[...]
        else:
            copy = pltpu.make_async_copy(source, target, local_sem)
            copy.start()
            copy.wait()

    left, right = slot_copies(out, into, r, there, dz, dx, send_sem, recv_sem, sign)

    @pl.when(jnp.logical_not(is_local(there, dx)))
    def _():
        left().start()

    @pl.when(is_local(there, dx))
    def _():
        keep(LEFT)

    @pl.when(jnp.logical_not(is_local(there, dz)))
    def _():
        right().start()

    @pl.when(is_local(there, dz))
    def _():
        keep(RIGHT)


def slots_arrived(out, into, core, dz, dx, send_sem, recv_sem, left=True, right=True):
    copies = slot_copies(out, into, core, core, dz, dx, send_sem, recv_sem, 1)
    for copy, offset, wanted in zip(copies, (dx, dz), (left, right)):
        if wanted:

            @pl.when(jnp.logical_not(is_local(core, offset)))
            def _():
                copy().wait_recv()


def slots_sent(out, into, send_sem, recv_sem):
    @pl.loop(0, GROUP)
    def _(k):
        there, dz, dx = k // CHIPS, lax.rem(k // 4, 4), lax.rem(k, 4)
        copies = slot_copies(out, into, there, there, dz, dx, send_sem, recv_sem, 1)
        for copy, offset in zip(copies, (dx, dz)):

            @pl.when(jnp.logical_not(is_local(there, offset)))
            def _():
                copy().wait_send()


def line_rows(line, d, axis):
    y, r, x, z = place()
    own = x if axis == 0 else z
    return [
        line[d, pl.ds(core * 4 + lax.rem(own + i, 4), 1), :] for core in range(2) for i in range(4)
    ]


def line_hot(line, d, axis):
    return as_hot(jnp.concatenate([picks(p) for p in line_rows(line, d, axis)], axis=0))


def add_up(mid, line, d, axis):
    if axis == 0:
        rows = mid[:, d, :, :, 0:HALF]
    else:
        rows = mid[:, :, d, :, HALF:D]
    return dot(line_hot(line, d, axis), rows.reshape(8 * CAP, HALF), ((0,), (0,))).astype(
        jnp.bfloat16
    )


def part_copies(d, out, into, send_sem, recv_sem):
    y, r, x, z = place()
    return (
        lambda: remote(
            out.at[d, :, LEFT],
            into.at[d, :, LEFT],
            send_sem.at[d],
            recv_sem.at[d],
            moved(0, -d, r)[0],
        ),
        lambda: remote(
            out.at[d, :, RIGHT],
            into.at[d, :, RIGHT],
            send_sem.at[4 + d],
            recv_sem.at[4 + d],
            moved(-d, 0, r)[0],
        ),
    )


def fold_parts(out, into, mid, slots, slot_send, slot_recv, posz_ref, posx_ref, send_sem, recv_sem):
    @pl.loop(0, 4)
    def _(d):
        for core in range(2):
            for i in range(4):
                slots_arrived(slots, mid, core, d, i, slot_send, slot_recv, right=False)
        left = add_up(mid, posz_ref, d, 0)

        @pl.when(d == 0)
        def _():
            into[0, :, 0:HALF] = left

        @pl.when(d != 0)
        def _():
            out[d, :, 0:HALF] = left
            part_copies(d, out, into, send_sem, recv_sem)[0]().start()

        for core in range(2):
            for i in range(4):
                slots_arrived(slots, mid, core, i, d, slot_send, slot_recv, left=False)
        right = add_up(mid, posx_ref, d, 1)

        @pl.when(d == 0)
        def _():
            into[0, :, HALF:D] = right

        @pl.when(d != 0)
        def _():
            out[d, :, HALF:D] = right
            part_copies(d, out, into, send_sem, recv_sem)[1]().start()


def parts_arrived(out, into, send_sem, recv_sem):
    @pl.loop(1, 4)
    def _(d):
        for copy in part_copies(d, out, into, send_sem, recv_sem):
            copy().wait_recv()


def parts_sent(out, into, send_sem, recv_sem):
    @pl.loop(1, 4)
    def _(d):
        for copy in part_copies(d, out, into, send_sem, recv_sem):
            copy().wait_send()


def front_kernel(
    length_ref,
    hidden_ref,
    cot_ref,
    routes_ref,
    prio_ref,
    again_ref,
    mgain_ref,
    wq_ref,
    wk_ref,
    wv_ref,
    wo_ref,
    router_ref,
    cos_ref,
    sin_ref,
    w_ref,
    normed_ref,
    q_ref,
    k_ref,
    v_ref,
    lse_ref,
    mixed_ref,
    middle_ref,
    routed_ref,
    gates_ref,
    pos_ref,
    posz_ref,
    posx_ref,
    grads_ref,
    mixed_t,
    posz_out,
    posx_out,
    tok_z,
    tok_x,
    outgoing,
    w_send,
    w_recv,
    core_send,
    core_recv,
    kv_send,
    kv_recv,
    first_send,
    first_recv,
    slot_send,
    slot_recv,
    pos_send,
    pos_recv,
):
    y, r, x, z = place()
    f32, bf16 = jnp.float32, jnp.bfloat16
    sibling = moved(0, 0, 1 - r)[0]
    meet(False, False)

    for p in range(2):
        part = slice(256 * p, 256 * p + 256)
        w_ref[r, z, x, :, D * p : D * p + HALF] = wq_ref[:, HALF * p : HALF * p + HALF]
        w_ref[r, z, x, :, D * p + HALF : D * p + 768] = wk_ref[:, part]
        w_ref[r, z, x, :, D * p + 768 : D * p + D] = wv_ref[:, part]
    w_ref[r, z, x, :, 2 * D : 3 * D] = wo_ref[...]
    front, rear = pl.ds(0, D + HALF), pl.ds(D + HALF, D + HALF)

    def line_step(d):
        mine_q, mine_o = w_ref.at[r, z, x, :, front], w_ref.at[r, z, x, :, rear]
        return (
            remote(mine_q, mine_q, w_send.at[d], w_recv.at[d], moved(0, d, r)[0]),
            remote(mine_o, mine_o, w_send.at[4 + d], w_recv.at[4 + d], moved(d, 0, r)[0]),
        )

    def cross_step(e, d):
        at = 8 + 4 * e + d
        from_z = w_ref.at[r, lax.rem(z - e + 4, 4), x, :, front]
        from_x = w_ref.at[r, z, lax.rem(x - e + 4, 4), :, rear]
        return (
            remote(from_z, from_z, w_send.at[at], w_recv.at[at], moved(d, 0, r)[0]),
            remote(from_x, from_x, w_send.at[16 + at], w_recv.at[16 + at], moved(0, d, r)[0]),
        )

    def core_step(d):
        from_x = w_ref.at[r, :, lax.rem(x - d + 4, 4), :, front]
        from_z = w_ref.at[r, lax.rem(z - d + 4, 4), :, :, rear]
        return (
            remote(from_x, from_x, core_send.at[d], core_recv.at[d], sibling),
            remote(from_z, from_z, core_send.at[4 + d], core_recv.at[4 + d], sibling),
        )

    @pl.loop(1, 4)
    def _(d):
        for copy in line_step(d):
            copy.start()

    @pl.loop(1, 4)
    def _(d):
        for copy in cross_step(0, d):
            copy.start()

    tokens = hidden_ref.shape[0]
    experts_iota = lax.broadcasted_iota(jnp.int32, (EXPERTS, tokens), 0)
    live = r * tokens + lax.broadcasted_iota(jnp.int32, (1, tokens), 1) < length_ref[0]
    routed_to = jnp.zeros((EXPERTS, tokens), f32)
    ranks = jnp.zeros((EXPERTS, tokens), f32)
    for j in range(TOP):
        match = experts_iota == routes_ref[j : j + 1, :]
        routed_to = jnp.where(match, 1.0, routed_to)
        ranks = jnp.where(match, prio_ref[j : j + 1, :].astype(f32), ranks)
    far = float(1 << 20)
    ranks = jnp.where((routed_to > 0.0) & live, ranks, far)
    ranks_t = ranks.T
    rows = []
    for e in range(EXPERTS):
        earlier = ranks_t[:, e : e + 1] < ranks[e : e + 1, :]
        rows.append(jnp.sum(earlier.astype(f32), axis=0, keepdims=True))
    slots = jnp.concatenate(rows, axis=0)
    pos = jnp.where((ranks < far) & (slots < CAP), slots, -1.0).astype(jnp.int32)
    pos_ref[...] = pos
    for core in range(2):
        for i in range(4):
            at = core * CHIPS + 4 * i
            posz_out[i, 4 * core : 4 * core + 4, :] = pos[at : at + 4, :]
            for j in range(4):
                posx_out[j, 4 * core + i : 4 * core + i + 1, :] = pos[at + j : at + j + 1, :]
    posz_ref[0] = posz_out[z]
    posx_ref[0] = posx_out[x]
    tok_z[0] = cot_ref[:, 0:HALF]
    tok_x[0] = cot_ref[:, HALF:D]

    def pos_step(d):
        to_z, to_x = lax.rem(z + d, 4), lax.rem(x + d, 4)
        return (
            remote(
                posz_out.at[to_z],
                posz_ref.at[d],
                pos_send.at[d],
                pos_recv.at[d],
                moved(0, d, r)[0],
            ),
            remote(
                posx_out.at[to_x],
                posx_ref.at[d],
                pos_send.at[4 + d],
                pos_recv.at[4 + d],
                moved(d, 0, r)[0],
            ),
        )

    @pl.loop(1, 4)
    def _(d):
        for copy in pos_step(d):
            copy.start()

    @pl.loop(1, 4)
    def _(e):
        for copy in line_step(e):
            copy.wait_recv()

        @pl.loop(1, 4)
        def _(d):
            for copy in cross_step(e, d):
                copy.start()

    @pl.loop(1, 4)
    def _(d):
        for copy in spread(d, cot_ref, tok_z, tok_x, first_send, first_recv):
            copy.start()

    for copy in core_step(0):
        copy.start()

    inputs = hidden_ref[...].astype(f32)
    scale = lax.rsqrt(jnp.mean(inputs * inputs, axis=1, keepdims=True) + epsilon)
    normed_ref[...] = (inputs * scale * again_ref[...]).astype(bf16)

    @pl.loop(1, 4)
    def _(d):
        for copy in spread(d, cot_ref, tok_z, tok_x, first_send, first_recv):
            copy.wait_recv()
        for copy in pos_step(d):
            copy.wait_recv()

    @pl.loop(0, 4)
    def _(d):
        left = dot(line_hot(posz_ref, d, 0), tok_z[d], ((1,), (0,))).astype(bf16)
        right = dot(line_hot(posx_ref, d, 1), tok_x[d], ((1,), (0,))).astype(bf16)
        for core in range(2):
            for i in range(4):
                part = slice((core * 4 + i) * CAP, (core * 4 + i + 1) * CAP)
                outgoing[core, d, i, :, 0:HALF] = left[part]
                outgoing[core, i, d, :, HALF:D] = right[part]

    @pl.loop(1, 4)
    def _(d):
        @pl.loop(0, 4)
        def _(e):
            for copy in cross_step(e, d):
                copy.wait_recv()

        for copy in core_step(d):
            copy.start()

    @pl.loop(0, CHIPS)
    def _(k):
        dx = lax.rem(k, 4)
        dz = lax.rem(dx + k // 4, 4)
        for core in range(2):
            send_slots(outgoing, grads_ref, core, dz, dx, slot_send, slot_recv, 1)

    @pl.loop(0, 4)
    def _(d):
        for copy in core_step(d):
            copy.wait_recv()

    cosine, sine = cos_ref[...], sin_ref[...]
    here = pl.ds(pl.multiple_of(r * tokens, tokens), tokens)

    def projected(first):
        weight = w_ref[:, :, :, :, first : first + HALF].reshape(D, HALF)
        return dot(normed_ref[...], weight, ((1,), (0,))).T

    def turned(rows):
        parts = []
        for h in range(rows.shape[0] // HEAD):
            first, second = rows[HEAD * h : HEAD * h + 32], rows[HEAD * h + 32 : HEAD * h + HEAD]
            parts += [first * cosine - second * sine, second * cosine + first * sine]
        return jnp.concatenate(parts, axis=0).astype(bf16)

    key_copy = remote(
        k_ref.at[:, here], k_ref.at[:, here], kv_send.at[0], kv_recv.at[0], sibling
    )
    value_copy = remote(
        v_ref.at[:, here], v_ref.at[:, here], kv_send.at[1], kv_recv.at[1], sibling
    )
    for p in range(2):
        both = projected(D * p + HALF)
        k_ref[256 * p : 256 * p + 256, here] = turned(both[0:256])
        v_ref[256 * p : 256 * p + 256, here] = both[256:512].astype(bf16)
    key_copy.start()
    value_copy.start()
    for p in range(2):
        q_ref[HALF * p : HALF * p + HALF, :] = turned(projected(D * p))

    key_copy.wait_recv()
    value_copy.wait_recv()

    key_live = lax.broadcasted_iota(jnp.int32, (2 * tokens, 1), 0) < length_ref[0]
    score_scale = HEAD ** (-0.5)

    @pl.loop(0, KV_HEADS)
    def _(g):
        head = pl.ds(pl.multiple_of(g * HEAD, HEAD), HEAD)
        keys, values = k_ref[head, :], v_ref[head, :]
        for j in range(2):
            at = pl.ds(pl.multiple_of((2 * g + j) * HEAD, HEAD), HEAD)
            scores = dot(keys, q_ref[at, :], ((0,), (0,))) * score_scale
            scores = jnp.where(key_live, scores, NEG)
            top = jnp.max(scores, axis=0, keepdims=True)
            weights = jnp.exp(scores - top)
            total = jnp.sum(weights, axis=0, keepdims=True)
            lse_ref[pl.ds(2 * g + j, 1), :] = top + jnp.log(total)
            probs = (weights * (1.0 / total)).astype(bf16)
            mixed_t[at, :] = dot(values, probs, ((1,), (0,))).astype(bf16)

    mixed_ref[...] = mixed_t[...].T
    w_out = w_ref[:, :, :, :, 2 * D : 3 * D].reshape(D, D)
    middle = hidden_ref[...].astype(f32) + dot(mixed_ref[...], w_out, ((1,), (0,)))
    middle_ref[...] = middle
    scale = lax.rsqrt(jnp.mean(middle * middle, axis=1, keepdims=True) + epsilon)
    routed_ref[...] = (middle * scale * mgain_ref[...]).astype(bf16)
    logits = dot(router_ref[...], routed_ref[...], ((1,), (1,)))
    logits = jnp.where(routed_to > 0.0, logits, -jnp.inf)
    picked = jnp.exp(logits - jnp.max(logits, axis=0, keepdims=True))
    gates_ref[...] = picked / jnp.sum(picked, axis=0, keepdims=True)

    @pl.loop(0, GROUP)
    def _(k):
        slots_arrived(
            outgoing,
            grads_ref,
            k // CHIPS,
            lax.rem(k // 4, 4),
            lax.rem(k, 4),
            slot_send,
            slot_recv,
        )

    slots_sent(outgoing, grads_ref, slot_send, slot_recv)

    @pl.loop(1, 4)
    def _(d):
        for copies in (
            line_step(d),
            core_step(d),
            pos_step(d),
            spread(d, cot_ref, tok_z, tok_x, first_send, first_recv),
        ):
            for copy in copies:
                copy.wait_send()

        @pl.loop(0, 4)
        def _(e):
            for copy in cross_step(e, d):
                copy.wait_send()

    for copy in core_step(0):
        copy.wait_send()
    key_copy.wait_send()
    value_copy.wait_send()


def front(length, *arrays):
    f32, bf16, i32 = jnp.float32, jnp.bfloat16, jnp.int32
    vmem = pl.BlockSpec(memory_space=pltpu.VMEM)
    shape = jax.ShapeDtypeStruct
    out_shape = (
        shape((2, 4, 4, 32, 3 * D), bf16),
        shape((TOKENS, D), bf16),
        shape((D, TOKENS), bf16),
        shape((HALF, 2 * TOKENS), bf16),
        shape((HALF, 2 * TOKENS), bf16),
        shape((HEADS, TOKENS), f32),
        shape((TOKENS, D), bf16),
        shape((TOKENS, D), f32),
        shape((TOKENS, D), bf16),
        shape((EXPERTS, TOKENS), f32),
        shape((EXPERTS, TOKENS), i32),
        shape((4, 8, TOKENS), i32),
        shape((4, 8, TOKENS), i32),
        shape((2, 4, 4, CAP, D), bf16),
    )
    scratch = [
        pltpu.VMEM((D, TOKENS), bf16),
        pltpu.VMEM((4, 8, TOKENS), i32),
        pltpu.VMEM((4, 8, TOKENS), i32),
        pltpu.VMEM((4, TOKENS, HALF), bf16),
        pltpu.VMEM((4, TOKENS, HALF), bf16),
        pltpu.VMEM((2, 4, 4, CAP, D), bf16),
    ]
    for count in (40, 8, 2, 8, 2 * GROUP, 8):
        scratch += [pltpu.SemaphoreType.DMA((count,))] * 2
    return pl.pallas_call(
        front_kernel,
        out_shape=out_shape,
        in_specs=[pl.BlockSpec(memory_space=pltpu.SMEM)] + [vmem] * len(arrays),
        out_specs=[vmem] * len(out_shape),
        scratch_shapes=scratch,
        compiler_params=pltpu.CompilerParams(
            collective_id=3, has_side_effects=True, vmem_limit_bytes=60 << 20
        ),
        name="front",
    )(length, *arrays)


def expert_kernel(
    routed_ref,
    pos_ref,
    posz_ref,
    posx_ref,
    gates_ref,
    grads_ref,
    wg_ref,
    wu_ref,
    wd_ref,
    rg_ref,
    gdot_ref,
    prod_ref,
    grad_ref,
    tok_z,
    tok_x,
    outgoing,
    arrived,
    going_back,
    mid,
    parts_out,
    parts_in,
    gate_out,
    gate_in,
    dot_out,
    dot_in,
    active,
    weighted,
    pre_grads,
    first_send,
    first_recv,
    slot_send,
    slot_recv,
    back_send,
    back_recv,
    part_send,
    part_recv,
    small_send,
    small_recv,
):
    y, r, x, z = place()
    f32, bf16 = jnp.float32, jnp.bfloat16
    meet(True, False)

    @pl.loop(1, 4)
    def _(d):
        for copy in spread(d, routed_ref, tok_z, tok_x, first_send, first_recv):
            copy.start()

    tok_z[0] = routed_ref[:, 0:HALF]
    tok_x[0] = routed_ref[:, HALF:D]

    def small(k, out, into, sign, base, arriving=False):
        there, dz, dx = k // CHIPS, lax.rem(k // 4, 4), lax.rem(k, 4)
        slot = k if arriving else r * CHIPS + lax.rem(k, CHIPS)
        return remote(
            out.at[k],
            into.at[slot],
            small_send.at[base + k],
            small_recv.at[base + slot],
            moved(sign * dx, sign * dz, there)[0],
        )

    def own_slot(k):
        return k == r * CHIPS

    @pl.loop(0, GROUP)
    def _(k):
        there, dz, dx = k // CHIPS, lax.rem(k // 4, 4), lax.rem(k, 4)
        _, expert = moved(dx, dz, there)
        chosen = picks(pos_ref[pl.ds(expert, 1), :])
        gate_col = jnp.sum(
            jnp.where(chosen, gates_ref[pl.ds(expert, 1), :], 0.0), axis=1, keepdims=True
        )
        gate_out[k, 0:1, 0:CAP] = as_row(gate_col)

        @pl.when(own_slot(k))
        def _():
            gate_in[k] = gate_out[k]

        @pl.when(jnp.logical_not(own_slot(k)))
        def _():
            small(k, gate_out, gate_in, 1, 0).start()

    @pl.loop(1, 4)
    def _(d):
        for copy in spread(d, routed_ref, tok_z, tok_x, first_send, first_recv):
            copy.wait_recv()

    @pl.loop(0, 4)
    def _(g):
        for dx in range(4):
            dz = lax.rem(dx + g, 4)
            left_rows, right_rows = [], []
            for core in range(2):
                at_x = core * 4 + lax.rem(x + dx, 4)
                at_z = core * 4 + lax.rem(z + dz, 4)
                left_rows.append(picks(posz_ref[dz, pl.ds(at_x, 1), :]))
                right_rows.append(picks(posx_ref[dx, pl.ds(at_z, 1), :]))
            left = dot(as_hot(jnp.concatenate(left_rows, axis=0)), tok_z[dz], ((1,), (0,)))
            right = dot(as_hot(jnp.concatenate(right_rows, axis=0)), tok_x[dx], ((1,), (0,)))
            for core in range(2):
                part = slice(core * CAP, core * CAP + CAP)
                outgoing[core, dz, dx, :, 0:HALF] = left[part].astype(bf16)
                outgoing[core, dz, dx, :, HALF:D] = right[part].astype(bf16)
                send_slots(outgoing, arrived, core, dz, dx, slot_send, slot_recv, 1)

    @pl.loop(0, 8)
    def _(c):
        g, core = c // 2, lax.rem(c, 2)
        rows, gate_cols, grads = [], [], []
        for dx in range(4):
            dz = lax.rem(dx + g, 4)
            k = core * CHIPS + dz * 4 + dx
            slots_arrived(outgoing, arrived, core, dz, dx, slot_send, slot_recv)

            @pl.when(jnp.logical_not(own_slot(k)))
            def _():
                small(k, gate_out, gate_in, 1, 0, True).wait_recv()

            rows.append(arrived[core, dz, dx])
            gate_cols.append(as_column(gate_in[k, 0:1, 0:CAP]))
            grads.append(grads_ref[core, dz, dx])
        rows = jnp.concatenate(rows, axis=0)
        gate_cols = jnp.concatenate(gate_cols, axis=0)
        grads = jnp.concatenate(grads, axis=0).astype(f32)
        gate_pre = dot(rows, wg_ref[...], ((1,), (0,)))
        up_pre = dot(rows, wu_ref[...], ((1,), (0,)))
        gate_sig = jax.nn.sigmoid(gate_pre)
        gate_act = gate_pre * gate_sig
        act = (gate_act * up_pre).astype(bf16)
        produced = dot(act, wd_ref[...], ((1,), (0,))).astype(bf16).astype(f32)
        dots = jnp.sum(produced * grads, axis=1, keepdims=True)
        produced_grad = (gate_cols * grads).astype(bf16)
        act_grad = dot(produced_grad, wd_ref[...], ((1,), (1,))).astype(bf16).astype(f32)
        gate_grad = (
            act_grad * up_pre * gate_sig * (1.0 + gate_pre * (1.0 - gate_sig))
        ).astype(bf16)
        up_grad = (act_grad * gate_act).astype(bf16)
        row_grads = dot(gate_grad, wg_ref[...], ((1,), (1,)))
        row_grads = (row_grads + dot(up_grad, wu_ref[...], ((1,), (1,)))).astype(bf16)
        produced = (produced * gate_cols).astype(bf16)
        for dx in range(4):
            dz = lax.rem(dx + g, 4)
            k = core * CHIPS + dz * 4 + dx
            part = slice(dx * CAP, dx * CAP + CAP)
            going_back[core, dz, dx] = row_grads[part]
            send_slots(going_back, mid, core, dz, dx, back_send, back_recv, -1)
            dot_out[k, 0:1, 0:CAP] = as_row(dots[part])

            @pl.when(own_slot(k))
            def _():
                dot_in[k] = dot_out[k]

            @pl.when(jnp.logical_not(own_slot(k)))
            def _():
                small(k, dot_out, dot_in, -1, GROUP).start()

            prod_ref[core, dz, dx] = produced[part]
            active[core, dz, dx] = act[part]
            weighted[core, dz, dx] = produced_grad[part]
            pre_grads[core, dz, dx, :, 0:HALF] = gate_grad[part]
            pre_grads[core, dz, dx, :, HALF:D] = up_grad[part]

    all_rows = GROUP * CAP

    @pl.loop(0, 2)
    def _(n):
        span = pl.ds(pl.multiple_of(n * 256, 256), 256)
        left = active[:, :, :, :, span].reshape(all_rows, 256)
        right = weighted[...].reshape(all_rows, D)
        part = dot(left, right, ((0,), (0,))).astype(bf16)
        for i in range(2):
            for h in range(2):
                rows = part[128 * i + 64 * h : 128 * i + 64 * h + 64]
                grad_ref[2 * n + i, h, 256:320, :] = rows[:, 0:HALF]
                grad_ref[2 * n + i, h, 320:384, :] = rows[:, HALF:D]

    fold_parts(
        parts_out,
        parts_in,
        mid,
        going_back,
        back_send,
        back_recv,
        posz_ref,
        posx_ref,
        part_send,
        part_recv,
    )

    @pl.loop(0, 4)
    def _(n):
        span = pl.ds(pl.multiple_of(n * 256, 256), 256)
        left = arrived[:, :, :, :, span].reshape(all_rows, 256)
        part = dot(left, pre_grads[...].reshape(all_rows, D), ((0,), (0,)))
        for h in range(2):
            rows = part[128 * h : 128 * h + 128].astype(bf16)
            grad_ref[n, h, 0:128, :] = rows[:, 0:HALF]
            grad_ref[n, h, 128:256, :] = rows[:, HALF:D]

    @pl.loop(0, GROUP)
    def _(k):
        @pl.when(jnp.logical_not(own_slot(k)))
        def _():
            small(k, dot_out, dot_in, -1, GROUP, True).wait_recv()

        there, dz, dx = k // CHIPS, lax.rem(k // 4, 4), lax.rem(k, 4)
        _, expert = moved(dx, dz, there)
        at = pl.ds(expert, 1)
        dots = as_column(dot_in[k, 0:1, 0:CAP])
        gdot_ref[at, :] = jnp.sum(
            jnp.where(picks(pos_ref[at, :]), dots, 0.0), axis=0, keepdims=True
        )

    parts_arrived(parts_out, parts_in, part_send, part_recv)
    rg_ref[...] = (parts_in[0].astype(f32) + parts_in[1].astype(f32)) + (
        parts_in[2].astype(f32) + parts_in[3].astype(f32)
    )
    slots_sent(outgoing, arrived, slot_send, slot_recv)
    slots_sent(going_back, mid, back_send, back_recv)
    parts_sent(parts_out, parts_in, part_send, part_recv)

    @pl.loop(1, 4)
    def _(d):
        for copy in spread(d, routed_ref, tok_z, tok_x, first_send, first_recv):
            copy.wait_send()

    @pl.loop(0, GROUP)
    def _(k):
        @pl.when(jnp.logical_not(own_slot(k)))
        def _():
            small(k, gate_out, gate_in, 1, 0).wait_send()
            small(k, dot_out, dot_in, -1, GROUP).wait_send()


def experts(*arrays):
    f32, bf16 = jnp.float32, jnp.bfloat16
    vmem = pl.BlockSpec(memory_space=pltpu.VMEM)
    shape = jax.ShapeDtypeStruct
    block = pltpu.VMEM((2, 4, 4, CAP, D), bf16)
    narrow = pltpu.VMEM((2, 4, 4, CAP, HALF), bf16)
    line = pltpu.VMEM((4, TOKENS, HALF), bf16)
    wide = pltpu.VMEM((4, TOKENS, D), bf16)
    little = pltpu.VMEM((GROUP, 8, 128), f32)
    scratch = [line, line, block, block, block, block, wide, wide]
    scratch += [little] * 4 + [narrow, block, block]
    for count in (8, 2 * GROUP, 2 * GROUP, 8, 2 * GROUP):
        scratch += [pltpu.SemaphoreType.DMA((count,))] * 2
    out_shape = (
        shape((TOKENS, D), f32),
        shape((EXPERTS, TOKENS), f32),
        shape((2, 4, 4, CAP, D), bf16),
        shape((4, 2, 384, HALF), bf16),
    )
    return pl.pallas_call(
        expert_kernel,
        out_shape=out_shape,
        in_specs=[vmem] * len(arrays),
        out_specs=[vmem] * len(out_shape),
        scratch_shapes=scratch,
        compiler_params=pltpu.CompilerParams(
            collective_id=1, has_side_effects=True, vmem_limit_bytes=60 << 20
        ),
        name="experts",
    )(*arrays)


def turned_back(rows, cosine, sine):
    first, second = rows[0:32], rows[32:64]
    return jnp.concatenate(
        [first * cosine + second * sine, second * cosine - first * sine], axis=0
    )


def finish_kernel(
    length_ref,
    prod_ref,
    posz_ref,
    posx_ref,
    gates_ref,
    rg_ref,
    gdot_ref,
    expert_ref,
    routed_ref,
    router_ref,
    middle_ref,
    cot_ref,
    hidden_ref,
    again_ref,
    mgain_ref,
    normed_ref,
    mixed_ref,
    w_hbm,
    q_ref,
    k_ref,
    v_ref,
    lse_ref,
    cos_ref,
    sin_ref,
    hout_ref,
    hgrad_ref,
    again_out,
    mgain_out,
    router_out,
    own_out,
    esum_ref,
    w_ref,
    mid,
    parts_out,
    parts_in,
    relay_in,
    relay_out,
    y_in,
    branch_own,
    branch_sib,
    normed_sib,
    mixed_sib,
    mg_t,
    grad_t,
    grad_sib,
    kv_own,
    kv_out,
    kv_in,
    weight_part,
    rs_in,
    rs_out,
    rs_in2,
    y_out,
    y_parts,
    small_out,
    small_in,
    small_y,
    small_y_in,
    gain_out,
    gain_in,
    gain_y,
    gain_y_in,
    router_all,
    w_sem,
    c_send,
    c_recv,
    part_send,
    part_recv,
    ex_send,
    ex_recv,
    sib_send,
    sib_recv,
    rs_send,
    rs_recv,
    rs_send2,
    rs_recv2,
    ys_send,
    ys_recv,
    sm_send,
    sm_recv,
):
    y, r, x, z = place()
    me = r * CHIPS + z * 4 + x
    sibling = moved(0, 0, 1 - r)[0]
    tokens = routed_ref.shape[0]
    f32, bf16 = jnp.float32, jnp.bfloat16
    weights_in = pltpu.make_async_copy(w_hbm, w_ref, w_sem)
    weights_in.start()
    meet(True, True)

    above, below = plane_shift(1), plane_shift(3)
    opposite = plane_shift(2)[1]

    def relayed(n):
        device = (above, below)[n][0]
        return remote(
            expert_ref.at[opposite, n], relay_in.at[n], ex_send.at[n], ex_recv.at[n], device
        )

    def direct(n):
        device, other = (above, below)[n]
        return remote(
            expert_ref.at[other, 1 - n],
            y_in.at[n, 1 - n],
            ex_send.at[2 + n],
            ex_recv.at[2 + n],
            device,
        )

    def merged(n):
        device = (above, below)[n][0]
        return remote(
            relay_out.at[n], y_in.at[n, n], ex_send.at[4 + n], ex_recv.at[4 + n], device
        )

    def handed(n):
        device = (above, below)[n][0]
        return remote(
            esum_ref.at[y], esum_ref.at[y], ex_send.at[6 + n], ex_recv.at[6 + n], device
        )

    def passed_on(n):
        device, came_from = (above, below)[n][0], (below, above)[n][1]
        part = esum_ref.at[came_from, n]
        return remote(part, part, ex_send.at[8 + n], ex_recv.at[8 + n], device)

    def weight(first, width):
        return w_ref[:, :, :, :, first : first + width].reshape(D, width)

    def to_sibling(at, src, dst):
        return remote(src, dst, sib_send.at[at], sib_recv.at[at], sibling)

    half = pl.ds(pl.multiple_of((1 - r) * HALF, HALF), HALF)
    sib_normed = to_sibling(0, normed_ref.at[:, half], normed_sib)
    sib_mixed = to_sibling(1, mixed_ref.at[:, half], mixed_sib)
    sib_branch = to_sibling(2, branch_own, branch_sib)

    def sib_keyval(p):
        return to_sibling(3 + p, kv_out.at[p], kv_in.at[p])

    def sib_grads(p, part):
        rows = pl.ds(p * D + part * HALF, HALF)
        return to_sibling(5 + 2 * p + part, grad_t.at[rows], grad_sib.at[rows])

    for n in range(2):
        relayed(n).start()
    for n in range(2):
        direct(n).start()
    sib_mixed.start()
    sib_normed.start()

    @pl.loop(0, CHIPS)
    def _(k):
        dx = lax.rem(k, 4)
        dz = lax.rem(dx + k // 4, 4)
        for core in range(2):
            send_slots(prod_ref, mid, core, dz, dx, c_send, c_recv, -1, c_send.at[2 * GROUP])

    gates = gates_ref[...]
    gdot = gdot_ref[...]
    logit_grad = gates * (gdot - jnp.sum(gates * gdot, axis=0, keepdims=True))
    high, rest = split_two(logit_grad)
    router_part = dot(high, routed_ref[...], ((1,), (0,)))
    router_part = router_part + dot(rest, routed_ref[...], ((1,), (0,)))
    routed_grad = dot(high, router_ref[...], ((0,), (0,)))
    routed_grad = routed_grad + dot(rest, router_ref[...], ((0,), (0,)))
    routed_grad = routed_grad + rg_ref[...]
    live = (
        r * tokens + lax.broadcasted_iota(jnp.int32, (tokens, 1), 0) < length_ref[0]
    ).astype(f32)
    middle = middle_ref[...]
    scale = lax.rsqrt(jnp.mean(middle * middle, axis=1, keepdims=True) + epsilon)
    rows = middle * scale
    moe_part = jnp.sum(routed_grad * rows, axis=0, keepdims=True)
    scaled = routed_grad * mgain_ref[...]
    inner = jnp.mean(scaled * rows, axis=1, keepdims=True)
    middle_grad = cot_ref[...].astype(f32) * live + scale * (scaled - rows * inner)
    hgrad_ref[...] = middle_grad
    branch_own[...] = middle_grad.astype(bf16)
    sib_branch.start()
    for j in range(8):
        part = slice(128 * j, 128 * j + 128)
        small_out[:, j, :] = router_part[:, part]
        small_out[:, 8 + j, :] = jnp.broadcast_to(moe_part[:, part], (GROUP, 128))

    def small(k):
        device, other = step_of(k, 1)
        return remote(small_out.at[other], small_in.at[me], sm_send.at[k], sm_recv.at[k], device)

    @pl.loop(1, GROUP)
    def _(k):
        small(k).start()

    small_in[me] = small_out[me]

    weights_in.wait()
    mg_t[...] = dot(weight(2 * D, D), branch_own[...], ((1,), (1,))).astype(bf16)

    for n in range(2):
        relayed(n).wait_recv()
        target = (above, below)[n][1]
        total = relay_in[n].astype(f32) + expert_ref[target, n].astype(f32)
        relay_out[n] = total.astype(bf16)
        merged(n).start()

    mine = pl.ds(pl.multiple_of(r * HALF, HALF), HALF)

    def columns(p):
        return pl.ds(p * D, HALF), pl.ds(p * D + HALF, HALF)

    def first_step(p, d):
        left, right = columns(p)
        at = 8 * p + d
        return (
            remote(
                weight_part.at[lax.rem(z + d, 4), :, :, left],
                rs_in.at[d, :, :, left],
                rs_send.at[at],
                rs_recv.at[at],
                moved(0, d, r)[0],
            ),
            remote(
                weight_part.at[:, lax.rem(x + d, 4), :, right],
                rs_in.at[d, :, :, right],
                rs_send.at[4 + at],
                rs_recv.at[4 + at],
                moved(d, 0, r)[0],
            ),
        )

    def second_step(p, d):
        left, right = columns(p)
        at = 8 * p + d
        return (
            remote(
                rs_out.at[lax.rem(x + d, 4), :, left],
                rs_in2.at[d, :, left],
                rs_send2.at[at],
                rs_recv2.at[at],
                moved(d, 0, r)[0],
            ),
            remote(
                rs_out.at[lax.rem(z + d, 4), :, right],
                rs_in2.at[d, :, right],
                rs_send2.at[4 + at],
                rs_recv2.at[4 + at],
                moved(0, d, r)[0],
            ),
        )

    def across(p, n):
        cols = pl.ds(p * D, D)
        at = 3 * p + n - 1
        return remote(
            y_out.at[:, cols],
            y_parts.at[y, :, cols],
            ys_send.at[at],
            ys_recv.at[at],
            plane_shift(n)[0],
        )

    def sum_first(p, total):
        weight_part[:, :, :, p * D : p * D + D] = total.astype(bf16).reshape(4, 4, 32, D)

        @pl.loop(1, 4)
        def _(d):
            for copy in first_step(p, d):
                copy.start()

    def sum_second(p):
        left, right = columns(p)

        @pl.loop(1, 4)
        def _(d):
            for copy in first_step(p, d):
                copy.wait_recv()

        total = weight_part[z, :, :, left].astype(f32)
        other = weight_part[:, x, :, right].astype(f32)
        for d in range(1, 4):
            total = total + rs_in[d, :, :, left].astype(f32)
            other = other + rs_in[d, :, :, right].astype(f32)
        rs_out[:, :, left] = total.astype(bf16)
        rs_out[:, :, right] = other.astype(bf16)

        @pl.loop(1, 4)
        def _(d):
            for copy in second_step(p, d):
                copy.start()

    def sum_third(p):
        left, right = columns(p)

        @pl.loop(1, 4)
        def _(d):
            for copy in second_step(p, d):
                copy.wait_recv()

        total = rs_out[x, :, left].astype(f32)
        other = rs_out[z, :, right].astype(f32)
        for d in range(1, 4):
            total = total + rs_in2[d, :, left].astype(f32)
            other = other + rs_in2[d, :, right].astype(f32)
        y_out[:, left] = total.astype(bf16)
        y_out[:, right] = other.astype(bf16)
        y_parts[y, :, left] = total.astype(bf16)
        y_parts[y, :, right] = other.astype(bf16)
        for n in range(1, PLANES):
            across(p, n).start()

    sib_mixed.wait_recv()
    sib_branch.wait_recv()
    total = dot(mixed_ref[:, mine], branch_own[...], ((0,), (0,)))
    sum_first(2, total + dot(mixed_sib[...], branch_sib[...], ((0,), (0,))))

    key_live = lax.broadcasted_iota(jnp.int32, (2 * tokens, 1), 0) < length_ref[0]
    score_scale = HEAD ** (-0.5)
    cosine, sine = cos_ref[...], sin_ref[...]
    first_core = r == 0

    def key_head(p, i):
        g = 4 * p + i
        head = pl.ds(pl.multiple_of(g * HEAD, HEAD), HEAD)
        keys, values = k_ref[head, :], v_ref[head, :]
        key_sum, value_sum = None, None
        for j in range(2):
            at = pl.ds(pl.multiple_of((2 * g + j) * HEAD, HEAD), HEAD)
            query, mixed_grad = q_ref[at, :], mg_t[at, :]
            scores = dot(keys, query, ((0,), (0,))) * score_scale
            scores = jnp.where(key_live, scores, NEG)
            probs = jnp.exp(scores - lse_ref[pl.ds(2 * g + j, 1), :])
            prob_grad = dot(values, mixed_grad, ((0,), (0,)))
            value_part = dot(mixed_grad, probs.astype(bf16), ((1,), (1,)))
            inner = jnp.sum(probs * prob_grad, axis=0, keepdims=True)
            score_grad = (probs * (prob_grad - inner)).astype(bf16)
            key_part = dot(query, score_grad, ((1,), (1,)))
            query_grad = dot(keys, score_grad, ((1,), (0,))) * score_scale
            to = pl.ds(pl.multiple_of(p * D + (2 * i + j) * HEAD, HEAD), HEAD)
            grad_t[to, :] = turned_back(query_grad, cosine, sine).astype(bf16)
            key_sum = key_part if key_sum is None else key_sum + key_part
            value_sum = value_part if value_sum is None else value_sum + value_part
        key_sum = key_sum * score_scale
        for n, part in enumerate((key_sum, value_sum)):
            to = pl.ds(pl.multiple_of(256 * n + i * HEAD, HEAD), HEAD)
            kv_own[p, to, :] = jnp.where(first_core, part[:, :tokens], part[:, tokens:])
            away = jnp.where(first_core, part[:, tokens:], part[:, :tokens])
            kv_out[p, to, :] = away.astype(bf16)

    def heads(p, first, last):
        @pl.loop(first, last)
        def _(i):
            key_head(p, i)

    def whole_keyval(p):
        sib_keyval(p).wait_recv()
        for i in range(4):
            rows = slice(HEAD * i, HEAD * i + HEAD)
            total = kv_own[p, rows, :] + kv_in[p, rows, :].astype(f32)
            to = p * D + HALF + HEAD * i
            grad_t[to : to + HEAD, :] = turned_back(total, cosine, sine).astype(bf16)
        total = kv_own[p, 256:512, :] + kv_in[p, 256:512, :].astype(f32)
        grad_t[p * D + HALF + 256 : p * D + D, :] = total.astype(bf16)
        sib_grads(p, 1).start()

    def projections(p):
        rows = slice(p * D, p * D + D)
        for part in range(2):
            sib_grads(p, part).wait_recv()
        total = dot(normed_ref[:, mine], grad_t[rows, :], ((0,), (1,)))
        sum_first(p, total + dot(normed_sib[...], grad_sib[rows, :], ((0,), (1,))))

    def inputs_part(p):
        return dot(grad_t[p * D : p * D + D, :], weight(p * D, D), ((0,), (1,)))

    heads(0, 0, 4)
    sib_keyval(0).start()
    sib_grads(0, 0).start()

    for n in range(2):
        direct(n).wait_recv()
        merged(n).wait_recv()
    for n in range(2):
        total = expert_ref[y, n].astype(f32) + (y_in[0, n].astype(f32) + y_in[1, n].astype(f32))
        esum_ref[y, n] = total.astype(bf16)
    for n in range(2):
        handed(n).start()

    whole_keyval(0)

    @pl.loop(1, GROUP)
    def _(k):
        small(k).wait_recv()

    def small_across(n):
        device, _ = plane_shift(n)
        return remote(
            small_y, small_y_in.at[y], sm_send.at[GROUP + n], sm_recv.at[GROUP + n], device
        )

    small_y[...] = jnp.sum(small_in[...], axis=0)
    small_y_in[y] = small_y[...]
    for n in range(1, PLANES):
        small_across(n).start()

    sum_second(2)
    sib_normed.wait_recv()
    projections(0)
    heads(1, 0, 4)
    sib_keyval(1).start()
    sib_grads(1, 0).start()

    for n in range(1, PLANES):
        small_across(n).wait_recv()
    totals = small_y_in[0] + small_y_in[1] + small_y_in[2] + small_y_in[3]
    mgain_out[...] = totals[8:16]
    router_all[me] = totals[0:8]

    def router_row(k):
        device, _ = step_of(k, 1)
        at = 2 * GROUP + k
        return remote(
            router_all.at[me], router_all.at[me], sm_send.at[at], sm_recv.at[at], device
        )

    @pl.loop(1, GROUP)
    def _(k):
        router_row(k).start()

    whole_keyval(1)
    normed_grad = inputs_part(0)
    projections(1)
    sum_second(0)
    sum_third(2)
    normed_grad = normed_grad + inputs_part(1)

    inputs = hidden_ref[...].astype(f32)
    scale = lax.rsqrt(jnp.mean(inputs * inputs, axis=1, keepdims=True) + epsilon)
    rows = inputs * scale
    attn_part = jnp.sum(normed_grad * rows, axis=0, keepdims=True)
    for j in range(8):
        gain_out[j : j + 1, :] = attn_part[:, 128 * j : 128 * j + 128]

    def gain(k):
        device, _ = step_of(k, 1)
        at = 3 * GROUP + k
        return remote(gain_out, gain_in.at[me], sm_send.at[at], sm_recv.at[at], device)

    @pl.loop(1, GROUP)
    def _(k):
        gain(k).start()

    gain_in[me] = gain_out[...]
    scaled = normed_grad * again_ref[...]
    inner = jnp.mean(scaled * rows, axis=1, keepdims=True)
    hgrad_ref[...] += scale * (scaled - rows * inner)

    for n in range(2):
        handed(n).wait_recv()
        passed_on(n).start()

    fold_parts(
        parts_out,
        parts_in,
        mid,
        prod_ref,
        c_send,
        c_recv,
        posz_ref,
        posx_ref,
        part_send,
        part_recv,
    )
    sum_second(1)
    sum_third(0)

    @pl.loop(1, GROUP)
    def _(k):
        gain(k).wait_recv()

    gain_y[...] = jnp.sum(gain_in[...], axis=0)
    gain_y_in[y] = gain_y[...]

    def gain_across(n):
        device, _ = plane_shift(n)
        at = 4 * GROUP + n
        return remote(gain_y, gain_y_in.at[y], sm_send.at[at], sm_recv.at[at], device)

    for n in range(1, PLANES):
        gain_across(n).start()

    sum_third(1)

    parts_arrived(parts_out, parts_in, part_send, part_recv)
    mixture = (parts_in[0].astype(f32) + parts_in[1].astype(f32)) + (
        parts_in[2].astype(f32) + parts_in[3].astype(f32)
    )
    hout_ref[...] = ((middle_ref[...] + mixture) * live).astype(bf16)

    for n in range(1, PLANES):
        gain_across(n).wait_recv()
    again_out[...] = (gain_y_in[0] + gain_y_in[1]) + (gain_y_in[2] + gain_y_in[3])

    @pl.loop(1, GROUP)
    def _(k):
        router_row(k).wait_recv()

    router_out[...] = router_all[...]

    slots_sent(prod_ref, mid, c_send, c_recv)
    parts_sent(parts_out, parts_in, part_send, part_recv)

    @pl.loop(1, GROUP)
    def _(k):
        small(k).wait_send()
        router_row(k).wait_send()
        gain(k).wait_send()

    @pl.loop(1, 4)
    def _(d):
        for p in range(3):
            for copy in first_step(p, d) + second_step(p, d):
                copy.wait_send()

    for n in range(2):
        for copy in (relayed(n), direct(n), merged(n), handed(n), passed_on(n)):
            copy.wait_send()
    for copy in (sib_normed, sib_mixed, sib_branch):
        copy.wait_send()
    for p in range(2):
        sib_keyval(p).wait_send()
        for part in range(2):
            sib_grads(p, part).wait_send()
    for n in range(1, PLANES):
        small_across(n).wait_send()
        gain_across(n).wait_send()
        for p in range(3):
            across(p, n).wait()
    for n in range(2):
        passed_on(n).wait_recv()
    own_out[...] = (y_parts[0].astype(f32) + y_parts[1].astype(f32)) + (
        y_parts[2].astype(f32) + y_parts[3].astype(f32)
    )


def finish(length, *arrays):
    tokens = TOKENS
    f32, bf16 = jnp.float32, jnp.bfloat16
    vmem = pl.BlockSpec(memory_space=pltpu.VMEM)
    shape = jax.ShapeDtypeStruct
    sems = pltpu.SemaphoreType.DMA
    in_specs = [pl.BlockSpec(memory_space=pltpu.SMEM)] + [vmem] * len(arrays)
    in_specs[1] = pl.BlockSpec(memory_space=pl.ANY)
    in_specs[17] = pl.BlockSpec(memory_space=pl.ANY)
    scratch = [
        pltpu.VMEM((2, 4, 4, 32, 3 * D), bf16),
        pltpu.VMEM((2, 4, 4, CAP, D), bf16),
        pltpu.VMEM((4, tokens, D), bf16),
        pltpu.VMEM((4, tokens, D), bf16),
        pltpu.VMEM((2, 384, HALF), bf16),
        pltpu.VMEM((2, 384, HALF), bf16),
        pltpu.VMEM((2, 2, 384, HALF), bf16),
        pltpu.VMEM((tokens, D), bf16),
        pltpu.VMEM((tokens, D), bf16),
        pltpu.VMEM((tokens, HALF), bf16),
        pltpu.VMEM((tokens, HALF), bf16),
        pltpu.VMEM((D, tokens), bf16),
        pltpu.VMEM((2 * D, tokens), bf16),
        pltpu.VMEM((2 * D, tokens), bf16),
        pltpu.VMEM((2, HALF, tokens), f32),
        pltpu.VMEM((2, HALF, tokens), bf16),
        pltpu.VMEM((2, HALF, tokens), bf16),
        pltpu.VMEM((4, 4, 32, 3 * D), bf16),
        pltpu.VMEM((4, 4, 32, 3 * D), bf16),
        pltpu.VMEM((4, 32, 3 * D), bf16),
        pltpu.VMEM((4, 32, 3 * D), bf16),
        pltpu.VMEM((32, 3 * D), bf16),
        pltpu.VMEM((PLANES, 32, 3 * D), bf16),
        pltpu.VMEM((GROUP, 16, 128), f32),
        pltpu.VMEM((GROUP, 16, 128), f32),
        pltpu.VMEM((16, 128), f32),
        pltpu.VMEM((PLANES, 16, 128), f32),
        pltpu.VMEM((8, 128), f32),
        pltpu.VMEM((GROUP, 8, 128), f32),
        pltpu.VMEM((8, 128), f32),
        pltpu.VMEM((PLANES, 8, 128), f32),
        pltpu.VMEM((GROUP, 8, 128), f32),
        sems,
    ]
    for count in (2 * GROUP + 1, 8, 10, 9, 24, 24, 9, 5 * GROUP):
        scratch += [sems((count,)), sems((count,))]
    return pl.pallas_call(
        finish_kernel,
        out_shape=(
            shape((tokens, D), bf16),
            shape((tokens, D), f32),
            shape((8, 128), f32),
            shape((8, 128), f32),
            shape((GROUP, 8, 128), f32),
            shape((32, 3 * D), f32),
            shape((4, 2, 384, HALF), bf16),
        ),
        in_specs=in_specs,
        out_specs=[vmem] * 7,
        scratch_shapes=scratch,
        compiler_params=pltpu.CompilerParams(
            collective_id=2, has_side_effects=True, vmem_limit_bytes=60 << 20
        ),
        name="finish",
    )(length, *arrays)


def spread_kernel(
    hout_ref,
    hgrad_ref,
    own_ref,
    esum_ref,
    router_ref,
    hout_out,
    hgrad_out,
    q_out,
    k_out,
    v_out,
    o_out,
    gate_out,
    up_out,
    down_out,
    router_out,
):
    f32 = jnp.float32
    hout_out[...] = hout_ref[...]
    hgrad_out[...] = hgrad_ref[...]
    for p in range(2):
        q_out[:, p * HALF : p * HALF + HALF] = own_ref[:, p * D : p * D + HALF]
        k_out[:, p * 256 : p * 256 + 256] = own_ref[:, p * D + HALF : p * D + 768]
        v_out[:, p * 256 : p * 256 + 256] = own_ref[:, p * D + 768 : p * D + D]
    o_out[...] = own_ref[:, 2 * D : 3 * D]
    for h in range(2):
        gate_out[0, 128 * h : 128 * h + 128, :] = esum_ref[0, h, 0:128, :].astype(f32)
        up_out[0, 128 * h : 128 * h + 128, :] = esum_ref[0, h, 128:256, :].astype(f32)
        down_out[0, 64 * h : 64 * h + 64, 0:HALF] = esum_ref[0, h, 256:320, :].astype(f32)
        down_out[0, 64 * h : 64 * h + 64, HALF:D] = esum_ref[0, h, 320:384, :].astype(f32)
    for j in range(8):
        router_out[128 * j : 128 * j + 128, :] = router_ref[:, j, :].T


def spread_out(*arrays):
    f32, bf16 = jnp.float32, jnp.bfloat16
    shape = jax.ShapeDtypeStruct

    def whole(*dims):
        return pl.BlockSpec(dims, lambda i: (0,) * len(dims))

    def rows(count, width):
        return pl.BlockSpec((count, width), lambda i: (i, 0))

    def expert_rows(count, width):
        return pl.BlockSpec((1, count, width), lambda i: (0, i, 0))

    return pl.pallas_call(
        spread_kernel,
        grid=(4,),
        out_shape=(
            shape((TOKENS, D), bf16),
            shape((TOKENS, D), f32),
            shape((32, D), f32),
            shape((32, HALF), f32),
            shape((32, HALF), f32),
            shape((32, D), f32),
            shape((1, D, HALF), f32),
            shape((1, D, HALF), f32),
            shape((1, HALF, D), f32),
            shape((D, EXPERTS), f32),
        ),
        in_specs=[
            rows(64, D),
            rows(64, D),
            whole(32, 3 * D),
            pl.BlockSpec((1, 2, 384, HALF), lambda i: (i, 0, 0, 0)),
            whole(GROUP, 8, 128),
        ],
        out_specs=[
            rows(64, D),
            rows(64, D),
            whole(32, D),
            whole(32, HALF),
            whole(32, HALF),
            whole(32, D),
            expert_rows(256, HALF),
            expert_rows(256, HALF),
            expert_rows(128, D),
            whole(D, EXPERTS),
        ],
        name="spread_out",
    )(*arrays)


def on_device(
    hidden_in,
    cotangent,
    lengths,
    routes,
    priority,
    attn_gain,
    query_weight,
    key_weight,
    value_weight,
    output_weight,
    moe_gain,
    router,
    gate_weight,
    up_weight,
    down_weight,
):
    tok_count = hidden_in.shape[0]
    positions = lax.axis_index("row") * tok_count + jnp.arange(tok_count, dtype=jnp.int32)
    half_dim = HEAD // 2
    frequency = rotary_base ** (-jnp.arange(half_dim, dtype=jnp.float32) / half_dim)
    angles = frequency[:, None] * positions.astype(jnp.float32)[None, :]
    cosine, sine = jnp.cos(angles), jnp.sin(angles)
    router_t = router.T
    (
        weights,
        normed,
        queries,
        keys,
        values,
        log_total,
        mixed_rows,
        middle,
        routed,
        gates,
        pos,
        posz,
        posx,
        arrived_grad,
    ) = front(
        lengths,
        hidden_in,
        cotangent,
        routes.T,
        priority.reshape(tok_count, TOP).T,
        attn_gain[None],
        moe_gain[None],
        query_weight,
        key_weight,
        value_weight,
        output_weight,
        router_t,
        cosine,
        sine,
    )
    returned_rows, gate_dot, produced, expert_grads = experts(
        routed,
        pos,
        posz,
        posx,
        gates,
        arrived_grad,
        gate_weight[0],
        up_weight[0],
        down_weight[0],
    )
    (
        hidden_out,
        hidden_grad,
        attn_gain_sum,
        moe_gain_sum,
        router_sum,
        own_rows,
        expert_sum,
    ) = finish(
        lengths,
        produced,
        posz,
        posx,
        gates,
        returned_rows,
        gate_dot,
        expert_grads,
        routed,
        router_t,
        middle,
        cotangent,
        hidden_in,
        attn_gain[None],
        moe_gain[None],
        normed,
        mixed_rows,
        weights,
        queries,
        keys,
        values,
        log_total,
        cosine,
        sine,
    )
    (
        hidden_out,
        hidden_grad,
        query_grad,
        key_grad,
        value_grad,
        output_grad,
        gate_grad,
        up_grad,
        down_grad,
        router_grad,
    ) = spread_out(hidden_out, hidden_grad, own_rows, expert_sum, router_sum)
    return (
        hidden_out,
        hidden_grad,
        attn_gain_sum.reshape(D),
        query_grad,
        key_grad,
        value_grad,
        output_grad,
        moe_gain_sum.reshape(D),
        router_grad,
        gate_grad,
        up_grad,
        down_grad,
    )


def solution(mesh):
    return jax.shard_map(
        on_device,
        mesh=mesh,
        in_specs=(
            P(("dp", "col", "row"), None),
            P(("dp", "col", "row"), None),
            P(("dp", "col")),
            P(("dp", "col", "row"), None),
            P(("dp", "col", "row"), None),
            P(),
            P(("row", "col"), None),
            P(("row", "col"), None),
            P(("row", "col"), None),
            P(("row", "col"), None),
            P(),
            P(),
            P(("row", "col"), None, None),
            P(("row", "col"), None, None),
            P(("row", "col"), None, None),
        ),
        out_specs=(
            P(("dp", "col", "row"), None),
            P(("dp", "col", "row"), None),
            P(),
            P(("row", "col"), None),
            P(("row", "col"), None),
            P(("row", "col"), None),
            P(("row", "col"), None),
            P(),
            P(),
            P(("row", "col"), None, None),
            P(("row", "col"), None, None),
            P(("row", "col"), None, None),
        ),
        check_vma=False,
    )
```

```python
import jax
import jax.numpy as jnp
from jax import lax
from jax.experimental import pallas as pl
from jax.experimental.pallas import tpu as pltpu
from jax.sharding import PartitionSpec as P

D = 1024
HEADS = 16
HEAD = 64
KV_HEADS = 8
EXPERTS = 32
TOP = 8
CAP = 64


epsilon = 1e-05
rotary_base = 10000.0


MESH = pl.DeviceIdType.MESH
GROUP = 32
PLANES = 4
CHIPS = 16
HALF = D // 2
TOKENS = 256
NEG = -1000000000.0


def place():
    col = lax.axis_index("col")
    return lax.axis_index("dp"), lax.axis_index("row"), lax.rem(col, 4), col // 4


def moved(dx, dz, core):
    y, r, x, z = place()
    col = lax.rem(z + dz + 4, 4) * 4 + lax.rem(x + dx + 4, 4)
    return (y, core, col), core * CHIPS + col


def plane_shift(n):
    y, r, x, z = place()
    other = lax.rem(y + n, PLANES)
    return (other, r, z * 4 + x), other


def step_of(k, sign):
    y, r, x, z = place()
    return moved(sign * lax.rem(k, 4), sign * lax.rem(k // 4, 4), lax.rem(r + k // CHIPS, 2))


def remote(src, dst, send_sem, recv_sem, device):
    return pltpu.make_async_remote_copy(
        src_ref=src,
        dst_ref=dst,
        send_sem=send_sem,
        recv_sem=recv_sem,
        device_id=device,
        device_id_type=MESH,
    )


def meet(plane, planes):
    barrier = pltpu.get_barrier_semaphore()
    y, r, x, z = place()

    def greet(device):
        pl.semaphore_signal(barrier, inc=1, device_id=device, device_id_type=MESH)

    if plane:

        @pl.loop(1, GROUP)
        def _(k):
            greet(step_of(k, 1)[0])

        count = GROUP - 1
    else:
        for core in range(2):

            @pl.loop(1, 4)
            def _(d):
                greet(moved(d, 0, core)[0])
                greet(moved(0, d, core)[0])

        greet(moved(0, 0, 1 - r)[0])
        count = 13
    if planes:
        for n in range(1, PLANES):
            greet(plane_shift(n)[0])
        count += PLANES - 1
    pl.semaphore_wait(barrier, count)


def eye(n):
    return lax.broadcasted_iota(jnp.int32, (n, n), 0) == lax.broadcasted_iota(
        jnp.int32, (n, n), 1
    )


def as_row(column):
    return jnp.sum(jnp.where(eye(column.shape[0]), column, 0.0), axis=0, keepdims=True)


def as_column(row_vec):
    return jnp.sum(jnp.where(eye(row_vec.shape[1]), row_vec, 0.0), axis=1, keepdims=True)


def dot(a, b, dims):
    return lax.dot_general(a, b, (dims, ((), ())), preferred_element_type=jnp.float32)


def split_two(values):
    high = values.astype(jnp.bfloat16)
    return high, (values - high.astype(jnp.float32)).astype(jnp.bfloat16)


def picks(positions):
    slots = lax.broadcasted_iota(jnp.int32, (CAP, positions.shape[1]), 0)
    return slots == positions


def as_hot(mask):
    return mask.astype(jnp.float32).astype(jnp.bfloat16)


LEFT = pl.ds(0, HALF)
RIGHT = pl.ds(HALF, HALF)


def spread(d, source, tok_z, tok_x, send_sem, recv_sem):
    y, r, x, z = place()
    return (
        remote(
            source.at[:, LEFT], tok_z.at[d], send_sem.at[d], recv_sem.at[d], moved(0, d, r)[0]
        ),
        remote(
            source.at[:, RIGHT],
            tok_x.at[d],
            send_sem.at[4 + d],
            recv_sem.at[4 + d],
            moved(d, 0, r)[0],
        ),
    )


def slot_copies(out, into, core, there, dz, dx, send_sem, recv_sem, sign):
    y, r, x, z = place()
    at = there * CHIPS + dz * 4 + dx
    to = core * CHIPS + dz * 4 + dx
    return (
        lambda: remote(
            out.at[there, dz, dx, :, LEFT],
            into.at[core, dz, dx, :, LEFT],
            send_sem.at[at],
            recv_sem.at[to],
            moved(sign * dx, 0, there)[0],
        ),
        lambda: remote(
            out.at[there, dz, dx, :, RIGHT],
            into.at[core, dz, dx, :, RIGHT],
            send_sem.at[GROUP + at],
            recv_sem.at[GROUP + to],
            moved(0, sign * dz, there)[0],
        ),
    )


def is_local(core, offset):
    y, r, x, z = place()
    return (core == r) & (offset == 0)


def send_slots(out, into, there, dz, dx, send_sem, recv_sem, sign, local_sem=None):
    y, r, x, z = place()

    def keep(cols):
        source, target = out.at[there, dz, dx, :, cols], into.at[r, dz, dx, :, cols]
        if local_sem is None:
            target[...] = source[...]
        else:
            copy = pltpu.make_async_copy(source, target, local_sem)
            copy.start()
            copy.wait()

    left, right = slot_copies(out, into, r, there, dz, dx, send_sem, recv_sem, sign)

    @pl.when(jnp.logical_not(is_local(there, dx)))
    def _():
        left().start()

    @pl.when(is_local(there, dx))
    def _():
        keep(LEFT)

    @pl.when(jnp.logical_not(is_local(there, dz)))
    def _():
        right().start()

    @pl.when(is_local(there, dz))
    def _():
        keep(RIGHT)


def slots_arrived(out, into, core, dz, dx, send_sem, recv_sem, left=True, right=True):
    copies = slot_copies(out, into, core, core, dz, dx, send_sem, recv_sem, 1)
    for copy, offset, wanted in zip(copies, (dx, dz), (left, right)):
        if wanted:

            @pl.when(jnp.logical_not(is_local(core, offset)))
            def _():
                copy().wait_recv()


def slots_sent(out, into, send_sem, recv_sem):
    @pl.loop(0, GROUP)
    def _(k):
        there, dz, dx = k // CHIPS, lax.rem(k // 4, 4), lax.rem(k, 4)
        copies = slot_copies(out, into, there, there, dz, dx, send_sem, recv_sem, 1)
        for copy, offset in zip(copies, (dx, dz)):

            @pl.when(jnp.logical_not(is_local(there, offset)))
            def _():
                copy().wait_send()


def line_rows(line, d, axis):
    y, r, x, z = place()
    own = x if axis == 0 else z
    return [
        line[d, pl.ds(core * 4 + lax.rem(own + i, 4), 1), :] for core in range(2) for i in range(4)
    ]


def line_hot(line, d, axis):
    return as_hot(jnp.concatenate([picks(p) for p in line_rows(line, d, axis)], axis=0))


def add_up(mid, line, d, axis):
    if axis == 0:
        rows = mid[:, d, :, :, 0:HALF]
    else:
        rows = mid[:, :, d, :, HALF:D]
    return dot(line_hot(line, d, axis), rows.reshape(8 * CAP, HALF), ((0,), (0,))).astype(
        jnp.bfloat16
    )


def part_copies(d, out, into, send_sem, recv_sem):
    y, r, x, z = place()
    return (
        lambda: remote(
            out.at[d, :, LEFT],
            into.at[d, :, LEFT],
            send_sem.at[d],
            recv_sem.at[d],
            moved(0, -d, r)[0],
        ),
        lambda: remote(
            out.at[d, :, RIGHT],
            into.at[d, :, RIGHT],
            send_sem.at[4 + d],
            recv_sem.at[4 + d],
            moved(-d, 0, r)[0],
        ),
    )


def fold_parts(out, into, mid, slots, slot_send, slot_recv, posz_ref, posx_ref, send_sem, recv_sem):
    @pl.loop(0, 4)
    def _(d):
        for core in range(2):
            for i in range(4):
                slots_arrived(slots, mid, core, d, i, slot_send, slot_recv, right=False)
        left = add_up(mid, posz_ref, d, 0)

        @pl.when(d == 0)
        def _():
            into[0, :, 0:HALF] = left

        @pl.when(d != 0)
        def _():
            out[d, :, 0:HALF] = left
            part_copies(d, out, into, send_sem, recv_sem)[0]().start()

        for core in range(2):
            for i in range(4):
                slots_arrived(slots, mid, core, i, d, slot_send, slot_recv, left=False)
        right = add_up(mid, posx_ref, d, 1)

        @pl.when(d == 0)
        def _():
            into[0, :, HALF:D] = right

        @pl.when(d != 0)
        def _():
            out[d, :, HALF:D] = right
            part_copies(d, out, into, send_sem, recv_sem)[1]().start()


def parts_arrived(out, into, send_sem, recv_sem):
    @pl.loop(1, 4)
    def _(d):
        for copy in part_copies(d, out, into, send_sem, recv_sem):
            copy().wait_recv()


def parts_sent(out, into, send_sem, recv_sem):
    @pl.loop(1, 4)
    def _(d):
        for copy in part_copies(d, out, into, send_sem, recv_sem):
            copy().wait_send()

def front_kernel(
    length_ref,
    hidden_ref,
    cot_ref,
    routes_ref,
    prio_ref,
    again_ref,
    mgain_ref,
    wq_ref,
    wk_ref,
    wv_ref,
    wo_ref,
    router_ref,
    cos_ref,
    sin_ref,
    w_hbm,
    normed_ref,
    q_ref,
    k_ref,
    v_ref,
    lse_ref,
    mixed_ref,
    middle_ref,
    routed_ref,
    gates_ref,
    pos_ref,
    posz_ref,
    posx_ref,
    grads_ref,
    w_ref,
    mixed_t,
    posz_out,
    posx_out,
    tok_z,
    tok_x,
    outgoing,
    store_sem,
    w_send,
    w_recv,
    o_send,
    o_recv,
    core_send,
    core_recv,
    kv_send,
    kv_recv,
    first_send,
    first_recv,
    slot_send,
    slot_recv,
    pos_send,
    pos_recv,
):
    y, r, x, z = place()
    f32, bf16 = jnp.float32, jnp.bfloat16
    sibling = moved(0, 0, 1 - r)[0]
    meet(False, True)

    for p in range(2):
        part = slice(256 * p, 256 * p + 256)
        w_ref[r, z, x, :, D * p : D * p + HALF] = wq_ref[:, HALF * p : HALF * p + HALF]
        w_ref[r, z, x, :, D * p + HALF : D * p + 768] = wk_ref[:, part]
        w_ref[r, z, x, :, D * p + 768 : D * p + D] = wv_ref[:, part]
    front, rear, output = pl.ds(0, D), pl.ds(D, D), pl.ds(2 * D, D)
    quarter = pl.ds(pl.multiple_of(2 * D + 256 * y, 256), 256)

    def line_step(d):
        mine_q, mine_o = w_ref.at[r, z, x, :, front], w_ref.at[r, z, x, :, rear]
        return (
            remote(mine_q, mine_q, w_send.at[d], w_recv.at[d], moved(0, d, r)[0]),
            remote(mine_o, mine_o, w_send.at[4 + d], w_recv.at[4 + d], moved(d, 0, r)[0]),
        )

    def cross_step(e, d):
        at = 8 + 4 * e + d
        from_z = w_ref.at[r, lax.rem(z - e + 4, 4), x, :, front]
        from_x = w_ref.at[r, z, lax.rem(x - e + 4, 4), :, rear]
        return (
            remote(from_z, from_z, w_send.at[at], w_recv.at[at], moved(d, 0, r)[0]),
            remote(from_x, from_x, w_send.at[16 + at], w_recv.at[16 + at], moved(0, d, r)[0]),
        )

    w_ref[r, z, x, :, quarter] = wo_ref[:, pl.ds(pl.multiple_of(256 * y, 256), 256)]

    def output_line(d):
        own = w_ref.at[r, z, x, :, quarter]
        return remote(own, own, o_send.at[d], o_recv.at[d], moved(0, d, r)[0])

    def output_cross(d):
        own = w_ref.at[r, :, x, :, quarter]
        return remote(own, own, o_send.at[4 + d], o_recv.at[4 + d], moved(d, 0, r)[0])

    def output_plane(n):
        own = w_ref.at[r, :, :, :, quarter]
        return remote(own, own, o_send.at[8 + n], o_recv.at[8 + n], plane_shift(n)[0])

    def output_core():
        own = w_ref.at[r, :, :, :, output]
        return remote(own, own, o_send.at[0], o_recv.at[0], sibling)

    def core_step(d):
        from_x = w_ref.at[r, :, lax.rem(x - d + 4, 4), :, front]
        from_z = w_ref.at[r, lax.rem(z - d + 4, 4), :, :, rear]
        return (
            remote(from_x, from_x, core_send.at[d], core_recv.at[d], sibling),
            remote(from_z, from_z, core_send.at[4 + d], core_recv.at[4 + d], sibling),
        )

    @pl.loop(1, 4)
    def _(d):
        for copy in line_step(d):
            copy.start()

    @pl.loop(1, 4)
    def _(d):
        for copy in cross_step(0, d):
            copy.start()
        output_line(d).start()

    tokens = hidden_ref.shape[0]
    experts_iota = lax.broadcasted_iota(jnp.int32, (EXPERTS, tokens), 0).astype(f32)
    live = r * tokens + lax.broadcasted_iota(jnp.int32, (1, tokens), 1) < length_ref[0]
    routed_to = jnp.zeros((EXPERTS, tokens), f32)
    ranks = jnp.zeros((EXPERTS, tokens), f32)
    routes = routes_ref[...].astype(f32).T
    priority = prio_ref[...].astype(f32).T
    for j in range(TOP):
        match = experts_iota == routes[j : j + 1, :]
        routed_to = jnp.where(match, 1.0, routed_to)
        ranks = jnp.where(match, priority[j : j + 1, :], ranks)
    far = float(1 << 20)
    ranks = jnp.where((routed_to > 0.0) & live, ranks, far)
    ranks_t = ranks.T
    rows = []
    for e in range(EXPERTS):
        earlier = ranks_t[:, e : e + 1] < ranks[e : e + 1, :]
        rows.append(jnp.sum(earlier.astype(f32), axis=0, keepdims=True))
    slots = jnp.concatenate(rows, axis=0)
    pos = jnp.where((ranks < far) & (slots < CAP), slots, -1.0).astype(jnp.int32)
    pos_ref[...] = pos
    for core in range(2):
        for i in range(4):
            at = core * CHIPS + 4 * i
            posz_out[i, 4 * core : 4 * core + 4, :] = pos[at : at + 4, :]
            for j in range(4):
                posx_out[j, 4 * core + i : 4 * core + i + 1, :] = pos[at + j : at + j + 1, :]
    posz_ref[0] = posz_out[z]
    posx_ref[0] = posx_out[x]
    tok_z[0] = cot_ref[:, 0:HALF]
    tok_x[0] = cot_ref[:, HALF:D]

    def pos_step(d):
        to_z, to_x = lax.rem(z + d, 4), lax.rem(x + d, 4)
        return (
            remote(
                posz_out.at[to_z],
                posz_ref.at[d],
                pos_send.at[d],
                pos_recv.at[d],
                moved(0, d, r)[0],
            ),
            remote(
                posx_out.at[to_x],
                posx_ref.at[d],
                pos_send.at[4 + d],
                pos_recv.at[4 + d],
                moved(d, 0, r)[0],
            ),
        )

    @pl.loop(1, 4)
    def _(d):
        for copy in pos_step(d):
            copy.start()

    @pl.loop(1, 4)
    def _(d):
        output_line(d).wait_recv()

    @pl.loop(1, 4)
    def _(d):
        output_cross(d).start()

    @pl.loop(1, 4)
    def _(e):
        for copy in line_step(e):
            copy.wait_recv()

        @pl.loop(1, 4)
        def _(d):
            for copy in cross_step(e, d):
                copy.start()

    @pl.loop(1, 4)
    def _(d):
        for copy in spread(d, cot_ref, tok_z, tok_x, first_send, first_recv):
            copy.start()

    for copy in core_step(0):
        copy.start()

    inputs = hidden_ref[...].astype(f32)
    scale = lax.rsqrt(jnp.mean(inputs * inputs, axis=1, keepdims=True) + epsilon)
    normed_ref[...] = (inputs * scale * again_ref[...]).astype(bf16)

    @pl.loop(1, 4)
    def _(d):
        for copy in spread(d, cot_ref, tok_z, tok_x, first_send, first_recv):
            copy.wait_recv()
        for copy in pos_step(d):
            copy.wait_recv()

    @pl.loop(0, 4)
    def _(d):
        left = dot(line_hot(posz_ref, d, 0), tok_z[d], ((1,), (0,))).astype(bf16)
        right = dot(line_hot(posx_ref, d, 1), tok_x[d], ((1,), (0,))).astype(bf16)
        for core in range(2):
            for i in range(4):
                part = slice((core * 4 + i) * CAP, (core * 4 + i + 1) * CAP)
                outgoing[core, d, i, :, 0:HALF] = left[part]
                outgoing[core, i, d, :, HALF:D] = right[part]

    @pl.loop(1, 4)
    def _(d):
        output_cross(d).wait_recv()

    for n in range(1, PLANES):
        output_plane(n).start()

    @pl.loop(1, 4)
    def _(d):
        @pl.loop(0, 4)
        def _(e):
            for copy in cross_step(e, d):
                copy.wait_recv()

        for copy in core_step(d):
            copy.start()

    @pl.loop(0, CHIPS)
    def _(k):
        dx = lax.rem(k, 4)
        dz = lax.rem(dx + k // 4, 4)
        for core in range(2):
            send_slots(
                outgoing, grads_ref, core, dz, dx, slot_send, slot_recv, 1, store_sem.at[1]
            )

    @pl.loop(0, 4)
    def _(d):
        for copy in core_step(d):
            copy.wait_recv()

    cosine, sine = cos_ref[...], sin_ref[...]
    here = pl.ds(pl.multiple_of(r * tokens, tokens), tokens)

    def projected(first):
        weight = w_ref[:, :, :, :, first : first + HALF].reshape(D, HALF)
        return dot(normed_ref[...], weight, ((1,), (0,))).T

    def turned(rows):
        parts = []
        for h in range(rows.shape[0] // HEAD):
            first, second = rows[HEAD * h : HEAD * h + 32], rows[HEAD * h + 32 : HEAD * h + HEAD]
            parts += [first * cosine - second * sine, second * cosine + first * sine]
        return jnp.concatenate(parts, axis=0).astype(bf16)

    key_copy = remote(
        k_ref.at[:, here], k_ref.at[:, here], kv_send.at[0], kv_recv.at[0], sibling
    )
    value_copy = remote(
        v_ref.at[:, here], v_ref.at[:, here], kv_send.at[1], kv_recv.at[1], sibling
    )
    for p in range(2):
        both = projected(D * p + HALF)
        k_ref[256 * p : 256 * p + 256, here] = turned(both[0:256])
        v_ref[256 * p : 256 * p + 256, here] = both[256:512].astype(bf16)
    key_copy.start()
    value_copy.start()
    for p in range(2):
        q_ref[HALF * p : HALF * p + HALF, :] = turned(projected(D * p))

    key_copy.wait_recv()
    value_copy.wait_recv()

    for n in range(1, PLANES):
        output_plane(n).wait_recv()
    output_core().start()

    key_live = lax.broadcasted_iota(jnp.int32, (2 * tokens, 1), 0) < length_ref[0]
    score_scale = HEAD ** (-0.5)

    @pl.loop(0, KV_HEADS)
    def _(g):
        head = pl.ds(pl.multiple_of(g * HEAD, HEAD), HEAD)
        keys, values = k_ref[head, :], v_ref[head, :]
        for j in range(2):
            at = pl.ds(pl.multiple_of((2 * g + j) * HEAD, HEAD), HEAD)
            scores = dot(keys, q_ref[at, :], ((0,), (0,))) * score_scale
            scores = jnp.where(key_live, scores, NEG)
            top = jnp.max(scores, axis=0, keepdims=True)
            weights = jnp.exp(scores - top)
            total = jnp.sum(weights, axis=0, keepdims=True)
            lse_ref[pl.ds(2 * g + j, 1), :] = top + jnp.log(total)
            probs = (weights * (1.0 / total)).astype(bf16)
            mixed_t[at, :] = dot(values, probs, ((1,), (0,))).astype(bf16)

    mixed_ref[...] = mixed_t[...].T
    output_core().wait_recv()
    weights_out = pltpu.make_async_copy(w_ref, w_hbm, store_sem.at[0])
    weights_out.start()
    w_out = w_ref[:, :, :, :, 2 * D : 3 * D].reshape(D, D)
    middle = hidden_ref[...].astype(f32) + dot(mixed_ref[...], w_out, ((1,), (0,)))
    middle_ref[...] = middle
    scale = lax.rsqrt(jnp.mean(middle * middle, axis=1, keepdims=True) + epsilon)
    routed_ref[...] = (middle * scale * mgain_ref[...]).astype(bf16)
    logits = dot(router_ref[...], routed_ref[...], ((1,), (1,)))
    logits = jnp.where(routed_to > 0.0, logits, -jnp.inf)
    picked = jnp.exp(logits - jnp.max(logits, axis=0, keepdims=True))
    gates_ref[...] = picked / jnp.sum(picked, axis=0, keepdims=True)

    @pl.loop(0, GROUP)
    def _(k):
        slots_arrived(
            outgoing,
            grads_ref,
            k // CHIPS,
            lax.rem(k // 4, 4),
            lax.rem(k, 4),
            slot_send,
            slot_recv,
        )

    slots_sent(outgoing, grads_ref, slot_send, slot_recv)

    @pl.loop(1, 4)
    def _(d):
        for copies in (
            line_step(d),
            core_step(d),
            pos_step(d),
            spread(d, cot_ref, tok_z, tok_x, first_send, first_recv),
        ):
            for copy in copies:
                copy.wait_send()

        @pl.loop(0, 4)
        def _(e):
            for copy in cross_step(e, d):
                copy.wait_send()

    @pl.loop(1, 4)
    def _(d):
        output_line(d).wait_send()
        output_cross(d).wait_send()
        output_plane(d).wait_send()

    output_core().wait_send()
    weights_out.wait()
    for copy in core_step(0):
        copy.wait_send()
    key_copy.wait_send()
    value_copy.wait_send()


def front(length, *arrays):
    f32, bf16, i32 = jnp.float32, jnp.bfloat16, jnp.int32
    vmem = pl.BlockSpec(memory_space=pltpu.VMEM)
    hbm = pl.BlockSpec(memory_space=pl.ANY)
    shape = jax.ShapeDtypeStruct
    out_shape = (
        shape((2, 4, 4, 32, 3 * D), bf16),
        shape((TOKENS, D), bf16),
        shape((D, TOKENS), bf16),
        shape((HALF, 2 * TOKENS), bf16),
        shape((HALF, 2 * TOKENS), bf16),
        shape((HEADS, TOKENS), f32),
        shape((TOKENS, D), bf16),
        shape((TOKENS, D), f32),
        shape((TOKENS, D), bf16),
        shape((EXPERTS, TOKENS), f32),
        shape((EXPERTS, TOKENS), i32),
        shape((4, 8, TOKENS), i32),
        shape((4, 8, TOKENS), i32),
        shape((2, 4, 4, CAP, D), bf16),
    )
    scratch = [
        pltpu.VMEM((2, 4, 4, 32, 3 * D), bf16),
        pltpu.VMEM((D, TOKENS), bf16),
        pltpu.VMEM((4, 8, TOKENS), i32),
        pltpu.VMEM((4, 8, TOKENS), i32),
        pltpu.VMEM((4, TOKENS, HALF), bf16),
        pltpu.VMEM((4, TOKENS, HALF), bf16),
        pltpu.VMEM((2, 4, 4, CAP, D), bf16),
    ]
    scratch += [pltpu.SemaphoreType.DMA((2,))]
    for count in (40, 12, 8, 2, 8, 2 * GROUP, 8):
        scratch += [pltpu.SemaphoreType.DMA((count,))] * 2
    return pl.pallas_call(
        front_kernel,
        out_shape=out_shape,
        in_specs=[pl.BlockSpec(memory_space=pltpu.SMEM)] + [vmem] * len(arrays),
        out_specs=[hbm] + [vmem] * (len(out_shape) - 2) + [hbm],
        scratch_shapes=scratch,
        compiler_params=pltpu.CompilerParams(
            collective_id=3, has_side_effects=True, vmem_limit_bytes=60 << 20
        ),
        name="front",
    )(length, *arrays)

def expert_kernel(
    routed_ref,
    pos_ref,
    posz_ref,
    posx_ref,
    gates_ref,
    grads_hbm,
    wg_hbm,
    wu_hbm,
    wd_hbm,
    rg_ref,
    gdot_ref,
    prod_hbm,
    grad_hbm,
    grads_ref,
    wg_ref,
    wu_ref,
    wd_ref,
    prod_ref,
    grad_ref,
    tok_z,
    tok_x,
    outgoing,
    arrived,
    going_back,
    mid,
    parts_out,
    parts_in,
    gate_out,
    gate_in,
    dot_out,
    dot_in,
    active,
    weighted,
    pre_grads,
    load_sem,
    store_sem,
    first_send,
    first_recv,
    slot_send,
    slot_recv,
    back_send,
    back_recv,
    part_send,
    part_recv,
    small_send,
    small_recv,
):
    y, r, x, z = place()
    f32, bf16 = jnp.float32, jnp.bfloat16
    loads = [
        pltpu.make_async_copy(source, target, load_sem.at[n])
        for n, (source, target) in enumerate(
            (
                (wg_hbm, wg_ref),
                (wu_hbm, wu_ref),
                (wd_hbm, wd_ref),
                (grads_hbm, grads_ref),
            )
        )
    ]
    for load in loads:
        load.start()
    meet(True, False)

    @pl.loop(1, 4)
    def _(d):
        for copy in spread(d, routed_ref, tok_z, tok_x, first_send, first_recv):
            copy.start()

    tok_z[0] = routed_ref[:, 0:HALF]
    tok_x[0] = routed_ref[:, HALF:D]

    def small(k, out, into, sign, base, arriving=False):
        there, dz, dx = k // CHIPS, lax.rem(k // 4, 4), lax.rem(k, 4)
        slot = k if arriving else r * CHIPS + lax.rem(k, CHIPS)
        return remote(
            out.at[k],
            into.at[slot],
            small_send.at[base + k],
            small_recv.at[base + slot],
            moved(sign * dx, sign * dz, there)[0],
        )

    def own_slot(k):
        return k == r * CHIPS

    @pl.loop(0, GROUP)
    def _(k):
        there, dz, dx = k // CHIPS, lax.rem(k // 4, 4), lax.rem(k, 4)
        _, expert = moved(dx, dz, there)
        chosen = picks(pos_ref[pl.ds(expert, 1), :])
        gate_col = jnp.sum(
            jnp.where(chosen, gates_ref[pl.ds(expert, 1), :], 0.0), axis=1, keepdims=True
        )
        gate_out[k, 0:1, 0:CAP] = as_row(gate_col)

        @pl.when(own_slot(k))
        def _():
            gate_in[k] = gate_out[k]

        @pl.when(jnp.logical_not(own_slot(k)))
        def _():
            small(k, gate_out, gate_in, 1, 0).start()

    @pl.loop(1, 4)
    def _(d):
        for copy in spread(d, routed_ref, tok_z, tok_x, first_send, first_recv):
            copy.wait_recv()

    @pl.loop(0, 4)
    def _(g):
        for dx in range(4):
            dz = lax.rem(dx + g, 4)
            left_rows, right_rows = [], []
            for core in range(2):
                at_x = core * 4 + lax.rem(x + dx, 4)
                at_z = core * 4 + lax.rem(z + dz, 4)
                left_rows.append(picks(posz_ref[dz, pl.ds(at_x, 1), :]))
                right_rows.append(picks(posx_ref[dx, pl.ds(at_z, 1), :]))
            left = dot(as_hot(jnp.concatenate(left_rows, axis=0)), tok_z[dz], ((1,), (0,)))
            right = dot(as_hot(jnp.concatenate(right_rows, axis=0)), tok_x[dx], ((1,), (0,)))
            for core in range(2):
                part = slice(core * CAP, core * CAP + CAP)
                outgoing[core, dz, dx, :, 0:HALF] = left[part].astype(bf16)
                outgoing[core, dz, dx, :, HALF:D] = right[part].astype(bf16)
                send_slots(outgoing, arrived, core, dz, dx, slot_send, slot_recv, 1)

    def keep_produced(k):
        core, dz, dx = k // CHIPS, lax.rem(k // 4, 4), lax.rem(k, 4)
        return pltpu.make_async_copy(
            prod_ref.at[core, dz, dx], prod_hbm.at[core, dz, dx], store_sem.at[k]
        )

    for load in loads:
        load.wait()

    @pl.loop(0, 8)
    def _(c):
        g, core = c // 2, lax.rem(c, 2)
        rows, gate_cols, grads = [], [], []
        for dx in range(4):
            dz = lax.rem(dx + g, 4)
            k = core * CHIPS + dz * 4 + dx
            slots_arrived(outgoing, arrived, core, dz, dx, slot_send, slot_recv)

            @pl.when(jnp.logical_not(own_slot(k)))
            def _():
                small(k, gate_out, gate_in, 1, 0, True).wait_recv()

            rows.append(arrived[core, dz, dx])
            gate_cols.append(as_column(gate_in[k, 0:1, 0:CAP]))
            grads.append(grads_ref[core, dz, dx])
        rows = jnp.concatenate(rows, axis=0)
        gate_cols = jnp.concatenate(gate_cols, axis=0)
        grads = jnp.concatenate(grads, axis=0).astype(f32)
        gate_pre = dot(rows, wg_ref[...], ((1,), (0,)))
        up_pre = dot(rows, wu_ref[...], ((1,), (0,)))
        gate_sig = jax.nn.sigmoid(gate_pre)
        gate_act = gate_pre * gate_sig
        act = (gate_act * up_pre).astype(bf16)
        produced = dot(act, wd_ref[...], ((1,), (0,))).astype(bf16).astype(f32)
        dots = jnp.sum(produced * grads, axis=1, keepdims=True)
        produced_grad = (gate_cols * grads).astype(bf16)
        act_grad = dot(produced_grad, wd_ref[...], ((1,), (1,))).astype(bf16).astype(f32)
        gate_grad = (
            act_grad * up_pre * gate_sig * (1.0 + gate_pre * (1.0 - gate_sig))
        ).astype(bf16)
        up_grad = (act_grad * gate_act).astype(bf16)
        row_grads = dot(gate_grad, wg_ref[...], ((1,), (1,)))
        row_grads = (row_grads + dot(up_grad, wu_ref[...], ((1,), (1,)))).astype(bf16)
        produced = (produced * gate_cols).astype(bf16)
        for dx in range(4):
            dz = lax.rem(dx + g, 4)
            k = core * CHIPS + dz * 4 + dx
            part = slice(dx * CAP, dx * CAP + CAP)
            going_back[core, dz, dx] = row_grads[part]
            send_slots(going_back, mid, core, dz, dx, back_send, back_recv, -1)
            dot_out[k, 0:1, 0:CAP] = as_row(dots[part])

            @pl.when(own_slot(k))
            def _():
                dot_in[k] = dot_out[k]

            @pl.when(jnp.logical_not(own_slot(k)))
            def _():
                small(k, dot_out, dot_in, -1, GROUP).start()

            prod_ref[core, dz, dx] = produced[part]
            keep_produced(k).start()
            active[core, dz, dx] = act[part]
            weighted[core, dz, dx] = produced_grad[part]
            pre_grads[core, dz, dx, :, 0:HALF] = gate_grad[part]
            pre_grads[core, dz, dx, :, HALF:D] = up_grad[part]

    all_rows = GROUP * CAP

    def keep_grads(n):
        return pltpu.make_async_copy(grad_ref.at[n], grad_hbm.at[n], store_sem.at[GROUP + n])

    @pl.loop(0, 2)
    def _(n):
        span = pl.ds(pl.multiple_of(n * 256, 256), 256)
        left = active[:, :, :, :, span].reshape(all_rows, 256)
        right = weighted[...].reshape(all_rows, D)
        part = dot(left, right, ((0,), (0,))).astype(bf16)
        for i in range(2):
            for h in range(2):
                rows = part[128 * i + 64 * h : 128 * i + 64 * h + 64]
                grad_ref[2 * n + i, h, 256:320, :] = rows[:, 0:HALF]
                grad_ref[2 * n + i, h, 320:384, :] = rows[:, HALF:D]

    fold_parts(
        parts_out,
        parts_in,
        mid,
        going_back,
        back_send,
        back_recv,
        posz_ref,
        posx_ref,
        part_send,
        part_recv,
    )

    @pl.loop(0, 4)
    def _(n):
        span = pl.ds(pl.multiple_of(n * 256, 256), 256)
        left = arrived[:, :, :, :, span].reshape(all_rows, 256)
        part = dot(left, pre_grads[...].reshape(all_rows, D), ((0,), (0,)))
        for h in range(2):
            rows = part[128 * h : 128 * h + 128].astype(bf16)
            grad_ref[n, h, 0:128, :] = rows[:, 0:HALF]
            grad_ref[n, h, 128:256, :] = rows[:, HALF:D]
        keep_grads(n).start()

    @pl.loop(0, GROUP)
    def _(k):
        @pl.when(jnp.logical_not(own_slot(k)))
        def _():
            small(k, dot_out, dot_in, -1, GROUP, True).wait_recv()

        there, dz, dx = k // CHIPS, lax.rem(k // 4, 4), lax.rem(k, 4)
        _, expert = moved(dx, dz, there)
        at = pl.ds(expert, 1)
        dots = as_column(dot_in[k, 0:1, 0:CAP])
        gdot_ref[at, :] = jnp.sum(
            jnp.where(picks(pos_ref[at, :]), dots, 0.0), axis=0, keepdims=True
        )

    parts_arrived(parts_out, parts_in, part_send, part_recv)
    rg_ref[...] = (parts_in[0].astype(f32) + parts_in[1].astype(f32)) + (
        parts_in[2].astype(f32) + parts_in[3].astype(f32)
    )
    @pl.loop(0, GROUP)
    def _(k):
        keep_produced(k).wait()

    @pl.loop(0, 4)
    def _(n):
        keep_grads(n).wait()

    slots_sent(outgoing, arrived, slot_send, slot_recv)
    slots_sent(going_back, mid, back_send, back_recv)
    parts_sent(parts_out, parts_in, part_send, part_recv)

    @pl.loop(1, 4)
    def _(d):
        for copy in spread(d, routed_ref, tok_z, tok_x, first_send, first_recv):
            copy.wait_send()

    @pl.loop(0, GROUP)
    def _(k):
        @pl.when(jnp.logical_not(own_slot(k)))
        def _():
            small(k, gate_out, gate_in, 1, 0).wait_send()
            small(k, dot_out, dot_in, -1, GROUP).wait_send()


def experts(*arrays):
    f32, bf16 = jnp.float32, jnp.bfloat16
    vmem = pl.BlockSpec(memory_space=pltpu.VMEM)
    hbm = pl.BlockSpec(memory_space=pl.ANY)
    shape = jax.ShapeDtypeStruct
    block = pltpu.VMEM((2, 4, 4, CAP, D), bf16)
    narrow = pltpu.VMEM((2, 4, 4, CAP, HALF), bf16)
    line = pltpu.VMEM((4, TOKENS, HALF), bf16)
    wide = pltpu.VMEM((4, TOKENS, D), bf16)
    little = pltpu.VMEM((GROUP, 8, 128), f32)
    scratch = [block]
    scratch += [pltpu.VMEM(w.shape, bf16) for w in arrays[-3:]]
    scratch += [block, pltpu.VMEM((4, 2, 384, HALF), bf16)]
    scratch += [line, line, block, block, block, block, wide, wide]
    scratch += [little] * 4 + [narrow, block, block]
    scratch += [pltpu.SemaphoreType.DMA((4,)), pltpu.SemaphoreType.DMA((GROUP + 4,))]
    for count in (8, 2 * GROUP, 2 * GROUP, 8, 2 * GROUP):
        scratch += [pltpu.SemaphoreType.DMA((count,))] * 2
    out_shape = (
        shape((TOKENS, D), f32),
        shape((EXPERTS, TOKENS), f32),
        shape((2, 4, 4, CAP, D), bf16),
        shape((4, 2, 384, HALF), bf16),
    )
    return pl.pallas_call(
        expert_kernel,
        out_shape=out_shape,
        in_specs=[vmem] * (len(arrays) - 4) + [hbm] * 4,
        out_specs=[vmem, vmem, hbm, hbm],
        scratch_shapes=scratch,
        compiler_params=pltpu.CompilerParams(
            collective_id=1, has_side_effects=True, vmem_limit_bytes=60 << 20
        ),
        name="experts",
    )(*arrays)


def turned_back(rows, cosine, sine):
    first, second = rows[0:32], rows[32:64]
    return jnp.concatenate(
        [first * cosine + second * sine, second * cosine - first * sine], axis=0
    )


def finish_kernel(
    length_ref,
    prod_ref,
    posz_ref,
    posx_ref,
    gates_ref,
    rg_ref,
    gdot_ref,
    expert_hbm,
    routed_ref,
    router_ref,
    middle_ref,
    cot_ref,
    hidden_ref,
    again_ref,
    mgain_ref,
    normed_ref,
    mixed_ref,
    w_hbm,
    q_ref,
    k_ref,
    v_ref,
    lse_ref,
    cos_ref,
    sin_ref,
    hout_ref,
    hgrad_ref,
    again_out,
    mgain_out,
    router_out,
    own_out,
    esum_hbm,
    w_ref,
    own_quarter,
    next_quarter,
    quarter_sum,
    mid,
    parts_out,
    parts_in,
    relay_in,
    relay_out,
    y_in,
    branch_own,
    branch_sib,
    normed_sib,
    mixed_sib,
    mg_t,
    grad_t,
    grad_sib,
    kv_own,
    kv_out,
    kv_in,
    weight_part,
    rs_in,
    rs_out,
    rs_in2,
    y_out,
    y_parts,
    small_out,
    small_in,
    small_y,
    small_y_in,
    gain_out,
    gain_in,
    gain_y,
    gain_y_in,
    router_all,
    load_sem,
    c_send,
    c_recv,
    part_send,
    part_recv,
    ex_send,
    ex_recv,
    sib_send,
    sib_recv,
    rs_send,
    rs_recv,
    rs_send2,
    rs_recv2,
    ys_send,
    ys_recv,
    sm_send,
    sm_recv,
):
    y, r, x, z = place()
    me = r * CHIPS + z * 4 + x
    sibling = moved(0, 0, 1 - r)[0]
    tokens = routed_ref.shape[0]
    f32, bf16 = jnp.float32, jnp.bfloat16

    above, below = plane_shift(1), plane_shift(3)
    opposite = plane_shift(2)[1]
    loads = [pltpu.make_async_copy(w_hbm, w_ref, load_sem.at[0])]
    loads.append(pltpu.make_async_copy(expert_hbm.at[y], own_quarter, load_sem.at[1]))
    for n in range(2):
        source = expert_hbm.at[(above, below)[n][1], n]
        loads.append(pltpu.make_async_copy(source, next_quarter.at[n], load_sem.at[2 + n]))
    for load in loads:
        load.start()
    meet(True, True)

    def relayed(n):
        device = (above, below)[n][0]
        return remote(
            expert_hbm.at[opposite, n], relay_in.at[n], ex_send.at[n], ex_recv.at[n], device
        )

    def direct(n):
        device, other = (above, below)[n]
        return remote(
            expert_hbm.at[other, 1 - n],
            y_in.at[n, 1 - n],
            ex_send.at[2 + n],
            ex_recv.at[2 + n],
            device,
        )

    def merged(n):
        device = (above, below)[n][0]
        return remote(
            relay_out.at[n], y_in.at[n, n], ex_send.at[4 + n], ex_recv.at[4 + n], device
        )

    def handed(n):
        device = (above, below)[n][0]
        return remote(
            quarter_sum, esum_hbm.at[y], ex_send.at[6 + n], ex_recv.at[6 + n], device
        )

    def passed_on(n):
        device, came_from = (above, below)[n][0], (below, above)[n][1]
        part = esum_hbm.at[came_from, n]
        return remote(part, part, ex_send.at[8 + n], ex_recv.at[8 + n], device)

    def weight(first, width):
        return w_ref[:, :, :, :, first : first + width].reshape(D, width)

    def to_sibling(at, src, dst):
        return remote(src, dst, sib_send.at[at], sib_recv.at[at], sibling)

    half = pl.ds(pl.multiple_of((1 - r) * HALF, HALF), HALF)
    sib_normed = to_sibling(0, normed_ref.at[:, half], normed_sib)
    sib_mixed = to_sibling(1, mixed_ref.at[:, half], mixed_sib)
    sib_branch = to_sibling(2, branch_own, branch_sib)

    def sib_keyval(p):
        return to_sibling(3 + p, kv_out.at[p], kv_in.at[p])

    def sib_grads(p, part):
        rows = pl.ds(p * D + part * HALF, HALF)
        return to_sibling(5 + 2 * p + part, grad_t.at[rows], grad_sib.at[rows])

    for n in range(2):
        relayed(n).start()
    sib_mixed.start()
    sib_normed.start()

    @pl.loop(0, CHIPS)
    def _(k):
        dx = lax.rem(k, 4)
        dz = lax.rem(dx + k // 4, 4)
        for core in range(2):
            send_slots(prod_ref, mid, core, dz, dx, c_send, c_recv, -1, c_send.at[2 * GROUP])

    gates = gates_ref[...]
    gdot = gdot_ref[...]
    logit_grad = gates * (gdot - jnp.sum(gates * gdot, axis=0, keepdims=True))
    high, rest = split_two(logit_grad)
    router_part = dot(high, routed_ref[...], ((1,), (0,)))
    router_part = router_part + dot(rest, routed_ref[...], ((1,), (0,)))
    routed_grad = dot(high, router_ref[...], ((0,), (0,)))
    routed_grad = routed_grad + dot(rest, router_ref[...], ((0,), (0,)))
    routed_grad = routed_grad + rg_ref[...]
    live = (
        r * tokens + lax.broadcasted_iota(jnp.int32, (tokens, 1), 0) < length_ref[0]
    ).astype(f32)
    middle = middle_ref[...]
    scale = lax.rsqrt(jnp.mean(middle * middle, axis=1, keepdims=True) + epsilon)
    rows = middle * scale
    moe_part = jnp.sum(routed_grad * rows, axis=0, keepdims=True)
    scaled = routed_grad * mgain_ref[...]
    inner = jnp.mean(scaled * rows, axis=1, keepdims=True)
    middle_grad = cot_ref[...].astype(f32) * live + scale * (scaled - rows * inner)
    hgrad_ref[...] = middle_grad
    branch_own[...] = middle_grad.astype(bf16)
    sib_branch.start()
    for j in range(8):
        part = slice(128 * j, 128 * j + 128)
        small_out[:, j, :] = router_part[:, part]
        small_out[:, 8 + j, :] = jnp.broadcast_to(moe_part[:, part], (GROUP, 128))

    def small(k):
        device, other = step_of(k, 1)
        return remote(small_out.at[other], small_in.at[me], sm_send.at[k], sm_recv.at[k], device)

    @pl.loop(1, GROUP)
    def _(k):
        small(k).start()

    small_in[me] = small_out[me]

    for n in range(2):
        direct(n).start()
    loads[0].wait()
    mg_t[...] = dot(weight(2 * D, D), branch_own[...], ((1,), (1,))).astype(bf16)

    mine = pl.ds(pl.multiple_of(r * HALF, HALF), HALF)

    def columns(p):
        return pl.ds(p * D, HALF), pl.ds(p * D + HALF, HALF)

    def first_step(p, d):
        left, right = columns(p)
        at = 8 * p + d
        return (
            remote(
                weight_part.at[lax.rem(z + d, 4), :, :, left],
                rs_in.at[d, :, :, left],
                rs_send.at[at],
                rs_recv.at[at],
                moved(0, d, r)[0],
            ),
            remote(
                weight_part.at[:, lax.rem(x + d, 4), :, right],
                rs_in.at[d, :, :, right],
                rs_send.at[4 + at],
                rs_recv.at[4 + at],
                moved(d, 0, r)[0],
            ),
        )

    def second_step(p, d):
        left, right = columns(p)
        at = 8 * p + d
        return (
            remote(
                rs_out.at[lax.rem(x + d, 4), :, left],
                rs_in2.at[d, :, left],
                rs_send2.at[at],
                rs_recv2.at[at],
                moved(d, 0, r)[0],
            ),
            remote(
                rs_out.at[lax.rem(z + d, 4), :, right],
                rs_in2.at[d, :, right],
                rs_send2.at[4 + at],
                rs_recv2.at[4 + at],
                moved(0, d, r)[0],
            ),
        )

    def across(p, n):
        cols = pl.ds(p * D, D)
        at = 3 * p + n - 1
        return remote(
            y_out.at[:, cols],
            y_parts.at[y, :, cols],
            ys_send.at[at],
            ys_recv.at[at],
            plane_shift(n)[0],
        )

    def sum_first(p, total):
        weight_part[:, :, :, p * D : p * D + D] = total.astype(bf16).reshape(4, 4, 32, D)

        @pl.loop(1, 4)
        def _(d):
            for copy in first_step(p, d):
                copy.start()

    def sum_second(p):
        left, right = columns(p)

        @pl.loop(1, 4)
        def _(d):
            for copy in first_step(p, d):
                copy.wait_recv()

        total = weight_part[z, :, :, left].astype(f32)
        other = weight_part[:, x, :, right].astype(f32)
        for d in range(1, 4):
            total = total + rs_in[d, :, :, left].astype(f32)
            other = other + rs_in[d, :, :, right].astype(f32)
        rs_out[:, :, left] = total.astype(bf16)
        rs_out[:, :, right] = other.astype(bf16)

        @pl.loop(1, 4)
        def _(d):
            for copy in second_step(p, d):
                copy.start()

    def sum_third(p):
        left, right = columns(p)

        @pl.loop(1, 4)
        def _(d):
            for copy in second_step(p, d):
                copy.wait_recv()

        total = rs_out[x, :, left].astype(f32)
        other = rs_out[z, :, right].astype(f32)
        for d in range(1, 4):
            total = total + rs_in2[d, :, left].astype(f32)
            other = other + rs_in2[d, :, right].astype(f32)
        y_out[:, left] = total.astype(bf16)
        y_out[:, right] = other.astype(bf16)
        y_parts[y, :, left] = total.astype(bf16)
        y_parts[y, :, right] = other.astype(bf16)
        for n in range(1, PLANES):
            across(p, n).start()

    sib_mixed.wait_recv()
    sib_branch.wait_recv()
    total = dot(mixed_ref[:, mine], branch_own[...], ((0,), (0,)))
    sum_first(2, total + dot(mixed_sib[...], branch_sib[...], ((0,), (0,))))

    key_live = lax.broadcasted_iota(jnp.int32, (2 * tokens, 1), 0) < length_ref[0]
    score_scale = HEAD ** (-0.5)
    cosine, sine = cos_ref[...], sin_ref[...]
    first_core = r == 0

    def key_head(p, i):
        g = 4 * p + i
        head = pl.ds(pl.multiple_of(g * HEAD, HEAD), HEAD)
        keys, values = k_ref[head, :], v_ref[head, :]
        key_sum, value_sum = None, None
        for j in range(2):
            at = pl.ds(pl.multiple_of((2 * g + j) * HEAD, HEAD), HEAD)
            query, mixed_grad = q_ref[at, :], mg_t[at, :]
            scores = dot(keys, query, ((0,), (0,))) * score_scale
            scores = jnp.where(key_live, scores, NEG)
            probs = jnp.exp(scores - lse_ref[pl.ds(2 * g + j, 1), :])
            prob_grad = dot(values, mixed_grad, ((0,), (0,)))
            value_part = dot(mixed_grad, probs.astype(bf16), ((1,), (1,)))
            inner = jnp.sum(probs * prob_grad, axis=0, keepdims=True)
            score_grad = (probs * (prob_grad - inner)).astype(bf16)
            key_part = dot(query, score_grad, ((1,), (1,)))
            query_grad = dot(keys, score_grad, ((1,), (0,))) * score_scale
            to = pl.ds(pl.multiple_of(p * D + (2 * i + j) * HEAD, HEAD), HEAD)
            grad_t[to, :] = turned_back(query_grad, cosine, sine).astype(bf16)
            key_sum = key_part if key_sum is None else key_sum + key_part
            value_sum = value_part if value_sum is None else value_sum + value_part
        key_sum = key_sum * score_scale
        for n, part in enumerate((key_sum, value_sum)):
            to = pl.ds(pl.multiple_of(256 * n + i * HEAD, HEAD), HEAD)
            kv_own[p, to, :] = jnp.where(first_core, part[:, :tokens], part[:, tokens:])
            away = jnp.where(first_core, part[:, tokens:], part[:, :tokens])
            kv_out[p, to, :] = away.astype(bf16)

    def heads(p, first, last):
        @pl.loop(first, last)
        def _(i):
            key_head(p, i)

    def whole_keyval(p):
        sib_keyval(p).wait_recv()
        for i in range(4):
            rows = slice(HEAD * i, HEAD * i + HEAD)
            total = kv_own[p, rows, :] + kv_in[p, rows, :].astype(f32)
            to = p * D + HALF + HEAD * i
            grad_t[to : to + HEAD, :] = turned_back(total, cosine, sine).astype(bf16)
        total = kv_own[p, 256:512, :] + kv_in[p, 256:512, :].astype(f32)
        grad_t[p * D + HALF + 256 : p * D + D, :] = total.astype(bf16)
        sib_grads(p, 1).start()

    def projections(p):
        rows = slice(p * D, p * D + D)
        for part in range(2):
            sib_grads(p, part).wait_recv()
        total = dot(normed_ref[:, mine], grad_t[rows, :], ((0,), (1,)))
        sum_first(p, total + dot(normed_sib[...], grad_sib[rows, :], ((0,), (1,))))

    def inputs_part(p):
        return dot(grad_t[p * D : p * D + D, :], weight(p * D, D), ((0,), (1,)))

    heads(0, 0, 4)
    sib_keyval(0).start()
    sib_grads(0, 0).start()

    for n in range(2):
        relayed(n).wait_recv()
        loads[2 + n].wait()
        total = relay_in[n].astype(f32) + next_quarter[n].astype(f32)
        relay_out[n] = total.astype(bf16)
        merged(n).start()

    heads(1, 0, 4)
    sib_keyval(1).start()
    sib_grads(1, 0).start()
    whole_keyval(0)
    sib_normed.wait_recv()
    projections(0)
    whole_keyval(1)
    normed_grad = inputs_part(0)
    projections(1)
    normed_grad = normed_grad + inputs_part(1)

    inputs = hidden_ref[...].astype(f32)
    scale = lax.rsqrt(jnp.mean(inputs * inputs, axis=1, keepdims=True) + epsilon)
    rows = inputs * scale
    attn_part = jnp.sum(normed_grad * rows, axis=0, keepdims=True)
    for j in range(8):
        gain_out[j : j + 1, :] = attn_part[:, 128 * j : 128 * j + 128]

    def gain(k):
        device, _ = step_of(k, 1)
        at = 3 * GROUP + k
        return remote(gain_out, gain_in.at[me], sm_send.at[at], sm_recv.at[at], device)

    @pl.loop(1, GROUP)
    def _(k):
        gain(k).start()

    gain_in[me] = gain_out[...]
    scaled = normed_grad * again_ref[...]
    inner = jnp.mean(scaled * rows, axis=1, keepdims=True)
    hgrad_ref[...] += scale * (scaled - rows * inner)

    loads[1].wait()
    for n in range(2):
        direct(n).wait_recv()
        merged(n).wait_recv()
    for n in range(2):
        total = own_quarter[n].astype(f32) + (y_in[0, n].astype(f32) + y_in[1, n].astype(f32))
        quarter_sum[n] = total.astype(bf16)
    quarter_out = pltpu.make_async_copy(quarter_sum, esum_hbm.at[y], load_sem.at[4])
    quarter_out.start()
    for n in range(2):
        handed(n).start()

    sum_second(2)

    @pl.loop(1, GROUP)
    def _(k):
        small(k).wait_recv()

    def small_across(n):
        device, _ = plane_shift(n)
        return remote(
            small_y, small_y_in.at[y], sm_send.at[GROUP + n], sm_recv.at[GROUP + n], device
        )

    small_y[...] = jnp.sum(small_in[...], axis=0)
    small_y_in[y] = small_y[...]
    for n in range(1, PLANES):
        small_across(n).start()

    fold_parts(
        parts_out,
        parts_in,
        mid,
        prod_ref,
        c_send,
        c_recv,
        posz_ref,
        posx_ref,
        part_send,
        part_recv,
    )
    sum_third(2)
    sum_second(0)

    for n in range(1, PLANES):
        small_across(n).wait_recv()
    totals = small_y_in[0] + small_y_in[1] + small_y_in[2] + small_y_in[3]
    mgain_out[...] = totals[8:16]
    router_all[me] = totals[0:8]

    def router_row(k):
        device, _ = step_of(k, 1)
        at = 2 * GROUP + k
        return remote(
            router_all.at[me], router_all.at[me], sm_send.at[at], sm_recv.at[at], device
        )

    @pl.loop(1, GROUP)
    def _(k):
        router_row(k).start()

    @pl.loop(1, GROUP)
    def _(k):
        gain(k).wait_recv()

    gain_y[...] = jnp.sum(gain_in[...], axis=0)
    gain_y_in[y] = gain_y[...]

    def gain_across(n):
        device, _ = plane_shift(n)
        at = 4 * GROUP + n
        return remote(gain_y, gain_y_in.at[y], sm_send.at[at], sm_recv.at[at], device)

    for n in range(1, PLANES):
        gain_across(n).start()

    sum_second(1)
    sum_third(0)

    for n in range(2):
        handed(n).wait_recv()
        passed_on(n).start()

    sum_third(1)

    parts_arrived(parts_out, parts_in, part_send, part_recv)
    mixture = (parts_in[0].astype(f32) + parts_in[1].astype(f32)) + (
        parts_in[2].astype(f32) + parts_in[3].astype(f32)
    )
    hout_ref[...] = ((middle_ref[...] + mixture) * live).astype(bf16)

    for n in range(1, PLANES):
        gain_across(n).wait_recv()
    again_out[...] = (gain_y_in[0] + gain_y_in[1]) + (gain_y_in[2] + gain_y_in[3])

    @pl.loop(1, GROUP)
    def _(k):
        router_row(k).wait_recv()

    router_out[...] = router_all[...]

    slots_sent(prod_ref, mid, c_send, c_recv)
    parts_sent(parts_out, parts_in, part_send, part_recv)

    @pl.loop(1, GROUP)
    def _(k):
        small(k).wait_send()
        router_row(k).wait_send()
        gain(k).wait_send()

    @pl.loop(1, 4)
    def _(d):
        for p in range(3):
            for copy in first_step(p, d) + second_step(p, d):
                copy.wait_send()

    for n in range(2):
        for copy in (relayed(n), direct(n), merged(n), handed(n), passed_on(n)):
            copy.wait_send()
    for copy in (sib_normed, sib_mixed, sib_branch):
        copy.wait_send()
    for p in range(2):
        sib_keyval(p).wait_send()
        for part in range(2):
            sib_grads(p, part).wait_send()
    for n in range(1, PLANES):
        small_across(n).wait_send()
        gain_across(n).wait_send()
        for p in range(3):
            across(p, n).wait()
    for n in range(2):
        passed_on(n).wait_recv()
    quarter_out.wait()
    own_out[...] = (y_parts[0].astype(f32) + y_parts[1].astype(f32)) + (
        y_parts[2].astype(f32) + y_parts[3].astype(f32)
    )


def finish(length, *arrays):
    tokens = TOKENS
    f32, bf16 = jnp.float32, jnp.bfloat16
    vmem = pl.BlockSpec(memory_space=pltpu.VMEM)
    shape = jax.ShapeDtypeStruct
    sems = pltpu.SemaphoreType.DMA
    in_specs = [pl.BlockSpec(memory_space=pltpu.SMEM)] + [vmem] * len(arrays)
    in_specs[1] = pl.BlockSpec(memory_space=pl.ANY)
    in_specs[7] = pl.BlockSpec(memory_space=pl.ANY)
    in_specs[17] = pl.BlockSpec(memory_space=pl.ANY)
    scratch = [
        pltpu.VMEM((2, 4, 4, 32, 3 * D), bf16),
        pltpu.VMEM((2, 384, HALF), bf16),
        pltpu.VMEM((2, 384, HALF), bf16),
        pltpu.VMEM((2, 384, HALF), bf16),
        pltpu.VMEM((2, 4, 4, CAP, D), bf16),
        pltpu.VMEM((4, tokens, D), bf16),
        pltpu.VMEM((4, tokens, D), bf16),
        pltpu.VMEM((2, 384, HALF), bf16),
        pltpu.VMEM((2, 384, HALF), bf16),
        pltpu.VMEM((2, 2, 384, HALF), bf16),
        pltpu.VMEM((tokens, D), bf16),
        pltpu.VMEM((tokens, D), bf16),
        pltpu.VMEM((tokens, HALF), bf16),
        pltpu.VMEM((tokens, HALF), bf16),
        pltpu.VMEM((D, tokens), bf16),
        pltpu.VMEM((2 * D, tokens), bf16),
        pltpu.VMEM((2 * D, tokens), bf16),
        pltpu.VMEM((2, HALF, tokens), f32),
        pltpu.VMEM((2, HALF, tokens), bf16),
        pltpu.VMEM((2, HALF, tokens), bf16),
        pltpu.VMEM((4, 4, 32, 3 * D), bf16),
        pltpu.VMEM((4, 4, 32, 3 * D), bf16),
        pltpu.VMEM((4, 32, 3 * D), bf16),
        pltpu.VMEM((4, 32, 3 * D), bf16),
        pltpu.VMEM((32, 3 * D), bf16),
        pltpu.VMEM((PLANES, 32, 3 * D), bf16),
        pltpu.VMEM((GROUP, 16, 128), f32),
        pltpu.VMEM((GROUP, 16, 128), f32),
        pltpu.VMEM((16, 128), f32),
        pltpu.VMEM((PLANES, 16, 128), f32),
        pltpu.VMEM((8, 128), f32),
        pltpu.VMEM((GROUP, 8, 128), f32),
        pltpu.VMEM((8, 128), f32),
        pltpu.VMEM((PLANES, 8, 128), f32),
        pltpu.VMEM((GROUP, 8, 128), f32),
        sems((5,)),
    ]
    for count in (2 * GROUP + 1, 8, 10, 9, 24, 24, 9, 5 * GROUP):
        scratch += [sems((count,)), sems((count,))]
    return pl.pallas_call(
        finish_kernel,
        out_shape=(
            shape((tokens, D), bf16),
            shape((tokens, D), f32),
            shape((8, 128), f32),
            shape((8, 128), f32),
            shape((GROUP, 8, 128), f32),
            shape((32, 3 * D), f32),
            shape((4, 2, 384, HALF), bf16),
        ),
        in_specs=in_specs,
        out_specs=[vmem] * 6 + [pl.BlockSpec(memory_space=pl.ANY)],
        scratch_shapes=scratch,
        compiler_params=pltpu.CompilerParams(
            collective_id=2, has_side_effects=True, vmem_limit_bytes=60 << 20
        ),
        name="finish",
    )(length, *arrays)


def spread_kernel(
    hout_ref,
    hgrad_ref,
    own_ref,
    esum_ref,
    router_ref,
    hout_out,
    hgrad_out,
    q_out,
    k_out,
    v_out,
    o_out,
    gate_out,
    up_out,
    down_out,
    router_out,
):
    f32 = jnp.float32
    hout_out[...] = hout_ref[...]
    hgrad_out[...] = hgrad_ref[...]
    for p in range(2):
        q_out[:, p * HALF : p * HALF + HALF] = own_ref[:, p * D : p * D + HALF]
        k_out[:, p * 256 : p * 256 + 256] = own_ref[:, p * D + HALF : p * D + 768]
        v_out[:, p * 256 : p * 256 + 256] = own_ref[:, p * D + 768 : p * D + D]
    o_out[...] = own_ref[:, 2 * D : 3 * D]
    for h in range(2):
        gate_out[0, 128 * h : 128 * h + 128, :] = esum_ref[0, h, 0:128, :].astype(f32)
        up_out[0, 128 * h : 128 * h + 128, :] = esum_ref[0, h, 128:256, :].astype(f32)
        down_out[0, 64 * h : 64 * h + 64, 0:HALF] = esum_ref[0, h, 256:320, :].astype(f32)
        down_out[0, 64 * h : 64 * h + 64, HALF:D] = esum_ref[0, h, 320:384, :].astype(f32)
    for j in range(8):
        router_out[128 * j : 128 * j + 128, :] = router_ref[:, j, :].T


def spread_out(*arrays):
    f32, bf16 = jnp.float32, jnp.bfloat16
    shape = jax.ShapeDtypeStruct

    def whole(*dims):
        return pl.BlockSpec(dims, lambda i: (0,) * len(dims))

    def rows(count, width):
        return pl.BlockSpec((count, width), lambda i: (i, 0))

    def expert_rows(count, width):
        return pl.BlockSpec((1, count, width), lambda i: (0, i, 0))

    return pl.pallas_call(
        spread_kernel,
        grid=(4,),
        out_shape=(
            shape((TOKENS, D), bf16),
            shape((TOKENS, D), f32),
            shape((32, D), f32),
            shape((32, HALF), f32),
            shape((32, HALF), f32),
            shape((32, D), f32),
            shape((1, D, HALF), f32),
            shape((1, D, HALF), f32),
            shape((1, HALF, D), f32),
            shape((D, EXPERTS), f32),
        ),
        in_specs=[
            rows(64, D),
            rows(64, D),
            whole(32, 3 * D),
            pl.BlockSpec((1, 2, 384, HALF), lambda i: (i, 0, 0, 0)),
            whole(GROUP, 8, 128),
        ],
        out_specs=[
            rows(64, D),
            rows(64, D),
            whole(32, D),
            whole(32, HALF),
            whole(32, HALF),
            whole(32, D),
            expert_rows(256, HALF),
            expert_rows(256, HALF),
            expert_rows(128, D),
            whole(D, EXPERTS),
        ],
        name="spread_out",
    )(*arrays)


def on_device(
    hidden_in,
    cotangent,
    lengths,
    routes,
    priority,
    attn_gain,
    query_weight,
    key_weight,
    value_weight,
    output_weight,
    moe_gain,
    router,
    gate_weight,
    up_weight,
    down_weight,
):
    tok_count = hidden_in.shape[0]
    positions = lax.axis_index("row") * tok_count + jnp.arange(tok_count, dtype=jnp.int32)
    half_dim = HEAD // 2
    frequency = rotary_base ** (-jnp.arange(half_dim, dtype=jnp.float32) / half_dim)
    angles = frequency[:, None] * positions.astype(jnp.float32)[None, :]
    cosine, sine = jnp.cos(angles), jnp.sin(angles)
    router_t = router.T
    (
        weights,
        normed,
        queries,
        keys,
        values,
        log_total,
        mixed_rows,
        middle,
        routed,
        gates,
        pos,
        posz,
        posx,
        arrived_grad,
    ) = front(
        lengths,
        hidden_in,
        cotangent,
        routes,
        priority.reshape(tok_count, TOP),
        attn_gain[None],
        moe_gain[None],
        query_weight,
        key_weight,
        value_weight,
        output_weight,
        router_t,
        cosine,
        sine,
    )
    returned_rows, gate_dot, produced, expert_grads = experts(
        routed,
        pos,
        posz,
        posx,
        gates,
        arrived_grad,
        gate_weight[0],
        up_weight[0],
        down_weight[0],
    )
    (
        hidden_out,
        hidden_grad,
        attn_gain_sum,
        moe_gain_sum,
        router_sum,
        own_rows,
        expert_sum,
    ) = finish(
        lengths,
        produced,
        posz,
        posx,
        gates,
        returned_rows,
        gate_dot,
        expert_grads,
        routed,
        router_t,
        middle,
        cotangent,
        hidden_in,
        attn_gain[None],
        moe_gain[None],
        normed,
        mixed_rows,
        weights,
        queries,
        keys,
        values,
        log_total,
        cosine,
        sine,
    )
    (
        hidden_out,
        hidden_grad,
        query_grad,
        key_grad,
        value_grad,
        output_grad,
        gate_grad,
        up_grad,
        down_grad,
        router_grad,
    ) = spread_out(hidden_out, hidden_grad, own_rows, expert_sum, router_sum)
    return (
        hidden_out,
        hidden_grad,
        attn_gain_sum.reshape(D),
        query_grad,
        key_grad,
        value_grad,
        output_grad,
        moe_gain_sum.reshape(D),
        router_grad,
        gate_grad,
        up_grad,
        down_grad,
    )


def solution(mesh):
    return jax.shard_map(
        on_device,
        mesh=mesh,
        in_specs=(
            P(("dp", "col", "row"), None),
            P(("dp", "col", "row"), None),
            P(("dp", "col")),
            P(("dp", "col", "row"), None),
            P(("dp", "col", "row"), None),
            P(),
            P(("row", "col"), None),
            P(("row", "col"), None),
            P(("row", "col"), None),
            P(("row", "col"), None),
            P(),
            P(),
            P(("row", "col"), None, None),
            P(("row", "col"), None, None),
            P(("row", "col"), None, None),
        ),
        out_specs=(
            P(("dp", "col", "row"), None),
            P(("dp", "col", "row"), None),
            P(),
            P(("row", "col"), None),
            P(("row", "col"), None),
            P(("row", "col"), None),
            P(("row", "col"), None),
            P(),
            P(),
            P(("row", "col"), None, None),
            P(("row", "col"), None, None),
            P(("row", "col"), None, None),
        ),
        check_vma=False,
    )
```

```python
import jax
import jax.numpy as jnp
from jax import lax
from jax.experimental import pallas as pl
from jax.experimental.pallas import tpu as pltpu
from jax.sharding import PartitionSpec as P

D = 1024
HEADS = 16
HEAD = 64
KV_HEADS = 8
EXPERTS = 32
TOP = 8
CAP = 64


epsilon = 1e-05
rotary_base = 10000.0


MESH = pl.DeviceIdType.MESH
GROUP = 32
PLANES = 4
CHIPS = 16
HALF = D // 2
TOKENS = 256
NEG = -1000000000.0


def place():
    col = lax.axis_index("col")
    return lax.axis_index("dp"), lax.axis_index("row"), lax.rem(col, 4), col // 4


def moved(dx, dz, core):
    y, r, x, z = place()
    col = lax.rem(z + dz + 4, 4) * 4 + lax.rem(x + dx + 4, 4)
    return (y, core, col), core * CHIPS + col


def plane_shift(n):
    y, r, x, z = place()
    other = lax.rem(y + n, PLANES)
    return (other, r, z * 4 + x), other


def step_of(k, sign):
    y, r, x, z = place()
    return moved(sign * lax.rem(k, 4), sign * lax.rem(k // 4, 4), lax.rem(r + k // CHIPS, 2))


def remote(src, dst, send_sem, recv_sem, device):
    return pltpu.make_async_remote_copy(
        src_ref=src,
        dst_ref=dst,
        send_sem=send_sem,
        recv_sem=recv_sem,
        device_id=device,
        device_id_type=MESH,
    )


def meet(plane, planes):
    barrier = pltpu.get_barrier_semaphore()
    y, r, x, z = place()

    def greet(device):
        pl.semaphore_signal(barrier, inc=1, device_id=device, device_id_type=MESH)

    if plane:

        @pl.loop(1, GROUP)
        def _(k):
            greet(step_of(k, 1)[0])

        count = GROUP - 1
    else:
        for core in range(2):

            @pl.loop(1, 4)
            def _(d):
                greet(moved(d, 0, core)[0])
                greet(moved(0, d, core)[0])

        greet(moved(0, 0, 1 - r)[0])
        count = 13
    if planes:
        for n in range(1, PLANES):
            greet(plane_shift(n)[0])
        count += PLANES - 1
    pl.semaphore_wait(barrier, count)


def eye(n):
    return lax.broadcasted_iota(jnp.int32, (n, n), 0) == lax.broadcasted_iota(
        jnp.int32, (n, n), 1
    )


def as_row(column):
    return jnp.sum(jnp.where(eye(column.shape[0]), column, 0.0), axis=0, keepdims=True)


def as_column(row_vec):
    return jnp.sum(jnp.where(eye(row_vec.shape[1]), row_vec, 0.0), axis=1, keepdims=True)


def dot(a, b, dims):
    return lax.dot_general(a, b, (dims, ((), ())), preferred_element_type=jnp.float32)


def split_two(values):
    high = values.astype(jnp.bfloat16)
    return high, (values - high.astype(jnp.float32)).astype(jnp.bfloat16)


def picks(positions):
    slots = lax.broadcasted_iota(jnp.int32, (CAP, positions.shape[1]), 0)
    return slots == positions


def as_hot(mask):
    return mask.astype(jnp.float32).astype(jnp.bfloat16)


LEFT = pl.ds(0, HALF)
RIGHT = pl.ds(HALF, HALF)


def spread(d, source, tok_z, tok_x, send_sem, recv_sem):
    y, r, x, z = place()
    return (
        remote(
            source.at[:, LEFT], tok_z.at[d], send_sem.at[d], recv_sem.at[d], moved(0, d, r)[0]
        ),
        remote(
            source.at[:, RIGHT],
            tok_x.at[d],
            send_sem.at[4 + d],
            recv_sem.at[4 + d],
            moved(d, 0, r)[0],
        ),
    )


def slot_copies(out, into, core, there, dz, dx, send_sem, recv_sem, sign):
    y, r, x, z = place()
    at = there * CHIPS + dz * 4 + dx
    to = core * CHIPS + dz * 4 + dx
    return (
        lambda: remote(
            out.at[there, dz, dx, :, LEFT],
            into.at[core, dz, dx, :, LEFT],
            send_sem.at[at],
            recv_sem.at[to],
            moved(sign * dx, 0, there)[0],
        ),
        lambda: remote(
            out.at[there, dz, dx, :, RIGHT],
            into.at[core, dz, dx, :, RIGHT],
            send_sem.at[GROUP + at],
            recv_sem.at[GROUP + to],
            moved(0, sign * dz, there)[0],
        ),
    )


def is_local(core, offset):
    y, r, x, z = place()
    return (core == r) & (offset == 0)


def send_slots(out, into, there, dz, dx, send_sem, recv_sem, sign, local_sem=None):
    y, r, x, z = place()

    def keep(cols):
        source, target = out.at[there, dz, dx, :, cols], into.at[r, dz, dx, :, cols]
        if local_sem is None:
            target[...] = source[...]
        else:
            copy = pltpu.make_async_copy(source, target, local_sem)
            copy.start()
            copy.wait()

    left, right = slot_copies(out, into, r, there, dz, dx, send_sem, recv_sem, sign)

    @pl.when(jnp.logical_not(is_local(there, dx)))
    def _():
        left().start()

    @pl.when(is_local(there, dx))
    def _():
        keep(LEFT)

    @pl.when(jnp.logical_not(is_local(there, dz)))
    def _():
        right().start()

    @pl.when(is_local(there, dz))
    def _():
        keep(RIGHT)


def slots_arrived(out, into, core, dz, dx, send_sem, recv_sem, left=True, right=True):
    copies = slot_copies(out, into, core, core, dz, dx, send_sem, recv_sem, 1)
    for copy, offset, wanted in zip(copies, (dx, dz), (left, right)):
        if wanted:

            @pl.when(jnp.logical_not(is_local(core, offset)))
            def _():
                copy().wait_recv()


def block_sent(out, into, there, dz, dx, send_sem, recv_sem):
    copies = slot_copies(out, into, there, there, dz, dx, send_sem, recv_sem, 1)
    for copy, offset in zip(copies, (dx, dz)):

        @pl.when(jnp.logical_not(is_local(there, offset)))
        def _():
            copy().wait_send()


def slots_sent(out, into, send_sem, recv_sem):
    @pl.loop(0, GROUP)
    def _(k):
        block_sent(out, into, k // CHIPS, lax.rem(k // 4, 4), lax.rem(k, 4), send_sem, recv_sem)


def line_rows(line, d, axis):
    y, r, x, z = place()
    own = x if axis == 0 else z
    return [
        line[d, pl.ds(core * 4 + lax.rem(own + i, 4), 1), :] for core in range(2) for i in range(4)
    ]


def line_hot(line, d, axis):
    return as_hot(jnp.concatenate([picks(p) for p in line_rows(line, d, axis)], axis=0))


def add_up(mid, line, d, axis):
    if axis == 0:
        rows = mid[:, d, :, :, 0:HALF]
    else:
        rows = mid[:, :, d, :, HALF:D]
    return dot(line_hot(line, d, axis), rows.reshape(8 * CAP, HALF), ((0,), (0,))).astype(
        jnp.bfloat16
    )


def part_copies(d, out, into, send_sem, recv_sem):
    y, r, x, z = place()
    return (
        lambda: remote(
            out.at[d, :, LEFT],
            into.at[d, :, LEFT],
            send_sem.at[d],
            recv_sem.at[d],
            moved(0, -d, r)[0],
        ),
        lambda: remote(
            out.at[d, :, RIGHT],
            into.at[d, :, RIGHT],
            send_sem.at[4 + d],
            recv_sem.at[4 + d],
            moved(-d, 0, r)[0],
        ),
    )


def fold_parts(out, into, mid, slots, slot_send, slot_recv, posz_ref, posx_ref, send_sem, recv_sem):
    @pl.loop(0, 4)
    def _(d):
        if slots is not None:
            for core in range(2):
                for i in range(4):
                    slots_arrived(slots, mid, core, d, i, slot_send, slot_recv, right=False)
        left = add_up(mid, posz_ref, d, 0)

        @pl.when(d == 0)
        def _():
            into[0, :, 0:HALF] = left

        @pl.when(d != 0)
        def _():
            out[d, :, 0:HALF] = left
            part_copies(d, out, into, send_sem, recv_sem)[0]().start()

        if slots is not None:
            for core in range(2):
                for i in range(4):
                    slots_arrived(slots, mid, core, i, d, slot_send, slot_recv, left=False)
        right = add_up(mid, posx_ref, d, 1)

        @pl.when(d == 0)
        def _():
            into[0, :, HALF:D] = right

        @pl.when(d != 0)
        def _():
            out[d, :, HALF:D] = right
            part_copies(d, out, into, send_sem, recv_sem)[1]().start()


def parts_arrived(out, into, send_sem, recv_sem):
    @pl.loop(1, 4)
    def _(d):
        for copy in part_copies(d, out, into, send_sem, recv_sem):
            copy().wait_recv()


def parts_sent(out, into, send_sem, recv_sem):
    @pl.loop(1, 4)
    def _(d):
        for copy in part_copies(d, out, into, send_sem, recv_sem):
            copy().wait_send()

def front_kernel(
    length_ref,
    hidden_ref,
    cot_ref,
    routes_ref,
    prio_ref,
    again_ref,
    mgain_ref,
    wq_ref,
    wk_ref,
    wv_ref,
    wo_ref,
    router_ref,
    cos_ref,
    sin_ref,
    w_hbm,
    normed_ref,
    q_ref,
    k_ref,
    v_ref,
    lse_ref,
    mixed_ref,
    middle_ref,
    routed_ref,
    gates_ref,
    pos_ref,
    posz_ref,
    posx_ref,
    grads_ref,
    w_ref,
    mixed_t,
    posz_out,
    posx_out,
    tok_z,
    tok_x,
    outgoing,
    store_sem,
    w_send,
    w_recv,
    o_send,
    o_recv,
    core_send,
    core_recv,
    kv_send,
    kv_recv,
    first_send,
    first_recv,
    slot_send,
    slot_recv,
    pos_send,
    pos_recv,
):
    y, r, x, z = place()
    f32, bf16 = jnp.float32, jnp.bfloat16
    sibling = moved(0, 0, 1 - r)[0]
    meet(False, True)

    for p in range(2):
        part = slice(256 * p, 256 * p + 256)
        w_ref[r, z, x, :, D * p : D * p + HALF] = wq_ref[:, HALF * p : HALF * p + HALF]
        w_ref[r, z, x, :, D * p + HALF : D * p + 768] = wk_ref[:, part]
        w_ref[r, z, x, :, D * p + 768 : D * p + D] = wv_ref[:, part]
    front, rear, output = pl.ds(0, D), pl.ds(D, D), pl.ds(2 * D, D)
    quarter = pl.ds(pl.multiple_of(2 * D + 256 * y, 256), 256)

    def line_step(d):
        mine_q, mine_o = w_ref.at[r, z, x, :, front], w_ref.at[r, z, x, :, rear]
        return (
            remote(mine_q, mine_q, w_send.at[d], w_recv.at[d], moved(0, d, r)[0]),
            remote(mine_o, mine_o, w_send.at[4 + d], w_recv.at[4 + d], moved(d, 0, r)[0]),
        )

    def cross_step(e, d):
        at = 8 + 4 * e + d
        from_z = w_ref.at[r, lax.rem(z - e + 4, 4), x, :, front]
        from_x = w_ref.at[r, z, lax.rem(x - e + 4, 4), :, rear]
        return (
            remote(from_z, from_z, w_send.at[at], w_recv.at[at], moved(d, 0, r)[0]),
            remote(from_x, from_x, w_send.at[16 + at], w_recv.at[16 + at], moved(0, d, r)[0]),
        )

    w_ref[r, z, x, :, quarter] = wo_ref[:, pl.ds(pl.multiple_of(256 * y, 256), 256)]

    def output_line(d):
        own = w_ref.at[r, z, x, :, quarter]
        return remote(own, own, o_send.at[d], o_recv.at[d], moved(0, d, r)[0])

    def output_cross(d):
        own = w_ref.at[r, :, x, :, quarter]
        return remote(own, own, o_send.at[4 + d], o_recv.at[4 + d], moved(d, 0, r)[0])

    def output_plane(n):
        own = w_ref.at[r, :, :, :, quarter]
        return remote(own, own, o_send.at[8 + n], o_recv.at[8 + n], plane_shift(n)[0])

    def output_core():
        own = w_ref.at[r, :, :, :, output]
        return remote(own, own, o_send.at[0], o_recv.at[0], sibling)

    def core_step(d):
        from_x = w_ref.at[r, :, lax.rem(x - d + 4, 4), :, front]
        from_z = w_ref.at[r, lax.rem(z - d + 4, 4), :, :, rear]
        return (
            remote(from_x, from_x, core_send.at[d], core_recv.at[d], sibling),
            remote(from_z, from_z, core_send.at[4 + d], core_recv.at[4 + d], sibling),
        )

    @pl.loop(1, 4)
    def _(d):
        for copy in line_step(d):
            copy.start()

    @pl.loop(1, 4)
    def _(d):
        for copy in cross_step(0, d):
            copy.start()
        output_line(d).start()

    tokens = hidden_ref.shape[0]
    experts_iota = lax.broadcasted_iota(jnp.int32, (EXPERTS, tokens), 0).astype(f32)
    live = r * tokens + lax.broadcasted_iota(jnp.int32, (1, tokens), 1) < length_ref[0]
    routed_to = jnp.zeros((EXPERTS, tokens), f32)
    ranks = jnp.zeros((EXPERTS, tokens), f32)
    prio = prio_ref[...]
    lines = jnp.concatenate([prio[:, 128 * i : 128 * i + 128] for i in range(CHIPS)], axis=0)
    token = lax.broadcasted_iota(jnp.int32, (tokens, CHIPS), 0) // CHIPS
    owner = (token == lax.broadcasted_iota(jnp.int32, (tokens, CHIPS), 1)).astype(f32)
    token = lax.rem(lax.broadcasted_iota(jnp.int32, (tokens, 128), 0), CHIPS)
    lane = lax.broadcasted_iota(jnp.int32, (tokens, 128), 1)
    place_of = lax.rem(lax.broadcasted_iota(jnp.int32, (TOP, 128), 1), TOP)
    place_of = (place_of == lax.broadcasted_iota(jnp.int32, (TOP, 128), 0)).astype(f32)
    priority = jnp.zeros((TOP, tokens), f32)
    for unit, part in ((64.0, lines // 64), (1.0, lax.rem(lines, 64))):
        part = part.astype(f32).astype(bf16)
        rows = dot(owner.astype(bf16), part, ((1,), (0,)))
        rows = jnp.where(lane // TOP == token, rows, 0.0).astype(bf16)
        priority = priority + unit * dot(place_of.astype(bf16), rows, ((1,), (1,)))
    routes = routes_ref[...].astype(f32)
    for j in range(TOP):
        match = experts_iota == routes[j : j + 1, :]
        routed_to = jnp.where(match, 1.0, routed_to)
        ranks = jnp.where(match, priority[j : j + 1, :], ranks)
    far = float(1 << 20)
    ranks = jnp.where((routed_to > 0.0) & live, ranks, far)
    ranks_t = ranks.T
    rows = []
    for e in range(EXPERTS):
        earlier = ranks_t[:, e : e + 1] < ranks[e : e + 1, :]
        rows.append(jnp.sum(earlier.astype(f32), axis=0, keepdims=True))
    slots = jnp.concatenate(rows, axis=0)
    pos = jnp.where((ranks < far) & (slots < CAP), slots, -1.0).astype(jnp.int32)
    pos_ref[...] = pos
    for core in range(2):
        for i in range(4):
            at = core * CHIPS + 4 * i
            posz_out[i, 4 * core : 4 * core + 4, :] = pos[at : at + 4, :]
            for j in range(4):
                posx_out[j, 4 * core + i : 4 * core + i + 1, :] = pos[at + j : at + j + 1, :]
    posz_ref[0] = posz_out[z]
    posx_ref[0] = posx_out[x]
    tok_z[0] = cot_ref[:, 0:HALF]
    tok_x[0] = cot_ref[:, HALF:D]

    def pos_step(d):
        to_z, to_x = lax.rem(z + d, 4), lax.rem(x + d, 4)
        return (
            remote(
                posz_out.at[to_z],
                posz_ref.at[d],
                pos_send.at[d],
                pos_recv.at[d],
                moved(0, d, r)[0],
            ),
            remote(
                posx_out.at[to_x],
                posx_ref.at[d],
                pos_send.at[4 + d],
                pos_recv.at[4 + d],
                moved(d, 0, r)[0],
            ),
        )

    @pl.loop(1, 4)
    def _(d):
        for copy in pos_step(d):
            copy.start()

    @pl.loop(1, 4)
    def _(d):
        output_line(d).wait_recv()

    @pl.loop(1, 4)
    def _(d):
        output_cross(d).start()

    @pl.loop(1, 4)
    def _(e):
        for copy in line_step(e):
            copy.wait_recv()

        @pl.loop(1, 4)
        def _(d):
            for copy in cross_step(e, d):
                copy.start()

    @pl.loop(1, 4)
    def _(d):
        for copy in spread(d, cot_ref, tok_z, tok_x, first_send, first_recv):
            copy.start()

    for copy in core_step(0):
        copy.start()

    inputs = hidden_ref[...].astype(f32)
    scale = lax.rsqrt(jnp.mean(inputs * inputs, axis=1, keepdims=True) + epsilon)
    normed_ref[...] = (inputs * scale * again_ref[...]).astype(bf16)

    @pl.loop(1, 4)
    def _(d):
        for copy in spread(d, cot_ref, tok_z, tok_x, first_send, first_recv):
            copy.wait_recv()
        for copy in pos_step(d):
            copy.wait_recv()

    @pl.loop(0, 4)
    def _(d):
        left = dot(line_hot(posz_ref, d, 0), tok_z[d], ((1,), (0,))).astype(bf16)
        right = dot(line_hot(posx_ref, d, 1), tok_x[d], ((1,), (0,))).astype(bf16)
        for core in range(2):
            for i in range(4):
                part = slice((core * 4 + i) * CAP, (core * 4 + i + 1) * CAP)
                outgoing[core, d, i, :, 0:HALF] = left[part]
                outgoing[core, i, d, :, HALF:D] = right[part]

    @pl.loop(1, 4)
    def _(d):
        output_cross(d).wait_recv()

    for n in range(1, PLANES):
        output_plane(n).start()

    @pl.loop(1, 4)
    def _(d):
        @pl.loop(0, 4)
        def _(e):
            for copy in cross_step(e, d):
                copy.wait_recv()

        for copy in core_step(d):
            copy.start()

    @pl.loop(0, CHIPS)
    def _(k):
        dx = lax.rem(k, 4)
        dz = lax.rem(dx + k // 4, 4)
        for core in range(2):
            send_slots(
                outgoing, grads_ref, core, dz, dx, slot_send, slot_recv, 1, store_sem.at[1]
            )

    @pl.loop(0, 4)
    def _(d):
        for copy in core_step(d):
            copy.wait_recv()

    cosine, sine = cos_ref[...], sin_ref[...]
    here = pl.ds(pl.multiple_of(r * tokens, tokens), tokens)

    def projected(first):
        weight = w_ref[:, :, :, :, first : first + HALF].reshape(D, HALF)
        return dot(normed_ref[...], weight, ((1,), (0,))).T

    def turned(rows):
        parts = []
        for h in range(rows.shape[0] // HEAD):
            first, second = rows[HEAD * h : HEAD * h + 32], rows[HEAD * h + 32 : HEAD * h + HEAD]
            parts += [first * cosine - second * sine, second * cosine + first * sine]
        return jnp.concatenate(parts, axis=0).astype(bf16)

    key_copy = remote(
        k_ref.at[:, here], k_ref.at[:, here], kv_send.at[0], kv_recv.at[0], sibling
    )
    value_copy = remote(
        v_ref.at[:, here], v_ref.at[:, here], kv_send.at[1], kv_recv.at[1], sibling
    )
    for p in range(2):
        both = projected(D * p + HALF)
        k_ref[256 * p : 256 * p + 256, here] = turned(both[0:256])
        v_ref[256 * p : 256 * p + 256, here] = both[256:512].astype(bf16)
    key_copy.start()
    value_copy.start()
    for p in range(2):
        q_ref[HALF * p : HALF * p + HALF, :] = turned(projected(D * p))

    key_copy.wait_recv()
    value_copy.wait_recv()

    for n in range(1, PLANES):
        output_plane(n).wait_recv()
    output_core().start()

    key_live = lax.broadcasted_iota(jnp.int32, (2 * tokens, 1), 0) < length_ref[0]
    score_scale = HEAD ** (-0.5)

    @pl.loop(0, KV_HEADS)
    def _(g):
        head = pl.ds(pl.multiple_of(g * HEAD, HEAD), HEAD)
        keys, values = k_ref[head, :], v_ref[head, :]
        for j in range(2):
            at = pl.ds(pl.multiple_of((2 * g + j) * HEAD, HEAD), HEAD)
            scores = dot(keys, q_ref[at, :], ((0,), (0,))) * score_scale
            scores = jnp.where(key_live, scores, NEG)
            top = jnp.max(scores, axis=0, keepdims=True)
            weights = jnp.exp(scores - top)
            total = jnp.sum(weights, axis=0, keepdims=True)
            lse_ref[pl.ds(2 * g + j, 1), :] = top + jnp.log(total)
            probs = (weights * (1.0 / total)).astype(bf16)
            mixed_t[at, :] = dot(values, probs, ((1,), (0,))).astype(bf16)

    mixed_ref[...] = mixed_t[...].T
    output_core().wait_recv()
    weights_out = pltpu.make_async_copy(w_ref, w_hbm, store_sem.at[0])
    weights_out.start()
    w_out = w_ref[:, :, :, :, 2 * D : 3 * D].reshape(D, D)
    middle = hidden_ref[...].astype(f32) + dot(mixed_ref[...], w_out, ((1,), (0,)))
    middle_ref[...] = middle
    scale = lax.rsqrt(jnp.mean(middle * middle, axis=1, keepdims=True) + epsilon)
    routed_ref[...] = (middle * scale * mgain_ref[...]).astype(bf16)
    logits = dot(router_ref[...], routed_ref[...], ((1,), (1,)))
    logits = jnp.where(routed_to > 0.0, logits, -jnp.inf)
    picked = jnp.exp(logits - jnp.max(logits, axis=0, keepdims=True))
    gates_ref[...] = picked / jnp.sum(picked, axis=0, keepdims=True)

    @pl.loop(0, GROUP)
    def _(k):
        slots_arrived(
            outgoing,
            grads_ref,
            k // CHIPS,
            lax.rem(k // 4, 4),
            lax.rem(k, 4),
            slot_send,
            slot_recv,
        )

    slots_sent(outgoing, grads_ref, slot_send, slot_recv)

    @pl.loop(1, 4)
    def _(d):
        for copies in (
            line_step(d),
            core_step(d),
            pos_step(d),
            spread(d, cot_ref, tok_z, tok_x, first_send, first_recv),
        ):
            for copy in copies:
                copy.wait_send()

        @pl.loop(0, 4)
        def _(e):
            for copy in cross_step(e, d):
                copy.wait_send()

    @pl.loop(1, 4)
    def _(d):
        output_line(d).wait_send()
        output_cross(d).wait_send()
        output_plane(d).wait_send()

    output_core().wait_send()
    weights_out.wait()
    for copy in core_step(0):
        copy.wait_send()
    key_copy.wait_send()
    value_copy.wait_send()


def front(length, *arrays):
    f32, bf16, i32 = jnp.float32, jnp.bfloat16, jnp.int32
    vmem = pl.BlockSpec(memory_space=pltpu.VMEM)
    hbm = pl.BlockSpec(memory_space=pl.ANY)
    shape = jax.ShapeDtypeStruct
    out_shape = (
        shape((2, 4, 4, 32, 3 * D), bf16),
        shape((TOKENS, D), bf16),
        shape((D, TOKENS), bf16),
        shape((HALF, 2 * TOKENS), bf16),
        shape((HALF, 2 * TOKENS), bf16),
        shape((HEADS, TOKENS), f32),
        shape((TOKENS, D), bf16),
        shape((TOKENS, D), f32),
        shape((TOKENS, D), bf16),
        shape((EXPERTS, TOKENS), f32),
        shape((EXPERTS, TOKENS), i32),
        shape((4, 8, TOKENS), i32),
        shape((4, 8, TOKENS), i32),
        shape((2, 4, 4, CAP, D), bf16),
    )
    scratch = [
        pltpu.VMEM((2, 4, 4, 32, 3 * D), bf16),
        pltpu.VMEM((D, TOKENS), bf16),
        pltpu.VMEM((4, 8, TOKENS), i32),
        pltpu.VMEM((4, 8, TOKENS), i32),
        pltpu.VMEM((4, TOKENS, HALF), bf16),
        pltpu.VMEM((4, TOKENS, HALF), bf16),
        pltpu.VMEM((2, 4, 4, CAP, D), bf16),
    ]
    scratch += [pltpu.SemaphoreType.DMA((2,))]
    for count in (40, 12, 8, 2, 8, 2 * GROUP, 8):
        scratch += [pltpu.SemaphoreType.DMA((count,))] * 2
    return pl.pallas_call(
        front_kernel,
        out_shape=out_shape,
        in_specs=[pl.BlockSpec(memory_space=pltpu.SMEM)] + [vmem] * len(arrays),
        out_specs=[hbm] + [vmem] * (len(out_shape) - 2) + [hbm],
        scratch_shapes=scratch,
        compiler_params=pltpu.CompilerParams(
            collective_id=3, has_side_effects=True, vmem_limit_bytes=60 << 20
        ),
        name="front",
    )(length, *arrays)


def turned_back(rows, cosine, sine):
    first, second = rows[0:32], rows[32:64]
    return jnp.concatenate(
        [first * cosine + second * sine, second * cosine - first * sine], axis=0
    )


def rest_kernel(
    length_ref,
    routed_ref,
    pos_ref,
    posz_ref,
    posx_ref,
    gates_ref,
    grads_hbm,
    wg_hbm,
    wu_hbm,
    wd_hbm,
    router_ref,
    middle_ref,
    cot_ref,
    hidden_hbm,
    again_ref,
    mgain_ref,
    normed_hbm,
    mixed_hbm,
    w_hbm,
    q_hbm,
    k_hbm,
    v_hbm,
    lse_ref,
    cos_ref,
    sin_ref,
    hout_ref,
    hgrad_ref,
    again_out,
    mgain_out,
    router_out,
    own_out,
    esum_hbm,
    prod_hbm,
    mid_hbm,
    tok_z,
    tok_x,
    arrived,
    mid,
    parts_in,
    parts_in2,
    gate_out,
    gate_in,
    dot_out,
    dot_in,
    rg_ref,
    gdot_ref,
    expert_ref,
    relay_in,
    y_in,
    branch_sib,
    normed_sib,
    mixed_sib,
    grad_sib,
    kv_in,
    rs_in,
    rs_in2,
    y_parts,
    small_in,
    small_y_in,
    gain_in,
    gain_y_in,
    router_all,
    load_sem,
    store_sem,
    first_send,
    first_recv,
    slot_send,
    slot_recv,
    back_send,
    back_recv,
    part_send,
    part_recv,
    small_send,
    small_recv,
    c_send,
    c_recv,
    part_send2,
    part_recv2,
    ex_send,
    ex_recv,
    sib_send,
    sib_recv,
    rs_send,
    rs_recv,
    rs_send2,
    rs_recv2,
    ys_send,
    ys_recv,
    sm_send,
    sm_recv,
):
    y, r, x, z = place()
    me = r * CHIPS + z * 4 + x
    sibling = moved(0, 0, 1 - r)[0]
    tokens = TOKENS
    f32, bf16 = jnp.float32, jnp.bfloat16

    above, below = plane_shift(1), plane_shift(3)
    opposite = plane_shift(2)[1]
    def relayed(n):
        device = (above, below)[n][0]
        return remote(
            expert_ref.at[0, n], relay_in.at[n], ex_send.at[n], ex_recv.at[n], device
        )

    def direct(n):
        device = (above, below)[n][0]
        return remote(
            expert_ref.at[1 + n, 1 - n],
            y_in.at[n, 1 - n],
            ex_send.at[2 + n],
            ex_recv.at[2 + n],
            device,
        )

    def passed_on(n):
        device, came_from = (above, below)[n][0], (below, above)[n][1]
        part = esum_hbm.at[came_from, n]
        return remote(part, part, ex_send.at[8 + n], ex_recv.at[8 + n], device)

    def to_sibling(at, src, dst):
        return remote(src, dst, sib_send.at[at], sib_recv.at[at], sibling)

    half = pl.ds(pl.multiple_of((1 - r) * HALF, HALF), HALF)
    sib_normed = to_sibling(0, normed_hbm.at[:, half], normed_sib)
    sib_mixed = to_sibling(1, mixed_hbm.at[:, half], mixed_sib)

    meet(True, True)
    sib_mixed.start()
    sib_normed.start()

    def expert_phase(grads_ref, wg_ref, wu_ref, wd_ref, outgoing, parts_out, active, weighted, pre_grads):
        loads = [
            pltpu.make_async_copy(source, target, load_sem.at[n])
            for n, (source, target) in enumerate(
                (
                    (wg_hbm, wg_ref),
                    (wu_hbm, wu_ref),
                    (wd_hbm, wd_ref),
                    (grads_hbm, grads_ref),
                )
            )
        ]
        for load in loads:
            load.start()
        @pl.loop(1, 4)
        def _(d):
            for copy in spread(d, routed_ref, tok_z, tok_x, first_send, first_recv):
                copy.start()

        tok_z[0] = routed_ref[:, 0:HALF]
        tok_x[0] = routed_ref[:, HALF:D]

        def small(k, out, into, sign, base, arriving=False):
            there, dz, dx = k // CHIPS, lax.rem(k // 4, 4), lax.rem(k, 4)
            slot = k if arriving else r * CHIPS + lax.rem(k, CHIPS)
            return remote(
                out.at[k],
                into.at[slot],
                small_send.at[base + k],
                small_recv.at[base + slot],
                moved(sign * dx, sign * dz, there)[0],
            )

        def own_slot(k):
            return k == r * CHIPS

        @pl.loop(0, GROUP)
        def _(k):
            there, dz, dx = k // CHIPS, lax.rem(k // 4, 4), lax.rem(k, 4)
            _, expert = moved(dx, dz, there)
            chosen = picks(pos_ref[pl.ds(expert, 1), :])
            gate_col = jnp.sum(
                jnp.where(chosen, gates_ref[pl.ds(expert, 1), :], 0.0), axis=1, keepdims=True
            )
            gate_out[k, 0:1, 0:CAP] = as_row(gate_col)

            @pl.when(own_slot(k))
            def _():
                gate_in[k] = gate_out[k]

            @pl.when(jnp.logical_not(own_slot(k)))
            def _():
                small(k, gate_out, gate_in, 1, 0).start()

        @pl.loop(1, 4)
        def _(d):
            for copy in spread(d, routed_ref, tok_z, tok_x, first_send, first_recv):
                copy.wait_recv()

        @pl.loop(0, 4)
        def _(g):
            for dx in range(4):
                dz = lax.rem(dx + g, 4)
                left_rows, right_rows = [], []
                for core in range(2):
                    at_x = core * 4 + lax.rem(x + dx, 4)
                    at_z = core * 4 + lax.rem(z + dz, 4)
                    left_rows.append(picks(posz_ref[dz, pl.ds(at_x, 1), :]))
                    right_rows.append(picks(posx_ref[dx, pl.ds(at_z, 1), :]))
                left = dot(as_hot(jnp.concatenate(left_rows, axis=0)), tok_z[dz], ((1,), (0,)))
                right = dot(as_hot(jnp.concatenate(right_rows, axis=0)), tok_x[dx], ((1,), (0,)))
                for core in range(2):
                    part = slice(core * CAP, core * CAP + CAP)
                    outgoing[core, dz, dx, :, 0:HALF] = left[part].astype(bf16)
                    outgoing[core, dz, dx, :, HALF:D] = right[part].astype(bf16)
                    send_slots(outgoing, arrived, core, dz, dx, slot_send, slot_recv, 1)

        def keep_produced(k):
            core, dz, dx = k // CHIPS, lax.rem(k // 4, 4), lax.rem(k, 4)
            return pltpu.make_async_copy(
                grads_ref.at[core, dz, dx], prod_hbm.at[core, dz, dx], store_sem.at[k]
            )

        for load in loads:
            load.wait()

        @pl.loop(0, 8)
        def _(c):
            g, core = c // 2, lax.rem(c, 2)
            rows, gate_cols, grads = [], [], []
            for dx in range(4):
                dz = lax.rem(dx + g, 4)
                k = core * CHIPS + dz * 4 + dx
                slots_arrived(outgoing, arrived, core, dz, dx, slot_send, slot_recv)

                @pl.when(jnp.logical_not(own_slot(k)))
                def _():
                    small(k, gate_out, gate_in, 1, 0, True).wait_recv()

                rows.append(arrived[core, dz, dx])
                gate_cols.append(as_column(gate_in[k, 0:1, 0:CAP]))
                grads.append(grads_ref[core, dz, dx])
            rows = jnp.concatenate(rows, axis=0)
            gate_cols = jnp.concatenate(gate_cols, axis=0)
            grads = jnp.concatenate(grads, axis=0).astype(f32)
            gate_pre = dot(rows, wg_ref[...], ((1,), (0,)))
            up_pre = dot(rows, wu_ref[...], ((1,), (0,)))
            gate_sig = jax.nn.sigmoid(gate_pre)
            gate_act = gate_pre * gate_sig
            act = (gate_act * up_pre).astype(bf16)
            produced = dot(act, wd_ref[...], ((1,), (0,))).astype(bf16).astype(f32)
            dots = jnp.sum(produced * grads, axis=1, keepdims=True)
            produced_grad = (gate_cols * grads).astype(bf16)
            act_grad = dot(produced_grad, wd_ref[...], ((1,), (1,))).astype(bf16).astype(f32)
            gate_grad = (
                act_grad * up_pre * gate_sig * (1.0 + gate_pre * (1.0 - gate_sig))
            ).astype(bf16)
            up_grad = (act_grad * gate_act).astype(bf16)
            row_grads = dot(gate_grad, wg_ref[...], ((1,), (1,)))
            row_grads = (row_grads + dot(up_grad, wu_ref[...], ((1,), (1,)))).astype(bf16)
            produced = (produced * gate_cols).astype(bf16)
            for dx in range(4):
                dz = lax.rem(dx + g, 4)
                k = core * CHIPS + dz * 4 + dx
                part = slice(dx * CAP, dx * CAP + CAP)
                block_sent(outgoing, arrived, core, dz, dx, slot_send, slot_recv)
                outgoing[core, dz, dx] = row_grads[part]
                send_slots(outgoing, mid, core, dz, dx, back_send, back_recv, -1)
                dot_out[k, 0:1, 0:CAP] = as_row(dots[part])

                @pl.when(own_slot(k))
                def _():
                    dot_in[k] = dot_out[k]

                @pl.when(jnp.logical_not(own_slot(k)))
                def _():
                    small(k, dot_out, dot_in, -1, GROUP).start()

                grads_ref[core, dz, dx] = produced[part]
                keep_produced(k).start()
                active[core, dz, dx] = act[part]
                weighted[core, dz, dx] = produced_grad[part]
                pre_grads[core, dz, dx, :, 0:HALF] = gate_grad[part]
                pre_grads[core, dz, dx, :, HALF:D] = up_grad[part]

        def send_results(g):
            for dx in range(4):
                dz = (dx + g) % 4
                for core in range(2):
                    keep_produced(core * CHIPS + dz * 4 + dx).wait()
                    send_slots(prod_hbm, mid_hbm, core, dz, dx, c_send, c_recv, -1, load_sem.at[4])

        send_results(0)

        all_rows = GROUP * CAP

        def quarter_grads(slot, n):
            span = pl.ds(pl.multiple_of(n * 256, 256), 256)
            left = arrived[:, :, :, :, span].reshape(all_rows, 256)
            part = dot(left, pre_grads[...].reshape(all_rows, D), ((0,), (0,))).astype(bf16)
            narrow = pl.ds(pl.multiple_of(n * 128, 128), 128)
            left = active[:, :, :, :, narrow].reshape(all_rows, 128)
            down = dot(left, weighted[...].reshape(all_rows, D), ((0,), (0,))).astype(bf16)
            for h in range(2):
                rows = part[128 * h : 128 * h + 128]
                expert_ref[slot, h, 0:128, :] = rows[:, 0:HALF]
                expert_ref[slot, h, 128:256, :] = rows[:, HALF:D]
                rows = down[64 * h : 64 * h + 64]
                expert_ref[slot, h, 256:320, :] = rows[:, 0:HALF]
                expert_ref[slot, h, 320:384, :] = rows[:, HALF:D]

        quarter_grads(0, opposite)
        for n in range(2):
            relayed(n).start()

        fold_parts(
            parts_out,
            parts_in,
            mid,
            outgoing,
            back_send,
            back_recv,
            posz_ref,
            posx_ref,
            part_send,
            part_recv,
        )
        for g in range(1, 4):
            send_results(g)

        @pl.loop(1, 4)
        def _(slot):
            quarter_grads(slot, lax.rem(y + jnp.where(slot == 1, 1, jnp.where(slot == 2, 3, 0)), 4))

        for n in range(2):
            direct(n).start()

        @pl.loop(0, GROUP)
        def _(k):
            @pl.when(jnp.logical_not(own_slot(k)))
            def _():
                small(k, dot_out, dot_in, -1, GROUP, True).wait_recv()

            there, dz, dx = k // CHIPS, lax.rem(k // 4, 4), lax.rem(k, 4)
            _, expert = moved(dx, dz, there)
            at = pl.ds(expert, 1)
            dots = as_column(dot_in[k, 0:1, 0:CAP])
            gdot_ref[at, :] = jnp.sum(
                jnp.where(picks(pos_ref[at, :]), dots, 0.0), axis=0, keepdims=True
            )

        parts_arrived(parts_out, parts_in, part_send, part_recv)
        rg_ref[...] = (parts_in[0].astype(f32) + parts_in[1].astype(f32)) + (
            parts_in[2].astype(f32) + parts_in[3].astype(f32)
        )
        slots_sent(outgoing, mid, back_send, back_recv)
        parts_sent(parts_out, parts_in, part_send, part_recv)

        @pl.loop(1, 4)
        def _(d):
            for copy in spread(d, routed_ref, tok_z, tok_x, first_send, first_recv):
                copy.wait_send()

        @pl.loop(0, GROUP)
        def _(k):
            @pl.when(jnp.logical_not(own_slot(k)))
            def _():
                small(k, gate_out, gate_in, 1, 0).wait_send()
                small(k, dot_out, dot_in, -1, GROUP).wait_send()

    pl.run_scoped(
        expert_phase,
        pltpu.VMEM((2, 4, 4, CAP, D), bf16),
        pltpu.VMEM((D, HALF), bf16),
        pltpu.VMEM((D, HALF), bf16),
        pltpu.VMEM((HALF, D), bf16),
        pltpu.VMEM((2, 4, 4, CAP, D), bf16),
        pltpu.VMEM((4, tokens, D), bf16),
        pltpu.VMEM((2, 4, 4, CAP, HALF), bf16),
        pltpu.VMEM((2, 4, 4, CAP, D), bf16),
        pltpu.VMEM((2, 4, 4, CAP, D), bf16),
    )

    def finish_phase(w_ref, q_ref, k_ref, v_ref, normed_ref, mixed_ref, hidden_ref, parts_out2, quarter_sum, relay_out, branch_own, mg_t, grad_t, kv_own, kv_out, weight_part, rs_out, y_out, small_out, small_y, gain_out, gain_y):
        loads = [
            pltpu.make_async_copy(source, target, load_sem.at[n])
            for n, (source, target) in enumerate(
                (
                    (w_hbm, w_ref),
                    (q_hbm, q_ref),
                    (k_hbm, k_ref),
                    (v_hbm, v_ref),
                    (normed_hbm, normed_ref),
                    (mixed_hbm, mixed_ref),
                    (hidden_hbm, hidden_ref),
                )
            )
        ]
        for load in loads:
            load.start()

        def weight(first, width):
            return w_ref[:, :, :, :, first : first + width].reshape(D, width)

        def merged(n):
            device = (above, below)[n][0]
            return remote(
                relay_out.at[n], y_in.at[n, n], ex_send.at[4 + n], ex_recv.at[4 + n], device
            )

        def handed(n):
            device = (above, below)[n][0]
            return remote(
                quarter_sum, esum_hbm.at[y], ex_send.at[6 + n], ex_recv.at[6 + n], device
            )

        def sib_keyval(p):
            return to_sibling(3 + p, kv_out.at[p], kv_in.at[p])

        def sib_grads(p, part):
            rows = pl.ds(p * D + part * HALF, HALF)
            return to_sibling(5 + 2 * p + part, grad_t.at[rows], grad_sib.at[rows])

        sib_branch = to_sibling(2, branch_own, branch_sib)

        for n in range(2):
            relayed(n).wait_recv()
            total = relay_in[n].astype(f32) + expert_ref[1 + n, n].astype(f32)
            relay_out[n] = total.astype(bf16)
            merged(n).start()

        gates = gates_ref[...]
        gdot = gdot_ref[...]
        logit_grad = gates * (gdot - jnp.sum(gates * gdot, axis=0, keepdims=True))
        high, rest = split_two(logit_grad)
        router_part = dot(high, routed_ref[...], ((1,), (0,)))
        router_part = router_part + dot(rest, routed_ref[...], ((1,), (0,)))
        routed_grad = dot(high, router_ref[...], ((0,), (0,)))
        routed_grad = routed_grad + dot(rest, router_ref[...], ((0,), (0,)))
        routed_grad = routed_grad + rg_ref[...]
        live = (
            r * tokens + lax.broadcasted_iota(jnp.int32, (tokens, 1), 0) < length_ref[0]
        ).astype(f32)
        middle = middle_ref[...]
        scale = lax.rsqrt(jnp.mean(middle * middle, axis=1, keepdims=True) + epsilon)
        rows = middle * scale
        moe_part = jnp.sum(routed_grad * rows, axis=0, keepdims=True)
        scaled = routed_grad * mgain_ref[...]
        inner = jnp.mean(scaled * rows, axis=1, keepdims=True)
        middle_grad = cot_ref[...].astype(f32) * live + scale * (scaled - rows * inner)
        hgrad_ref[...] = middle_grad
        branch_own[...] = middle_grad.astype(bf16)
        sib_branch.start()
        for j in range(8):
            part = slice(128 * j, 128 * j + 128)
            small_out[:, j, :] = router_part[:, part]
            small_out[:, 8 + j, :] = jnp.broadcast_to(moe_part[:, part], (GROUP, 128))

        def tiny(k):
            device, other = step_of(k, 1)
            return remote(small_out.at[other], small_in.at[me], sm_send.at[k], sm_recv.at[k], device)

        @pl.loop(1, GROUP)
        def _(k):
            tiny(k).start()

        small_in[me] = small_out[me]

        for load in loads:
            load.wait()
        mg_t[...] = dot(weight(2 * D, D), branch_own[...], ((1,), (1,))).astype(bf16)

        mine = pl.ds(pl.multiple_of(r * HALF, HALF), HALF)

        def columns(p):
            return pl.ds(p * D, HALF), pl.ds(p * D + HALF, HALF)

        def first_step(p, d):
            left, right = columns(p)
            at = 8 * p + d
            return (
                remote(
                    weight_part.at[lax.rem(z + d, 4), :, :, left],
                    rs_in.at[d, :, :, left],
                    rs_send.at[at],
                    rs_recv.at[at],
                    moved(0, d, r)[0],
                ),
                remote(
                    weight_part.at[:, lax.rem(x + d, 4), :, right],
                    rs_in.at[d, :, :, right],
                    rs_send.at[4 + at],
                    rs_recv.at[4 + at],
                    moved(d, 0, r)[0],
                ),
            )

        def second_step(p, d):
            left, right = columns(p)
            at = 8 * p + d
            return (
                remote(
                    rs_out.at[lax.rem(x + d, 4), :, left],
                    rs_in2.at[d, :, left],
                    rs_send2.at[at],
                    rs_recv2.at[at],
                    moved(d, 0, r)[0],
                ),
                remote(
                    rs_out.at[lax.rem(z + d, 4), :, right],
                    rs_in2.at[d, :, right],
                    rs_send2.at[4 + at],
                    rs_recv2.at[4 + at],
                    moved(0, d, r)[0],
                ),
            )

        def across(p, n):
            cols = pl.ds(p * D, D)
            at = 3 * p + n - 1
            return remote(
                y_out.at[:, cols],
                y_parts.at[y, :, cols],
                ys_send.at[at],
                ys_recv.at[at],
                plane_shift(n)[0],
            )

        def sum_first(p, total):
            weight_part[:, :, :, p * D : p * D + D] = total.astype(bf16).reshape(4, 4, 32, D)

            @pl.loop(1, 4)
            def _(d):
                for copy in first_step(p, d):
                    copy.start()

        def sum_second(p):
            left, right = columns(p)

            @pl.loop(1, 4)
            def _(d):
                for copy in first_step(p, d):
                    copy.wait_recv()

            total = weight_part[z, :, :, left].astype(f32)
            other = weight_part[:, x, :, right].astype(f32)
            for d in range(1, 4):
                total = total + rs_in[d, :, :, left].astype(f32)
                other = other + rs_in[d, :, :, right].astype(f32)
            rs_out[:, :, left] = total.astype(bf16)
            rs_out[:, :, right] = other.astype(bf16)

            @pl.loop(1, 4)
            def _(d):
                for copy in second_step(p, d):
                    copy.start()

        def sum_third(p):
            left, right = columns(p)

            @pl.loop(1, 4)
            def _(d):
                for copy in second_step(p, d):
                    copy.wait_recv()

            total = rs_out[x, :, left].astype(f32)
            other = rs_out[z, :, right].astype(f32)
            for d in range(1, 4):
                total = total + rs_in2[d, :, left].astype(f32)
                other = other + rs_in2[d, :, right].astype(f32)
            y_out[:, left] = total.astype(bf16)
            y_out[:, right] = other.astype(bf16)
            y_parts[y, :, left] = total.astype(bf16)
            y_parts[y, :, right] = other.astype(bf16)
            for n in range(1, PLANES):
                across(p, n).start()

        sib_mixed.wait_recv()
        sib_branch.wait_recv()
        total = dot(mixed_ref[:, mine], branch_own[...], ((0,), (0,)))
        sum_first(2, total + dot(mixed_sib[...], branch_sib[...], ((0,), (0,))))

        key_live = lax.broadcasted_iota(jnp.int32, (2 * tokens, 1), 0) < length_ref[0]
        score_scale = HEAD ** (-0.5)
        cosine, sine = cos_ref[...], sin_ref[...]
        first_core = r == 0

        def key_head(p, i):
            g = 4 * p + i
            head = pl.ds(pl.multiple_of(g * HEAD, HEAD), HEAD)
            keys, values = k_ref[head, :], v_ref[head, :]
            key_sum, value_sum = None, None
            for j in range(2):
                at = pl.ds(pl.multiple_of((2 * g + j) * HEAD, HEAD), HEAD)
                query, mixed_grad = q_ref[at, :], mg_t[at, :]
                scores = dot(keys, query, ((0,), (0,))) * score_scale
                scores = jnp.where(key_live, scores, NEG)
                probs = jnp.exp(scores - lse_ref[pl.ds(2 * g + j, 1), :])
                prob_grad = dot(values, mixed_grad, ((0,), (0,)))
                value_part = dot(mixed_grad, probs.astype(bf16), ((1,), (1,)))
                inner = jnp.sum(probs * prob_grad, axis=0, keepdims=True)
                score_grad = (probs * (prob_grad - inner)).astype(bf16)
                key_part = dot(query, score_grad, ((1,), (1,)))
                query_grad = dot(keys, score_grad, ((1,), (0,))) * score_scale
                to = pl.ds(pl.multiple_of(p * D + (2 * i + j) * HEAD, HEAD), HEAD)
                grad_t[to, :] = turned_back(query_grad, cosine, sine).astype(bf16)
                key_sum = key_part if key_sum is None else key_sum + key_part
                value_sum = value_part if value_sum is None else value_sum + value_part
            key_sum = key_sum * score_scale
            for n, part in enumerate((key_sum, value_sum)):
                to = pl.ds(pl.multiple_of(256 * n + i * HEAD, HEAD), HEAD)
                kv_own[p, to, :] = jnp.where(first_core, part[:, :tokens], part[:, tokens:])
                away = jnp.where(first_core, part[:, tokens:], part[:, :tokens])
                kv_out[p, to, :] = away.astype(bf16)

        def heads(p, first, last):
            @pl.loop(first, last)
            def _(i):
                key_head(p, i)

        def whole_keyval(p):
            sib_keyval(p).wait_recv()
            for i in range(4):
                rows = slice(HEAD * i, HEAD * i + HEAD)
                total = kv_own[p, rows, :] + kv_in[p, rows, :].astype(f32)
                to = p * D + HALF + HEAD * i
                grad_t[to : to + HEAD, :] = turned_back(total, cosine, sine).astype(bf16)
            total = kv_own[p, 256:512, :] + kv_in[p, 256:512, :].astype(f32)
            grad_t[p * D + HALF + 256 : p * D + D, :] = total.astype(bf16)
            sib_grads(p, 1).start()

        def projections(p):
            rows = slice(p * D, p * D + D)
            for part in range(2):
                sib_grads(p, part).wait_recv()
            total = dot(normed_ref[:, mine], grad_t[rows, :], ((0,), (1,)))
            sum_first(p, total + dot(normed_sib[...], grad_sib[rows, :], ((0,), (1,))))

        def inputs_part(p):
            return dot(grad_t[p * D : p * D + D, :], weight(p * D, D), ((0,), (1,)))

        heads(0, 0, 4)
        sib_keyval(0).start()
        sib_grads(0, 0).start()

        heads(1, 0, 4)
        sib_keyval(1).start()
        sib_grads(1, 0).start()
        whole_keyval(0)
        sib_normed.wait_recv()
        projections(0)
        whole_keyval(1)
        normed_grad = inputs_part(0)
        projections(1)
        normed_grad = normed_grad + inputs_part(1)

        inputs = hidden_ref[...].astype(f32)
        scale = lax.rsqrt(jnp.mean(inputs * inputs, axis=1, keepdims=True) + epsilon)
        rows = inputs * scale
        attn_part = jnp.sum(normed_grad * rows, axis=0, keepdims=True)
        for j in range(8):
            gain_out[j : j + 1, :] = attn_part[:, 128 * j : 128 * j + 128]

        def gain(k):
            device, _ = step_of(k, 1)
            at = 3 * GROUP + k
            return remote(gain_out, gain_in.at[me], sm_send.at[at], sm_recv.at[at], device)

        @pl.loop(1, GROUP)
        def _(k):
            gain(k).start()

        gain_in[me] = gain_out[...]
        scaled = normed_grad * again_ref[...]
        inner = jnp.mean(scaled * rows, axis=1, keepdims=True)
        hgrad_ref[...] += scale * (scaled - rows * inner)

        for n in range(2):
            direct(n).wait_recv()
            merged(n).wait_recv()
        for n in range(2):
            total = expert_ref[3, n].astype(f32) + (y_in[0, n].astype(f32) + y_in[1, n].astype(f32))
            quarter_sum[n] = total.astype(bf16)
        quarter_out = pltpu.make_async_copy(quarter_sum, esum_hbm.at[y], load_sem.at[9])
        quarter_out.start()
        for n in range(2):
            handed(n).start()

        sum_second(2)

        @pl.loop(1, GROUP)
        def _(k):
            tiny(k).wait_recv()

        def small_across(n):
            device, _ = plane_shift(n)
            return remote(
                small_y, small_y_in.at[y], sm_send.at[GROUP + n], sm_recv.at[GROUP + n], device
            )

        small_y[...] = jnp.sum(small_in[...], axis=0)
        small_y_in[y] = small_y[...]
        for n in range(1, PLANES):
            small_across(n).start()

        @pl.loop(0, GROUP)
        def _(k):
            slots_arrived(
                prod_hbm, mid_hbm, k // CHIPS, lax.rem(k // 4, 4), lax.rem(k, 4), c_send, c_recv
            )

        results_in = pltpu.make_async_copy(mid_hbm, mid, load_sem.at[10])
        results_in.start()
        results_in.wait()
        fold_parts(
            parts_out2,
            parts_in2,
            mid,
            None,
            c_send,
            c_recv,
            posz_ref,
            posx_ref,
            part_send2,
            part_recv2,
        )
        sum_third(2)
        sum_second(0)

        for n in range(1, PLANES):
            small_across(n).wait_recv()
        totals = small_y_in[0] + small_y_in[1] + small_y_in[2] + small_y_in[3]
        mgain_out[...] = totals[8:16]
        router_all[me] = totals[0:8]

        def router_row(k):
            device, _ = step_of(k, 1)
            at = 2 * GROUP + k
            return remote(
                router_all.at[me], router_all.at[me], sm_send.at[at], sm_recv.at[at], device
            )

        @pl.loop(1, GROUP)
        def _(k):
            router_row(k).start()

        @pl.loop(1, GROUP)
        def _(k):
            gain(k).wait_recv()

        gain_y[...] = jnp.sum(gain_in[...], axis=0)
        gain_y_in[y] = gain_y[...]

        def gain_across(n):
            device, _ = plane_shift(n)
            at = 4 * GROUP + n
            return remote(gain_y, gain_y_in.at[y], sm_send.at[at], sm_recv.at[at], device)

        for n in range(1, PLANES):
            gain_across(n).start()

        sum_second(1)
        sum_third(0)

        for n in range(2):
            handed(n).wait_recv()
            passed_on(n).start()

        sum_third(1)

        parts_arrived(parts_out2, parts_in2, part_send2, part_recv2)
        mixture = (parts_in2[0].astype(f32) + parts_in2[1].astype(f32)) + (
            parts_in2[2].astype(f32) + parts_in2[3].astype(f32)
        )
        hout_ref[...] = ((middle_ref[...] + mixture) * live).astype(bf16)

        for n in range(1, PLANES):
            gain_across(n).wait_recv()
        again_out[...] = (gain_y_in[0] + gain_y_in[1]) + (gain_y_in[2] + gain_y_in[3])

        @pl.loop(1, GROUP)
        def _(k):
            router_row(k).wait_recv()

        router_out[...] = router_all[...]

        slots_sent(prod_hbm, mid_hbm, c_send, c_recv)
        parts_sent(parts_out2, parts_in2, part_send2, part_recv2)

        @pl.loop(1, GROUP)
        def _(k):
            tiny(k).wait_send()
            router_row(k).wait_send()
            gain(k).wait_send()

        @pl.loop(1, 4)
        def _(d):
            for p in range(3):
                for copy in first_step(p, d) + second_step(p, d):
                    copy.wait_send()

        for n in range(2):
            for copy in (relayed(n), direct(n), merged(n), handed(n), passed_on(n)):
                copy.wait_send()
        for copy in (sib_normed, sib_mixed, sib_branch):
            copy.wait_send()
        for p in range(2):
            sib_keyval(p).wait_send()
            for part in range(2):
                sib_grads(p, part).wait_send()
        for n in range(1, PLANES):
            small_across(n).wait_send()
            gain_across(n).wait_send()
            for p in range(3):
                across(p, n).wait()
        for n in range(2):
            passed_on(n).wait_recv()
        quarter_out.wait()
        own_out[...] = (y_parts[0].astype(f32) + y_parts[1].astype(f32)) + (
            y_parts[2].astype(f32) + y_parts[3].astype(f32)
        )

    pl.run_scoped(
        finish_phase,
        pltpu.VMEM((2, 4, 4, 32, 3 * D), bf16),
        pltpu.VMEM((D, tokens), bf16),
        pltpu.VMEM((HALF, 2 * tokens), bf16),
        pltpu.VMEM((HALF, 2 * tokens), bf16),
        pltpu.VMEM((tokens, D), bf16),
        pltpu.VMEM((tokens, D), bf16),
        pltpu.VMEM((tokens, D), bf16),
        pltpu.VMEM((4, tokens, D), bf16),
        pltpu.VMEM((2, 384, HALF), bf16),
        pltpu.VMEM((2, 384, HALF), bf16),
        pltpu.VMEM((tokens, D), bf16),
        pltpu.VMEM((D, tokens), bf16),
        pltpu.VMEM((2 * D, tokens), bf16),
        pltpu.VMEM((2, HALF, tokens), f32),
        pltpu.VMEM((2, HALF, tokens), bf16),
        pltpu.VMEM((4, 4, 32, 3 * D), bf16),
        pltpu.VMEM((4, 32, 3 * D), bf16),
        pltpu.VMEM((32, 3 * D), bf16),
        pltpu.VMEM((GROUP, 16, 128), f32),
        pltpu.VMEM((16, 128), f32),
        pltpu.VMEM((8, 128), f32),
        pltpu.VMEM((8, 128), f32),
    )


def rest(length, *arrays):
    tokens = TOKENS
    f32, bf16 = jnp.float32, jnp.bfloat16
    vmem = pl.BlockSpec(memory_space=pltpu.VMEM)
    hbm = pl.BlockSpec(memory_space=pl.ANY)
    shape = jax.ShapeDtypeStruct
    sems = pltpu.SemaphoreType.DMA
    scratch = [
        pltpu.VMEM((4, tokens, HALF), bf16),
        pltpu.VMEM((4, tokens, HALF), bf16),
        pltpu.VMEM((2, 4, 4, CAP, D), bf16),
        pltpu.VMEM((2, 4, 4, CAP, D), bf16),
        pltpu.VMEM((4, tokens, D), bf16),
        pltpu.VMEM((4, tokens, D), bf16),
        pltpu.VMEM((GROUP, 8, 128), f32),
        pltpu.VMEM((GROUP, 8, 128), f32),
        pltpu.VMEM((GROUP, 8, 128), f32),
        pltpu.VMEM((GROUP, 8, 128), f32),
        pltpu.VMEM((tokens, D), f32),
        pltpu.VMEM((EXPERTS, tokens), f32),
        pltpu.VMEM((4, 2, 384, HALF), bf16),
        pltpu.VMEM((2, 384, HALF), bf16),
        pltpu.VMEM((2, 2, 384, HALF), bf16),
        pltpu.VMEM((tokens, D), bf16),
        pltpu.VMEM((tokens, HALF), bf16),
        pltpu.VMEM((tokens, HALF), bf16),
        pltpu.VMEM((2 * D, tokens), bf16),
        pltpu.VMEM((2, HALF, tokens), bf16),
        pltpu.VMEM((4, 4, 32, 3 * D), bf16),
        pltpu.VMEM((4, 32, 3 * D), bf16),
        pltpu.VMEM((PLANES, 32, 3 * D), bf16),
        pltpu.VMEM((GROUP, 16, 128), f32),
        pltpu.VMEM((PLANES, 16, 128), f32),
        pltpu.VMEM((GROUP, 8, 128), f32),
        pltpu.VMEM((PLANES, 8, 128), f32),
        pltpu.VMEM((GROUP, 8, 128), f32),
    ]
    for count in (11, GROUP, 8, 8, 2 * GROUP, 2 * GROUP, 2 * GROUP, 2 * GROUP, 8, 8, 2 * GROUP, 2 * GROUP, 2 * GROUP, 2 * GROUP, 8, 8, 10, 10, 9, 9, 24, 24, 24, 24, 9, 9, 5 * GROUP, 5 * GROUP):
        scratch += [sems((count,))]
    in_specs = [pl.BlockSpec(memory_space=pltpu.SMEM)] + [vmem] * len(arrays)
    for n in (6, 7, 8, 9, 13, 16, 17, 18, 19, 20, 21):
        in_specs[n] = hbm
    return pl.pallas_call(
        rest_kernel,
        out_shape=(
            shape((tokens, D), bf16),
            shape((tokens, D), f32),
            shape((8, 128), f32),
            shape((8, 128), f32),
            shape((GROUP, 8, 128), f32),
            shape((32, 3 * D), f32),
            shape((4, 2, 384, HALF), bf16),
            shape((2, 4, 4, CAP, D), bf16),
            shape((2, 4, 4, CAP, D), bf16),
        ),
        in_specs=in_specs,
        out_specs=[vmem] * 6 + [hbm] * 3,
        scratch_shapes=scratch,
        compiler_params=pltpu.CompilerParams(
            collective_id=2, has_side_effects=True, vmem_limit_bytes=62 << 20
        ),
        name="rest",
    )(length, *arrays)[:7]


def spread_kernel(
    hout_ref,
    hgrad_ref,
    own_ref,
    esum_ref,
    router_ref,
    again_ref,
    mgain_ref,
    hout_out,
    hgrad_out,
    q_out,
    k_out,
    v_out,
    o_out,
    gate_out,
    up_out,
    down_out,
    router_out,
    again_out,
    mgain_out,
):
    f32 = jnp.float32
    hout_out[...] = hout_ref[...]
    hgrad_out[...] = hgrad_ref[...]
    for p in range(2):
        q_out[:, p * HALF : p * HALF + HALF] = own_ref[:, p * D : p * D + HALF]
        k_out[:, p * 256 : p * 256 + 256] = own_ref[:, p * D + HALF : p * D + 768]
        v_out[:, p * 256 : p * 256 + 256] = own_ref[:, p * D + 768 : p * D + D]
    o_out[...] = own_ref[:, 2 * D : 3 * D]
    for h in range(2):
        gate_out[0, 128 * h : 128 * h + 128, :] = esum_ref[0, h, 0:128, :].astype(f32)
        up_out[0, 128 * h : 128 * h + 128, :] = esum_ref[0, h, 128:256, :].astype(f32)
        down_out[0, 64 * h : 64 * h + 64, 0:HALF] = esum_ref[0, h, 256:320, :].astype(f32)
        down_out[0, 64 * h : 64 * h + 64, HALF:D] = esum_ref[0, h, 320:384, :].astype(f32)
    for j in range(8):
        router_out[:, 128 * j : 128 * j + 128] = router_ref[:, j, :]
    again_out[...] = again_ref[...]
    mgain_out[...] = mgain_ref[...]


def spread_out(*arrays):
    f32, bf16 = jnp.float32, jnp.bfloat16
    shape = jax.ShapeDtypeStruct

    def whole(*dims):
        return pl.BlockSpec(dims, lambda i: (0,) * len(dims))

    def rows(count, width):
        return pl.BlockSpec((count, width), lambda i: (i, 0))

    def expert_rows(count, width):
        return pl.BlockSpec((1, count, width), lambda i: (0, i, 0))

    return pl.pallas_call(
        spread_kernel,
        grid=(4,),
        out_shape=(
            shape((TOKENS, D), bf16),
            shape((TOKENS, D), f32),
            shape((32, D), f32),
            shape((32, HALF), f32),
            shape((32, HALF), f32),
            shape((32, D), f32),
            shape((1, D, HALF), f32),
            shape((1, D, HALF), f32),
            shape((1, HALF, D), f32),
            shape((EXPERTS, D), f32),
            shape((8, 128), f32),
            shape((8, 128), f32),
        ),
        in_specs=[
            rows(64, D),
            rows(64, D),
            whole(32, 3 * D),
            pl.BlockSpec((1, 2, 384, HALF), lambda i: (i, 0, 0, 0)),
            whole(GROUP, 8, 128),
            whole(8, 128),
            whole(8, 128),
        ],
        out_specs=[
            rows(64, D),
            rows(64, D),
            whole(32, D),
            whole(32, HALF),
            whole(32, HALF),
            whole(32, D),
            expert_rows(256, HALF),
            expert_rows(256, HALF),
            expert_rows(128, D),
            whole(EXPERTS, D),
            whole(8, 128),
            whole(8, 128),
        ],
        name="spread_out",
    )(*arrays)


def on_device(
    hidden_in,
    cotangent,
    lengths,
    routes,
    priority,
    attn_gain,
    query_weight,
    key_weight,
    value_weight,
    output_weight,
    moe_gain,
    router,
    gate_weight,
    up_weight,
    down_weight,
):
    tok_count = hidden_in.shape[0]
    positions = lax.axis_index("row") * tok_count + jnp.arange(tok_count, dtype=jnp.int32)
    half_dim = HEAD // 2
    frequency = rotary_base ** (-jnp.arange(half_dim, dtype=jnp.float32) / half_dim)
    angles = frequency[:, None] * positions.astype(jnp.float32)[None, :]
    cosine, sine = jnp.cos(angles), jnp.sin(angles)
    router_t = router.T
    (
        weights,
        normed,
        queries,
        keys,
        values,
        log_total,
        mixed_rows,
        middle,
        routed,
        gates,
        pos,
        posz,
        posx,
        arrived_grad,
    ) = front(
        lengths,
        hidden_in,
        cotangent,
        routes.T,
        priority,
        attn_gain[None],
        moe_gain[None],
        query_weight,
        key_weight,
        value_weight,
        output_weight,
        router_t,
        cosine,
        sine,
    )
    summed = rest(
        lengths,
        routed,
        pos,
        posz,
        posx,
        gates,
        arrived_grad,
        gate_weight[0],
        up_weight[0],
        down_weight[0],
        router_t,
        middle,
        cotangent,
        hidden_in,
        attn_gain[None],
        moe_gain[None],
        normed,
        mixed_rows,
        weights,
        queries,
        keys,
        values,
        log_total,
        cosine,
        sine,
    )
    hidden_out, hidden_grad, attn_gain_sum, moe_gain_sum, router_sum, own_rows, expert_sum = summed
    (
        hidden_out,
        hidden_grad,
        query_grad,
        key_grad,
        value_grad,
        output_grad,
        gate_grad,
        up_grad,
        down_grad,
        router_grad,
        attn_gain_sum,
        moe_gain_sum,
    ) = spread_out(
        hidden_out, hidden_grad, own_rows, expert_sum, router_sum, attn_gain_sum, moe_gain_sum
    )
    return (
        hidden_out,
        hidden_grad,
        attn_gain_sum.reshape(D),
        query_grad,
        key_grad,
        value_grad,
        output_grad,
        moe_gain_sum.reshape(D),
        router_grad.T,
        gate_grad,
        up_grad,
        down_grad,
    )


def solution(mesh):
    return jax.shard_map(
        on_device,
        mesh=mesh,
        in_specs=(
            P(("dp", "col", "row"), None),
            P(("dp", "col", "row"), None),
            P(("dp", "col")),
            P(("dp", "col", "row"), None),
            P(("dp", "col", "row"), None),
            P(),
            P(("row", "col"), None),
            P(("row", "col"), None),
            P(("row", "col"), None),
            P(("row", "col"), None),
            P(),
            P(),
            P(("row", "col"), None, None),
            P(("row", "col"), None, None),
            P(("row", "col"), None, None),
        ),
        out_specs=(
            P(("dp", "col", "row"), None),
            P(("dp", "col", "row"), None),
            P(),
            P(("row", "col"), None),
            P(("row", "col"), None),
            P(("row", "col"), None),
            P(("row", "col"), None),
            P(),
            P(),
            P(("row", "col"), None, None),
            P(("row", "col"), None, None),
            P(("row", "col"), None, None),
        ),
        check_vma=False,
    )
```

```python
import jax
import jax.numpy as jnp
from jax import lax
from jax.experimental import pallas as pl
from jax.experimental.pallas import tpu as pltpu
from jax.sharding import PartitionSpec as P

D = 1024
HEADS = 16
HEAD = 64
KV_HEADS = 8
EXPERTS = 32
TOP = 8
CAP = 64


epsilon = 1e-05
rotary_base = 10000.0


MESH = pl.DeviceIdType.MESH
GROUP = 32
PLANES = 4
CHIPS = 16
HALF = D // 2
TOKENS = 256
NEG = -1000000000.0


def place():
    col = lax.axis_index("col")
    return lax.axis_index("dp"), lax.axis_index("row"), lax.rem(col, 4), col // 4


def moved(dx, dz, core):
    y, r, x, z = place()
    col = lax.rem(z + dz + 4, 4) * 4 + lax.rem(x + dx + 4, 4)
    return (y, core, col), core * CHIPS + col


def plane_shift(n):
    y, r, x, z = place()
    other = lax.rem(y + n, PLANES)
    return (other, r, z * 4 + x), other


def step_of(k, sign):
    y, r, x, z = place()
    return moved(sign * lax.rem(k, 4), sign * lax.rem(k // 4, 4), lax.rem(r + k // CHIPS, 2))


def remote(src, dst, send_sem, recv_sem, device):
    return pltpu.make_async_remote_copy(
        src_ref=src,
        dst_ref=dst,
        send_sem=send_sem,
        recv_sem=recv_sem,
        device_id=device,
        device_id_type=MESH,
    )


def done(ref, sem):
    pltpu.make_async_copy(ref, ref, sem).wait()


def meet(plane, planes):
    barrier = pltpu.get_barrier_semaphore()
    y, r, x, z = place()

    def greet(device):
        pl.semaphore_signal(barrier, inc=1, device_id=device, device_id_type=MESH)

    if plane:

        @pl.loop(1, GROUP)
        def _(k):
            greet(step_of(k, 1)[0])

        count = GROUP - 1
    else:
        for core in range(2):

            @pl.loop(1, 4)
            def _(d):
                greet(moved(d, 0, core)[0])
                greet(moved(0, d, core)[0])

        greet(moved(0, 0, 1 - r)[0])
        count = 13
    if planes:
        for n in range(1, PLANES):
            greet(plane_shift(n)[0])
        count += PLANES - 1
    pl.semaphore_wait(barrier, count)


def eye(n):
    return lax.broadcasted_iota(jnp.int32, (n, n), 0) == lax.broadcasted_iota(
        jnp.int32, (n, n), 1
    )


def as_row(column):
    return jnp.sum(jnp.where(eye(column.shape[0]), column, 0.0), axis=0, keepdims=True)


def as_column(row_vec):
    return jnp.sum(jnp.where(eye(row_vec.shape[1]), row_vec, 0.0), axis=1, keepdims=True)


def dot(a, b, dims):
    return lax.dot_general(a, b, (dims, ((), ())), preferred_element_type=jnp.float32)


def split_two(values):
    high = values.astype(jnp.bfloat16)
    return high, (values - high.astype(jnp.float32)).astype(jnp.bfloat16)


def picks(positions):
    slots = lax.broadcasted_iota(jnp.int32, (CAP, positions.shape[1]), 0)
    return slots == positions


def as_hot(mask):
    return mask.astype(jnp.float32).astype(jnp.bfloat16)


LEFT = pl.ds(0, HALF)
RIGHT = pl.ds(HALF, HALF)


def spread(d, source, tok_z, tok_x, send_sem, recv_sem):
    y, r, x, z = place()
    return (
        remote(
            source.at[:, LEFT], tok_z.at[d], send_sem.at[0], recv_sem.at[0], moved(0, d, r)[0]
        ),
        remote(
            source.at[:, RIGHT], tok_x.at[d], send_sem.at[1], recv_sem.at[1], moved(d, 0, r)[0]
        ),
    )


def spread_done(tok_z, tok_x, sem):
    done(tok_z.at[pl.ds(1, 3)], sem.at[0])
    done(tok_x.at[pl.ds(1, 3)], sem.at[1])


def is_local(core, offset):
    y, r, x, z = place()
    return (core == r) & (offset == 0)


def send_slots(out, into, there, dz, dx, send_sem, recv_left, recv_right, sign, local_sem=None):
    y, r, x, z = place()

    def one(cols, offset, device, recv_sem):
        source, target = out.at[there, dz, dx, :, cols], into.at[r, dz, dx, :, cols]

        @pl.when(jnp.logical_not(is_local(there, offset)))
        def _():
            remote(source, target, send_sem, recv_sem, device).start()

        @pl.when(is_local(there, offset))
        def _():
            if local_sem is None:
                target[...] = source[...]
            else:
                pltpu.make_async_copy(source, target, local_sem).start()

    one(LEFT, dx, moved(sign * dx, 0, there)[0], recv_left)
    one(RIGHT, dz, moved(0, sign * dz, there)[0], recv_right)


def all_slots(ref):
    return ref.at[:, :, :, :, pl.ds(0, 896)]


def line_rows(line, d, axis):
    y, r, x, z = place()
    own = x if axis == 0 else z
    return [
        line[d, pl.ds(core * 4 + lax.rem(own + i, 4), 1), :] for core in range(2) for i in range(4)
    ]


def line_hot(line, d, axis):
    return as_hot(jnp.concatenate([picks(p) for p in line_rows(line, d, axis)], axis=0))


def add_up(mid, line, d, axis):
    if axis == 0:
        rows = mid[:, d, :, :, 0:HALF]
    else:
        rows = mid[:, :, d, :, HALF:D]
    return dot(line_hot(line, d, axis), rows.reshape(8 * CAP, HALF), ((0,), (0,))).astype(
        jnp.bfloat16
    )


def part_copies(d, out, into, send_sem, recv_sem):
    y, r, x, z = place()
    return (
        lambda: remote(
            out.at[d, :, LEFT], into.at[d, :, LEFT], send_sem, recv_sem, moved(0, -d, r)[0]
        ),
        lambda: remote(
            out.at[d, :, RIGHT], into.at[d, :, RIGHT], send_sem, recv_sem, moved(-d, 0, r)[0]
        ),
    )


def fold_parts(out, into, mid, slot_recv, posz_ref, posx_ref, send_sem, recv_sem):
    @pl.loop(0, 4)
    def _(d):
        if slot_recv is not None:
            done(mid.at[0, 0, :, :, pl.ds(0, 896)], slot_recv.at[d])
        left = add_up(mid, posz_ref, d, 0)

        @pl.when(d == 0)
        def _():
            into[0, :, 0:HALF] = left

        @pl.when(d != 0)
        def _():
            out[d, :, 0:HALF] = left
            part_copies(d, out, into, send_sem, recv_sem)[0]().start()

        if slot_recv is not None:
            done(mid.at[0, 0, :, :, pl.ds(0, 896)], slot_recv.at[4 + d])
        right = add_up(mid, posx_ref, d, 1)

        @pl.when(d == 0)
        def _():
            into[0, :, HALF:D] = right

        @pl.when(d != 0)
        def _():
            out[d, :, HALF:D] = right
            part_copies(d, out, into, send_sem, recv_sem)[1]().start()


def front_kernel(
    length_ref,
    hidden_ref,
    cot_ref,
    routes_ref,
    prio_ref,
    again_ref,
    mgain_ref,
    wq_ref,
    wk_ref,
    wv_ref,
    wo_ref,
    router_ref,
    cos_ref,
    sin_ref,
    w_hbm,
    normed_ref,
    q_ref,
    k_ref,
    v_ref,
    lse_ref,
    mixed_ref,
    middle_ref,
    routed_ref,
    gates_ref,
    pos_ref,
    posz_ref,
    posx_ref,
    grads_ref,
    w_ref,
    mixed_t,
    posz_out,
    posx_out,
    tok_z,
    tok_x,
    outgoing,
    store_sem,
    w_send,
    w_recv,
    o_send,
    o_recv,
    core_send,
    core_recv,
    kv_send,
    kv_recv,
    first_send,
    first_recv,
    slot_send,
    slot_recv,
    pos_send,
    pos_recv,
):
    y, r, x, z = place()
    f32, bf16 = jnp.float32, jnp.bfloat16
    sibling = moved(0, 0, 1 - r)[0]
    meet(False, True)

    for p in range(2):
        part = slice(256 * p, 256 * p + 256)
        w_ref[r, z, x, :, D * p : D * p + HALF] = wq_ref[:, HALF * p : HALF * p + HALF]
        w_ref[r, z, x, :, D * p + HALF : D * p + 768] = wk_ref[:, part]
        w_ref[r, z, x, :, D * p + 768 : D * p + D] = wv_ref[:, part]
    front, rear, output = pl.ds(0, D), pl.ds(D, D), pl.ds(2 * D, D)
    quarter = pl.ds(pl.multiple_of(2 * D + 256 * y, 256), 256)

    def line_step(d):
        mine_q, mine_o = w_ref.at[r, z, x, :, front], w_ref.at[r, z, x, :, rear]
        return (
            remote(mine_q, mine_q, w_send.at[0], w_recv.at[d], moved(0, d, r)[0]),
            remote(mine_o, mine_o, w_send.at[0], w_recv.at[4 + d], moved(d, 0, r)[0]),
        )

    def cross_step(e, d):
        from_z = w_ref.at[r, lax.rem(z - e + 4, 4), x, :, front]
        from_x = w_ref.at[r, z, lax.rem(x - e + 4, 4), :, rear]
        return (
            remote(from_z, from_z, w_send.at[1], w_recv.at[8 + d], moved(d, 0, r)[0]),
            remote(from_x, from_x, w_send.at[1], w_recv.at[8 + d], moved(0, d, r)[0]),
        )

    w_ref[r, z, x, :, quarter] = wo_ref[:, pl.ds(pl.multiple_of(256 * y, 256), 256)]

    def output_line(d):
        own = w_ref.at[r, z, x, :, quarter]
        return remote(own, own, o_send.at[0], o_recv.at[0], moved(0, d, r)[0])

    def output_cross(d):
        own = w_ref.at[r, :, x, :, quarter]
        return remote(own, own, o_send.at[1], o_recv.at[1], moved(d, 0, r)[0])

    def output_plane(n):
        own = w_ref.at[r, :, :, :, quarter]
        return remote(own, own, o_send.at[2], o_recv.at[2], plane_shift(n)[0])

    def output_core():
        own = w_ref.at[r, :, :, :, output]
        return remote(own, own, o_send.at[3], o_recv.at[3], sibling)

    def some(rows, width):
        return w_ref.at[0, pl.ds(0, rows), :, :, pl.ds(0, width)]

    def core_step(d):
        from_x = w_ref.at[r, :, lax.rem(x - d + 4, 4), :, front]
        from_z = w_ref.at[r, lax.rem(z - d + 4, 4), :, :, rear]
        return (
            remote(from_x, from_x, core_send.at[0], core_recv.at[0], sibling),
            remote(from_z, from_z, core_send.at[0], core_recv.at[0], sibling),
        )

    @pl.loop(1, 4)
    def _(d):
        for copy in line_step(d):
            copy.start()

    @pl.loop(1, 4)
    def _(d):
        for copy in cross_step(0, d):
            copy.start()
        output_line(d).start()

    tokens = hidden_ref.shape[0]
    experts_iota = lax.broadcasted_iota(jnp.int32, (EXPERTS, tokens), 0).astype(f32)
    live = r * tokens + lax.broadcasted_iota(jnp.int32, (1, tokens), 1) < length_ref[0]
    routed_to = jnp.zeros((EXPERTS, tokens), f32)
    ranks = jnp.zeros((EXPERTS, tokens), f32)
    prio = prio_ref[...]
    lines = jnp.concatenate([prio[:, 128 * i : 128 * i + 128] for i in range(CHIPS)], axis=0)
    token = lax.broadcasted_iota(jnp.int32, (tokens, CHIPS), 0) // CHIPS
    owner = (token == lax.broadcasted_iota(jnp.int32, (tokens, CHIPS), 1)).astype(f32)
    token = lax.rem(lax.broadcasted_iota(jnp.int32, (tokens, 128), 0), CHIPS)
    lane = lax.broadcasted_iota(jnp.int32, (tokens, 128), 1)
    place_of = lax.rem(lax.broadcasted_iota(jnp.int32, (TOP, 128), 1), TOP)
    place_of = (place_of == lax.broadcasted_iota(jnp.int32, (TOP, 128), 0)).astype(f32)
    priority = jnp.zeros((TOP, tokens), f32)
    for unit, part in ((64.0, lines // 64), (1.0, lax.rem(lines, 64))):
        part = part.astype(f32).astype(bf16)
        rows = dot(owner.astype(bf16), part, ((1,), (0,)))
        rows = jnp.where(lane // TOP == token, rows, 0.0).astype(bf16)
        priority = priority + unit * dot(place_of.astype(bf16), rows, ((1,), (1,)))
    routes = routes_ref[...].astype(f32)
    for j in range(TOP):
        match = experts_iota == routes[j : j + 1, :]
        routed_to = jnp.where(match, 1.0, routed_to)
        ranks = jnp.where(match, priority[j : j + 1, :], ranks)
    far = float(1 << 20)
    ranks = jnp.where((routed_to > 0.0) & live, ranks, far)
    ranks_t = ranks.T
    rows = []
    for e in range(EXPERTS):
        earlier = ranks_t[:, e : e + 1] < ranks[e : e + 1, :]
        rows.append(jnp.sum(earlier.astype(f32), axis=0, keepdims=True))
    slots = jnp.concatenate(rows, axis=0)
    pos = jnp.where((ranks < far) & (slots < CAP), slots, -1.0).astype(jnp.int32)
    pos_ref[...] = pos
    for core in range(2):
        for i in range(4):
            at = core * CHIPS + 4 * i
            posz_out[i, 4 * core : 4 * core + 4, :] = pos[at : at + 4, :]
            for j in range(4):
                posx_out[j, 4 * core + i : 4 * core + i + 1, :] = pos[at + j : at + j + 1, :]
    posz_ref[0] = posz_out[z]
    posx_ref[0] = posx_out[x]
    tok_z[0] = cot_ref[:, 0:HALF]
    tok_x[0] = cot_ref[:, HALF:D]

    def pos_step(d):
        to_z, to_x = lax.rem(z + d, 4), lax.rem(x + d, 4)
        return (
            remote(
                posz_out.at[to_z],
                posz_ref.at[d],
                pos_send.at[0],
                pos_recv.at[0],
                moved(0, d, r)[0],
            ),
            remote(
                posx_out.at[to_x],
                posx_ref.at[d],
                pos_send.at[1],
                pos_recv.at[1],
                moved(d, 0, r)[0],
            ),
        )

    @pl.loop(1, 4)
    def _(d):
        for copy in pos_step(d):
            copy.start()

    done(w_ref.at[0, 0, pl.ds(0, 3), :, pl.ds(0, 256)], o_recv.at[0])

    @pl.loop(1, 4)
    def _(d):
        output_cross(d).start()

    @pl.loop(1, 4)
    def _(e):
        for copy in line_step(e):
            copy.wait_recv()

        @pl.loop(1, 4)
        def _(d):
            for copy in cross_step(e, d):
                copy.start()

    @pl.loop(1, 4)
    def _(d):
        for copy in spread(d, cot_ref, tok_z, tok_x, first_send, first_recv):
            copy.start()

    for copy in core_step(0):
        copy.start()

    inputs = hidden_ref[...].astype(f32)
    scale = lax.rsqrt(jnp.mean(inputs * inputs, axis=1, keepdims=True) + epsilon)
    normed_ref[...] = (inputs * scale * again_ref[...]).astype(bf16)

    spread_done(tok_z, tok_x, first_recv)
    done(posz_ref.at[pl.ds(1, 3)], pos_recv.at[0])
    done(posx_ref.at[pl.ds(1, 3)], pos_recv.at[1])

    @pl.loop(0, 4)
    def _(d):
        left = dot(line_hot(posz_ref, d, 0), tok_z[d], ((1,), (0,))).astype(bf16)
        right = dot(line_hot(posx_ref, d, 1), tok_x[d], ((1,), (0,))).astype(bf16)
        for core in range(2):
            for i in range(4):
                part = slice((core * 4 + i) * CAP, (core * 4 + i + 1) * CAP)
                outgoing[core, d, i, :, 0:HALF] = left[part]
                outgoing[core, i, d, :, HALF:D] = right[part]

    done(some(3, 256), o_recv.at[1])

    for n in range(1, PLANES):
        output_plane(n).start()

    @pl.loop(1, 4)
    def _(d):
        done(some(1, 2 * D), w_recv.at[8 + d])
        for copy in core_step(d):
            copy.start()

    @pl.loop(0, CHIPS)
    def _(k):
        dx = lax.rem(k, 4)
        dz = lax.rem(dx + k // 4, 4)
        for core in range(2):
            send_slots(
                outgoing,
                grads_ref,
                core,
                dz,
                dx,
                slot_send.at[0],
                slot_recv.at[0],
                slot_recv.at[0],
                1,
                store_sem.at[1],
            )

    done(some(4, 2 * D), core_recv.at[0])

    cosine, sine = cos_ref[...], sin_ref[...]
    here = pl.ds(pl.multiple_of(r * tokens, tokens), tokens)

    def projected(first):
        weight = w_ref[:, :, :, :, first : first + HALF].reshape(D, HALF)
        return dot(normed_ref[...], weight, ((1,), (0,))).T

    def turned(rows):
        parts = []
        for h in range(rows.shape[0] // HEAD):
            first, second = rows[HEAD * h : HEAD * h + 32], rows[HEAD * h + 32 : HEAD * h + HEAD]
            parts += [first * cosine - second * sine, second * cosine + first * sine]
        return jnp.concatenate(parts, axis=0).astype(bf16)

    key_copy = remote(
        k_ref.at[:, here], k_ref.at[:, here], kv_send.at[0], kv_recv.at[0], sibling
    )
    value_copy = remote(
        v_ref.at[:, here], v_ref.at[:, here], kv_send.at[1], kv_recv.at[1], sibling
    )
    for p in range(2):
        both = projected(D * p + HALF)
        k_ref[256 * p : 256 * p + 256, here] = turned(both[0:256])
        v_ref[256 * p : 256 * p + 256, here] = both[256:512].astype(bf16)
    key_copy.start()
    value_copy.start()
    for p in range(2):
        q_ref[HALF * p : HALF * p + HALF, :] = turned(projected(D * p))

    key_copy.wait_recv()
    value_copy.wait_recv()

    done(some(4, 768), o_recv.at[2])
    output_core().start()

    key_live = lax.broadcasted_iota(jnp.int32, (2 * tokens, 1), 0) < length_ref[0]
    score_scale = HEAD ** (-0.5)

    @pl.loop(0, KV_HEADS)
    def _(g):
        head = pl.ds(pl.multiple_of(g * HEAD, HEAD), HEAD)
        keys, values = k_ref[head, :], v_ref[head, :]
        for j in range(2):
            at = pl.ds(pl.multiple_of((2 * g + j) * HEAD, HEAD), HEAD)
            scores = dot(keys, q_ref[at, :], ((0,), (0,))) * score_scale
            scores = jnp.where(key_live, scores, NEG)
            top = jnp.max(scores, axis=0, keepdims=True)
            weights = jnp.exp(scores - top)
            total = jnp.sum(weights, axis=0, keepdims=True)
            lse_ref[pl.ds(2 * g + j, 1), :] = top + jnp.log(total)
            probs = (weights * (1.0 / total)).astype(bf16)
            mixed_t[at, :] = dot(values, probs, ((1,), (0,))).astype(bf16)

    mixed_ref[...] = mixed_t[...].T
    output_core().wait_recv()
    weights_out = pltpu.make_async_copy(w_ref, w_hbm, store_sem.at[0])
    weights_out.start()
    w_out = w_ref[:, :, :, :, 2 * D : 3 * D].reshape(D, D)
    middle = hidden_ref[...].astype(f32) + dot(mixed_ref[...], w_out, ((1,), (0,)))
    middle_ref[...] = middle
    scale = lax.rsqrt(jnp.mean(middle * middle, axis=1, keepdims=True) + epsilon)
    routed_ref[...] = (middle * scale * mgain_ref[...]).astype(bf16)
    logits = dot(router_ref[...], routed_ref[...], ((1,), (1,)))
    logits = jnp.where(routed_to > 0.0, logits, -jnp.inf)
    picked = jnp.exp(logits - jnp.max(logits, axis=0, keepdims=True))
    gates_ref[...] = picked / jnp.sum(picked, axis=0, keepdims=True)

    done(all_slots(grads_ref), slot_recv.at[0])
    done(grads_ref.at[0, 0], store_sem.at[1])
    done(all_slots(outgoing), slot_send.at[0])
    done(w_ref.at[0, 0, pl.ds(0, 3), :, pl.ds(0, 2 * D)], w_send.at[0])
    done(some(3, 2 * D), w_send.at[1])
    done(some(4, 2 * D), core_send.at[0])
    done(w_ref.at[0, 0, pl.ds(0, 3), :, pl.ds(0, 256)], o_send.at[0])
    done(some(3, 256), o_send.at[1])
    done(some(4, 768), o_send.at[2])
    output_core().wait_send()
    spread_done(tok_z, tok_x, first_send)
    done(posz_ref.at[pl.ds(1, 3)], pos_send.at[0])
    done(posx_ref.at[pl.ds(1, 3)], pos_send.at[1])
    weights_out.wait()
    key_copy.wait_send()
    value_copy.wait_send()


def front(length, *arrays):
    f32, bf16, i32 = jnp.float32, jnp.bfloat16, jnp.int32
    vmem = pl.BlockSpec(memory_space=pltpu.VMEM)
    hbm = pl.BlockSpec(memory_space=pl.ANY)
    shape = jax.ShapeDtypeStruct
    out_shape = (
        shape((2, 4, 4, 32, 3 * D), bf16),
        shape((TOKENS, D), bf16),
        shape((D, TOKENS), bf16),
        shape((HALF, 2 * TOKENS), bf16),
        shape((HALF, 2 * TOKENS), bf16),
        shape((HEADS, TOKENS), f32),
        shape((TOKENS, D), bf16),
        shape((TOKENS, D), f32),
        shape((TOKENS, D), bf16),
        shape((EXPERTS, TOKENS), f32),
        shape((EXPERTS, TOKENS), i32),
        shape((4, 8, TOKENS), i32),
        shape((4, 8, TOKENS), i32),
        shape((2, 4, 4, CAP, D), bf16),
    )
    scratch = [
        pltpu.VMEM((2, 4, 4, 32, 3 * D), bf16),
        pltpu.VMEM((D, TOKENS), bf16),
        pltpu.VMEM((4, 8, TOKENS), i32),
        pltpu.VMEM((4, 8, TOKENS), i32),
        pltpu.VMEM((4, TOKENS, HALF), bf16),
        pltpu.VMEM((4, TOKENS, HALF), bf16),
        pltpu.VMEM((2, 4, 4, CAP, D), bf16),
    ]
    scratch += [pltpu.SemaphoreType.DMA((2,))]
    for count in (12, 4, 1, 2, 2, 1, 2):
        scratch += [pltpu.SemaphoreType.DMA((count,))] * 2
    return pl.pallas_call(
        front_kernel,
        out_shape=out_shape,
        in_specs=[pl.BlockSpec(memory_space=pltpu.SMEM)] + [vmem] * len(arrays),
        out_specs=[hbm] + [vmem] * (len(out_shape) - 2) + [hbm],
        scratch_shapes=scratch,
        compiler_params=pltpu.CompilerParams(
            collective_id=3, has_side_effects=True, vmem_limit_bytes=60 << 20
        ),
        name="front",
    )(length, *arrays)


def turned_back(rows, cosine, sine):
    first, second = rows[0:32], rows[32:64]
    return jnp.concatenate(
        [first * cosine + second * sine, second * cosine - first * sine], axis=0
    )


def rest_kernel(
    length_ref,
    routed_ref,
    pos_ref,
    posz_ref,
    posx_ref,
    gates_ref,
    grads_hbm,
    wg_hbm,
    wu_hbm,
    wd_hbm,
    router_ref,
    middle_ref,
    cot_ref,
    hidden_hbm,
    again_ref,
    mgain_ref,
    normed_hbm,
    mixed_hbm,
    w_hbm,
    q_hbm,
    k_hbm,
    v_hbm,
    lse_ref,
    cos_ref,
    sin_ref,
    hout_ref,
    hgrad_ref,
    again_out,
    mgain_out,
    router_out,
    own_out,
    esum_hbm,
    prod_hbm,
    mid_hbm,
    tok_z,
    tok_x,
    arrived,
    mid,
    parts_in,
    parts_in2,
    gate_out,
    gate_in,
    dot_out,
    dot_in,
    gdot_ref,
    expert_ref,
    relay_in,
    y_in,
    branch_sib,
    normed_sib,
    mixed_sib,
    grad_sib,
    kv_in,
    rs_in,
    rs_in2,
    y_parts,
    small_in,
    small_y_in,
    gain_in,
    gain_y_in,
    router_all,
    load_sem,
    store_sem,
    first_send,
    first_recv,
    slot_send,
    slot_recv,
    back_send,
    back_recv,
    part_send,
    part_recv,
    small_send,
    small_recv,
    c_send,
    c_recv,
    part_send2,
    part_recv2,
    ex_send,
    ex_recv,
    sib_send,
    sib_recv,
    rs_send,
    rs_recv,
    rs_send2,
    rs_recv2,
    ys_send,
    ys_recv,
    sm_send,
    sm_recv,
):
    y, r, x, z = place()
    me = r * CHIPS + z * 4 + x
    sibling = moved(0, 0, 1 - r)[0]
    tokens = TOKENS
    f32, bf16 = jnp.float32, jnp.bfloat16

    above, below = plane_shift(1), plane_shift(3)
    opposite = plane_shift(2)[1]
    def relayed(n):
        device = (above, below)[n][0]
        return remote(
            expert_ref.at[0, n], relay_in.at[n], ex_send.at[n], ex_recv.at[n], device
        )

    def direct(n):
        device = (above, below)[n][0]
        return remote(
            expert_ref.at[1 + n, 1 - n],
            y_in.at[n, 1 - n],
            ex_send.at[2 + n],
            ex_recv.at[2 + n],
            device,
        )

    def passed_on(n):
        device, came_from = (above, below)[n][0], (below, above)[n][1]
        part = esum_hbm.at[came_from, n]
        return remote(part, part, ex_send.at[8 + n], ex_recv.at[8 + n], device)

    def to_sibling(at, src, dst):
        return remote(src, dst, sib_send.at[at], sib_recv.at[at], sibling)

    half = pl.ds(pl.multiple_of((1 - r) * HALF, HALF), HALF)
    sib_normed = to_sibling(0, normed_hbm.at[:, half], normed_sib)
    sib_mixed = to_sibling(1, mixed_hbm.at[:, half], mixed_sib)

    meet(True, True)
    sib_mixed.start()
    sib_normed.start()

    def expert_phase(grads_ref, wg_ref, wu_ref, wd_ref, outgoing, parts_out, active, weighted, pre_grads):
        loads = [
            pltpu.make_async_copy(source, target, load_sem.at[n])
            for n, (source, target) in enumerate(
                (
                    (wg_hbm, wg_ref),
                    (wu_hbm, wu_ref),
                    (wd_hbm, wd_ref),
                    (grads_hbm, grads_ref),
                )
            )
        ]
        for load in loads:
            load.start()
        @pl.loop(1, 4)
        def _(d):
            for copy in spread(d, routed_ref, tok_z, tok_x, first_send, first_recv):
                copy.start()

        tok_z[0] = routed_ref[:, 0:HALF]
        tok_x[0] = routed_ref[:, HALF:D]

        def small(k, out, into, sign, base):
            there, dz, dx = k // CHIPS, lax.rem(k // 4, 4), lax.rem(k, 4)
            slot = r * CHIPS + lax.rem(k, CHIPS)
            return remote(
                out.at[k],
                into.at[slot],
                small_send.at[base],
                small_recv.at[base],
                moved(sign * dx, sign * dz, there)[0],
            )

        def own_slot(k):
            return k == r * CHIPS

        @pl.loop(0, GROUP)
        def _(k):
            there, dz, dx = k // CHIPS, lax.rem(k // 4, 4), lax.rem(k, 4)
            _, expert = moved(dx, dz, there)
            chosen = picks(pos_ref[pl.ds(expert, 1), :])
            gate_col = jnp.sum(
                jnp.where(chosen, gates_ref[pl.ds(expert, 1), :], 0.0), axis=1, keepdims=True
            )
            gate_out[k, 0:1, 0:CAP] = as_row(gate_col)

            @pl.when(own_slot(k))
            def _():
                gate_in[k] = gate_out[k]

            @pl.when(jnp.logical_not(own_slot(k)))
            def _():
                small(k, gate_out, gate_in, 1, 0).start()

        spread_done(tok_z, tok_x, first_recv)

        @pl.loop(0, 4)
        def _(g):
            for dx in range(4):
                dz = lax.rem(dx + g, 4)
                left_rows, right_rows = [], []
                for core in range(2):
                    at_x = core * 4 + lax.rem(x + dx, 4)
                    at_z = core * 4 + lax.rem(z + dz, 4)
                    left_rows.append(picks(posz_ref[dz, pl.ds(at_x, 1), :]))
                    right_rows.append(picks(posx_ref[dx, pl.ds(at_z, 1), :]))
                left = dot(as_hot(jnp.concatenate(left_rows, axis=0)), tok_z[dz], ((1,), (0,)))
                right = dot(as_hot(jnp.concatenate(right_rows, axis=0)), tok_x[dx], ((1,), (0,)))
                for core in range(2):
                    part = slice(core * CAP, core * CAP + CAP)
                    outgoing[core, dz, dx, :, 0:HALF] = left[part].astype(bf16)
                    outgoing[core, dz, dx, :, HALF:D] = right[part].astype(bf16)
                    came = slot_recv.at[2 * g + r]
                    send_slots(outgoing, arrived, core, dz, dx, slot_send.at[g], came, came, 1)

        def keep_produced(k):
            core, dz, dx = k // CHIPS, lax.rem(k // 4, 4), lax.rem(k, 4)
            return pltpu.make_async_copy(
                grads_ref.at[core, dz, dx],
                prod_hbm.at[core, dz, dx],
                store_sem.at[lax.rem(dz - dx + 4, 4)],
            )

        for load in loads:
            load.wait()
        done(gate_in.at[pl.ds(0, GROUP - 1)], small_recv.at[0])

        @pl.loop(0, 8)
        def _(c):
            g, core = c // 2, lax.rem(c, 2)

            @pl.when(core == r)
            def _():
                done(arrived.at[0, 0, pl.ds(0, 3)], slot_recv.at[c])

            @pl.when(core != r)
            def _():
                done(arrived.at[0, 0], slot_recv.at[c])

            @pl.when(core == 0)
            def _():
                done(outgoing.at[0, pl.ds(0, 2), :, :, pl.ds(0, 896)], slot_send.at[g])

            rows, gate_cols, grads = [], [], []
            for dx in range(4):
                dz = lax.rem(dx + g, 4)
                k = core * CHIPS + dz * 4 + dx
                rows.append(arrived[core, dz, dx])
                gate_cols.append(as_column(gate_in[k, 0:1, 0:CAP]))
                grads.append(grads_ref[core, dz, dx])
            rows = jnp.concatenate(rows, axis=0)
            gate_cols = jnp.concatenate(gate_cols, axis=0)
            grads = jnp.concatenate(grads, axis=0).astype(f32)
            gate_pre = dot(rows, wg_ref[...], ((1,), (0,)))
            up_pre = dot(rows, wu_ref[...], ((1,), (0,)))
            gate_sig = jax.nn.sigmoid(gate_pre)
            gate_act = gate_pre * gate_sig
            act = (gate_act * up_pre).astype(bf16)
            produced = dot(act, wd_ref[...], ((1,), (0,))).astype(bf16).astype(f32)
            dots = jnp.sum(produced * grads, axis=1, keepdims=True)
            produced_grad = (gate_cols * grads).astype(bf16)
            act_grad = dot(produced_grad, wd_ref[...], ((1,), (1,))).astype(bf16).astype(f32)
            gate_grad = (
                act_grad * up_pre * gate_sig * (1.0 + gate_pre * (1.0 - gate_sig))
            ).astype(bf16)
            up_grad = (act_grad * gate_act).astype(bf16)
            row_grads = dot(gate_grad, wg_ref[...], ((1,), (1,)))
            row_grads = (row_grads + dot(up_grad, wu_ref[...], ((1,), (1,)))).astype(bf16)
            produced = (produced * gate_cols).astype(bf16)
            for dx in range(4):
                dz = lax.rem(dx + g, 4)
                k = core * CHIPS + dz * 4 + dx
                part = slice(dx * CAP, dx * CAP + CAP)
                outgoing[core, dz, dx] = row_grads[part]
                send_slots(
                    outgoing,
                    mid,
                    core,
                    dz,
                    dx,
                    back_send.at[0],
                    back_recv.at[dz],
                    back_recv.at[4 + dx],
                    -1,
                )
                dot_out[k, 0:1, 0:CAP] = as_row(dots[part])

                @pl.when(own_slot(k))
                def _():
                    dot_in[k] = dot_out[k]

                @pl.when(jnp.logical_not(own_slot(k)))
                def _():
                    small(k, dot_out, dot_in, -1, 1).start()

                grads_ref[core, dz, dx] = produced[part]
                keep_produced(k).start()
                active[core, dz, dx] = act[part]
                weighted[core, dz, dx] = produced_grad[part]
                pre_grads[core, dz, dx, :, 0:HALF] = gate_grad[part]
                pre_grads[core, dz, dx, :, HALF:D] = up_grad[part]

        def send_results(g):
            done(prod_hbm.at[0, pl.ds(0, 2)], store_sem.at[g])
            for dx in range(4):
                dz = lax.rem(dx + g, 4)
                for core in range(2):
                    send_slots(
                        prod_hbm,
                        mid_hbm,
                        core,
                        dz,
                        dx,
                        c_send.at[0],
                        c_recv.at[0],
                        c_recv.at[0],
                        -1,
                        load_sem.at[8],
                    )

        send_results(0)

        all_rows = GROUP * CAP

        def quarter_grads(slot, n):
            span = pl.ds(pl.multiple_of(n * 256, 256), 256)
            left = arrived[:, :, :, :, span].reshape(all_rows, 256)
            part = dot(left, pre_grads[...].reshape(all_rows, D), ((0,), (0,))).astype(bf16)
            narrow = pl.ds(pl.multiple_of(n * 128, 128), 128)
            left = active[:, :, :, :, narrow].reshape(all_rows, 128)
            down = dot(left, weighted[...].reshape(all_rows, D), ((0,), (0,))).astype(bf16)
            for h in range(2):
                rows = part[128 * h : 128 * h + 128]
                expert_ref[slot, h, 0:128, :] = rows[:, 0:HALF]
                expert_ref[slot, h, 128:256, :] = rows[:, HALF:D]
                rows = down[64 * h : 64 * h + 64]
                expert_ref[slot, h, 256:320, :] = rows[:, 0:HALF]
                expert_ref[slot, h, 320:384, :] = rows[:, HALF:D]

        quarter_grads(0, opposite)
        for n in range(2):
            relayed(n).start()

        fold_parts(
            parts_out,
            parts_in,
            mid,
            back_recv,
            posz_ref,
            posx_ref,
            part_send.at[0],
            part_recv.at[0],
        )
        pl.loop(1, 4)(send_results)

        @pl.loop(1, 4)
        def _(slot):
            quarter_grads(slot, lax.rem(y + jnp.where(slot == 1, 1, jnp.where(slot == 2, 3, 0)), 4))

        for n in range(2):
            direct(n).start()

        done(dot_in.at[pl.ds(0, GROUP - 1)], small_recv.at[1])

        @pl.loop(0, GROUP)
        def _(k):
            there, dz, dx = k // CHIPS, lax.rem(k // 4, 4), lax.rem(k, 4)
            _, expert = moved(dx, dz, there)
            at = pl.ds(expert, 1)
            dots = as_column(dot_in[k, 0:1, 0:CAP])
            gdot_ref[at, :] = jnp.sum(
                jnp.where(picks(pos_ref[at, :]), dots, 0.0), axis=0, keepdims=True
            )

        done(parts_in.at[pl.ds(1, 3)], part_recv.at[0])
        hgrad_ref[...] = (parts_in[0].astype(f32) + parts_in[1].astype(f32)) + (
            parts_in[2].astype(f32) + parts_in[3].astype(f32)
        )
        done(all_slots(outgoing), back_send.at[0])
        done(parts_out.at[pl.ds(1, 3)], part_send.at[0])
        spread_done(tok_z, tok_x, first_send)
        done(gate_in.at[pl.ds(0, GROUP - 1)], small_send.at[0])
        done(dot_in.at[pl.ds(0, GROUP - 1)], small_send.at[1])

    pl.run_scoped(
        expert_phase,
        pltpu.VMEM((2, 4, 4, CAP, D), bf16),
        pltpu.VMEM((D, HALF), bf16),
        pltpu.VMEM((D, HALF), bf16),
        pltpu.VMEM((HALF, D), bf16),
        pltpu.VMEM((2, 4, 4, CAP, D), bf16),
        pltpu.VMEM((4, tokens, D), bf16),
        pltpu.VMEM((2, 4, 4, CAP, HALF), bf16),
        pltpu.VMEM((2, 4, 4, CAP, D), bf16),
        pltpu.VMEM((2, 4, 4, CAP, D), bf16),
    )

    def finish_phase(w_ref, q_ref, k_ref, v_ref, normed_ref, mixed_ref, hidden_ref, parts_out2, quarter_sum, relay_out, branch_own, mg_t, grad_t, kv_own, kv_out, weight_part, rs_out, y_out, small_out, small_y, gain_out, gain_y):
        loads = [
            pltpu.make_async_copy(source, target, load_sem.at[n])
            for n, (source, target) in enumerate(
                (
                    (w_hbm, w_ref),
                    (q_hbm, q_ref),
                    (k_hbm, k_ref),
                    (v_hbm, v_ref),
                    (normed_hbm, normed_ref),
                    (mixed_hbm, mixed_ref),
                    (hidden_hbm, hidden_ref),
                )
            )
        ]
        for load in loads:
            load.start()

        def weight(first, width):
            return w_ref[:, :, :, :, first : first + width].reshape(D, width)

        def merged(n):
            device = (above, below)[n][0]
            return remote(
                relay_out.at[n], y_in.at[n, n], ex_send.at[4 + n], ex_recv.at[4 + n], device
            )

        def handed(n):
            device = (above, below)[n][0]
            return remote(
                quarter_sum, esum_hbm.at[y], ex_send.at[6 + n], ex_recv.at[6 + n], device
            )

        def sib_keyval(p):
            return to_sibling(3 + p, kv_out.at[p], kv_in.at[p])

        def sib_grads(p, part):
            rows = pl.ds(p * D + part * HALF, HALF)
            return to_sibling(5 + 2 * p + part, grad_t.at[rows], grad_sib.at[rows])

        sib_branch = to_sibling(2, branch_own, branch_sib)

        for n in range(2):
            relayed(n).wait_recv()
            total = relay_in[n].astype(f32) + expert_ref[1 + n, n].astype(f32)
            relay_out[n] = total.astype(bf16)
            merged(n).start()

        gates = gates_ref[...]
        gdot = gdot_ref[...]
        logit_grad = gates * (gdot - jnp.sum(gates * gdot, axis=0, keepdims=True))
        high, rest = split_two(logit_grad)
        router_part = dot(high, routed_ref[...], ((1,), (0,)))
        router_part = router_part + dot(rest, routed_ref[...], ((1,), (0,)))
        routed_grad = dot(high, router_ref[...], ((0,), (0,)))
        routed_grad = routed_grad + dot(rest, router_ref[...], ((0,), (0,)))
        routed_grad = routed_grad + hgrad_ref[...]
        live = (
            r * tokens + lax.broadcasted_iota(jnp.int32, (tokens, 1), 0) < length_ref[0]
        ).astype(f32)
        middle = middle_ref[...]
        scale = lax.rsqrt(jnp.mean(middle * middle, axis=1, keepdims=True) + epsilon)
        rows = middle * scale
        moe_part = jnp.sum(routed_grad * rows, axis=0, keepdims=True)
        scaled = routed_grad * mgain_ref[...]
        inner = jnp.mean(scaled * rows, axis=1, keepdims=True)
        middle_grad = cot_ref[...].astype(f32) * live + scale * (scaled - rows * inner)
        hgrad_ref[...] = middle_grad
        branch_own[...] = middle_grad.astype(bf16)
        sib_branch.start()
        for j in range(8):
            part = slice(128 * j, 128 * j + 128)
            small_out[:, j, :] = router_part[:, part]
            small_out[:, 8 + j, :] = jnp.broadcast_to(moe_part[:, part], (GROUP, 128))

        def tiny(k):
            device, other = step_of(k, 1)
            return remote(small_out.at[other], small_in.at[me], sm_send.at[0], sm_recv.at[0], device)

        @pl.loop(1, GROUP)
        def _(k):
            tiny(k).start()

        small_in[me] = small_out[me]

        for load in loads:
            load.wait()
        mg_t[...] = dot(weight(2 * D, D), branch_own[...], ((1,), (1,))).astype(bf16)

        mine = pl.ds(pl.multiple_of(r * HALF, HALF), HALF)

        def columns(p):
            return pl.ds(p * D, HALF), pl.ds(p * D + HALF, HALF)

        def first_step(p, d):
            left, right = columns(p)
            return (
                remote(
                    weight_part.at[lax.rem(z + d, 4), :, :, left],
                    rs_in.at[d, :, :, left],
                    rs_send.at[p],
                    rs_recv.at[p],
                    moved(0, d, r)[0],
                ),
                remote(
                    weight_part.at[:, lax.rem(x + d, 4), :, right],
                    rs_in.at[d, :, :, right],
                    rs_send.at[p],
                    rs_recv.at[p],
                    moved(d, 0, r)[0],
                ),
            )

        def second_step(p, d):
            left, right = columns(p)
            return (
                remote(
                    rs_out.at[lax.rem(x + d, 4), :, left],
                    rs_in2.at[d, :, left],
                    rs_send2.at[p],
                    rs_recv2.at[p],
                    moved(d, 0, r)[0],
                ),
                remote(
                    rs_out.at[lax.rem(z + d, 4), :, right],
                    rs_in2.at[d, :, right],
                    rs_send2.at[p],
                    rs_recv2.at[p],
                    moved(0, d, r)[0],
                ),
            )

        def across(p, n):
            cols = pl.ds(p * D, D)
            return remote(
                y_out.at[:, cols],
                y_parts.at[y, :, cols],
                ys_send.at[p],
                ys_recv.at[p],
                plane_shift(n)[0],
            )

        def sum_first(p, total):
            weight_part[:, :, :, p * D : p * D + D] = total.astype(bf16).reshape(4, 4, 32, D)

            @pl.loop(1, 4)
            def _(d):
                for copy in first_step(p, d):
                    copy.start()

        def sum_second(p):
            left, right = columns(p)

            done(rs_in.at[pl.ds(1, 3), :, :, pl.ds(p * D, D)], rs_recv.at[p])

            total = weight_part[z, :, :, left].astype(f32)
            other = weight_part[:, x, :, right].astype(f32)
            for d in range(1, 4):
                total = total + rs_in[d, :, :, left].astype(f32)
                other = other + rs_in[d, :, :, right].astype(f32)
            rs_out[:, :, left] = total.astype(bf16)
            rs_out[:, :, right] = other.astype(bf16)

            @pl.loop(1, 4)
            def _(d):
                for copy in second_step(p, d):
                    copy.start()

        def sum_third(p):
            left, right = columns(p)

            done(rs_in2.at[pl.ds(1, 3), :, pl.ds(p * D, D)], rs_recv2.at[p])

            total = rs_out[x, :, left].astype(f32)
            other = rs_out[z, :, right].astype(f32)
            for d in range(1, 4):
                total = total + rs_in2[d, :, left].astype(f32)
                other = other + rs_in2[d, :, right].astype(f32)
            y_out[:, left] = total.astype(bf16)
            y_out[:, right] = other.astype(bf16)
            y_parts[y, :, left] = total.astype(bf16)
            y_parts[y, :, right] = other.astype(bf16)
            for n in range(1, PLANES):
                across(p, n).start()

        sib_mixed.wait_recv()
        sib_branch.wait_recv()
        total = dot(mixed_ref[:, mine], branch_own[...], ((0,), (0,)))
        sum_first(2, total + dot(mixed_sib[...], branch_sib[...], ((0,), (0,))))

        key_live = lax.broadcasted_iota(jnp.int32, (2 * tokens, 1), 0) < length_ref[0]
        score_scale = HEAD ** (-0.5)
        cosine, sine = cos_ref[...], sin_ref[...]
        first_core = r == 0

        def key_head(p, i):
            g = 4 * p + i
            head = pl.ds(pl.multiple_of(g * HEAD, HEAD), HEAD)
            keys, values = k_ref[head, :], v_ref[head, :]
            key_sum, value_sum = None, None
            for j in range(2):
                at = pl.ds(pl.multiple_of((2 * g + j) * HEAD, HEAD), HEAD)
                query, mixed_grad = q_ref[at, :], mg_t[at, :]
                scores = dot(keys, query, ((0,), (0,))) * score_scale
                scores = jnp.where(key_live, scores, NEG)
                probs = jnp.exp(scores - lse_ref[pl.ds(2 * g + j, 1), :])
                prob_grad = dot(values, mixed_grad, ((0,), (0,)))
                value_part = dot(mixed_grad, probs.astype(bf16), ((1,), (1,)))
                inner = jnp.sum(probs * prob_grad, axis=0, keepdims=True)
                score_grad = (probs * (prob_grad - inner)).astype(bf16)
                key_part = dot(query, score_grad, ((1,), (1,)))
                query_grad = dot(keys, score_grad, ((1,), (0,))) * score_scale
                to = pl.ds(pl.multiple_of(p * D + (2 * i + j) * HEAD, HEAD), HEAD)
                grad_t[to, :] = turned_back(query_grad, cosine, sine).astype(bf16)
                key_sum = key_part if key_sum is None else key_sum + key_part
                value_sum = value_part if value_sum is None else value_sum + value_part
            key_sum = key_sum * score_scale
            for n, part in enumerate((key_sum, value_sum)):
                to = pl.ds(pl.multiple_of(256 * n + i * HEAD, HEAD), HEAD)
                kv_own[p, to, :] = jnp.where(first_core, part[:, :tokens], part[:, tokens:])
                away = jnp.where(first_core, part[:, tokens:], part[:, :tokens])
                kv_out[p, to, :] = away.astype(bf16)

        def heads(p, first, last):
            @pl.loop(first, last)
            def _(i):
                key_head(p, i)

        def whole_keyval(p):
            sib_keyval(p).wait_recv()
            for i in range(4):
                rows = slice(HEAD * i, HEAD * i + HEAD)
                total = kv_own[p, rows, :] + kv_in[p, rows, :].astype(f32)
                to = p * D + HALF + HEAD * i
                grad_t[to : to + HEAD, :] = turned_back(total, cosine, sine).astype(bf16)
            total = kv_own[p, 256:512, :] + kv_in[p, 256:512, :].astype(f32)
            grad_t[p * D + HALF + 256 : p * D + D, :] = total.astype(bf16)
            sib_grads(p, 1).start()

        def projections(p):
            rows = slice(p * D, p * D + D)
            for part in range(2):
                sib_grads(p, part).wait_recv()
            total = dot(normed_ref[:, mine], grad_t[rows, :], ((0,), (1,)))
            sum_first(p, total + dot(normed_sib[...], grad_sib[rows, :], ((0,), (1,))))

        def inputs_part(p):
            return dot(grad_t[p * D : p * D + D, :], weight(p * D, D), ((0,), (1,)))

        heads(0, 0, 4)
        sib_keyval(0).start()
        sib_grads(0, 0).start()

        heads(1, 0, 4)
        sib_keyval(1).start()
        sib_grads(1, 0).start()
        whole_keyval(0)
        sib_normed.wait_recv()
        projections(0)
        whole_keyval(1)
        normed_grad = inputs_part(0)
        projections(1)
        normed_grad = normed_grad + inputs_part(1)

        inputs = hidden_ref[...].astype(f32)
        scale = lax.rsqrt(jnp.mean(inputs * inputs, axis=1, keepdims=True) + epsilon)
        rows = inputs * scale
        attn_part = jnp.sum(normed_grad * rows, axis=0, keepdims=True)
        for j in range(8):
            gain_out[j : j + 1, :] = attn_part[:, 128 * j : 128 * j + 128]

        def gain(k):
            device, _ = step_of(k, 1)
            return remote(gain_out, gain_in.at[me], sm_send.at[3], sm_recv.at[3], device)

        @pl.loop(1, GROUP)
        def _(k):
            gain(k).start()

        gain_in[me] = gain_out[...]
        scaled = normed_grad * again_ref[...]
        inner = jnp.mean(scaled * rows, axis=1, keepdims=True)
        hgrad_ref[...] += scale * (scaled - rows * inner)

        for n in range(2):
            direct(n).wait_recv()
            merged(n).wait_recv()
        for n in range(2):
            total = expert_ref[3, n].astype(f32) + (y_in[0, n].astype(f32) + y_in[1, n].astype(f32))
            quarter_sum[n] = total.astype(bf16)
        quarter_out = pltpu.make_async_copy(quarter_sum, esum_hbm.at[y], load_sem.at[9])
        quarter_out.start()
        for n in range(2):
            handed(n).start()

        sum_second(2)

        done(small_in.at[pl.ds(0, GROUP - 1)], sm_recv.at[0])

        def small_across(n):
            device, _ = plane_shift(n)
            return remote(
                small_y, small_y_in.at[y], sm_send.at[1], sm_recv.at[1], device
            )

        small_y[...] = jnp.sum(small_in[...], axis=0)
        small_y_in[y] = small_y[...]
        for n in range(1, PLANES):
            small_across(n).start()

        done(all_slots(mid_hbm), c_recv.at[0])
        done(mid_hbm.at[0, 0], load_sem.at[8])
        results_in = pltpu.make_async_copy(mid_hbm, mid, load_sem.at[10])
        results_in.start()
        results_in.wait()
        fold_parts(
            parts_out2,
            parts_in2,
            mid,
            None,
            posz_ref,
            posx_ref,
            part_send2.at[0],
            part_recv2.at[0],
        )
        sum_third(2)
        sum_second(0)

        done(small_y_in.at[pl.ds(0, 3)], sm_recv.at[1])
        totals = small_y_in[0] + small_y_in[1] + small_y_in[2] + small_y_in[3]
        mgain_out[...] = totals[8:16]
        router_all[me] = totals[0:8]

        def router_row(k):
            device, _ = step_of(k, 1)
            return remote(
                router_all.at[me], router_all.at[me], sm_send.at[2], sm_recv.at[2], device
            )

        @pl.loop(1, GROUP)
        def _(k):
            router_row(k).start()

        done(gain_in.at[pl.ds(0, GROUP - 1)], sm_recv.at[3])

        gain_y[...] = jnp.sum(gain_in[...], axis=0)
        gain_y_in[y] = gain_y[...]

        def gain_across(n):
            device, _ = plane_shift(n)
            return remote(gain_y, gain_y_in.at[y], sm_send.at[4], sm_recv.at[4], device)

        for n in range(1, PLANES):
            gain_across(n).start()

        sum_second(1)
        sum_third(0)

        for n in range(2):
            handed(n).wait_recv()
            passed_on(n).start()

        sum_third(1)

        done(parts_in2.at[pl.ds(1, 3)], part_recv2.at[0])
        mixture = (parts_in2[0].astype(f32) + parts_in2[1].astype(f32)) + (
            parts_in2[2].astype(f32) + parts_in2[3].astype(f32)
        )
        hout_ref[...] = ((middle_ref[...] + mixture) * live).astype(bf16)

        done(gain_y_in.at[pl.ds(0, 3)], sm_recv.at[4])
        again_out[...] = (gain_y_in[0] + gain_y_in[1]) + (gain_y_in[2] + gain_y_in[3])

        done(router_all.at[pl.ds(0, GROUP - 1)], sm_recv.at[2])

        router_out[...] = router_all[...]

        done(all_slots(mid_hbm), c_send.at[0])
        done(parts_out2.at[pl.ds(1, 3)], part_send2.at[0])
        done(small_in.at[pl.ds(0, GROUP - 1)], sm_send.at[0])
        done(small_y_in.at[pl.ds(0, 3)], sm_send.at[1])
        done(router_all.at[pl.ds(0, GROUP - 1)], sm_send.at[2])
        done(gain_in.at[pl.ds(0, GROUP - 1)], sm_send.at[3])
        done(gain_y_in.at[pl.ds(0, 3)], sm_send.at[4])
        for p in range(3):
            done(rs_in.at[pl.ds(1, 3), :, :, pl.ds(p * D, D)], rs_send.at[p])
            done(rs_in2.at[pl.ds(1, 3), :, pl.ds(p * D, D)], rs_send2.at[p])
            done(y_parts.at[pl.ds(0, 3), :, pl.ds(p * D, D)], ys_recv.at[p])
            done(y_parts.at[pl.ds(0, 3), :, pl.ds(p * D, D)], ys_send.at[p])
        for n in range(2):
            for copy in (relayed(n), direct(n), merged(n), handed(n), passed_on(n)):
                copy.wait_send()
        for copy in (sib_normed, sib_mixed, sib_branch):
            copy.wait_send()
        for p in range(2):
            sib_keyval(p).wait_send()
            for part in range(2):
                sib_grads(p, part).wait_send()
        for n in range(2):
            passed_on(n).wait_recv()
        quarter_out.wait()
        own_out[...] = (y_parts[0].astype(f32) + y_parts[1].astype(f32)) + (
            y_parts[2].astype(f32) + y_parts[3].astype(f32)
        )

    pl.run_scoped(
        finish_phase,
        pltpu.VMEM((2, 4, 4, 32, 3 * D), bf16),
        pltpu.VMEM((D, tokens), bf16),
        pltpu.VMEM((HALF, 2 * tokens), bf16),
        pltpu.VMEM((HALF, 2 * tokens), bf16),
        pltpu.VMEM((tokens, D), bf16),
        pltpu.VMEM((tokens, D), bf16),
        pltpu.VMEM((tokens, D), bf16),
        pltpu.VMEM((4, tokens, D), bf16),
        pltpu.VMEM((2, 384, HALF), bf16),
        pltpu.VMEM((2, 384, HALF), bf16),
        pltpu.VMEM((tokens, D), bf16),
        pltpu.VMEM((D, tokens), bf16),
        pltpu.VMEM((2 * D, tokens), bf16),
        pltpu.VMEM((2, HALF, tokens), f32),
        pltpu.VMEM((2, HALF, tokens), bf16),
        pltpu.VMEM((4, 4, 32, 3 * D), bf16),
        pltpu.VMEM((4, 32, 3 * D), bf16),
        pltpu.VMEM((32, 3 * D), bf16),
        pltpu.VMEM((GROUP, 16, 128), f32),
        pltpu.VMEM((16, 128), f32),
        pltpu.VMEM((8, 128), f32),
        pltpu.VMEM((8, 128), f32),
    )


def rest(length, *arrays):
    tokens = TOKENS
    f32, bf16 = jnp.float32, jnp.bfloat16
    vmem = pl.BlockSpec(memory_space=pltpu.VMEM)
    hbm = pl.BlockSpec(memory_space=pl.ANY)
    shape = jax.ShapeDtypeStruct
    sems = pltpu.SemaphoreType.DMA
    scratch = [
        pltpu.VMEM((4, tokens, HALF), bf16),
        pltpu.VMEM((4, tokens, HALF), bf16),
        pltpu.VMEM((2, 4, 4, CAP, D), bf16),
        pltpu.VMEM((2, 4, 4, CAP, D), bf16),
        pltpu.VMEM((4, tokens, D), bf16),
        pltpu.VMEM((4, tokens, D), bf16),
        pltpu.VMEM((GROUP, 8, 128), f32),
        pltpu.VMEM((GROUP, 8, 128), f32),
        pltpu.VMEM((GROUP, 8, 128), f32),
        pltpu.VMEM((GROUP, 8, 128), f32),
        pltpu.VMEM((EXPERTS, tokens), f32),
        pltpu.VMEM((4, 2, 384, HALF), bf16),
        pltpu.VMEM((2, 384, HALF), bf16),
        pltpu.VMEM((2, 2, 384, HALF), bf16),
        pltpu.VMEM((tokens, D), bf16),
        pltpu.VMEM((tokens, HALF), bf16),
        pltpu.VMEM((tokens, HALF), bf16),
        pltpu.VMEM((2 * D, tokens), bf16),
        pltpu.VMEM((2, HALF, tokens), bf16),
        pltpu.VMEM((4, 4, 32, 3 * D), bf16),
        pltpu.VMEM((4, 32, 3 * D), bf16),
        pltpu.VMEM((PLANES, 32, 3 * D), bf16),
        pltpu.VMEM((GROUP, 16, 128), f32),
        pltpu.VMEM((PLANES, 16, 128), f32),
        pltpu.VMEM((GROUP, 8, 128), f32),
        pltpu.VMEM((PLANES, 8, 128), f32),
        pltpu.VMEM((GROUP, 8, 128), f32),
    ]
    for count in (11, 4, 2, 2, 4, 8, 1, 8, 1, 1, 2, 2, 1, 1, 1, 1, 10, 10, 9, 9, 3, 3, 3, 3, 3, 3, 5, 5):
        scratch += [sems((count,))]
    in_specs = [pl.BlockSpec(memory_space=pltpu.SMEM)] + [vmem] * len(arrays)
    for n in (6, 7, 8, 9, 13, 16, 17, 18, 19, 20, 21):
        in_specs[n] = hbm
    return pl.pallas_call(
        rest_kernel,
        out_shape=(
            shape((tokens, D), bf16),
            shape((tokens, D), f32),
            shape((8, 128), f32),
            shape((8, 128), f32),
            shape((GROUP, 8, 128), f32),
            shape((32, 3 * D), f32),
            shape((4, 2, 384, HALF), bf16),
            shape((2, 4, 4, CAP, D), bf16),
            shape((2, 4, 4, CAP, D), bf16),
        ),
        in_specs=in_specs,
        out_specs=[vmem] * 6 + [hbm] * 3,
        scratch_shapes=scratch,
        compiler_params=pltpu.CompilerParams(
            collective_id=2, has_side_effects=True, vmem_limit_bytes=62 << 20
        ),
        name="rest",
    )(length, *arrays)[:7]


def spread_kernel(
    hout_ref,
    hgrad_ref,
    own_ref,
    esum_ref,
    router_ref,
    again_ref,
    mgain_ref,
    hout_out,
    hgrad_out,
    q_out,
    k_out,
    v_out,
    o_out,
    gate_out,
    up_out,
    down_out,
    router_out,
    again_out,
    mgain_out,
):
    f32 = jnp.float32
    hout_out[...] = hout_ref[...]
    hgrad_out[...] = hgrad_ref[...]
    for p in range(2):
        q_out[:, p * HALF : p * HALF + HALF] = own_ref[:, p * D : p * D + HALF]
        k_out[:, p * 256 : p * 256 + 256] = own_ref[:, p * D + HALF : p * D + 768]
        v_out[:, p * 256 : p * 256 + 256] = own_ref[:, p * D + 768 : p * D + D]
    o_out[...] = own_ref[:, 2 * D : 3 * D]
    for h in range(2):
        gate_out[0, 128 * h : 128 * h + 128, :] = esum_ref[0, h, 0:128, :].astype(f32)
        up_out[0, 128 * h : 128 * h + 128, :] = esum_ref[0, h, 128:256, :].astype(f32)
        down_out[0, 64 * h : 64 * h + 64, 0:HALF] = esum_ref[0, h, 256:320, :].astype(f32)
        down_out[0, 64 * h : 64 * h + 64, HALF:D] = esum_ref[0, h, 320:384, :].astype(f32)
    for j in range(8):
        router_out[:, 128 * j : 128 * j + 128] = router_ref[:, j, :]
    again_out[...] = again_ref[...]
    mgain_out[...] = mgain_ref[...]


def spread_out(*arrays):
    f32, bf16 = jnp.float32, jnp.bfloat16
    shape = jax.ShapeDtypeStruct

    def whole(*dims):
        return pl.BlockSpec(dims, lambda i: (0,) * len(dims))

    def rows(count, width):
        return pl.BlockSpec((count, width), lambda i: (i, 0))

    def expert_rows(count, width):
        return pl.BlockSpec((1, count, width), lambda i: (0, i, 0))

    return pl.pallas_call(
        spread_kernel,
        grid=(4,),
        out_shape=(
            shape((TOKENS, D), bf16),
            shape((TOKENS, D), f32),
            shape((32, D), f32),
            shape((32, HALF), f32),
            shape((32, HALF), f32),
            shape((32, D), f32),
            shape((1, D, HALF), f32),
            shape((1, D, HALF), f32),
            shape((1, HALF, D), f32),
            shape((EXPERTS, D), f32),
            shape((8, 128), f32),
            shape((8, 128), f32),
        ),
        in_specs=[
            rows(64, D),
            rows(64, D),
            whole(32, 3 * D),
            pl.BlockSpec((1, 2, 384, HALF), lambda i: (i, 0, 0, 0)),
            whole(GROUP, 8, 128),
            whole(8, 128),
            whole(8, 128),
        ],
        out_specs=[
            rows(64, D),
            rows(64, D),
            whole(32, D),
            whole(32, HALF),
            whole(32, HALF),
            whole(32, D),
            expert_rows(256, HALF),
            expert_rows(256, HALF),
            expert_rows(128, D),
            whole(EXPERTS, D),
            whole(8, 128),
            whole(8, 128),
        ],
        name="spread_out",
    )(*arrays)


def on_device(
    hidden_in,
    cotangent,
    lengths,
    routes,
    priority,
    attn_gain,
    query_weight,
    key_weight,
    value_weight,
    output_weight,
    moe_gain,
    router,
    gate_weight,
    up_weight,
    down_weight,
):
    tok_count = hidden_in.shape[0]
    positions = lax.axis_index("row") * tok_count + jnp.arange(tok_count, dtype=jnp.int32)
    half_dim = HEAD // 2
    frequency = rotary_base ** (-jnp.arange(half_dim, dtype=jnp.float32) / half_dim)
    angles = frequency[:, None] * positions.astype(jnp.float32)[None, :]
    cosine, sine = jnp.cos(angles), jnp.sin(angles)
    router_t = router.T
    (
        weights,
        normed,
        queries,
        keys,
        values,
        log_total,
        mixed_rows,
        middle,
        routed,
        gates,
        pos,
        posz,
        posx,
        arrived_grad,
    ) = front(
        lengths,
        hidden_in,
        cotangent,
        routes.T,
        priority,
        attn_gain[None],
        moe_gain[None],
        query_weight,
        key_weight,
        value_weight,
        output_weight,
        router_t,
        cosine,
        sine,
    )
    summed = rest(
        lengths,
        routed,
        pos,
        posz,
        posx,
        gates,
        arrived_grad,
        gate_weight[0],
        up_weight[0],
        down_weight[0],
        router_t,
        middle,
        cotangent,
        hidden_in,
        attn_gain[None],
        moe_gain[None],
        normed,
        mixed_rows,
        weights,
        queries,
        keys,
        values,
        log_total,
        cosine,
        sine,
    )
    hidden_out, hidden_grad, attn_gain_sum, moe_gain_sum, router_sum, own_rows, expert_sum = summed
    (
        hidden_out,
        hidden_grad,
        query_grad,
        key_grad,
        value_grad,
        output_grad,
        gate_grad,
        up_grad,
        down_grad,
        router_grad,
        attn_gain_sum,
        moe_gain_sum,
    ) = spread_out(
        hidden_out, hidden_grad, own_rows, expert_sum, router_sum, attn_gain_sum, moe_gain_sum
    )
    return (
        hidden_out,
        hidden_grad,
        attn_gain_sum.reshape(D),
        query_grad,
        key_grad,
        value_grad,
        output_grad,
        moe_gain_sum.reshape(D),
        router_grad.T,
        gate_grad,
        up_grad,
        down_grad,
    )


def solution(mesh):
    return jax.shard_map(
        on_device,
        mesh=mesh,
        in_specs=(
            P(("dp", "col", "row"), None),
            P(("dp", "col", "row"), None),
            P(("dp", "col")),
            P(("dp", "col", "row"), None),
            P(("dp", "col", "row"), None),
            P(),
            P(("row", "col"), None),
            P(("row", "col"), None),
            P(("row", "col"), None),
            P(("row", "col"), None),
            P(),
            P(),
            P(("row", "col"), None, None),
            P(("row", "col"), None, None),
            P(("row", "col"), None, None),
        ),
        out_specs=(
            P(("dp", "col", "row"), None),
            P(("dp", "col", "row"), None),
            P(),
            P(("row", "col"), None),
            P(("row", "col"), None),
            P(("row", "col"), None),
            P(("row", "col"), None),
            P(),
            P(),
            P(("row", "col"), None, None),
            P(("row", "col"), None, None),
            P(("row", "col"), None, None),
        ),
        check_vma=False,
    )
```

```python
import jax
import jax.numpy as jnp
from jax import lax
from jax.experimental import pallas as pl
from jax.experimental.pallas import tpu as pltpu
from jax.sharding import PartitionSpec as P

D = 1024
HEADS = 16
HEAD = 64
KV_HEADS = 8
EXPERTS = 32
TOP = 8
CAP = 64


epsilon = 1e-05
rotary_base = 10000.0


MESH = pl.DeviceIdType.MESH
GROUP = 32
PLANES = 4
CHIPS = 16
HALF = D // 2
TOKENS = 256
NEG = -1000000000.0


def place():
    col = lax.axis_index("col")
    return lax.axis_index("dp"), lax.axis_index("row"), lax.rem(col, 4), col // 4


def moved(dx, dz, core):
    y, r, x, z = place()
    col = lax.rem(z + dz + 4, 4) * 4 + lax.rem(x + dx + 4, 4)
    return (y, core, col), core * CHIPS + col


def plane_shift(n):
    y, r, x, z = place()
    other = lax.rem(y + n, PLANES)
    return (other, r, z * 4 + x), other


def step_of(k, sign):
    y, r, x, z = place()
    return moved(sign * lax.rem(k, 4), sign * lax.rem(k // 4, 4), lax.rem(r + k // CHIPS, 2))


def remote(src, dst, send_sem, recv_sem, device):
    return pltpu.make_async_remote_copy(
        src_ref=src,
        dst_ref=dst,
        send_sem=send_sem,
        recv_sem=recv_sem,
        device_id=device,
        device_id_type=MESH,
    )


def done(ref, sem):
    pltpu.make_async_copy(ref, ref, sem).wait()


def meet(plane, planes):
    barrier = pltpu.get_barrier_semaphore()
    y, r, x, z = place()

    def greet(device):
        pl.semaphore_signal(barrier, inc=1, device_id=device, device_id_type=MESH)

    if plane:

        @pl.loop(1, GROUP)
        def _(k):
            greet(step_of(k, 1)[0])

        count = GROUP - 1
    else:
        for core in range(2):

            @pl.loop(1, 4)
            def _(d):
                greet(moved(d, 0, core)[0])
                greet(moved(0, d, core)[0])

        greet(moved(0, 0, 1 - r)[0])
        count = 13
    if planes:
        for n in range(1, PLANES):
            greet(plane_shift(n)[0])
        count += PLANES - 1
    pl.semaphore_wait(barrier, count)


def eye(n):
    return lax.broadcasted_iota(jnp.int32, (n, n), 0) == lax.broadcasted_iota(
        jnp.int32, (n, n), 1
    )


def as_row(column):
    return jnp.sum(jnp.where(eye(column.shape[0]), column, 0.0), axis=0, keepdims=True)


def as_column(row_vec):
    return jnp.sum(jnp.where(eye(row_vec.shape[1]), row_vec, 0.0), axis=1, keepdims=True)


def dot(a, b, dims):
    return lax.dot_general(a, b, (dims, ((), ())), preferred_element_type=jnp.float32)


def split_two(values):
    high = values.astype(jnp.bfloat16)
    return high, (values - high.astype(jnp.float32)).astype(jnp.bfloat16)


def picks(positions):
    slots = lax.broadcasted_iota(jnp.int32, (CAP, positions.shape[1]), 0)
    return slots == positions


def as_hot(mask):
    return mask.astype(jnp.float32).astype(jnp.bfloat16)


LEFT = pl.ds(0, HALF)
RIGHT = pl.ds(HALF, HALF)


def spread(d, source, tok_z, tok_x, send_sem, recv_sem):
    y, r, x, z = place()
    return (
        remote(
            source.at[:, LEFT], tok_z.at[d], send_sem.at[0], recv_sem.at[0], moved(0, d, r)[0]
        ),
        remote(
            source.at[:, RIGHT], tok_x.at[d], send_sem.at[1], recv_sem.at[1], moved(d, 0, r)[0]
        ),
    )


def spread_done(tok_z, tok_x, sem):
    done(tok_z.at[pl.ds(1, 3)], sem.at[0])
    done(tok_x.at[pl.ds(1, 3)], sem.at[1])


def is_local(core, offset):
    y, r, x, z = place()
    return (core == r) & (offset == 0)


def send_slots(
    out,
    into,
    there,
    dz,
    dx,
    send_sem,
    recv_left,
    recv_right,
    sign,
    local_sem=None,
    halves=(True, True),
):
    y, r, x, z = place()

    def one(cols, offset, device, recv_sem):
        source, target = out.at[there, dz, dx, :, cols], into.at[r, dz, dx, :, cols]

        @pl.when(jnp.logical_not(is_local(there, offset)))
        def _():
            remote(source, target, send_sem, recv_sem, device).start()

        @pl.when(is_local(there, offset))
        def _():
            if local_sem is None:
                target[...] = source[...]
            else:
                pltpu.make_async_copy(source, target, local_sem).start()

    if halves[0]:
        one(LEFT, dx, moved(sign * dx, 0, there)[0], recv_left)
    if halves[1]:
        one(RIGHT, dz, moved(0, sign * dz, there)[0], recv_right)


def all_slots(ref):
    return ref.at[:, :, :, :, pl.ds(0, 896)]


def line_rows(line, d, axis):
    y, r, x, z = place()
    own = x if axis == 0 else z
    return [
        line[d, pl.ds(core * 4 + lax.rem(own + i, 4), 1), :] for core in range(2) for i in range(4)
    ]


def line_hot(line, d, axis):
    return as_hot(jnp.concatenate([picks(p) for p in line_rows(line, d, axis)], axis=0))


def add_up(mid, line, d, axis):
    if axis == 0:
        rows = mid[:, d, :, :, 0:HALF]
    else:
        rows = mid[:, :, d, :, HALF:D]
    return dot(line_hot(line, d, axis), rows.reshape(8 * CAP, HALF), ((0,), (0,))).astype(
        jnp.bfloat16
    )


def part_copies(d, out, into, send_sem, recv_sem):
    y, r, x, z = place()
    return (
        lambda: remote(
            out.at[d, :, LEFT], into.at[d, :, LEFT], send_sem, recv_sem, moved(0, -d, r)[0]
        ),
        lambda: remote(
            out.at[d, :, RIGHT], into.at[d, :, RIGHT], send_sem, recv_sem, moved(-d, 0, r)[0]
        ),
    )


def fold_left(out, into, mid, slot_recv, posz_ref, send_sem, recv_sem):
    @pl.loop(0, 4)
    def _(d):
        if slot_recv is not None:
            done(mid.at[0, 0, :, :, pl.ds(0, 896)], slot_recv.at[d])
        left = add_up(mid, posz_ref, d, 0)

        @pl.when(d == 0)
        def _():
            into[0, :, 0:HALF] = left

        @pl.when(d != 0)
        def _():
            out[d, :, 0:HALF] = left
            part_copies(d, out, into, send_sem, recv_sem)[0]().start()


def fold_right(out, into, mid, slot_recv, posx_ref, send_sem, recv_sem):
    @pl.loop(0, 4)
    def _(d):
        if slot_recv is not None:
            done(mid.at[0, 0, :, :, pl.ds(0, 896)], slot_recv.at[4 + d])
        right = add_up(mid, posx_ref, d, 1)

        @pl.when(d == 0)
        def _():
            into[0, :, HALF:D] = right

        @pl.when(d != 0)
        def _():
            out[d, :, HALF:D] = right
            part_copies(d, out, into, send_sem, recv_sem)[1]().start()


def front_kernel(
    length_ref,
    hidden_ref,
    cot_ref,
    routes_ref,
    prio_ref,
    again_ref,
    mgain_ref,
    wq_ref,
    wk_ref,
    wv_ref,
    wo_ref,
    router_ref,
    cos_ref,
    sin_ref,
    w_hbm,
    normed_ref,
    q_ref,
    k_ref,
    v_ref,
    lse_ref,
    mixed_ref,
    middle_ref,
    routed_ref,
    gates_ref,
    pos_ref,
    posz_ref,
    posx_ref,
    grads_ref,
    w_ref,
    mixed_t,
    posz_out,
    posx_out,
    tok_z,
    tok_x,
    outgoing,
    store_sem,
    w_send,
    w_recv,
    o_send,
    o_recv,
    core_send,
    core_recv,
    kv_send,
    kv_recv,
    first_send,
    first_recv,
    slot_send,
    slot_recv,
    pos_send,
    pos_recv,
):
    y, r, x, z = place()
    f32, bf16 = jnp.float32, jnp.bfloat16
    sibling = moved(0, 0, 1 - r)[0]
    meet(False, True)

    for p in range(2):
        part = slice(256 * p, 256 * p + 256)
        w_ref[r, z, x, :, D * p : D * p + HALF] = wq_ref[:, HALF * p : HALF * p + HALF]
        w_ref[r, z, x, :, D * p + HALF : D * p + 768] = wk_ref[:, part]
        w_ref[r, z, x, :, D * p + 768 : D * p + D] = wv_ref[:, part]
    front, rear, output = pl.ds(0, D), pl.ds(D, D), pl.ds(2 * D, D)
    quarter = pl.ds(pl.multiple_of(2 * D + 256 * y, 256), 256)

    def line_step(d):
        mine_q, mine_o = w_ref.at[r, z, x, :, front], w_ref.at[r, z, x, :, rear]
        return (
            remote(mine_q, mine_q, w_send.at[0], w_recv.at[d], moved(0, d, r)[0]),
            remote(mine_o, mine_o, w_send.at[0], w_recv.at[4 + d], moved(d, 0, r)[0]),
        )

    def cross_step(e, d):
        from_z = w_ref.at[r, lax.rem(z - e + 4, 4), x, :, front]
        from_x = w_ref.at[r, z, lax.rem(x - e + 4, 4), :, rear]
        return (
            remote(from_z, from_z, w_send.at[1], w_recv.at[8 + d], moved(d, 0, r)[0]),
            remote(from_x, from_x, w_send.at[1], w_recv.at[8 + d], moved(0, d, r)[0]),
        )

    w_ref[r, z, x, :, quarter] = wo_ref[:, pl.ds(pl.multiple_of(256 * y, 256), 256)]

    def output_line(d):
        own = w_ref.at[r, z, x, :, quarter]
        return remote(own, own, o_send.at[0], o_recv.at[0], moved(0, d, r)[0])

    def output_cross(d):
        own = w_ref.at[r, :, x, :, quarter]
        return remote(own, own, o_send.at[1], o_recv.at[1], moved(d, 0, r)[0])

    def output_plane(n):
        own = w_ref.at[r, :, :, :, quarter]
        return remote(own, own, o_send.at[2], o_recv.at[2], plane_shift(n)[0])

    def output_core():
        own = w_ref.at[r, :, :, :, output]
        return remote(own, own, o_send.at[3], o_recv.at[3], sibling)

    def some(rows, width):
        return w_ref.at[0, pl.ds(0, rows), :, :, pl.ds(0, width)]

    def core_step(d):
        from_x = w_ref.at[r, :, lax.rem(x - d + 4, 4), :, front]
        from_z = w_ref.at[r, lax.rem(z - d + 4, 4), :, :, rear]
        return (
            remote(from_x, from_x, core_send.at[0], core_recv.at[0], sibling),
            remote(from_z, from_z, core_send.at[0], core_recv.at[0], sibling),
        )

    @pl.loop(1, 4)
    def _(d):
        for copy in line_step(d):
            copy.start()

    @pl.loop(1, 4)
    def _(d):
        for copy in cross_step(0, d):
            copy.start()
        output_line(d).start()

    tokens = hidden_ref.shape[0]
    experts_iota = lax.broadcasted_iota(jnp.int32, (EXPERTS, tokens), 0).astype(f32)
    live = r * tokens + lax.broadcasted_iota(jnp.int32, (1, tokens), 1) < length_ref[0]
    routed_to = jnp.zeros((EXPERTS, tokens), f32)
    ranks = jnp.zeros((EXPERTS, tokens), f32)
    prio = prio_ref[...]
    lines = jnp.concatenate([prio[:, 128 * i : 128 * i + 128] for i in range(CHIPS)], axis=0)
    token = lax.broadcasted_iota(jnp.int32, (tokens, CHIPS), 0) // CHIPS
    owner = (token == lax.broadcasted_iota(jnp.int32, (tokens, CHIPS), 1)).astype(f32)
    token = lax.rem(lax.broadcasted_iota(jnp.int32, (tokens, 128), 0), CHIPS)
    lane = lax.broadcasted_iota(jnp.int32, (tokens, 128), 1)
    place_of = lax.rem(lax.broadcasted_iota(jnp.int32, (TOP, 128), 1), TOP)
    place_of = (place_of == lax.broadcasted_iota(jnp.int32, (TOP, 128), 0)).astype(f32)
    priority = jnp.zeros((TOP, tokens), f32)
    for unit, part in ((64.0, lines // 64), (1.0, lax.rem(lines, 64))):
        part = part.astype(f32).astype(bf16)
        rows = dot(owner.astype(bf16), part, ((1,), (0,)))
        rows = jnp.where(lane // TOP == token, rows, 0.0).astype(bf16)
        priority = priority + unit * dot(place_of.astype(bf16), rows, ((1,), (1,)))
    routes = routes_ref[...].astype(f32)
    for j in range(TOP):
        match = experts_iota == routes[j : j + 1, :]
        routed_to = jnp.where(match, 1.0, routed_to)
        ranks = jnp.where(match, priority[j : j + 1, :], ranks)
    far = float(1 << 20)
    ranks = jnp.where((routed_to > 0.0) & live, ranks, far)
    ranks_t = ranks.T
    rows = []
    for e in range(EXPERTS):
        earlier = ranks_t[:, e : e + 1] < ranks[e : e + 1, :]
        rows.append(jnp.sum(earlier.astype(f32), axis=0, keepdims=True))
    slots = jnp.concatenate(rows, axis=0)
    pos = jnp.where((ranks < far) & (slots < CAP), slots, -1.0).astype(jnp.int32)
    pos_ref[...] = pos
    for core in range(2):
        for i in range(4):
            at = core * CHIPS + 4 * i
            posz_out[i, 4 * core : 4 * core + 4, :] = pos[at : at + 4, :]
            for j in range(4):
                posx_out[j, 4 * core + i : 4 * core + i + 1, :] = pos[at + j : at + j + 1, :]
    posz_ref[0] = posz_out[z]
    posx_ref[0] = posx_out[x]
    tok_z[0] = cot_ref[:, 0:HALF]
    tok_x[0] = cot_ref[:, HALF:D]

    def pos_step(d):
        to_z, to_x = lax.rem(z + d, 4), lax.rem(x + d, 4)
        return (
            remote(
                posz_out.at[to_z],
                posz_ref.at[d],
                pos_send.at[0],
                pos_recv.at[0],
                moved(0, d, r)[0],
            ),
            remote(
                posx_out.at[to_x],
                posx_ref.at[d],
                pos_send.at[1],
                pos_recv.at[1],
                moved(d, 0, r)[0],
            ),
        )

    @pl.loop(1, 4)
    def _(d):
        for copy in pos_step(d):
            copy.start()

    done(w_ref.at[0, 0, pl.ds(0, 3), :, pl.ds(0, 256)], o_recv.at[0])

    @pl.loop(1, 4)
    def _(d):
        output_cross(d).start()

    @pl.loop(1, 4)
    def _(e):
        for copy in line_step(e):
            copy.wait_recv()

        @pl.loop(1, 4)
        def _(d):
            for copy in cross_step(e, d):
                copy.start()

    @pl.loop(1, 4)
    def _(d):
        for copy in spread(d, cot_ref, tok_z, tok_x, first_send, first_recv):
            copy.start()

    for copy in core_step(0):
        copy.start()

    def cut_slots(d):
        left = dot(line_hot(posz_ref, d, 0), tok_z[d], ((1,), (0,))).astype(bf16)
        right = dot(line_hot(posx_ref, d, 1), tok_x[d], ((1,), (0,))).astype(bf16)
        sems = slot_send.at[0], slot_recv.at[0], slot_recv.at[0], 1, store_sem.at[1]
        for core in range(2):
            for i in range(4):
                part = slice((core * 4 + i) * CAP, (core * 4 + i + 1) * CAP)
                outgoing[core, d, i, :, 0:HALF] = left[part]
                send_slots(outgoing, grads_ref, core, d, i, *sems, (True, False))
                outgoing[core, i, d, :, HALF:D] = right[part]
                send_slots(outgoing, grads_ref, core, i, d, *sems, (False, True))

    cut_slots(0)

    inputs = hidden_ref[...].astype(f32)
    scale = lax.rsqrt(jnp.mean(inputs * inputs, axis=1, keepdims=True) + epsilon)
    normed_ref[...] = (inputs * scale * again_ref[...]).astype(bf16)

    done(some(3, 256), o_recv.at[1])

    for n in range(1, PLANES):
        output_plane(n).start()

    @pl.loop(1, 4)
    def _(d):
        done(some(1, 2 * D), w_recv.at[8 + d])
        for copy in core_step(d):
            copy.start()

    done(some(4, 2 * D), core_recv.at[0])

    cosine, sine = cos_ref[...], sin_ref[...]
    here = pl.ds(pl.multiple_of(r * tokens, tokens), tokens)

    def projected(first):
        weight = w_ref[:, :, :, :, first : first + HALF].reshape(D, HALF)
        return dot(normed_ref[...], weight, ((1,), (0,))).T

    def turned(rows):
        parts = []
        for h in range(rows.shape[0] // HEAD):
            first, second = rows[HEAD * h : HEAD * h + 32], rows[HEAD * h + 32 : HEAD * h + HEAD]
            parts += [first * cosine - second * sine, second * cosine + first * sine]
        return jnp.concatenate(parts, axis=0).astype(bf16)

    key_copy = remote(
        k_ref.at[:, here], k_ref.at[:, here], kv_send.at[0], kv_recv.at[0], sibling
    )
    value_copy = remote(
        v_ref.at[:, here], v_ref.at[:, here], kv_send.at[1], kv_recv.at[1], sibling
    )
    for p in range(2):
        both = projected(D * p + HALF)
        k_ref[256 * p : 256 * p + 256, here] = turned(both[0:256])
        v_ref[256 * p : 256 * p + 256, here] = both[256:512].astype(bf16)
    key_copy.start()
    value_copy.start()
    for p in range(2):
        q_ref[HALF * p : HALF * p + HALF, :] = turned(projected(D * p))

    spread_done(tok_z, tok_x, first_recv)
    done(posz_ref.at[pl.ds(1, 3)], pos_recv.at[0])
    done(posx_ref.at[pl.ds(1, 3)], pos_recv.at[1])
    pl.loop(1, 4)(cut_slots)

    key_copy.wait_recv()
    value_copy.wait_recv()

    done(some(4, 768), o_recv.at[2])
    output_core().start()

    key_live = lax.broadcasted_iota(jnp.int32, (2 * tokens, 1), 0) < length_ref[0]
    score_scale = HEAD ** (-0.5)

    @pl.loop(0, KV_HEADS)
    def _(g):
        head = pl.ds(pl.multiple_of(g * HEAD, HEAD), HEAD)
        keys, values = k_ref[head, :], v_ref[head, :]
        for j in range(2):
            at = pl.ds(pl.multiple_of((2 * g + j) * HEAD, HEAD), HEAD)
            scores = dot(keys, q_ref[at, :], ((0,), (0,))) * score_scale
            scores = jnp.where(key_live, scores, NEG)
            top = jnp.max(scores, axis=0, keepdims=True)
            weights = jnp.exp(scores - top)
            total = jnp.sum(weights, axis=0, keepdims=True)
            lse_ref[pl.ds(2 * g + j, 1), :] = top + jnp.log(total)
            probs = (weights * (1.0 / total)).astype(bf16)
            mixed_t[at, :] = dot(values, probs, ((1,), (0,))).astype(bf16)

    mixed_ref[...] = mixed_t[...].T
    output_core().wait_recv()
    weights_out = pltpu.make_async_copy(w_ref, w_hbm, store_sem.at[0])
    weights_out.start()
    w_out = w_ref[:, :, :, :, 2 * D : 3 * D].reshape(D, D)
    middle = hidden_ref[...].astype(f32) + dot(mixed_ref[...], w_out, ((1,), (0,)))
    middle_ref[...] = middle
    scale = lax.rsqrt(jnp.mean(middle * middle, axis=1, keepdims=True) + epsilon)
    routed_ref[...] = (middle * scale * mgain_ref[...]).astype(bf16)
    logits = dot(router_ref[...], routed_ref[...], ((1,), (1,)))
    logits = jnp.where(routed_to > 0.0, logits, -jnp.inf)
    picked = jnp.exp(logits - jnp.max(logits, axis=0, keepdims=True))
    gates_ref[...] = picked / jnp.sum(picked, axis=0, keepdims=True)

    done(all_slots(grads_ref), slot_recv.at[0])
    done(grads_ref.at[0, 0], store_sem.at[1])
    done(all_slots(outgoing), slot_send.at[0])
    done(w_ref.at[0, 0, pl.ds(0, 3), :, pl.ds(0, 2 * D)], w_send.at[0])
    done(some(3, 2 * D), w_send.at[1])
    done(some(4, 2 * D), core_send.at[0])
    done(w_ref.at[0, 0, pl.ds(0, 3), :, pl.ds(0, 256)], o_send.at[0])
    done(some(3, 256), o_send.at[1])
    done(some(4, 768), o_send.at[2])
    output_core().wait_send()
    spread_done(tok_z, tok_x, first_send)
    done(posz_ref.at[pl.ds(1, 3)], pos_send.at[0])
    done(posx_ref.at[pl.ds(1, 3)], pos_send.at[1])
    weights_out.wait()
    key_copy.wait_send()
    value_copy.wait_send()


def front(length, *arrays):
    f32, bf16, i32 = jnp.float32, jnp.bfloat16, jnp.int32
    vmem = pl.BlockSpec(memory_space=pltpu.VMEM)
    hbm = pl.BlockSpec(memory_space=pl.ANY)
    shape = jax.ShapeDtypeStruct
    out_shape = (
        shape((2, 4, 4, 32, 3 * D), bf16),
        shape((TOKENS, D), bf16),
        shape((D, TOKENS), bf16),
        shape((HALF, 2 * TOKENS), bf16),
        shape((HALF, 2 * TOKENS), bf16),
        shape((HEADS, TOKENS), f32),
        shape((TOKENS, D), bf16),
        shape((TOKENS, D), f32),
        shape((TOKENS, D), bf16),
        shape((EXPERTS, TOKENS), f32),
        shape((EXPERTS, TOKENS), i32),
        shape((4, 8, TOKENS), i32),
        shape((4, 8, TOKENS), i32),
        shape((2, 4, 4, CAP, D), bf16),
    )
    scratch = [
        pltpu.VMEM((2, 4, 4, 32, 3 * D), bf16),
        pltpu.VMEM((D, TOKENS), bf16),
        pltpu.VMEM((4, 8, TOKENS), i32),
        pltpu.VMEM((4, 8, TOKENS), i32),
        pltpu.VMEM((4, TOKENS, HALF), bf16),
        pltpu.VMEM((4, TOKENS, HALF), bf16),
        pltpu.VMEM((2, 4, 4, CAP, D), bf16),
    ]
    scratch += [pltpu.SemaphoreType.DMA((2,))]
    for count in (12, 4, 1, 2, 2, 1, 2):
        scratch += [pltpu.SemaphoreType.DMA((count,))] * 2
    return pl.pallas_call(
        front_kernel,
        out_shape=out_shape,
        in_specs=[pl.BlockSpec(memory_space=pltpu.SMEM)] + [vmem] * len(arrays),
        out_specs=[hbm] + [vmem] * (len(out_shape) - 2) + [hbm],
        scratch_shapes=scratch,
        compiler_params=pltpu.CompilerParams(
            collective_id=3, has_side_effects=True, vmem_limit_bytes=60 << 20
        ),
        name="front",
    )(length, *arrays)


def turned_back(rows, cosine, sine):
    first, second = rows[0:32], rows[32:64]
    return jnp.concatenate(
        [first * cosine + second * sine, second * cosine - first * sine], axis=0
    )


def rest_kernel(
    length_ref,
    routed_ref,
    pos_ref,
    posz_ref,
    posx_ref,
    gates_ref,
    grads_hbm,
    wg_hbm,
    wu_hbm,
    wd_hbm,
    router_ref,
    middle_ref,
    cot_ref,
    hidden_hbm,
    again_ref,
    mgain_ref,
    normed_hbm,
    mixed_hbm,
    w_hbm,
    q_hbm,
    k_hbm,
    v_hbm,
    lse_ref,
    cos_ref,
    sin_ref,
    hout_ref,
    hgrad_ref,
    again_out,
    mgain_out,
    router_out,
    own_out,
    esum_hbm,
    prod_hbm,
    mid_hbm,
    tok_z,
    tok_x,
    arrived,
    mid,
    parts_in,
    parts_in2,
    gate_out,
    gate_in,
    dot_out,
    dot_in,
    gdot_ref,
    expert_ref,
    relay_in,
    y_in,
    branch_sib,
    normed_sib,
    mixed_sib,
    grad_sib,
    kv_in,
    rs_in,
    rs_in2,
    y_parts,
    small_in,
    small_y_in,
    gain_in,
    gain_y_in,
    router_all,
    load_sem,
    store_sem,
    first_send,
    first_recv,
    slot_send,
    slot_recv,
    back_send,
    back_recv,
    part_send,
    part_recv,
    small_send,
    small_recv,
    c_send,
    c_recv,
    part_send2,
    part_recv2,
    ex_send,
    ex_recv,
    sib_send,
    sib_recv,
    rs_send,
    rs_recv,
    rs_send2,
    rs_recv2,
    ys_send,
    ys_recv,
    sm_send,
    sm_recv,
):
    y, r, x, z = place()
    me = r * CHIPS + z * 4 + x
    sibling = moved(0, 0, 1 - r)[0]
    tokens = TOKENS
    f32, bf16 = jnp.float32, jnp.bfloat16

    above, below = plane_shift(1), plane_shift(3)
    opposite = plane_shift(2)[1]
    def relayed(n):
        device = (above, below)[n][0]
        return remote(
            expert_ref.at[0, n], relay_in.at[n], ex_send.at[n], ex_recv.at[n], device
        )

    def direct(n):
        device = (above, below)[n][0]
        return remote(
            expert_ref.at[1 + n, 1 - n],
            y_in.at[n, 1 - n],
            ex_send.at[2 + n],
            ex_recv.at[2 + n],
            device,
        )

    def passed_on(n):
        device, came_from = (above, below)[n][0], (below, above)[n][1]
        part = esum_hbm.at[came_from, n]
        return remote(part, part, ex_send.at[8 + n], ex_recv.at[8 + n], device)

    def to_sibling(at, src, dst):
        return remote(src, dst, sib_send.at[at], sib_recv.at[at], sibling)

    half = pl.ds(pl.multiple_of((1 - r) * HALF, HALF), HALF)
    sib_normed = to_sibling(0, normed_hbm.at[:, half], normed_sib)
    sib_mixed = to_sibling(1, mixed_hbm.at[:, half], mixed_sib)

    meet(True, True)
    sib_mixed.start()
    sib_normed.start()

    def expert_phase(grads_ref, wg_ref, wu_ref, wd_ref, outgoing, parts_out, active, weighted, pre_grads):
        loads = [
            pltpu.make_async_copy(source, target, load_sem.at[n])
            for n, (source, target) in enumerate(
                (
                    (wg_hbm, wg_ref),
                    (wu_hbm, wu_ref),
                    (wd_hbm, wd_ref),
                    (grads_hbm, grads_ref),
                )
            )
        ]
        for load in loads:
            load.start()
        @pl.loop(1, 4)
        def _(d):
            for copy in spread(d, routed_ref, tok_z, tok_x, first_send, first_recv):
                copy.start()

        tok_z[0] = routed_ref[:, 0:HALF]
        tok_x[0] = routed_ref[:, HALF:D]

        def send_rows(core, dz, dx, g, halves):
            came = slot_recv.at[2 * g + r]
            sems = slot_send.at[g], came, came, 1, None
            send_slots(outgoing, arrived, core, dz, dx, *sems, halves)

        left = dot(line_hot(posz_ref, 0, 0), tok_z[0], ((1,), (0,))).astype(bf16)
        right = dot(line_hot(posx_ref, 0, 1), tok_x[0], ((1,), (0,))).astype(bf16)
        for core in range(2):
            for i in range(4):
                part = slice((core * 4 + i) * CAP, (core * 4 + i + 1) * CAP)
                outgoing[core, 0, i, :, 0:HALF] = left[part]
                send_rows(core, 0, i, (4 - i) % 4, (True, False))
                outgoing[core, i, 0, :, HALF:D] = right[part]
                send_rows(core, i, 0, i, (False, True))

        def small(k, out, into, sign, base):
            there, dz, dx = k // CHIPS, lax.rem(k // 4, 4), lax.rem(k, 4)
            slot = r * CHIPS + lax.rem(k, CHIPS)
            return remote(
                out.at[k],
                into.at[slot],
                small_send.at[base],
                small_recv.at[base],
                moved(sign * dx, sign * dz, there)[0],
            )

        def own_slot(k):
            return k == r * CHIPS

        @pl.loop(0, GROUP)
        def _(k):
            there, dz, dx = k // CHIPS, lax.rem(k // 4, 4), lax.rem(k, 4)
            _, expert = moved(dx, dz, there)
            chosen = picks(pos_ref[pl.ds(expert, 1), :])
            gate_col = jnp.sum(
                jnp.where(chosen, gates_ref[pl.ds(expert, 1), :], 0.0), axis=1, keepdims=True
            )
            gate_out[k, 0:1, 0:CAP] = as_row(gate_col)

            @pl.when(own_slot(k))
            def _():
                gate_in[k] = gate_out[k]

            @pl.when(jnp.logical_not(own_slot(k)))
            def _():
                small(k, gate_out, gate_in, 1, 0).start()

        spread_done(tok_z, tok_x, first_recv)

        @pl.loop(0, 4)
        def _(g):
            for dx in range(4):
                dz = lax.rem(dx + g, 4)

                @pl.when(dz != 0)
                def _():
                    rows = [
                        picks(posz_ref[dz, pl.ds(core * 4 + lax.rem(x + dx, 4), 1), :])
                        for core in range(2)
                    ]
                    rows = dot(as_hot(jnp.concatenate(rows, axis=0)), tok_z[dz], ((1,), (0,)))
                    for core in range(2):
                        part = slice(core * CAP, core * CAP + CAP)
                        outgoing[core, dz, dx, :, 0:HALF] = rows[part].astype(bf16)
                        send_rows(core, dz, dx, g, (True, False))

                if dx == 0:
                    continue
                rows = [
                    picks(posx_ref[dx, pl.ds(core * 4 + lax.rem(z + dz, 4), 1), :])
                    for core in range(2)
                ]
                rows = dot(as_hot(jnp.concatenate(rows, axis=0)), tok_x[dx], ((1,), (0,)))
                for core in range(2):
                    part = slice(core * CAP, core * CAP + CAP)
                    outgoing[core, dz, dx, :, HALF:D] = rows[part].astype(bf16)
                    send_rows(core, dz, dx, g, (False, True))

        def keep_produced(k):
            core, dz, dx = k // CHIPS, lax.rem(k // 4, 4), lax.rem(k, 4)
            return pltpu.make_async_copy(
                grads_ref.at[core, dz, dx],
                prod_hbm.at[core, dz, dx],
                store_sem.at[lax.rem(dz - dx + 4, 4)],
            )

        for load in loads:
            load.wait()
        done(gate_in.at[pl.ds(0, GROUP - 1)], small_recv.at[0])

        @pl.loop(0, 8)
        def _(c):
            g, core = c // 2, lax.rem(c, 2)

            @pl.when(core == r)
            def _():
                done(arrived.at[0, 0, pl.ds(0, 3)], slot_recv.at[c])

            @pl.when(core != r)
            def _():
                done(arrived.at[0, 0], slot_recv.at[c])

            @pl.when(core == 0)
            def _():
                done(outgoing.at[0, pl.ds(0, 2), :, :, pl.ds(0, 896)], slot_send.at[g])

            rows, gate_cols, grads = [], [], []
            for dx in range(4):
                dz = lax.rem(dx + g, 4)
                k = core * CHIPS + dz * 4 + dx
                rows.append(arrived[core, dz, dx])
                gate_cols.append(as_column(gate_in[k, 0:1, 0:CAP]))
                grads.append(grads_ref[core, dz, dx])
            rows = jnp.concatenate(rows, axis=0)
            gate_cols = jnp.concatenate(gate_cols, axis=0)
            grads = jnp.concatenate(grads, axis=0).astype(f32)
            gate_pre = dot(rows, wg_ref[...], ((1,), (0,)))
            up_pre = dot(rows, wu_ref[...], ((1,), (0,)))
            gate_sig = jax.nn.sigmoid(gate_pre)
            gate_act = gate_pre * gate_sig
            act = (gate_act * up_pre).astype(bf16)
            produced = dot(act, wd_ref[...], ((1,), (0,))).astype(bf16).astype(f32)
            dots = jnp.sum(produced * grads, axis=1, keepdims=True)
            produced_grad = (gate_cols * grads).astype(bf16)
            act_grad = dot(produced_grad, wd_ref[...], ((1,), (1,))).astype(bf16).astype(f32)
            gate_grad = (
                act_grad * up_pre * gate_sig * (1.0 + gate_pre * (1.0 - gate_sig))
            ).astype(bf16)
            up_grad = (act_grad * gate_act).astype(bf16)
            row_grads = dot(gate_grad, wg_ref[...], ((1,), (1,)))
            row_grads = (row_grads + dot(up_grad, wu_ref[...], ((1,), (1,)))).astype(bf16)
            produced = (produced * gate_cols).astype(bf16)
            for dx in range(4):
                dz = lax.rem(dx + g, 4)
                k = core * CHIPS + dz * 4 + dx
                part = slice(dx * CAP, dx * CAP + CAP)
                outgoing[core, dz, dx] = row_grads[part]
                send_slots(
                    outgoing,
                    mid,
                    core,
                    dz,
                    dx,
                    back_send.at[0],
                    back_recv.at[dz],
                    back_recv.at[4 + dx],
                    -1,
                )
                dot_out[k, 0:1, 0:CAP] = as_row(dots[part])

                @pl.when(own_slot(k))
                def _():
                    dot_in[k] = dot_out[k]

                @pl.when(jnp.logical_not(own_slot(k)))
                def _():
                    small(k, dot_out, dot_in, -1, 1).start()

                grads_ref[core, dz, dx] = produced[part]
                keep_produced(k).start()
                active[core, dz, dx] = act[part]
                weighted[core, dz, dx] = produced_grad[part]
                pre_grads[core, dz, dx, :, 0:HALF] = gate_grad[part]
                pre_grads[core, dz, dx, :, HALF:D] = up_grad[part]

        def send_results(g):
            done(prod_hbm.at[0, pl.ds(0, 2)], store_sem.at[g])
            for dx in range(4):
                dz = lax.rem(dx + g, 4)
                for core in range(2):
                    send_slots(
                        prod_hbm,
                        mid_hbm,
                        core,
                        dz,
                        dx,
                        c_send.at[0],
                        c_recv.at[0],
                        c_recv.at[0],
                        -1,
                        load_sem.at[8],
                    )

        send_results(0)

        all_rows = GROUP * CAP

        def quarter_grads(slot, n):
            span = pl.ds(pl.multiple_of(n * 256, 256), 256)
            left = arrived[:, :, :, :, span].reshape(all_rows, 256)
            part = dot(left, pre_grads[...].reshape(all_rows, D), ((0,), (0,))).astype(bf16)
            narrow = pl.ds(pl.multiple_of(n * 128, 128), 128)
            left = active[:, :, :, :, narrow].reshape(all_rows, 128)
            down = dot(left, weighted[...].reshape(all_rows, D), ((0,), (0,))).astype(bf16)
            for h in range(2):
                rows = part[128 * h : 128 * h + 128]
                expert_ref[slot, h, 0:128, :] = rows[:, 0:HALF]
                expert_ref[slot, h, 128:256, :] = rows[:, HALF:D]
                rows = down[64 * h : 64 * h + 64]
                expert_ref[slot, h, 256:320, :] = rows[:, 0:HALF]
                expert_ref[slot, h, 320:384, :] = rows[:, HALF:D]

        quarter_grads(0, opposite)
        for n in range(2):
            relayed(n).start()

        sends = part_send.at[0], part_recv.at[0]
        fold_left(parts_out, parts_in, mid, back_recv, posz_ref, *sends)
        fold_right(parts_out, parts_in, mid, back_recv, posx_ref, *sends)
        pl.loop(1, 4)(send_results)

        @pl.loop(1, 4)
        def _(slot):
            quarter_grads(slot, lax.rem(y + jnp.where(slot == 1, 1, jnp.where(slot == 2, 3, 0)), 4))

        for n in range(2):
            direct(n).start()

        done(dot_in.at[pl.ds(0, GROUP - 1)], small_recv.at[1])

        @pl.loop(0, GROUP)
        def _(k):
            there, dz, dx = k // CHIPS, lax.rem(k // 4, 4), lax.rem(k, 4)
            _, expert = moved(dx, dz, there)
            at = pl.ds(expert, 1)
            dots = as_column(dot_in[k, 0:1, 0:CAP])
            gdot_ref[at, :] = jnp.sum(
                jnp.where(picks(pos_ref[at, :]), dots, 0.0), axis=0, keepdims=True
            )

        done(parts_in.at[pl.ds(1, 3)], part_recv.at[0])
        hgrad_ref[...] = (parts_in[0].astype(f32) + parts_in[1].astype(f32)) + (
            parts_in[2].astype(f32) + parts_in[3].astype(f32)
        )
        done(all_slots(outgoing), back_send.at[0])
        done(parts_out.at[pl.ds(1, 3)], part_send.at[0])
        spread_done(tok_z, tok_x, first_send)
        done(gate_in.at[pl.ds(0, GROUP - 1)], small_send.at[0])
        done(dot_in.at[pl.ds(0, GROUP - 1)], small_send.at[1])

    pl.run_scoped(
        expert_phase,
        pltpu.VMEM((2, 4, 4, CAP, D), bf16),
        pltpu.VMEM((D, HALF), bf16),
        pltpu.VMEM((D, HALF), bf16),
        pltpu.VMEM((HALF, D), bf16),
        pltpu.VMEM((2, 4, 4, CAP, D), bf16),
        pltpu.VMEM((4, tokens, D), bf16),
        pltpu.VMEM((2, 4, 4, CAP, HALF), bf16),
        pltpu.VMEM((2, 4, 4, CAP, D), bf16),
        pltpu.VMEM((2, 4, 4, CAP, D), bf16),
    )

    def finish_phase(w_ref, q_ref, k_ref, v_ref, normed_ref, mixed_ref, hidden_ref, parts_out2, quarter_sum, relay_out, branch_own, mg_t, grad_t, kv_own, kv_out, weight_part, rs_out, y_out, small_out, small_y, gain_out, gain_y):
        loads = [
            pltpu.make_async_copy(source, target, load_sem.at[n])
            for n, (source, target) in enumerate(
                (
                    (w_hbm, w_ref),
                    (mixed_hbm, mixed_ref),
                    (q_hbm, q_ref),
                    (k_hbm, k_ref),
                    (v_hbm, v_ref),
                    (normed_hbm, normed_ref),
                    (hidden_hbm, hidden_ref),
                )
            )
        ]
        for load in loads:
            load.start()

        def weight(first, width):
            return w_ref[:, :, :, :, first : first + width].reshape(D, width)

        def merged(n):
            device = (above, below)[n][0]
            return remote(
                relay_out.at[n], y_in.at[n, n], ex_send.at[4 + n], ex_recv.at[4 + n], device
            )

        def handed(n):
            device = (above, below)[n][0]
            return remote(
                quarter_sum, esum_hbm.at[y], ex_send.at[6 + n], ex_recv.at[6 + n], device
            )

        def sib_keyval(p):
            return to_sibling(3 + p, kv_out.at[p], kv_in.at[p])

        def sib_grads(p, part):
            rows = pl.ds(p * D + part * HALF, HALF)
            return to_sibling(5 + 2 * p + part, grad_t.at[rows], grad_sib.at[rows])

        sib_branch = to_sibling(2, branch_own, branch_sib)

        for n in range(2):
            relayed(n).wait_recv()
            total = relay_in[n].astype(f32) + expert_ref[1 + n, n].astype(f32)
            relay_out[n] = total.astype(bf16)
            merged(n).start()

        gates = gates_ref[...]
        gdot = gdot_ref[...]
        logit_grad = gates * (gdot - jnp.sum(gates * gdot, axis=0, keepdims=True))
        high, rest = split_two(logit_grad)
        router_part = dot(high, routed_ref[...], ((1,), (0,)))
        router_part = router_part + dot(rest, routed_ref[...], ((1,), (0,)))
        routed_grad = dot(high, router_ref[...], ((0,), (0,)))
        routed_grad = routed_grad + dot(rest, router_ref[...], ((0,), (0,)))
        routed_grad = routed_grad + hgrad_ref[...]
        live = (
            r * tokens + lax.broadcasted_iota(jnp.int32, (tokens, 1), 0) < length_ref[0]
        ).astype(f32)
        middle = middle_ref[...]
        scale = lax.rsqrt(jnp.mean(middle * middle, axis=1, keepdims=True) + epsilon)
        rows = middle * scale
        moe_part = jnp.sum(routed_grad * rows, axis=0, keepdims=True)
        scaled = routed_grad * mgain_ref[...]
        inner = jnp.mean(scaled * rows, axis=1, keepdims=True)
        middle_grad = cot_ref[...].astype(f32) * live + scale * (scaled - rows * inner)
        hgrad_ref[...] = middle_grad
        branch_own[...] = middle_grad.astype(bf16)
        sib_branch.start()
        for j in range(8):
            part = slice(128 * j, 128 * j + 128)
            small_out[:, j, :] = router_part[:, part]
            small_out[:, 8 + j, :] = jnp.broadcast_to(moe_part[:, part], (GROUP, 128))

        def tiny(k):
            device, other = step_of(k, 1)
            return remote(small_out.at[other], small_in.at[me], sm_send.at[0], sm_recv.at[0], device)

        @pl.loop(1, GROUP)
        def _(k):
            tiny(k).start()

        small_in[me] = small_out[me]

        loads[0].wait()
        mg_t[...] = dot(weight(2 * D, D), branch_own[...], ((1,), (1,))).astype(bf16)

        mine = pl.ds(pl.multiple_of(r * HALF, HALF), HALF)

        def columns(p):
            return pl.ds(p * D, HALF), pl.ds(p * D + HALF, HALF)

        def first_step(p, d):
            left, right = columns(p)
            return (
                remote(
                    weight_part.at[lax.rem(z + d, 4), :, :, left],
                    rs_in.at[d, :, :, left],
                    rs_send.at[p],
                    rs_recv.at[p],
                    moved(0, d, r)[0],
                ),
                remote(
                    weight_part.at[:, lax.rem(x + d, 4), :, right],
                    rs_in.at[d, :, :, right],
                    rs_send.at[p],
                    rs_recv.at[p],
                    moved(d, 0, r)[0],
                ),
            )

        def second_step(p, d):
            left, right = columns(p)
            return (
                remote(
                    rs_out.at[lax.rem(x + d, 4), :, left],
                    rs_in2.at[d, :, left],
                    rs_send2.at[p],
                    rs_recv2.at[p],
                    moved(d, 0, r)[0],
                ),
                remote(
                    rs_out.at[lax.rem(z + d, 4), :, right],
                    rs_in2.at[d, :, right],
                    rs_send2.at[p],
                    rs_recv2.at[p],
                    moved(0, d, r)[0],
                ),
            )

        def across(p, n):
            cols = pl.ds(p * D, D)
            return remote(
                y_out.at[:, cols],
                y_parts.at[y, :, cols],
                ys_send.at[p],
                ys_recv.at[p],
                plane_shift(n)[0],
            )

        def sum_first(p, total):
            weight_part[:, :, :, p * D : p * D + D] = total.astype(bf16).reshape(4, 4, 32, D)

            @pl.loop(1, 4)
            def _(d):
                for copy in first_step(p, d):
                    copy.start()

        def sum_second(p):
            left, right = columns(p)

            done(rs_in.at[pl.ds(1, 3), :, :, pl.ds(p * D, D)], rs_recv.at[p])

            total = weight_part[z, :, :, left].astype(f32)
            other = weight_part[:, x, :, right].astype(f32)
            for d in range(1, 4):
                total = total + rs_in[d, :, :, left].astype(f32)
                other = other + rs_in[d, :, :, right].astype(f32)
            rs_out[:, :, left] = total.astype(bf16)
            rs_out[:, :, right] = other.astype(bf16)

            @pl.loop(1, 4)
            def _(d):
                for copy in second_step(p, d):
                    copy.start()

        def sum_third(p):
            left, right = columns(p)

            done(rs_in2.at[pl.ds(1, 3), :, pl.ds(p * D, D)], rs_recv2.at[p])

            total = rs_out[x, :, left].astype(f32)
            other = rs_out[z, :, right].astype(f32)
            for d in range(1, 4):
                total = total + rs_in2[d, :, left].astype(f32)
                other = other + rs_in2[d, :, right].astype(f32)
            y_out[:, left] = total.astype(bf16)
            y_out[:, right] = other.astype(bf16)
            y_parts[y, :, left] = total.astype(bf16)
            y_parts[y, :, right] = other.astype(bf16)
            for n in range(1, PLANES):
                across(p, n).start()

        sib_mixed.wait_recv()
        sib_branch.wait_recv()
        loads[1].wait()
        total = dot(mixed_ref[:, mine], branch_own[...], ((0,), (0,)))
        sum_first(2, total + dot(mixed_sib[...], branch_sib[...], ((0,), (0,))))

        key_live = lax.broadcasted_iota(jnp.int32, (2 * tokens, 1), 0) < length_ref[0]
        score_scale = HEAD ** (-0.5)
        cosine, sine = cos_ref[...], sin_ref[...]
        first_core = r == 0

        def key_head(p, i):
            g = 4 * p + i
            head = pl.ds(pl.multiple_of(g * HEAD, HEAD), HEAD)
            keys, values = k_ref[head, :], v_ref[head, :]
            key_sum, value_sum = None, None
            for j in range(2):
                at = pl.ds(pl.multiple_of((2 * g + j) * HEAD, HEAD), HEAD)
                query, mixed_grad = q_ref[at, :], mg_t[at, :]
                scores = dot(keys, query, ((0,), (0,))) * score_scale
                scores = jnp.where(key_live, scores, NEG)
                probs = jnp.exp(scores - lse_ref[pl.ds(2 * g + j, 1), :])
                prob_grad = dot(values, mixed_grad, ((0,), (0,)))
                value_part = dot(mixed_grad, probs.astype(bf16), ((1,), (1,)))
                inner = jnp.sum(probs * prob_grad, axis=0, keepdims=True)
                score_grad = (probs * (prob_grad - inner)).astype(bf16)
                key_part = dot(query, score_grad, ((1,), (1,)))
                query_grad = dot(keys, score_grad, ((1,), (0,))) * score_scale
                to = pl.ds(pl.multiple_of(p * D + (2 * i + j) * HEAD, HEAD), HEAD)
                grad_t[to, :] = turned_back(query_grad, cosine, sine).astype(bf16)
                key_sum = key_part if key_sum is None else key_sum + key_part
                value_sum = value_part if value_sum is None else value_sum + value_part
            key_sum = key_sum * score_scale
            for n, part in enumerate((key_sum, value_sum)):
                to = pl.ds(pl.multiple_of(256 * n + i * HEAD, HEAD), HEAD)
                kv_own[p, to, :] = jnp.where(first_core, part[:, :tokens], part[:, tokens:])
                away = jnp.where(first_core, part[:, tokens:], part[:, :tokens])
                kv_out[p, to, :] = away.astype(bf16)

        def heads(p, first, last):
            @pl.loop(first, last)
            def _(i):
                key_head(p, i)

        def whole_keyval(p):
            sib_keyval(p).wait_recv()
            for i in range(4):
                rows = slice(HEAD * i, HEAD * i + HEAD)
                total = kv_own[p, rows, :] + kv_in[p, rows, :].astype(f32)
                to = p * D + HALF + HEAD * i
                grad_t[to : to + HEAD, :] = turned_back(total, cosine, sine).astype(bf16)
            total = kv_own[p, 256:512, :] + kv_in[p, 256:512, :].astype(f32)
            grad_t[p * D + HALF + 256 : p * D + D, :] = total.astype(bf16)
            sib_grads(p, 1).start()

        def projections(p):
            rows = slice(p * D, p * D + D)
            for part in range(2):
                sib_grads(p, part).wait_recv()
            total = dot(normed_ref[:, mine], grad_t[rows, :], ((0,), (1,)))
            sum_first(p, total + dot(normed_sib[...], grad_sib[rows, :], ((0,), (1,))))

        def inputs_part(p):
            return dot(grad_t[p * D : p * D + D, :], weight(p * D, D), ((0,), (1,)))

        for load in loads[2:5]:
            load.wait()
        heads(0, 0, 4)
        sib_keyval(0).start()
        sib_grads(0, 0).start()

        heads(1, 0, 4)
        sib_keyval(1).start()
        sib_grads(1, 0).start()
        for n in range(2):
            direct(n).wait_recv()
            merged(n).wait_recv()
        for n in range(2):
            total = expert_ref[3, n].astype(f32) + (y_in[0, n].astype(f32) + y_in[1, n].astype(f32))
            quarter_sum[n] = total.astype(bf16)
        quarter_out = pltpu.make_async_copy(quarter_sum, esum_hbm.at[y], load_sem.at[9])
        quarter_out.start()
        for n in range(2):
            handed(n).start()

        whole_keyval(0)
        for load in loads[5:]:
            load.wait()
        sib_normed.wait_recv()
        projections(0)
        done(all_slots(mid_hbm), c_recv.at[0])
        done(mid_hbm.at[0, 0], load_sem.at[8])
        results_in = pltpu.make_async_copy(mid_hbm, mid, load_sem.at[10])
        results_in.start()
        whole_keyval(1)
        normed_grad = inputs_part(0)
        projections(1)
        normed_grad = normed_grad + inputs_part(1)

        inputs = hidden_ref[...].astype(f32)
        scale = lax.rsqrt(jnp.mean(inputs * inputs, axis=1, keepdims=True) + epsilon)
        rows = inputs * scale
        attn_part = jnp.sum(normed_grad * rows, axis=0, keepdims=True)
        for j in range(8):
            gain_out[j : j + 1, :] = attn_part[:, 128 * j : 128 * j + 128]

        def gain(k):
            device, _ = step_of(k, 1)
            return remote(gain_out, gain_in.at[me], sm_send.at[3], sm_recv.at[3], device)

        @pl.loop(1, GROUP)
        def _(k):
            gain(k).start()

        gain_in[me] = gain_out[...]
        scaled = normed_grad * again_ref[...]
        inner = jnp.mean(scaled * rows, axis=1, keepdims=True)
        hgrad_ref[...] += scale * (scaled - rows * inner)

        sum_second(2)
        done(small_in.at[pl.ds(0, GROUP - 1)], sm_recv.at[0])

        def small_across(n):
            device, _ = plane_shift(n)
            return remote(
                small_y, small_y_in.at[y], sm_send.at[1], sm_recv.at[1], device
            )

        small_y[...] = jnp.sum(small_in[...], axis=0)
        small_y_in[y] = small_y[...]
        for n in range(1, PLANES):
            small_across(n).start()

        sum_second(0)
        results_in.wait()
        sends = part_send2.at[0], part_recv2.at[0]
        fold_left(parts_out2, parts_in2, mid, None, posz_ref, *sends)
        for n in range(2):
            handed(n).wait_recv()
            passed_on(n).start()

        done(small_y_in.at[pl.ds(0, 3)], sm_recv.at[1])
        totals = small_y_in[0] + small_y_in[1] + small_y_in[2] + small_y_in[3]
        mgain_out[...] = totals[8:16]
        router_all[me] = totals[0:8]

        def router_row(k):
            device, _ = step_of(k, 1)
            return remote(
                router_all.at[me], router_all.at[me], sm_send.at[2], sm_recv.at[2], device
            )

        @pl.loop(1, GROUP)
        def _(k):
            router_row(k).start()

        sum_second(1)
        fold_right(parts_out2, parts_in2, mid, None, posx_ref, *sends)
        sum_third(2)
        sum_third(0)

        done(gain_in.at[pl.ds(0, GROUP - 1)], sm_recv.at[3])

        gain_y[...] = jnp.sum(gain_in[...], axis=0)
        gain_y_in[y] = gain_y[...]

        def gain_across(n):
            device, _ = plane_shift(n)
            return remote(gain_y, gain_y_in.at[y], sm_send.at[4], sm_recv.at[4], device)

        for n in range(1, PLANES):
            gain_across(n).start()

        sum_third(1)

        done(parts_in2.at[pl.ds(1, 3)], part_recv2.at[0])
        mixture = (parts_in2[0].astype(f32) + parts_in2[1].astype(f32)) + (
            parts_in2[2].astype(f32) + parts_in2[3].astype(f32)
        )
        hout_ref[...] = ((middle_ref[...] + mixture) * live).astype(bf16)

        done(gain_y_in.at[pl.ds(0, 3)], sm_recv.at[4])
        again_out[...] = (gain_y_in[0] + gain_y_in[1]) + (gain_y_in[2] + gain_y_in[3])

        done(router_all.at[pl.ds(0, GROUP - 1)], sm_recv.at[2])

        router_out[...] = router_all[...]

        done(all_slots(mid_hbm), c_send.at[0])
        done(parts_out2.at[pl.ds(1, 3)], part_send2.at[0])
        done(small_in.at[pl.ds(0, GROUP - 1)], sm_send.at[0])
        done(small_y_in.at[pl.ds(0, 3)], sm_send.at[1])
        done(router_all.at[pl.ds(0, GROUP - 1)], sm_send.at[2])
        done(gain_in.at[pl.ds(0, GROUP - 1)], sm_send.at[3])
        done(gain_y_in.at[pl.ds(0, 3)], sm_send.at[4])
        for p in range(3):
            done(rs_in.at[pl.ds(1, 3), :, :, pl.ds(p * D, D)], rs_send.at[p])
            done(rs_in2.at[pl.ds(1, 3), :, pl.ds(p * D, D)], rs_send2.at[p])
            done(y_parts.at[pl.ds(0, 3), :, pl.ds(p * D, D)], ys_recv.at[p])
            done(y_parts.at[pl.ds(0, 3), :, pl.ds(p * D, D)], ys_send.at[p])
        for n in range(2):
            for copy in (relayed(n), direct(n), merged(n), handed(n), passed_on(n)):
                copy.wait_send()
        for copy in (sib_normed, sib_mixed, sib_branch):
            copy.wait_send()
        for p in range(2):
            sib_keyval(p).wait_send()
            for part in range(2):
                sib_grads(p, part).wait_send()
        for n in range(2):
            passed_on(n).wait_recv()
        quarter_out.wait()
        own_out[...] = (y_parts[0].astype(f32) + y_parts[1].astype(f32)) + (
            y_parts[2].astype(f32) + y_parts[3].astype(f32)
        )

    pl.run_scoped(
        finish_phase,
        pltpu.VMEM((2, 4, 4, 32, 3 * D), bf16),
        pltpu.VMEM((D, tokens), bf16),
        pltpu.VMEM((HALF, 2 * tokens), bf16),
        pltpu.VMEM((HALF, 2 * tokens), bf16),
        pltpu.VMEM((tokens, D), bf16),
        pltpu.VMEM((tokens, D), bf16),
        pltpu.VMEM((tokens, D), bf16),
        pltpu.VMEM((4, tokens, D), bf16),
        pltpu.VMEM((2, 384, HALF), bf16),
        pltpu.VMEM((2, 384, HALF), bf16),
        pltpu.VMEM((tokens, D), bf16),
        pltpu.VMEM((D, tokens), bf16),
        pltpu.VMEM((2 * D, tokens), bf16),
        pltpu.VMEM((2, HALF, tokens), f32),
        pltpu.VMEM((2, HALF, tokens), bf16),
        pltpu.VMEM((4, 4, 32, 3 * D), bf16),
        pltpu.VMEM((4, 32, 3 * D), bf16),
        pltpu.VMEM((32, 3 * D), bf16),
        pltpu.VMEM((GROUP, 16, 128), f32),
        pltpu.VMEM((16, 128), f32),
        pltpu.VMEM((8, 128), f32),
        pltpu.VMEM((8, 128), f32),
    )


def rest(length, *arrays):
    tokens = TOKENS
    f32, bf16 = jnp.float32, jnp.bfloat16
    vmem = pl.BlockSpec(memory_space=pltpu.VMEM)
    hbm = pl.BlockSpec(memory_space=pl.ANY)
    shape = jax.ShapeDtypeStruct
    sems = pltpu.SemaphoreType.DMA
    scratch = [
        pltpu.VMEM((4, tokens, HALF), bf16),
        pltpu.VMEM((4, tokens, HALF), bf16),
        pltpu.VMEM((2, 4, 4, CAP, D), bf16),
        pltpu.VMEM((2, 4, 4, CAP, D), bf16),
        pltpu.VMEM((4, tokens, D), bf16),
        pltpu.VMEM((4, tokens, D), bf16),
        pltpu.VMEM((GROUP, 8, 128), f32),
        pltpu.VMEM((GROUP, 8, 128), f32),
        pltpu.VMEM((GROUP, 8, 128), f32),
        pltpu.VMEM((GROUP, 8, 128), f32),
        pltpu.VMEM((EXPERTS, tokens), f32),
        pltpu.VMEM((4, 2, 384, HALF), bf16),
        pltpu.VMEM((2, 384, HALF), bf16),
        pltpu.VMEM((2, 2, 384, HALF), bf16),
        pltpu.VMEM((tokens, D), bf16),
        pltpu.VMEM((tokens, HALF), bf16),
        pltpu.VMEM((tokens, HALF), bf16),
        pltpu.VMEM((2 * D, tokens), bf16),
        pltpu.VMEM((2, HALF, tokens), bf16),
        pltpu.VMEM((4, 4, 32, 3 * D), bf16),
        pltpu.VMEM((4, 32, 3 * D), bf16),
        pltpu.VMEM((PLANES, 32, 3 * D), bf16),
        pltpu.VMEM((GROUP, 16, 128), f32),
        pltpu.VMEM((PLANES, 16, 128), f32),
        pltpu.VMEM((GROUP, 8, 128), f32),
        pltpu.VMEM((PLANES, 8, 128), f32),
        pltpu.VMEM((GROUP, 8, 128), f32),
    ]
    for count in (11, 4, 2, 2, 4, 8, 1, 8, 1, 1, 2, 2, 1, 1, 1, 1, 10, 10, 9, 9, 3, 3, 3, 3, 3, 3, 5, 5):
        scratch += [sems((count,))]
    in_specs = [pl.BlockSpec(memory_space=pltpu.SMEM)] + [vmem] * len(arrays)
    for n in (6, 7, 8, 9, 13, 16, 17, 18, 19, 20, 21):
        in_specs[n] = hbm
    return pl.pallas_call(
        rest_kernel,
        out_shape=(
            shape((tokens, D), bf16),
            shape((tokens, D), f32),
            shape((8, 128), f32),
            shape((8, 128), f32),
            shape((GROUP, 8, 128), f32),
            shape((32, 3 * D), f32),
            shape((4, 2, 384, HALF), bf16),
            shape((2, 4, 4, CAP, D), bf16),
            shape((2, 4, 4, CAP, D), bf16),
        ),
        in_specs=in_specs,
        out_specs=[vmem] * 6 + [hbm] * 3,
        scratch_shapes=scratch,
        compiler_params=pltpu.CompilerParams(
            collective_id=2, has_side_effects=True, vmem_limit_bytes=62 << 20
        ),
        name="rest",
    )(length, *arrays)[:7]


def spread_kernel(
    hout_ref,
    hgrad_ref,
    own_ref,
    esum_ref,
    router_ref,
    again_ref,
    mgain_ref,
    hout_out,
    hgrad_out,
    q_out,
    k_out,
    v_out,
    o_out,
    gate_out,
    up_out,
    down_out,
    router_out,
    again_out,
    mgain_out,
):
    f32 = jnp.float32
    hout_out[...] = hout_ref[...]
    hgrad_out[...] = hgrad_ref[...]
    for p in range(2):
        q_out[:, p * HALF : p * HALF + HALF] = own_ref[:, p * D : p * D + HALF]
        k_out[:, p * 256 : p * 256 + 256] = own_ref[:, p * D + HALF : p * D + 768]
        v_out[:, p * 256 : p * 256 + 256] = own_ref[:, p * D + 768 : p * D + D]
    o_out[...] = own_ref[:, 2 * D : 3 * D]
    for h in range(2):
        gate_out[0, 128 * h : 128 * h + 128, :] = esum_ref[0, h, 0:128, :].astype(f32)
        up_out[0, 128 * h : 128 * h + 128, :] = esum_ref[0, h, 128:256, :].astype(f32)
        down_out[0, 64 * h : 64 * h + 64, 0:HALF] = esum_ref[0, h, 256:320, :].astype(f32)
        down_out[0, 64 * h : 64 * h + 64, HALF:D] = esum_ref[0, h, 320:384, :].astype(f32)
    for j in range(8):
        router_out[:, 128 * j : 128 * j + 128] = router_ref[:, j, :]
    again_out[...] = again_ref[...]
    mgain_out[...] = mgain_ref[...]


def spread_out(*arrays):
    f32, bf16 = jnp.float32, jnp.bfloat16
    shape = jax.ShapeDtypeStruct

    def whole(*dims):
        return pl.BlockSpec(dims, lambda i: (0,) * len(dims))

    def rows(count, width):
        return pl.BlockSpec((count, width), lambda i: (i, 0))

    def expert_rows(count, width):
        return pl.BlockSpec((1, count, width), lambda i: (0, i, 0))

    return pl.pallas_call(
        spread_kernel,
        grid=(4,),
        out_shape=(
            shape((TOKENS, D), bf16),
            shape((TOKENS, D), f32),
            shape((32, D), f32),
            shape((32, HALF), f32),
            shape((32, HALF), f32),
            shape((32, D), f32),
            shape((1, D, HALF), f32),
            shape((1, D, HALF), f32),
            shape((1, HALF, D), f32),
            shape((EXPERTS, D), f32),
            shape((8, 128), f32),
            shape((8, 128), f32),
        ),
        in_specs=[
            rows(64, D),
            rows(64, D),
            whole(32, 3 * D),
            pl.BlockSpec((1, 2, 384, HALF), lambda i: (i, 0, 0, 0)),
            whole(GROUP, 8, 128),
            whole(8, 128),
            whole(8, 128),
        ],
        out_specs=[
            rows(64, D),
            rows(64, D),
            whole(32, D),
            whole(32, HALF),
            whole(32, HALF),
            whole(32, D),
            expert_rows(256, HALF),
            expert_rows(256, HALF),
            expert_rows(128, D),
            whole(EXPERTS, D),
            whole(8, 128),
            whole(8, 128),
        ],
        name="spread_out",
    )(*arrays)


def on_device(
    hidden_in,
    cotangent,
    lengths,
    routes,
    priority,
    attn_gain,
    query_weight,
    key_weight,
    value_weight,
    output_weight,
    moe_gain,
    router,
    gate_weight,
    up_weight,
    down_weight,
):
    tok_count = hidden_in.shape[0]
    positions = lax.axis_index("row") * tok_count + jnp.arange(tok_count, dtype=jnp.int32)
    half_dim = HEAD // 2
    frequency = rotary_base ** (-jnp.arange(half_dim, dtype=jnp.float32) / half_dim)
    angles = frequency[:, None] * positions.astype(jnp.float32)[None, :]
    cosine, sine = jnp.cos(angles), jnp.sin(angles)
    router_t = router.T
    (
        weights,
        normed,
        queries,
        keys,
        values,
        log_total,
        mixed_rows,
        middle,
        routed,
        gates,
        pos,
        posz,
        posx,
        arrived_grad,
    ) = front(
        lengths,
        hidden_in,
        cotangent,
        routes.T,
        priority,
        attn_gain[None],
        moe_gain[None],
        query_weight,
        key_weight,
        value_weight,
        output_weight,
        router_t,
        cosine,
        sine,
    )
    summed = rest(
        lengths,
        routed,
        pos,
        posz,
        posx,
        gates,
        arrived_grad,
        gate_weight[0],
        up_weight[0],
        down_weight[0],
        router_t,
        middle,
        cotangent,
        hidden_in,
        attn_gain[None],
        moe_gain[None],
        normed,
        mixed_rows,
        weights,
        queries,
        keys,
        values,
        log_total,
        cosine,
        sine,
    )
    hidden_out, hidden_grad, attn_gain_sum, moe_gain_sum, router_sum, own_rows, expert_sum = summed
    (
        hidden_out,
        hidden_grad,
        query_grad,
        key_grad,
        value_grad,
        output_grad,
        gate_grad,
        up_grad,
        down_grad,
        router_grad,
        attn_gain_sum,
        moe_gain_sum,
    ) = spread_out(
        hidden_out, hidden_grad, own_rows, expert_sum, router_sum, attn_gain_sum, moe_gain_sum
    )
    return (
        hidden_out,
        hidden_grad,
        attn_gain_sum.reshape(D),
        query_grad,
        key_grad,
        value_grad,
        output_grad,
        moe_gain_sum.reshape(D),
        router_grad.T,
        gate_grad,
        up_grad,
        down_grad,
    )


def solution(mesh):
    return jax.shard_map(
        on_device,
        mesh=mesh,
        in_specs=(
            P(("dp", "col", "row"), None),
            P(("dp", "col", "row"), None),
            P(("dp", "col")),
            P(("dp", "col", "row"), None),
            P(("dp", "col", "row"), None),
            P(),
            P(("row", "col"), None),
            P(("row", "col"), None),
            P(("row", "col"), None),
            P(("row", "col"), None),
            P(),
            P(),
            P(("row", "col"), None, None),
            P(("row", "col"), None, None),
            P(("row", "col"), None, None),
        ),
        out_specs=(
            P(("dp", "col", "row"), None),
            P(("dp", "col", "row"), None),
            P(),
            P(("row", "col"), None),
            P(("row", "col"), None),
            P(("row", "col"), None),
            P(("row", "col"), None),
            P(),
            P(),
            P(("row", "col"), None, None),
            P(("row", "col"), None, None),
            P(("row", "col"), None, None),
        ),
        check_vma=False,
    )
```

```python
import jax
import jax.numpy as jnp
import numpy as np
from jax import lax
from jax.experimental import pallas as pl
from jax.experimental.pallas import tpu as pltpu
from jax.sharding import PartitionSpec as P

D = 1024
HEADS = 16
HEAD = 64
KV_HEADS = 8
EXPERTS = 32
TOP = 8
CAP = 64


epsilon = 1e-05
rotary_base = 10000.0


MESH = pl.DeviceIdType.MESH
GROUP = 32
PLANES = 4
CHIPS = 16
HALF = D // 2
TOKENS = 256
NEG = -1000000000.0


def place():
    col = lax.axis_index("col")
    return lax.axis_index("dp"), lax.axis_index("row"), lax.rem(col, 4), col // 4


def moved(dx, dz, core):
    y, r, x, z = place()
    col = lax.rem(z + dz + 4, 4) * 4 + lax.rem(x + dx + 4, 4)
    return (y, core, col), core * CHIPS + col


def plane_shift(n):
    y, r, x, z = place()
    other = lax.rem(y + n, PLANES)
    return (other, r, z * 4 + x), other


def step_of(k, sign):
    y, r, x, z = place()
    return moved(sign * lax.rem(k, 4), sign * lax.rem(k // 4, 4), lax.rem(r + k // CHIPS, 2))


def remote(src, dst, send_sem, recv_sem, device):
    return pltpu.make_async_remote_copy(
        src_ref=src,
        dst_ref=dst,
        send_sem=send_sem,
        recv_sem=recv_sem,
        device_id=device,
        device_id_type=MESH,
    )


def done(ref, sem):
    pltpu.make_async_copy(ref, ref, sem).wait()


def meet(plane, planes):
    barrier = pltpu.get_barrier_semaphore()
    y, r, x, z = place()

    def greet(device):
        pl.semaphore_signal(barrier, inc=1, device_id=device, device_id_type=MESH)

    if plane:

        @pl.loop(1, GROUP)
        def _(k):
            greet(step_of(k, 1)[0])

        count = GROUP - 1
    else:
        for core in range(2):

            @pl.loop(1, 4)
            def _(d):
                greet(moved(d, 0, core)[0])
                greet(moved(0, d, core)[0])

        greet(moved(0, 0, 1 - r)[0])
        count = 13
    if planes:
        for n in range(1, PLANES):
            greet(plane_shift(n)[0])
        count += PLANES - 1
    pl.semaphore_wait(barrier, count)


def eye(n):
    return lax.broadcasted_iota(jnp.int32, (n, n), 0) == lax.broadcasted_iota(
        jnp.int32, (n, n), 1
    )


def as_row(column):
    return jnp.sum(jnp.where(eye(column.shape[0]), column, 0.0), axis=0, keepdims=True)


def as_column(row_vec):
    return jnp.sum(jnp.where(eye(row_vec.shape[1]), row_vec, 0.0), axis=1, keepdims=True)


def dot(a, b, dims):
    return lax.dot_general(a, b, (dims, ((), ())), preferred_element_type=jnp.float32)


def split_two(values):
    high = values.astype(jnp.bfloat16)
    return high, (values - high.astype(jnp.float32)).astype(jnp.bfloat16)


def picks(positions):
    slots = lax.broadcasted_iota(jnp.int32, (CAP, positions.shape[1]), 0)
    return slots == positions


def as_hot(mask):
    return mask.astype(jnp.float32).astype(jnp.bfloat16)


LEFT = pl.ds(0, HALF)
RIGHT = pl.ds(HALF, HALF)


def spread(d, source, tok_z, tok_x, send_sem, recv_sem):
    y, r, x, z = place()
    return (
        remote(
            source.at[:, LEFT], tok_z.at[d], send_sem.at[0], recv_sem.at[0], moved(0, d, r)[0]
        ),
        remote(
            source.at[:, RIGHT], tok_x.at[d], send_sem.at[1], recv_sem.at[1], moved(d, 0, r)[0]
        ),
    )


def pass_on(tok_z, tok_x, send_sem, recv_sem):
    y, r, x, z = place()
    copies = []
    for n, (d, sign) in enumerate(((1, 1), (3, -1))):
        rows = pl.ds(n * 128, 128)
        for tok, at, device in (
            (tok_z, 2, moved(0, sign, r)[0]),
            (tok_x, 3, moved(sign, 0, r)[0]),
        ):
            copies.append(
                remote(
                    tok.at[d, rows], tok.at[2, rows], send_sem.at[at], recv_sem.at[at], device
                )
            )
    return copies


def near_done(tok_z, tok_x, sem):
    done(tok_z.at[pl.ds(0, 2)], sem.at[0])
    done(tok_x.at[pl.ds(0, 2)], sem.at[1])


def far_done(tok_z, tok_x, sem):
    done(tok_z.at[2], sem.at[2])
    done(tok_x.at[2], sem.at[3])


def is_local(core, offset):
    y, r, x, z = place()
    return (core == r) & (offset == 0)


def send_slots(
    out,
    into,
    there,
    dz,
    dx,
    send_sem,
    recv_left,
    recv_right,
    sign,
    local_sem=None,
    halves=(True, True),
):
    y, r, x, z = place()

    def one(cols, offset, device, recv_sem):
        source, target = out.at[there, dz, dx, :, cols], into.at[r, dz, dx, :, cols]

        @pl.when(jnp.logical_not(is_local(there, offset)))
        def _():
            remote(source, target, send_sem, recv_sem, device).start()

        @pl.when(is_local(there, offset))
        def _():
            if local_sem is None:
                target[...] = source[...]
            else:
                pltpu.make_async_copy(source, target, local_sem).start()

    if halves[0]:
        one(LEFT, dx, moved(sign * dx, 0, there)[0], recv_left)
    if halves[1]:
        one(RIGHT, dz, moved(0, sign * dz, there)[0], recv_right)


def all_slots(ref):
    return ref.at[:, :, :, :, pl.ds(0, 896)]


def line_rows(line, d, axis):
    y, r, x, z = place()
    own = x if axis == 0 else z
    return [
        line[d, pl.ds(core * 4 + lax.rem(own + i, 4), 1), :] for core in range(2) for i in range(4)
    ]


def line_hot(line, d, axis):
    return as_hot(jnp.concatenate([picks(p) for p in line_rows(line, d, axis)], axis=0))


def add_up(mid, line, d, axis):
    if axis == 0:
        rows = mid[:, d, :, :, 0:HALF]
    else:
        rows = mid[:, :, d, :, HALF:D]
    return dot(line_hot(line, d, axis), rows.reshape(8 * CAP, HALF), ((0,), (0,))).astype(
        jnp.bfloat16
    )


def part_copy(d, rows, axis, sign, out, into, send_sem, recv_sem):
    y, r, x, z = place()
    cols = (LEFT, RIGHT)[axis]
    device = moved(sign * axis, sign * (1 - axis), r)[0]
    part = pl.ds(rows, 128)
    return remote(out.at[d, part, cols], into.at[d, part, cols], send_sem, recv_sem, device)


def fold_start(out, into, mid, slot_recv, posz_ref, posx_ref, sems):
    send_sem, recv_sem = sems
    for d in (2, 0, 1, 3):
        for axis, pos in enumerate((posz_ref, posx_ref)):
            if slot_recv is not None:
                done(mid.at[0, 0, :, :, pl.ds(0, 896)], slot_recv.at[4 * axis + d])
            total = add_up(mid, pos, d, axis)
            cols = slice(axis * HALF, axis * HALF + HALF)
            if d == 0:
                into[0, :, cols] = total
                continue
            out[d, :, cols] = total
            if d == 2:
                for rows, sign in ((0, -1), (128, 1)):
                    args = rows, axis, sign, out, into, send_sem.at[0], recv_sem.at[axis]
                    part_copy(2, *args).start()
            else:
                rows, sign = (128, -1) if d == 1 else (0, 1)
                args = rows, axis, sign, out, into, send_sem.at[0], recv_sem.at[2]
                part_copy(d, *args).start()


def fold_end(out, into, sems):
    send_sem, recv_sem = sems
    for axis in range(2):
        cols = slice(axis * HALF, axis * HALF + HALF)
        done(into.at[2, :, (LEFT, RIGHT)[axis]], recv_sem.at[axis])
        for d, rows, sign in ((1, 0, -1), (3, 128, 1)):
            part = slice(rows, rows + 128)
            total = out[d, part, cols].astype(jnp.float32) + into[2, part, cols].astype(jnp.float32)
            out[d, part, cols] = total.astype(jnp.bfloat16)
            args = rows, axis, sign, out, into, send_sem.at[0], recv_sem.at[2]
            part_copy(d, *args).start()


def folded(into, sems):
    done(into.at[pl.ds(0, 2)], sems[1].at[2])
    f32 = jnp.float32
    return into[0].astype(f32) + (into[1].astype(f32) + into[3].astype(f32))


def front_kernel(
    length_ref,
    hidden_ref,
    cot_ref,
    routes_ref,
    prio_ref,
    again_ref,
    mgain_ref,
    wq_ref,
    wk_ref,
    wv_ref,
    wo_ref,
    router_ref,
    cos_ref,
    sin_ref,
    w_hbm,
    normed_ref,
    q_ref,
    k_ref,
    v_ref,
    lse_ref,
    mixed_ref,
    middle_ref,
    routed_ref,
    gates_ref,
    pos_ref,
    posz_ref,
    posx_ref,
    grads_ref,
    w_ref,
    mixed_t,
    posz_out,
    posx_out,
    tok_z,
    tok_x,
    outgoing,
    store_sem,
    w_send,
    w_recv,
    o_send,
    o_recv,
    core_send,
    core_recv,
    kv_send,
    kv_recv,
    first_send,
    first_recv,
    slot_send,
    slot_recv,
    pos_send,
    pos_recv,
):
    y, r, x, z = place()
    f32, bf16 = jnp.float32, jnp.bfloat16
    sibling = moved(0, 0, 1 - r)[0]
    meet(False, True)

    for p in range(2):
        part = slice(256 * p, 256 * p + 256)
        w_ref[r, z, x, :, D * p : D * p + HALF] = wq_ref[:, HALF * p : HALF * p + HALF]
        w_ref[r, z, x, :, D * p + HALF : D * p + 768] = wk_ref[:, part]
        w_ref[r, z, x, :, D * p + 768 : D * p + D] = wv_ref[:, part]
    front, rear, output = pl.ds(0, D), pl.ds(D, D), pl.ds(2 * D, D)
    quarter = pl.ds(pl.multiple_of(2 * D + 256 * y, 256), 256)

    def line_step(d):
        mine_q, mine_o = w_ref.at[r, z, x, :, front], w_ref.at[r, z, x, :, rear]
        return (
            remote(mine_q, mine_q, w_send.at[0], w_recv.at[d], moved(0, d, r)[0]),
            remote(mine_o, mine_o, w_send.at[0], w_recv.at[4 + d], moved(d, 0, r)[0]),
        )

    def cross_step(e, d):
        from_z = w_ref.at[r, lax.rem(z - e + 4, 4), x, :, front]
        from_x = w_ref.at[r, z, lax.rem(x - e + 4, 4), :, rear]
        return (
            remote(from_z, from_z, w_send.at[1], w_recv.at[8 + d], moved(d, 0, r)[0]),
            remote(from_x, from_x, w_send.at[1], w_recv.at[8 + d], moved(0, d, r)[0]),
        )

    w_ref[r, z, x, :, quarter] = wo_ref[:, pl.ds(pl.multiple_of(256 * y, 256), 256)]

    def output_line(d):
        own = w_ref.at[r, z, x, :, quarter]
        return remote(own, own, o_send.at[0], o_recv.at[0], moved(0, d, r)[0])

    def output_cross(d):
        own = w_ref.at[r, :, x, :, quarter]
        return remote(own, own, o_send.at[1], o_recv.at[1], moved(d, 0, r)[0])

    def output_plane(n):
        own = w_ref.at[r, :, :, :, quarter]
        return remote(own, own, o_send.at[2], o_recv.at[2], plane_shift(n)[0])

    def output_core():
        own = w_ref.at[r, :, :, :, output]
        return remote(own, own, o_send.at[3], o_recv.at[3], sibling)

    def some(rows, width):
        return w_ref.at[0, pl.ds(0, rows), :, :, pl.ds(0, width)]

    def core_step(d):
        from_x = w_ref.at[r, :, lax.rem(x - d + 4, 4), :, front]
        from_z = w_ref.at[r, lax.rem(z - d + 4, 4), :, :, rear]
        return (
            remote(from_x, from_x, core_send.at[0], core_recv.at[0], sibling),
            remote(from_z, from_z, core_send.at[0], core_recv.at[0], sibling),
        )

    @pl.loop(1, 4)
    def _(d):
        for copy in line_step(d):
            copy.start()

    @pl.loop(1, 4)
    def _(d):
        for copy in cross_step(0, d):
            copy.start()
        output_line(d).start()

    tokens = hidden_ref.shape[0]
    experts_iota = lax.broadcasted_iota(jnp.int32, (EXPERTS, tokens), 0).astype(f32)
    live = r * tokens + lax.broadcasted_iota(jnp.int32, (1, tokens), 1) < length_ref[0]
    routed_to = jnp.zeros((EXPERTS, tokens), f32)
    ranks = jnp.zeros((EXPERTS, tokens), f32)
    prio = prio_ref[...]
    lines = jnp.concatenate([prio[:, 128 * i : 128 * i + 128] for i in range(CHIPS)], axis=0)
    token = lax.broadcasted_iota(jnp.int32, (tokens, CHIPS), 0) // CHIPS
    owner = (token == lax.broadcasted_iota(jnp.int32, (tokens, CHIPS), 1)).astype(f32)
    token = lax.rem(lax.broadcasted_iota(jnp.int32, (tokens, 128), 0), CHIPS)
    lane = lax.broadcasted_iota(jnp.int32, (tokens, 128), 1)
    place_of = lax.rem(lax.broadcasted_iota(jnp.int32, (TOP, 128), 1), TOP)
    place_of = (place_of == lax.broadcasted_iota(jnp.int32, (TOP, 128), 0)).astype(f32)
    priority = jnp.zeros((TOP, tokens), f32)
    for unit, part in ((64.0, lines // 64), (1.0, lax.rem(lines, 64))):
        part = part.astype(f32).astype(bf16)
        rows = dot(owner.astype(bf16), part, ((1,), (0,)))
        rows = jnp.where(lane // TOP == token, rows, 0.0).astype(bf16)
        priority = priority + unit * dot(place_of.astype(bf16), rows, ((1,), (1,)))
    routes = routes_ref[...].astype(f32)
    for j in range(TOP):
        match = experts_iota == routes[j : j + 1, :]
        routed_to = jnp.where(match, 1.0, routed_to)
        ranks = jnp.where(match, priority[j : j + 1, :], ranks)
    far = float(1 << 20)
    ranks = jnp.where((routed_to > 0.0) & live, ranks, far)
    ranks_t = ranks.T
    rows = []
    for e in range(EXPERTS):
        earlier = ranks_t[:, e : e + 1] < ranks[e : e + 1, :]
        rows.append(jnp.sum(earlier.astype(f32), axis=0, keepdims=True))
    slots = jnp.concatenate(rows, axis=0)
    pos = jnp.where((ranks < far) & (slots < CAP), slots, -1.0).astype(jnp.int32)
    pos_ref[...] = pos
    for core in range(2):
        for i in range(4):
            at = core * CHIPS + 4 * i
            posz_out[i, 4 * core : 4 * core + 4, :] = pos[at : at + 4, :]
            for j in range(4):
                posx_out[j, 4 * core + i : 4 * core + i + 1, :] = pos[at + j : at + j + 1, :]
    posz_ref[0] = posz_out[z]
    posx_ref[0] = posx_out[x]
    tok_z[0] = cot_ref[:, 0:HALF]
    tok_x[0] = cot_ref[:, HALF:D]

    def pos_step(d):
        to_z, to_x = lax.rem(z + d, 4), lax.rem(x + d, 4)
        return (
            remote(
                posz_out.at[to_z],
                posz_ref.at[d],
                pos_send.at[0],
                pos_recv.at[0],
                moved(0, d, r)[0],
            ),
            remote(
                posx_out.at[to_x],
                posx_ref.at[d],
                pos_send.at[1],
                pos_recv.at[1],
                moved(d, 0, r)[0],
            ),
        )

    @pl.loop(1, 4)
    def _(d):
        for copy in pos_step(d):
            copy.start()

    done(w_ref.at[0, 0, pl.ds(0, 3), :, pl.ds(0, 256)], o_recv.at[0])

    @pl.loop(1, 4)
    def _(d):
        output_cross(d).start()

    @pl.loop(1, 4)
    def _(e):
        for copy in line_step(e):
            copy.wait_recv()

        @pl.loop(1, 4)
        def _(d):
            for copy in cross_step(e, d):
                copy.start()

    for d in (1, 3):
        for copy in spread(d, cot_ref, tok_z, tok_x, first_send, first_recv):
            copy.start()

    for copy in core_step(0):
        copy.start()

    def cut_slots(d):
        left = dot(line_hot(posz_ref, d, 0), tok_z[d], ((1,), (0,))).astype(bf16)
        right = dot(line_hot(posx_ref, d, 1), tok_x[d], ((1,), (0,))).astype(bf16)
        sems = slot_send.at[0], slot_recv.at[0], slot_recv.at[0], 1, store_sem.at[1]
        for core in range(2):
            for i in range(4):
                part = slice((core * 4 + i) * CAP, (core * 4 + i + 1) * CAP)
                outgoing[core, d, i, :, 0:HALF] = left[part]
                send_slots(outgoing, grads_ref, core, d, i, *sems, (True, False))
                outgoing[core, i, d, :, HALF:D] = right[part]
                send_slots(outgoing, grads_ref, core, i, d, *sems, (False, True))

    cut_slots(0)

    inputs = hidden_ref[...].astype(f32)
    scale = lax.rsqrt(jnp.mean(inputs * inputs, axis=1, keepdims=True) + epsilon)
    normed_ref[...] = (inputs * scale * again_ref[...]).astype(bf16)

    done(some(3, 256), o_recv.at[1])

    for n in range(1, PLANES):
        output_plane(n).start()

    @pl.loop(1, 4)
    def _(d):
        done(some(1, 2 * D), w_recv.at[8 + d])
        for copy in core_step(d):
            copy.start()

    near_done(tok_z, tok_x, first_recv)
    for copy in pass_on(tok_z, tok_x, first_send, first_recv):
        copy.start()
    done(posz_ref.at[pl.ds(1, 3)], pos_recv.at[0])
    done(posx_ref.at[pl.ds(1, 3)], pos_recv.at[1])

    @pl.loop(0, 2)
    def _(n):
        cut_slots(1 + 2 * n)

    done(some(4, 2 * D), core_recv.at[0])

    here = pl.ds(pl.multiple_of(r * tokens, tokens), tokens)
    cosine, sine = cos_ref[:, here], sin_ref[:, here]

    def projected(first):
        weight = w_ref[:, :, :, :, first : first + HALF].reshape(D, HALF)
        return dot(normed_ref[...], weight, ((1,), (0,))).T

    def turned(rows):
        parts = []
        for h in range(rows.shape[0] // HEAD):
            first, second = rows[HEAD * h : HEAD * h + 32], rows[HEAD * h + 32 : HEAD * h + HEAD]
            parts += [first * cosine - second * sine, second * cosine + first * sine]
        return jnp.concatenate(parts, axis=0).astype(bf16)

    key_copy = remote(
        k_ref.at[:, here], k_ref.at[:, here], kv_send.at[0], kv_recv.at[0], sibling
    )
    value_copy = remote(
        v_ref.at[:, here], v_ref.at[:, here], kv_send.at[1], kv_recv.at[1], sibling
    )
    for p in range(2):
        both = projected(D * p + HALF)
        k_ref[256 * p : 256 * p + 256, here] = turned(both[0:256])
        v_ref[256 * p : 256 * p + 256, here] = both[256:512].astype(bf16)
    key_copy.start()
    value_copy.start()
    for p in range(2):
        q_ref[HALF * p : HALF * p + HALF, :] = turned(projected(D * p))

    far_done(tok_z, tok_x, first_recv)
    cut_slots(2)

    key_copy.wait_recv()
    value_copy.wait_recv()

    done(some(4, 768), o_recv.at[2])
    output_core().start()

    key_live = lax.broadcasted_iota(jnp.int32, (2 * tokens, 1), 0) < length_ref[0]
    score_scale = HEAD ** (-0.5)

    @pl.loop(0, KV_HEADS)
    def _(g):
        head = pl.ds(pl.multiple_of(g * HEAD, HEAD), HEAD)
        keys, values = k_ref[head, :], v_ref[head, :]
        for j in range(2):
            at = pl.ds(pl.multiple_of((2 * g + j) * HEAD, HEAD), HEAD)
            scores = dot(keys, q_ref[at, :], ((0,), (0,))) * score_scale
            scores = jnp.where(key_live, scores, NEG)
            top = jnp.max(scores, axis=0, keepdims=True)
            weights = jnp.exp(scores - top)
            total = jnp.sum(weights, axis=0, keepdims=True)
            lse_ref[pl.ds(2 * g + j, 1), :] = top + jnp.log(total)
            probs = (weights * (1.0 / total)).astype(bf16)
            mixed_t[at, :] = dot(values, probs, ((1,), (0,))).astype(bf16)

    mixed_ref[...] = mixed_t[...].T
    output_core().wait_recv()
    weights_out = pltpu.make_async_copy(w_ref, w_hbm, store_sem.at[0])
    weights_out.start()
    w_out = w_ref[:, :, :, :, 2 * D : 3 * D].reshape(D, D)
    middle = hidden_ref[...].astype(f32) + dot(mixed_ref[...], w_out, ((1,), (0,)))
    middle_ref[...] = middle
    scale = lax.rsqrt(jnp.mean(middle * middle, axis=1, keepdims=True) + epsilon)
    routed_ref[...] = (middle * scale * mgain_ref[...]).astype(bf16)
    logits = dot(router_ref[...], routed_ref[...], ((1,), (1,)))
    logits = jnp.where(routed_to > 0.0, logits, -jnp.inf)
    picked = jnp.exp(logits - jnp.max(logits, axis=0, keepdims=True))
    gates_ref[...] = picked / jnp.sum(picked, axis=0, keepdims=True)

    done(all_slots(grads_ref), slot_recv.at[0])
    done(grads_ref.at[0, 0], store_sem.at[1])
    done(all_slots(outgoing), slot_send.at[0])
    done(w_ref.at[0, 0, pl.ds(0, 3), :, pl.ds(0, 2 * D)], w_send.at[0])
    done(some(3, 2 * D), w_send.at[1])
    done(some(4, 2 * D), core_send.at[0])
    done(w_ref.at[0, 0, pl.ds(0, 3), :, pl.ds(0, 256)], o_send.at[0])
    done(some(3, 256), o_send.at[1])
    done(some(4, 768), o_send.at[2])
    output_core().wait_send()
    near_done(tok_z, tok_x, first_send)
    far_done(tok_z, tok_x, first_send)
    done(posz_ref.at[pl.ds(1, 3)], pos_send.at[0])
    done(posx_ref.at[pl.ds(1, 3)], pos_send.at[1])
    weights_out.wait()
    key_copy.wait_send()
    value_copy.wait_send()


def front(length, *arrays):
    f32, bf16, i32 = jnp.float32, jnp.bfloat16, jnp.int32
    vmem = pl.BlockSpec(memory_space=pltpu.VMEM)
    hbm = pl.BlockSpec(memory_space=pl.ANY)
    shape = jax.ShapeDtypeStruct
    out_shape = (
        shape((2, 4, 4, 32, 3 * D), bf16),
        shape((TOKENS, D), bf16),
        shape((D, TOKENS), bf16),
        shape((HALF, 2 * TOKENS), bf16),
        shape((HALF, 2 * TOKENS), bf16),
        shape((HEADS, TOKENS), f32),
        shape((TOKENS, D), bf16),
        shape((TOKENS, D), f32),
        shape((TOKENS, D), bf16),
        shape((EXPERTS, TOKENS), f32),
        shape((EXPERTS, TOKENS), i32),
        shape((4, 8, TOKENS), i32),
        shape((4, 8, TOKENS), i32),
        shape((2, 4, 4, CAP, D), bf16),
    )
    scratch = [
        pltpu.VMEM((2, 4, 4, 32, 3 * D), bf16),
        pltpu.VMEM((D, TOKENS), bf16),
        pltpu.VMEM((4, 8, TOKENS), i32),
        pltpu.VMEM((4, 8, TOKENS), i32),
        pltpu.VMEM((4, TOKENS, HALF), bf16),
        pltpu.VMEM((4, TOKENS, HALF), bf16),
        pltpu.VMEM((2, 4, 4, CAP, D), bf16),
    ]
    scratch += [pltpu.SemaphoreType.DMA((2,))]
    for count in (12, 4, 1, 2, 4, 1, 2):
        scratch += [pltpu.SemaphoreType.DMA((count,))] * 2
    return pl.pallas_call(
        front_kernel,
        out_shape=out_shape,
        in_specs=[pl.BlockSpec(memory_space=pltpu.SMEM)] + [vmem] * len(arrays),
        out_specs=[hbm] + [vmem] * (len(out_shape) - 2) + [hbm],
        scratch_shapes=scratch,
        compiler_params=pltpu.CompilerParams(
            collective_id=3, has_side_effects=True, vmem_limit_bytes=60 << 20
        ),
        name="front",
    )(length, *arrays)


def turned_back(rows, cosine, sine):
    first, second = rows[0:32], rows[32:64]
    return jnp.concatenate(
        [first * cosine + second * sine, second * cosine - first * sine], axis=0
    )


def rest_kernel(
    length_ref,
    routed_ref,
    pos_ref,
    posz_ref,
    posx_ref,
    gates_ref,
    grads_hbm,
    wg_hbm,
    wu_hbm,
    wd_hbm,
    router_ref,
    middle_ref,
    cot_ref,
    hidden_hbm,
    again_ref,
    mgain_ref,
    normed_hbm,
    mixed_hbm,
    w_hbm,
    q_hbm,
    k_hbm,
    v_hbm,
    lse_ref,
    cos_ref,
    sin_ref,
    hout_ref,
    hgrad_ref,
    again_out,
    mgain_out,
    router_out,
    own_out,
    esum_hbm,
    prod_hbm,
    mid_hbm,
    tok_z,
    tok_x,
    arrived,
    mid,
    parts_in,
    parts_in2,
    gate_out,
    gate_in,
    dot_out,
    dot_in,
    gdot_ref,
    expert_ref,
    relay_in,
    y_in,
    branch_sib,
    normed_sib,
    mixed_sib,
    grad_sib,
    kv_in,
    rs_in,
    rs_in2,
    y_parts,
    small_in,
    small_y_in,
    gain_in,
    gain_y_in,
    router_all,
    load_sem,
    store_sem,
    first_send,
    first_recv,
    slot_send,
    slot_recv,
    back_send,
    back_recv,
    part_send,
    part_recv,
    small_send,
    small_recv,
    c_send,
    c_recv,
    part_send2,
    part_recv2,
    ex_send,
    ex_recv,
    sib_send,
    sib_recv,
    rs_send,
    rs_recv,
    rs_send2,
    rs_recv2,
    ys_send,
    ys_recv,
    sm_send,
    sm_recv,
):
    y, r, x, z = place()
    me = r * CHIPS + z * 4 + x
    sibling = moved(0, 0, 1 - r)[0]
    tokens = TOKENS
    f32, bf16 = jnp.float32, jnp.bfloat16

    above, below = plane_shift(1), plane_shift(3)
    opposite = plane_shift(2)[1]
    def relayed(n):
        device = (above, below)[n][0]
        return remote(
            expert_ref.at[0, n], relay_in.at[n], ex_send.at[n], ex_recv.at[n], device
        )

    def direct(n):
        device = (above, below)[n][0]
        return remote(
            expert_ref.at[1 + n, 1 - n],
            y_in.at[n, 1 - n],
            ex_send.at[2 + n],
            ex_recv.at[2 + n],
            device,
        )

    def passed_on(n):
        device, came_from = (above, below)[n][0], (below, above)[n][1]
        part = esum_hbm.at[came_from, n]
        return remote(part, part, ex_send.at[8 + n], ex_recv.at[8 + n], device)

    def to_sibling(at, src, dst):
        return remote(src, dst, sib_send.at[at], sib_recv.at[at], sibling)

    half = pl.ds(pl.multiple_of((1 - r) * HALF, HALF), HALF)
    sib_normed = to_sibling(0, normed_hbm.at[:, half], normed_sib)
    sib_mixed = to_sibling(1, mixed_hbm.at[:, half], mixed_sib)

    meet(True, True)
    sib_mixed.start()
    sib_normed.start()

    def expert_phase(grads_ref, wg_ref, wu_ref, wd_ref, outgoing, parts_out, active, weighted, pre_grads):
        loads = [
            pltpu.make_async_copy(source, target, load_sem.at[n])
            for n, (source, target) in enumerate(
                (
                    (wg_hbm, wg_ref),
                    (wu_hbm, wu_ref),
                    (wd_hbm, wd_ref),
                    (grads_hbm, grads_ref),
                )
            )
        ]
        for load in loads:
            load.start()

        for d in (1, 3):
            for copy in spread(d, routed_ref, tok_z, tok_x, first_send, first_recv):
                copy.start()

        tok_z[0] = routed_ref[:, 0:HALF]
        tok_x[0] = routed_ref[:, HALF:D]

        def send_rows(core, dz, dx, g, halves):
            came = slot_recv.at[2 * g + r]
            sems = slot_send.at[g], came, came, 1, None
            send_slots(outgoing, arrived, core, dz, dx, *sems, halves)

        left = dot(line_hot(posz_ref, 0, 0), tok_z[0], ((1,), (0,))).astype(bf16)
        right = dot(line_hot(posx_ref, 0, 1), tok_x[0], ((1,), (0,))).astype(bf16)
        for core in range(2):
            for i in range(4):
                part = slice((core * 4 + i) * CAP, (core * 4 + i + 1) * CAP)
                outgoing[core, 0, i, :, 0:HALF] = left[part]
                send_rows(core, 0, i, (4 - i) % 4, (True, False))
                outgoing[core, i, 0, :, HALF:D] = right[part]
                send_rows(core, i, 0, i, (False, True))

        def small(k, out, into, sign, base):
            there, dz, dx = k // CHIPS, lax.rem(k // 4, 4), lax.rem(k, 4)
            slot = r * CHIPS + lax.rem(k, CHIPS)
            return remote(
                out.at[k],
                into.at[slot],
                small_send.at[base],
                small_recv.at[base],
                moved(sign * dx, sign * dz, there)[0],
            )

        def own_slot(k):
            return k == r * CHIPS

        near_done(tok_z, tok_x, first_recv)
        for copy in pass_on(tok_z, tok_x, first_send, first_recv):
            copy.start()

        @pl.loop(0, GROUP)
        def _(k):
            there, dz, dx = k // CHIPS, lax.rem(k // 4, 4), lax.rem(k, 4)
            _, expert = moved(dx, dz, there)
            chosen = picks(pos_ref[pl.ds(expert, 1), :])
            gate_col = jnp.sum(
                jnp.where(chosen, gates_ref[pl.ds(expert, 1), :], 0.0), axis=1, keepdims=True
            )
            gate_out[k, 0:1, 0:CAP] = as_row(gate_col)

            @pl.when(own_slot(k))
            def _():
                gate_in[k] = gate_out[k]

            @pl.when(jnp.logical_not(own_slot(k)))
            def _():
                small(k, gate_out, gate_in, 1, 0).start()

        far_done(tok_z, tok_x, first_recv)

        @pl.loop(0, 4)
        def _(g):
            for dx in range(4):
                dz = lax.rem(dx + g, 4)

                @pl.when(dz != 0)
                def _():
                    rows = [
                        picks(posz_ref[dz, pl.ds(core * 4 + lax.rem(x + dx, 4), 1), :])
                        for core in range(2)
                    ]
                    rows = dot(as_hot(jnp.concatenate(rows, axis=0)), tok_z[dz], ((1,), (0,)))
                    for core in range(2):
                        part = slice(core * CAP, core * CAP + CAP)
                        outgoing[core, dz, dx, :, 0:HALF] = rows[part].astype(bf16)
                        send_rows(core, dz, dx, g, (True, False))

                if dx == 0:
                    continue
                rows = [
                    picks(posx_ref[dx, pl.ds(core * 4 + lax.rem(z + dz, 4), 1), :])
                    for core in range(2)
                ]
                rows = dot(as_hot(jnp.concatenate(rows, axis=0)), tok_x[dx], ((1,), (0,)))
                for core in range(2):
                    part = slice(core * CAP, core * CAP + CAP)
                    outgoing[core, dz, dx, :, HALF:D] = rows[part].astype(bf16)
                    send_rows(core, dz, dx, g, (False, True))

        def keep_produced(k):
            core, dz, dx = k // CHIPS, lax.rem(k // 4, 4), lax.rem(k, 4)
            return pltpu.make_async_copy(
                grads_ref.at[core, dz, dx],
                prod_hbm.at[core, dz, dx],
                store_sem.at[lax.rem(dz - dx + 4, 4)],
            )

        for load in loads:
            load.wait()
        done(gate_in.at[pl.ds(0, GROUP - 1)], small_recv.at[0])

        @pl.loop(0, 8)
        def _(c):
            g, core = c // 2, lax.rem(c, 2)

            @pl.when(core == r)
            def _():
                done(arrived.at[0, 0, pl.ds(0, 3)], slot_recv.at[c])

            @pl.when(core != r)
            def _():
                done(arrived.at[0, 0], slot_recv.at[c])

            @pl.when(core == 0)
            def _():
                done(outgoing.at[0, pl.ds(0, 2), :, :, pl.ds(0, 896)], slot_send.at[g])

            rows, gate_cols, grads = [], [], []
            for dx in range(4):
                dz = lax.rem(dx + g, 4)
                k = core * CHIPS + dz * 4 + dx
                rows.append(arrived[core, dz, dx])
                gate_cols.append(as_column(gate_in[k, 0:1, 0:CAP]))
                grads.append(grads_ref[core, dz, dx])
            rows = jnp.concatenate(rows, axis=0)
            gate_cols = jnp.concatenate(gate_cols, axis=0)
            grads = jnp.concatenate(grads, axis=0).astype(f32)
            gate_pre = dot(rows, wg_ref[...], ((1,), (0,)))
            up_pre = dot(rows, wu_ref[...], ((1,), (0,)))
            gate_sig = jax.nn.sigmoid(gate_pre)
            gate_act = gate_pre * gate_sig
            act = (gate_act * up_pre).astype(bf16)
            produced = dot(act, wd_ref[...], ((1,), (0,))).astype(bf16).astype(f32)
            dots = jnp.sum(produced * grads, axis=1, keepdims=True)
            produced_grad = (gate_cols * grads).astype(bf16)
            act_grad = dot(produced_grad, wd_ref[...], ((1,), (1,))).astype(bf16).astype(f32)
            gate_grad = (
                act_grad * up_pre * gate_sig * (1.0 + gate_pre * (1.0 - gate_sig))
            ).astype(bf16)
            up_grad = (act_grad * gate_act).astype(bf16)
            row_grads = dot(gate_grad, wg_ref[...], ((1,), (1,)))
            row_grads = (row_grads + dot(up_grad, wu_ref[...], ((1,), (1,)))).astype(bf16)
            produced = (produced * gate_cols).astype(bf16)
            for dx in range(4):
                dz = lax.rem(dx + g, 4)
                k = core * CHIPS + dz * 4 + dx
                part = slice(dx * CAP, dx * CAP + CAP)
                outgoing[core, dz, dx] = row_grads[part]
                send_slots(
                    outgoing,
                    mid,
                    core,
                    dz,
                    dx,
                    back_send.at[0],
                    back_recv.at[dz],
                    back_recv.at[4 + dx],
                    -1,
                )
                dot_out[k, 0:1, 0:CAP] = as_row(dots[part])

                @pl.when(own_slot(k))
                def _():
                    dot_in[k] = dot_out[k]

                @pl.when(jnp.logical_not(own_slot(k)))
                def _():
                    small(k, dot_out, dot_in, -1, 1).start()

                grads_ref[core, dz, dx] = produced[part]
                keep_produced(k).start()
                active[core, dz, dx] = act[part]
                weighted[core, dz, dx] = produced_grad[part]
                pre_grads[core, dz, dx, :, 0:HALF] = gate_grad[part]
                pre_grads[core, dz, dx, :, HALF:D] = up_grad[part]

        def send_results(g):
            done(prod_hbm.at[0, pl.ds(0, 2)], store_sem.at[g])
            for dx in range(4):
                dz = lax.rem(dx + g, 4)
                for core in range(2):
                    send_slots(
                        prod_hbm,
                        mid_hbm,
                        core,
                        dz,
                        dx,
                        c_send.at[0],
                        c_recv.at[0],
                        c_recv.at[0],
                        -1,
                        load_sem.at[8],
                    )

        send_results(0)

        all_rows = GROUP * CAP

        def quarter_grads(slot, n):
            span = pl.ds(pl.multiple_of(n * 256, 256), 256)
            left = arrived[:, :, :, :, span].reshape(all_rows, 256)
            part = dot(left, pre_grads[...].reshape(all_rows, D), ((0,), (0,))).astype(bf16)
            narrow = pl.ds(pl.multiple_of(n * 128, 128), 128)
            left = active[:, :, :, :, narrow].reshape(all_rows, 128)
            down = dot(left, weighted[...].reshape(all_rows, D), ((0,), (0,))).astype(bf16)
            for h in range(2):
                rows = part[128 * h : 128 * h + 128]
                expert_ref[slot, h, 0:128, :] = rows[:, 0:HALF]
                expert_ref[slot, h, 128:256, :] = rows[:, HALF:D]
                rows = down[64 * h : 64 * h + 64]
                expert_ref[slot, h, 256:320, :] = rows[:, 0:HALF]
                expert_ref[slot, h, 320:384, :] = rows[:, HALF:D]

        quarter_grads(0, opposite)
        for n in range(2):
            relayed(n).start()

        part_sems = part_send, part_recv
        fold_start(parts_out, parts_in, mid, back_recv, posz_ref, posx_ref, part_sems)

        @pl.loop(1, 4)
        def _(slot):
            quarter_grads(slot, lax.rem(y + jnp.where(slot == 1, 1, jnp.where(slot == 2, 3, 0)), 4))

            @pl.when(slot == 1)
            def _():
                fold_end(parts_out, parts_in, part_sems)
                pl.loop(1, 4)(send_results)

        for n in range(2):
            direct(n).start()

        done(dot_in.at[pl.ds(0, GROUP - 1)], small_recv.at[1])

        @pl.loop(0, GROUP)
        def _(k):
            there, dz, dx = k // CHIPS, lax.rem(k // 4, 4), lax.rem(k, 4)
            _, expert = moved(dx, dz, there)
            at = pl.ds(expert, 1)
            dots = as_column(dot_in[k, 0:1, 0:CAP])
            gdot_ref[at, :] = jnp.sum(
                jnp.where(picks(pos_ref[at, :]), dots, 0.0), axis=0, keepdims=True
            )

        hgrad_ref[...] = folded(parts_in, part_sems)
        done(all_slots(outgoing), back_send.at[0])
        done(parts_out.at[pl.ds(0, 3)], part_send.at[0])
        near_done(tok_z, tok_x, first_send)
        far_done(tok_z, tok_x, first_send)
        done(gate_in.at[pl.ds(0, GROUP - 1)], small_send.at[0])
        done(dot_in.at[pl.ds(0, GROUP - 1)], small_send.at[1])

    pl.run_scoped(
        expert_phase,
        pltpu.VMEM((2, 4, 4, CAP, D), bf16),
        pltpu.VMEM((D, HALF), bf16),
        pltpu.VMEM((D, HALF), bf16),
        pltpu.VMEM((HALF, D), bf16),
        pltpu.VMEM((2, 4, 4, CAP, D), bf16),
        pltpu.VMEM((4, tokens, D), bf16),
        pltpu.VMEM((2, 4, 4, CAP, HALF), bf16),
        pltpu.VMEM((2, 4, 4, CAP, D), bf16),
        pltpu.VMEM((2, 4, 4, CAP, D), bf16),
    )

    def finish_phase(w_ref, q_ref, k_ref, v_ref, normed_ref, mixed_ref, hidden_ref, parts_out2, quarter_sum, relay_out, branch_own, mg_t, grad_t, kv_own, kv_out, weight_part, rs_out, y_out, small_out, small_y, gain_out, gain_y):
        loads = [
            pltpu.make_async_copy(source, target, load_sem.at[n])
            for n, (source, target) in enumerate(
                (
                    (w_hbm, w_ref),
                    (mixed_hbm, mixed_ref),
                    (q_hbm, q_ref),
                    (k_hbm, k_ref),
                    (v_hbm, v_ref),
                    (normed_hbm, normed_ref),
                    (hidden_hbm, hidden_ref),
                )
            )
        ]
        for load in loads:
            load.start()

        def weight(first, width):
            return w_ref[:, :, :, :, first : first + width].reshape(D, width)

        def merged(n):
            device = (above, below)[n][0]
            return remote(
                relay_out.at[n], y_in.at[n, n], ex_send.at[4 + n], ex_recv.at[4 + n], device
            )

        def handed(n):
            device = (above, below)[n][0]
            return remote(
                quarter_sum, esum_hbm.at[y], ex_send.at[6 + n], ex_recv.at[6 + n], device
            )

        def sib_keyval(p):
            return to_sibling(3 + p, kv_out.at[p], kv_in.at[p])

        def sib_grads(p, part):
            rows = pl.ds(p * D + part * HALF, HALF)
            return to_sibling(5 + 2 * p + part, grad_t.at[rows], grad_sib.at[rows])

        sib_branch = to_sibling(2, branch_own, branch_sib)

        for n in range(2):
            relayed(n).wait_recv()
            total = relay_in[n].astype(f32) + expert_ref[1 + n, n].astype(f32)
            relay_out[n] = total.astype(bf16)
            merged(n).start()

        gates = gates_ref[...]
        gdot = gdot_ref[...]
        logit_grad = gates * (gdot - jnp.sum(gates * gdot, axis=0, keepdims=True))
        high, rest = split_two(logit_grad)
        router_part = dot(high, routed_ref[...], ((1,), (0,)))
        router_part = router_part + dot(rest, routed_ref[...], ((1,), (0,)))
        routed_grad = dot(high, router_ref[...], ((0,), (0,)))
        routed_grad = routed_grad + dot(rest, router_ref[...], ((0,), (0,)))
        routed_grad = routed_grad + hgrad_ref[...]
        live = (
            r * tokens + lax.broadcasted_iota(jnp.int32, (tokens, 1), 0) < length_ref[0]
        ).astype(f32)
        middle = middle_ref[...]
        scale = lax.rsqrt(jnp.mean(middle * middle, axis=1, keepdims=True) + epsilon)
        rows = middle * scale
        moe_part = jnp.sum(routed_grad * rows, axis=0, keepdims=True)
        scaled = routed_grad * mgain_ref[...]
        inner = jnp.mean(scaled * rows, axis=1, keepdims=True)
        middle_grad = cot_ref[...].astype(f32) * live + scale * (scaled - rows * inner)
        hgrad_ref[...] = middle_grad
        branch_own[...] = middle_grad.astype(bf16)
        sib_branch.start()
        for j in range(8):
            part = slice(128 * j, 128 * j + 128)
            small_out[:, j, :] = router_part[:, part]
            small_out[:, 8 + j, :] = jnp.broadcast_to(moe_part[:, part], (GROUP, 128))

        def tiny(k):
            device, other = step_of(k, 1)
            return remote(small_out.at[other], small_in.at[me], sm_send.at[0], sm_recv.at[0], device)

        @pl.loop(1, GROUP)
        def _(k):
            tiny(k).start()

        small_in[me] = small_out[me]

        loads[0].wait()
        mg_t[...] = dot(weight(2 * D, D), branch_own[...], ((1,), (1,))).astype(bf16)

        mine = pl.ds(pl.multiple_of(r * HALF, HALF), HALF)

        def columns(p):
            return pl.ds(p * D, HALF), pl.ds(p * D + HALF, HALF)

        def first_step(p, d):
            left, right = columns(p)
            return (
                remote(
                    weight_part.at[lax.rem(z + d, 4), :, :, left],
                    rs_in.at[d, :, :, left],
                    rs_send.at[p],
                    rs_recv.at[p],
                    moved(0, d, r)[0],
                ),
                remote(
                    weight_part.at[:, lax.rem(x + d, 4), :, right],
                    rs_in.at[d, :, :, right],
                    rs_send.at[p],
                    rs_recv.at[p],
                    moved(d, 0, r)[0],
                ),
            )

        def second_step(p, d):
            left, right = columns(p)
            return (
                remote(
                    rs_out.at[lax.rem(x + d, 4), :, left],
                    rs_in2.at[d, :, left],
                    rs_send2.at[p],
                    rs_recv2.at[p],
                    moved(d, 0, r)[0],
                ),
                remote(
                    rs_out.at[lax.rem(z + d, 4), :, right],
                    rs_in2.at[d, :, right],
                    rs_send2.at[p],
                    rs_recv2.at[p],
                    moved(0, d, r)[0],
                ),
            )

        def across(p, n):
            cols = pl.ds(p * D, D)
            return remote(
                y_out.at[:, cols],
                y_parts.at[y, :, cols],
                ys_send.at[p],
                ys_recv.at[p],
                plane_shift(n)[0],
            )

        def sum_first(p, total):
            weight_part[:, :, :, p * D : p * D + D] = total.astype(bf16).reshape(4, 4, 32, D)

            @pl.loop(1, 4)
            def _(d):
                for copy in first_step(p, d):
                    copy.start()

        def sum_second(p):
            left, right = columns(p)

            done(rs_in.at[pl.ds(1, 3), :, :, pl.ds(p * D, D)], rs_recv.at[p])

            total = weight_part[z, :, :, left].astype(f32)
            other = weight_part[:, x, :, right].astype(f32)
            for d in range(1, 4):
                total = total + rs_in[d, :, :, left].astype(f32)
                other = other + rs_in[d, :, :, right].astype(f32)
            rs_out[:, :, left] = total.astype(bf16)
            rs_out[:, :, right] = other.astype(bf16)

            @pl.loop(1, 4)
            def _(d):
                for copy in second_step(p, d):
                    copy.start()

        def sum_third(p):
            left, right = columns(p)

            done(rs_in2.at[pl.ds(1, 3), :, pl.ds(p * D, D)], rs_recv2.at[p])

            total = rs_out[x, :, left].astype(f32)
            other = rs_out[z, :, right].astype(f32)
            for d in range(1, 4):
                total = total + rs_in2[d, :, left].astype(f32)
                other = other + rs_in2[d, :, right].astype(f32)
            y_out[:, left] = total.astype(bf16)
            y_out[:, right] = other.astype(bf16)
            y_parts[y, :, left] = total.astype(bf16)
            y_parts[y, :, right] = other.astype(bf16)
            for n in range(1, PLANES):
                across(p, n).start()

        sib_mixed.wait_recv()
        sib_branch.wait_recv()
        loads[1].wait()
        total = dot(mixed_ref[:, mine], branch_own[...], ((0,), (0,)))
        sum_first(2, total + dot(mixed_sib[...], branch_sib[...], ((0,), (0,))))

        key_live = lax.broadcasted_iota(jnp.int32, (2 * tokens, 1), 0) < length_ref[0]
        score_scale = HEAD ** (-0.5)
        here = pl.ds(pl.multiple_of(r * tokens, tokens), tokens)
        cosine, sine = cos_ref[:, here], sin_ref[:, here]
        first_core = r == 0

        def key_head(p, i):
            g = 4 * p + i
            head = pl.ds(pl.multiple_of(g * HEAD, HEAD), HEAD)
            keys, values = k_ref[head, :], v_ref[head, :]
            key_sum, value_sum = None, None
            for j in range(2):
                at = pl.ds(pl.multiple_of((2 * g + j) * HEAD, HEAD), HEAD)
                query, mixed_grad = q_ref[at, :], mg_t[at, :]
                scores = dot(keys, query, ((0,), (0,))) * score_scale
                scores = jnp.where(key_live, scores, NEG)
                probs = jnp.exp(scores - lse_ref[pl.ds(2 * g + j, 1), :])
                prob_grad = dot(values, mixed_grad, ((0,), (0,)))
                value_part = dot(mixed_grad, probs.astype(bf16), ((1,), (1,)))
                inner = jnp.sum(probs * prob_grad, axis=0, keepdims=True)
                score_grad = (probs * (prob_grad - inner)).astype(bf16)
                key_part = dot(query, score_grad, ((1,), (1,)))
                query_grad = dot(keys, score_grad, ((1,), (0,))) * score_scale
                to = pl.ds(pl.multiple_of(p * D + (2 * i + j) * HEAD, HEAD), HEAD)
                grad_t[to, :] = turned_back(query_grad, cosine, sine).astype(bf16)
                key_sum = key_part if key_sum is None else key_sum + key_part
                value_sum = value_part if value_sum is None else value_sum + value_part
            key_sum = key_sum * score_scale
            for n, part in enumerate((key_sum, value_sum)):
                to = pl.ds(pl.multiple_of(256 * n + i * HEAD, HEAD), HEAD)
                kv_own[p, to, :] = jnp.where(first_core, part[:, :tokens], part[:, tokens:])
                away = jnp.where(first_core, part[:, tokens:], part[:, :tokens])
                kv_out[p, to, :] = away.astype(bf16)

        def heads(p, first, last):
            @pl.loop(first, last)
            def _(i):
                key_head(p, i)

        def whole_keyval(p):
            sib_keyval(p).wait_recv()
            for i in range(4):
                rows = slice(HEAD * i, HEAD * i + HEAD)
                total = kv_own[p, rows, :] + kv_in[p, rows, :].astype(f32)
                to = p * D + HALF + HEAD * i
                grad_t[to : to + HEAD, :] = turned_back(total, cosine, sine).astype(bf16)
            total = kv_own[p, 256:512, :] + kv_in[p, 256:512, :].astype(f32)
            grad_t[p * D + HALF + 256 : p * D + D, :] = total.astype(bf16)
            sib_grads(p, 1).start()

        def projections(p):
            rows = slice(p * D, p * D + D)
            for part in range(2):
                sib_grads(p, part).wait_recv()
            total = dot(normed_ref[:, mine], grad_t[rows, :], ((0,), (1,)))
            sum_first(p, total + dot(normed_sib[...], grad_sib[rows, :], ((0,), (1,))))

        def inputs_part(p):
            return dot(grad_t[p * D : p * D + D, :], weight(p * D, D), ((0,), (1,)))

        for load in loads[2:5]:
            load.wait()
        heads(0, 0, 4)
        sib_keyval(0).start()
        sib_grads(0, 0).start()

        heads(1, 0, 4)
        sib_keyval(1).start()
        sib_grads(1, 0).start()
        for n in range(2):
            direct(n).wait_recv()
            merged(n).wait_recv()
        for n in range(2):
            total = expert_ref[3, n].astype(f32) + (y_in[0, n].astype(f32) + y_in[1, n].astype(f32))
            quarter_sum[n] = total.astype(bf16)
        quarter_out = pltpu.make_async_copy(quarter_sum, esum_hbm.at[y], load_sem.at[9])
        quarter_out.start()
        for n in range(2):
            handed(n).start()

        whole_keyval(0)
        for load in loads[5:]:
            load.wait()
        sib_normed.wait_recv()
        projections(0)
        done(all_slots(mid_hbm), c_recv.at[0])
        done(mid_hbm.at[0, 0], load_sem.at[8])
        results_in = pltpu.make_async_copy(mid_hbm, mid, load_sem.at[10])
        results_in.start()
        whole_keyval(1)
        normed_grad = inputs_part(0)
        projections(1)
        normed_grad = normed_grad + inputs_part(1)

        inputs = hidden_ref[...].astype(f32)
        scale = lax.rsqrt(jnp.mean(inputs * inputs, axis=1, keepdims=True) + epsilon)
        rows = inputs * scale
        attn_part = jnp.sum(normed_grad * rows, axis=0, keepdims=True)
        for j in range(8):
            gain_out[j : j + 1, :] = attn_part[:, 128 * j : 128 * j + 128]

        def gain(k):
            device, _ = step_of(k, 1)
            return remote(gain_out, gain_in.at[me], sm_send.at[3], sm_recv.at[3], device)

        @pl.loop(1, GROUP)
        def _(k):
            gain(k).start()

        gain_in[me] = gain_out[...]
        scaled = normed_grad * again_ref[...]
        inner = jnp.mean(scaled * rows, axis=1, keepdims=True)
        hgrad_ref[...] += scale * (scaled - rows * inner)

        sum_second(2)
        done(small_in.at[pl.ds(0, GROUP - 1)], sm_recv.at[0])

        def small_across(n):
            device, _ = plane_shift(n)
            return remote(
                small_y, small_y_in.at[y], sm_send.at[1], sm_recv.at[1], device
            )

        small_y[...] = jnp.sum(small_in[...], axis=0)
        small_y_in[y] = small_y[...]
        for n in range(1, PLANES):
            small_across(n).start()

        sum_second(0)
        results_in.wait()
        part_sems = part_send2, part_recv2
        fold_start(parts_out2, parts_in2, mid, None, posz_ref, posx_ref, part_sems)
        for n in range(2):
            handed(n).wait_recv()
            passed_on(n).start()

        done(small_y_in.at[pl.ds(0, 3)], sm_recv.at[1])
        totals = small_y_in[0] + small_y_in[1] + small_y_in[2] + small_y_in[3]
        mgain_out[...] = totals[8:16]
        router_all[me] = totals[0:8]

        def router_row(k):
            device, _ = step_of(k, 1)
            return remote(
                router_all.at[me], router_all.at[me], sm_send.at[2], sm_recv.at[2], device
            )

        @pl.loop(1, GROUP)
        def _(k):
            router_row(k).start()

        sum_second(1)
        fold_end(parts_out2, parts_in2, part_sems)
        sum_third(2)
        sum_third(0)

        done(gain_in.at[pl.ds(0, GROUP - 1)], sm_recv.at[3])

        gain_y[...] = jnp.sum(gain_in[...], axis=0)
        gain_y_in[y] = gain_y[...]

        def gain_across(n):
            device, _ = plane_shift(n)
            return remote(gain_y, gain_y_in.at[y], sm_send.at[4], sm_recv.at[4], device)

        for n in range(1, PLANES):
            gain_across(n).start()

        sum_third(1)

        mixture = folded(parts_in2, part_sems)
        hout_ref[...] = ((middle_ref[...] + mixture) * live).astype(bf16)

        done(gain_y_in.at[pl.ds(0, 3)], sm_recv.at[4])
        again_out[...] = (gain_y_in[0] + gain_y_in[1]) + (gain_y_in[2] + gain_y_in[3])

        done(router_all.at[pl.ds(0, GROUP - 1)], sm_recv.at[2])

        router_out[...] = router_all[...]

        done(all_slots(mid_hbm), c_send.at[0])
        done(parts_out2.at[pl.ds(0, 3)], part_send2.at[0])
        done(small_in.at[pl.ds(0, GROUP - 1)], sm_send.at[0])
        done(small_y_in.at[pl.ds(0, 3)], sm_send.at[1])
        done(router_all.at[pl.ds(0, GROUP - 1)], sm_send.at[2])
        done(gain_in.at[pl.ds(0, GROUP - 1)], sm_send.at[3])
        done(gain_y_in.at[pl.ds(0, 3)], sm_send.at[4])
        for p in range(3):
            done(rs_in.at[pl.ds(1, 3), :, :, pl.ds(p * D, D)], rs_send.at[p])
            done(rs_in2.at[pl.ds(1, 3), :, pl.ds(p * D, D)], rs_send2.at[p])
            done(y_parts.at[pl.ds(0, 3), :, pl.ds(p * D, D)], ys_recv.at[p])
            done(y_parts.at[pl.ds(0, 3), :, pl.ds(p * D, D)], ys_send.at[p])
        for n in range(2):
            for copy in (relayed(n), direct(n), merged(n), handed(n), passed_on(n)):
                copy.wait_send()
        for copy in (sib_normed, sib_mixed, sib_branch):
            copy.wait_send()
        for p in range(2):
            sib_keyval(p).wait_send()
            for part in range(2):
                sib_grads(p, part).wait_send()
        for n in range(2):
            passed_on(n).wait_recv()
        quarter_out.wait()
        own_out[...] = (y_parts[0].astype(f32) + y_parts[1].astype(f32)) + (
            y_parts[2].astype(f32) + y_parts[3].astype(f32)
        )

    pl.run_scoped(
        finish_phase,
        pltpu.VMEM((2, 4, 4, 32, 3 * D), bf16),
        pltpu.VMEM((D, tokens), bf16),
        pltpu.VMEM((HALF, 2 * tokens), bf16),
        pltpu.VMEM((HALF, 2 * tokens), bf16),
        pltpu.VMEM((tokens, D), bf16),
        pltpu.VMEM((tokens, D), bf16),
        pltpu.VMEM((tokens, D), bf16),
        pltpu.VMEM((4, tokens, D), bf16),
        pltpu.VMEM((2, 384, HALF), bf16),
        pltpu.VMEM((2, 384, HALF), bf16),
        pltpu.VMEM((tokens, D), bf16),
        pltpu.VMEM((D, tokens), bf16),
        pltpu.VMEM((2 * D, tokens), bf16),
        pltpu.VMEM((2, HALF, tokens), f32),
        pltpu.VMEM((2, HALF, tokens), bf16),
        pltpu.VMEM((4, 4, 32, 3 * D), bf16),
        pltpu.VMEM((4, 32, 3 * D), bf16),
        pltpu.VMEM((32, 3 * D), bf16),
        pltpu.VMEM((GROUP, 16, 128), f32),
        pltpu.VMEM((16, 128), f32),
        pltpu.VMEM((8, 128), f32),
        pltpu.VMEM((8, 128), f32),
    )


def rest(length, *arrays):
    tokens = TOKENS
    f32, bf16 = jnp.float32, jnp.bfloat16
    vmem = pl.BlockSpec(memory_space=pltpu.VMEM)
    hbm = pl.BlockSpec(memory_space=pl.ANY)
    shape = jax.ShapeDtypeStruct
    sems = pltpu.SemaphoreType.DMA
    scratch = [
        pltpu.VMEM((4, tokens, HALF), bf16),
        pltpu.VMEM((4, tokens, HALF), bf16),
        pltpu.VMEM((2, 4, 4, CAP, D), bf16),
        pltpu.VMEM((2, 4, 4, CAP, D), bf16),
        pltpu.VMEM((4, tokens, D), bf16),
        pltpu.VMEM((4, tokens, D), bf16),
        pltpu.VMEM((GROUP, 8, 128), f32),
        pltpu.VMEM((GROUP, 8, 128), f32),
        pltpu.VMEM((GROUP, 8, 128), f32),
        pltpu.VMEM((GROUP, 8, 128), f32),
        pltpu.VMEM((EXPERTS, tokens), f32),
        pltpu.VMEM((4, 2, 384, HALF), bf16),
        pltpu.VMEM((2, 384, HALF), bf16),
        pltpu.VMEM((2, 2, 384, HALF), bf16),
        pltpu.VMEM((tokens, D), bf16),
        pltpu.VMEM((tokens, HALF), bf16),
        pltpu.VMEM((tokens, HALF), bf16),
        pltpu.VMEM((2 * D, tokens), bf16),
        pltpu.VMEM((2, HALF, tokens), bf16),
        pltpu.VMEM((4, 4, 32, 3 * D), bf16),
        pltpu.VMEM((4, 32, 3 * D), bf16),
        pltpu.VMEM((PLANES, 32, 3 * D), bf16),
        pltpu.VMEM((GROUP, 16, 128), f32),
        pltpu.VMEM((PLANES, 16, 128), f32),
        pltpu.VMEM((GROUP, 8, 128), f32),
        pltpu.VMEM((PLANES, 8, 128), f32),
        pltpu.VMEM((GROUP, 8, 128), f32),
    ]
    for count in (11, 4, 4, 4, 4, 8, 1, 8, 1, 3, 2, 2, 1, 1, 1, 3, 10, 10, 9, 9, 3, 3, 3, 3, 3, 3, 5, 5):
        scratch += [sems((count,))]
    in_specs = [pl.BlockSpec(memory_space=pltpu.SMEM)] + [vmem] * len(arrays)
    for n in (6, 7, 8, 9, 13, 16, 17, 18, 19, 20, 21):
        in_specs[n] = hbm
    return pl.pallas_call(
        rest_kernel,
        out_shape=(
            shape((tokens, D), bf16),
            shape((tokens, D), f32),
            shape((8, 128), f32),
            shape((8, 128), f32),
            shape((GROUP, 8, 128), f32),
            shape((32, 3 * D), f32),
            shape((4, 2, 384, HALF), bf16),
            shape((2, 4, 4, CAP, D), bf16),
            shape((2, 4, 4, CAP, D), bf16),
        ),
        in_specs=in_specs,
        out_specs=[vmem] * 6 + [hbm] * 3,
        scratch_shapes=scratch,
        compiler_params=pltpu.CompilerParams(
            collective_id=2, has_side_effects=True, vmem_limit_bytes=62 << 20
        ),
        name="rest",
    )(length, *arrays)[:7]


def spread_kernel(
    hout_ref,
    hgrad_ref,
    own_ref,
    esum_ref,
    router_ref,
    again_ref,
    mgain_ref,
    hout_out,
    hgrad_out,
    q_out,
    k_out,
    v_out,
    o_out,
    gate_out,
    up_out,
    down_out,
    router_out,
    again_out,
    mgain_out,
):
    f32 = jnp.float32
    hout_out[...] = hout_ref[...]
    hgrad_out[...] = hgrad_ref[...]
    for p in range(2):
        q_out[:, p * HALF : p * HALF + HALF] = own_ref[:, p * D : p * D + HALF]
        k_out[:, p * 256 : p * 256 + 256] = own_ref[:, p * D + HALF : p * D + 768]
        v_out[:, p * 256 : p * 256 + 256] = own_ref[:, p * D + 768 : p * D + D]
    o_out[...] = own_ref[:, 2 * D : 3 * D]
    for h in range(2):
        gate_out[0, 128 * h : 128 * h + 128, :] = esum_ref[0, h, 0:128, :].astype(f32)
        up_out[0, 128 * h : 128 * h + 128, :] = esum_ref[0, h, 128:256, :].astype(f32)
        down_out[0, 64 * h : 64 * h + 64, 0:HALF] = esum_ref[0, h, 256:320, :].astype(f32)
        down_out[0, 64 * h : 64 * h + 64, HALF:D] = esum_ref[0, h, 320:384, :].astype(f32)
    for j in range(8):
        router_out[:, 128 * j : 128 * j + 128] = router_ref[:, j, :]
    again_out[...] = again_ref[...]
    mgain_out[...] = mgain_ref[...]


def spread_out(*arrays):
    f32, bf16 = jnp.float32, jnp.bfloat16
    shape = jax.ShapeDtypeStruct

    def whole(*dims):
        return pl.BlockSpec(dims, lambda i: (0,) * len(dims))

    def rows(count, width):
        return pl.BlockSpec((count, width), lambda i: (i, 0))

    def expert_rows(count, width):
        return pl.BlockSpec((1, count, width), lambda i: (0, i, 0))

    return pl.pallas_call(
        spread_kernel,
        grid=(4,),
        out_shape=(
            shape((TOKENS, D), bf16),
            shape((TOKENS, D), f32),
            shape((32, D), f32),
            shape((32, HALF), f32),
            shape((32, HALF), f32),
            shape((32, D), f32),
            shape((1, D, HALF), f32),
            shape((1, D, HALF), f32),
            shape((1, HALF, D), f32),
            shape((EXPERTS, D), f32),
            shape((8, 128), f32),
            shape((8, 128), f32),
        ),
        in_specs=[
            rows(64, D),
            rows(64, D),
            whole(32, 3 * D),
            pl.BlockSpec((1, 2, 384, HALF), lambda i: (i, 0, 0, 0)),
            whole(GROUP, 8, 128),
            whole(8, 128),
            whole(8, 128),
        ],
        out_specs=[
            rows(64, D),
            rows(64, D),
            whole(32, D),
            whole(32, HALF),
            whole(32, HALF),
            whole(32, D),
            expert_rows(256, HALF),
            expert_rows(256, HALF),
            expert_rows(128, D),
            whole(EXPERTS, D),
            whole(8, 128),
            whole(8, 128),
        ],
        name="spread_out",
    )(*arrays)


def on_device(
    hidden_in,
    cotangent,
    lengths,
    routes,
    priority,
    attn_gain,
    query_weight,
    key_weight,
    value_weight,
    output_weight,
    moe_gain,
    router,
    gate_weight,
    up_weight,
    down_weight,
):
    tok_count = hidden_in.shape[0]
    half_dim = HEAD // 2
    frequency = rotary_base ** (-np.arange(half_dim, dtype=np.float32) / half_dim)
    positions = np.arange(2 * tok_count, dtype=np.float32)
    angles = frequency.astype(np.float32)[:, None] * positions[None, :]
    cosine, sine = jnp.asarray(np.cos(angles)), jnp.asarray(np.sin(angles))
    router_t = router.T
    (
        weights,
        normed,
        queries,
        keys,
        values,
        log_total,
        mixed_rows,
        middle,
        routed,
        gates,
        pos,
        posz,
        posx,
        arrived_grad,
    ) = front(
        lengths,
        hidden_in,
        cotangent,
        routes.T,
        priority,
        attn_gain[None],
        moe_gain[None],
        query_weight,
        key_weight,
        value_weight,
        output_weight,
        router_t,
        cosine,
        sine,
    )
    summed = rest(
        lengths,
        routed,
        pos,
        posz,
        posx,
        gates,
        arrived_grad,
        gate_weight[0],
        up_weight[0],
        down_weight[0],
        router_t,
        middle,
        cotangent,
        hidden_in,
        attn_gain[None],
        moe_gain[None],
        normed,
        mixed_rows,
        weights,
        queries,
        keys,
        values,
        log_total,
        cosine,
        sine,
    )
    hidden_out, hidden_grad, attn_gain_sum, moe_gain_sum, router_sum, own_rows, expert_sum = summed
    (
        hidden_out,
        hidden_grad,
        query_grad,
        key_grad,
        value_grad,
        output_grad,
        gate_grad,
        up_grad,
        down_grad,
        router_grad,
        attn_gain_sum,
        moe_gain_sum,
    ) = spread_out(
        hidden_out, hidden_grad, own_rows, expert_sum, router_sum, attn_gain_sum, moe_gain_sum
    )
    return (
        hidden_out,
        hidden_grad,
        attn_gain_sum.reshape(D),
        query_grad,
        key_grad,
        value_grad,
        output_grad,
        moe_gain_sum.reshape(D),
        router_grad.T,
        gate_grad,
        up_grad,
        down_grad,
    )


def solution(mesh):
    return jax.shard_map(
        on_device,
        mesh=mesh,
        in_specs=(
            P(("dp", "col", "row"), None),
            P(("dp", "col", "row"), None),
            P(("dp", "col")),
            P(("dp", "col", "row"), None),
            P(("dp", "col", "row"), None),
            P(),
            P(("row", "col"), None),
            P(("row", "col"), None),
            P(("row", "col"), None),
            P(("row", "col"), None),
            P(),
            P(),
            P(("row", "col"), None, None),
            P(("row", "col"), None, None),
            P(("row", "col"), None, None),
        ),
        out_specs=(
            P(("dp", "col", "row"), None),
            P(("dp", "col", "row"), None),
            P(),
            P(("row", "col"), None),
            P(("row", "col"), None),
            P(("row", "col"), None),
            P(("row", "col"), None),
            P(),
            P(),
            P(("row", "col"), None, None),
            P(("row", "col"), None, None),
            P(("row", "col"), None, None),
        ),
        check_vma=False,
    )
```

```python
import jax
import jax.numpy as jnp
import numpy as np
from jax import lax
from jax.experimental import pallas as pl
from jax.experimental.pallas import tpu as pltpu
from jax.sharding import PartitionSpec as P

D = 1024
HEADS = 16
HEAD = 64
KV_HEADS = 8
EXPERTS = 32
TOP = 8
CAP = 64


epsilon = 1e-05
rotary_base = 10000.0


MESH = pl.DeviceIdType.MESH
GROUP = 32
PLANES = 4
CHIPS = 16
HALF = D // 2
TOKENS = 256
NEG = -1000000000.0


def place():
    col = lax.axis_index("col")
    return lax.axis_index("dp"), lax.axis_index("row"), lax.rem(col, 4), col // 4


def moved(dx, dz, core):
    y, r, x, z = place()
    col = lax.rem(z + dz + 4, 4) * 4 + lax.rem(x + dx + 4, 4)
    return (y, core, col), core * CHIPS + col


def plane_shift(n):
    y, r, x, z = place()
    other = lax.rem(y + n, PLANES)
    return (other, r, z * 4 + x), other


def step_of(k, sign):
    y, r, x, z = place()
    return moved(sign * lax.rem(k, 4), sign * lax.rem(k // 4, 4), lax.rem(r + k // CHIPS, 2))


def remote(src, dst, send_sem, recv_sem, device):
    return pltpu.make_async_remote_copy(
        src_ref=src,
        dst_ref=dst,
        send_sem=send_sem,
        recv_sem=recv_sem,
        device_id=device,
        device_id_type=MESH,
    )


def done(ref, sem):
    pltpu.make_async_copy(ref, ref, sem).wait()


def meet(plane, planes):
    barrier = pltpu.get_barrier_semaphore()
    y, r, x, z = place()

    def greet(device):
        pl.semaphore_signal(barrier, inc=1, device_id=device, device_id_type=MESH)

    if plane:

        @pl.loop(1, GROUP)
        def _(k):
            greet(step_of(k, 1)[0])

        count = GROUP - 1
    else:
        for core in range(2):

            @pl.loop(1, 4)
            def _(d):
                greet(moved(d, 0, core)[0])
                greet(moved(0, d, core)[0])

        greet(moved(0, 0, 1 - r)[0])
        count = 13
    if planes:
        for n in range(1, PLANES):
            greet(plane_shift(n)[0])
        count += PLANES - 1
    pl.semaphore_wait(barrier, count)


def eye(n):
    return lax.broadcasted_iota(jnp.int32, (n, n), 0) == lax.broadcasted_iota(
        jnp.int32, (n, n), 1
    )


def as_row(column):
    return jnp.sum(jnp.where(eye(column.shape[0]), column, 0.0), axis=0, keepdims=True)


def as_column(row_vec):
    return jnp.sum(jnp.where(eye(row_vec.shape[1]), row_vec, 0.0), axis=1, keepdims=True)


def dot(a, b, dims):
    return lax.dot_general(a, b, (dims, ((), ())), preferred_element_type=jnp.float32)


def split_two(values):
    high = values.astype(jnp.bfloat16)
    return high, (values - high.astype(jnp.float32)).astype(jnp.bfloat16)


def picks(positions):
    slots = lax.broadcasted_iota(jnp.int32, (CAP, positions.shape[1]), 0)
    return slots == positions


def as_hot(mask):
    return mask.astype(jnp.float32).astype(jnp.bfloat16)


LEFT = pl.ds(0, HALF)
RIGHT = pl.ds(HALF, HALF)


def spread(d, source, tok_z, tok_x, send_sem, recv_sem):
    y, r, x, z = place()
    return (
        remote(
            source.at[:, LEFT], tok_z.at[d], send_sem.at[0], recv_sem.at[0], moved(0, d, r)[0]
        ),
        remote(
            source.at[:, RIGHT], tok_x.at[d], send_sem.at[1], recv_sem.at[1], moved(d, 0, r)[0]
        ),
    )


def pass_on(tok_z, tok_x, send_sem, recv_sem):
    y, r, x, z = place()
    copies = []
    for n, (d, sign) in enumerate(((1, 1), (3, -1))):
        rows = pl.ds(n * 128, 128)
        for tok, at, device in (
            (tok_z, 2, moved(0, sign, r)[0]),
            (tok_x, 3, moved(sign, 0, r)[0]),
        ):
            copies.append(
                remote(
                    tok.at[d, rows], tok.at[2, rows], send_sem.at[at], recv_sem.at[at], device
                )
            )
    return copies


def near_done(tok_z, tok_x, sem):
    done(tok_z.at[pl.ds(0, 2)], sem.at[0])
    done(tok_x.at[pl.ds(0, 2)], sem.at[1])


def far_done(tok_z, tok_x, sem):
    done(tok_z.at[2], sem.at[2])
    done(tok_x.at[2], sem.at[3])


def is_local(core, offset):
    y, r, x, z = place()
    return (core == r) & (offset == 0)


def send_slots(
    out,
    into,
    there,
    dz,
    dx,
    send_sem,
    recv_left,
    recv_right,
    sign,
    local_sem=None,
    halves=(True, True),
):
    y, r, x, z = place()

    def one(cols, offset, device, recv_sem):
        source, target = out.at[there, dz, dx, :, cols], into.at[r, dz, dx, :, cols]

        @pl.when(jnp.logical_not(is_local(there, offset)))
        def _():
            remote(source, target, send_sem, recv_sem, device).start()

        @pl.when(is_local(there, offset))
        def _():
            if local_sem is None:
                target[...] = source[...]
            else:
                pltpu.make_async_copy(source, target, local_sem).start()

    if halves[0]:
        one(LEFT, dx, moved(sign * dx, 0, there)[0], recv_left)
    if halves[1]:
        one(RIGHT, dz, moved(0, sign * dz, there)[0], recv_right)


def all_slots(ref):
    return ref.at[:, :, :, :, pl.ds(0, 896)]


def line_rows(line, d, axis):
    y, r, x, z = place()
    own = x if axis == 0 else z
    return [
        line[d, pl.ds(core * 4 + lax.rem(own + i, 4), 1), :] for core in range(2) for i in range(4)
    ]


def line_hot(line, d, axis):
    return as_hot(jnp.concatenate([picks(p) for p in line_rows(line, d, axis)], axis=0))


def add_up(mid, line, d, axis):
    if axis == 0:
        rows = mid[:, d, :, :, 0:HALF]
    else:
        rows = mid[:, :, d, :, HALF:D]
    return dot(line_hot(line, d, axis), rows.reshape(8 * CAP, HALF), ((0,), (0,))).astype(
        jnp.bfloat16
    )


def part_copy(d, rows, axis, sign, out, into, send_sem, recv_sem):
    y, r, x, z = place()
    cols = (LEFT, RIGHT)[axis]
    device = moved(sign * axis, sign * (1 - axis), r)[0]
    part = pl.ds(rows, 128)
    return remote(out.at[d, part, cols], into.at[d, part, cols], send_sem, recv_sem, device)


def fold_start(out, into, mid, slot_recv, posz_ref, posx_ref, sems):
    send_sem, recv_sem = sems
    for d in (2, 0, 1, 3):
        for axis, pos in enumerate((posz_ref, posx_ref)):
            if slot_recv is not None:
                done(mid.at[0, 0, :, :, pl.ds(0, 896)], slot_recv.at[4 * axis + d])
            total = add_up(mid, pos, d, axis)
            cols = slice(axis * HALF, axis * HALF + HALF)
            if d == 0:
                into[0, :, cols] = total
                continue
            out[d, :, cols] = total
            if d == 2:
                for rows, sign in ((0, -1), (128, 1)):
                    args = rows, axis, sign, out, into, send_sem.at[0], recv_sem.at[axis]
                    part_copy(2, *args).start()
            else:
                rows, sign = (128, -1) if d == 1 else (0, 1)
                args = rows, axis, sign, out, into, send_sem.at[0], recv_sem.at[2]
                part_copy(d, *args).start()


def fold_end(out, into, sems):
    send_sem, recv_sem = sems
    for axis in range(2):
        cols = slice(axis * HALF, axis * HALF + HALF)
        done(into.at[2, :, (LEFT, RIGHT)[axis]], recv_sem.at[axis])
        for d, rows, sign in ((1, 0, -1), (3, 128, 1)):
            part = slice(rows, rows + 128)
            total = out[d, part, cols].astype(jnp.float32) + into[2, part, cols].astype(jnp.float32)
            out[d, part, cols] = total.astype(jnp.bfloat16)
            args = rows, axis, sign, out, into, send_sem.at[0], recv_sem.at[2]
            part_copy(d, *args).start()


def folded(into, sems):
    done(into.at[pl.ds(0, 2)], sems[1].at[2])
    f32 = jnp.float32
    return into[0].astype(f32) + (into[1].astype(f32) + into[3].astype(f32))


def front_kernel(
    length_ref,
    hidden_ref,
    cot_ref,
    routes_ref,
    prio_ref,
    again_ref,
    mgain_ref,
    wq_ref,
    wk_ref,
    wv_ref,
    wo_ref,
    router_ref,
    cos_ref,
    sin_ref,
    w_hbm,
    normed_ref,
    q_ref,
    k_ref,
    v_ref,
    lse_ref,
    mixed_ref,
    middle_ref,
    routed_ref,
    gates_ref,
    pos_ref,
    posz_ref,
    posx_ref,
    grads_ref,
    w_ref,
    mixed_t,
    posz_out,
    posx_out,
    tok_z,
    tok_x,
    outgoing,
    store_sem,
    w_send,
    w_recv,
    o_send,
    o_recv,
    core_send,
    core_recv,
    kv_send,
    kv_recv,
    first_send,
    first_recv,
    slot_send,
    slot_recv,
    pos_send,
    pos_recv,
):
    y, r, x, z = place()
    f32, bf16 = jnp.float32, jnp.bfloat16
    sibling = moved(0, 0, 1 - r)[0]
    meet(False, True)

    w_ref[r, z, x, :, 0:HALF] = wq_ref[:, 0:HALF]
    w_ref[r, z, x, :, HALF:768] = wk_ref[:, 0:256]
    w_ref[r, z, x, :, 768:D] = wv_ref[:, 0:256]

    @pl.when(y == 0)
    def _():
        w_ref[r, z, x, :, D : D + HALF] = wq_ref[:, HALF:D]

    @pl.when(y == 1)
    def _():
        w_ref[r, z, x, :, D + HALF : D + 768] = wk_ref[:, 256:HALF]
        w_ref[r, z, x, :, D + 768 : 2 * D] = wv_ref[:, 256:HALF]

    @pl.when(y > 1)
    def _():
        own = pl.ds(pl.multiple_of(HALF * (y - 2), HALF), HALF)
        w_ref[r, z, x, :, pl.ds(pl.multiple_of(D + HALF * y, HALF), HALF)] = wo_ref[:, own]

    front, rear = pl.ds(0, HALF), pl.ds(HALF, HALF)

    def quarter(plane, part=None):
        if part is None:
            return pl.ds(pl.multiple_of(D + HALF * plane, HALF), HALF)
        return pl.ds(pl.multiple_of(D + HALF * plane + 256 * part, 256), 256)

    def line_step(d):
        mine_q, mine_o = w_ref.at[r, z, x, :, front], w_ref.at[r, z, x, :, rear]
        return (
            remote(mine_q, mine_q, w_send.at[0], w_recv.at[d], moved(0, d, r)[0]),
            remote(mine_o, mine_o, w_send.at[0], w_recv.at[4 + d], moved(d, 0, r)[0]),
        )

    def cross_step(e, d):
        from_z = w_ref.at[r, lax.rem(z - e + 4, 4), x, :, front]
        from_x = w_ref.at[r, z, lax.rem(x - e + 4, 4), :, rear]
        return (
            remote(from_z, from_z, w_send.at[1], w_recv.at[8 + d], moved(d, 0, r)[0]),
            remote(from_x, from_x, w_send.at[1], w_recv.at[8 + d], moved(0, d, r)[0]),
        )

    def later_line(d):
        left, right = w_ref.at[r, z, x, :, quarter(y, 0)], w_ref.at[r, z, x, :, quarter(y, 1)]
        return (
            remote(left, left, o_send.at[0], o_recv.at[0], moved(0, d, r)[0]),
            remote(right, right, o_send.at[0], o_recv.at[0], moved(d, 0, r)[0]),
        )

    def later_cross(d):
        left, right = w_ref.at[r, :, x, :, quarter(y, 0)], w_ref.at[r, z, :, :, quarter(y, 1)]
        return (
            remote(left, left, o_send.at[1], o_recv.at[1], moved(d, 0, r)[0]),
            remote(right, right, o_send.at[1], o_recv.at[1], moved(0, d, r)[0]),
        )

    def later_plane(n):
        own = w_ref.at[r, :, :, :, quarter(y)]
        return remote(own, own, o_send.at[2], o_recv.at[2], plane_shift(n)[0])

    def later_relay(n):
        device, came_from = plane_shift(1 + 2 * n)[0], plane_shift(3 - 2 * n)[1]
        part = w_ref.at[r, :, :, :, quarter(came_from, n)]
        return remote(part, part, o_send.at[4], o_recv.at[4], device)

    def later_core(n):
        part = w_ref.at[r, :, :, :, quarter(plane_shift(n)[1])]
        return remote(part, part, o_send.at[3], o_recv.at[3], sibling)

    def some(rows, width):
        return w_ref.at[0, pl.ds(0, rows), :, :, pl.ds(0, width)]

    def core_step(d):
        from_x = w_ref.at[r, :, lax.rem(x - d + 4, 4), :, front]
        from_z = w_ref.at[r, lax.rem(z - d + 4, 4), :, :, rear]
        return (
            remote(from_x, from_x, core_send.at[0], core_recv.at[0], sibling),
            remote(from_z, from_z, core_send.at[0], core_recv.at[0], sibling),
        )

    @pl.loop(1, 4)
    def _(d):
        for copy in line_step(d):
            copy.start()

    @pl.loop(1, 4)
    def _(d):
        for copy in cross_step(0, d):
            copy.start()
        for copy in later_line(d):
            copy.start()

    tokens = hidden_ref.shape[0]
    experts_iota = lax.broadcasted_iota(jnp.int32, (EXPERTS, tokens), 0).astype(f32)
    live = r * tokens + lax.broadcasted_iota(jnp.int32, (1, tokens), 1) < length_ref[0]
    routed_to = jnp.zeros((EXPERTS, tokens), f32)
    ranks = jnp.zeros((EXPERTS, tokens), f32)
    prio = prio_ref[...]
    lines = jnp.concatenate([prio[:, 128 * i : 128 * i + 128] for i in range(CHIPS)], axis=0)
    token = lax.broadcasted_iota(jnp.int32, (tokens, CHIPS), 0) // CHIPS
    owner = (token == lax.broadcasted_iota(jnp.int32, (tokens, CHIPS), 1)).astype(f32)
    token = lax.rem(lax.broadcasted_iota(jnp.int32, (tokens, 128), 0), CHIPS)
    lane = lax.broadcasted_iota(jnp.int32, (tokens, 128), 1)
    place_of = lax.rem(lax.broadcasted_iota(jnp.int32, (TOP, 128), 1), TOP)
    place_of = (place_of == lax.broadcasted_iota(jnp.int32, (TOP, 128), 0)).astype(f32)
    priority = jnp.zeros((TOP, tokens), f32)
    for unit, part in ((64.0, lines // 64), (1.0, lax.rem(lines, 64))):
        part = part.astype(f32).astype(bf16)
        rows = dot(owner.astype(bf16), part, ((1,), (0,)))
        rows = jnp.where(lane // TOP == token, rows, 0.0).astype(bf16)
        priority = priority + unit * dot(place_of.astype(bf16), rows, ((1,), (1,)))
    routes = routes_ref[...].astype(f32)
    for j in range(TOP):
        match = experts_iota == routes[j : j + 1, :]
        routed_to = jnp.where(match, 1.0, routed_to)
        ranks = jnp.where(match, priority[j : j + 1, :], ranks)
    far = float(1 << 20)
    ranks = jnp.where((routed_to > 0.0) & live, ranks, far)
    ranks_t = ranks.T
    rows = []
    for e in range(EXPERTS):
        earlier = ranks_t[:, e : e + 1] < ranks[e : e + 1, :]
        rows.append(jnp.sum(earlier.astype(f32), axis=0, keepdims=True))
    slots = jnp.concatenate(rows, axis=0)
    pos = jnp.where((ranks < far) & (slots < CAP), slots, -1.0).astype(jnp.int32)
    pos_ref[...] = pos
    for core in range(2):
        for i in range(4):
            at = core * CHIPS + 4 * i
            posz_out[i, 4 * core : 4 * core + 4, :] = pos[at : at + 4, :]
            for j in range(4):
                posx_out[j, 4 * core + i : 4 * core + i + 1, :] = pos[at + j : at + j + 1, :]
    posz_ref[0] = posz_out[z]
    posx_ref[0] = posx_out[x]
    tok_z[0] = cot_ref[:, 0:HALF]
    tok_x[0] = cot_ref[:, HALF:D]

    def pos_step(d):
        to_z, to_x = lax.rem(z + d, 4), lax.rem(x + d, 4)
        return (
            remote(
                posz_out.at[to_z],
                posz_ref.at[d],
                pos_send.at[0],
                pos_recv.at[0],
                moved(0, d, r)[0],
            ),
            remote(
                posx_out.at[to_x],
                posx_ref.at[d],
                pos_send.at[1],
                pos_recv.at[1],
                moved(d, 0, r)[0],
            ),
        )

    @pl.loop(1, 4)
    def _(d):
        for copy in pos_step(d):
            copy.start()

    done(w_ref.at[0, 0, pl.ds(0, 3), :, pl.ds(0, HALF)], o_recv.at[0])

    @pl.loop(1, 4)
    def _(d):
        for copy in later_cross(d):
            copy.start()

    @pl.loop(1, 4)
    def _(e):
        for copy in line_step(e):
            copy.wait_recv()

        @pl.loop(1, 4)
        def _(d):
            for copy in cross_step(e, d):
                copy.start()

    for d in (1, 3):
        for copy in spread(d, cot_ref, tok_z, tok_x, first_send, first_recv):
            copy.start()

    for copy in core_step(0):
        copy.start()

    def cut_slots(d):
        left = dot(line_hot(posz_ref, d, 0), tok_z[d], ((1,), (0,))).astype(bf16)
        right = dot(line_hot(posx_ref, d, 1), tok_x[d], ((1,), (0,))).astype(bf16)
        sems = slot_send.at[0], slot_recv.at[0], slot_recv.at[0], 1, store_sem.at[1]
        for core in range(2):
            for i in range(4):
                part = slice((core * 4 + i) * CAP, (core * 4 + i + 1) * CAP)
                outgoing[core, d, i, :, 0:HALF] = left[part]
                send_slots(outgoing, grads_ref, core, d, i, *sems, (True, False))
                outgoing[core, i, d, :, HALF:D] = right[part]
                send_slots(outgoing, grads_ref, core, i, d, *sems, (False, True))

    cut_slots(0)

    inputs = hidden_ref[...].astype(f32)
    scale = lax.rsqrt(jnp.mean(inputs * inputs, axis=1, keepdims=True) + epsilon)
    normed_ref[...] = (inputs * scale * again_ref[...]).astype(bf16)

    done(some(3, HALF), o_recv.at[1])

    for n in (1, 3):
        later_plane(n).start()
    later_core(0).start()

    @pl.loop(1, 4)
    def _(d):
        done(some(1, D), w_recv.at[8 + d])
        for copy in core_step(d):
            copy.start()

    near_done(tok_z, tok_x, first_recv)
    for copy in pass_on(tok_z, tok_x, first_send, first_recv):
        copy.start()
    done(posz_ref.at[pl.ds(1, 3)], pos_recv.at[0])
    done(posx_ref.at[pl.ds(1, 3)], pos_recv.at[1])

    @pl.loop(0, 2)
    def _(n):
        cut_slots(1 + 2 * n)

    done(some(4, D), core_recv.at[0])

    here = pl.ds(pl.multiple_of(r * tokens, tokens), tokens)
    cosine, sine = cos_ref[:, here], sin_ref[:, here]

    def projected(first):
        weight = w_ref[:, :, :, :, first : first + HALF].reshape(D, HALF)
        return dot(normed_ref[...], weight, ((1,), (0,))).T

    def turned(rows):
        parts = []
        for h in range(rows.shape[0] // HEAD):
            first, second = rows[HEAD * h : HEAD * h + 32], rows[HEAD * h + 32 : HEAD * h + HEAD]
            parts += [first * cosine - second * sine, second * cosine + first * sine]
        return jnp.concatenate(parts, axis=0).astype(bf16)

    def keys_values(p):
        rows = pl.ds(256 * p, 256)
        return [
            remote(
                ref.at[rows, here],
                ref.at[rows, here],
                kv_send.at[2 * p + n],
                kv_recv.at[2 * p + n],
                sibling,
            )
            for n, ref in enumerate((k_ref, v_ref))
        ]

    def project(p):
        both = projected(D * p + HALF)
        k_ref[256 * p : 256 * p + 256, here] = turned(both[0:256])
        v_ref[256 * p : 256 * p + 256, here] = both[256:512].astype(bf16)
        for copy in keys_values(p):
            copy.start()
        q_ref[HALF * p : HALF * p + HALF, :] = turned(projected(D * p))

    project(0)
    far_done(tok_z, tok_x, first_recv)
    cut_slots(2)
    done(some(4, D), o_recv.at[2])
    for n in range(2):
        later_relay(n).start()
    for n in (1, 3):
        later_core(n).start()
    for copy in keys_values(0):
        copy.wait_recv()

    key_live = lax.broadcasted_iota(jnp.int32, (2 * tokens, 1), 0) < length_ref[0]
    score_scale = HEAD ** (-0.5)

    def attend(g):
        head = pl.ds(pl.multiple_of(g * HEAD, HEAD), HEAD)
        keys, values = k_ref[head, :], v_ref[head, :]
        for j in range(2):
            at = pl.ds(pl.multiple_of((2 * g + j) * HEAD, HEAD), HEAD)
            scores = dot(keys, q_ref[at, :], ((0,), (0,))) * score_scale
            scores = jnp.where(key_live, scores, NEG)
            top = jnp.max(scores, axis=0, keepdims=True)
            weights = jnp.exp(scores - top)
            total = jnp.sum(weights, axis=0, keepdims=True)
            lse_ref[pl.ds(2 * g + j, 1), :] = top + jnp.log(total)
            probs = (weights * (1.0 / total)).astype(bf16)
            mixed_t[at, :] = dot(values, probs, ((1,), (0,))).astype(bf16)

    pl.loop(0, 4)(attend)
    done(some(4, HALF), o_recv.at[4])
    later_core(2).start()
    done(some(4, 2 * D), o_recv.at[3])
    project(1)
    for copy in keys_values(1):
        copy.wait_recv()
    pl.loop(4, 8)(attend)
    mixed_ref[...] = mixed_t[...].T
    weights_out = pltpu.make_async_copy(w_ref, w_hbm, store_sem.at[0])
    weights_out.start()
    w_out = w_ref[:, :, :, :, 2 * D : 3 * D].reshape(D, D)
    middle = hidden_ref[...].astype(f32) + dot(mixed_ref[...], w_out, ((1,), (0,)))
    middle_ref[...] = middle
    scale = lax.rsqrt(jnp.mean(middle * middle, axis=1, keepdims=True) + epsilon)
    routed_ref[...] = (middle * scale * mgain_ref[...]).astype(bf16)
    logits = dot(router_ref[...], routed_ref[...], ((1,), (1,)))
    logits = jnp.where(routed_to > 0.0, logits, -jnp.inf)
    picked = jnp.exp(logits - jnp.max(logits, axis=0, keepdims=True))
    gates_ref[...] = picked / jnp.sum(picked, axis=0, keepdims=True)

    done(all_slots(grads_ref), slot_recv.at[0])
    done(grads_ref.at[0, 0], store_sem.at[1])
    done(all_slots(outgoing), slot_send.at[0])
    done(w_ref.at[0, 0, pl.ds(0, 3), :, pl.ds(0, D)], w_send.at[0])
    done(some(3, D), w_send.at[1])
    done(some(4, D), core_send.at[0])
    done(w_ref.at[0, 0, pl.ds(0, 3), :, pl.ds(0, HALF)], o_send.at[0])
    done(some(3, HALF), o_send.at[1])
    done(some(4, D), o_send.at[2])
    done(some(4, 2 * D), o_send.at[3])
    done(some(4, HALF), o_send.at[4])
    near_done(tok_z, tok_x, first_send)
    far_done(tok_z, tok_x, first_send)
    done(posz_ref.at[pl.ds(1, 3)], pos_send.at[0])
    done(posx_ref.at[pl.ds(1, 3)], pos_send.at[1])
    weights_out.wait()
    for p in range(2):
        for copy in keys_values(p):
            copy.wait_send()


def front(length, *arrays):
    f32, bf16, i32 = jnp.float32, jnp.bfloat16, jnp.int32
    vmem = pl.BlockSpec(memory_space=pltpu.VMEM)
    hbm = pl.BlockSpec(memory_space=pl.ANY)
    shape = jax.ShapeDtypeStruct
    out_shape = (
        shape((2, 4, 4, 32, 3 * D), bf16),
        shape((TOKENS, D), bf16),
        shape((D, TOKENS), bf16),
        shape((HALF, 2 * TOKENS), bf16),
        shape((HALF, 2 * TOKENS), bf16),
        shape((HEADS, TOKENS), f32),
        shape((TOKENS, D), bf16),
        shape((TOKENS, D), f32),
        shape((TOKENS, D), bf16),
        shape((EXPERTS, TOKENS), f32),
        shape((EXPERTS, TOKENS), i32),
        shape((4, 8, TOKENS), i32),
        shape((4, 8, TOKENS), i32),
        shape((2, 4, 4, CAP, D), bf16),
    )
    scratch = [
        pltpu.VMEM((2, 4, 4, 32, 3 * D), bf16),
        pltpu.VMEM((D, TOKENS), bf16),
        pltpu.VMEM((4, 8, TOKENS), i32),
        pltpu.VMEM((4, 8, TOKENS), i32),
        pltpu.VMEM((4, TOKENS, HALF), bf16),
        pltpu.VMEM((4, TOKENS, HALF), bf16),
        pltpu.VMEM((2, 4, 4, CAP, D), bf16),
    ]
    scratch += [pltpu.SemaphoreType.DMA((2,))]
    for count in (12, 5, 1, 4, 4, 1, 2):
        scratch += [pltpu.SemaphoreType.DMA((count,))] * 2
    return pl.pallas_call(
        front_kernel,
        out_shape=out_shape,
        in_specs=[pl.BlockSpec(memory_space=pltpu.SMEM)] + [vmem] * len(arrays),
        out_specs=[hbm] + [vmem] * (len(out_shape) - 2) + [hbm],
        scratch_shapes=scratch,
        compiler_params=pltpu.CompilerParams(
            collective_id=3, has_side_effects=True, vmem_limit_bytes=60 << 20
        ),
        name="front",
    )(length, *arrays)


def turned_back(rows, cosine, sine):
    first, second = rows[0:32], rows[32:64]
    return jnp.concatenate(
        [first * cosine + second * sine, second * cosine - first * sine], axis=0
    )


def rest_kernel(
    length_ref,
    routed_ref,
    pos_ref,
    posz_ref,
    posx_ref,
    gates_ref,
    grads_hbm,
    wg_hbm,
    wu_hbm,
    wd_hbm,
    router_ref,
    middle_ref,
    cot_ref,
    hidden_hbm,
    again_ref,
    mgain_ref,
    normed_hbm,
    mixed_hbm,
    w_hbm,
    q_hbm,
    k_hbm,
    v_hbm,
    lse_ref,
    cos_ref,
    sin_ref,
    hout_ref,
    hgrad_ref,
    again_out,
    mgain_out,
    router_out,
    own_out,
    esum_hbm,
    prod_hbm,
    mid_hbm,
    tok_z,
    tok_x,
    arrived,
    mid,
    parts_in,
    parts_in2,
    gate_out,
    gate_in,
    dot_out,
    dot_in,
    gdot_ref,
    expert_ref,
    relay_in,
    y_in,
    branch_sib,
    normed_sib,
    mixed_sib,
    grad_sib,
    kv_in,
    rs_in,
    rs_in2,
    y_parts,
    small_in,
    small_y_in,
    gain_in,
    gain_y_in,
    router_all,
    load_sem,
    store_sem,
    first_send,
    first_recv,
    slot_send,
    slot_recv,
    back_send,
    back_recv,
    part_send,
    part_recv,
    small_send,
    small_recv,
    c_send,
    c_recv,
    part_send2,
    part_recv2,
    ex_send,
    ex_recv,
    sib_send,
    sib_recv,
    rs_send,
    rs_recv,
    rs_send2,
    rs_recv2,
    ys_send,
    ys_recv,
    sm_send,
    sm_recv,
):
    y, r, x, z = place()
    me = r * CHIPS + z * 4 + x
    sibling = moved(0, 0, 1 - r)[0]
    tokens = TOKENS
    f32, bf16 = jnp.float32, jnp.bfloat16

    above, below = plane_shift(1), plane_shift(3)
    opposite = plane_shift(2)[1]
    def relayed(n):
        device = (above, below)[n][0]
        return remote(
            expert_ref.at[0, n], relay_in.at[n], ex_send.at[n], ex_recv.at[n], device
        )

    def direct(n):
        device = (above, below)[n][0]
        return remote(
            expert_ref.at[1 + n, 1 - n],
            y_in.at[n, 1 - n],
            ex_send.at[2 + n],
            ex_recv.at[2 + n],
            device,
        )

    def passed_on(n):
        device, came_from = (above, below)[n][0], (below, above)[n][1]
        part = esum_hbm.at[came_from, n]
        return remote(part, part, ex_send.at[8 + n], ex_recv.at[8 + n], device)

    def to_sibling(at, src, dst):
        return remote(src, dst, sib_send.at[at], sib_recv.at[at], sibling)

    half = pl.ds(pl.multiple_of((1 - r) * HALF, HALF), HALF)
    sib_normed = to_sibling(0, normed_hbm.at[:, half], normed_sib)
    sib_mixed = to_sibling(1, mixed_hbm.at[:, half], mixed_sib)

    meet(True, True)
    sib_mixed.start()
    sib_normed.start()

    def expert_phase(grads_ref, wg_ref, wu_ref, wd_ref, outgoing, parts_out, active, weighted, pre_grads):
        loads = [
            pltpu.make_async_copy(source, target, load_sem.at[n])
            for n, (source, target) in enumerate(
                (
                    (wg_hbm, wg_ref),
                    (wu_hbm, wu_ref),
                    (wd_hbm, wd_ref),
                    (grads_hbm, grads_ref),
                )
            )
        ]
        for load in loads:
            load.start()

        for d in (1, 3):
            for copy in spread(d, routed_ref, tok_z, tok_x, first_send, first_recv):
                copy.start()

        tok_z[0] = routed_ref[:, 0:HALF]
        tok_x[0] = routed_ref[:, HALF:D]

        def send_rows(core, dz, dx, g, halves):
            came = slot_recv.at[2 * g + r]
            sems = slot_send.at[g], came, came, 1, None
            send_slots(outgoing, arrived, core, dz, dx, *sems, halves)

        left = dot(line_hot(posz_ref, 0, 0), tok_z[0], ((1,), (0,))).astype(bf16)
        right = dot(line_hot(posx_ref, 0, 1), tok_x[0], ((1,), (0,))).astype(bf16)
        for core in range(2):
            for i in range(4):
                part = slice((core * 4 + i) * CAP, (core * 4 + i + 1) * CAP)
                outgoing[core, 0, i, :, 0:HALF] = left[part]
                send_rows(core, 0, i, (4 - i) % 4, (True, False))
                outgoing[core, i, 0, :, HALF:D] = right[part]
                send_rows(core, i, 0, i, (False, True))

        def small(k, out, into, sign, base):
            there, dz, dx = k // CHIPS, lax.rem(k // 4, 4), lax.rem(k, 4)
            slot = r * CHIPS + lax.rem(k, CHIPS)
            return remote(
                out.at[k],
                into.at[slot],
                small_send.at[base],
                small_recv.at[base],
                moved(sign * dx, sign * dz, there)[0],
            )

        def own_slot(k):
            return k == r * CHIPS

        near_done(tok_z, tok_x, first_recv)
        for copy in pass_on(tok_z, tok_x, first_send, first_recv):
            copy.start()

        @pl.loop(0, GROUP)
        def _(k):
            there, dz, dx = k // CHIPS, lax.rem(k // 4, 4), lax.rem(k, 4)
            _, expert = moved(dx, dz, there)
            chosen = picks(pos_ref[pl.ds(expert, 1), :])
            gate_col = jnp.sum(
                jnp.where(chosen, gates_ref[pl.ds(expert, 1), :], 0.0), axis=1, keepdims=True
            )
            gate_out[k, 0:1, 0:CAP] = as_row(gate_col)

            @pl.when(own_slot(k))
            def _():
                gate_in[k] = gate_out[k]

            @pl.when(jnp.logical_not(own_slot(k)))
            def _():
                small(k, gate_out, gate_in, 1, 0).start()

        far_done(tok_z, tok_x, first_recv)

        @pl.loop(0, 4)
        def _(g):
            for dx in range(4):
                dz = lax.rem(dx + g, 4)

                @pl.when(dz != 0)
                def _():
                    rows = [
                        picks(posz_ref[dz, pl.ds(core * 4 + lax.rem(x + dx, 4), 1), :])
                        for core in range(2)
                    ]
                    rows = dot(as_hot(jnp.concatenate(rows, axis=0)), tok_z[dz], ((1,), (0,)))
                    for core in range(2):
                        part = slice(core * CAP, core * CAP + CAP)
                        outgoing[core, dz, dx, :, 0:HALF] = rows[part].astype(bf16)
                        send_rows(core, dz, dx, g, (True, False))

                if dx == 0:
                    continue
                rows = [
                    picks(posx_ref[dx, pl.ds(core * 4 + lax.rem(z + dz, 4), 1), :])
                    for core in range(2)
                ]
                rows = dot(as_hot(jnp.concatenate(rows, axis=0)), tok_x[dx], ((1,), (0,)))
                for core in range(2):
                    part = slice(core * CAP, core * CAP + CAP)
                    outgoing[core, dz, dx, :, HALF:D] = rows[part].astype(bf16)
                    send_rows(core, dz, dx, g, (False, True))

        def keep_produced(k):
            core, dz, dx = k // CHIPS, lax.rem(k // 4, 4), lax.rem(k, 4)
            return pltpu.make_async_copy(
                grads_ref.at[core, dz, dx],
                prod_hbm.at[core, dz, dx],
                store_sem.at[lax.rem(dz - dx + 4, 4)],
            )

        for load in loads:
            load.wait()
        done(gate_in.at[pl.ds(0, GROUP - 1)], small_recv.at[0])

        @pl.loop(0, 8)
        def _(c):
            g, core = c // 2, lax.rem(c, 2)

            @pl.when(core == r)
            def _():
                done(arrived.at[0, 0, pl.ds(0, 3)], slot_recv.at[c])

            @pl.when(core != r)
            def _():
                done(arrived.at[0, 0], slot_recv.at[c])

            @pl.when(core == 0)
            def _():
                done(outgoing.at[0, pl.ds(0, 2), :, :, pl.ds(0, 896)], slot_send.at[g])

            rows, gate_cols, grads = [], [], []
            for dx in range(4):
                dz = lax.rem(dx + g, 4)
                k = core * CHIPS + dz * 4 + dx
                rows.append(arrived[core, dz, dx])
                gate_cols.append(as_column(gate_in[k, 0:1, 0:CAP]))
                grads.append(grads_ref[core, dz, dx])
            rows = jnp.concatenate(rows, axis=0)
            gate_cols = jnp.concatenate(gate_cols, axis=0)
            grads = jnp.concatenate(grads, axis=0).astype(f32)
            gate_pre = dot(rows, wg_ref[...], ((1,), (0,)))
            up_pre = dot(rows, wu_ref[...], ((1,), (0,)))
            gate_sig = jax.nn.sigmoid(gate_pre)
            gate_act = gate_pre * gate_sig
            act = (gate_act * up_pre).astype(bf16)
            produced = dot(act, wd_ref[...], ((1,), (0,))).astype(bf16).astype(f32)
            dots = jnp.sum(produced * grads, axis=1, keepdims=True)
            produced_grad = (gate_cols * grads).astype(bf16)
            act_grad = dot(produced_grad, wd_ref[...], ((1,), (1,))).astype(bf16).astype(f32)
            gate_grad = (
                act_grad * up_pre * gate_sig * (1.0 + gate_pre * (1.0 - gate_sig))
            ).astype(bf16)
            up_grad = (act_grad * gate_act).astype(bf16)
            row_grads = dot(gate_grad, wg_ref[...], ((1,), (1,)))
            row_grads = (row_grads + dot(up_grad, wu_ref[...], ((1,), (1,)))).astype(bf16)
            produced = (produced * gate_cols).astype(bf16)
            for dx in range(4):
                dz = lax.rem(dx + g, 4)
                k = core * CHIPS + dz * 4 + dx
                part = slice(dx * CAP, dx * CAP + CAP)
                outgoing[core, dz, dx] = row_grads[part]
                send_slots(
                    outgoing,
                    mid,
                    core,
                    dz,
                    dx,
                    back_send.at[0],
                    back_recv.at[dz],
                    back_recv.at[4 + dx],
                    -1,
                )
                dot_out[k, 0:1, 0:CAP] = as_row(dots[part])

                @pl.when(own_slot(k))
                def _():
                    dot_in[k] = dot_out[k]

                @pl.when(jnp.logical_not(own_slot(k)))
                def _():
                    small(k, dot_out, dot_in, -1, 1).start()

                grads_ref[core, dz, dx] = produced[part]
                keep_produced(k).start()
                active[core, dz, dx] = act[part]
                weighted[core, dz, dx] = produced_grad[part]
                pre_grads[core, dz, dx, :, 0:HALF] = gate_grad[part]
                pre_grads[core, dz, dx, :, HALF:D] = up_grad[part]

        def send_results(g):
            done(prod_hbm.at[0, pl.ds(0, 2)], store_sem.at[g])
            for dx in range(4):
                dz = lax.rem(dx + g, 4)
                for core in range(2):
                    send_slots(
                        prod_hbm,
                        mid_hbm,
                        core,
                        dz,
                        dx,
                        c_send.at[0],
                        c_recv.at[0],
                        c_recv.at[0],
                        -1,
                        load_sem.at[8],
                    )

        send_results(0)

        all_rows = GROUP * CAP

        def quarter_grads(slot, n):
            span = pl.ds(pl.multiple_of(n * 256, 256), 256)
            left = arrived[:, :, :, :, span].reshape(all_rows, 256)
            part = dot(left, pre_grads[...].reshape(all_rows, D), ((0,), (0,))).astype(bf16)
            narrow = pl.ds(pl.multiple_of(n * 128, 128), 128)
            left = active[:, :, :, :, narrow].reshape(all_rows, 128)
            down = dot(left, weighted[...].reshape(all_rows, D), ((0,), (0,))).astype(bf16)
            for h in range(2):
                rows = part[128 * h : 128 * h + 128]
                expert_ref[slot, h, 0:128, :] = rows[:, 0:HALF]
                expert_ref[slot, h, 128:256, :] = rows[:, HALF:D]
                rows = down[64 * h : 64 * h + 64]
                expert_ref[slot, h, 256:320, :] = rows[:, 0:HALF]
                expert_ref[slot, h, 320:384, :] = rows[:, HALF:D]

        quarter_grads(0, opposite)
        for n in range(2):
            relayed(n).start()

        part_sems = part_send, part_recv
        fold_start(parts_out, parts_in, mid, back_recv, posz_ref, posx_ref, part_sems)

        @pl.loop(1, 4)
        def _(slot):
            quarter_grads(slot, lax.rem(y + jnp.where(slot == 1, 1, jnp.where(slot == 2, 3, 0)), 4))

            @pl.when(slot == 1)
            def _():
                fold_end(parts_out, parts_in, part_sems)
                pl.loop(1, 4)(send_results)

        for n in range(2):
            direct(n).start()

        done(dot_in.at[pl.ds(0, GROUP - 1)], small_recv.at[1])

        @pl.loop(0, GROUP)
        def _(k):
            there, dz, dx = k // CHIPS, lax.rem(k // 4, 4), lax.rem(k, 4)
            _, expert = moved(dx, dz, there)
            at = pl.ds(expert, 1)
            dots = as_column(dot_in[k, 0:1, 0:CAP])
            gdot_ref[at, :] = jnp.sum(
                jnp.where(picks(pos_ref[at, :]), dots, 0.0), axis=0, keepdims=True
            )

        hgrad_ref[...] = folded(parts_in, part_sems)
        done(all_slots(outgoing), back_send.at[0])
        done(parts_out.at[pl.ds(0, 3)], part_send.at[0])
        near_done(tok_z, tok_x, first_send)
        far_done(tok_z, tok_x, first_send)
        done(gate_in.at[pl.ds(0, GROUP - 1)], small_send.at[0])
        done(dot_in.at[pl.ds(0, GROUP - 1)], small_send.at[1])

    pl.run_scoped(
        expert_phase,
        pltpu.VMEM((2, 4, 4, CAP, D), bf16),
        pltpu.VMEM((D, HALF), bf16),
        pltpu.VMEM((D, HALF), bf16),
        pltpu.VMEM((HALF, D), bf16),
        pltpu.VMEM((2, 4, 4, CAP, D), bf16),
        pltpu.VMEM((4, tokens, D), bf16),
        pltpu.VMEM((2, 4, 4, CAP, HALF), bf16),
        pltpu.VMEM((2, 4, 4, CAP, D), bf16),
        pltpu.VMEM((2, 4, 4, CAP, D), bf16),
    )

    def finish_phase(w_ref, q_ref, k_ref, v_ref, normed_ref, mixed_ref, hidden_ref, parts_out2, quarter_sum, relay_out, branch_own, mg_t, grad_t, kv_own, kv_out, weight_part, rs_out, y_out, small_out, small_y, gain_out, gain_y):
        loads = [
            pltpu.make_async_copy(source, target, load_sem.at[n])
            for n, (source, target) in enumerate(
                (
                    (w_hbm, w_ref),
                    (mixed_hbm, mixed_ref),
                    (q_hbm, q_ref),
                    (k_hbm, k_ref),
                    (v_hbm, v_ref),
                    (normed_hbm, normed_ref),
                    (hidden_hbm, hidden_ref),
                )
            )
        ]
        for load in loads:
            load.start()

        def weight(first, width):
            return w_ref[:, :, :, :, first : first + width].reshape(D, width)

        def merged(n):
            device = (above, below)[n][0]
            return remote(
                relay_out.at[n], y_in.at[n, n], ex_send.at[4 + n], ex_recv.at[4 + n], device
            )

        def handed(n):
            device = (above, below)[n][0]
            return remote(
                quarter_sum, esum_hbm.at[y], ex_send.at[6 + n], ex_recv.at[6 + n], device
            )

        def sib_keyval(p):
            return to_sibling(3 + p, kv_out.at[p], kv_in.at[p])

        def sib_grads(p, part):
            rows = pl.ds(p * D + part * HALF, HALF)
            return to_sibling(5 + 2 * p + part, grad_t.at[rows], grad_sib.at[rows])

        sib_branch = to_sibling(2, branch_own, branch_sib)

        for n in range(2):
            relayed(n).wait_recv()
            total = relay_in[n].astype(f32) + expert_ref[1 + n, n].astype(f32)
            relay_out[n] = total.astype(bf16)
            merged(n).start()

        gates = gates_ref[...]
        gdot = gdot_ref[...]
        logit_grad = gates * (gdot - jnp.sum(gates * gdot, axis=0, keepdims=True))
        high, rest = split_two(logit_grad)
        router_part = dot(high, routed_ref[...], ((1,), (0,)))
        router_part = router_part + dot(rest, routed_ref[...], ((1,), (0,)))
        routed_grad = dot(high, router_ref[...], ((0,), (0,)))
        routed_grad = routed_grad + dot(rest, router_ref[...], ((0,), (0,)))
        routed_grad = routed_grad + hgrad_ref[...]
        live = (
            r * tokens + lax.broadcasted_iota(jnp.int32, (tokens, 1), 0) < length_ref[0]
        ).astype(f32)
        middle = middle_ref[...]
        scale = lax.rsqrt(jnp.mean(middle * middle, axis=1, keepdims=True) + epsilon)
        rows = middle * scale
        moe_part = jnp.sum(routed_grad * rows, axis=0, keepdims=True)
        scaled = routed_grad * mgain_ref[...]
        inner = jnp.mean(scaled * rows, axis=1, keepdims=True)
        middle_grad = cot_ref[...].astype(f32) * live + scale * (scaled - rows * inner)
        hgrad_ref[...] = middle_grad
        branch_own[...] = middle_grad.astype(bf16)
        sib_branch.start()
        for j in range(8):
            part = slice(128 * j, 128 * j + 128)
            small_out[:, j, :] = router_part[:, part]
            small_out[:, 8 + j, :] = jnp.broadcast_to(moe_part[:, part], (GROUP, 128))

        def tiny(k):
            device, other = step_of(k, 1)
            return remote(small_out.at[other], small_in.at[me], sm_send.at[0], sm_recv.at[0], device)

        @pl.loop(1, GROUP)
        def _(k):
            tiny(k).start()

        small_in[me] = small_out[me]

        loads[0].wait()
        mg_t[...] = dot(weight(2 * D, D), branch_own[...], ((1,), (1,))).astype(bf16)

        mine = pl.ds(pl.multiple_of(r * HALF, HALF), HALF)

        def columns(p):
            return pl.ds(p * D, HALF), pl.ds(p * D + HALF, HALF)

        def first_step(p, d):
            left, right = columns(p)
            return (
                remote(
                    weight_part.at[lax.rem(z + d, 4), :, :, left],
                    rs_in.at[d, :, :, left],
                    rs_send.at[p],
                    rs_recv.at[p],
                    moved(0, d, r)[0],
                ),
                remote(
                    weight_part.at[:, lax.rem(x + d, 4), :, right],
                    rs_in.at[d, :, :, right],
                    rs_send.at[p],
                    rs_recv.at[p],
                    moved(d, 0, r)[0],
                ),
            )

        def second_step(p, d):
            left, right = columns(p)
            return (
                remote(
                    rs_out.at[lax.rem(x + d, 4), :, left],
                    rs_in2.at[d, :, left],
                    rs_send2.at[p],
                    rs_recv2.at[p],
                    moved(d, 0, r)[0],
                ),
                remote(
                    rs_out.at[lax.rem(z + d, 4), :, right],
                    rs_in2.at[d, :, right],
                    rs_send2.at[p],
                    rs_recv2.at[p],
                    moved(0, d, r)[0],
                ),
            )

        def across(p, n):
            cols = pl.ds(p * D, D)
            return remote(
                y_out.at[:, cols],
                y_parts.at[y, :, cols],
                ys_send.at[p],
                ys_recv.at[p],
                plane_shift(n)[0],
            )

        def sum_first(p, total):
            weight_part[:, :, :, p * D : p * D + D] = total.astype(bf16).reshape(4, 4, 32, D)

            @pl.loop(1, 4)
            def _(d):
                for copy in first_step(p, d):
                    copy.start()

        def sum_second(p):
            left, right = columns(p)

            done(rs_in.at[pl.ds(1, 3), :, :, pl.ds(p * D, D)], rs_recv.at[p])

            total = weight_part[z, :, :, left].astype(f32)
            other = weight_part[:, x, :, right].astype(f32)
            for d in range(1, 4):
                total = total + rs_in[d, :, :, left].astype(f32)
                other = other + rs_in[d, :, :, right].astype(f32)
            rs_out[:, :, left] = total.astype(bf16)
            rs_out[:, :, right] = other.astype(bf16)

            @pl.loop(1, 4)
            def _(d):
                for copy in second_step(p, d):
                    copy.start()

        def sum_third(p):
            left, right = columns(p)

            done(rs_in2.at[pl.ds(1, 3), :, pl.ds(p * D, D)], rs_recv2.at[p])

            total = rs_out[x, :, left].astype(f32)
            other = rs_out[z, :, right].astype(f32)
            for d in range(1, 4):
                total = total + rs_in2[d, :, left].astype(f32)
                other = other + rs_in2[d, :, right].astype(f32)
            y_out[:, left] = total.astype(bf16)
            y_out[:, right] = other.astype(bf16)
            y_parts[y, :, left] = total.astype(bf16)
            y_parts[y, :, right] = other.astype(bf16)
            for n in range(1, PLANES):
                across(p, n).start()

        sib_mixed.wait_recv()
        sib_branch.wait_recv()
        loads[1].wait()
        total = dot(mixed_ref[:, mine], branch_own[...], ((0,), (0,)))
        sum_first(2, total + dot(mixed_sib[...], branch_sib[...], ((0,), (0,))))

        key_live = lax.broadcasted_iota(jnp.int32, (2 * tokens, 1), 0) < length_ref[0]
        score_scale = HEAD ** (-0.5)
        here = pl.ds(pl.multiple_of(r * tokens, tokens), tokens)
        cosine, sine = cos_ref[:, here], sin_ref[:, here]
        first_core = r == 0

        def key_head(p, i):
            g = 4 * p + i
            head = pl.ds(pl.multiple_of(g * HEAD, HEAD), HEAD)
            keys, values = k_ref[head, :], v_ref[head, :]
            key_sum, value_sum = None, None
            for j in range(2):
                at = pl.ds(pl.multiple_of((2 * g + j) * HEAD, HEAD), HEAD)
                query, mixed_grad = q_ref[at, :], mg_t[at, :]
                scores = dot(keys, query, ((0,), (0,))) * score_scale
                scores = jnp.where(key_live, scores, NEG)
                probs = jnp.exp(scores - lse_ref[pl.ds(2 * g + j, 1), :])
                prob_grad = dot(values, mixed_grad, ((0,), (0,)))
                value_part = dot(mixed_grad, probs.astype(bf16), ((1,), (1,)))
                inner = jnp.sum(probs * prob_grad, axis=0, keepdims=True)
                score_grad = (probs * (prob_grad - inner)).astype(bf16)
                key_part = dot(query, score_grad, ((1,), (1,)))
                query_grad = dot(keys, score_grad, ((1,), (0,))) * score_scale
                to = pl.ds(pl.multiple_of(p * D + (2 * i + j) * HEAD, HEAD), HEAD)
                grad_t[to, :] = turned_back(query_grad, cosine, sine).astype(bf16)
                key_sum = key_part if key_sum is None else key_sum + key_part
                value_sum = value_part if value_sum is None else value_sum + value_part
            key_sum = key_sum * score_scale
            for n, part in enumerate((key_sum, value_sum)):
                to = pl.ds(pl.multiple_of(256 * n + i * HEAD, HEAD), HEAD)
                kv_own[p, to, :] = jnp.where(first_core, part[:, :tokens], part[:, tokens:])
                away = jnp.where(first_core, part[:, tokens:], part[:, :tokens])
                kv_out[p, to, :] = away.astype(bf16)

        def heads(p, first, last):
            @pl.loop(first, last)
            def _(i):
                key_head(p, i)

        def whole_keyval(p):
            sib_keyval(p).wait_recv()
            for i in range(4):
                rows = slice(HEAD * i, HEAD * i + HEAD)
                total = kv_own[p, rows, :] + kv_in[p, rows, :].astype(f32)
                to = p * D + HALF + HEAD * i
                grad_t[to : to + HEAD, :] = turned_back(total, cosine, sine).astype(bf16)
            total = kv_own[p, 256:512, :] + kv_in[p, 256:512, :].astype(f32)
            grad_t[p * D + HALF + 256 : p * D + D, :] = total.astype(bf16)
            sib_grads(p, 1).start()

        def projections(p):
            rows = slice(p * D, p * D + D)
            for part in range(2):
                sib_grads(p, part).wait_recv()
            total = dot(normed_ref[:, mine], grad_t[rows, :], ((0,), (1,)))
            sum_first(p, total + dot(normed_sib[...], grad_sib[rows, :], ((0,), (1,))))

        def inputs_part(p):
            return dot(grad_t[p * D : p * D + D, :], weight(p * D, D), ((0,), (1,)))

        for load in loads[2:5]:
            load.wait()
        heads(0, 0, 4)
        sib_keyval(0).start()
        sib_grads(0, 0).start()

        heads(1, 0, 4)
        sib_keyval(1).start()
        sib_grads(1, 0).start()
        for n in range(2):
            direct(n).wait_recv()
            merged(n).wait_recv()
        for n in range(2):
            total = expert_ref[3, n].astype(f32) + (y_in[0, n].astype(f32) + y_in[1, n].astype(f32))
            quarter_sum[n] = total.astype(bf16)
        quarter_out = pltpu.make_async_copy(quarter_sum, esum_hbm.at[y], load_sem.at[9])
        quarter_out.start()
        for n in range(2):
            handed(n).start()

        whole_keyval(0)
        for load in loads[5:]:
            load.wait()
        sib_normed.wait_recv()
        projections(0)
        done(all_slots(mid_hbm), c_recv.at[0])
        done(mid_hbm.at[0, 0], load_sem.at[8])
        results_in = pltpu.make_async_copy(mid_hbm, mid, load_sem.at[10])
        results_in.start()
        whole_keyval(1)
        normed_grad = inputs_part(0)
        projections(1)
        normed_grad = normed_grad + inputs_part(1)

        inputs = hidden_ref[...].astype(f32)
        scale = lax.rsqrt(jnp.mean(inputs * inputs, axis=1, keepdims=True) + epsilon)
        rows = inputs * scale
        attn_part = jnp.sum(normed_grad * rows, axis=0, keepdims=True)
        for j in range(8):
            gain_out[j : j + 1, :] = attn_part[:, 128 * j : 128 * j + 128]

        def gain(k):
            device, _ = step_of(k, 1)
            return remote(gain_out, gain_in.at[me], sm_send.at[3], sm_recv.at[3], device)

        @pl.loop(1, GROUP)
        def _(k):
            gain(k).start()

        gain_in[me] = gain_out[...]
        scaled = normed_grad * again_ref[...]
        inner = jnp.mean(scaled * rows, axis=1, keepdims=True)
        hgrad_ref[...] += scale * (scaled - rows * inner)

        sum_second(2)
        done(small_in.at[pl.ds(0, GROUP - 1)], sm_recv.at[0])

        def small_across(n):
            device, _ = plane_shift(n)
            return remote(
                small_y, small_y_in.at[y], sm_send.at[1], sm_recv.at[1], device
            )

        small_y[...] = jnp.sum(small_in[...], axis=0)
        small_y_in[y] = small_y[...]
        for n in range(1, PLANES):
            small_across(n).start()

        sum_second(0)
        results_in.wait()
        part_sems = part_send2, part_recv2
        fold_start(parts_out2, parts_in2, mid, None, posz_ref, posx_ref, part_sems)
        for n in range(2):
            handed(n).wait_recv()
            passed_on(n).start()

        done(small_y_in.at[pl.ds(0, 3)], sm_recv.at[1])
        totals = small_y_in[0] + small_y_in[1] + small_y_in[2] + small_y_in[3]
        mgain_out[...] = totals[8:16]
        router_all[me] = totals[0:8]

        def router_row(k):
            device, _ = step_of(k, 1)
            return remote(
                router_all.at[me], router_all.at[me], sm_send.at[2], sm_recv.at[2], device
            )

        @pl.loop(1, GROUP)
        def _(k):
            router_row(k).start()

        sum_second(1)
        fold_end(parts_out2, parts_in2, part_sems)
        sum_third(2)
        sum_third(0)

        done(gain_in.at[pl.ds(0, GROUP - 1)], sm_recv.at[3])

        gain_y[...] = jnp.sum(gain_in[...], axis=0)
        gain_y_in[y] = gain_y[...]

        def gain_across(n):
            device, _ = plane_shift(n)
            return remote(gain_y, gain_y_in.at[y], sm_send.at[4], sm_recv.at[4], device)

        for n in range(1, PLANES):
            gain_across(n).start()

        sum_third(1)

        mixture = folded(parts_in2, part_sems)
        hout_ref[...] = ((middle_ref[...] + mixture) * live).astype(bf16)

        done(gain_y_in.at[pl.ds(0, 3)], sm_recv.at[4])
        again_out[...] = (gain_y_in[0] + gain_y_in[1]) + (gain_y_in[2] + gain_y_in[3])

        done(router_all.at[pl.ds(0, GROUP - 1)], sm_recv.at[2])

        router_out[...] = router_all[...]

        done(all_slots(mid_hbm), c_send.at[0])
        done(parts_out2.at[pl.ds(0, 3)], part_send2.at[0])
        done(small_in.at[pl.ds(0, GROUP - 1)], sm_send.at[0])
        done(small_y_in.at[pl.ds(0, 3)], sm_send.at[1])
        done(router_all.at[pl.ds(0, GROUP - 1)], sm_send.at[2])
        done(gain_in.at[pl.ds(0, GROUP - 1)], sm_send.at[3])
        done(gain_y_in.at[pl.ds(0, 3)], sm_send.at[4])
        for p in range(3):
            done(rs_in.at[pl.ds(1, 3), :, :, pl.ds(p * D, D)], rs_send.at[p])
            done(rs_in2.at[pl.ds(1, 3), :, pl.ds(p * D, D)], rs_send2.at[p])
            done(y_parts.at[pl.ds(0, 3), :, pl.ds(p * D, D)], ys_recv.at[p])
            done(y_parts.at[pl.ds(0, 3), :, pl.ds(p * D, D)], ys_send.at[p])
        for n in range(2):
            for copy in (relayed(n), direct(n), merged(n), handed(n), passed_on(n)):
                copy.wait_send()
        for copy in (sib_normed, sib_mixed, sib_branch):
            copy.wait_send()
        for p in range(2):
            sib_keyval(p).wait_send()
            for part in range(2):
                sib_grads(p, part).wait_send()
        for n in range(2):
            passed_on(n).wait_recv()
        quarter_out.wait()
        own_out[...] = (y_parts[0].astype(f32) + y_parts[1].astype(f32)) + (
            y_parts[2].astype(f32) + y_parts[3].astype(f32)
        )

    pl.run_scoped(
        finish_phase,
        pltpu.VMEM((2, 4, 4, 32, 3 * D), bf16),
        pltpu.VMEM((D, tokens), bf16),
        pltpu.VMEM((HALF, 2 * tokens), bf16),
        pltpu.VMEM((HALF, 2 * tokens), bf16),
        pltpu.VMEM((tokens, D), bf16),
        pltpu.VMEM((tokens, D), bf16),
        pltpu.VMEM((tokens, D), bf16),
        pltpu.VMEM((4, tokens, D), bf16),
        pltpu.VMEM((2, 384, HALF), bf16),
        pltpu.VMEM((2, 384, HALF), bf16),
        pltpu.VMEM((tokens, D), bf16),
        pltpu.VMEM((D, tokens), bf16),
        pltpu.VMEM((2 * D, tokens), bf16),
        pltpu.VMEM((2, HALF, tokens), f32),
        pltpu.VMEM((2, HALF, tokens), bf16),
        pltpu.VMEM((4, 4, 32, 3 * D), bf16),
        pltpu.VMEM((4, 32, 3 * D), bf16),
        pltpu.VMEM((32, 3 * D), bf16),
        pltpu.VMEM((GROUP, 16, 128), f32),
        pltpu.VMEM((16, 128), f32),
        pltpu.VMEM((8, 128), f32),
        pltpu.VMEM((8, 128), f32),
    )


def rest(length, *arrays):
    tokens = TOKENS
    f32, bf16 = jnp.float32, jnp.bfloat16
    vmem = pl.BlockSpec(memory_space=pltpu.VMEM)
    hbm = pl.BlockSpec(memory_space=pl.ANY)
    shape = jax.ShapeDtypeStruct
    sems = pltpu.SemaphoreType.DMA
    scratch = [
        pltpu.VMEM((4, tokens, HALF), bf16),
        pltpu.VMEM((4, tokens, HALF), bf16),
        pltpu.VMEM((2, 4, 4, CAP, D), bf16),
        pltpu.VMEM((2, 4, 4, CAP, D), bf16),
        pltpu.VMEM((4, tokens, D), bf16),
        pltpu.VMEM((4, tokens, D), bf16),
        pltpu.VMEM((GROUP, 8, 128), f32),
        pltpu.VMEM((GROUP, 8, 128), f32),
        pltpu.VMEM((GROUP, 8, 128), f32),
        pltpu.VMEM((GROUP, 8, 128), f32),
        pltpu.VMEM((EXPERTS, tokens), f32),
        pltpu.VMEM((4, 2, 384, HALF), bf16),
        pltpu.VMEM((2, 384, HALF), bf16),
        pltpu.VMEM((2, 2, 384, HALF), bf16),
        pltpu.VMEM((tokens, D), bf16),
        pltpu.VMEM((tokens, HALF), bf16),
        pltpu.VMEM((tokens, HALF), bf16),
        pltpu.VMEM((2 * D, tokens), bf16),
        pltpu.VMEM((2, HALF, tokens), bf16),
        pltpu.VMEM((4, 4, 32, 3 * D), bf16),
        pltpu.VMEM((4, 32, 3 * D), bf16),
        pltpu.VMEM((PLANES, 32, 3 * D), bf16),
        pltpu.VMEM((GROUP, 16, 128), f32),
        pltpu.VMEM((PLANES, 16, 128), f32),
        pltpu.VMEM((GROUP, 8, 128), f32),
        pltpu.VMEM((PLANES, 8, 128), f32),
        pltpu.VMEM((GROUP, 8, 128), f32),
    ]
    for count in (11, 4, 4, 4, 4, 8, 1, 8, 1, 3, 2, 2, 1, 1, 1, 3, 10, 10, 9, 9, 3, 3, 3, 3, 3, 3, 5, 5):
        scratch += [sems((count,))]
    in_specs = [pl.BlockSpec(memory_space=pltpu.SMEM)] + [vmem] * len(arrays)
    for n in (6, 7, 8, 9, 13, 16, 17, 18, 19, 20, 21):
        in_specs[n] = hbm
    return pl.pallas_call(
        rest_kernel,
        out_shape=(
            shape((tokens, D), bf16),
            shape((tokens, D), f32),
            shape((8, 128), f32),
            shape((8, 128), f32),
            shape((GROUP, 8, 128), f32),
            shape((32, 3 * D), f32),
            shape((4, 2, 384, HALF), bf16),
            shape((2, 4, 4, CAP, D), bf16),
            shape((2, 4, 4, CAP, D), bf16),
        ),
        in_specs=in_specs,
        out_specs=[vmem] * 6 + [hbm] * 3,
        scratch_shapes=scratch,
        compiler_params=pltpu.CompilerParams(
            collective_id=2, has_side_effects=True, vmem_limit_bytes=62 << 20
        ),
        name="rest",
    )(length, *arrays)[:7]


def spread_kernel(
    hout_ref,
    hgrad_ref,
    own_ref,
    esum_ref,
    router_ref,
    again_ref,
    mgain_ref,
    hout_out,
    hgrad_out,
    q_out,
    k_out,
    v_out,
    o_out,
    gate_out,
    up_out,
    down_out,
    router_out,
    again_out,
    mgain_out,
):
    f32 = jnp.float32
    hout_out[...] = hout_ref[...]
    hgrad_out[...] = hgrad_ref[...]
    gate_out[0] = esum_ref[0, 0, 0:128, :].astype(f32)
    up_out[0] = esum_ref[0, 0, 128:256, :].astype(f32)
    down_out[0, :, 0:HALF] = esum_ref[0, 0, 256:320, :].astype(f32)
    down_out[0, :, HALF:D] = esum_ref[0, 0, 320:384, :].astype(f32)

    @pl.when(pl.program_id(0) == 0)
    def _():
        for p in range(2):
            q_out[:, p * HALF : p * HALF + HALF] = own_ref[:, p * D : p * D + HALF]
            k_out[:, p * 256 : p * 256 + 256] = own_ref[:, p * D + HALF : p * D + 768]
            v_out[:, p * 256 : p * 256 + 256] = own_ref[:, p * D + 768 : p * D + D]
        o_out[...] = own_ref[:, 2 * D : 3 * D]
        for j in range(8):
            router_out[:, 128 * j : 128 * j + 128] = router_ref[:, j, :]
        again_out[...] = again_ref[...]
        mgain_out[...] = mgain_ref[...]


def spread_out(*arrays):
    f32, bf16 = jnp.float32, jnp.bfloat16
    shape = jax.ShapeDtypeStruct

    def whole(*dims):
        return pl.BlockSpec(dims, lambda i: (0,) * len(dims))

    def rows(count, width):
        return pl.BlockSpec((count, width), lambda i: (i, 0))

    def expert_rows(count, width):
        return pl.BlockSpec((1, count, width), lambda i: (0, i, 0))

    return pl.pallas_call(
        spread_kernel,
        grid=(8,),
        out_shape=(
            shape((TOKENS, D), bf16),
            shape((TOKENS, D), f32),
            shape((32, D), f32),
            shape((32, HALF), f32),
            shape((32, HALF), f32),
            shape((32, D), f32),
            shape((1, D, HALF), f32),
            shape((1, D, HALF), f32),
            shape((1, HALF, D), f32),
            shape((EXPERTS, D), f32),
            shape((8, 128), f32),
            shape((8, 128), f32),
        ),
        in_specs=[
            rows(32, D),
            rows(32, D),
            whole(32, 3 * D),
            pl.BlockSpec((1, 1, 384, HALF), lambda i: (i // 2, i % 2, 0, 0)),
            whole(GROUP, 8, 128),
            whole(8, 128),
            whole(8, 128),
        ],
        out_specs=[
            rows(32, D),
            rows(32, D),
            whole(32, D),
            whole(32, HALF),
            whole(32, HALF),
            whole(32, D),
            expert_rows(128, HALF),
            expert_rows(128, HALF),
            expert_rows(64, D),
            whole(EXPERTS, D),
            whole(8, 128),
            whole(8, 128),
        ],
        name="spread_out",
    )(*arrays)


def on_device(
    hidden_in,
    cotangent,
    lengths,
    routes,
    priority,
    attn_gain,
    query_weight,
    key_weight,
    value_weight,
    output_weight,
    moe_gain,
    router,
    gate_weight,
    up_weight,
    down_weight,
):
    tok_count = hidden_in.shape[0]
    half_dim = HEAD // 2
    frequency = rotary_base ** (-np.arange(half_dim, dtype=np.float32) / half_dim)
    positions = np.arange(2 * tok_count, dtype=np.float32)
    angles = frequency.astype(np.float32)[:, None] * positions[None, :]
    cosine, sine = jnp.asarray(np.cos(angles)), jnp.asarray(np.sin(angles))
    router_t = router.T
    (
        weights,
        normed,
        queries,
        keys,
        values,
        log_total,
        mixed_rows,
        middle,
        routed,
        gates,
        pos,
        posz,
        posx,
        arrived_grad,
    ) = front(
        lengths,
        hidden_in,
        cotangent,
        routes.T,
        priority,
        attn_gain[None],
        moe_gain[None],
        query_weight,
        key_weight,
        value_weight,
        output_weight,
        router_t,
        cosine,
        sine,
    )
    summed = rest(
        lengths,
        routed,
        pos,
        posz,
        posx,
        gates,
        arrived_grad,
        gate_weight[0],
        up_weight[0],
        down_weight[0],
        router_t,
        middle,
        cotangent,
        hidden_in,
        attn_gain[None],
        moe_gain[None],
        normed,
        mixed_rows,
        weights,
        queries,
        keys,
        values,
        log_total,
        cosine,
        sine,
    )
    hidden_out, hidden_grad, attn_gain_sum, moe_gain_sum, router_sum, own_rows, expert_sum = summed
    (
        hidden_out,
        hidden_grad,
        query_grad,
        key_grad,
        value_grad,
        output_grad,
        gate_grad,
        up_grad,
        down_grad,
        router_grad,
        attn_gain_sum,
        moe_gain_sum,
    ) = spread_out(
        hidden_out, hidden_grad, own_rows, expert_sum, router_sum, attn_gain_sum, moe_gain_sum
    )
    return (
        hidden_out,
        hidden_grad,
        attn_gain_sum.reshape(D),
        query_grad,
        key_grad,
        value_grad,
        output_grad,
        moe_gain_sum.reshape(D),
        router_grad.T,
        gate_grad,
        up_grad,
        down_grad,
    )


def solution(mesh):
    return jax.shard_map(
        on_device,
        mesh=mesh,
        in_specs=(
            P(("dp", "col", "row"), None),
            P(("dp", "col", "row"), None),
            P(("dp", "col")),
            P(("dp", "col", "row"), None),
            P(("dp", "col", "row"), None),
            P(),
            P(("row", "col"), None),
            P(("row", "col"), None),
            P(("row", "col"), None),
            P(("row", "col"), None),
            P(),
            P(),
            P(("row", "col"), None, None),
            P(("row", "col"), None, None),
            P(("row", "col"), None, None),
        ),
        out_specs=(
            P(("dp", "col", "row"), None),
            P(("dp", "col", "row"), None),
            P(),
            P(("row", "col"), None),
            P(("row", "col"), None),
            P(("row", "col"), None),
            P(("row", "col"), None),
            P(),
            P(),
            P(("row", "col"), None, None),
            P(("row", "col"), None, None),
            P(("row", "col"), None, None),
        ),
        check_vma=False,
    )
```

```python
import jax
import jax.numpy as jnp
import numpy as np
from jax import lax
from jax.experimental import pallas as pl
from jax.experimental.pallas import tpu as pltpu
from jax.sharding import PartitionSpec as P

D = 1024
HEADS = 16
HEAD = 64
KV_HEADS = 8
EXPERTS = 32
TOP = 8
CAP = 64


epsilon = 1e-05
rotary_base = 10000.0


MESH = pl.DeviceIdType.MESH
GROUP = 32
PLANES = 4
CHIPS = 16
HALF = D // 2
TOKENS = 256
NEG = -1000000000.0


def place():
    col = lax.axis_index("col")
    return lax.axis_index("dp"), lax.axis_index("row"), lax.rem(col, 4), col // 4


def moved(dx, dz, core):
    y, r, x, z = place()
    col = lax.rem(z + dz + 4, 4) * 4 + lax.rem(x + dx + 4, 4)
    return (y, core, col), core * CHIPS + col


def plane_shift(n):
    y, r, x, z = place()
    other = lax.rem(y + n, PLANES)
    return (other, r, z * 4 + x), other


def step_of(k, sign):
    y, r, x, z = place()
    return moved(sign * lax.rem(k, 4), sign * lax.rem(k // 4, 4), lax.rem(r + k // CHIPS, 2))


def remote(src, dst, send_sem, recv_sem, device):
    return pltpu.make_async_remote_copy(
        src_ref=src,
        dst_ref=dst,
        send_sem=send_sem,
        recv_sem=recv_sem,
        device_id=device,
        device_id_type=MESH,
    )


def done(ref, sem):
    pltpu.make_async_copy(ref, ref, sem).wait()


def meet(plane, planes):
    barrier = pltpu.get_barrier_semaphore()
    y, r, x, z = place()

    def greet(device):
        pl.semaphore_signal(barrier, inc=1, device_id=device, device_id_type=MESH)

    if plane:

        @pl.loop(1, GROUP)
        def _(k):
            greet(step_of(k, 1)[0])

        count = GROUP - 1
    else:
        for core in range(2):

            @pl.loop(1, 4)
            def _(d):
                greet(moved(d, 0, core)[0])
                greet(moved(0, d, core)[0])

        greet(moved(0, 0, 1 - r)[0])
        count = 13
    if planes:
        for n in range(1, PLANES):
            greet(plane_shift(n)[0])
        count += PLANES - 1
    pl.semaphore_wait(barrier, count)


def eye(n):
    return lax.broadcasted_iota(jnp.int32, (n, n), 0) == lax.broadcasted_iota(
        jnp.int32, (n, n), 1
    )


def as_row(column):
    return jnp.sum(jnp.where(eye(column.shape[0]), column, 0.0), axis=0, keepdims=True)


def as_column(row_vec):
    return jnp.sum(jnp.where(eye(row_vec.shape[1]), row_vec, 0.0), axis=1, keepdims=True)


def dot(a, b, dims):
    return lax.dot_general(a, b, (dims, ((), ())), preferred_element_type=jnp.float32)


def split_two(values):
    high = values.astype(jnp.bfloat16)
    return high, (values - high.astype(jnp.float32)).astype(jnp.bfloat16)


def picks(positions):
    slots = lax.broadcasted_iota(jnp.int32, (CAP, positions.shape[1]), 0)
    return slots == positions


def as_hot(mask):
    return mask.astype(jnp.float32).astype(jnp.bfloat16)


LEFT = pl.ds(0, HALF)
RIGHT = pl.ds(HALF, HALF)


def spread(d, source, tok_z, tok_x, send_sem, recv_sem):
    y, r, x, z = place()
    return (
        remote(
            source.at[:, LEFT], tok_z.at[d], send_sem.at[0], recv_sem.at[0], moved(0, d, r)[0]
        ),
        remote(
            source.at[:, RIGHT], tok_x.at[d], send_sem.at[1], recv_sem.at[1], moved(d, 0, r)[0]
        ),
    )


def pass_on(tok_z, tok_x, send_sem, recv_sem):
    y, r, x, z = place()
    copies = []
    for n, (d, sign) in enumerate(((1, 1), (3, -1))):
        rows = pl.ds(n * 128, 128)
        for tok, at, device in (
            (tok_z, 2, moved(0, sign, r)[0]),
            (tok_x, 3, moved(sign, 0, r)[0]),
        ):
            copies.append(
                remote(
                    tok.at[d, rows], tok.at[2, rows], send_sem.at[at], recv_sem.at[at], device
                )
            )
    return copies


def near_done(tok_z, tok_x, sem):
    done(tok_z.at[pl.ds(0, 2)], sem.at[0])
    done(tok_x.at[pl.ds(0, 2)], sem.at[1])


def far_done(tok_z, tok_x, sem):
    done(tok_z.at[2], sem.at[2])
    done(tok_x.at[2], sem.at[3])


def is_local(core, offset):
    y, r, x, z = place()
    return (core == r) & (offset == 0)


def send_slots(
    out,
    into,
    there,
    dz,
    dx,
    send_sem,
    recv_left,
    recv_right,
    sign,
    local_sem=None,
    halves=(True, True),
):
    y, r, x, z = place()

    def one(cols, offset, device, recv_sem):
        source, target = out.at[there, dz, dx, :, cols], into.at[r, dz, dx, :, cols]

        @pl.when(jnp.logical_not(is_local(there, offset)))
        def _():
            remote(source, target, send_sem, recv_sem, device).start()

        @pl.when(is_local(there, offset))
        def _():
            if local_sem is None:
                target[...] = source[...]
            else:
                pltpu.make_async_copy(source, target, local_sem).start()

    if halves[0]:
        one(LEFT, dx, moved(sign * dx, 0, there)[0], recv_left)
    if halves[1]:
        one(RIGHT, dz, moved(0, sign * dz, there)[0], recv_right)


def all_slots(ref):
    return ref.at[:, :, :, :, pl.ds(0, 896)]


def line_rows(line, d, axis):
    y, r, x, z = place()
    own = x if axis == 0 else z
    return [
        line[d, pl.ds(core * 4 + lax.rem(own + i, 4), 1), :] for core in range(2) for i in range(4)
    ]


def line_hot(line, d, axis):
    return as_hot(jnp.concatenate([picks(p) for p in line_rows(line, d, axis)], axis=0))


def add_up(mid, line, d, axis):
    if axis == 0:
        rows = mid[:, d, :, :, 0:HALF]
    else:
        rows = mid[:, :, d, :, HALF:D]
    return dot(line_hot(line, d, axis), rows.reshape(8 * CAP, HALF), ((0,), (0,))).astype(
        jnp.bfloat16
    )


def part_copy(d, rows, axis, sign, out, into, send_sem, recv_sem):
    y, r, x, z = place()
    cols = (LEFT, RIGHT)[axis]
    device = moved(sign * axis, sign * (1 - axis), r)[0]
    part = pl.ds(rows, 128)
    return remote(out.at[d, part, cols], into.at[d, part, cols], send_sem, recv_sem, device)


def fold_start(out, into, mid, slot_recv, posz_ref, posx_ref, sems):
    send_sem, recv_sem = sems
    for d in (2, 0, 1, 3):
        for axis, pos in enumerate((posz_ref, posx_ref)):
            if slot_recv is not None:
                done(mid.at[0, 0, :, :, pl.ds(0, 896)], slot_recv.at[4 * axis + d])
            total = add_up(mid, pos, d, axis)
            cols = slice(axis * HALF, axis * HALF + HALF)
            if d == 0:
                into[0, :, cols] = total
                continue
            out[d, :, cols] = total
            if d == 2:
                for rows, sign in ((0, -1), (128, 1)):
                    args = rows, axis, sign, out, into, send_sem.at[0], recv_sem.at[axis]
                    part_copy(2, *args).start()
            else:
                rows, sign = (128, -1) if d == 1 else (0, 1)
                args = rows, axis, sign, out, into, send_sem.at[0], recv_sem.at[2]
                part_copy(d, *args).start()


def fold_end(out, into, sems):
    send_sem, recv_sem = sems
    for axis in range(2):
        cols = slice(axis * HALF, axis * HALF + HALF)
        done(into.at[2, :, (LEFT, RIGHT)[axis]], recv_sem.at[axis])
        for d, rows, sign in ((1, 0, -1), (3, 128, 1)):
            part = slice(rows, rows + 128)
            total = out[d, part, cols].astype(jnp.float32) + into[2, part, cols].astype(jnp.float32)
            out[d, part, cols] = total.astype(jnp.bfloat16)
            args = rows, axis, sign, out, into, send_sem.at[0], recv_sem.at[2]
            part_copy(d, *args).start()


def folded(into, sems):
    done(into.at[pl.ds(0, 2)], sems[1].at[2])
    f32 = jnp.float32
    return into[0].astype(f32) + (into[1].astype(f32) + into[3].astype(f32))


def front_kernel(
    length_ref,
    hidden_ref,
    cot_ref,
    routes_ref,
    prio_ref,
    again_ref,
    mgain_ref,
    wq_ref,
    wk_ref,
    wv_ref,
    wo_ref,
    router_ref,
    cos_ref,
    sin_ref,
    w_hbm,
    normed_ref,
    q_ref,
    k_ref,
    v_ref,
    lse_ref,
    mixed_ref,
    middle_ref,
    routed_ref,
    gates_ref,
    pos_ref,
    posz_ref,
    posx_ref,
    grads_ref,
    w_ref,
    mixed_t,
    posz_out,
    posx_out,
    tok_z,
    tok_x,
    outgoing,
    store_sem,
    w_send,
    w_recv,
    o_send,
    o_recv,
    core_send,
    core_recv,
    kv_send,
    kv_recv,
    first_send,
    first_recv,
    slot_send,
    slot_recv,
    pos_send,
    pos_recv,
):
    y, r, x, z = place()
    f32, bf16 = jnp.float32, jnp.bfloat16
    sibling = moved(0, 0, 1 - r)[0]
    meet(False, True)

    w_ref[r, z, x, :, 0:HALF] = wq_ref[:, 0:HALF]
    w_ref[r, z, x, :, HALF:768] = wk_ref[:, 0:256]
    w_ref[r, z, x, :, 768:D] = wv_ref[:, 0:256]

    @pl.when(y == 0)
    def _():
        w_ref[r, z, x, :, D : D + HALF] = wq_ref[:, HALF:D]

    @pl.when(y == 1)
    def _():
        w_ref[r, z, x, :, D + HALF : D + 768] = wk_ref[:, 256:HALF]
        w_ref[r, z, x, :, D + 768 : 2 * D] = wv_ref[:, 256:HALF]

    @pl.when(y > 1)
    def _():
        own = pl.ds(pl.multiple_of(HALF * (y - 2), HALF), HALF)
        w_ref[r, z, x, :, pl.ds(pl.multiple_of(D + HALF * y, HALF), HALF)] = wo_ref[:, own]

    front, rear = pl.ds(0, HALF), pl.ds(HALF, HALF)

    def quarter(plane, part=None):
        if part is None:
            return pl.ds(pl.multiple_of(D + HALF * plane, HALF), HALF)
        return pl.ds(pl.multiple_of(D + HALF * plane + 256 * part, 256), 256)

    def line_step(d):
        mine_q, mine_o = w_ref.at[r, z, x, :, front], w_ref.at[r, z, x, :, rear]
        return (
            remote(mine_q, mine_q, w_send.at[0], w_recv.at[d], moved(0, d, r)[0]),
            remote(mine_o, mine_o, w_send.at[0], w_recv.at[4 + d], moved(d, 0, r)[0]),
        )

    def cross_step(e, d):
        from_z = w_ref.at[r, lax.rem(z - e + 4, 4), x, :, front]
        from_x = w_ref.at[r, z, lax.rem(x - e + 4, 4), :, rear]
        return (
            remote(from_z, from_z, w_send.at[1], w_recv.at[8 + d], moved(d, 0, r)[0]),
            remote(from_x, from_x, w_send.at[1], w_recv.at[8 + d], moved(0, d, r)[0]),
        )

    def later_line(d):
        left, right = w_ref.at[r, z, x, :, quarter(y, 0)], w_ref.at[r, z, x, :, quarter(y, 1)]
        return (
            remote(left, left, o_send.at[0], o_recv.at[0], moved(0, d, r)[0]),
            remote(right, right, o_send.at[0], o_recv.at[0], moved(d, 0, r)[0]),
        )

    def later_cross(d):
        left, right = w_ref.at[r, :, x, :, quarter(y, 0)], w_ref.at[r, z, :, :, quarter(y, 1)]
        return (
            remote(left, left, o_send.at[1], o_recv.at[1], moved(d, 0, r)[0]),
            remote(right, right, o_send.at[1], o_recv.at[1], moved(0, d, r)[0]),
        )

    def later_plane(n):
        own = w_ref.at[r, :, :, :, quarter(y)]
        return remote(own, own, o_send.at[2], o_recv.at[2], plane_shift(n)[0])

    def later_relay(n):
        device, came_from = plane_shift(1 + 2 * n)[0], plane_shift(3 - 2 * n)[1]
        part = w_ref.at[r, :, :, :, quarter(came_from, n)]
        return remote(part, part, o_send.at[4], o_recv.at[4], device)

    def later_core(n):
        part = w_ref.at[r, :, :, :, quarter(plane_shift(n)[1])]
        return remote(part, part, o_send.at[3], o_recv.at[3], sibling)

    def some(rows, width):
        return w_ref.at[0, pl.ds(0, rows), :, :, pl.ds(0, width)]

    def core_step(d):
        from_x = w_ref.at[r, :, lax.rem(x - d + 4, 4), :, front]
        from_z = w_ref.at[r, lax.rem(z - d + 4, 4), :, :, rear]
        return (
            remote(from_x, from_x, core_send.at[0], core_recv.at[0], sibling),
            remote(from_z, from_z, core_send.at[0], core_recv.at[0], sibling),
        )

    @pl.loop(1, 4)
    def _(d):
        for copy in line_step(d):
            copy.start()

    @pl.loop(1, 4)
    def _(d):
        for copy in cross_step(0, d):
            copy.start()
        for copy in later_line(d):
            copy.start()

    tokens = hidden_ref.shape[0]
    experts_iota = lax.broadcasted_iota(jnp.int32, (EXPERTS, tokens), 0).astype(f32)
    live = r * tokens + lax.broadcasted_iota(jnp.int32, (1, tokens), 1) < length_ref[0]
    routed_to = jnp.zeros((EXPERTS, tokens), f32)
    ranks = jnp.zeros((EXPERTS, tokens), f32)
    prio = prio_ref[...]
    lines = jnp.concatenate([prio[:, 128 * i : 128 * i + 128] for i in range(CHIPS)], axis=0)
    token = lax.broadcasted_iota(jnp.int32, (tokens, CHIPS), 0) // CHIPS
    owner = (token == lax.broadcasted_iota(jnp.int32, (tokens, CHIPS), 1)).astype(f32)
    token = lax.rem(lax.broadcasted_iota(jnp.int32, (tokens, 128), 0), CHIPS)
    lane = lax.broadcasted_iota(jnp.int32, (tokens, 128), 1)
    place_of = lax.rem(lax.broadcasted_iota(jnp.int32, (TOP, 128), 1), TOP)
    place_of = (place_of == lax.broadcasted_iota(jnp.int32, (TOP, 128), 0)).astype(f32)
    priority = jnp.zeros((TOP, tokens), f32)
    for unit, part in ((64.0, lines // 64), (1.0, lax.rem(lines, 64))):
        part = part.astype(f32).astype(bf16)
        rows = dot(owner.astype(bf16), part, ((1,), (0,)))
        rows = jnp.where(lane // TOP == token, rows, 0.0).astype(bf16)
        priority = priority + unit * dot(place_of.astype(bf16), rows, ((1,), (1,)))
    routes = routes_ref[...].astype(f32)
    for j in range(TOP):
        match = experts_iota == routes[j : j + 1, :]
        routed_to = jnp.where(match, 1.0, routed_to)
        ranks = jnp.where(match, priority[j : j + 1, :], ranks)
    far = float(1 << 20)
    ranks = jnp.where((routed_to > 0.0) & live, ranks, far)
    ranks_t = ranks.T
    rows = []
    for e in range(EXPERTS):
        earlier = ranks_t[:, e : e + 1] < ranks[e : e + 1, :]
        rows.append(jnp.sum(earlier.astype(f32), axis=0, keepdims=True))
    slots = jnp.concatenate(rows, axis=0)
    pos = jnp.where((ranks < far) & (slots < CAP), slots, -1.0).astype(jnp.int32)
    pos_ref[...] = pos
    for core in range(2):
        for i in range(4):
            at = core * CHIPS + 4 * i
            posz_out[i, 4 * core : 4 * core + 4, :] = pos[at : at + 4, :]
            for j in range(4):
                posx_out[j, 4 * core + i : 4 * core + i + 1, :] = pos[at + j : at + j + 1, :]
    posz_ref[0] = posz_out[z]
    posx_ref[0] = posx_out[x]
    tok_z[0] = cot_ref[:, 0:HALF]
    tok_x[0] = cot_ref[:, HALF:D]

    def pos_step(d):
        to_z, to_x = lax.rem(z + d, 4), lax.rem(x + d, 4)
        return (
            remote(
                posz_out.at[to_z],
                posz_ref.at[d],
                pos_send.at[0],
                pos_recv.at[0],
                moved(0, d, r)[0],
            ),
            remote(
                posx_out.at[to_x],
                posx_ref.at[d],
                pos_send.at[1],
                pos_recv.at[1],
                moved(d, 0, r)[0],
            ),
        )

    @pl.loop(1, 4)
    def _(d):
        for copy in pos_step(d):
            copy.start()

    done(w_ref.at[0, 0, pl.ds(0, 3), :, pl.ds(0, HALF)], o_recv.at[0])

    @pl.loop(1, 4)
    def _(d):
        for copy in later_cross(d):
            copy.start()

    @pl.loop(1, 4)
    def _(e):
        for copy in line_step(e):
            copy.wait_recv()

        @pl.loop(1, 4)
        def _(d):
            for copy in cross_step(e, d):
                copy.start()

    for d in (1, 3):
        for copy in spread(d, cot_ref, tok_z, tok_x, first_send, first_recv):
            copy.start()

    for copy in core_step(0):
        copy.start()

    def cut_slots(d):
        left = dot(line_hot(posz_ref, d, 0), tok_z[d], ((1,), (0,))).astype(bf16)
        right = dot(line_hot(posx_ref, d, 1), tok_x[d], ((1,), (0,))).astype(bf16)
        sems = slot_send.at[0], slot_recv.at[0], slot_recv.at[0], 1, store_sem.at[1]
        for core in range(2):
            for i in range(4):
                part = slice((core * 4 + i) * CAP, (core * 4 + i + 1) * CAP)
                outgoing[core, d, i, :, 0:HALF] = left[part]
                send_slots(outgoing, grads_ref, core, d, i, *sems, (True, False))
                outgoing[core, i, d, :, HALF:D] = right[part]
                send_slots(outgoing, grads_ref, core, i, d, *sems, (False, True))

    cut_slots(0)

    inputs = hidden_ref[...].astype(f32)
    scale = lax.rsqrt(jnp.mean(inputs * inputs, axis=1, keepdims=True) + epsilon)
    normed_ref[...] = (inputs * scale * again_ref[...]).astype(bf16)

    done(some(3, HALF), o_recv.at[1])

    for n in (1, 3):
        later_plane(n).start()
    later_core(0).start()

    @pl.loop(1, 4)
    def _(d):
        done(some(1, D), w_recv.at[8 + d])
        for copy in core_step(d):
            copy.start()

    near_done(tok_z, tok_x, first_recv)
    for copy in pass_on(tok_z, tok_x, first_send, first_recv):
        copy.start()
    done(posz_ref.at[pl.ds(1, 3)], pos_recv.at[0])
    done(posx_ref.at[pl.ds(1, 3)], pos_recv.at[1])

    @pl.loop(0, 2)
    def _(n):
        cut_slots(1 + 2 * n)

    done(some(4, D), core_recv.at[0])

    here = pl.ds(pl.multiple_of(r * tokens, tokens), tokens)
    cosine, sine = cos_ref[:, here], sin_ref[:, here]

    def projected(first):
        weight = w_ref[:, :, :, :, first : first + HALF].reshape(D, HALF)
        return dot(normed_ref[...], weight, ((1,), (0,))).T

    def turned(rows):
        parts = []
        for h in range(rows.shape[0] // HEAD):
            first, second = rows[HEAD * h : HEAD * h + 32], rows[HEAD * h + 32 : HEAD * h + HEAD]
            parts += [first * cosine - second * sine, second * cosine + first * sine]
        return jnp.concatenate(parts, axis=0).astype(bf16)

    def keys_values(p):
        rows = pl.ds(256 * p, 256)
        return [
            remote(
                ref.at[rows, here],
                ref.at[rows, here],
                kv_send.at[2 * p + n],
                kv_recv.at[2 * p + n],
                sibling,
            )
            for n, ref in enumerate((k_ref, v_ref))
        ]

    def project(p):
        both = projected(D * p + HALF)
        k_ref[256 * p : 256 * p + 256, here] = turned(both[0:256])
        v_ref[256 * p : 256 * p + 256, here] = both[256:512].astype(bf16)
        for copy in keys_values(p):
            copy.start()
        q_ref[HALF * p : HALF * p + HALF, :] = turned(projected(D * p))

    project(0)
    far_done(tok_z, tok_x, first_recv)
    cut_slots(2)
    done(some(4, D), o_recv.at[2])
    for n in range(2):
        later_relay(n).start()
    for n in (1, 3):
        later_core(n).start()
    for copy in keys_values(0):
        copy.wait_recv()

    key_live = lax.broadcasted_iota(jnp.int32, (2 * tokens, 1), 0) < length_ref[0]
    score_scale = HEAD ** (-0.5)

    def attend(g):
        head = pl.ds(pl.multiple_of(g * HEAD, HEAD), HEAD)
        keys, values = k_ref[head, :], v_ref[head, :]
        for j in range(2):
            at = pl.ds(pl.multiple_of((2 * g + j) * HEAD, HEAD), HEAD)
            scores = dot(keys, q_ref[at, :], ((0,), (0,))) * score_scale
            scores = jnp.where(key_live, scores, NEG)
            top = jnp.max(scores, axis=0, keepdims=True)
            weights = jnp.exp(scores - top)
            total = jnp.sum(weights, axis=0, keepdims=True)
            lse_ref[pl.ds(2 * g + j, 1), :] = top + jnp.log(total)
            probs = (weights * (1.0 / total)).astype(bf16)
            mixed_t[at, :] = dot(values, probs, ((1,), (0,))).astype(bf16)

    pl.loop(0, 4)(attend)
    done(some(4, HALF), o_recv.at[4])
    later_core(2).start()
    done(some(4, 2 * D), o_recv.at[3])
    project(1)
    for copy in keys_values(1):
        copy.wait_recv()
    pl.loop(4, 8)(attend)
    mixed_ref[...] = mixed_t[...].T
    weights_out = pltpu.make_async_copy(w_ref, w_hbm, store_sem.at[0])
    weights_out.start()
    w_out = w_ref[:, :, :, :, 2 * D : 3 * D].reshape(D, D)
    middle = hidden_ref[...].astype(f32) + dot(mixed_ref[...], w_out, ((1,), (0,)))
    middle_ref[...] = middle
    scale = lax.rsqrt(jnp.mean(middle * middle, axis=1, keepdims=True) + epsilon)
    routed_ref[...] = (middle * scale * mgain_ref[...]).astype(bf16)
    logits = dot(router_ref[...], routed_ref[...], ((1,), (1,)))
    logits = jnp.where(routed_to > 0.0, logits, -jnp.inf)
    picked = jnp.exp(logits - jnp.max(logits, axis=0, keepdims=True))
    gates_ref[...] = picked / jnp.sum(picked, axis=0, keepdims=True)

    done(all_slots(grads_ref), slot_recv.at[0])
    done(grads_ref.at[0, 0], store_sem.at[1])
    done(all_slots(outgoing), slot_send.at[0])
    done(w_ref.at[0, 0, pl.ds(0, 3), :, pl.ds(0, D)], w_send.at[0])
    done(some(3, D), w_send.at[1])
    done(some(4, D), core_send.at[0])
    done(w_ref.at[0, 0, pl.ds(0, 3), :, pl.ds(0, HALF)], o_send.at[0])
    done(some(3, HALF), o_send.at[1])
    done(some(4, D), o_send.at[2])
    done(some(4, 2 * D), o_send.at[3])
    done(some(4, HALF), o_send.at[4])
    near_done(tok_z, tok_x, first_send)
    far_done(tok_z, tok_x, first_send)
    done(posz_ref.at[pl.ds(1, 3)], pos_send.at[0])
    done(posx_ref.at[pl.ds(1, 3)], pos_send.at[1])
    weights_out.wait()
    for p in range(2):
        for copy in keys_values(p):
            copy.wait_send()


def front(length, *arrays):
    f32, bf16, i32 = jnp.float32, jnp.bfloat16, jnp.int32
    vmem = pl.BlockSpec(memory_space=pltpu.VMEM)
    hbm = pl.BlockSpec(memory_space=pl.ANY)
    shape = jax.ShapeDtypeStruct
    out_shape = (
        shape((2, 4, 4, 32, 3 * D), bf16),
        shape((TOKENS, D), bf16),
        shape((D, TOKENS), bf16),
        shape((HALF, 2 * TOKENS), bf16),
        shape((HALF, 2 * TOKENS), bf16),
        shape((HEADS, TOKENS), f32),
        shape((TOKENS, D), bf16),
        shape((TOKENS, D), f32),
        shape((TOKENS, D), bf16),
        shape((EXPERTS, TOKENS), f32),
        shape((EXPERTS, TOKENS), i32),
        shape((4, 8, TOKENS), i32),
        shape((4, 8, TOKENS), i32),
        shape((2, 4, 4, CAP, D), bf16),
    )
    scratch = [
        pltpu.VMEM((2, 4, 4, 32, 3 * D), bf16),
        pltpu.VMEM((D, TOKENS), bf16),
        pltpu.VMEM((4, 8, TOKENS), i32),
        pltpu.VMEM((4, 8, TOKENS), i32),
        pltpu.VMEM((4, TOKENS, HALF), bf16),
        pltpu.VMEM((4, TOKENS, HALF), bf16),
        pltpu.VMEM((2, 4, 4, CAP, D), bf16),
    ]
    scratch += [pltpu.SemaphoreType.DMA((2,))]
    for count in (12, 5, 1, 4, 4, 1, 2):
        scratch += [pltpu.SemaphoreType.DMA((count,))] * 2
    return pl.pallas_call(
        front_kernel,
        out_shape=out_shape,
        in_specs=[pl.BlockSpec(memory_space=pltpu.SMEM)] + [vmem] * len(arrays),
        out_specs=[hbm] + [vmem] * (len(out_shape) - 2) + [hbm],
        scratch_shapes=scratch,
        compiler_params=pltpu.CompilerParams(
            collective_id=3, has_side_effects=True, vmem_limit_bytes=60 << 20
        ),
        name="front",
    )(length, *arrays)


def turned_back(rows, cosine, sine):
    first, second = rows[0:32], rows[32:64]
    return jnp.concatenate(
        [first * cosine + second * sine, second * cosine - first * sine], axis=0
    )


def rest_kernel(
    length_ref,
    routed_ref,
    pos_ref,
    posz_ref,
    posx_ref,
    gates_ref,
    grads_hbm,
    wg_hbm,
    wu_hbm,
    wd_hbm,
    router_ref,
    middle_ref,
    cot_ref,
    hidden_hbm,
    again_ref,
    mgain_ref,
    normed_hbm,
    mixed_hbm,
    w_hbm,
    q_hbm,
    k_hbm,
    v_hbm,
    lse_ref,
    cos_ref,
    sin_ref,
    hout_ref,
    hgrad_ref,
    again_out,
    mgain_out,
    router_out,
    own_out,
    esum_hbm,
    prod_hbm,
    mid_hbm,
    tok_z,
    tok_x,
    arrived,
    mid,
    parts_in,
    parts_in2,
    gate_out,
    gate_in,
    dot_out,
    dot_in,
    gdot_ref,
    expert_ref,
    relay_in,
    y_in,
    branch_sib,
    normed_sib,
    mixed_sib,
    grad_sib,
    kv_in,
    rs_in,
    rs_in2,
    y_parts,
    small_in,
    small_y_in,
    gain_in,
    gain_y_in,
    router_all,
    load_sem,
    store_sem,
    first_send,
    first_recv,
    slot_send,
    slot_recv,
    back_send,
    back_recv,
    part_send,
    part_recv,
    small_send,
    small_recv,
    c_send,
    c_recv,
    part_send2,
    part_recv2,
    ex_send,
    ex_recv,
    sib_send,
    sib_recv,
    rs_send,
    rs_recv,
    rr_recv,
    rs_send2,
    rs_recv2,
    ys_send,
    ys_recv,
    sm_send,
    sm_recv,
):
    y, r, x, z = place()
    me = r * CHIPS + z * 4 + x
    sibling = moved(0, 0, 1 - r)[0]
    tokens = TOKENS
    f32, bf16 = jnp.float32, jnp.bfloat16

    above, below = plane_shift(1), plane_shift(3)
    opposite = plane_shift(2)[1]
    def relayed(n):
        device = (above, below)[n][0]
        return remote(
            expert_ref.at[0, n], relay_in.at[n], ex_send.at[n], ex_recv.at[n], device
        )

    def direct(n):
        device = (above, below)[n][0]
        return remote(
            expert_ref.at[1 + n, 1 - n],
            y_in.at[n, 1 - n],
            ex_send.at[2 + n],
            ex_recv.at[2 + n],
            device,
        )

    def passed_on(n):
        device, came_from = (above, below)[n][0], (below, above)[n][1]
        part = esum_hbm.at[came_from, n]
        return remote(part, part, ex_send.at[8 + n], ex_recv.at[8 + n], device)

    def to_sibling(at, src, dst):
        return remote(src, dst, sib_send.at[at], sib_recv.at[at], sibling)

    half = pl.ds(pl.multiple_of((1 - r) * HALF, HALF), HALF)
    sib_normed = to_sibling(0, normed_hbm.at[:, half], normed_sib)
    sib_mixed = to_sibling(1, mixed_hbm.at[:, half], mixed_sib)

    meet(True, True)
    sib_mixed.start()
    sib_normed.start()

    def expert_phase(grads_ref, wg_ref, wu_ref, wd_ref, outgoing, parts_out, active, weighted, pre_grads):
        loads = [
            pltpu.make_async_copy(source, target, load_sem.at[n])
            for n, (source, target) in enumerate(
                (
                    (wg_hbm, wg_ref),
                    (wu_hbm, wu_ref),
                    (wd_hbm, wd_ref),
                    (grads_hbm, grads_ref),
                )
            )
        ]
        for load in loads:
            load.start()

        for d in (1, 3):
            for copy in spread(d, routed_ref, tok_z, tok_x, first_send, first_recv):
                copy.start()

        tok_z[0] = routed_ref[:, 0:HALF]
        tok_x[0] = routed_ref[:, HALF:D]

        def send_rows(core, dz, dx, g, halves):
            came = slot_recv.at[2 * g + r]
            sems = slot_send.at[g], came, came, 1, None
            send_slots(outgoing, arrived, core, dz, dx, *sems, halves)

        left = dot(line_hot(posz_ref, 0, 0), tok_z[0], ((1,), (0,))).astype(bf16)
        right = dot(line_hot(posx_ref, 0, 1), tok_x[0], ((1,), (0,))).astype(bf16)
        for core in range(2):
            for i in range(4):
                part = slice((core * 4 + i) * CAP, (core * 4 + i + 1) * CAP)
                outgoing[core, 0, i, :, 0:HALF] = left[part]
                send_rows(core, 0, i, (4 - i) % 4, (True, False))
                outgoing[core, i, 0, :, HALF:D] = right[part]
                send_rows(core, i, 0, i, (False, True))

        def small(k, out, into, sign, base):
            there, dz, dx = k // CHIPS, lax.rem(k // 4, 4), lax.rem(k, 4)
            slot = r * CHIPS + lax.rem(k, CHIPS)
            return remote(
                out.at[k],
                into.at[slot],
                small_send.at[base],
                small_recv.at[base],
                moved(sign * dx, sign * dz, there)[0],
            )

        def own_slot(k):
            return k == r * CHIPS

        near_done(tok_z, tok_x, first_recv)
        for copy in pass_on(tok_z, tok_x, first_send, first_recv):
            copy.start()

        @pl.loop(0, GROUP)
        def _(k):
            there, dz, dx = k // CHIPS, lax.rem(k // 4, 4), lax.rem(k, 4)
            _, expert = moved(dx, dz, there)
            chosen = picks(pos_ref[pl.ds(expert, 1), :])
            gate_col = jnp.sum(
                jnp.where(chosen, gates_ref[pl.ds(expert, 1), :], 0.0), axis=1, keepdims=True
            )
            gate_out[k, 0:1, 0:CAP] = as_row(gate_col)

            @pl.when(own_slot(k))
            def _():
                gate_in[k] = gate_out[k]

            @pl.when(jnp.logical_not(own_slot(k)))
            def _():
                small(k, gate_out, gate_in, 1, 0).start()

        far_done(tok_z, tok_x, first_recv)

        @pl.loop(0, 4)
        def _(g):
            for dx in range(4):
                dz = lax.rem(dx + g, 4)

                @pl.when(dz != 0)
                def _():
                    rows = [
                        picks(posz_ref[dz, pl.ds(core * 4 + lax.rem(x + dx, 4), 1), :])
                        for core in range(2)
                    ]
                    rows = dot(as_hot(jnp.concatenate(rows, axis=0)), tok_z[dz], ((1,), (0,)))
                    for core in range(2):
                        part = slice(core * CAP, core * CAP + CAP)
                        outgoing[core, dz, dx, :, 0:HALF] = rows[part].astype(bf16)
                        send_rows(core, dz, dx, g, (True, False))

                if dx == 0:
                    continue
                rows = [
                    picks(posx_ref[dx, pl.ds(core * 4 + lax.rem(z + dz, 4), 1), :])
                    for core in range(2)
                ]
                rows = dot(as_hot(jnp.concatenate(rows, axis=0)), tok_x[dx], ((1,), (0,)))
                for core in range(2):
                    part = slice(core * CAP, core * CAP + CAP)
                    outgoing[core, dz, dx, :, HALF:D] = rows[part].astype(bf16)
                    send_rows(core, dz, dx, g, (False, True))

        def keep_produced(k):
            core, dz, dx = k // CHIPS, lax.rem(k // 4, 4), lax.rem(k, 4)
            return pltpu.make_async_copy(
                grads_ref.at[core, dz, dx],
                prod_hbm.at[core, dz, dx],
                store_sem.at[lax.rem(dz - dx + 4, 4)],
            )

        for load in loads:
            load.wait()
        done(gate_in.at[pl.ds(0, GROUP - 1)], small_recv.at[0])

        @pl.loop(0, 8)
        def _(c):
            g, core = c // 2, lax.rem(c, 2)

            @pl.when(core == r)
            def _():
                done(arrived.at[0, 0, pl.ds(0, 3)], slot_recv.at[c])

            @pl.when(core != r)
            def _():
                done(arrived.at[0, 0], slot_recv.at[c])

            @pl.when(core == 0)
            def _():
                done(outgoing.at[0, pl.ds(0, 2), :, :, pl.ds(0, 896)], slot_send.at[g])

            rows, gate_cols, grads = [], [], []
            for dx in range(4):
                dz = lax.rem(dx + g, 4)
                k = core * CHIPS + dz * 4 + dx
                rows.append(arrived[core, dz, dx])
                gate_cols.append(as_column(gate_in[k, 0:1, 0:CAP]))
                grads.append(grads_ref[core, dz, dx])
            rows = jnp.concatenate(rows, axis=0)
            gate_cols = jnp.concatenate(gate_cols, axis=0)
            grads = jnp.concatenate(grads, axis=0).astype(f32)
            gate_pre = dot(rows, wg_ref[...], ((1,), (0,)))
            up_pre = dot(rows, wu_ref[...], ((1,), (0,)))
            gate_sig = jax.nn.sigmoid(gate_pre)
            gate_act = gate_pre * gate_sig
            act = (gate_act * up_pre).astype(bf16)
            produced = dot(act, wd_ref[...], ((1,), (0,))).astype(bf16).astype(f32)
            dots = jnp.sum(produced * grads, axis=1, keepdims=True)
            produced_grad = (gate_cols * grads).astype(bf16)
            act_grad = dot(produced_grad, wd_ref[...], ((1,), (1,))).astype(bf16).astype(f32)
            gate_grad = (
                act_grad * up_pre * gate_sig * (1.0 + gate_pre * (1.0 - gate_sig))
            ).astype(bf16)
            up_grad = (act_grad * gate_act).astype(bf16)
            row_grads = dot(gate_grad, wg_ref[...], ((1,), (1,)))
            row_grads = (row_grads + dot(up_grad, wu_ref[...], ((1,), (1,)))).astype(bf16)
            produced = (produced * gate_cols).astype(bf16)
            for dx in range(4):
                dz = lax.rem(dx + g, 4)
                k = core * CHIPS + dz * 4 + dx
                part = slice(dx * CAP, dx * CAP + CAP)
                outgoing[core, dz, dx] = row_grads[part]
                send_slots(
                    outgoing,
                    mid,
                    core,
                    dz,
                    dx,
                    back_send.at[0],
                    back_recv.at[dz],
                    back_recv.at[4 + dx],
                    -1,
                )
                dot_out[k, 0:1, 0:CAP] = as_row(dots[part])

                @pl.when(own_slot(k))
                def _():
                    dot_in[k] = dot_out[k]

                @pl.when(jnp.logical_not(own_slot(k)))
                def _():
                    small(k, dot_out, dot_in, -1, 1).start()

                grads_ref[core, dz, dx] = produced[part]
                keep_produced(k).start()
                active[core, dz, dx] = act[part]
                weighted[core, dz, dx] = produced_grad[part]
                pre_grads[core, dz, dx, :, 0:HALF] = gate_grad[part]
                pre_grads[core, dz, dx, :, HALF:D] = up_grad[part]

        def send_results(g):
            done(prod_hbm.at[0, pl.ds(0, 2)], store_sem.at[g])
            for dx in range(4):
                dz = lax.rem(dx + g, 4)
                for core in range(2):
                    send_slots(
                        prod_hbm,
                        mid_hbm,
                        core,
                        dz,
                        dx,
                        c_send.at[0],
                        c_recv.at[0],
                        c_recv.at[0],
                        -1,
                        load_sem.at[8],
                    )

        send_results(0)

        all_rows = GROUP * CAP

        def quarter_grads(slot, n):
            span = pl.ds(pl.multiple_of(n * 256, 256), 256)
            left = arrived[:, :, :, :, span].reshape(all_rows, 256)
            part = dot(left, pre_grads[...].reshape(all_rows, D), ((0,), (0,))).astype(bf16)
            narrow = pl.ds(pl.multiple_of(n * 128, 128), 128)
            left = active[:, :, :, :, narrow].reshape(all_rows, 128)
            down = dot(left, weighted[...].reshape(all_rows, D), ((0,), (0,))).astype(bf16)
            for h in range(2):
                rows = part[128 * h : 128 * h + 128]
                expert_ref[slot, h, 0:128, :] = rows[:, 0:HALF]
                expert_ref[slot, h, 128:256, :] = rows[:, HALF:D]
                rows = down[64 * h : 64 * h + 64]
                expert_ref[slot, h, 256:320, :] = rows[:, 0:HALF]
                expert_ref[slot, h, 320:384, :] = rows[:, HALF:D]

        quarter_grads(0, opposite)
        for n in range(2):
            relayed(n).start()

        part_sems = part_send, part_recv
        fold_start(parts_out, parts_in, mid, back_recv, posz_ref, posx_ref, part_sems)

        @pl.loop(1, 4)
        def _(slot):
            quarter_grads(slot, lax.rem(y + jnp.where(slot == 1, 1, jnp.where(slot == 2, 3, 0)), 4))

            @pl.when(slot == 1)
            def _():
                fold_end(parts_out, parts_in, part_sems)
                pl.loop(1, 4)(send_results)

        for n in range(2):
            direct(n).start()

        done(dot_in.at[pl.ds(0, GROUP - 1)], small_recv.at[1])

        @pl.loop(0, GROUP)
        def _(k):
            there, dz, dx = k // CHIPS, lax.rem(k // 4, 4), lax.rem(k, 4)
            _, expert = moved(dx, dz, there)
            at = pl.ds(expert, 1)
            dots = as_column(dot_in[k, 0:1, 0:CAP])
            gdot_ref[at, :] = jnp.sum(
                jnp.where(picks(pos_ref[at, :]), dots, 0.0), axis=0, keepdims=True
            )

        hgrad_ref[...] = folded(parts_in, part_sems)
        done(all_slots(outgoing), back_send.at[0])
        done(parts_out.at[pl.ds(0, 3)], part_send.at[0])
        near_done(tok_z, tok_x, first_send)
        far_done(tok_z, tok_x, first_send)
        done(gate_in.at[pl.ds(0, GROUP - 1)], small_send.at[0])
        done(dot_in.at[pl.ds(0, GROUP - 1)], small_send.at[1])

    pl.run_scoped(
        expert_phase,
        pltpu.VMEM((2, 4, 4, CAP, D), bf16),
        pltpu.VMEM((D, HALF), bf16),
        pltpu.VMEM((D, HALF), bf16),
        pltpu.VMEM((HALF, D), bf16),
        pltpu.VMEM((2, 4, 4, CAP, D), bf16),
        pltpu.VMEM((4, tokens, D), bf16),
        pltpu.VMEM((2, 4, 4, CAP, HALF), bf16),
        pltpu.VMEM((2, 4, 4, CAP, D), bf16),
        pltpu.VMEM((2, 4, 4, CAP, D), bf16),
    )

    def finish_phase(w_ref, q_ref, k_ref, v_ref, normed_ref, mixed_ref, hidden_ref, parts_out2, quarter_sum, relay_out, branch_own, mg_t, grad_t, kv_own, kv_out, weight_part, rs_out, y_out, small_out, small_y, gain_out, gain_y):
        loads = [
            pltpu.make_async_copy(source, target, load_sem.at[n])
            for n, (source, target) in enumerate(
                (
                    (w_hbm, w_ref),
                    (mixed_hbm, mixed_ref),
                    (q_hbm, q_ref),
                    (k_hbm, k_ref),
                    (v_hbm, v_ref),
                    (normed_hbm, normed_ref),
                    (hidden_hbm, hidden_ref),
                )
            )
        ]
        for load in loads:
            load.start()

        def weight(first, width):
            return w_ref[:, :, :, :, first : first + width].reshape(D, width)

        def merged(n):
            device = (above, below)[n][0]
            return remote(
                relay_out.at[n], y_in.at[n, n], ex_send.at[4 + n], ex_recv.at[4 + n], device
            )

        def handed(n):
            device = (above, below)[n][0]
            return remote(
                quarter_sum, esum_hbm.at[y], ex_send.at[6 + n], ex_recv.at[6 + n], device
            )

        def sib_keyval(p):
            return to_sibling(3 + p, kv_out.at[p], kv_in.at[p])

        def sib_grads(p, part):
            rows = pl.ds(p * D + part * HALF, HALF)
            return to_sibling(5 + 2 * p + part, grad_t.at[rows], grad_sib.at[rows])

        sib_branch = to_sibling(2, branch_own, branch_sib)

        for n in range(2):
            relayed(n).wait_recv()
            total = relay_in[n].astype(f32) + expert_ref[1 + n, n].astype(f32)
            relay_out[n] = total.astype(bf16)
            merged(n).start()

        gates = gates_ref[...]
        gdot = gdot_ref[...]
        logit_grad = gates * (gdot - jnp.sum(gates * gdot, axis=0, keepdims=True))
        high, rest = split_two(logit_grad)
        router_part = dot(high, routed_ref[...], ((1,), (0,)))
        router_part = router_part + dot(rest, routed_ref[...], ((1,), (0,)))
        routed_grad = dot(high, router_ref[...], ((0,), (0,)))
        routed_grad = routed_grad + dot(rest, router_ref[...], ((0,), (0,)))
        routed_grad = routed_grad + hgrad_ref[...]
        live = (
            r * tokens + lax.broadcasted_iota(jnp.int32, (tokens, 1), 0) < length_ref[0]
        ).astype(f32)
        middle = middle_ref[...]
        scale = lax.rsqrt(jnp.mean(middle * middle, axis=1, keepdims=True) + epsilon)
        rows = middle * scale
        moe_part = jnp.sum(routed_grad * rows, axis=0, keepdims=True)
        scaled = routed_grad * mgain_ref[...]
        inner = jnp.mean(scaled * rows, axis=1, keepdims=True)
        middle_grad = cot_ref[...].astype(f32) * live + scale * (scaled - rows * inner)
        hgrad_ref[...] = middle_grad
        branch_own[...] = middle_grad.astype(bf16)
        sib_branch.start()
        for j in range(8):
            part = slice(128 * j, 128 * j + 128)
            small_out[:, j, :] = router_part[:, part]
            small_out[:, 8 + j, :] = jnp.broadcast_to(moe_part[:, part], (GROUP, 128))

        def tiny(k):
            device, other = step_of(k, 1)
            return remote(small_out.at[other], small_in.at[me], sm_send.at[0], sm_recv.at[0], device)

        @pl.loop(1, GROUP)
        def _(k):
            tiny(k).start()

        small_in[me] = small_out[me]

        loads[0].wait()
        mg_t[...] = dot(weight(2 * D, D), branch_own[...], ((1,), (1,))).astype(bf16)

        mine = pl.ds(pl.multiple_of(r * HALF, HALF), HALF)

        def columns(p):
            return pl.ds(p * D, HALF), pl.ds(p * D + HALF, HALF)

        def first_step(p, d):
            left, right = columns(p)
            return (
                remote(
                    weight_part.at[lax.rem(z + d, 4), :, :, left],
                    rs_in.at[d, :, :, left],
                    rs_send.at[p],
                    rs_recv.at[p],
                    moved(0, d, r)[0],
                ),
                remote(
                    weight_part.at[:, lax.rem(x + d, 4), :, right],
                    rs_in.at[d, :, :, right],
                    rs_send.at[p],
                    rs_recv.at[p],
                    moved(d, 0, r)[0],
                ),
            )

        def second_step(p, d):
            left, right = columns(p)
            return (
                remote(
                    rs_out.at[lax.rem(x + d, 4), :, left],
                    rs_in2.at[d, :, left],
                    rs_send2.at[p],
                    rs_recv2.at[p],
                    moved(d, 0, r)[0],
                ),
                remote(
                    rs_out.at[lax.rem(z + d, 4), :, right],
                    rs_in2.at[d, :, right],
                    rs_send2.at[p],
                    rs_recv2.at[p],
                    moved(0, d, r)[0],
                ),
            )

        def across(p, n):
            cols = pl.ds(p * D, D)
            return remote(
                y_out.at[:, cols],
                y_parts.at[y, :, cols],
                ys_send.at[p],
                ys_recv.at[p],
                plane_shift(n)[0],
            )

        def sum_first(p, total):
            weight_part[:, :, :, p * D : p * D + D] = total.astype(bf16).reshape(4, 4, 32, D)

            @pl.loop(1, 4)
            def _(d):
                for copy in first_step(p, d):
                    copy.start()

        def near_step(p, n, axis, kind):
            cols = columns(p)[axis]
            to, far = ((z, x)[axis] + 1 + 2 * n) % 4, ((z, x)[axis] + 2) % 4
            sign = 1 - 2 * n
            device = moved(sign * axis, sign * (1 - axis), r)[0]
            target, slot = (far, 2) if kind == 0 else (to, 1 + 2 * n)
            half = n if kind != 1 else 1 - n
            blocks = pl.ds(2 * half, 2)
            if axis == 0:
                source = weight_part.at[target, blocks, :, cols]
            else:
                source = weight_part.at[blocks, target, :, cols]
            recv = rr_recv.at[p] if kind == 0 else rs_recv.at[p]
            return remote(source, rs_in.at[slot, blocks, :, cols], rs_send.at[p], recv, device)

        def sum_start(p, total):
            weight_part[:, :, :, p * D : p * D + D] = total.astype(bf16).reshape(4, 4, 32, D)
            for kind in range(2):
                for axis in range(2):
                    for n in range(2):
                        near_step(p, n, axis, kind).start()

        def sum_relay(p):
            done(rs_in.at[2, :, :, pl.ds(p * D, D)], rr_recv.at[p])
            for axis in range(2):
                cols = columns(p)[axis]
                for n in range(2):
                    to = lax.rem((z, x)[axis] + 1 + 2 * n, 4)
                    blocks = pl.ds(2 * n, 2)
                    more = rs_in[2, blocks, :, cols].astype(f32)
                    if axis == 0:
                        mine_too = weight_part[to, blocks, :, cols].astype(f32)
                        weight_part[to, blocks, :, cols] = (more + mine_too).astype(bf16)
                    else:
                        mine_too = weight_part[blocks, to, :, cols].astype(f32)
                        weight_part[blocks, to, :, cols] = (more + mine_too).astype(bf16)
                    near_step(p, n, axis, 2).start()

        def sum_second(p):
            left, right = columns(p)

            count, slots = (3, (1, 2, 3)) if p == 1 else (2, (1, 3))
            done(rs_in.at[pl.ds(0, count), :, :, pl.ds(p * D, D)], rs_recv.at[p])

            total = weight_part[z, :, :, left].astype(f32)
            other = weight_part[:, x, :, right].astype(f32)
            for d in slots:
                total = total + rs_in[d, :, :, left].astype(f32)
                other = other + rs_in[d, :, :, right].astype(f32)
            rs_out[:, :, left] = total.astype(bf16)
            rs_out[:, :, right] = other.astype(bf16)

            @pl.loop(1, 4)
            def _(d):
                for copy in second_step(p, d):
                    copy.start()

        def sum_third(p):
            left, right = columns(p)

            done(rs_in2.at[pl.ds(1, 3), :, pl.ds(p * D, D)], rs_recv2.at[p])

            total = rs_out[x, :, left].astype(f32)
            other = rs_out[z, :, right].astype(f32)
            for d in range(1, 4):
                total = total + rs_in2[d, :, left].astype(f32)
                other = other + rs_in2[d, :, right].astype(f32)
            y_out[:, left] = total.astype(bf16)
            y_out[:, right] = other.astype(bf16)
            y_parts[y, :, left] = total.astype(bf16)
            y_parts[y, :, right] = other.astype(bf16)
            for n in range(1, PLANES):
                across(p, n).start()

        sib_mixed.wait_recv()
        sib_branch.wait_recv()
        loads[1].wait()
        total = dot(mixed_ref[:, mine], branch_own[...], ((0,), (0,)))
        sum_start(2, total + dot(mixed_sib[...], branch_sib[...], ((0,), (0,))))

        key_live = lax.broadcasted_iota(jnp.int32, (2 * tokens, 1), 0) < length_ref[0]
        score_scale = HEAD ** (-0.5)
        here = pl.ds(pl.multiple_of(r * tokens, tokens), tokens)
        cosine, sine = cos_ref[:, here], sin_ref[:, here]
        first_core = r == 0

        def key_head(p, i):
            g = 4 * p + i
            head = pl.ds(pl.multiple_of(g * HEAD, HEAD), HEAD)
            keys, values = k_ref[head, :], v_ref[head, :]
            key_sum, value_sum = None, None
            for j in range(2):
                at = pl.ds(pl.multiple_of((2 * g + j) * HEAD, HEAD), HEAD)
                query, mixed_grad = q_ref[at, :], mg_t[at, :]
                scores = dot(keys, query, ((0,), (0,))) * score_scale
                scores = jnp.where(key_live, scores, NEG)
                probs = jnp.exp(scores - lse_ref[pl.ds(2 * g + j, 1), :])
                prob_grad = dot(values, mixed_grad, ((0,), (0,)))
                value_part = dot(mixed_grad, probs.astype(bf16), ((1,), (1,)))
                inner = jnp.sum(probs * prob_grad, axis=0, keepdims=True)
                score_grad = (probs * (prob_grad - inner)).astype(bf16)
                key_part = dot(query, score_grad, ((1,), (1,)))
                query_grad = dot(keys, score_grad, ((1,), (0,))) * score_scale
                to = pl.ds(pl.multiple_of(p * D + (2 * i + j) * HEAD, HEAD), HEAD)
                grad_t[to, :] = turned_back(query_grad, cosine, sine).astype(bf16)
                key_sum = key_part if key_sum is None else key_sum + key_part
                value_sum = value_part if value_sum is None else value_sum + value_part
            key_sum = key_sum * score_scale
            for n, part in enumerate((key_sum, value_sum)):
                to = pl.ds(pl.multiple_of(256 * n + i * HEAD, HEAD), HEAD)
                kv_own[p, to, :] = jnp.where(first_core, part[:, :tokens], part[:, tokens:])
                away = jnp.where(first_core, part[:, tokens:], part[:, :tokens])
                kv_out[p, to, :] = away.astype(bf16)

        def heads(p, first, last):
            @pl.loop(first, last)
            def _(i):
                key_head(p, i)

        def whole_keyval(p):
            sib_keyval(p).wait_recv()
            for i in range(4):
                rows = slice(HEAD * i, HEAD * i + HEAD)
                total = kv_own[p, rows, :] + kv_in[p, rows, :].astype(f32)
                to = p * D + HALF + HEAD * i
                grad_t[to : to + HEAD, :] = turned_back(total, cosine, sine).astype(bf16)
            total = kv_own[p, 256:512, :] + kv_in[p, 256:512, :].astype(f32)
            grad_t[p * D + HALF + 256 : p * D + D, :] = total.astype(bf16)
            sib_grads(p, 1).start()

        def projections(p):
            rows = slice(p * D, p * D + D)
            for part in range(2):
                sib_grads(p, part).wait_recv()
            total = dot(normed_ref[:, mine], grad_t[rows, :], ((0,), (1,)))
            summing = sum_first if p == 1 else sum_start
            summing(p, total + dot(normed_sib[...], grad_sib[rows, :], ((0,), (1,))))

        def inputs_part(p):
            return dot(grad_t[p * D : p * D + D, :], weight(p * D, D), ((0,), (1,)))

        for load in loads[2:5]:
            load.wait()
        heads(0, 0, 4)
        sib_keyval(0).start()
        sib_grads(0, 0).start()

        sum_relay(2)
        heads(1, 0, 4)
        sib_keyval(1).start()
        sib_grads(1, 0).start()
        for n in range(2):
            direct(n).wait_recv()
            merged(n).wait_recv()
        for n in range(2):
            total = expert_ref[3, n].astype(f32) + (y_in[0, n].astype(f32) + y_in[1, n].astype(f32))
            quarter_sum[n] = total.astype(bf16)
        quarter_out = pltpu.make_async_copy(quarter_sum, esum_hbm.at[y], load_sem.at[9])
        quarter_out.start()
        for n in range(2):
            handed(n).start()

        whole_keyval(0)
        for load in loads[5:]:
            load.wait()
        sib_normed.wait_recv()
        projections(0)
        done(all_slots(mid_hbm), c_recv.at[0])
        done(mid_hbm.at[0, 0], load_sem.at[8])
        results_in = pltpu.make_async_copy(mid_hbm, mid, load_sem.at[10])
        results_in.start()
        whole_keyval(1)
        normed_grad = inputs_part(0)
        projections(1)
        sum_relay(0)
        normed_grad = normed_grad + inputs_part(1)

        inputs = hidden_ref[...].astype(f32)
        scale = lax.rsqrt(jnp.mean(inputs * inputs, axis=1, keepdims=True) + epsilon)
        rows = inputs * scale
        attn_part = jnp.sum(normed_grad * rows, axis=0, keepdims=True)
        for j in range(8):
            gain_out[j : j + 1, :] = attn_part[:, 128 * j : 128 * j + 128]

        def gain(k):
            device, _ = step_of(k, 1)
            return remote(gain_out, gain_in.at[me], sm_send.at[3], sm_recv.at[3], device)

        @pl.loop(1, GROUP)
        def _(k):
            gain(k).start()

        gain_in[me] = gain_out[...]
        scaled = normed_grad * again_ref[...]
        inner = jnp.mean(scaled * rows, axis=1, keepdims=True)
        hgrad_ref[...] += scale * (scaled - rows * inner)

        sum_second(2)
        done(small_in.at[pl.ds(0, GROUP - 1)], sm_recv.at[0])

        def small_across(n):
            device, _ = plane_shift(n)
            return remote(
                small_y, small_y_in.at[y], sm_send.at[1], sm_recv.at[1], device
            )

        small_y[...] = jnp.sum(small_in[...], axis=0)
        small_y_in[y] = small_y[...]
        for n in range(1, PLANES):
            small_across(n).start()

        sum_second(0)
        results_in.wait()
        part_sems = part_send2, part_recv2
        fold_start(parts_out2, parts_in2, mid, None, posz_ref, posx_ref, part_sems)
        for n in range(2):
            handed(n).wait_recv()
            passed_on(n).start()

        done(small_y_in.at[pl.ds(0, 3)], sm_recv.at[1])
        totals = small_y_in[0] + small_y_in[1] + small_y_in[2] + small_y_in[3]
        mgain_out[...] = totals[8:16]
        router_all[me] = totals[0:8]

        def router_row(k):
            device, _ = step_of(k, 1)
            return remote(
                router_all.at[me], router_all.at[me], sm_send.at[2], sm_recv.at[2], device
            )

        @pl.loop(1, GROUP)
        def _(k):
            router_row(k).start()

        sum_second(1)
        fold_end(parts_out2, parts_in2, part_sems)
        sum_third(2)
        sum_third(0)

        done(gain_in.at[pl.ds(0, GROUP - 1)], sm_recv.at[3])

        gain_y[...] = jnp.sum(gain_in[...], axis=0)
        gain_y_in[y] = gain_y[...]

        def gain_across(n):
            device, _ = plane_shift(n)
            return remote(gain_y, gain_y_in.at[y], sm_send.at[4], sm_recv.at[4], device)

        for n in range(1, PLANES):
            gain_across(n).start()

        sum_third(1)

        mixture = folded(parts_in2, part_sems)
        hout_ref[...] = ((middle_ref[...] + mixture) * live).astype(bf16)

        done(gain_y_in.at[pl.ds(0, 3)], sm_recv.at[4])
        again_out[...] = (gain_y_in[0] + gain_y_in[1]) + (gain_y_in[2] + gain_y_in[3])

        done(router_all.at[pl.ds(0, GROUP - 1)], sm_recv.at[2])

        router_out[...] = router_all[...]

        done(all_slots(mid_hbm), c_send.at[0])
        done(parts_out2.at[pl.ds(0, 3)], part_send2.at[0])
        done(small_in.at[pl.ds(0, GROUP - 1)], sm_send.at[0])
        done(small_y_in.at[pl.ds(0, 3)], sm_send.at[1])
        done(router_all.at[pl.ds(0, GROUP - 1)], sm_send.at[2])
        done(gain_in.at[pl.ds(0, GROUP - 1)], sm_send.at[3])
        done(gain_y_in.at[pl.ds(0, 3)], sm_send.at[4])
        for p in range(3):
            done(rs_in.at[pl.ds(1, 3), :, :, pl.ds(p * D, D)], rs_send.at[p])
            done(rs_in2.at[pl.ds(1, 3), :, pl.ds(p * D, D)], rs_send2.at[p])
            done(y_parts.at[pl.ds(0, 3), :, pl.ds(p * D, D)], ys_recv.at[p])
            done(y_parts.at[pl.ds(0, 3), :, pl.ds(p * D, D)], ys_send.at[p])
        for n in range(2):
            for copy in (relayed(n), direct(n), merged(n), handed(n), passed_on(n)):
                copy.wait_send()
        for copy in (sib_normed, sib_mixed, sib_branch):
            copy.wait_send()
        for p in range(2):
            sib_keyval(p).wait_send()
            for part in range(2):
                sib_grads(p, part).wait_send()
        for n in range(2):
            passed_on(n).wait_recv()
        quarter_out.wait()
        own_out[...] = (y_parts[0].astype(f32) + y_parts[1].astype(f32)) + (
            y_parts[2].astype(f32) + y_parts[3].astype(f32)
        )

    pl.run_scoped(
        finish_phase,
        pltpu.VMEM((2, 4, 4, 32, 3 * D), bf16),
        pltpu.VMEM((D, tokens), bf16),
        pltpu.VMEM((HALF, 2 * tokens), bf16),
        pltpu.VMEM((HALF, 2 * tokens), bf16),
        pltpu.VMEM((tokens, D), bf16),
        pltpu.VMEM((tokens, D), bf16),
        pltpu.VMEM((tokens, D), bf16),
        pltpu.VMEM((4, tokens, D), bf16),
        pltpu.VMEM((2, 384, HALF), bf16),
        pltpu.VMEM((2, 384, HALF), bf16),
        pltpu.VMEM((tokens, D), bf16),
        pltpu.VMEM((D, tokens), bf16),
        pltpu.VMEM((2 * D, tokens), bf16),
        pltpu.VMEM((2, HALF, tokens), f32),
        pltpu.VMEM((2, HALF, tokens), bf16),
        pltpu.VMEM((4, 4, 32, 3 * D), bf16),
        pltpu.VMEM((4, 32, 3 * D), bf16),
        pltpu.VMEM((32, 3 * D), bf16),
        pltpu.VMEM((GROUP, 16, 128), f32),
        pltpu.VMEM((16, 128), f32),
        pltpu.VMEM((8, 128), f32),
        pltpu.VMEM((8, 128), f32),
    )


def rest(length, *arrays):
    tokens = TOKENS
    f32, bf16 = jnp.float32, jnp.bfloat16
    vmem = pl.BlockSpec(memory_space=pltpu.VMEM)
    hbm = pl.BlockSpec(memory_space=pl.ANY)
    shape = jax.ShapeDtypeStruct
    sems = pltpu.SemaphoreType.DMA
    scratch = [
        pltpu.VMEM((4, tokens, HALF), bf16),
        pltpu.VMEM((4, tokens, HALF), bf16),
        pltpu.VMEM((2, 4, 4, CAP, D), bf16),
        pltpu.VMEM((2, 4, 4, CAP, D), bf16),
        pltpu.VMEM((4, tokens, D), bf16),
        pltpu.VMEM((4, tokens, D), bf16),
        pltpu.VMEM((GROUP, 8, 128), f32),
        pltpu.VMEM((GROUP, 8, 128), f32),
        pltpu.VMEM((GROUP, 8, 128), f32),
        pltpu.VMEM((GROUP, 8, 128), f32),
        pltpu.VMEM((EXPERTS, tokens), f32),
        pltpu.VMEM((4, 2, 384, HALF), bf16),
        pltpu.VMEM((2, 384, HALF), bf16),
        pltpu.VMEM((2, 2, 384, HALF), bf16),
        pltpu.VMEM((tokens, D), bf16),
        pltpu.VMEM((tokens, HALF), bf16),
        pltpu.VMEM((tokens, HALF), bf16),
        pltpu.VMEM((2 * D, tokens), bf16),
        pltpu.VMEM((2, HALF, tokens), bf16),
        pltpu.VMEM((4, 4, 32, 3 * D), bf16),
        pltpu.VMEM((4, 32, 3 * D), bf16),
        pltpu.VMEM((PLANES, 32, 3 * D), bf16),
        pltpu.VMEM((GROUP, 16, 128), f32),
        pltpu.VMEM((PLANES, 16, 128), f32),
        pltpu.VMEM((GROUP, 8, 128), f32),
        pltpu.VMEM((PLANES, 8, 128), f32),
        pltpu.VMEM((GROUP, 8, 128), f32),
    ]
    for count in (11, 4, 4, 4, 4, 8, 1, 8, 1, 3, 2, 2, 1, 1, 1, 3, 10, 10, 9, 9, 3, 3, 3, 3, 3, 3, 3, 5, 5):
        scratch += [sems((count,))]
    in_specs = [pl.BlockSpec(memory_space=pltpu.SMEM)] + [vmem] * len(arrays)
    for n in (6, 7, 8, 9, 13, 16, 17, 18, 19, 20, 21):
        in_specs[n] = hbm
    return pl.pallas_call(
        rest_kernel,
        out_shape=(
            shape((tokens, D), bf16),
            shape((tokens, D), f32),
            shape((8, 128), f32),
            shape((8, 128), f32),
            shape((GROUP, 8, 128), f32),
            shape((32, 3 * D), f32),
            shape((4, 2, 384, HALF), bf16),
            shape((2, 4, 4, CAP, D), bf16),
            shape((2, 4, 4, CAP, D), bf16),
        ),
        in_specs=in_specs,
        out_specs=[vmem] * 6 + [hbm] * 3,
        scratch_shapes=scratch,
        compiler_params=pltpu.CompilerParams(
            collective_id=2, has_side_effects=True, vmem_limit_bytes=62 << 20
        ),
        name="rest",
    )(length, *arrays)[:7]


def spread_kernel(
    hout_ref,
    hgrad_ref,
    own_ref,
    esum_ref,
    router_ref,
    again_ref,
    mgain_ref,
    hout_out,
    hgrad_out,
    q_out,
    k_out,
    v_out,
    o_out,
    gate_out,
    up_out,
    down_out,
    router_out,
    again_out,
    mgain_out,
    esum,
    gate,
    up,
    down,
    hout,
    hgrad,
    in_sem,
    out_sem,
):
    f32 = jnp.float32

    def quarter_in(n):
        return pltpu.make_async_copy(esum_ref.at[n], esum.at[n], in_sem.at[n])

    def quarter_out(n):
        wide, narrow = pl.ds(256 * n, 256), pl.ds(128 * n, 128)
        return [
            pltpu.make_async_copy(source.at[rows], target.at[0, rows], out_sem.at[3 * n + m])
            for m, (source, target, rows) in enumerate(
                ((gate, gate_out, wide), (up, up_out, wide), (down, down_out, narrow))
            )
        ]

    for n in range(4):
        quarter_in(n).start()
    rows_in = [
        pltpu.make_async_copy(hout_ref, hout, in_sem.at[4]),
        pltpu.make_async_copy(hgrad_ref, hgrad, in_sem.at[5]),
    ]
    rows_out = [
        pltpu.make_async_copy(hout, hout_out, out_sem.at[12]),
        pltpu.make_async_copy(hgrad, hgrad_out, out_sem.at[13]),
    ]
    for copy in rows_in:
        copy.start()
    for n in range(4):
        quarter_in(n).wait()
        for h in range(2):
            rows = pl.ds(256 * n + 128 * h, 128)
            gate[rows, :] = esum[n, h, 0:128, :].astype(f32)
            up[rows, :] = esum[n, h, 128:256, :].astype(f32)
            rows = pl.ds(128 * n + 64 * h, 64)
            down[rows, 0:HALF] = esum[n, h, 256:320, :].astype(f32)
            down[rows, HALF:D] = esum[n, h, 320:384, :].astype(f32)
        for copy in quarter_out(n):
            copy.start()
        if n < 2:
            rows_in[n].wait()
            rows_out[n].start()
    for p in range(2):
        q_out[:, p * HALF : p * HALF + HALF] = own_ref[:, p * D : p * D + HALF]
        k_out[:, p * 256 : p * 256 + 256] = own_ref[:, p * D + HALF : p * D + 768]
        v_out[:, p * 256 : p * 256 + 256] = own_ref[:, p * D + 768 : p * D + D]
    o_out[...] = own_ref[:, 2 * D : 3 * D]
    for j in range(8):
        router_out[:, 128 * j : 128 * j + 128] = router_ref[:, j, :]
    again_out[...] = again_ref[...]
    mgain_out[...] = mgain_ref[...]
    for copy in rows_out:
        copy.wait()
    for n in range(4):
        for copy in quarter_out(n):
            copy.wait()


def spread_out(*arrays):
    f32, bf16 = jnp.float32, jnp.bfloat16
    shape = jax.ShapeDtypeStruct
    vmem = pl.BlockSpec(memory_space=pltpu.VMEM)
    hbm = pl.BlockSpec(memory_space=pl.ANY)
    return pl.pallas_call(
        spread_kernel,
        out_shape=(
            shape((TOKENS, D), bf16),
            shape((TOKENS, D), f32),
            shape((32, D), f32),
            shape((32, HALF), f32),
            shape((32, HALF), f32),
            shape((32, D), f32),
            shape((1, D, HALF), f32),
            shape((1, D, HALF), f32),
            shape((1, HALF, D), f32),
            shape((EXPERTS, D), f32),
            shape((8, 128), f32),
            shape((8, 128), f32),
        ),
        in_specs=[hbm, hbm, vmem, hbm, vmem, vmem, vmem],
        out_specs=[hbm, hbm] + [vmem] * 4 + [hbm] * 3 + [vmem] * 3,
        scratch_shapes=[
            pltpu.VMEM((4, 2, 384, HALF), bf16),
            pltpu.VMEM((D, HALF), f32),
            pltpu.VMEM((D, HALF), f32),
            pltpu.VMEM((HALF, D), f32),
            pltpu.VMEM((TOKENS, D), bf16),
            pltpu.VMEM((TOKENS, D), f32),
            pltpu.SemaphoreType.DMA((6,)),
            pltpu.SemaphoreType.DMA((14,)),
        ],
        compiler_params=pltpu.CompilerParams(vmem_limit_bytes=32 << 20),
        name="spread_out",
    )(*arrays)


def on_device(
    hidden_in,
    cotangent,
    lengths,
    routes,
    priority,
    attn_gain,
    query_weight,
    key_weight,
    value_weight,
    output_weight,
    moe_gain,
    router,
    gate_weight,
    up_weight,
    down_weight,
):
    tok_count = hidden_in.shape[0]
    half_dim = HEAD // 2
    frequency = rotary_base ** (-np.arange(half_dim, dtype=np.float32) / half_dim)
    positions = np.arange(2 * tok_count, dtype=np.float32)
    angles = frequency.astype(np.float32)[:, None] * positions[None, :]
    cosine, sine = jnp.asarray(np.cos(angles)), jnp.asarray(np.sin(angles))
    router_t = router.T
    (
        weights,
        normed,
        queries,
        keys,
        values,
        log_total,
        mixed_rows,
        middle,
        routed,
        gates,
        pos,
        posz,
        posx,
        arrived_grad,
    ) = front(
        lengths,
        hidden_in,
        cotangent,
        routes.T,
        priority,
        attn_gain[None],
        moe_gain[None],
        query_weight,
        key_weight,
        value_weight,
        output_weight,
        router_t,
        cosine,
        sine,
    )
    summed = rest(
        lengths,
        routed,
        pos,
        posz,
        posx,
        gates,
        arrived_grad,
        gate_weight[0],
        up_weight[0],
        down_weight[0],
        router_t,
        middle,
        cotangent,
        hidden_in,
        attn_gain[None],
        moe_gain[None],
        normed,
        mixed_rows,
        weights,
        queries,
        keys,
        values,
        log_total,
        cosine,
        sine,
    )
    hidden_out, hidden_grad, attn_gain_sum, moe_gain_sum, router_sum, own_rows, expert_sum = summed
    (
        hidden_out,
        hidden_grad,
        query_grad,
        key_grad,
        value_grad,
        output_grad,
        gate_grad,
        up_grad,
        down_grad,
        router_grad,
        attn_gain_sum,
        moe_gain_sum,
    ) = spread_out(
        hidden_out, hidden_grad, own_rows, expert_sum, router_sum, attn_gain_sum, moe_gain_sum
    )
    return (
        hidden_out,
        hidden_grad,
        attn_gain_sum.reshape(D),
        query_grad,
        key_grad,
        value_grad,
        output_grad,
        moe_gain_sum.reshape(D),
        router_grad.T,
        gate_grad,
        up_grad,
        down_grad,
    )


def solution(mesh):
    return jax.shard_map(
        on_device,
        mesh=mesh,
        in_specs=(
            P(("dp", "col", "row"), None),
            P(("dp", "col", "row"), None),
            P(("dp", "col")),
            P(("dp", "col", "row"), None),
            P(("dp", "col", "row"), None),
            P(),
            P(("row", "col"), None),
            P(("row", "col"), None),
            P(("row", "col"), None),
            P(("row", "col"), None),
            P(),
            P(),
            P(("row", "col"), None, None),
            P(("row", "col"), None, None),
            P(("row", "col"), None, None),
        ),
        out_specs=(
            P(("dp", "col", "row"), None),
            P(("dp", "col", "row"), None),
            P(),
            P(("row", "col"), None),
            P(("row", "col"), None),
            P(("row", "col"), None),
            P(("row", "col"), None),
            P(),
            P(),
            P(("row", "col"), None, None),
            P(("row", "col"), None, None),
            P(("row", "col"), None, None),
        ),
        check_vma=False,
    )
```

```python
import jax
import jax.numpy as jnp
import numpy as np
from jax import lax
from jax.experimental import pallas as pl
from jax.experimental.pallas import tpu as pltpu
from jax.sharding import PartitionSpec as P

D = 1024
HEADS = 16
HEAD = 64
KV_HEADS = 8
EXPERTS = 32
TOP = 8
CAP = 64


epsilon = 1e-05
rotary_base = 10000.0


MESH = pl.DeviceIdType.MESH
GROUP = 32
PLANES = 4
CHIPS = 16
HALF = D // 2
TOKENS = 256
NEG = -1000000000.0


def place():
    col = lax.axis_index("col")
    return lax.axis_index("dp"), lax.axis_index("row"), lax.rem(col, 4), col // 4


def moved(dx, dz, core):
    y, r, x, z = place()
    col = lax.rem(z + dz + 4, 4) * 4 + lax.rem(x + dx + 4, 4)
    return (y, core, col), core * CHIPS + col


def plane_shift(n):
    y, r, x, z = place()
    other = lax.rem(y + n, PLANES)
    return (other, r, z * 4 + x), other


def step_of(k, sign):
    y, r, x, z = place()
    return moved(sign * lax.rem(k, 4), sign * lax.rem(k // 4, 4), lax.rem(r + k // CHIPS, 2))


def remote(src, dst, send_sem, recv_sem, device):
    return pltpu.make_async_remote_copy(
        src_ref=src,
        dst_ref=dst,
        send_sem=send_sem,
        recv_sem=recv_sem,
        device_id=device,
        device_id_type=MESH,
    )


def done(ref, sem):
    pltpu.make_async_copy(ref, ref, sem).wait()


def meet(plane, planes):
    barrier = pltpu.get_barrier_semaphore()
    y, r, x, z = place()

    def greet(device):
        pl.semaphore_signal(barrier, inc=1, device_id=device, device_id_type=MESH)

    if plane:

        @pl.loop(1, GROUP)
        def _(k):
            greet(step_of(k, 1)[0])

        count = GROUP - 1
    else:
        for core in range(2):

            @pl.loop(1, 4)
            def _(d):
                greet(moved(d, 0, core)[0])
                greet(moved(0, d, core)[0])

        greet(moved(0, 0, 1 - r)[0])
        count = 13
    if planes:
        for n in range(1, PLANES):
            greet(plane_shift(n)[0])
        count += PLANES - 1
    pl.semaphore_wait(barrier, count)


def eye(n):
    return lax.broadcasted_iota(jnp.int32, (n, n), 0) == lax.broadcasted_iota(
        jnp.int32, (n, n), 1
    )


def as_row(column):
    return jnp.sum(jnp.where(eye(column.shape[0]), column, 0.0), axis=0, keepdims=True)


def as_column(row_vec):
    return jnp.sum(jnp.where(eye(row_vec.shape[1]), row_vec, 0.0), axis=1, keepdims=True)


def dot(a, b, dims):
    return lax.dot_general(a, b, (dims, ((), ())), preferred_element_type=jnp.float32)


def split_two(values):
    high = values.astype(jnp.bfloat16)
    return high, (values - high.astype(jnp.float32)).astype(jnp.bfloat16)


def picks(positions):
    slots = lax.broadcasted_iota(jnp.int32, (CAP, positions.shape[1]), 0)
    return slots == positions


def as_hot(mask):
    return mask.astype(jnp.float32).astype(jnp.bfloat16)


LEFT = pl.ds(0, HALF)
RIGHT = pl.ds(HALF, HALF)


def spread(d, source, tok_z, tok_x, send_sem, recv_sem):
    y, r, x, z = place()
    return (
        remote(
            source.at[:, LEFT], tok_z.at[d], send_sem.at[0], recv_sem.at[0], moved(0, d, r)[0]
        ),
        remote(
            source.at[:, RIGHT], tok_x.at[d], send_sem.at[1], recv_sem.at[1], moved(d, 0, r)[0]
        ),
    )


def pass_on(tok_z, tok_x, send_sem, recv_sem):
    y, r, x, z = place()
    copies = []
    for n, (d, sign) in enumerate(((1, 1), (3, -1))):
        rows = pl.ds(n * 128, 128)
        for tok, at, device in (
            (tok_z, 2, moved(0, sign, r)[0]),
            (tok_x, 3, moved(sign, 0, r)[0]),
        ):
            copies.append(
                remote(
                    tok.at[d, rows], tok.at[2, rows], send_sem.at[at], recv_sem.at[at], device
                )
            )
    return copies


def near_done(tok_z, tok_x, sem):
    done(tok_z.at[pl.ds(0, 2)], sem.at[0])
    done(tok_x.at[pl.ds(0, 2)], sem.at[1])


def far_done(tok_z, tok_x, sem):
    done(tok_z.at[2], sem.at[2])
    done(tok_x.at[2], sem.at[3])


def is_local(core, offset):
    y, r, x, z = place()
    return (core == r) & (offset == 0)


def send_slots(
    out,
    into,
    there,
    dz,
    dx,
    send_sem,
    recv_left,
    recv_right,
    sign,
    local_sem=None,
    halves=(True, True),
):
    y, r, x, z = place()

    def one(cols, offset, device, recv_sem):
        source, target = out.at[there, dz, dx, :, cols], into.at[r, dz, dx, :, cols]

        @pl.when(jnp.logical_not(is_local(there, offset)))
        def _():
            remote(source, target, send_sem, recv_sem, device).start()

        @pl.when(is_local(there, offset))
        def _():
            if local_sem is None:
                target[...] = source[...]
            else:
                pltpu.make_async_copy(source, target, local_sem).start()

    if halves[0]:
        one(LEFT, dx, moved(sign * dx, 0, there)[0], recv_left)
    if halves[1]:
        one(RIGHT, dz, moved(0, sign * dz, there)[0], recv_right)


def all_slots(ref):
    return ref.at[:, :, :, :, pl.ds(0, 896)]


def line_rows(line, d, axis):
    y, r, x, z = place()
    own = x if axis == 0 else z
    return [
        line[d, pl.ds(core * 4 + lax.rem(own + i, 4), 1), :] for core in range(2) for i in range(4)
    ]


def line_hot(line, d, axis):
    return as_hot(jnp.concatenate([picks(p) for p in line_rows(line, d, axis)], axis=0))


def add_up(mid, line, d, axis):
    if axis == 0:
        rows = mid[:, d, :, :, 0:HALF]
    else:
        rows = mid[:, :, d, :, HALF:D]
    return dot(line_hot(line, d, axis), rows.reshape(8 * CAP, HALF), ((0,), (0,))).astype(
        jnp.bfloat16
    )


def part_copy(d, rows, axis, sign, out, into, send_sem, recv_sem):
    y, r, x, z = place()
    cols = (LEFT, RIGHT)[axis]
    device = moved(sign * axis, sign * (1 - axis), r)[0]
    part = pl.ds(rows, 128)
    return remote(out.at[d, part, cols], into.at[d, part, cols], send_sem, recv_sem, device)


def fold_start(out, into, mid, slot_recv, posz_ref, posx_ref, sems):
    send_sem, recv_sem = sems
    for d in (2, 0, 1, 3):
        for axis, pos in enumerate((posz_ref, posx_ref)):
            if slot_recv is not None:
                done(mid.at[0, 0, :, :, pl.ds(0, 896)], slot_recv.at[4 * axis + d])
            total = add_up(mid, pos, d, axis)
            cols = slice(axis * HALF, axis * HALF + HALF)
            if d == 0:
                into[0, :, cols] = total
                continue
            out[d, :, cols] = total
            if d == 2:
                for rows, sign in ((0, -1), (128, 1)):
                    args = rows, axis, sign, out, into, send_sem.at[0], recv_sem.at[axis]
                    part_copy(2, *args).start()
            else:
                rows, sign = (128, -1) if d == 1 else (0, 1)
                args = rows, axis, sign, out, into, send_sem.at[0], recv_sem.at[2]
                part_copy(d, *args).start()


def fold_end(out, into, sems):
    send_sem, recv_sem = sems
    for axis in range(2):
        cols = slice(axis * HALF, axis * HALF + HALF)
        done(into.at[2, :, (LEFT, RIGHT)[axis]], recv_sem.at[axis])
        for d, rows, sign in ((1, 0, -1), (3, 128, 1)):
            part = slice(rows, rows + 128)
            total = out[d, part, cols].astype(jnp.float32) + into[2, part, cols].astype(jnp.float32)
            out[d, part, cols] = total.astype(jnp.bfloat16)
            args = rows, axis, sign, out, into, send_sem.at[0], recv_sem.at[2]
            part_copy(d, *args).start()


def folded(into, sems):
    done(into.at[pl.ds(0, 2)], sems[1].at[2])
    f32 = jnp.float32
    return into[0].astype(f32) + (into[1].astype(f32) + into[3].astype(f32))


def front_kernel(
    length_ref,
    hidden_ref,
    cot_ref,
    routes_ref,
    prio_ref,
    again_ref,
    mgain_ref,
    wq_ref,
    wk_ref,
    wv_ref,
    wo_ref,
    router_ref,
    cos_ref,
    sin_ref,
    w_hbm,
    normed_ref,
    q_ref,
    k_ref,
    v_ref,
    lse_ref,
    mixed_ref,
    middle_ref,
    routed_ref,
    gates_ref,
    pos_ref,
    posz_ref,
    posx_ref,
    grads_ref,
    w_ref,
    mixed_t,
    posz_out,
    posx_out,
    tok_z,
    tok_x,
    outgoing,
    store_sem,
    w_send,
    w_recv,
    o_send,
    o_recv,
    core_send,
    core_recv,
    kv_send,
    kv_recv,
    first_send,
    first_recv,
    slot_send,
    slot_recv,
    pos_send,
    pos_recv,
):
    y, r, x, z = place()
    f32, bf16 = jnp.float32, jnp.bfloat16
    sibling = moved(0, 0, 1 - r)[0]
    meet(False, True)

    w_ref[r, z, x, :, 0:HALF] = wq_ref[:, 0:HALF]
    w_ref[r, z, x, :, HALF:768] = wk_ref[:, 0:256]
    w_ref[r, z, x, :, 768:D] = wv_ref[:, 0:256]

    @pl.when(y == 0)
    def _():
        w_ref[r, z, x, :, D : D + HALF] = wq_ref[:, HALF:D]

    @pl.when(y == 1)
    def _():
        w_ref[r, z, x, :, D + HALF : D + 768] = wk_ref[:, 256:HALF]
        w_ref[r, z, x, :, D + 768 : 2 * D] = wv_ref[:, 256:HALF]

    @pl.when(y > 1)
    def _():
        own = pl.ds(pl.multiple_of(HALF * (y - 2), HALF), HALF)
        w_ref[r, z, x, :, pl.ds(pl.multiple_of(D + HALF * y, HALF), HALF)] = wo_ref[:, own]

    front, rear = pl.ds(0, HALF), pl.ds(HALF, HALF)

    def quarter(plane, part=None):
        if part is None:
            return pl.ds(pl.multiple_of(D + HALF * plane, HALF), HALF)
        return pl.ds(pl.multiple_of(D + HALF * plane + 256 * part, 256), 256)

    def line_step(d):
        mine_q, mine_o = w_ref.at[r, z, x, :, front], w_ref.at[r, z, x, :, rear]
        return (
            remote(mine_q, mine_q, w_send.at[0], w_recv.at[d], moved(0, d, r)[0]),
            remote(mine_o, mine_o, w_send.at[0], w_recv.at[4 + d], moved(d, 0, r)[0]),
        )

    def cross_step(e, d):
        from_z = w_ref.at[r, lax.rem(z - e + 4, 4), x, :, front]
        from_x = w_ref.at[r, z, lax.rem(x - e + 4, 4), :, rear]
        return (
            remote(from_z, from_z, w_send.at[1], w_recv.at[8 + d], moved(d, 0, r)[0]),
            remote(from_x, from_x, w_send.at[1], w_recv.at[8 + d], moved(0, d, r)[0]),
        )

    def later_line(d):
        left, right = w_ref.at[r, z, x, :, quarter(y, 0)], w_ref.at[r, z, x, :, quarter(y, 1)]
        return (
            remote(left, left, o_send.at[0], o_recv.at[0], moved(0, d, r)[0]),
            remote(right, right, o_send.at[0], o_recv.at[0], moved(d, 0, r)[0]),
        )

    def later_cross(d):
        left, right = w_ref.at[r, :, x, :, quarter(y, 0)], w_ref.at[r, z, :, :, quarter(y, 1)]
        return (
            remote(left, left, o_send.at[1], o_recv.at[1], moved(d, 0, r)[0]),
            remote(right, right, o_send.at[1], o_recv.at[1], moved(0, d, r)[0]),
        )

    def later_plane(n):
        own = w_ref.at[r, :, :, :, quarter(y)]
        return remote(own, own, o_send.at[2], o_recv.at[2], plane_shift(n)[0])

    def later_relay(n):
        device, came_from = plane_shift(1 + 2 * n)[0], plane_shift(3 - 2 * n)[1]
        part = w_ref.at[r, :, :, :, quarter(came_from, n)]
        return remote(part, part, o_send.at[4], o_recv.at[4], device)

    def later_core(n):
        part = w_ref.at[r, :, :, :, quarter(plane_shift(n)[1])]
        return remote(part, part, o_send.at[3], o_recv.at[3], sibling)

    def some(rows, width):
        return w_ref.at[0, pl.ds(0, rows), :, :, pl.ds(0, width)]

    def core_step(d):
        from_x = w_ref.at[r, :, lax.rem(x - d + 4, 4), :, front]
        from_z = w_ref.at[r, lax.rem(z - d + 4, 4), :, :, rear]
        return (
            remote(from_x, from_x, core_send.at[0], core_recv.at[0], sibling),
            remote(from_z, from_z, core_send.at[0], core_recv.at[0], sibling),
        )

    @pl.loop(1, 4)
    def _(d):
        for copy in line_step(d):
            copy.start()

    @pl.loop(1, 4)
    def _(d):
        for copy in cross_step(0, d):
            copy.start()
        for copy in later_line(d):
            copy.start()

    tokens = hidden_ref.shape[0]
    experts_iota = lax.broadcasted_iota(jnp.int32, (EXPERTS, tokens), 0).astype(f32)
    live = r * tokens + lax.broadcasted_iota(jnp.int32, (1, tokens), 1) < length_ref[0]
    routed_to = jnp.zeros((EXPERTS, tokens), f32)
    ranks = jnp.zeros((EXPERTS, tokens), f32)
    prio = prio_ref[...]
    lines = jnp.concatenate([prio[:, 128 * i : 128 * i + 128] for i in range(CHIPS)], axis=0)
    token = lax.broadcasted_iota(jnp.int32, (tokens, CHIPS), 0) // CHIPS
    owner = (token == lax.broadcasted_iota(jnp.int32, (tokens, CHIPS), 1)).astype(f32)
    token = lax.rem(lax.broadcasted_iota(jnp.int32, (tokens, 128), 0), CHIPS)
    lane = lax.broadcasted_iota(jnp.int32, (tokens, 128), 1)
    place_of = lax.rem(lax.broadcasted_iota(jnp.int32, (TOP, 128), 1), TOP)
    place_of = (place_of == lax.broadcasted_iota(jnp.int32, (TOP, 128), 0)).astype(f32)
    priority = jnp.zeros((TOP, tokens), f32)
    for unit, part in ((64.0, lines // 64), (1.0, lax.rem(lines, 64))):
        part = part.astype(f32).astype(bf16)
        rows = dot(owner.astype(bf16), part, ((1,), (0,)))
        rows = jnp.where(lane // TOP == token, rows, 0.0).astype(bf16)
        priority = priority + unit * dot(place_of.astype(bf16), rows, ((1,), (1,)))
    routes = routes_ref[...].astype(f32)
    for j in range(TOP):
        match = experts_iota == routes[j : j + 1, :]
        routed_to = jnp.where(match, 1.0, routed_to)
        ranks = jnp.where(match, priority[j : j + 1, :], ranks)
    far = float(1 << 20)
    ranks = jnp.where((routed_to > 0.0) & live, ranks, far)
    ranks_t = ranks.T
    rows = []
    for e in range(EXPERTS):
        earlier = ranks_t[:, e : e + 1] < ranks[e : e + 1, :]
        rows.append(jnp.sum(earlier.astype(f32), axis=0, keepdims=True))
    slots = jnp.concatenate(rows, axis=0)
    pos = jnp.where((ranks < far) & (slots < CAP), slots, -1.0).astype(jnp.int32)
    pos_ref[...] = pos
    for core in range(2):
        for i in range(4):
            at = core * CHIPS + 4 * i
            posz_out[i, 4 * core : 4 * core + 4, :] = pos[at : at + 4, :]
            for j in range(4):
                posx_out[j, 4 * core + i : 4 * core + i + 1, :] = pos[at + j : at + j + 1, :]
    posz_ref[0] = posz_out[z]
    posx_ref[0] = posx_out[x]
    tok_z[0] = cot_ref[:, 0:HALF]
    tok_x[0] = cot_ref[:, HALF:D]

    def pos_step(d):
        to_z, to_x = lax.rem(z + d, 4), lax.rem(x + d, 4)
        return (
            remote(
                posz_out.at[to_z],
                posz_ref.at[d],
                pos_send.at[0],
                pos_recv.at[0],
                moved(0, d, r)[0],
            ),
            remote(
                posx_out.at[to_x],
                posx_ref.at[d],
                pos_send.at[1],
                pos_recv.at[1],
                moved(d, 0, r)[0],
            ),
        )

    @pl.loop(1, 4)
    def _(d):
        for copy in pos_step(d):
            copy.start()

    done(w_ref.at[0, 0, pl.ds(0, 3), :, pl.ds(0, HALF)], o_recv.at[0])

    @pl.loop(1, 4)
    def _(d):
        for copy in later_cross(d):
            copy.start()

    @pl.loop(1, 4)
    def _(e):
        for copy in line_step(e):
            copy.wait_recv()

        @pl.loop(1, 4)
        def _(d):
            for copy in cross_step(e, d):
                copy.start()

    for d in (1, 3):
        for copy in spread(d, cot_ref, tok_z, tok_x, first_send, first_recv):
            copy.start()

    for copy in core_step(0):
        copy.start()

    def cut_slots(d):
        left = dot(line_hot(posz_ref, d, 0), tok_z[d], ((1,), (0,))).astype(bf16)
        right = dot(line_hot(posx_ref, d, 1), tok_x[d], ((1,), (0,))).astype(bf16)
        sems = slot_send.at[0], slot_recv.at[0], slot_recv.at[0], 1, store_sem.at[1]
        for core in range(2):
            for i in range(4):
                part = slice((core * 4 + i) * CAP, (core * 4 + i + 1) * CAP)
                outgoing[core, d, i, :, 0:HALF] = left[part]
                send_slots(outgoing, grads_ref, core, d, i, *sems, (True, False))
                outgoing[core, i, d, :, HALF:D] = right[part]
                send_slots(outgoing, grads_ref, core, i, d, *sems, (False, True))

    cut_slots(0)

    inputs = hidden_ref[...].astype(f32)
    scale = lax.rsqrt(jnp.mean(inputs * inputs, axis=1, keepdims=True) + epsilon)
    normed_ref[...] = (inputs * scale * again_ref[...]).astype(bf16)

    done(some(3, HALF), o_recv.at[1])

    for n in (1, 3):
        later_plane(n).start()
    later_core(0).start()

    @pl.loop(1, 4)
    def _(d):
        done(some(1, D), w_recv.at[8 + d])
        for copy in core_step(d):
            copy.start()

    near_done(tok_z, tok_x, first_recv)
    for copy in pass_on(tok_z, tok_x, first_send, first_recv):
        copy.start()
    done(posz_ref.at[pl.ds(1, 3)], pos_recv.at[0])
    done(posx_ref.at[pl.ds(1, 3)], pos_recv.at[1])

    @pl.loop(0, 2)
    def _(n):
        cut_slots(1 + 2 * n)

    done(some(4, D), core_recv.at[0])

    here = pl.ds(pl.multiple_of(r * tokens, tokens), tokens)
    cosine, sine = cos_ref[:, here], sin_ref[:, here]

    def projected(first):
        weight = w_ref[:, :, :, :, first : first + HALF].reshape(D, HALF)
        return dot(normed_ref[...], weight, ((1,), (0,))).T

    def turned(rows):
        parts = []
        for h in range(rows.shape[0] // HEAD):
            first, second = rows[HEAD * h : HEAD * h + 32], rows[HEAD * h + 32 : HEAD * h + HEAD]
            parts += [first * cosine - second * sine, second * cosine + first * sine]
        return jnp.concatenate(parts, axis=0).astype(bf16)

    def keys_values(p):
        rows = pl.ds(256 * p, 256)
        return [
            remote(
                ref.at[rows, here],
                ref.at[rows, here],
                kv_send.at[2 * p + n],
                kv_recv.at[2 * p + n],
                sibling,
            )
            for n, ref in enumerate((k_ref, v_ref))
        ]

    def project(p):
        both = projected(D * p + HALF)
        k_ref[256 * p : 256 * p + 256, here] = turned(both[0:256])
        v_ref[256 * p : 256 * p + 256, here] = both[256:512].astype(bf16)
        for copy in keys_values(p):
            copy.start()
        q_ref[HALF * p : HALF * p + HALF, :] = turned(projected(D * p))

    project(0)
    far_done(tok_z, tok_x, first_recv)
    cut_slots(2)
    done(some(4, D), o_recv.at[2])
    for n in range(2):
        later_relay(n).start()
    for n in (1, 3):
        later_core(n).start()
    for copy in keys_values(0):
        copy.wait_recv()

    key_live = lax.broadcasted_iota(jnp.int32, (2 * tokens, 1), 0) < length_ref[0]
    score_scale = HEAD ** (-0.5)

    def attend(g):
        head = pl.ds(pl.multiple_of(g * HEAD, HEAD), HEAD)
        keys, values = k_ref[head, :], v_ref[head, :]
        for j in range(2):
            at = pl.ds(pl.multiple_of((2 * g + j) * HEAD, HEAD), HEAD)
            scores = dot(keys, q_ref[at, :], ((0,), (0,))) * score_scale
            scores = jnp.where(key_live, scores, NEG)
            top = jnp.max(scores, axis=0, keepdims=True)
            weights = jnp.exp(scores - top)
            total = jnp.sum(weights, axis=0, keepdims=True)
            lse_ref[pl.ds(2 * g + j, 1), :] = top + jnp.log(total)
            probs = (weights * (1.0 / total)).astype(bf16)
            mixed_t[at, :] = dot(values, probs, ((1,), (0,))).astype(bf16)

    pl.loop(0, 4)(attend)
    done(some(4, HALF), o_recv.at[4])
    later_core(2).start()
    done(some(4, 2 * D), o_recv.at[3])
    project(1)
    for copy in keys_values(1):
        copy.wait_recv()
    pl.loop(4, 8)(attend)
    mixed_ref[...] = mixed_t[...].T
    weights_out = pltpu.make_async_copy(w_ref, w_hbm, store_sem.at[0])
    weights_out.start()
    w_out = w_ref[:, :, :, :, 2 * D : 3 * D].reshape(D, D)
    middle = hidden_ref[...].astype(f32) + dot(mixed_ref[...], w_out, ((1,), (0,)))
    middle_ref[...] = middle
    scale = lax.rsqrt(jnp.mean(middle * middle, axis=1, keepdims=True) + epsilon)
    routed_ref[...] = (middle * scale * mgain_ref[...]).astype(bf16)
    logits = dot(router_ref[...], routed_ref[...], ((1,), (1,)))
    logits = jnp.where(routed_to > 0.0, logits, -jnp.inf)
    picked = jnp.exp(logits - jnp.max(logits, axis=0, keepdims=True))
    gates_ref[...] = picked / jnp.sum(picked, axis=0, keepdims=True)

    done(all_slots(grads_ref), slot_recv.at[0])
    done(grads_ref.at[0, 0], store_sem.at[1])
    done(all_slots(outgoing), slot_send.at[0])
    done(w_ref.at[0, 0, pl.ds(0, 3), :, pl.ds(0, D)], w_send.at[0])
    done(some(3, D), w_send.at[1])
    done(some(4, D), core_send.at[0])
    done(w_ref.at[0, 0, pl.ds(0, 3), :, pl.ds(0, HALF)], o_send.at[0])
    done(some(3, HALF), o_send.at[1])
    done(some(4, D), o_send.at[2])
    done(some(4, 2 * D), o_send.at[3])
    done(some(4, HALF), o_send.at[4])
    near_done(tok_z, tok_x, first_send)
    far_done(tok_z, tok_x, first_send)
    done(posz_ref.at[pl.ds(1, 3)], pos_send.at[0])
    done(posx_ref.at[pl.ds(1, 3)], pos_send.at[1])
    weights_out.wait()
    for p in range(2):
        for copy in keys_values(p):
            copy.wait_send()


def front(length, *arrays):
    f32, bf16, i32 = jnp.float32, jnp.bfloat16, jnp.int32
    vmem = pl.BlockSpec(memory_space=pltpu.VMEM)
    hbm = pl.BlockSpec(memory_space=pl.ANY)
    shape = jax.ShapeDtypeStruct
    out_shape = (
        shape((2, 4, 4, 32, 3 * D), bf16),
        shape((TOKENS, D), bf16),
        shape((D, TOKENS), bf16),
        shape((HALF, 2 * TOKENS), bf16),
        shape((HALF, 2 * TOKENS), bf16),
        shape((HEADS, TOKENS), f32),
        shape((TOKENS, D), bf16),
        shape((TOKENS, D), f32),
        shape((TOKENS, D), bf16),
        shape((EXPERTS, TOKENS), f32),
        shape((EXPERTS, TOKENS), i32),
        shape((4, 8, TOKENS), i32),
        shape((4, 8, TOKENS), i32),
        shape((2, 4, 4, CAP, D), bf16),
    )
    scratch = [
        pltpu.VMEM((2, 4, 4, 32, 3 * D), bf16),
        pltpu.VMEM((D, TOKENS), bf16),
        pltpu.VMEM((4, 8, TOKENS), i32),
        pltpu.VMEM((4, 8, TOKENS), i32),
        pltpu.VMEM((4, TOKENS, HALF), bf16),
        pltpu.VMEM((4, TOKENS, HALF), bf16),
        pltpu.VMEM((2, 4, 4, CAP, D), bf16),
    ]
    scratch += [pltpu.SemaphoreType.DMA((2,))]
    for count in (12, 5, 1, 4, 4, 1, 2):
        scratch += [pltpu.SemaphoreType.DMA((count,))] * 2
    return pl.pallas_call(
        front_kernel,
        out_shape=out_shape,
        in_specs=[pl.BlockSpec(memory_space=pltpu.SMEM)] + [vmem] * len(arrays),
        out_specs=[hbm] + [vmem] * (len(out_shape) - 2) + [hbm],
        scratch_shapes=scratch,
        compiler_params=pltpu.CompilerParams(
            collective_id=3, has_side_effects=True, vmem_limit_bytes=60 << 20
        ),
        name="front",
    )(length, *arrays)


def turned_back(rows, cosine, sine):
    first, second = rows[0:32], rows[32:64]
    return jnp.concatenate(
        [first * cosine + second * sine, second * cosine - first * sine], axis=0
    )


def rest_kernel(
    length_ref,
    routed_ref,
    pos_ref,
    posz_ref,
    posx_ref,
    gates_ref,
    grads_hbm,
    wg_hbm,
    wu_hbm,
    wd_hbm,
    router_ref,
    middle_ref,
    cot_ref,
    hidden_hbm,
    again_ref,
    mgain_ref,
    normed_hbm,
    mixed_hbm,
    w_hbm,
    q_hbm,
    k_hbm,
    v_hbm,
    lse_ref,
    cos_ref,
    sin_ref,
    hout_ref,
    hgrad_ref,
    again_out,
    mgain_out,
    router_out,
    own_out,
    esum_hbm,
    prod_hbm,
    mid_hbm,
    tok_z,
    tok_x,
    arrived,
    mid,
    parts_in,
    parts_in2,
    gate_out,
    gate_in,
    dot_out,
    dot_in,
    gdot_ref,
    expert_ref,
    relay_in,
    y_in,
    branch_sib,
    normed_sib,
    mixed_sib,
    grad_sib,
    kv_in,
    rs_in,
    rs_in2,
    y_parts,
    small_in,
    small_y_in,
    gain_in,
    gain_y_in,
    router_all,
    load_sem,
    store_sem,
    first_send,
    first_recv,
    slot_send,
    slot_recv,
    back_send,
    back_recv,
    part_send,
    part_recv,
    small_send,
    small_recv,
    c_send,
    c_recv,
    part_send2,
    part_recv2,
    ex_send,
    ex_recv,
    sib_send,
    sib_recv,
    rs_send,
    rs_recv,
    rs_send2,
    rs_recv2,
    ys_send,
    ys_recv,
    sm_send,
    sm_recv,
):
    y, r, x, z = place()
    me = r * CHIPS + z * 4 + x
    sibling = moved(0, 0, 1 - r)[0]
    tokens = TOKENS
    f32, bf16 = jnp.float32, jnp.bfloat16

    above, below = plane_shift(1), plane_shift(3)
    opposite = plane_shift(2)[1]
    def relayed(n):
        device = (above, below)[n][0]
        return remote(
            expert_ref.at[0, n], relay_in.at[n], ex_send.at[n], ex_recv.at[n], device
        )

    def direct(n):
        device = (above, below)[n][0]
        return remote(
            expert_ref.at[1 + n, 1 - n],
            y_in.at[n, 1 - n],
            ex_send.at[2 + n],
            ex_recv.at[2 + n],
            device,
        )

    def passed_on(n):
        device, came_from = (above, below)[n][0], (below, above)[n][1]
        part = esum_hbm.at[came_from, n]
        return remote(part, part, ex_send.at[8 + n], ex_recv.at[8 + n], device)

    def to_sibling(at, src, dst):
        return remote(src, dst, sib_send.at[at], sib_recv.at[at], sibling)

    half = pl.ds(pl.multiple_of((1 - r) * HALF, HALF), HALF)
    sib_normed = to_sibling(0, normed_hbm.at[:, half], normed_sib)
    sib_mixed = to_sibling(1, mixed_hbm.at[:, half], mixed_sib)

    meet(True, True)
    sib_mixed.start()
    sib_normed.start()

    def expert_phase(grads_ref, wg_ref, wu_ref, wd_ref, outgoing, parts_out, active, weighted, pre_grads):
        loads = [
            pltpu.make_async_copy(source, target, load_sem.at[n])
            for n, (source, target) in enumerate(
                (
                    (wg_hbm, wg_ref),
                    (wu_hbm, wu_ref),
                    (wd_hbm, wd_ref),
                    (grads_hbm, grads_ref),
                )
            )
        ]
        for load in loads:
            load.start()

        for d in (1, 3):
            for copy in spread(d, routed_ref, tok_z, tok_x, first_send, first_recv):
                copy.start()

        tok_z[0] = routed_ref[:, 0:HALF]
        tok_x[0] = routed_ref[:, HALF:D]

        def send_rows(core, dz, dx, g, halves):
            came = slot_recv.at[2 * g + r]
            sems = slot_send.at[g], came, came, 1, None
            send_slots(outgoing, arrived, core, dz, dx, *sems, halves)

        left = dot(line_hot(posz_ref, 0, 0), tok_z[0], ((1,), (0,))).astype(bf16)
        right = dot(line_hot(posx_ref, 0, 1), tok_x[0], ((1,), (0,))).astype(bf16)
        for core in range(2):
            for i in range(4):
                part = slice((core * 4 + i) * CAP, (core * 4 + i + 1) * CAP)
                outgoing[core, 0, i, :, 0:HALF] = left[part]
                send_rows(core, 0, i, (4 - i) % 4, (True, False))
                outgoing[core, i, 0, :, HALF:D] = right[part]
                send_rows(core, i, 0, i, (False, True))

        def small(k, out, into, sign, base):
            there, dz, dx = k // CHIPS, lax.rem(k // 4, 4), lax.rem(k, 4)
            slot = r * CHIPS + lax.rem(k, CHIPS)
            return remote(
                out.at[k],
                into.at[slot],
                small_send.at[base],
                small_recv.at[base],
                moved(sign * dx, sign * dz, there)[0],
            )

        def own_slot(k):
            return k == r * CHIPS

        near_done(tok_z, tok_x, first_recv)
        for copy in pass_on(tok_z, tok_x, first_send, first_recv):
            copy.start()

        @pl.loop(0, GROUP)
        def _(k):
            there, dz, dx = k // CHIPS, lax.rem(k // 4, 4), lax.rem(k, 4)
            _, expert = moved(dx, dz, there)
            chosen = picks(pos_ref[pl.ds(expert, 1), :])
            gate_col = jnp.sum(
                jnp.where(chosen, gates_ref[pl.ds(expert, 1), :], 0.0), axis=1, keepdims=True
            )
            gate_out[k, 0:1, 0:CAP] = as_row(gate_col)

            @pl.when(own_slot(k))
            def _():
                gate_in[k] = gate_out[k]

            @pl.when(jnp.logical_not(own_slot(k)))
            def _():
                small(k, gate_out, gate_in, 1, 0).start()

        far_done(tok_z, tok_x, first_recv)

        @pl.loop(0, 4)
        def _(g):
            for dx in range(4):
                dz = lax.rem(dx + g, 4)

                @pl.when(dz != 0)
                def _():
                    rows = [
                        picks(posz_ref[dz, pl.ds(core * 4 + lax.rem(x + dx, 4), 1), :])
                        for core in range(2)
                    ]
                    rows = dot(as_hot(jnp.concatenate(rows, axis=0)), tok_z[dz], ((1,), (0,)))
                    for core in range(2):
                        part = slice(core * CAP, core * CAP + CAP)
                        outgoing[core, dz, dx, :, 0:HALF] = rows[part].astype(bf16)
                        send_rows(core, dz, dx, g, (True, False))

                if dx == 0:
                    continue
                rows = [
                    picks(posx_ref[dx, pl.ds(core * 4 + lax.rem(z + dz, 4), 1), :])
                    for core in range(2)
                ]
                rows = dot(as_hot(jnp.concatenate(rows, axis=0)), tok_x[dx], ((1,), (0,)))
                for core in range(2):
                    part = slice(core * CAP, core * CAP + CAP)
                    outgoing[core, dz, dx, :, HALF:D] = rows[part].astype(bf16)
                    send_rows(core, dz, dx, g, (False, True))

        def keep_produced(k):
            core, dz, dx = k // CHIPS, lax.rem(k // 4, 4), lax.rem(k, 4)
            return pltpu.make_async_copy(
                grads_ref.at[core, dz, dx],
                prod_hbm.at[core, dz, dx],
                store_sem.at[lax.rem(dz - dx + 4, 4)],
            )

        for load in loads:
            load.wait()
        done(gate_in.at[pl.ds(0, GROUP - 1)], small_recv.at[0])

        @pl.loop(0, 8)
        def _(c):
            g, core = c // 2, lax.rem(c, 2)

            @pl.when(core == r)
            def _():
                done(arrived.at[0, 0, pl.ds(0, 3)], slot_recv.at[c])

            @pl.when(core != r)
            def _():
                done(arrived.at[0, 0], slot_recv.at[c])

            @pl.when(core == 0)
            def _():
                done(outgoing.at[0, pl.ds(0, 2), :, :, pl.ds(0, 896)], slot_send.at[g])

            rows, gate_cols, grads = [], [], []
            for dx in range(4):
                dz = lax.rem(dx + g, 4)
                k = core * CHIPS + dz * 4 + dx
                rows.append(arrived[core, dz, dx])
                gate_cols.append(as_column(gate_in[k, 0:1, 0:CAP]))
                grads.append(grads_ref[core, dz, dx])
            rows = jnp.concatenate(rows, axis=0)
            gate_cols = jnp.concatenate(gate_cols, axis=0)
            grads = jnp.concatenate(grads, axis=0).astype(f32)
            gate_pre = dot(rows, wg_ref[...], ((1,), (0,)))
            up_pre = dot(rows, wu_ref[...], ((1,), (0,)))
            gate_sig = jax.nn.sigmoid(gate_pre)
            gate_act = gate_pre * gate_sig
            act = (gate_act * up_pre).astype(bf16)
            produced = dot(act, wd_ref[...], ((1,), (0,))).astype(bf16).astype(f32)
            dots = jnp.sum(produced * grads, axis=1, keepdims=True)
            produced_grad = (gate_cols * grads).astype(bf16)
            act_grad = dot(produced_grad, wd_ref[...], ((1,), (1,))).astype(bf16).astype(f32)
            gate_grad = (
                act_grad * up_pre * gate_sig * (1.0 + gate_pre * (1.0 - gate_sig))
            ).astype(bf16)
            up_grad = (act_grad * gate_act).astype(bf16)
            row_grads = dot(gate_grad, wg_ref[...], ((1,), (1,)))
            row_grads = (row_grads + dot(up_grad, wu_ref[...], ((1,), (1,)))).astype(bf16)
            produced = (produced * gate_cols).astype(bf16)
            for dx in range(4):
                dz = lax.rem(dx + g, 4)
                k = core * CHIPS + dz * 4 + dx
                part = slice(dx * CAP, dx * CAP + CAP)
                outgoing[core, dz, dx] = row_grads[part]
                send_slots(
                    outgoing,
                    mid,
                    core,
                    dz,
                    dx,
                    back_send.at[0],
                    back_recv.at[dz],
                    back_recv.at[4 + dx],
                    -1,
                )
                dot_out[k, 0:1, 0:CAP] = as_row(dots[part])

                @pl.when(own_slot(k))
                def _():
                    dot_in[k] = dot_out[k]

                @pl.when(jnp.logical_not(own_slot(k)))
                def _():
                    small(k, dot_out, dot_in, -1, 1).start()

                grads_ref[core, dz, dx] = produced[part]
                keep_produced(k).start()
                active[core, dz, dx] = act[part]
                weighted[core, dz, dx] = produced_grad[part]
                pre_grads[core, dz, dx, :, 0:HALF] = gate_grad[part]
                pre_grads[core, dz, dx, :, HALF:D] = up_grad[part]

        def send_results(g):
            done(prod_hbm.at[0, pl.ds(0, 2)], store_sem.at[g])
            for dx in range(4):
                dz = lax.rem(dx + g, 4)
                for core in range(2):
                    send_slots(
                        prod_hbm,
                        mid_hbm,
                        core,
                        dz,
                        dx,
                        c_send.at[0],
                        c_recv.at[0],
                        c_recv.at[0],
                        -1,
                        load_sem.at[8],
                    )

        send_results(0)

        all_rows = GROUP * CAP

        def quarter_grads(slot, n):
            span = pl.ds(pl.multiple_of(n * 256, 256), 256)
            left = arrived[:, :, :, :, span].reshape(all_rows, 256)
            part = dot(left, pre_grads[...].reshape(all_rows, D), ((0,), (0,))).astype(bf16)
            narrow = pl.ds(pl.multiple_of(n * 128, 128), 128)
            left = active[:, :, :, :, narrow].reshape(all_rows, 128)
            down = dot(left, weighted[...].reshape(all_rows, D), ((0,), (0,))).astype(bf16)
            for h in range(2):
                rows = part[128 * h : 128 * h + 128]
                expert_ref[slot, h, 0:128, :] = rows[:, 0:HALF]
                expert_ref[slot, h, 128:256, :] = rows[:, HALF:D]
                rows = down[64 * h : 64 * h + 64]
                expert_ref[slot, h, 256:320, :] = rows[:, 0:HALF]
                expert_ref[slot, h, 320:384, :] = rows[:, HALF:D]

        quarter_grads(0, opposite)
        for n in range(2):
            relayed(n).start()

        part_sems = part_send, part_recv
        fold_start(parts_out, parts_in, mid, back_recv, posz_ref, posx_ref, part_sems)

        @pl.loop(1, 4)
        def _(slot):
            quarter_grads(slot, lax.rem(y + jnp.where(slot == 1, 1, jnp.where(slot == 2, 3, 0)), 4))

            @pl.when(slot == 1)
            def _():
                fold_end(parts_out, parts_in, part_sems)
                pl.loop(1, 4)(send_results)

        for n in range(2):
            direct(n).start()

        done(dot_in.at[pl.ds(0, GROUP - 1)], small_recv.at[1])

        @pl.loop(0, GROUP)
        def _(k):
            there, dz, dx = k // CHIPS, lax.rem(k // 4, 4), lax.rem(k, 4)
            _, expert = moved(dx, dz, there)
            at = pl.ds(expert, 1)
            dots = as_column(dot_in[k, 0:1, 0:CAP])
            gdot_ref[at, :] = jnp.sum(
                jnp.where(picks(pos_ref[at, :]), dots, 0.0), axis=0, keepdims=True
            )

        hgrad_ref[...] = folded(parts_in, part_sems)
        done(all_slots(outgoing), back_send.at[0])
        done(parts_out.at[pl.ds(0, 3)], part_send.at[0])
        near_done(tok_z, tok_x, first_send)
        far_done(tok_z, tok_x, first_send)
        done(gate_in.at[pl.ds(0, GROUP - 1)], small_send.at[0])
        done(dot_in.at[pl.ds(0, GROUP - 1)], small_send.at[1])

    pl.run_scoped(
        expert_phase,
        pltpu.VMEM((2, 4, 4, CAP, D), bf16),
        pltpu.VMEM((D, HALF), bf16),
        pltpu.VMEM((D, HALF), bf16),
        pltpu.VMEM((HALF, D), bf16),
        pltpu.VMEM((2, 4, 4, CAP, D), bf16),
        pltpu.VMEM((4, tokens, D), bf16),
        pltpu.VMEM((2, 4, 4, CAP, HALF), bf16),
        pltpu.VMEM((2, 4, 4, CAP, D), bf16),
        pltpu.VMEM((2, 4, 4, CAP, D), bf16),
    )

    def finish_phase(w_ref, q_ref, k_ref, v_ref, normed_ref, mixed_ref, hidden_ref, parts_out2, quarter_sum, relay_out, branch_own, mg_t, grad_t, kv_own, kv_out, weight_part, rs_out, y_out, small_out, small_y, gain_out, gain_y):
        loads = [
            pltpu.make_async_copy(source, target, load_sem.at[n])
            for n, (source, target) in enumerate(
                (
                    (w_hbm, w_ref),
                    (mixed_hbm, mixed_ref),
                    (q_hbm, q_ref),
                    (k_hbm, k_ref),
                    (v_hbm, v_ref),
                    (normed_hbm, normed_ref),
                    (hidden_hbm, hidden_ref),
                )
            )
        ]
        for load in loads:
            load.start()

        def weight(first, width):
            return w_ref[:, :, :, :, first : first + width].reshape(D, width)

        def merged(n):
            device = (above, below)[n][0]
            return remote(
                relay_out.at[n], y_in.at[n, n], ex_send.at[4 + n], ex_recv.at[4 + n], device
            )

        def handed(n):
            device = (above, below)[n][0]
            return remote(
                quarter_sum, esum_hbm.at[y], ex_send.at[6 + n], ex_recv.at[6 + n], device
            )

        def sib_keyval(p):
            return to_sibling(3 + p, kv_out.at[p], kv_in.at[p])

        def sib_grads(p, part):
            rows = pl.ds(p * D + part * HALF, HALF)
            return to_sibling(5 + 2 * p + part, grad_t.at[rows], grad_sib.at[rows])

        sib_branch = to_sibling(2, branch_own, branch_sib)

        for n in range(2):
            relayed(n).wait_recv()
            total = relay_in[n].astype(f32) + expert_ref[1 + n, n].astype(f32)
            relay_out[n] = total.astype(bf16)
            merged(n).start()

        gates = gates_ref[...]
        gdot = gdot_ref[...]
        logit_grad = gates * (gdot - jnp.sum(gates * gdot, axis=0, keepdims=True))
        high, rest = split_two(logit_grad)
        router_part = dot(high, routed_ref[...], ((1,), (0,)))
        router_part = router_part + dot(rest, routed_ref[...], ((1,), (0,)))
        routed_grad = dot(high, router_ref[...], ((0,), (0,)))
        routed_grad = routed_grad + dot(rest, router_ref[...], ((0,), (0,)))
        routed_grad = routed_grad + hgrad_ref[...]
        live = (
            r * tokens + lax.broadcasted_iota(jnp.int32, (tokens, 1), 0) < length_ref[0]
        ).astype(f32)
        middle = middle_ref[...]
        scale = lax.rsqrt(jnp.mean(middle * middle, axis=1, keepdims=True) + epsilon)
        rows = middle * scale
        moe_part = jnp.sum(routed_grad * rows, axis=0, keepdims=True)
        scaled = routed_grad * mgain_ref[...]
        inner = jnp.mean(scaled * rows, axis=1, keepdims=True)
        middle_grad = cot_ref[...].astype(f32) * live + scale * (scaled - rows * inner)
        hgrad_ref[...] = middle_grad
        branch_own[...] = middle_grad.astype(bf16)
        sib_branch.start()
        for j in range(8):
            part = slice(128 * j, 128 * j + 128)
            small_out[:, j, :] = router_part[:, part]
            small_out[:, 8 + j, :] = jnp.broadcast_to(moe_part[:, part], (GROUP, 128))

        def tiny(k):
            device, other = step_of(k, 1)
            return remote(small_out.at[other], small_in.at[me], sm_send.at[0], sm_recv.at[0], device)

        @pl.loop(1, GROUP)
        def _(k):
            tiny(k).start()

        small_in[me] = small_out[me]

        loads[0].wait()
        mg_t[...] = dot(weight(2 * D, D), branch_own[...], ((1,), (1,))).astype(bf16)

        mine = pl.ds(pl.multiple_of(r * HALF, HALF), HALF)

        def columns(p):
            return pl.ds(p * D, HALF), pl.ds(p * D + HALF, HALF)

        def first_step(p, d):
            left, right = columns(p)
            return (
                remote(
                    weight_part.at[lax.rem(z + d, 4), :, :, left],
                    rs_in.at[d, :, :, left],
                    rs_send.at[p],
                    rs_recv.at[p],
                    moved(0, d, r)[0],
                ),
                remote(
                    weight_part.at[:, lax.rem(x + d, 4), :, right],
                    rs_in.at[d, :, :, right],
                    rs_send.at[p],
                    rs_recv.at[p],
                    moved(d, 0, r)[0],
                ),
            )

        def second_step(p, d):
            left, right = columns(p)
            return (
                remote(
                    rs_out.at[lax.rem(x + d, 4), :, left],
                    rs_in2.at[d, :, left],
                    rs_send2.at[p],
                    rs_recv2.at[p],
                    moved(d, 0, r)[0],
                ),
                remote(
                    rs_out.at[lax.rem(z + d, 4), :, right],
                    rs_in2.at[d, :, right],
                    rs_send2.at[p],
                    rs_recv2.at[p],
                    moved(0, d, r)[0],
                ),
            )

        def across(p, n):
            cols = pl.ds(p * D, D)
            return remote(
                y_out.at[:, cols],
                y_parts.at[y, :, cols],
                ys_send.at[p],
                ys_recv.at[p],
                plane_shift(n)[0],
            )

        def sum_first(p, total):
            weight_part[:, :, :, p * D : p * D + D] = total.astype(bf16).reshape(4, 4, 32, D)

            @pl.loop(1, 4)
            def _(d):
                for copy in first_step(p, d):
                    copy.start()

        def sum_second(p):
            left, right = columns(p)

            done(rs_in.at[pl.ds(1, 3), :, :, pl.ds(p * D, D)], rs_recv.at[p])

            total = weight_part[z, :, :, left].astype(f32)
            other = weight_part[:, x, :, right].astype(f32)
            for d in range(1, 4):
                total = total + rs_in[d, :, :, left].astype(f32)
                other = other + rs_in[d, :, :, right].astype(f32)
            rs_out[:, :, left] = total.astype(bf16)
            rs_out[:, :, right] = other.astype(bf16)

            @pl.loop(1, 4)
            def _(d):
                for copy in second_step(p, d):
                    copy.start()

        def sum_third(p):
            left, right = columns(p)

            done(rs_in2.at[pl.ds(1, 3), :, pl.ds(p * D, D)], rs_recv2.at[p])

            total = rs_out[x, :, left].astype(f32)
            other = rs_out[z, :, right].astype(f32)
            for d in range(1, 4):
                total = total + rs_in2[d, :, left].astype(f32)
                other = other + rs_in2[d, :, right].astype(f32)
            y_out[:, left] = total.astype(bf16)
            y_out[:, right] = other.astype(bf16)
            y_parts[y, :, left] = total.astype(bf16)
            y_parts[y, :, right] = other.astype(bf16)
            for n in range(1, PLANES):
                across(p, n).start()

        sib_mixed.wait_recv()
        sib_branch.wait_recv()
        loads[1].wait()
        total = dot(mixed_ref[:, mine], branch_own[...], ((0,), (0,)))
        sum_first(2, total + dot(mixed_sib[...], branch_sib[...], ((0,), (0,))))

        key_live = lax.broadcasted_iota(jnp.int32, (2 * tokens, 1), 0) < length_ref[0]
        score_scale = HEAD ** (-0.5)
        here = pl.ds(pl.multiple_of(r * tokens, tokens), tokens)
        cosine, sine = cos_ref[:, here], sin_ref[:, here]
        first_core = r == 0

        def key_head(p, i):
            g = 4 * p + i
            head = pl.ds(pl.multiple_of(g * HEAD, HEAD), HEAD)
            keys, values = k_ref[head, :], v_ref[head, :]
            key_sum, value_sum = None, None
            for j in range(2):
                at = pl.ds(pl.multiple_of((2 * g + j) * HEAD, HEAD), HEAD)
                query, mixed_grad = q_ref[at, :], mg_t[at, :]
                scores = dot(keys, query, ((0,), (0,))) * score_scale
                scores = jnp.where(key_live, scores, NEG)
                probs = jnp.exp(scores - lse_ref[pl.ds(2 * g + j, 1), :])
                prob_grad = dot(values, mixed_grad, ((0,), (0,)))
                value_part = dot(mixed_grad, probs.astype(bf16), ((1,), (1,)))
                inner = jnp.sum(probs * prob_grad, axis=0, keepdims=True)
                score_grad = (probs * (prob_grad - inner)).astype(bf16)
                key_part = dot(query, score_grad, ((1,), (1,)))
                query_grad = dot(keys, score_grad, ((1,), (0,))) * score_scale
                to = pl.ds(pl.multiple_of(p * D + (2 * i + j) * HEAD, HEAD), HEAD)
                grad_t[to, :] = turned_back(query_grad, cosine, sine).astype(bf16)
                key_sum = key_part if key_sum is None else key_sum + key_part
                value_sum = value_part if value_sum is None else value_sum + value_part
            key_sum = key_sum * score_scale
            for n, part in enumerate((key_sum, value_sum)):
                to = pl.ds(pl.multiple_of(256 * n + i * HEAD, HEAD), HEAD)
                kv_own[p, to, :] = jnp.where(first_core, part[:, :tokens], part[:, tokens:])
                away = jnp.where(first_core, part[:, tokens:], part[:, :tokens])
                kv_out[p, to, :] = away.astype(bf16)

        def heads(p, first, last):
            @pl.loop(first, last)
            def _(i):
                key_head(p, i)

        def whole_keyval(p):
            sib_keyval(p).wait_recv()
            for i in range(4):
                rows = slice(HEAD * i, HEAD * i + HEAD)
                total = kv_own[p, rows, :] + kv_in[p, rows, :].astype(f32)
                to = p * D + HALF + HEAD * i
                grad_t[to : to + HEAD, :] = turned_back(total, cosine, sine).astype(bf16)
            total = kv_own[p, 256:512, :] + kv_in[p, 256:512, :].astype(f32)
            grad_t[p * D + HALF + 256 : p * D + D, :] = total.astype(bf16)
            sib_grads(p, 1).start()

        def projections(p):
            rows = slice(p * D, p * D + D)
            for part in range(2):
                sib_grads(p, part).wait_recv()
            total = dot(normed_ref[:, mine], grad_t[rows, :], ((0,), (1,)))
            sum_first(p, total + dot(normed_sib[...], grad_sib[rows, :], ((0,), (1,))))

        def inputs_part(p):
            return dot(grad_t[p * D : p * D + D, :], weight(p * D, D), ((0,), (1,)))

        for load in loads[2:5]:
            load.wait()
        heads(0, 0, 4)
        sib_keyval(0).start()
        sib_grads(0, 0).start()

        heads(1, 0, 4)
        sib_keyval(1).start()
        sib_grads(1, 0).start()
        for n in range(2):
            direct(n).wait_recv()
            merged(n).wait_recv()
        for n in range(2):
            total = expert_ref[3, n].astype(f32) + (y_in[0, n].astype(f32) + y_in[1, n].astype(f32))
            quarter_sum[n] = total.astype(bf16)
        quarter_out = pltpu.make_async_copy(quarter_sum, esum_hbm.at[y], load_sem.at[9])
        quarter_out.start()
        for n in range(2):
            handed(n).start()

        whole_keyval(0)
        for load in loads[5:]:
            load.wait()
        sib_normed.wait_recv()
        projections(0)
        done(all_slots(mid_hbm), c_recv.at[0])
        done(mid_hbm.at[0, 0], load_sem.at[8])
        results_in = pltpu.make_async_copy(mid_hbm, mid, load_sem.at[10])
        results_in.start()
        whole_keyval(1)
        normed_grad = inputs_part(0)
        projections(1)
        normed_grad = normed_grad + inputs_part(1)

        inputs = hidden_ref[...].astype(f32)
        scale = lax.rsqrt(jnp.mean(inputs * inputs, axis=1, keepdims=True) + epsilon)
        rows = inputs * scale
        attn_part = jnp.sum(normed_grad * rows, axis=0, keepdims=True)
        for j in range(8):
            gain_out[j : j + 1, :] = attn_part[:, 128 * j : 128 * j + 128]

        def gain(k):
            device, _ = step_of(k, 1)
            return remote(gain_out, gain_in.at[me], sm_send.at[3], sm_recv.at[3], device)

        @pl.loop(1, GROUP)
        def _(k):
            gain(k).start()

        gain_in[me] = gain_out[...]
        scaled = normed_grad * again_ref[...]
        inner = jnp.mean(scaled * rows, axis=1, keepdims=True)
        hgrad_ref[...] += scale * (scaled - rows * inner)

        sum_second(2)
        done(small_in.at[pl.ds(0, GROUP - 1)], sm_recv.at[0])

        def small_across(n):
            device, _ = plane_shift(n)
            return remote(
                small_y, small_y_in.at[y], sm_send.at[1], sm_recv.at[1], device
            )

        small_y[...] = jnp.sum(small_in[...], axis=0)
        small_y_in[y] = small_y[...]
        for n in range(1, PLANES):
            small_across(n).start()

        sum_second(0)
        results_in.wait()
        part_sems = part_send2, part_recv2
        fold_start(parts_out2, parts_in2, mid, None, posz_ref, posx_ref, part_sems)
        for n in range(2):
            handed(n).wait_recv()
            passed_on(n).start()

        done(small_y_in.at[pl.ds(0, 3)], sm_recv.at[1])
        totals = small_y_in[0] + small_y_in[1] + small_y_in[2] + small_y_in[3]
        mgain_out[...] = totals[8:16]
        router_all[me] = totals[0:8]

        def router_row(k):
            device, _ = step_of(k, 1)
            return remote(
                router_all.at[me], router_all.at[me], sm_send.at[2], sm_recv.at[2], device
            )

        @pl.loop(1, GROUP)
        def _(k):
            router_row(k).start()

        sum_second(1)
        fold_end(parts_out2, parts_in2, part_sems)
        sum_third(2)
        sum_third(0)

        done(gain_in.at[pl.ds(0, GROUP - 1)], sm_recv.at[3])

        gain_y[...] = jnp.sum(gain_in[...], axis=0)
        gain_y_in[y] = gain_y[...]

        def gain_across(n):
            device, _ = plane_shift(n)
            return remote(gain_y, gain_y_in.at[y], sm_send.at[4], sm_recv.at[4], device)

        for n in range(1, PLANES):
            gain_across(n).start()

        sum_third(1)

        mixture = folded(parts_in2, part_sems)
        hout_ref[...] = ((middle_ref[...] + mixture) * live).astype(bf16)

        done(gain_y_in.at[pl.ds(0, 3)], sm_recv.at[4])
        again_out[...] = (gain_y_in[0] + gain_y_in[1]) + (gain_y_in[2] + gain_y_in[3])

        done(router_all.at[pl.ds(0, GROUP - 1)], sm_recv.at[2])

        router_out[...] = router_all[...]

        done(all_slots(mid_hbm), c_send.at[0])
        done(parts_out2.at[pl.ds(0, 3)], part_send2.at[0])
        done(small_in.at[pl.ds(0, GROUP - 1)], sm_send.at[0])
        done(small_y_in.at[pl.ds(0, 3)], sm_send.at[1])
        done(router_all.at[pl.ds(0, GROUP - 1)], sm_send.at[2])
        done(gain_in.at[pl.ds(0, GROUP - 1)], sm_send.at[3])
        done(gain_y_in.at[pl.ds(0, 3)], sm_send.at[4])
        for p in range(3):
            done(rs_in.at[pl.ds(1, 3), :, :, pl.ds(p * D, D)], rs_send.at[p])
            done(rs_in2.at[pl.ds(1, 3), :, pl.ds(p * D, D)], rs_send2.at[p])
            done(y_parts.at[pl.ds(0, 3), :, pl.ds(p * D, D)], ys_recv.at[p])
            done(y_parts.at[pl.ds(0, 3), :, pl.ds(p * D, D)], ys_send.at[p])
        for n in range(2):
            for copy in (relayed(n), direct(n), merged(n), handed(n), passed_on(n)):
                copy.wait_send()
        for copy in (sib_normed, sib_mixed, sib_branch):
            copy.wait_send()
        for p in range(2):
            sib_keyval(p).wait_send()
            for part in range(2):
                sib_grads(p, part).wait_send()
        for n in range(2):
            passed_on(n).wait_recv()
        quarter_out.wait()
        own_out[...] = (y_parts[0].astype(f32) + y_parts[1].astype(f32)) + (
            y_parts[2].astype(f32) + y_parts[3].astype(f32)
        )

    pl.run_scoped(
        finish_phase,
        pltpu.VMEM((2, 4, 4, 32, 3 * D), bf16),
        pltpu.VMEM((D, tokens), bf16),
        pltpu.VMEM((HALF, 2 * tokens), bf16),
        pltpu.VMEM((HALF, 2 * tokens), bf16),
        pltpu.VMEM((tokens, D), bf16),
        pltpu.VMEM((tokens, D), bf16),
        pltpu.VMEM((tokens, D), bf16),
        pltpu.VMEM((4, tokens, D), bf16),
        pltpu.VMEM((2, 384, HALF), bf16),
        pltpu.VMEM((2, 384, HALF), bf16),
        pltpu.VMEM((tokens, D), bf16),
        pltpu.VMEM((D, tokens), bf16),
        pltpu.VMEM((2 * D, tokens), bf16),
        pltpu.VMEM((2, HALF, tokens), f32),
        pltpu.VMEM((2, HALF, tokens), bf16),
        pltpu.VMEM((4, 4, 32, 3 * D), bf16),
        pltpu.VMEM((4, 32, 3 * D), bf16),
        pltpu.VMEM((32, 3 * D), bf16),
        pltpu.VMEM((GROUP, 16, 128), f32),
        pltpu.VMEM((16, 128), f32),
        pltpu.VMEM((8, 128), f32),
        pltpu.VMEM((8, 128), f32),
    )


def rest(length, *arrays):
    tokens = TOKENS
    f32, bf16 = jnp.float32, jnp.bfloat16
    vmem = pl.BlockSpec(memory_space=pltpu.VMEM)
    hbm = pl.BlockSpec(memory_space=pl.ANY)
    shape = jax.ShapeDtypeStruct
    sems = pltpu.SemaphoreType.DMA
    scratch = [
        pltpu.VMEM((4, tokens, HALF), bf16),
        pltpu.VMEM((4, tokens, HALF), bf16),
        pltpu.VMEM((2, 4, 4, CAP, D), bf16),
        pltpu.VMEM((2, 4, 4, CAP, D), bf16),
        pltpu.VMEM((4, tokens, D), bf16),
        pltpu.VMEM((4, tokens, D), bf16),
        pltpu.VMEM((GROUP, 8, 128), f32),
        pltpu.VMEM((GROUP, 8, 128), f32),
        pltpu.VMEM((GROUP, 8, 128), f32),
        pltpu.VMEM((GROUP, 8, 128), f32),
        pltpu.VMEM((EXPERTS, tokens), f32),
        pltpu.VMEM((4, 2, 384, HALF), bf16),
        pltpu.VMEM((2, 384, HALF), bf16),
        pltpu.VMEM((2, 2, 384, HALF), bf16),
        pltpu.VMEM((tokens, D), bf16),
        pltpu.VMEM((tokens, HALF), bf16),
        pltpu.VMEM((tokens, HALF), bf16),
        pltpu.VMEM((2 * D, tokens), bf16),
        pltpu.VMEM((2, HALF, tokens), bf16),
        pltpu.VMEM((4, 4, 32, 3 * D), bf16),
        pltpu.VMEM((4, 32, 3 * D), bf16),
        pltpu.VMEM((PLANES, 32, 3 * D), bf16),
        pltpu.VMEM((GROUP, 16, 128), f32),
        pltpu.VMEM((PLANES, 16, 128), f32),
        pltpu.VMEM((GROUP, 8, 128), f32),
        pltpu.VMEM((PLANES, 8, 128), f32),
        pltpu.VMEM((GROUP, 8, 128), f32),
    ]
    for count in (11, 4, 4, 4, 4, 8, 1, 8, 1, 3, 2, 2, 1, 1, 1, 3, 10, 10, 9, 9, 3, 3, 3, 3, 3, 3, 5, 5):
        scratch += [sems((count,))]
    in_specs = [pl.BlockSpec(memory_space=pltpu.SMEM)] + [vmem] * len(arrays)
    for n in (6, 7, 8, 9, 13, 16, 17, 18, 19, 20, 21):
        in_specs[n] = hbm
    return pl.pallas_call(
        rest_kernel,
        out_shape=(
            shape((tokens, D), bf16),
            shape((tokens, D), f32),
            shape((8, 128), f32),
            shape((8, 128), f32),
            shape((GROUP, 8, 128), f32),
            shape((32, 3 * D), f32),
            shape((4, 2, 384, HALF), bf16),
            shape((2, 4, 4, CAP, D), bf16),
            shape((2, 4, 4, CAP, D), bf16),
        ),
        in_specs=in_specs,
        out_specs=[vmem] * 6 + [hbm] * 3,
        scratch_shapes=scratch,
        compiler_params=pltpu.CompilerParams(
            collective_id=2, has_side_effects=True, vmem_limit_bytes=62 << 20
        ),
        name="rest",
    )(length, *arrays)[:7]


def spread_kernel(
    hout_ref,
    hgrad_ref,
    own_ref,
    esum_ref,
    router_ref,
    again_ref,
    mgain_ref,
    hout_out,
    hgrad_out,
    q_out,
    k_out,
    v_out,
    o_out,
    gate_out,
    up_out,
    down_out,
    router_out,
    again_out,
    mgain_out,
    esum,
    gate,
    up,
    down,
    hout,
    hgrad,
    in_sem,
    out_sem,
):
    f32 = jnp.float32

    def quarter_in(n):
        return pltpu.make_async_copy(esum_ref.at[n], esum.at[n], in_sem.at[n])

    def quarter_out(n):
        wide, narrow = pl.ds(256 * n, 256), pl.ds(128 * n, 128)
        return [
            pltpu.make_async_copy(source.at[rows], target.at[0, rows], out_sem.at[3 * n + m])
            for m, (source, target, rows) in enumerate(
                ((gate, gate_out, wide), (up, up_out, wide), (down, down_out, narrow))
            )
        ]

    for n in range(4):
        quarter_in(n).start()
    rows_in = [
        pltpu.make_async_copy(hout_ref, hout, in_sem.at[4]),
        pltpu.make_async_copy(hgrad_ref, hgrad, in_sem.at[5]),
    ]
    rows_out = [
        pltpu.make_async_copy(hout, hout_out, out_sem.at[12]),
        pltpu.make_async_copy(hgrad, hgrad_out, out_sem.at[13]),
    ]
    for copy in rows_in:
        copy.start()
    for n in range(4):
        quarter_in(n).wait()
        for h in range(2):
            rows = pl.ds(256 * n + 128 * h, 128)
            gate[rows, :] = esum[n, h, 0:128, :].astype(f32)
            up[rows, :] = esum[n, h, 128:256, :].astype(f32)
            rows = pl.ds(128 * n + 64 * h, 64)
            down[rows, 0:HALF] = esum[n, h, 256:320, :].astype(f32)
            down[rows, HALF:D] = esum[n, h, 320:384, :].astype(f32)
        for copy in quarter_out(n):
            copy.start()
        if n < 2:
            rows_in[n].wait()
            rows_out[n].start()
    for p in range(2):
        q_out[:, p * HALF : p * HALF + HALF] = own_ref[:, p * D : p * D + HALF]
        k_out[:, p * 256 : p * 256 + 256] = own_ref[:, p * D + HALF : p * D + 768]
        v_out[:, p * 256 : p * 256 + 256] = own_ref[:, p * D + 768 : p * D + D]
    o_out[...] = own_ref[:, 2 * D : 3 * D]
    for j in range(8):
        router_out[:, 128 * j : 128 * j + 128] = router_ref[:, j, :]
    again_out[...] = again_ref[...]
    mgain_out[...] = mgain_ref[...]
    for copy in rows_out:
        copy.wait()
    for n in range(4):
        for copy in quarter_out(n):
            copy.wait()


def spread_out(*arrays):
    f32, bf16 = jnp.float32, jnp.bfloat16
    shape = jax.ShapeDtypeStruct
    vmem = pl.BlockSpec(memory_space=pltpu.VMEM)
    hbm = pl.BlockSpec(memory_space=pl.ANY)
    return pl.pallas_call(
        spread_kernel,
        out_shape=(
            shape((TOKENS, D), bf16),
            shape((TOKENS, D), f32),
            shape((32, D), f32),
            shape((32, HALF), f32),
            shape((32, HALF), f32),
            shape((32, D), f32),
            shape((1, D, HALF), f32),
            shape((1, D, HALF), f32),
            shape((1, HALF, D), f32),
            shape((EXPERTS, D), f32),
            shape((8, 128), f32),
            shape((8, 128), f32),
        ),
        in_specs=[hbm, hbm, vmem, hbm, vmem, vmem, vmem],
        out_specs=[hbm, hbm] + [vmem] * 4 + [hbm] * 3 + [vmem] * 3,
        scratch_shapes=[
            pltpu.VMEM((4, 2, 384, HALF), bf16),
            pltpu.VMEM((D, HALF), f32),
            pltpu.VMEM((D, HALF), f32),
            pltpu.VMEM((HALF, D), f32),
            pltpu.VMEM((TOKENS, D), bf16),
            pltpu.VMEM((TOKENS, D), f32),
            pltpu.SemaphoreType.DMA((6,)),
            pltpu.SemaphoreType.DMA((14,)),
        ],
        compiler_params=pltpu.CompilerParams(vmem_limit_bytes=60 << 20),
        name="spread_out",
    )(*arrays)


def on_device(
    hidden_in,
    cotangent,
    lengths,
    routes,
    priority,
    attn_gain,
    query_weight,
    key_weight,
    value_weight,
    output_weight,
    moe_gain,
    router,
    gate_weight,
    up_weight,
    down_weight,
):
    tok_count = hidden_in.shape[0]
    half_dim = HEAD // 2
    frequency = rotary_base ** (-np.arange(half_dim, dtype=np.float32) / half_dim)
    positions = np.arange(2 * tok_count, dtype=np.float32)
    angles = frequency.astype(np.float32)[:, None] * positions[None, :]
    cosine, sine = jnp.asarray(np.cos(angles)), jnp.asarray(np.sin(angles))
    router_t = router.T
    (
        weights,
        normed,
        queries,
        keys,
        values,
        log_total,
        mixed_rows,
        middle,
        routed,
        gates,
        pos,
        posz,
        posx,
        arrived_grad,
    ) = front(
        lengths,
        hidden_in,
        cotangent,
        routes.T,
        priority,
        attn_gain[None],
        moe_gain[None],
        query_weight,
        key_weight,
        value_weight,
        output_weight,
        router_t,
        cosine,
        sine,
    )
    summed = rest(
        lengths,
        routed,
        pos,
        posz,
        posx,
        gates,
        arrived_grad,
        gate_weight[0],
        up_weight[0],
        down_weight[0],
        router_t,
        middle,
        cotangent,
        hidden_in,
        attn_gain[None],
        moe_gain[None],
        normed,
        mixed_rows,
        weights,
        queries,
        keys,
        values,
        log_total,
        cosine,
        sine,
    )
    hidden_out, hidden_grad, attn_gain_sum, moe_gain_sum, router_sum, own_rows, expert_sum = summed
    (
        hidden_out,
        hidden_grad,
        query_grad,
        key_grad,
        value_grad,
        output_grad,
        gate_grad,
        up_grad,
        down_grad,
        router_grad,
        attn_gain_sum,
        moe_gain_sum,
    ) = spread_out(
        hidden_out, hidden_grad, own_rows, expert_sum, router_sum, attn_gain_sum, moe_gain_sum
    )
    return (
        hidden_out,
        hidden_grad,
        attn_gain_sum.reshape(D),
        query_grad,
        key_grad,
        value_grad,
        output_grad,
        moe_gain_sum.reshape(D),
        router_grad.T,
        gate_grad,
        up_grad,
        down_grad,
    )


def solution(mesh):
    return jax.shard_map(
        on_device,
        mesh=mesh,
        in_specs=(
            P(("dp", "col", "row"), None),
            P(("dp", "col", "row"), None),
            P(("dp", "col")),
            P(("dp", "col", "row"), None),
            P(("dp", "col", "row"), None),
            P(),
            P(("row", "col"), None),
            P(("row", "col"), None),
            P(("row", "col"), None),
            P(("row", "col"), None),
            P(),
            P(),
            P(("row", "col"), None, None),
            P(("row", "col"), None, None),
            P(("row", "col"), None, None),
        ),
        out_specs=(
            P(("dp", "col", "row"), None),
            P(("dp", "col", "row"), None),
            P(),
            P(("row", "col"), None),
            P(("row", "col"), None),
            P(("row", "col"), None),
            P(("row", "col"), None),
            P(),
            P(),
            P(("row", "col"), None, None),
            P(("row", "col"), None, None),
            P(("row", "col"), None, None),
        ),
        check_vma=False,
    )
```

```python
import jax
import jax.numpy as jnp
import numpy as np
from jax import lax
from jax.experimental import pallas as pl
from jax.experimental.pallas import tpu as pltpu
from jax.sharding import PartitionSpec as P

D = 1024
HEADS = 16
HEAD = 64
KV_HEADS = 8
EXPERTS = 32
TOP = 8
CAP = 64


epsilon = 1e-05
rotary_base = 10000.0


MESH = pl.DeviceIdType.MESH
GROUP = 32
PLANES = 4
CHIPS = 16
HALF = D // 2
TOKENS = 256
NEG = -1000000000.0


def place():
    col = lax.axis_index("col")
    return lax.axis_index("dp"), lax.axis_index("row"), lax.rem(col, 4), col // 4


def moved(dx, dz, core):
    y, r, x, z = place()
    col = lax.rem(z + dz + 4, 4) * 4 + lax.rem(x + dx + 4, 4)
    return (y, core, col), core * CHIPS + col


def plane_shift(n):
    y, r, x, z = place()
    other = lax.rem(y + n, PLANES)
    return (other, r, z * 4 + x), other


def step_of(k, sign):
    y, r, x, z = place()
    return moved(sign * lax.rem(k, 4), sign * lax.rem(k // 4, 4), lax.rem(r + k // CHIPS, 2))


def remote(src, dst, send_sem, recv_sem, device):
    return pltpu.make_async_remote_copy(
        src_ref=src,
        dst_ref=dst,
        send_sem=send_sem,
        recv_sem=recv_sem,
        device_id=device,
        device_id_type=MESH,
    )


def done(ref, sem):
    pltpu.make_async_copy(ref, ref, sem).wait()


def meet(plane, planes):
    barrier = pltpu.get_barrier_semaphore()
    y, r, x, z = place()

    def greet(device):
        pl.semaphore_signal(barrier, inc=1, device_id=device, device_id_type=MESH)

    if plane:

        @pl.loop(1, GROUP)
        def _(k):
            greet(step_of(k, 1)[0])

        count = GROUP - 1
    else:
        for core in range(2):

            @pl.loop(1, 4)
            def _(d):
                greet(moved(d, 0, core)[0])
                greet(moved(0, d, core)[0])

        greet(moved(0, 0, 1 - r)[0])
        count = 13
    if planes:
        for n in range(1, PLANES):
            greet(plane_shift(n)[0])
        count += PLANES - 1
    pl.semaphore_wait(barrier, count)


def eye(n):
    return lax.broadcasted_iota(jnp.int32, (n, n), 0) == lax.broadcasted_iota(
        jnp.int32, (n, n), 1
    )


def as_row(column):
    return jnp.sum(jnp.where(eye(column.shape[0]), column, 0.0), axis=0, keepdims=True)


def as_column(row_vec):
    return jnp.sum(jnp.where(eye(row_vec.shape[1]), row_vec, 0.0), axis=1, keepdims=True)


def dot(a, b, dims):
    return lax.dot_general(a, b, (dims, ((), ())), preferred_element_type=jnp.float32)


def split_two(values):
    high = values.astype(jnp.bfloat16)
    return high, (values - high.astype(jnp.float32)).astype(jnp.bfloat16)


def picks(positions):
    slots = lax.broadcasted_iota(jnp.int32, (CAP, positions.shape[1]), 0)
    return slots == positions


def as_hot(mask):
    return mask.astype(jnp.float32).astype(jnp.bfloat16)


LEFT = pl.ds(0, HALF)
RIGHT = pl.ds(HALF, HALF)


def spread(d, source, tok_z, tok_x, send_sem, recv_sem):
    y, r, x, z = place()
    return (
        remote(
            source.at[:, LEFT], tok_z.at[d], send_sem.at[0], recv_sem.at[0], moved(0, d, r)[0]
        ),
        remote(
            source.at[:, RIGHT], tok_x.at[d], send_sem.at[1], recv_sem.at[1], moved(d, 0, r)[0]
        ),
    )


def pass_on(tok_z, tok_x, send_sem, recv_sem):
    y, r, x, z = place()
    copies = []
    for n, (d, sign) in enumerate(((1, 1), (3, -1))):
        rows = pl.ds(n * 128, 128)
        for tok, at, device in (
            (tok_z, 2, moved(0, sign, r)[0]),
            (tok_x, 3, moved(sign, 0, r)[0]),
        ):
            copies.append(
                remote(
                    tok.at[d, rows], tok.at[2, rows], send_sem.at[at], recv_sem.at[at], device
                )
            )
    return copies


def near_done(tok_z, tok_x, sem):
    done(tok_z.at[pl.ds(0, 2)], sem.at[0])
    done(tok_x.at[pl.ds(0, 2)], sem.at[1])


def far_done(tok_z, tok_x, sem):
    done(tok_z.at[2], sem.at[2])
    done(tok_x.at[2], sem.at[3])


def is_local(core, offset):
    y, r, x, z = place()
    return (core == r) & (offset == 0)


def send_slots(
    out,
    into,
    there,
    dz,
    dx,
    send_sem,
    recv_left,
    recv_right,
    sign,
    local_sem=None,
    halves=(True, True),
):
    y, r, x, z = place()

    def one(cols, offset, device, recv_sem):
        source, target = out.at[there, dz, dx, :, cols], into.at[r, dz, dx, :, cols]

        @pl.when(jnp.logical_not(is_local(there, offset)))
        def _():
            remote(source, target, send_sem, recv_sem, device).start()

        @pl.when(is_local(there, offset))
        def _():
            if local_sem is None:
                target[...] = source[...]
            else:
                pltpu.make_async_copy(source, target, local_sem).start()

    if halves[0]:
        one(LEFT, dx, moved(sign * dx, 0, there)[0], recv_left)
    if halves[1]:
        one(RIGHT, dz, moved(0, sign * dz, there)[0], recv_right)


def all_slots(ref):
    return ref.at[:, :, :, :, pl.ds(0, 896)]


def line_rows(line, d, axis):
    y, r, x, z = place()
    own = x if axis == 0 else z
    return [
        line[d, pl.ds(core * 4 + lax.rem(own + i, 4), 1), :] for core in range(2) for i in range(4)
    ]


def line_hot(line, d, axis):
    return as_hot(jnp.concatenate([picks(p) for p in line_rows(line, d, axis)], axis=0))


def add_up(mid, line, d, axis):
    if axis == 0:
        rows = mid[:, d, :, :, 0:HALF]
    else:
        rows = mid[:, :, d, :, HALF:D]
    return dot(line_hot(line, d, axis), rows.reshape(8 * CAP, HALF), ((0,), (0,))).astype(
        jnp.bfloat16
    )


def part_copy(d, rows, axis, sign, out, into, send_sem, recv_sem):
    y, r, x, z = place()
    cols = (LEFT, RIGHT)[axis]
    device = moved(sign * axis, sign * (1 - axis), r)[0]
    part = pl.ds(rows, 128)
    return remote(out.at[d, part, cols], into.at[d, part, cols], send_sem, recv_sem, device)


def fold_start(out, into, mid, slot_recv, posz_ref, posx_ref, sems):
    send_sem, recv_sem = sems
    for d in (2, 0, 1, 3):
        for axis, pos in enumerate((posz_ref, posx_ref)):
            if slot_recv is not None:
                done(mid.at[0, 0, :, :, pl.ds(0, 896)], slot_recv.at[4 * axis + d])
            total = add_up(mid, pos, d, axis)
            cols = slice(axis * HALF, axis * HALF + HALF)
            if d == 0:
                into[0, :, cols] = total
                continue
            out[d, :, cols] = total
            if d == 2:
                for rows, sign in ((0, -1), (128, 1)):
                    args = rows, axis, sign, out, into, send_sem.at[0], recv_sem.at[axis]
                    part_copy(2, *args).start()
            else:
                rows, sign = (128, -1) if d == 1 else (0, 1)
                args = rows, axis, sign, out, into, send_sem.at[0], recv_sem.at[2]
                part_copy(d, *args).start()


def fold_end(out, into, sems):
    send_sem, recv_sem = sems
    for axis in range(2):
        cols = slice(axis * HALF, axis * HALF + HALF)
        done(into.at[2, :, (LEFT, RIGHT)[axis]], recv_sem.at[axis])
        for d, rows, sign in ((1, 0, -1), (3, 128, 1)):
            part = slice(rows, rows + 128)
            total = out[d, part, cols].astype(jnp.float32) + into[2, part, cols].astype(jnp.float32)
            out[d, part, cols] = total.astype(jnp.bfloat16)
            args = rows, axis, sign, out, into, send_sem.at[0], recv_sem.at[2]
            part_copy(d, *args).start()


def folded(into, sems):
    done(into.at[pl.ds(0, 2)], sems[1].at[2])
    f32 = jnp.float32
    return into[0].astype(f32) + (into[1].astype(f32) + into[3].astype(f32))


def front_kernel(
    length_ref,
    hidden_ref,
    cot_ref,
    routes_ref,
    prio_ref,
    again_ref,
    mgain_ref,
    wq_ref,
    wk_ref,
    wv_ref,
    wo_ref,
    router_ref,
    cos_ref,
    sin_ref,
    w_hbm,
    normed_ref,
    q_ref,
    k_ref,
    v_ref,
    lse_ref,
    mixed_ref,
    middle_ref,
    routed_ref,
    gates_ref,
    pos_ref,
    posz_ref,
    posx_ref,
    grads_ref,
    w_ref,
    mixed_t,
    posz_out,
    posx_out,
    tok_z,
    tok_x,
    outgoing,
    store_sem,
    w_send,
    w_recv,
    o_send,
    o_recv,
    core_send,
    core_recv,
    kv_send,
    kv_recv,
    first_send,
    first_recv,
    slot_send,
    slot_recv,
    pos_send,
    pos_recv,
):
    y, r, x, z = place()
    f32, bf16 = jnp.float32, jnp.bfloat16
    sibling = moved(0, 0, 1 - r)[0]
    meet(False, True)

    w_ref[r, z, x, :, 0:HALF] = wq_ref[:, 0:HALF]
    w_ref[r, z, x, :, HALF:768] = wk_ref[:, 0:256]
    w_ref[r, z, x, :, 768:D] = wv_ref[:, 0:256]

    @pl.when(y == 0)
    def _():
        w_ref[r, z, x, :, D : D + HALF] = wq_ref[:, HALF:D]

    @pl.when(y == 1)
    def _():
        w_ref[r, z, x, :, D + HALF : D + 768] = wk_ref[:, 256:HALF]
        w_ref[r, z, x, :, D + 768 : 2 * D] = wv_ref[:, 256:HALF]

    @pl.when(y > 1)
    def _():
        own = pl.ds(pl.multiple_of(HALF * (y - 2), HALF), HALF)
        w_ref[r, z, x, :, pl.ds(pl.multiple_of(D + HALF * y, HALF), HALF)] = wo_ref[:, own]

    front, rear = pl.ds(0, HALF), pl.ds(HALF, HALF)

    def quarter(plane, part=None):
        if part is None:
            return pl.ds(pl.multiple_of(D + HALF * plane, HALF), HALF)
        return pl.ds(pl.multiple_of(D + HALF * plane + 256 * part, 256), 256)

    def line_step(d):
        mine_q, mine_o = w_ref.at[r, z, x, :, front], w_ref.at[r, z, x, :, rear]
        return (
            remote(mine_q, mine_q, w_send.at[0], w_recv.at[d], moved(0, d, r)[0]),
            remote(mine_o, mine_o, w_send.at[0], w_recv.at[4 + d], moved(d, 0, r)[0]),
        )

    def cross_step(e, d):
        from_z = w_ref.at[r, lax.rem(z - e + 4, 4), x, :, front]
        from_x = w_ref.at[r, z, lax.rem(x - e + 4, 4), :, rear]
        return (
            remote(from_z, from_z, w_send.at[1], w_recv.at[8 + d], moved(d, 0, r)[0]),
            remote(from_x, from_x, w_send.at[1], w_recv.at[8 + d], moved(0, d, r)[0]),
        )

    def later_line(d):
        left, right = w_ref.at[r, z, x, :, quarter(y, 0)], w_ref.at[r, z, x, :, quarter(y, 1)]
        return (
            remote(left, left, o_send.at[0], o_recv.at[0], moved(0, d, r)[0]),
            remote(right, right, o_send.at[0], o_recv.at[0], moved(d, 0, r)[0]),
        )

    def later_cross(d):
        left, right = w_ref.at[r, :, x, :, quarter(y, 0)], w_ref.at[r, z, :, :, quarter(y, 1)]
        return (
            remote(left, left, o_send.at[1], o_recv.at[1], moved(d, 0, r)[0]),
            remote(right, right, o_send.at[1], o_recv.at[1], moved(0, d, r)[0]),
        )

    def later_plane(n):
        own = w_ref.at[r, :, :, :, quarter(y)]
        return remote(own, own, o_send.at[2], o_recv.at[2], plane_shift(n)[0])

    def later_relay(n):
        device, came_from = plane_shift(1 + 2 * n)[0], plane_shift(3 - 2 * n)[1]
        part = w_ref.at[r, :, :, :, quarter(came_from, n)]
        return remote(part, part, o_send.at[4], o_recv.at[4], device)

    def later_core(n):
        part = w_ref.at[r, :, :, :, quarter(plane_shift(n)[1])]
        return remote(part, part, o_send.at[3], o_recv.at[3], sibling)

    def some(rows, width):
        return w_ref.at[0, pl.ds(0, rows), :, :, pl.ds(0, width)]

    def core_step(d):
        from_x = w_ref.at[r, :, lax.rem(x - d + 4, 4), :, front]
        from_z = w_ref.at[r, lax.rem(z - d + 4, 4), :, :, rear]
        return (
            remote(from_x, from_x, core_send.at[0], core_recv.at[0], sibling),
            remote(from_z, from_z, core_send.at[0], core_recv.at[0], sibling),
        )

    @pl.loop(1, 4)
    def _(d):
        for copy in line_step(d):
            copy.start()

    @pl.loop(1, 4)
    def _(d):
        for copy in cross_step(0, d):
            copy.start()
        for copy in later_line(d):
            copy.start()

    tokens = hidden_ref.shape[0]
    experts_iota = lax.broadcasted_iota(jnp.int32, (EXPERTS, tokens), 0).astype(f32)
    live = r * tokens + lax.broadcasted_iota(jnp.int32, (1, tokens), 1) < length_ref[0]
    routed_to = jnp.zeros((EXPERTS, tokens), f32)
    ranks = jnp.zeros((EXPERTS, tokens), f32)
    prio = prio_ref[...]
    lines = jnp.concatenate([prio[:, 128 * i : 128 * i + 128] for i in range(CHIPS)], axis=0)
    token = lax.broadcasted_iota(jnp.int32, (tokens, CHIPS), 0) // CHIPS
    owner = (token == lax.broadcasted_iota(jnp.int32, (tokens, CHIPS), 1)).astype(f32)
    token = lax.rem(lax.broadcasted_iota(jnp.int32, (tokens, 128), 0), CHIPS)
    lane = lax.broadcasted_iota(jnp.int32, (tokens, 128), 1)
    place_of = lax.rem(lax.broadcasted_iota(jnp.int32, (TOP, 128), 1), TOP)
    place_of = (place_of == lax.broadcasted_iota(jnp.int32, (TOP, 128), 0)).astype(f32)
    priority = jnp.zeros((TOP, tokens), f32)
    for unit, part in ((64.0, lines // 64), (1.0, lax.rem(lines, 64))):
        part = part.astype(f32).astype(bf16)
        rows = dot(owner.astype(bf16), part, ((1,), (0,)))
        rows = jnp.where(lane // TOP == token, rows, 0.0).astype(bf16)
        priority = priority + unit * dot(place_of.astype(bf16), rows, ((1,), (1,)))
    routes = routes_ref[...].astype(f32)
    for j in range(TOP):
        match = experts_iota == routes[j : j + 1, :]
        routed_to = jnp.where(match, 1.0, routed_to)
        ranks = jnp.where(match, priority[j : j + 1, :], ranks)
    far = float(1 << 20)
    ranks = jnp.where((routed_to > 0.0) & live, ranks, far)
    ranks_t = ranks.T
    rows = []
    for e in range(EXPERTS):
        earlier = ranks_t[:, e : e + 1] < ranks[e : e + 1, :]
        rows.append(jnp.sum(earlier.astype(f32), axis=0, keepdims=True))
    slots = jnp.concatenate(rows, axis=0)
    pos = jnp.where((ranks < far) & (slots < CAP), slots, -1.0).astype(jnp.int32)
    pos_ref[...] = pos
    for core in range(2):
        for i in range(4):
            at = core * CHIPS + 4 * i
            posz_out[i, 4 * core : 4 * core + 4, :] = pos[at : at + 4, :]
            for j in range(4):
                posx_out[j, 4 * core + i : 4 * core + i + 1, :] = pos[at + j : at + j + 1, :]
    posz_ref[0] = posz_out[z]
    posx_ref[0] = posx_out[x]
    tok_z[0] = cot_ref[:, 0:HALF]
    tok_x[0] = cot_ref[:, HALF:D]

    def pos_step(d):
        to_z, to_x = lax.rem(z + d, 4), lax.rem(x + d, 4)
        return (
            remote(
                posz_out.at[to_z],
                posz_ref.at[d],
                pos_send.at[0],
                pos_recv.at[0],
                moved(0, d, r)[0],
            ),
            remote(
                posx_out.at[to_x],
                posx_ref.at[d],
                pos_send.at[1],
                pos_recv.at[1],
                moved(d, 0, r)[0],
            ),
        )

    @pl.loop(1, 4)
    def _(d):
        for copy in pos_step(d):
            copy.start()

    done(w_ref.at[0, 0, pl.ds(0, 3), :, pl.ds(0, HALF)], o_recv.at[0])

    @pl.loop(1, 4)
    def _(d):
        for copy in later_cross(d):
            copy.start()

    @pl.loop(1, 4)
    def _(e):
        for copy in line_step(e):
            copy.wait_recv()

        @pl.loop(1, 4)
        def _(d):
            for copy in cross_step(e, d):
                copy.start()

    for d in (1, 3):
        for copy in spread(d, cot_ref, tok_z, tok_x, first_send, first_recv):
            copy.start()

    for copy in core_step(0):
        copy.start()

    def cut_slots(d):
        left = dot(line_hot(posz_ref, d, 0), tok_z[d], ((1,), (0,))).astype(bf16)
        right = dot(line_hot(posx_ref, d, 1), tok_x[d], ((1,), (0,))).astype(bf16)
        sems = slot_send.at[0], slot_recv.at[0], slot_recv.at[0], 1, store_sem.at[1]
        for core in range(2):
            for i in range(4):
                part = slice((core * 4 + i) * CAP, (core * 4 + i + 1) * CAP)
                outgoing[core, d, i, :, 0:HALF] = left[part]
                send_slots(outgoing, grads_ref, core, d, i, *sems, (True, False))
                outgoing[core, i, d, :, HALF:D] = right[part]
                send_slots(outgoing, grads_ref, core, i, d, *sems, (False, True))

    cut_slots(0)

    inputs = hidden_ref[...].astype(f32)
    scale = lax.rsqrt(jnp.mean(inputs * inputs, axis=1, keepdims=True) + epsilon)
    normed_ref[...] = (inputs * scale * again_ref[...]).astype(bf16)

    done(some(3, HALF), o_recv.at[1])

    for n in (1, 3):
        later_plane(n).start()
    later_core(0).start()

    @pl.loop(1, 4)
    def _(d):
        done(some(1, D), w_recv.at[8 + d])
        for copy in core_step(d):
            copy.start()

    near_done(tok_z, tok_x, first_recv)
    for copy in pass_on(tok_z, tok_x, first_send, first_recv):
        copy.start()
    done(posz_ref.at[pl.ds(1, 3)], pos_recv.at[0])
    done(posx_ref.at[pl.ds(1, 3)], pos_recv.at[1])

    @pl.loop(0, 2)
    def _(n):
        cut_slots(1 + 2 * n)

    done(some(4, D), core_recv.at[0])

    here = pl.ds(pl.multiple_of(r * tokens, tokens), tokens)
    cosine, sine = cos_ref[:, here], sin_ref[:, here]

    def projected(first):
        weight = w_ref[:, :, :, :, first : first + HALF].reshape(D, HALF)
        return dot(normed_ref[...], weight, ((1,), (0,))).T

    def turned(rows):
        parts = []
        for h in range(rows.shape[0] // HEAD):
            first, second = rows[HEAD * h : HEAD * h + 32], rows[HEAD * h + 32 : HEAD * h + HEAD]
            parts += [first * cosine - second * sine, second * cosine + first * sine]
        return jnp.concatenate(parts, axis=0).astype(bf16)

    def keys_values(p):
        rows = pl.ds(256 * p, 256)
        return [
            remote(
                ref.at[rows, here],
                ref.at[rows, here],
                kv_send.at[2 * p + n],
                kv_recv.at[2 * p + n],
                sibling,
            )
            for n, ref in enumerate((k_ref, v_ref))
        ]

    def project(p):
        both = projected(D * p + HALF)
        k_ref[256 * p : 256 * p + 256, here] = turned(both[0:256])
        v_ref[256 * p : 256 * p + 256, here] = both[256:512].astype(bf16)
        for copy in keys_values(p):
            copy.start()
        q_ref[HALF * p : HALF * p + HALF, :] = turned(projected(D * p))

    project(0)
    far_done(tok_z, tok_x, first_recv)
    cut_slots(2)
    done(some(4, D), o_recv.at[2])
    for n in range(2):
        later_relay(n).start()
    for n in (1, 3):
        later_core(n).start()
    for copy in keys_values(0):
        copy.wait_recv()

    key_live = lax.broadcasted_iota(jnp.int32, (2 * tokens, 1), 0) < length_ref[0]
    score_scale = HEAD ** (-0.5)

    def attend(g):
        head = pl.ds(pl.multiple_of(g * HEAD, HEAD), HEAD)
        keys, values = k_ref[head, :], v_ref[head, :]
        for j in range(2):
            at = pl.ds(pl.multiple_of((2 * g + j) * HEAD, HEAD), HEAD)
            scores = dot(keys, q_ref[at, :], ((0,), (0,))) * score_scale
            scores = jnp.where(key_live, scores, NEG)
            top = jnp.max(scores, axis=0, keepdims=True)
            weights = jnp.exp(scores - top)
            total = jnp.sum(weights, axis=0, keepdims=True)
            lse_ref[pl.ds(2 * g + j, 1), :] = top + jnp.log(total)
            probs = (weights * (1.0 / total)).astype(bf16)
            mixed_t[at, :] = dot(values, probs, ((1,), (0,))).astype(bf16)

    pl.loop(0, 4)(attend)
    done(some(4, HALF), o_recv.at[4])
    later_core(2).start()
    done(some(4, 2 * D), o_recv.at[3])
    project(1)
    for copy in keys_values(1):
        copy.wait_recv()
    pl.loop(4, 8)(attend)
    mixed_ref[...] = mixed_t[...].T
    weights_out = pltpu.make_async_copy(w_ref, w_hbm, store_sem.at[0])
    weights_out.start()
    w_out = w_ref[:, :, :, :, 2 * D : 3 * D].reshape(D, D)
    middle = hidden_ref[...].astype(f32) + dot(mixed_ref[...], w_out, ((1,), (0,)))
    middle_ref[...] = middle
    scale = lax.rsqrt(jnp.mean(middle * middle, axis=1, keepdims=True) + epsilon)
    routed_ref[...] = (middle * scale * mgain_ref[...]).astype(bf16)
    logits = dot(router_ref[...], routed_ref[...], ((1,), (1,)))
    logits = jnp.where(routed_to > 0.0, logits, -jnp.inf)
    picked = jnp.exp(logits - jnp.max(logits, axis=0, keepdims=True))
    gates_ref[...] = picked / jnp.sum(picked, axis=0, keepdims=True)

    done(all_slots(grads_ref), slot_recv.at[0])
    done(grads_ref.at[0, 0], store_sem.at[1])
    done(all_slots(outgoing), slot_send.at[0])
    done(w_ref.at[0, 0, pl.ds(0, 3), :, pl.ds(0, D)], w_send.at[0])
    done(some(3, D), w_send.at[1])
    done(some(4, D), core_send.at[0])
    done(w_ref.at[0, 0, pl.ds(0, 3), :, pl.ds(0, HALF)], o_send.at[0])
    done(some(3, HALF), o_send.at[1])
    done(some(4, D), o_send.at[2])
    done(some(4, 2 * D), o_send.at[3])
    done(some(4, HALF), o_send.at[4])
    near_done(tok_z, tok_x, first_send)
    far_done(tok_z, tok_x, first_send)
    done(posz_ref.at[pl.ds(1, 3)], pos_send.at[0])
    done(posx_ref.at[pl.ds(1, 3)], pos_send.at[1])
    weights_out.wait()
    for p in range(2):
        for copy in keys_values(p):
            copy.wait_send()


def front(length, *arrays):
    f32, bf16, i32 = jnp.float32, jnp.bfloat16, jnp.int32
    vmem = pl.BlockSpec(memory_space=pltpu.VMEM)
    hbm = pl.BlockSpec(memory_space=pl.ANY)
    shape = jax.ShapeDtypeStruct
    out_shape = (
        shape((2, 4, 4, 32, 3 * D), bf16),
        shape((TOKENS, D), bf16),
        shape((D, TOKENS), bf16),
        shape((HALF, 2 * TOKENS), bf16),
        shape((HALF, 2 * TOKENS), bf16),
        shape((HEADS, TOKENS), f32),
        shape((TOKENS, D), bf16),
        shape((TOKENS, D), f32),
        shape((TOKENS, D), bf16),
        shape((EXPERTS, TOKENS), f32),
        shape((EXPERTS, TOKENS), i32),
        shape((4, 8, TOKENS), i32),
        shape((4, 8, TOKENS), i32),
        shape((2, 4, 4, CAP, D), bf16),
    )
    scratch = [
        pltpu.VMEM((2, 4, 4, 32, 3 * D), bf16),
        pltpu.VMEM((D, TOKENS), bf16),
        pltpu.VMEM((4, 8, TOKENS), i32),
        pltpu.VMEM((4, 8, TOKENS), i32),
        pltpu.VMEM((4, TOKENS, HALF), bf16),
        pltpu.VMEM((4, TOKENS, HALF), bf16),
        pltpu.VMEM((2, 4, 4, CAP, D), bf16),
    ]
    scratch += [pltpu.SemaphoreType.DMA((2,))]
    for count in (12, 5, 1, 4, 4, 1, 2):
        scratch += [pltpu.SemaphoreType.DMA((count,))] * 2
    return pl.pallas_call(
        front_kernel,
        out_shape=out_shape,
        in_specs=[pl.BlockSpec(memory_space=pltpu.SMEM)] + [vmem] * len(arrays),
        out_specs=[hbm] + [vmem] * (len(out_shape) - 2) + [hbm],
        scratch_shapes=scratch,
        compiler_params=pltpu.CompilerParams(
            collective_id=3, has_side_effects=True, vmem_limit_bytes=60 << 20
        ),
        name="front",
    )(length, *arrays)


def turned_back(rows, cosine, sine):
    first, second = rows[0:32], rows[32:64]
    return jnp.concatenate(
        [first * cosine + second * sine, second * cosine - first * sine], axis=0
    )


def rest_kernel(
    length_ref,
    routed_ref,
    pos_ref,
    posz_ref,
    posx_ref,
    gates_ref,
    grads_hbm,
    wg_hbm,
    wu_hbm,
    wd_hbm,
    router_ref,
    middle_ref,
    cot_ref,
    hidden_hbm,
    again_ref,
    mgain_ref,
    normed_hbm,
    mixed_hbm,
    w_hbm,
    q_hbm,
    k_hbm,
    v_hbm,
    lse_ref,
    cos_ref,
    sin_ref,
    hout_ref,
    hgrad_ref,
    again_out,
    mgain_out,
    router_out,
    own_out,
    esum_hbm,
    prod_hbm,
    mid_hbm,
    tok_z,
    tok_x,
    arrived,
    mid,
    parts_in,
    parts_in2,
    gate_out,
    gate_in,
    dot_out,
    dot_in,
    gdot_ref,
    expert_ref,
    relay_in,
    y_in,
    branch_sib,
    normed_sib,
    mixed_sib,
    grad_sib,
    kv_in,
    rs_in,
    rs_in2,
    y_parts,
    small_in,
    small_y_in,
    gain_in,
    gain_y_in,
    router_all,
    load_sem,
    store_sem,
    first_send,
    first_recv,
    slot_send,
    slot_recv,
    back_send,
    back_recv,
    part_send,
    part_recv,
    small_send,
    small_recv,
    c_send,
    c_recv,
    part_send2,
    part_recv2,
    ex_send,
    ex_recv,
    sib_send,
    sib_recv,
    rs_send,
    rs_recv,
    rs_send2,
    rs_recv2,
    ys_send,
    ys_recv,
    sm_send,
    sm_recv,
):
    y, r, x, z = place()
    me = r * CHIPS + z * 4 + x
    sibling = moved(0, 0, 1 - r)[0]
    tokens = TOKENS
    f32, bf16 = jnp.float32, jnp.bfloat16

    above, below = plane_shift(1), plane_shift(3)
    opposite = plane_shift(2)[1]
    def relayed(n):
        device = (above, below)[n][0]
        return remote(
            expert_ref.at[0, n], relay_in.at[n], ex_send.at[n], ex_recv.at[n], device
        )

    def direct(n):
        device = (above, below)[n][0]
        return remote(
            expert_ref.at[1 + n, 1 - n],
            y_in.at[n, 1 - n],
            ex_send.at[2 + n],
            ex_recv.at[2 + n],
            device,
        )

    def passed_on(n):
        device, came_from = (above, below)[n][0], (below, above)[n][1]
        part = esum_hbm.at[came_from, n]
        return remote(part, part, ex_send.at[8 + n], ex_recv.at[8 + n], device)

    def to_sibling(at, src, dst):
        return remote(src, dst, sib_send.at[at], sib_recv.at[at], sibling)

    half = pl.ds(pl.multiple_of((1 - r) * HALF, HALF), HALF)
    sib_normed = to_sibling(0, normed_hbm.at[:, half], normed_sib)
    sib_mixed = to_sibling(1, mixed_hbm.at[:, half], mixed_sib)

    meet(True, True)
    sib_mixed.start()
    sib_normed.start()

    def expert_phase(grads_ref, wg_ref, wu_ref, wd_ref, outgoing, parts_out, active, weighted, pre_grads):
        loads = [
            pltpu.make_async_copy(source, target, load_sem.at[n])
            for n, (source, target) in enumerate(
                (
                    (wg_hbm, wg_ref),
                    (wu_hbm, wu_ref),
                    (wd_hbm, wd_ref),
                    (grads_hbm, grads_ref),
                )
            )
        ]
        for load in loads:
            load.start()

        for d in (1, 3):
            for copy in spread(d, routed_ref, tok_z, tok_x, first_send, first_recv):
                copy.start()

        tok_z[0] = routed_ref[:, 0:HALF]
        tok_x[0] = routed_ref[:, HALF:D]

        def send_rows(core, dz, dx, g, halves):
            came = slot_recv.at[2 * g + r]
            sems = slot_send.at[g], came, came, 1, None
            send_slots(outgoing, arrived, core, dz, dx, *sems, halves)

        left = dot(line_hot(posz_ref, 0, 0), tok_z[0], ((1,), (0,))).astype(bf16)
        right = dot(line_hot(posx_ref, 0, 1), tok_x[0], ((1,), (0,))).astype(bf16)
        for core in range(2):
            for i in range(4):
                part = slice((core * 4 + i) * CAP, (core * 4 + i + 1) * CAP)
                outgoing[core, 0, i, :, 0:HALF] = left[part]
                send_rows(core, 0, i, (4 - i) % 4, (True, False))
                outgoing[core, i, 0, :, HALF:D] = right[part]
                send_rows(core, i, 0, i, (False, True))

        def small(k, out, into, sign, base):
            there, dz, dx = k // CHIPS, lax.rem(k // 4, 4), lax.rem(k, 4)
            slot = r * CHIPS + lax.rem(k, CHIPS)
            return remote(
                out.at[k],
                into.at[slot],
                small_send.at[base],
                small_recv.at[base],
                moved(sign * dx, sign * dz, there)[0],
            )

        def own_slot(k):
            return k == r * CHIPS

        near_done(tok_z, tok_x, first_recv)
        for copy in pass_on(tok_z, tok_x, first_send, first_recv):
            copy.start()

        @pl.loop(0, GROUP)
        def _(k):
            there, dz, dx = k // CHIPS, lax.rem(k // 4, 4), lax.rem(k, 4)
            _, expert = moved(dx, dz, there)
            chosen = picks(pos_ref[pl.ds(expert, 1), :])
            gate_col = jnp.sum(
                jnp.where(chosen, gates_ref[pl.ds(expert, 1), :], 0.0), axis=1, keepdims=True
            )
            gate_out[k, 0:1, 0:CAP] = as_row(gate_col)

            @pl.when(own_slot(k))
            def _():
                gate_in[k] = gate_out[k]

            @pl.when(jnp.logical_not(own_slot(k)))
            def _():
                small(k, gate_out, gate_in, 1, 0).start()

        far_done(tok_z, tok_x, first_recv)

        @pl.loop(0, 4)
        def _(g):
            for dx in range(4):
                dz = lax.rem(dx + g, 4)

                @pl.when(dz != 0)
                def _():
                    rows = [
                        picks(posz_ref[dz, pl.ds(core * 4 + lax.rem(x + dx, 4), 1), :])
                        for core in range(2)
                    ]
                    rows = dot(as_hot(jnp.concatenate(rows, axis=0)), tok_z[dz], ((1,), (0,)))
                    for core in range(2):
                        part = slice(core * CAP, core * CAP + CAP)
                        outgoing[core, dz, dx, :, 0:HALF] = rows[part].astype(bf16)
                        send_rows(core, dz, dx, g, (True, False))

                if dx == 0:
                    continue
                rows = [
                    picks(posx_ref[dx, pl.ds(core * 4 + lax.rem(z + dz, 4), 1), :])
                    for core in range(2)
                ]
                rows = dot(as_hot(jnp.concatenate(rows, axis=0)), tok_x[dx], ((1,), (0,)))
                for core in range(2):
                    part = slice(core * CAP, core * CAP + CAP)
                    outgoing[core, dz, dx, :, HALF:D] = rows[part].astype(bf16)
                    send_rows(core, dz, dx, g, (False, True))

        def keep_produced(k):
            core, dz, dx = k // CHIPS, lax.rem(k // 4, 4), lax.rem(k, 4)
            return pltpu.make_async_copy(
                grads_ref.at[core, dz, dx],
                prod_hbm.at[core, dz, dx],
                store_sem.at[lax.rem(dz - dx + 4, 4)],
            )

        for load in loads:
            load.wait()
        done(gate_in.at[pl.ds(0, GROUP - 1)], small_recv.at[0])

        @pl.loop(0, 8)
        def _(c):
            g, core = c // 2, lax.rem(c, 2)

            @pl.when(core == r)
            def _():
                done(arrived.at[0, 0, pl.ds(0, 3)], slot_recv.at[c])

            @pl.when(core != r)
            def _():
                done(arrived.at[0, 0], slot_recv.at[c])

            @pl.when(core == 0)
            def _():
                done(outgoing.at[0, pl.ds(0, 2), :, :, pl.ds(0, 896)], slot_send.at[g])

            rows, gate_cols, grads = [], [], []
            for dx in range(4):
                dz = lax.rem(dx + g, 4)
                k = core * CHIPS + dz * 4 + dx
                rows.append(arrived[core, dz, dx])
                gate_cols.append(as_column(gate_in[k, 0:1, 0:CAP]))
                grads.append(grads_ref[core, dz, dx])
            rows = jnp.concatenate(rows, axis=0)
            gate_cols = jnp.concatenate(gate_cols, axis=0)
            grads = jnp.concatenate(grads, axis=0).astype(f32)
            gate_pre = dot(rows, wg_ref[...], ((1,), (0,)))
            up_pre = dot(rows, wu_ref[...], ((1,), (0,)))
            gate_sig = jax.nn.sigmoid(gate_pre)
            gate_act = gate_pre * gate_sig
            act = (gate_act * up_pre).astype(bf16)
            produced = dot(act, wd_ref[...], ((1,), (0,))).astype(bf16).astype(f32)
            dots = jnp.sum(produced * grads, axis=1, keepdims=True)
            produced_grad = (gate_cols * grads).astype(bf16)
            act_grad = dot(produced_grad, wd_ref[...], ((1,), (1,))).astype(bf16).astype(f32)
            gate_grad = (
                act_grad * up_pre * gate_sig * (1.0 + gate_pre * (1.0 - gate_sig))
            ).astype(bf16)
            up_grad = (act_grad * gate_act).astype(bf16)
            row_grads = dot(gate_grad, wg_ref[...], ((1,), (1,)))
            row_grads = (row_grads + dot(up_grad, wu_ref[...], ((1,), (1,)))).astype(bf16)
            produced = (produced * gate_cols).astype(bf16)
            for dx in range(4):
                dz = lax.rem(dx + g, 4)
                k = core * CHIPS + dz * 4 + dx
                part = slice(dx * CAP, dx * CAP + CAP)
                outgoing[core, dz, dx] = row_grads[part]
                send_slots(
                    outgoing,
                    mid,
                    core,
                    dz,
                    dx,
                    back_send.at[0],
                    back_recv.at[dz],
                    back_recv.at[4 + dx],
                    -1,
                )
                dot_out[k, 0:1, 0:CAP] = as_row(dots[part])

                @pl.when(own_slot(k))
                def _():
                    dot_in[k] = dot_out[k]

                @pl.when(jnp.logical_not(own_slot(k)))
                def _():
                    small(k, dot_out, dot_in, -1, 1).start()

                grads_ref[core, dz, dx] = produced[part]
                keep_produced(k).start()
                active[core, dz, dx] = act[part]
                weighted[core, dz, dx] = produced_grad[part]
                pre_grads[core, dz, dx, :, 0:HALF] = gate_grad[part]
                pre_grads[core, dz, dx, :, HALF:D] = up_grad[part]

        def send_results(g):
            done(prod_hbm.at[0, pl.ds(0, 2)], store_sem.at[g])
            for dx in range(4):
                dz = lax.rem(dx + g, 4)
                for core in range(2):
                    send_slots(
                        prod_hbm,
                        mid_hbm,
                        core,
                        dz,
                        dx,
                        c_send.at[0],
                        c_recv.at[0],
                        c_recv.at[0],
                        -1,
                        load_sem.at[8],
                    )

        send_results(0)

        all_rows = GROUP * CAP

        def quarter_grads(slot, n):
            span = pl.ds(pl.multiple_of(n * 256, 256), 256)
            left = arrived[:, :, :, :, span].reshape(all_rows, 256)
            part = dot(left, pre_grads[...].reshape(all_rows, D), ((0,), (0,))).astype(bf16)
            narrow = pl.ds(pl.multiple_of(n * 128, 128), 128)
            left = active[:, :, :, :, narrow].reshape(all_rows, 128)
            down = dot(left, weighted[...].reshape(all_rows, D), ((0,), (0,))).astype(bf16)
            for h in range(2):
                rows = part[128 * h : 128 * h + 128]
                expert_ref[slot, h, 0:128, :] = rows[:, 0:HALF]
                expert_ref[slot, h, 128:256, :] = rows[:, HALF:D]
                rows = down[64 * h : 64 * h + 64]
                expert_ref[slot, h, 256:320, :] = rows[:, 0:HALF]
                expert_ref[slot, h, 320:384, :] = rows[:, HALF:D]

        quarter_grads(0, opposite)
        for n in range(2):
            relayed(n).start()

        part_sems = part_send, part_recv
        fold_start(parts_out, parts_in, mid, back_recv, posz_ref, posx_ref, part_sems)

        @pl.loop(1, 4)
        def _(slot):
            quarter_grads(slot, lax.rem(y + jnp.where(slot == 1, 1, jnp.where(slot == 2, 3, 0)), 4))

            @pl.when(slot == 1)
            def _():
                fold_end(parts_out, parts_in, part_sems)
                pl.loop(1, 4)(send_results)

        for n in range(2):
            direct(n).start()

        done(dot_in.at[pl.ds(0, GROUP - 1)], small_recv.at[1])

        @pl.loop(0, GROUP)
        def _(k):
            there, dz, dx = k // CHIPS, lax.rem(k // 4, 4), lax.rem(k, 4)
            _, expert = moved(dx, dz, there)
            at = pl.ds(expert, 1)
            dots = as_column(dot_in[k, 0:1, 0:CAP])
            gdot_ref[at, :] = jnp.sum(
                jnp.where(picks(pos_ref[at, :]), dots, 0.0), axis=0, keepdims=True
            )

        hgrad_ref[...] = folded(parts_in, part_sems)
        done(all_slots(outgoing), back_send.at[0])
        done(parts_out.at[pl.ds(0, 3)], part_send.at[0])
        near_done(tok_z, tok_x, first_send)
        far_done(tok_z, tok_x, first_send)
        done(gate_in.at[pl.ds(0, GROUP - 1)], small_send.at[0])
        done(dot_in.at[pl.ds(0, GROUP - 1)], small_send.at[1])

    pl.run_scoped(
        expert_phase,
        pltpu.VMEM((2, 4, 4, CAP, D), bf16),
        pltpu.VMEM((D, HALF), bf16),
        pltpu.VMEM((D, HALF), bf16),
        pltpu.VMEM((HALF, D), bf16),
        pltpu.VMEM((2, 4, 4, CAP, D), bf16),
        pltpu.VMEM((4, tokens, D), bf16),
        pltpu.VMEM((2, 4, 4, CAP, HALF), bf16),
        pltpu.VMEM((2, 4, 4, CAP, D), bf16),
        pltpu.VMEM((2, 4, 4, CAP, D), bf16),
    )

    def finish_phase(w_ref, q_ref, k_ref, v_ref, normed_ref, mixed_ref, hidden_ref, parts_out2, quarter_sum, relay_out, branch_own, mg_t, grad_t, kv_own, kv_out, weight_part, rs_out, y_out, small_out, small_y, gain_out, gain_y):
        loads = [
            pltpu.make_async_copy(source, target, load_sem.at[n])
            for n, (source, target) in enumerate(
                (
                    (w_hbm, w_ref),
                    (mixed_hbm, mixed_ref),
                    (q_hbm, q_ref),
                    (k_hbm, k_ref),
                    (v_hbm, v_ref),
                    (normed_hbm, normed_ref),
                    (hidden_hbm, hidden_ref),
                )
            )
        ]
        for load in loads:
            load.start()

        def weight(first, width):
            return w_ref[:, :, :, :, first : first + width].reshape(D, width)

        def merged(n):
            device = (above, below)[n][0]
            return remote(
                relay_out.at[n], y_in.at[n, n], ex_send.at[4 + n], ex_recv.at[4 + n], device
            )

        def handed(n):
            device = (above, below)[n][0]
            return remote(
                quarter_sum, esum_hbm.at[y], ex_send.at[6 + n], ex_recv.at[6 + n], device
            )

        def sib_keyval(p):
            return to_sibling(3 + p, kv_out.at[p], kv_in.at[p])

        def sib_grads(p, part):
            rows = pl.ds(p * D + part * HALF, HALF)
            return to_sibling(5 + 2 * p + part, grad_t.at[rows], grad_sib.at[rows])

        sib_branch = to_sibling(2, branch_own, branch_sib)

        for n in range(2):
            relayed(n).wait_recv()
            total = relay_in[n].astype(f32) + expert_ref[1 + n, n].astype(f32)
            relay_out[n] = total.astype(bf16)
            merged(n).start()

        gates = gates_ref[...]
        gdot = gdot_ref[...]
        logit_grad = gates * (gdot - jnp.sum(gates * gdot, axis=0, keepdims=True))
        high, rest = split_two(logit_grad)
        router_part = dot(high, routed_ref[...], ((1,), (0,)))
        router_part = router_part + dot(rest, routed_ref[...], ((1,), (0,)))
        routed_grad = dot(high, router_ref[...], ((0,), (0,)))
        routed_grad = routed_grad + dot(rest, router_ref[...], ((0,), (0,)))
        routed_grad = routed_grad + hgrad_ref[...]
        live = (
            r * tokens + lax.broadcasted_iota(jnp.int32, (tokens, 1), 0) < length_ref[0]
        ).astype(f32)
        middle = middle_ref[...]
        scale = lax.rsqrt(jnp.mean(middle * middle, axis=1, keepdims=True) + epsilon)
        rows = middle * scale
        moe_part = jnp.sum(routed_grad * rows, axis=0, keepdims=True)
        scaled = routed_grad * mgain_ref[...]
        inner = jnp.mean(scaled * rows, axis=1, keepdims=True)
        middle_grad = cot_ref[...].astype(f32) * live + scale * (scaled - rows * inner)
        hgrad_ref[...] = middle_grad
        branch_own[...] = middle_grad.astype(bf16)
        sib_branch.start()
        for j in range(8):
            part = slice(128 * j, 128 * j + 128)
            small_out[:, j, :] = router_part[:, part]
            small_out[:, 8 + j, :] = jnp.broadcast_to(moe_part[:, part], (GROUP, 128))

        def tiny(k):
            device, other = step_of(k, 1)
            return remote(small_out.at[other], small_in.at[me], sm_send.at[0], sm_recv.at[0], device)

        @pl.loop(1, GROUP)
        def _(k):
            tiny(k).start()

        small_in[me] = small_out[me]

        loads[0].wait()
        mg_t[...] = dot(weight(2 * D, D), branch_own[...], ((1,), (1,))).astype(bf16)

        mine = pl.ds(pl.multiple_of(r * HALF, HALF), HALF)

        def columns(p):
            return pl.ds(p * D, HALF), pl.ds(p * D + HALF, HALF)

        def first_step(p, d):
            left, right = columns(p)
            return (
                remote(
                    weight_part.at[lax.rem(z + d, 4), :, :, left],
                    rs_in.at[d, :, :, left],
                    rs_send.at[p],
                    rs_recv.at[p],
                    moved(0, d, r)[0],
                ),
                remote(
                    weight_part.at[:, lax.rem(x + d, 4), :, right],
                    rs_in.at[d, :, :, right],
                    rs_send.at[p],
                    rs_recv.at[p],
                    moved(d, 0, r)[0],
                ),
            )

        def second_step(p, d):
            left, right = columns(p)
            return (
                remote(
                    rs_out.at[lax.rem(x + d, 4), :, left],
                    rs_in2.at[d, :, left],
                    rs_send2.at[p],
                    rs_recv2.at[p],
                    moved(d, 0, r)[0],
                ),
                remote(
                    rs_out.at[lax.rem(z + d, 4), :, right],
                    rs_in2.at[d, :, right],
                    rs_send2.at[p],
                    rs_recv2.at[p],
                    moved(0, d, r)[0],
                ),
            )

        def across(p, n):
            cols = pl.ds(p * D, D)
            return remote(
                y_out.at[:, cols],
                y_parts.at[y, :, cols],
                ys_send.at[p],
                ys_recv.at[p],
                plane_shift(n)[0],
            )

        def sum_first(p, total):
            weight_part[:, :, :, p * D : p * D + D] = total.astype(bf16).reshape(4, 4, 32, D)

            @pl.loop(1, 4)
            def _(d):
                for copy in first_step(p, d):
                    copy.start()

        def sum_second(p):
            left, right = columns(p)

            done(rs_in.at[pl.ds(1, 3), :, :, pl.ds(p * D, D)], rs_recv.at[p])

            total = weight_part[z, :, :, left].astype(f32)
            other = weight_part[:, x, :, right].astype(f32)
            for d in range(1, 4):
                total = total + rs_in[d, :, :, left].astype(f32)
                other = other + rs_in[d, :, :, right].astype(f32)
            rs_out[:, :, left] = total.astype(bf16)
            rs_out[:, :, right] = other.astype(bf16)

            @pl.loop(1, 4)
            def _(d):
                for copy in second_step(p, d):
                    copy.start()

        def sum_third(p):
            left, right = columns(p)

            done(rs_in2.at[pl.ds(1, 3), :, pl.ds(p * D, D)], rs_recv2.at[p])

            total = rs_out[x, :, left].astype(f32)
            other = rs_out[z, :, right].astype(f32)
            for d in range(1, 4):
                total = total + rs_in2[d, :, left].astype(f32)
                other = other + rs_in2[d, :, right].astype(f32)
            y_out[:, left] = total.astype(bf16)
            y_out[:, right] = other.astype(bf16)
            y_parts[y, :, left] = total.astype(bf16)
            y_parts[y, :, right] = other.astype(bf16)
            for n in range(1, PLANES):
                across(p, n).start()

        sib_mixed.wait_recv()
        sib_branch.wait_recv()
        loads[1].wait()
        total = dot(mixed_ref[:, mine], branch_own[...], ((0,), (0,)))
        sum_first(2, total + dot(mixed_sib[...], branch_sib[...], ((0,), (0,))))

        key_live = lax.broadcasted_iota(jnp.int32, (2 * tokens, 1), 0) < length_ref[0]
        score_scale = HEAD ** (-0.5)
        here = pl.ds(pl.multiple_of(r * tokens, tokens), tokens)
        cosine, sine = cos_ref[:, here], sin_ref[:, here]
        first_core = r == 0

        def key_head(p, i):
            g = 4 * p + i
            head = pl.ds(pl.multiple_of(g * HEAD, HEAD), HEAD)
            keys, values = k_ref[head, :], v_ref[head, :]
            key_sum, value_sum = None, None
            for j in range(2):
                at = pl.ds(pl.multiple_of((2 * g + j) * HEAD, HEAD), HEAD)
                query, mixed_grad = q_ref[at, :], mg_t[at, :]
                scores = dot(keys, query, ((0,), (0,))) * score_scale
                scores = jnp.where(key_live, scores, NEG)
                probs = jnp.exp(scores - lse_ref[pl.ds(2 * g + j, 1), :])
                prob_grad = dot(values, mixed_grad, ((0,), (0,)))
                value_part = dot(mixed_grad, probs.astype(bf16), ((1,), (1,)))
                inner = jnp.sum(probs * prob_grad, axis=0, keepdims=True)
                score_grad = (probs * (prob_grad - inner)).astype(bf16)
                key_part = dot(query, score_grad, ((1,), (1,)))
                query_grad = dot(keys, score_grad, ((1,), (0,))) * score_scale
                to = pl.ds(pl.multiple_of(p * D + (2 * i + j) * HEAD, HEAD), HEAD)
                grad_t[to, :] = turned_back(query_grad, cosine, sine).astype(bf16)
                key_sum = key_part if key_sum is None else key_sum + key_part
                value_sum = value_part if value_sum is None else value_sum + value_part
            key_sum = key_sum * score_scale
            for n, part in enumerate((key_sum, value_sum)):
                to = pl.ds(pl.multiple_of(256 * n + i * HEAD, HEAD), HEAD)
                kv_own[p, to, :] = jnp.where(first_core, part[:, :tokens], part[:, tokens:])
                away = jnp.where(first_core, part[:, tokens:], part[:, :tokens])
                kv_out[p, to, :] = away.astype(bf16)

        def heads(p, first, last):
            @pl.loop(first, last)
            def _(i):
                key_head(p, i)

        def whole_keyval(p):
            sib_keyval(p).wait_recv()
            for i in range(4):
                rows = slice(HEAD * i, HEAD * i + HEAD)
                total = kv_own[p, rows, :] + kv_in[p, rows, :].astype(f32)
                to = p * D + HALF + HEAD * i
                grad_t[to : to + HEAD, :] = turned_back(total, cosine, sine).astype(bf16)
            total = kv_own[p, 256:512, :] + kv_in[p, 256:512, :].astype(f32)
            grad_t[p * D + HALF + 256 : p * D + D, :] = total.astype(bf16)
            sib_grads(p, 1).start()

        def projections(p):
            rows = slice(p * D, p * D + D)
            for part in range(2):
                sib_grads(p, part).wait_recv()
            total = dot(normed_ref[:, mine], grad_t[rows, :], ((0,), (1,)))
            sum_first(p, total + dot(normed_sib[...], grad_sib[rows, :], ((0,), (1,))))

        def inputs_part(p):
            return dot(grad_t[p * D : p * D + D, :], weight(p * D, D), ((0,), (1,)))

        for load in loads[2:5]:
            load.wait()
        heads(0, 0, 4)
        sib_keyval(0).start()
        sib_grads(0, 0).start()

        heads(1, 0, 4)
        sib_keyval(1).start()
        sib_grads(1, 0).start()
        for n in range(2):
            direct(n).wait_recv()
            merged(n).wait_recv()
        for n in range(2):
            total = expert_ref[3, n].astype(f32) + (y_in[0, n].astype(f32) + y_in[1, n].astype(f32))
            quarter_sum[n] = total.astype(bf16)
        quarter_out = pltpu.make_async_copy(quarter_sum, esum_hbm.at[y], load_sem.at[9])
        quarter_out.start()
        for n in range(2):
            handed(n).start()

        whole_keyval(0)
        for load in loads[5:]:
            load.wait()
        sib_normed.wait_recv()
        projections(0)
        done(all_slots(mid_hbm), c_recv.at[0])
        done(mid_hbm.at[0, 0], load_sem.at[8])
        results_in = pltpu.make_async_copy(mid_hbm, mid, load_sem.at[10])
        results_in.start()
        whole_keyval(1)
        normed_grad = inputs_part(0)
        projections(1)
        normed_grad = normed_grad + inputs_part(1)

        inputs = hidden_ref[...].astype(f32)
        scale = lax.rsqrt(jnp.mean(inputs * inputs, axis=1, keepdims=True) + epsilon)
        rows = inputs * scale
        attn_part = jnp.sum(normed_grad * rows, axis=0, keepdims=True)
        for j in range(8):
            gain_out[j : j + 1, :] = attn_part[:, 128 * j : 128 * j + 128]

        def gain(k):
            device, _ = step_of(k, 1)
            return remote(gain_out, gain_in.at[me], sm_send.at[3], sm_recv.at[3], device)

        @pl.loop(1, GROUP)
        def _(k):
            gain(k).start()

        gain_in[me] = gain_out[...]
        scaled = normed_grad * again_ref[...]
        inner = jnp.mean(scaled * rows, axis=1, keepdims=True)
        hgrad_ref[...] += scale * (scaled - rows * inner)

        sum_second(2)
        done(small_in.at[pl.ds(0, GROUP - 1)], sm_recv.at[0])

        def small_across(n):
            device, _ = plane_shift(n)
            return remote(
                small_y, small_y_in.at[y], sm_send.at[1], sm_recv.at[1], device
            )

        small_y[...] = jnp.sum(small_in[...], axis=0)
        small_y_in[y] = small_y[...]
        for n in range(1, PLANES):
            small_across(n).start()

        sum_second(0)
        results_in.wait()
        part_sems = part_send2, part_recv2
        fold_start(parts_out2, parts_in2, mid, None, posz_ref, posx_ref, part_sems)
        for n in range(2):
            handed(n).wait_recv()
            passed_on(n).start()

        done(small_y_in.at[pl.ds(0, 3)], sm_recv.at[1])
        totals = small_y_in[0] + small_y_in[1] + small_y_in[2] + small_y_in[3]
        mgain_out[...] = totals[8:16]
        router_all[me] = totals[0:8]

        def router_row(k):
            device, _ = step_of(k, 1)
            return remote(
                router_all.at[me], router_all.at[me], sm_send.at[2], sm_recv.at[2], device
            )

        @pl.loop(1, GROUP)
        def _(k):
            router_row(k).start()

        sum_second(1)
        fold_end(parts_out2, parts_in2, part_sems)
        sum_third(2)
        sum_third(0)

        done(gain_in.at[pl.ds(0, GROUP - 1)], sm_recv.at[3])

        gain_y[...] = jnp.sum(gain_in[...], axis=0)
        gain_y_in[y] = gain_y[...]

        def gain_across(n):
            device, _ = plane_shift(n)
            return remote(gain_y, gain_y_in.at[y], sm_send.at[4], sm_recv.at[4], device)

        for n in range(1, PLANES):
            gain_across(n).start()

        sum_third(1)

        mixture = folded(parts_in2, part_sems)
        hout_ref[...] = ((middle_ref[...] + mixture) * live).astype(bf16)

        done(gain_y_in.at[pl.ds(0, 3)], sm_recv.at[4])
        again_out[...] = (gain_y_in[0] + gain_y_in[1]) + (gain_y_in[2] + gain_y_in[3])

        done(router_all.at[pl.ds(0, GROUP - 1)], sm_recv.at[2])

        router_out[...] = router_all[...]

        done(all_slots(mid_hbm), c_send.at[0])
        done(parts_out2.at[pl.ds(0, 3)], part_send2.at[0])
        done(small_in.at[pl.ds(0, GROUP - 1)], sm_send.at[0])
        done(small_y_in.at[pl.ds(0, 3)], sm_send.at[1])
        done(router_all.at[pl.ds(0, GROUP - 1)], sm_send.at[2])
        done(gain_in.at[pl.ds(0, GROUP - 1)], sm_send.at[3])
        done(gain_y_in.at[pl.ds(0, 3)], sm_send.at[4])
        for p in range(3):
            done(rs_in.at[pl.ds(1, 3), :, :, pl.ds(p * D, D)], rs_send.at[p])
            done(rs_in2.at[pl.ds(1, 3), :, pl.ds(p * D, D)], rs_send2.at[p])
            done(y_parts.at[pl.ds(0, 3), :, pl.ds(p * D, D)], ys_recv.at[p])
            done(y_parts.at[pl.ds(0, 3), :, pl.ds(p * D, D)], ys_send.at[p])
        for n in range(2):
            for copy in (relayed(n), direct(n), merged(n), handed(n), passed_on(n)):
                copy.wait_send()
        for copy in (sib_normed, sib_mixed, sib_branch):
            copy.wait_send()
        for p in range(2):
            sib_keyval(p).wait_send()
            for part in range(2):
                sib_grads(p, part).wait_send()
        for n in range(2):
            passed_on(n).wait_recv()
        quarter_out.wait()
        own_out[...] = (y_parts[0].astype(f32) + y_parts[1].astype(f32)) + (
            y_parts[2].astype(f32) + y_parts[3].astype(f32)
        )

    pl.run_scoped(
        finish_phase,
        pltpu.VMEM((2, 4, 4, 32, 3 * D), bf16),
        pltpu.VMEM((D, tokens), bf16),
        pltpu.VMEM((HALF, 2 * tokens), bf16),
        pltpu.VMEM((HALF, 2 * tokens), bf16),
        pltpu.VMEM((tokens, D), bf16),
        pltpu.VMEM((tokens, D), bf16),
        pltpu.VMEM((tokens, D), bf16),
        pltpu.VMEM((4, tokens, D), bf16),
        pltpu.VMEM((2, 384, HALF), bf16),
        pltpu.VMEM((2, 384, HALF), bf16),
        pltpu.VMEM((tokens, D), bf16),
        pltpu.VMEM((D, tokens), bf16),
        pltpu.VMEM((2 * D, tokens), bf16),
        pltpu.VMEM((2, HALF, tokens), f32),
        pltpu.VMEM((2, HALF, tokens), bf16),
        pltpu.VMEM((4, 4, 32, 3 * D), bf16),
        pltpu.VMEM((4, 32, 3 * D), bf16),
        pltpu.VMEM((32, 3 * D), bf16),
        pltpu.VMEM((GROUP, 16, 128), f32),
        pltpu.VMEM((16, 128), f32),
        pltpu.VMEM((8, 128), f32),
        pltpu.VMEM((8, 128), f32),
    )


def rest(length, *arrays):
    tokens = TOKENS
    f32, bf16 = jnp.float32, jnp.bfloat16
    vmem = pl.BlockSpec(memory_space=pltpu.VMEM)
    hbm = pl.BlockSpec(memory_space=pl.ANY)
    shape = jax.ShapeDtypeStruct
    sems = pltpu.SemaphoreType.DMA
    scratch = [
        pltpu.VMEM((4, tokens, HALF), bf16),
        pltpu.VMEM((4, tokens, HALF), bf16),
        pltpu.VMEM((2, 4, 4, CAP, D), bf16),
        pltpu.VMEM((2, 4, 4, CAP, D), bf16),
        pltpu.VMEM((4, tokens, D), bf16),
        pltpu.VMEM((4, tokens, D), bf16),
        pltpu.VMEM((GROUP, 8, 128), f32),
        pltpu.VMEM((GROUP, 8, 128), f32),
        pltpu.VMEM((GROUP, 8, 128), f32),
        pltpu.VMEM((GROUP, 8, 128), f32),
        pltpu.VMEM((EXPERTS, tokens), f32),
        pltpu.VMEM((4, 2, 384, HALF), bf16),
        pltpu.VMEM((2, 384, HALF), bf16),
        pltpu.VMEM((2, 2, 384, HALF), bf16),
        pltpu.VMEM((tokens, D), bf16),
        pltpu.VMEM((tokens, HALF), bf16),
        pltpu.VMEM((tokens, HALF), bf16),
        pltpu.VMEM((2 * D, tokens), bf16),
        pltpu.VMEM((2, HALF, tokens), bf16),
        pltpu.VMEM((4, 4, 32, 3 * D), bf16),
        pltpu.VMEM((4, 32, 3 * D), bf16),
        pltpu.VMEM((PLANES, 32, 3 * D), bf16),
        pltpu.VMEM((GROUP, 16, 128), f32),
        pltpu.VMEM((PLANES, 16, 128), f32),
        pltpu.VMEM((GROUP, 8, 128), f32),
        pltpu.VMEM((PLANES, 8, 128), f32),
        pltpu.VMEM((GROUP, 8, 128), f32),
    ]
    for count in (11, 4, 4, 4, 4, 8, 1, 8, 1, 3, 2, 2, 1, 1, 1, 3, 10, 10, 9, 9, 3, 3, 3, 3, 3, 3, 5, 5):
        scratch += [sems((count,))]
    in_specs = [pl.BlockSpec(memory_space=pltpu.SMEM)] + [vmem] * len(arrays)
    for n in (6, 7, 8, 9, 13, 16, 17, 18, 19, 20, 21):
        in_specs[n] = hbm
    return pl.pallas_call(
        rest_kernel,
        out_shape=(
            shape((tokens, D), bf16),
            shape((tokens, D), f32),
            shape((8, 128), f32),
            shape((8, 128), f32),
            shape((GROUP, 8, 128), f32),
            shape((32, 3 * D), f32),
            shape((4, 2, 384, HALF), bf16),
            shape((2, 4, 4, CAP, D), bf16),
            shape((2, 4, 4, CAP, D), bf16),
        ),
        in_specs=in_specs,
        out_specs=[vmem] * 6 + [hbm] * 3,
        scratch_shapes=scratch,
        compiler_params=pltpu.CompilerParams(
            collective_id=2, has_side_effects=True, vmem_limit_bytes=62 << 20
        ),
        name="rest",
    )(length, *arrays)[:7]


def spread_kernel(
    hout_ref,
    hgrad_ref,
    own_ref,
    esum_ref,
    router_ref,
    again_ref,
    mgain_ref,
    hout_out,
    hgrad_out,
    q_out,
    k_out,
    v_out,
    o_out,
    gate_out,
    up_out,
    down_out,
    router_out,
    again_out,
    mgain_out,
):
    f32 = jnp.float32
    hout_out[...] = hout_ref[...]
    hgrad_out[...] = hgrad_ref[...]
    for n in range(2):
        for h in range(2):
            rows = slice(256 * n + 128 * h, 256 * n + 128 * h + 128)
            gate_out[0, rows, :] = esum_ref[n, h, 0:128, :].astype(f32)
            up_out[0, rows, :] = esum_ref[n, h, 128:256, :].astype(f32)
            rows = slice(128 * n + 64 * h, 128 * n + 64 * h + 64)
            down_out[0, rows, 0:HALF] = esum_ref[n, h, 256:320, :].astype(f32)
            down_out[0, rows, HALF:D] = esum_ref[n, h, 320:384, :].astype(f32)

    @pl.when(pl.program_id(0) == 0)
    def _():
        for p in range(2):
            q_out[:, p * HALF : p * HALF + HALF] = own_ref[:, p * D : p * D + HALF]
            k_out[:, p * 256 : p * 256 + 256] = own_ref[:, p * D + HALF : p * D + 768]
            v_out[:, p * 256 : p * 256 + 256] = own_ref[:, p * D + 768 : p * D + D]
        o_out[...] = own_ref[:, 2 * D : 3 * D]
        for j in range(8):
            router_out[:, 128 * j : 128 * j + 128] = router_ref[:, j, :]
        again_out[...] = again_ref[...]
        mgain_out[...] = mgain_ref[...]


def spread_out(*arrays):
    f32, bf16 = jnp.float32, jnp.bfloat16
    shape = jax.ShapeDtypeStruct

    def whole(*dims):
        return pl.BlockSpec(dims, lambda i: (0,) * len(dims))

    def rows(count, width):
        return pl.BlockSpec((count, width), lambda i: (i, 0))

    def expert_rows(count, width):
        return pl.BlockSpec((1, count, width), lambda i: (0, i, 0))

    return pl.pallas_call(
        spread_kernel,
        grid=(2,),
        out_shape=(
            shape((TOKENS, D), bf16),
            shape((TOKENS, D), f32),
            shape((32, D), f32),
            shape((32, HALF), f32),
            shape((32, HALF), f32),
            shape((32, D), f32),
            shape((1, D, HALF), f32),
            shape((1, D, HALF), f32),
            shape((1, HALF, D), f32),
            shape((EXPERTS, D), f32),
            shape((8, 128), f32),
            shape((8, 128), f32),
        ),
        in_specs=[
            rows(128, D),
            rows(128, D),
            whole(32, 3 * D),
            pl.BlockSpec((2, 2, 384, HALF), lambda i: (i, 0, 0, 0)),
            whole(GROUP, 8, 128),
            whole(8, 128),
            whole(8, 128),
        ],
        out_specs=[
            rows(128, D),
            rows(128, D),
            whole(32, D),
            whole(32, HALF),
            whole(32, HALF),
            whole(32, D),
            expert_rows(512, HALF),
            expert_rows(512, HALF),
            expert_rows(256, D),
            whole(EXPERTS, D),
            whole(8, 128),
            whole(8, 128),
        ],
        compiler_params=pltpu.CompilerParams(vmem_limit_bytes=60 << 20),
        name="spread_out",
    )(*arrays)


def on_device(
    hidden_in,
    cotangent,
    lengths,
    routes,
    priority,
    attn_gain,
    query_weight,
    key_weight,
    value_weight,
    output_weight,
    moe_gain,
    router,
    gate_weight,
    up_weight,
    down_weight,
):
    tok_count = hidden_in.shape[0]
    half_dim = HEAD // 2
    frequency = rotary_base ** (-np.arange(half_dim, dtype=np.float32) / half_dim)
    positions = np.arange(2 * tok_count, dtype=np.float32)
    angles = frequency.astype(np.float32)[:, None] * positions[None, :]
    cosine, sine = jnp.asarray(np.cos(angles)), jnp.asarray(np.sin(angles))
    router_t = router.T
    (
        weights,
        normed,
        queries,
        keys,
        values,
        log_total,
        mixed_rows,
        middle,
        routed,
        gates,
        pos,
        posz,
        posx,
        arrived_grad,
    ) = front(
        lengths,
        hidden_in,
        cotangent,
        routes.T,
        priority,
        attn_gain[None],
        moe_gain[None],
        query_weight,
        key_weight,
        value_weight,
        output_weight,
        router_t,
        cosine,
        sine,
    )
    summed = rest(
        lengths,
        routed,
        pos,
        posz,
        posx,
        gates,
        arrived_grad,
        gate_weight[0],
        up_weight[0],
        down_weight[0],
        router_t,
        middle,
        cotangent,
        hidden_in,
        attn_gain[None],
        moe_gain[None],
        normed,
        mixed_rows,
        weights,
        queries,
        keys,
        values,
        log_total,
        cosine,
        sine,
    )
    hidden_out, hidden_grad, attn_gain_sum, moe_gain_sum, router_sum, own_rows, expert_sum = summed
    (
        hidden_out,
        hidden_grad,
        query_grad,
        key_grad,
        value_grad,
        output_grad,
        gate_grad,
        up_grad,
        down_grad,
        router_grad,
        attn_gain_sum,
        moe_gain_sum,
    ) = spread_out(
        hidden_out, hidden_grad, own_rows, expert_sum, router_sum, attn_gain_sum, moe_gain_sum
    )
    return (
        hidden_out,
        hidden_grad,
        attn_gain_sum.reshape(D),
        query_grad,
        key_grad,
        value_grad,
        output_grad,
        moe_gain_sum.reshape(D),
        router_grad.T,
        gate_grad,
        up_grad,
        down_grad,
    )


def solution(mesh):
    return jax.shard_map(
        on_device,
        mesh=mesh,
        in_specs=(
            P(("dp", "col", "row"), None),
            P(("dp", "col", "row"), None),
            P(("dp", "col")),
            P(("dp", "col", "row"), None),
            P(("dp", "col", "row"), None),
            P(),
            P(("row", "col"), None),
            P(("row", "col"), None),
            P(("row", "col"), None),
            P(("row", "col"), None),
            P(),
            P(),
            P(("row", "col"), None, None),
            P(("row", "col"), None, None),
            P(("row", "col"), None, None),
        ),
        out_specs=(
            P(("dp", "col", "row"), None),
            P(("dp", "col", "row"), None),
            P(),
            P(("row", "col"), None),
            P(("row", "col"), None),
            P(("row", "col"), None),
            P(("row", "col"), None),
            P(),
            P(),
            P(("row", "col"), None, None),
            P(("row", "col"), None, None),
            P(("row", "col"), None, None),
        ),
        check_vma=False,
    )
```

```python
import jax
import jax.numpy as jnp
import numpy as np
from jax import lax
from jax.experimental import pallas as pl
from jax.experimental.pallas import tpu as pltpu
from jax.sharding import PartitionSpec as P

D = 1024
HEADS = 16
HEAD = 64
KV_HEADS = 8
EXPERTS = 32
TOP = 8
CAP = 64


epsilon = 1e-05
rotary_base = 10000.0


MESH = pl.DeviceIdType.MESH
GROUP = 32
PLANES = 4
CHIPS = 16
HALF = D // 2
TOKENS = 256
NEG = -1000000000.0


def place():
    col = lax.axis_index("col")
    return lax.axis_index("dp"), lax.axis_index("row"), lax.rem(col, 4), col // 4


def moved(dx, dz, core):
    y, r, x, z = place()
    col = lax.rem(z + dz + 4, 4) * 4 + lax.rem(x + dx + 4, 4)
    return (y, core, col), core * CHIPS + col


def plane_shift(n):
    y, r, x, z = place()
    other = lax.rem(y + n, PLANES)
    return (other, r, z * 4 + x), other


def step_of(k, sign):
    y, r, x, z = place()
    return moved(sign * lax.rem(k, 4), sign * lax.rem(k // 4, 4), lax.rem(r + k // CHIPS, 2))


def remote(src, dst, send_sem, recv_sem, device):
    return pltpu.make_async_remote_copy(
        src_ref=src,
        dst_ref=dst,
        send_sem=send_sem,
        recv_sem=recv_sem,
        device_id=device,
        device_id_type=MESH,
    )


def done(ref, sem):
    pltpu.make_async_copy(ref, ref, sem).wait()


def meet(plane, planes):
    barrier = pltpu.get_barrier_semaphore()
    y, r, x, z = place()

    def greet(device):
        pl.semaphore_signal(barrier, inc=1, device_id=device, device_id_type=MESH)

    if plane:

        @pl.loop(1, GROUP)
        def _(k):
            greet(step_of(k, 1)[0])

        count = GROUP - 1
    else:
        for core in range(2):

            @pl.loop(1, 4)
            def _(d):
                greet(moved(d, 0, core)[0])
                greet(moved(0, d, core)[0])

        greet(moved(0, 0, 1 - r)[0])
        count = 13
    if planes:
        for n in range(1, PLANES):
            greet(plane_shift(n)[0])
        count += PLANES - 1
    pl.semaphore_wait(barrier, count)


def eye(n):
    return lax.broadcasted_iota(jnp.int32, (n, n), 0) == lax.broadcasted_iota(
        jnp.int32, (n, n), 1
    )


def as_row(column):
    return jnp.sum(jnp.where(eye(column.shape[0]), column, 0.0), axis=0, keepdims=True)


def as_column(row_vec):
    return jnp.sum(jnp.where(eye(row_vec.shape[1]), row_vec, 0.0), axis=1, keepdims=True)


def dot(a, b, dims):
    return lax.dot_general(a, b, (dims, ((), ())), preferred_element_type=jnp.float32)


def split_two(values):
    high = values.astype(jnp.bfloat16)
    return high, (values - high.astype(jnp.float32)).astype(jnp.bfloat16)


def picks(positions):
    slots = lax.broadcasted_iota(jnp.int32, (CAP, positions.shape[1]), 0)
    return slots == positions


def as_hot(mask):
    return mask.astype(jnp.float32).astype(jnp.bfloat16)


LEFT = pl.ds(0, HALF)
RIGHT = pl.ds(HALF, HALF)


def spread(d, source, tok_z, tok_x, send_sem, recv_sem):
    y, r, x, z = place()
    return (
        remote(
            source.at[:, LEFT], tok_z.at[d], send_sem.at[0], recv_sem.at[0], moved(0, d, r)[0]
        ),
        remote(
            source.at[:, RIGHT], tok_x.at[d], send_sem.at[1], recv_sem.at[1], moved(d, 0, r)[0]
        ),
    )


def pass_on(tok_z, tok_x, send_sem, recv_sem):
    y, r, x, z = place()
    copies = []
    for n, (d, sign) in enumerate(((1, 1), (3, -1))):
        rows = pl.ds(n * 128, 128)
        for tok, at, device in (
            (tok_z, 2, moved(0, sign, r)[0]),
            (tok_x, 3, moved(sign, 0, r)[0]),
        ):
            copies.append(
                remote(
                    tok.at[d, rows], tok.at[2, rows], send_sem.at[at], recv_sem.at[at], device
                )
            )
    return copies


def near_done(tok_z, tok_x, sem):
    done(tok_z.at[pl.ds(0, 2)], sem.at[0])
    done(tok_x.at[pl.ds(0, 2)], sem.at[1])


def far_done(tok_z, tok_x, sem):
    done(tok_z.at[2], sem.at[2])
    done(tok_x.at[2], sem.at[3])


def is_local(core, offset):
    y, r, x, z = place()
    return (core == r) & (offset == 0)


def send_slots(
    out,
    into,
    there,
    dz,
    dx,
    send_sem,
    recv_left,
    recv_right,
    sign,
    local_sem=None,
    halves=(True, True),
):
    y, r, x, z = place()

    def one(cols, offset, device, recv_sem):
        source, target = out.at[there, dz, dx, :, cols], into.at[r, dz, dx, :, cols]

        @pl.when(jnp.logical_not(is_local(there, offset)))
        def _():
            remote(source, target, send_sem, recv_sem, device).start()

        @pl.when(is_local(there, offset))
        def _():
            if local_sem is None:
                target[...] = source[...]
            else:
                pltpu.make_async_copy(source, target, local_sem).start()

    if halves[0]:
        one(LEFT, dx, moved(sign * dx, 0, there)[0], recv_left)
    if halves[1]:
        one(RIGHT, dz, moved(0, sign * dz, there)[0], recv_right)


def all_slots(ref):
    return ref.at[:, :, :, :, pl.ds(0, 896)]


def line_rows(line, d, axis):
    y, r, x, z = place()
    own = x if axis == 0 else z
    return [
        line[d, pl.ds(core * 4 + lax.rem(own + i, 4), 1), :] for core in range(2) for i in range(4)
    ]


def line_hot(line, d, axis):
    return as_hot(jnp.concatenate([picks(p) for p in line_rows(line, d, axis)], axis=0))


def add_up(mid, line, d, axis):
    if axis == 0:
        rows = mid[:, d, :, :, 0:HALF]
    else:
        rows = mid[:, :, d, :, HALF:D]
    return dot(line_hot(line, d, axis), rows.reshape(8 * CAP, HALF), ((0,), (0,))).astype(
        jnp.bfloat16
    )


def part_copy(d, rows, axis, sign, out, into, send_sem, recv_sem):
    y, r, x, z = place()
    cols = (LEFT, RIGHT)[axis]
    device = moved(sign * axis, sign * (1 - axis), r)[0]
    part = pl.ds(rows, 128)
    return remote(out.at[d, part, cols], into.at[d, part, cols], send_sem, recv_sem, device)


def fold_start(out, into, mid, slot_recv, posz_ref, posx_ref, sems):
    send_sem, recv_sem = sems
    for d in (2, 0, 1, 3):
        for axis, pos in enumerate((posz_ref, posx_ref)):
            if slot_recv is not None:
                done(mid.at[0, 0, :, :, pl.ds(0, 896)], slot_recv.at[4 * axis + d])
            total = add_up(mid, pos, d, axis)
            cols = slice(axis * HALF, axis * HALF + HALF)
            if d == 0:
                into[0, :, cols] = total
                continue
            out[d, :, cols] = total
            if d == 2:
                for rows, sign in ((0, -1), (128, 1)):
                    args = rows, axis, sign, out, into, send_sem.at[0], recv_sem.at[axis]
                    part_copy(2, *args).start()
            else:
                rows, sign = (128, -1) if d == 1 else (0, 1)
                args = rows, axis, sign, out, into, send_sem.at[0], recv_sem.at[2]
                part_copy(d, *args).start()


def fold_end(out, into, sems):
    send_sem, recv_sem = sems
    for axis in range(2):
        cols = slice(axis * HALF, axis * HALF + HALF)
        done(into.at[2, :, (LEFT, RIGHT)[axis]], recv_sem.at[axis])
        for d, rows, sign in ((1, 0, -1), (3, 128, 1)):
            part = slice(rows, rows + 128)
            total = out[d, part, cols].astype(jnp.float32) + into[2, part, cols].astype(jnp.float32)
            out[d, part, cols] = total.astype(jnp.bfloat16)
            args = rows, axis, sign, out, into, send_sem.at[0], recv_sem.at[2]
            part_copy(d, *args).start()


def folded(into, sems):
    done(into.at[pl.ds(0, 2)], sems[1].at[2])
    f32 = jnp.float32
    return into[0].astype(f32) + (into[1].astype(f32) + into[3].astype(f32))


def front_kernel(
    length_ref,
    hidden_ref,
    cot_ref,
    routes_ref,
    prio_ref,
    again_ref,
    mgain_ref,
    wq_ref,
    wk_ref,
    wv_ref,
    wo_ref,
    router_ref,
    cos_ref,
    sin_ref,
    w_hbm,
    normed_ref,
    q_ref,
    k_ref,
    v_ref,
    lse_ref,
    mixed_ref,
    middle_ref,
    routed_ref,
    gates_ref,
    pos_ref,
    posz_ref,
    posx_ref,
    grads_ref,
    w_ref,
    mixed_t,
    posz_out,
    posx_out,
    tok_z,
    tok_x,
    outgoing,
    store_sem,
    w_send,
    w_recv,
    o_send,
    o_recv,
    core_send,
    core_recv,
    kv_send,
    kv_recv,
    first_send,
    first_recv,
    slot_send,
    slot_recv,
    pos_send,
    pos_recv,
):
    y, r, x, z = place()
    f32, bf16 = jnp.float32, jnp.bfloat16
    sibling = moved(0, 0, 1 - r)[0]
    meet(False, True)

    w_ref[r, z, x, :, 0:HALF] = wq_ref[:, 0:HALF]
    w_ref[r, z, x, :, HALF:768] = wk_ref[:, 0:256]
    w_ref[r, z, x, :, 768:D] = wv_ref[:, 0:256]

    @pl.when(y == 0)
    def _():
        w_ref[r, z, x, :, D : D + HALF] = wq_ref[:, HALF:D]

    @pl.when(y == 1)
    def _():
        w_ref[r, z, x, :, D + HALF : D + 768] = wk_ref[:, 256:HALF]
        w_ref[r, z, x, :, D + 768 : 2 * D] = wv_ref[:, 256:HALF]

    @pl.when(y > 1)
    def _():
        own = pl.ds(pl.multiple_of(HALF * (y - 2), HALF), HALF)
        w_ref[r, z, x, :, pl.ds(pl.multiple_of(D + HALF * y, HALF), HALF)] = wo_ref[:, own]

    front, rear = pl.ds(0, HALF), pl.ds(HALF, HALF)

    def quarter(plane, part=None):
        if part is None:
            return pl.ds(pl.multiple_of(D + HALF * plane, HALF), HALF)
        return pl.ds(pl.multiple_of(D + HALF * plane + 256 * part, 256), 256)

    def line_step(d):
        mine_q, mine_o = w_ref.at[r, z, x, :, front], w_ref.at[r, z, x, :, rear]
        return (
            remote(mine_q, mine_q, w_send.at[0], w_recv.at[d], moved(0, d, r)[0]),
            remote(mine_o, mine_o, w_send.at[0], w_recv.at[4 + d], moved(d, 0, r)[0]),
        )

    def cross_step(e, d):
        from_z = w_ref.at[r, lax.rem(z - e + 4, 4), x, :, front]
        from_x = w_ref.at[r, z, lax.rem(x - e + 4, 4), :, rear]
        return (
            remote(from_z, from_z, w_send.at[1], w_recv.at[8 + d], moved(d, 0, r)[0]),
            remote(from_x, from_x, w_send.at[1], w_recv.at[8 + d], moved(0, d, r)[0]),
        )

    def later_line(d):
        left, right = w_ref.at[r, z, x, :, quarter(y, 0)], w_ref.at[r, z, x, :, quarter(y, 1)]
        return (
            remote(left, left, o_send.at[0], o_recv.at[0], moved(0, d, r)[0]),
            remote(right, right, o_send.at[0], o_recv.at[0], moved(d, 0, r)[0]),
        )

    def later_cross(d):
        left, right = w_ref.at[r, :, x, :, quarter(y, 0)], w_ref.at[r, z, :, :, quarter(y, 1)]
        return (
            remote(left, left, o_send.at[1], o_recv.at[1], moved(d, 0, r)[0]),
            remote(right, right, o_send.at[1], o_recv.at[1], moved(0, d, r)[0]),
        )

    def later_plane(n):
        own = w_ref.at[r, :, :, :, quarter(y)]
        return remote(own, own, o_send.at[2], o_recv.at[2], plane_shift(n)[0])

    def later_relay(n):
        device, came_from = plane_shift(1 + 2 * n)[0], plane_shift(3 - 2 * n)[1]
        part = w_ref.at[r, :, :, :, quarter(came_from, n)]
        return remote(part, part, o_send.at[4], o_recv.at[4], device)

    def later_core(n):
        part = w_ref.at[r, :, :, :, quarter(plane_shift(n)[1])]
        return remote(part, part, o_send.at[3], o_recv.at[3], sibling)

    def some(rows, width):
        return w_ref.at[0, pl.ds(0, rows), :, :, pl.ds(0, width)]

    def core_step(d):
        from_x = w_ref.at[r, :, lax.rem(x - d + 4, 4), :, front]
        from_z = w_ref.at[r, lax.rem(z - d + 4, 4), :, :, rear]
        return (
            remote(from_x, from_x, core_send.at[0], core_recv.at[0], sibling),
            remote(from_z, from_z, core_send.at[0], core_recv.at[0], sibling),
        )

    @pl.loop(1, 4)
    def _(d):
        for copy in line_step(d):
            copy.start()

    @pl.loop(1, 4)
    def _(d):
        for copy in cross_step(0, d):
            copy.start()
        for copy in later_line(d):
            copy.start()

    tokens = hidden_ref.shape[0]
    experts_iota = lax.broadcasted_iota(jnp.int32, (EXPERTS, tokens), 0).astype(f32)
    live = r * tokens + lax.broadcasted_iota(jnp.int32, (1, tokens), 1) < length_ref[0]
    routed_to = jnp.zeros((EXPERTS, tokens), f32)
    ranks = jnp.zeros((EXPERTS, tokens), f32)
    prio = prio_ref[...]
    lines = jnp.concatenate([prio[:, 128 * i : 128 * i + 128] for i in range(CHIPS)], axis=0)
    token = lax.broadcasted_iota(jnp.int32, (tokens, CHIPS), 0) // CHIPS
    owner = (token == lax.broadcasted_iota(jnp.int32, (tokens, CHIPS), 1)).astype(f32)
    token = lax.rem(lax.broadcasted_iota(jnp.int32, (tokens, 128), 0), CHIPS)
    lane = lax.broadcasted_iota(jnp.int32, (tokens, 128), 1)
    place_of = lax.rem(lax.broadcasted_iota(jnp.int32, (TOP, 128), 1), TOP)
    place_of = (place_of == lax.broadcasted_iota(jnp.int32, (TOP, 128), 0)).astype(f32)
    priority = jnp.zeros((TOP, tokens), f32)
    for unit, part in ((64.0, lines // 64), (1.0, lax.rem(lines, 64))):
        part = part.astype(f32).astype(bf16)
        rows = dot(owner.astype(bf16), part, ((1,), (0,)))
        rows = jnp.where(lane // TOP == token, rows, 0.0).astype(bf16)
        priority = priority + unit * dot(place_of.astype(bf16), rows, ((1,), (1,)))
    routes = routes_ref[...].astype(f32)
    for j in range(TOP):
        match = experts_iota == routes[j : j + 1, :]
        routed_to = jnp.where(match, 1.0, routed_to)
        ranks = jnp.where(match, priority[j : j + 1, :], ranks)
    far = float(1 << 20)
    ranks = jnp.where((routed_to > 0.0) & live, ranks, far)
    ranks_t = ranks.T
    rows = []
    for e in range(EXPERTS):
        earlier = ranks_t[:, e : e + 1] < ranks[e : e + 1, :]
        rows.append(jnp.sum(earlier.astype(f32), axis=0, keepdims=True))
    slots = jnp.concatenate(rows, axis=0)
    pos = jnp.where((ranks < far) & (slots < CAP), slots, -1.0).astype(jnp.int32)
    pos_ref[...] = pos
    for core in range(2):
        for i in range(4):
            at = core * CHIPS + 4 * i
            posz_out[i, 4 * core : 4 * core + 4, :] = pos[at : at + 4, :]
            for j in range(4):
                posx_out[j, 4 * core + i : 4 * core + i + 1, :] = pos[at + j : at + j + 1, :]
    posz_ref[0] = posz_out[z]
    posx_ref[0] = posx_out[x]
    tok_z[0] = cot_ref[:, 0:HALF]
    tok_x[0] = cot_ref[:, HALF:D]

    def pos_step(d):
        to_z, to_x = lax.rem(z + d, 4), lax.rem(x + d, 4)
        return (
            remote(
                posz_out.at[to_z],
                posz_ref.at[d],
                pos_send.at[0],
                pos_recv.at[0],
                moved(0, d, r)[0],
            ),
            remote(
                posx_out.at[to_x],
                posx_ref.at[d],
                pos_send.at[1],
                pos_recv.at[1],
                moved(d, 0, r)[0],
            ),
        )

    @pl.loop(1, 4)
    def _(d):
        for copy in pos_step(d):
            copy.start()

    done(w_ref.at[0, 0, pl.ds(0, 3), :, pl.ds(0, HALF)], o_recv.at[0])

    @pl.loop(1, 4)
    def _(d):
        for copy in later_cross(d):
            copy.start()

    @pl.loop(1, 4)
    def _(e):
        for copy in line_step(e):
            copy.wait_recv()

        @pl.loop(1, 4)
        def _(d):
            for copy in cross_step(e, d):
                copy.start()

    for d in (1, 3):
        for copy in spread(d, cot_ref, tok_z, tok_x, first_send, first_recv):
            copy.start()

    for copy in core_step(0):
        copy.start()

    def cut_slots(d):
        left = dot(line_hot(posz_ref, d, 0), tok_z[d], ((1,), (0,))).astype(bf16)
        right = dot(line_hot(posx_ref, d, 1), tok_x[d], ((1,), (0,))).astype(bf16)
        sems = slot_send.at[0], slot_recv.at[0], slot_recv.at[0], 1, store_sem.at[1]
        for core in range(2):
            for i in range(4):
                part = slice((core * 4 + i) * CAP, (core * 4 + i + 1) * CAP)
                outgoing[core, d, i, :, 0:HALF] = left[part]
                send_slots(outgoing, grads_ref, core, d, i, *sems, (True, False))
                outgoing[core, i, d, :, HALF:D] = right[part]
                send_slots(outgoing, grads_ref, core, i, d, *sems, (False, True))

    cut_slots(0)

    inputs = hidden_ref[...].astype(f32)
    scale = lax.rsqrt(jnp.mean(inputs * inputs, axis=1, keepdims=True) + epsilon)
    normed_ref[...] = (inputs * scale * again_ref[...]).astype(bf16)

    done(some(3, HALF), o_recv.at[1])

    for n in (1, 3):
        later_plane(n).start()
    later_core(0).start()

    @pl.loop(1, 4)
    def _(d):
        done(some(1, D), w_recv.at[8 + d])
        for copy in core_step(d):
            copy.start()

    near_done(tok_z, tok_x, first_recv)
    for copy in pass_on(tok_z, tok_x, first_send, first_recv):
        copy.start()
    done(posz_ref.at[pl.ds(1, 3)], pos_recv.at[0])
    done(posx_ref.at[pl.ds(1, 3)], pos_recv.at[1])

    @pl.loop(0, 2)
    def _(n):
        cut_slots(1 + 2 * n)

    done(some(4, D), core_recv.at[0])

    here = pl.ds(pl.multiple_of(r * tokens, tokens), tokens)
    cosine, sine = cos_ref[:, here], sin_ref[:, here]

    def projected(first):
        weight = w_ref[:, :, :, :, first : first + HALF].reshape(D, HALF)
        return dot(normed_ref[...], weight, ((1,), (0,))).T

    def turned(rows):
        parts = []
        for h in range(rows.shape[0] // HEAD):
            first, second = rows[HEAD * h : HEAD * h + 32], rows[HEAD * h + 32 : HEAD * h + HEAD]
            parts += [first * cosine - second * sine, second * cosine + first * sine]
        return jnp.concatenate(parts, axis=0).astype(bf16)

    def keys_values(p):
        rows = pl.ds(256 * p, 256)
        return [
            remote(
                ref.at[rows, here],
                ref.at[rows, here],
                kv_send.at[2 * p + n],
                kv_recv.at[2 * p + n],
                sibling,
            )
            for n, ref in enumerate((k_ref, v_ref))
        ]

    def project(p):
        both = projected(D * p + HALF)
        k_ref[256 * p : 256 * p + 256, here] = turned(both[0:256])
        v_ref[256 * p : 256 * p + 256, here] = both[256:512].astype(bf16)
        for copy in keys_values(p):
            copy.start()
        q_ref[HALF * p : HALF * p + HALF, :] = turned(projected(D * p))

    project(0)
    far_done(tok_z, tok_x, first_recv)
    cut_slots(2)
    done(some(4, D), o_recv.at[2])
    for n in range(2):
        later_relay(n).start()
    for n in (1, 3):
        later_core(n).start()
    for copy in keys_values(0):
        copy.wait_recv()

    key_live = lax.broadcasted_iota(jnp.int32, (2 * tokens, 1), 0) < length_ref[0]
    score_scale = HEAD ** (-0.5)

    def attend(g):
        head = pl.ds(pl.multiple_of(g * HEAD, HEAD), HEAD)
        keys, values = k_ref[head, :], v_ref[head, :]
        for j in range(2):
            at = pl.ds(pl.multiple_of((2 * g + j) * HEAD, HEAD), HEAD)
            scores = dot(keys, q_ref[at, :], ((0,), (0,))) * score_scale
            scores = jnp.where(key_live, scores, NEG)
            top = jnp.max(scores, axis=0, keepdims=True)
            weights = jnp.exp(scores - top)
            total = jnp.sum(weights, axis=0, keepdims=True)
            lse_ref[pl.ds(2 * g + j, 1), :] = top + jnp.log(total)
            probs = (weights * (1.0 / total)).astype(bf16)
            mixed_t[at, :] = dot(values, probs, ((1,), (0,))).astype(bf16)

    pl.loop(0, 4)(attend)
    done(some(4, HALF), o_recv.at[4])
    later_core(2).start()
    done(some(4, 2 * D), o_recv.at[3])
    project(1)
    for copy in keys_values(1):
        copy.wait_recv()
    pl.loop(4, 8)(attend)
    mixed_ref[...] = mixed_t[...].T
    weights_out = pltpu.make_async_copy(w_ref, w_hbm, store_sem.at[0])
    weights_out.start()
    w_out = w_ref[:, :, :, :, 2 * D : 3 * D].reshape(D, D)
    middle = hidden_ref[...].astype(f32) + dot(mixed_ref[...], w_out, ((1,), (0,)))
    middle_ref[...] = middle
    scale = lax.rsqrt(jnp.mean(middle * middle, axis=1, keepdims=True) + epsilon)
    routed_ref[...] = (middle * scale * mgain_ref[...]).astype(bf16)
    logits = dot(router_ref[...], routed_ref[...], ((1,), (1,)))
    logits = jnp.where(routed_to > 0.0, logits, -jnp.inf)
    picked = jnp.exp(logits - jnp.max(logits, axis=0, keepdims=True))
    gates_ref[...] = picked / jnp.sum(picked, axis=0, keepdims=True)

    done(all_slots(grads_ref), slot_recv.at[0])
    done(grads_ref.at[0, 0], store_sem.at[1])
    done(all_slots(outgoing), slot_send.at[0])
    done(w_ref.at[0, 0, pl.ds(0, 3), :, pl.ds(0, D)], w_send.at[0])
    done(some(3, D), w_send.at[1])
    done(some(4, D), core_send.at[0])
    done(w_ref.at[0, 0, pl.ds(0, 3), :, pl.ds(0, HALF)], o_send.at[0])
    done(some(3, HALF), o_send.at[1])
    done(some(4, D), o_send.at[2])
    done(some(4, 2 * D), o_send.at[3])
    done(some(4, HALF), o_send.at[4])
    near_done(tok_z, tok_x, first_send)
    far_done(tok_z, tok_x, first_send)
    done(posz_ref.at[pl.ds(1, 3)], pos_send.at[0])
    done(posx_ref.at[pl.ds(1, 3)], pos_send.at[1])
    weights_out.wait()
    for p in range(2):
        for copy in keys_values(p):
            copy.wait_send()


def front(length, *arrays):
    f32, bf16, i32 = jnp.float32, jnp.bfloat16, jnp.int32
    vmem = pl.BlockSpec(memory_space=pltpu.VMEM)
    hbm = pl.BlockSpec(memory_space=pl.ANY)
    shape = jax.ShapeDtypeStruct
    out_shape = (
        shape((2, 4, 4, 32, 3 * D), bf16),
        shape((TOKENS, D), bf16),
        shape((D, TOKENS), bf16),
        shape((HALF, 2 * TOKENS), bf16),
        shape((HALF, 2 * TOKENS), bf16),
        shape((HEADS, TOKENS), f32),
        shape((TOKENS, D), bf16),
        shape((TOKENS, D), f32),
        shape((TOKENS, D), bf16),
        shape((EXPERTS, TOKENS), f32),
        shape((EXPERTS, TOKENS), i32),
        shape((4, 8, TOKENS), i32),
        shape((4, 8, TOKENS), i32),
        shape((2, 4, 4, CAP, D), bf16),
    )
    scratch = [
        pltpu.VMEM((2, 4, 4, 32, 3 * D), bf16),
        pltpu.VMEM((D, TOKENS), bf16),
        pltpu.VMEM((4, 8, TOKENS), i32),
        pltpu.VMEM((4, 8, TOKENS), i32),
        pltpu.VMEM((4, TOKENS, HALF), bf16),
        pltpu.VMEM((4, TOKENS, HALF), bf16),
        pltpu.VMEM((2, 4, 4, CAP, D), bf16),
    ]
    scratch += [pltpu.SemaphoreType.DMA((2,))]
    for count in (12, 5, 1, 4, 4, 1, 2):
        scratch += [pltpu.SemaphoreType.DMA((count,))] * 2
    return pl.pallas_call(
        front_kernel,
        out_shape=out_shape,
        in_specs=[pl.BlockSpec(memory_space=pltpu.SMEM)] + [vmem] * len(arrays),
        out_specs=[hbm] + [vmem] * (len(out_shape) - 2) + [hbm],
        scratch_shapes=scratch,
        compiler_params=pltpu.CompilerParams(
            collective_id=3, has_side_effects=True, vmem_limit_bytes=60 << 20
        ),
        name="front",
    )(length, *arrays)


def turned_back(rows, cosine, sine):
    first, second = rows[0:32], rows[32:64]
    return jnp.concatenate(
        [first * cosine + second * sine, second * cosine - first * sine], axis=0
    )


def rest_kernel(
    length_ref,
    routed_ref,
    pos_ref,
    posz_ref,
    posx_ref,
    gates_ref,
    grads_hbm,
    wg_hbm,
    wu_hbm,
    wd_hbm,
    router_ref,
    middle_ref,
    cot_ref,
    hidden_hbm,
    again_ref,
    mgain_ref,
    normed_hbm,
    mixed_hbm,
    w_hbm,
    q_hbm,
    k_hbm,
    v_hbm,
    lse_ref,
    cos_ref,
    sin_ref,
    hout_ref,
    hgrad_ref,
    again_out,
    mgain_out,
    router_out,
    own_out,
    esum_hbm,
    prod_hbm,
    mid_hbm,
    tok_z,
    tok_x,
    arrived,
    mid,
    parts_in,
    parts_in2,
    gate_out,
    gate_in,
    dot_out,
    dot_in,
    gdot_ref,
    expert_ref,
    relay_in,
    y_in,
    branch_sib,
    normed_sib,
    mixed_sib,
    grad_sib,
    kv_in,
    rs_in,
    rs_in2,
    y_parts,
    small_in,
    small_y_in,
    gain_in,
    gain_y_in,
    router_all,
    load_sem,
    store_sem,
    first_send,
    first_recv,
    slot_send,
    slot_recv,
    back_send,
    back_recv,
    part_send,
    part_recv,
    small_send,
    small_recv,
    c_send,
    c_recv,
    part_send2,
    part_recv2,
    ex_send,
    ex_recv,
    sib_send,
    sib_recv,
    rs_send,
    rs_recv,
    rs_send2,
    rs_recv2,
    ys_send,
    ys_recv,
    sm_send,
    sm_recv,
):
    y, r, x, z = place()
    me = r * CHIPS + z * 4 + x
    sibling = moved(0, 0, 1 - r)[0]
    tokens = TOKENS
    f32, bf16 = jnp.float32, jnp.bfloat16

    above, below = plane_shift(1), plane_shift(3)
    opposite = plane_shift(2)[1]
    def relayed(n):
        device = (above, below)[n][0]
        return remote(
            expert_ref.at[0, n], relay_in.at[n], ex_send.at[n], ex_recv.at[n], device
        )

    def direct(n):
        device = (above, below)[n][0]
        return remote(
            expert_ref.at[1 + n, 1 - n],
            y_in.at[n, 1 - n],
            ex_send.at[2 + n],
            ex_recv.at[2 + n],
            device,
        )

    def passed_on(n):
        device, came_from = (above, below)[n][0], (below, above)[n][1]
        part = esum_hbm.at[came_from, n]
        return remote(part, part, ex_send.at[8 + n], ex_recv.at[8 + n], device)

    def to_sibling(at, src, dst):
        return remote(src, dst, sib_send.at[at], sib_recv.at[at], sibling)

    half = pl.ds(pl.multiple_of((1 - r) * HALF, HALF), HALF)
    sib_normed = to_sibling(0, normed_hbm.at[:, half], normed_sib)
    sib_mixed = to_sibling(1, mixed_hbm.at[:, half], mixed_sib)

    meet(True, True)
    sib_mixed.start()
    sib_normed.start()

    def expert_phase(grads_ref, wg_ref, wu_ref, wd_ref, outgoing, parts_out, active, weighted, pre_grads):
        loads = [
            pltpu.make_async_copy(source, target, load_sem.at[n])
            for n, (source, target) in enumerate(
                (
                    (wg_hbm, wg_ref),
                    (wu_hbm, wu_ref),
                    (wd_hbm, wd_ref),
                    (grads_hbm, grads_ref),
                )
            )
        ]
        for load in loads:
            load.start()

        for d in (1, 3):
            for copy in spread(d, routed_ref, tok_z, tok_x, first_send, first_recv):
                copy.start()

        tok_z[0] = routed_ref[:, 0:HALF]
        tok_x[0] = routed_ref[:, HALF:D]

        def send_rows(core, dz, dx, g, halves):
            came = slot_recv.at[2 * g + r]
            sems = slot_send.at[g], came, came, 1, None
            send_slots(outgoing, arrived, core, dz, dx, *sems, halves)

        left = dot(line_hot(posz_ref, 0, 0), tok_z[0], ((1,), (0,))).astype(bf16)
        right = dot(line_hot(posx_ref, 0, 1), tok_x[0], ((1,), (0,))).astype(bf16)
        for core in range(2):
            for i in range(4):
                part = slice((core * 4 + i) * CAP, (core * 4 + i + 1) * CAP)
                outgoing[core, 0, i, :, 0:HALF] = left[part]
                send_rows(core, 0, i, (4 - i) % 4, (True, False))
                outgoing[core, i, 0, :, HALF:D] = right[part]
                send_rows(core, i, 0, i, (False, True))

        def small(k, out, into, sign, base):
            there, dz, dx = k // CHIPS, lax.rem(k // 4, 4), lax.rem(k, 4)
            slot = r * CHIPS + lax.rem(k, CHIPS)
            return remote(
                out.at[k],
                into.at[slot],
                small_send.at[base],
                small_recv.at[base],
                moved(sign * dx, sign * dz, there)[0],
            )

        def own_slot(k):
            return k == r * CHIPS

        near_done(tok_z, tok_x, first_recv)
        for copy in pass_on(tok_z, tok_x, first_send, first_recv):
            copy.start()

        @pl.loop(0, GROUP)
        def _(k):
            there, dz, dx = k // CHIPS, lax.rem(k // 4, 4), lax.rem(k, 4)
            _, expert = moved(dx, dz, there)
            chosen = picks(pos_ref[pl.ds(expert, 1), :])
            gate_col = jnp.sum(
                jnp.where(chosen, gates_ref[pl.ds(expert, 1), :], 0.0), axis=1, keepdims=True
            )
            gate_out[k, 0:1, 0:CAP] = as_row(gate_col)

            @pl.when(own_slot(k))
            def _():
                gate_in[k] = gate_out[k]

            @pl.when(jnp.logical_not(own_slot(k)))
            def _():
                small(k, gate_out, gate_in, 1, 0).start()

        far_done(tok_z, tok_x, first_recv)

        @pl.loop(0, 4)
        def _(g):
            for dx in range(4):
                dz = lax.rem(dx + g, 4)

                @pl.when(dz != 0)
                def _():
                    rows = [
                        picks(posz_ref[dz, pl.ds(core * 4 + lax.rem(x + dx, 4), 1), :])
                        for core in range(2)
                    ]
                    rows = dot(as_hot(jnp.concatenate(rows, axis=0)), tok_z[dz], ((1,), (0,)))
                    for core in range(2):
                        part = slice(core * CAP, core * CAP + CAP)
                        outgoing[core, dz, dx, :, 0:HALF] = rows[part].astype(bf16)
                        send_rows(core, dz, dx, g, (True, False))

                if dx == 0:
                    continue
                rows = [
                    picks(posx_ref[dx, pl.ds(core * 4 + lax.rem(z + dz, 4), 1), :])
                    for core in range(2)
                ]
                rows = dot(as_hot(jnp.concatenate(rows, axis=0)), tok_x[dx], ((1,), (0,)))
                for core in range(2):
                    part = slice(core * CAP, core * CAP + CAP)
                    outgoing[core, dz, dx, :, HALF:D] = rows[part].astype(bf16)
                    send_rows(core, dz, dx, g, (False, True))

        def keep_produced(k):
            core, dz, dx = k // CHIPS, lax.rem(k // 4, 4), lax.rem(k, 4)
            return pltpu.make_async_copy(
                grads_ref.at[core, dz, dx],
                prod_hbm.at[core, dz, dx],
                store_sem.at[lax.rem(dz - dx + 4, 4)],
            )

        for load in loads:
            load.wait()
        done(gate_in.at[pl.ds(0, GROUP - 1)], small_recv.at[0])

        @pl.loop(0, 8)
        def _(c):
            g, core = c // 2, lax.rem(c, 2)

            @pl.when(core == r)
            def _():
                done(arrived.at[0, 0, pl.ds(0, 3)], slot_recv.at[c])

            @pl.when(core != r)
            def _():
                done(arrived.at[0, 0], slot_recv.at[c])

            @pl.when(core == 0)
            def _():
                done(outgoing.at[0, pl.ds(0, 2), :, :, pl.ds(0, 896)], slot_send.at[g])

            rows, gate_cols, grads = [], [], []
            for dx in range(4):
                dz = lax.rem(dx + g, 4)
                k = core * CHIPS + dz * 4 + dx
                rows.append(arrived[core, dz, dx])
                gate_cols.append(as_column(gate_in[k, 0:1, 0:CAP]))
                grads.append(grads_ref[core, dz, dx])
            rows = jnp.concatenate(rows, axis=0)
            gate_cols = jnp.concatenate(gate_cols, axis=0)
            grads = jnp.concatenate(grads, axis=0).astype(f32)
            gate_pre = dot(rows, wg_ref[...], ((1,), (0,)))
            up_pre = dot(rows, wu_ref[...], ((1,), (0,)))
            gate_sig = jax.nn.sigmoid(gate_pre)
            gate_act = gate_pre * gate_sig
            act = (gate_act * up_pre).astype(bf16)
            produced = dot(act, wd_ref[...], ((1,), (0,))).astype(bf16).astype(f32)
            dots = jnp.sum(produced * grads, axis=1, keepdims=True)
            produced_grad = (gate_cols * grads).astype(bf16)
            act_grad = dot(produced_grad, wd_ref[...], ((1,), (1,))).astype(bf16).astype(f32)
            gate_grad = (
                act_grad * up_pre * gate_sig * (1.0 + gate_pre * (1.0 - gate_sig))
            ).astype(bf16)
            up_grad = (act_grad * gate_act).astype(bf16)
            row_grads = dot(gate_grad, wg_ref[...], ((1,), (1,)))
            row_grads = (row_grads + dot(up_grad, wu_ref[...], ((1,), (1,)))).astype(bf16)
            produced = (produced * gate_cols).astype(bf16)
            for dx in range(4):
                dz = lax.rem(dx + g, 4)
                k = core * CHIPS + dz * 4 + dx
                part = slice(dx * CAP, dx * CAP + CAP)
                outgoing[core, dz, dx] = row_grads[part]
                send_slots(
                    outgoing,
                    mid,
                    core,
                    dz,
                    dx,
                    back_send.at[0],
                    back_recv.at[dz],
                    back_recv.at[4 + dx],
                    -1,
                )
                dot_out[k, 0:1, 0:CAP] = as_row(dots[part])

                @pl.when(own_slot(k))
                def _():
                    dot_in[k] = dot_out[k]

                @pl.when(jnp.logical_not(own_slot(k)))
                def _():
                    small(k, dot_out, dot_in, -1, 1).start()

                grads_ref[core, dz, dx] = produced[part]
                keep_produced(k).start()
                active[core, dz, dx] = act[part]
                weighted[core, dz, dx] = produced_grad[part]
                pre_grads[core, dz, dx, :, 0:HALF] = gate_grad[part]
                pre_grads[core, dz, dx, :, HALF:D] = up_grad[part]

        def send_results(g):
            done(prod_hbm.at[0, pl.ds(0, 2)], store_sem.at[g])
            for dx in range(4):
                dz = lax.rem(dx + g, 4)
                for core in range(2):
                    send_slots(
                        prod_hbm,
                        mid_hbm,
                        core,
                        dz,
                        dx,
                        c_send.at[0],
                        c_recv.at[0],
                        c_recv.at[0],
                        -1,
                        load_sem.at[8],
                    )

        send_results(0)

        all_rows = GROUP * CAP

        def quarter_grads(slot, n):
            span = pl.ds(pl.multiple_of(n * 256, 256), 256)
            left = arrived[:, :, :, :, span].reshape(all_rows, 256)
            part = dot(left, pre_grads[...].reshape(all_rows, D), ((0,), (0,))).astype(bf16)
            narrow = pl.ds(pl.multiple_of(n * 128, 128), 128)
            left = active[:, :, :, :, narrow].reshape(all_rows, 128)
            down = dot(left, weighted[...].reshape(all_rows, D), ((0,), (0,))).astype(bf16)
            for h in range(2):
                rows = part[128 * h : 128 * h + 128]
                expert_ref[slot, h, 0:128, :] = rows[:, 0:HALF]
                expert_ref[slot, h, 128:256, :] = rows[:, HALF:D]
                rows = down[64 * h : 64 * h + 64]
                expert_ref[slot, h, 256:320, :] = rows[:, 0:HALF]
                expert_ref[slot, h, 320:384, :] = rows[:, HALF:D]

        quarter_grads(0, opposite)
        for n in range(2):
            relayed(n).start()

        part_sems = part_send, part_recv
        fold_start(parts_out, parts_in, mid, back_recv, posz_ref, posx_ref, part_sems)

        @pl.loop(1, 4)
        def _(slot):
            quarter_grads(slot, lax.rem(y + jnp.where(slot == 1, 1, jnp.where(slot == 2, 3, 0)), 4))

            @pl.when(slot == 1)
            def _():
                fold_end(parts_out, parts_in, part_sems)
                pl.loop(1, 4)(send_results)

        for n in range(2):
            direct(n).start()

        done(dot_in.at[pl.ds(0, GROUP - 1)], small_recv.at[1])

        @pl.loop(0, GROUP)
        def _(k):
            there, dz, dx = k // CHIPS, lax.rem(k // 4, 4), lax.rem(k, 4)
            _, expert = moved(dx, dz, there)
            at = pl.ds(expert, 1)
            dots = as_column(dot_in[k, 0:1, 0:CAP])
            gdot_ref[at, :] = jnp.sum(
                jnp.where(picks(pos_ref[at, :]), dots, 0.0), axis=0, keepdims=True
            )

        hgrad_ref[...] = folded(parts_in, part_sems)
        done(all_slots(outgoing), back_send.at[0])
        done(parts_out.at[pl.ds(0, 3)], part_send.at[0])
        near_done(tok_z, tok_x, first_send)
        far_done(tok_z, tok_x, first_send)
        done(gate_in.at[pl.ds(0, GROUP - 1)], small_send.at[0])
        done(dot_in.at[pl.ds(0, GROUP - 1)], small_send.at[1])

    pl.run_scoped(
        expert_phase,
        pltpu.VMEM((2, 4, 4, CAP, D), bf16),
        pltpu.VMEM((D, HALF), bf16),
        pltpu.VMEM((D, HALF), bf16),
        pltpu.VMEM((HALF, D), bf16),
        pltpu.VMEM((2, 4, 4, CAP, D), bf16),
        pltpu.VMEM((4, tokens, D), bf16),
        pltpu.VMEM((2, 4, 4, CAP, HALF), bf16),
        pltpu.VMEM((2, 4, 4, CAP, D), bf16),
        pltpu.VMEM((2, 4, 4, CAP, D), bf16),
    )

    def finish_phase(w_ref, q_ref, k_ref, v_ref, normed_ref, mixed_ref, hidden_ref, parts_out2, quarter_sum, relay_out, branch_own, mg_t, grad_t, kv_own, kv_out, weight_part, rs_out, y_out, small_out, small_y, gain_out, gain_y):
        early, late = pl.ds(0, 2 * D), pl.ds(2 * D, D)
        loads = [
            pltpu.make_async_copy(source, target, load_sem.at[n])
            for n, (source, target) in enumerate(
                (
                    (w_hbm.at[:, :, :, :, late], w_ref.at[:, :, :, :, late]),
                    (mixed_hbm, mixed_ref),
                    (q_hbm, q_ref),
                    (k_hbm, k_ref),
                    (v_hbm, v_ref),
                    (normed_hbm, normed_ref),
                    (hidden_hbm, hidden_ref),
                    (w_hbm.at[:, :, :, :, early], w_ref.at[:, :, :, :, early]),
                )
            )
        ]
        for load in loads:
            load.start()

        def weight(first, width):
            return w_ref[:, :, :, :, first : first + width].reshape(D, width)

        def merged(n):
            device = (above, below)[n][0]
            return remote(
                relay_out.at[n], y_in.at[n, n], ex_send.at[4 + n], ex_recv.at[4 + n], device
            )

        def handed(n):
            device = (above, below)[n][0]
            return remote(
                quarter_sum, esum_hbm.at[y], ex_send.at[6 + n], ex_recv.at[6 + n], device
            )

        def sib_keyval(p):
            return to_sibling(3 + p, kv_out.at[p], kv_in.at[p])

        def sib_grads(p, part):
            rows = pl.ds(p * D + part * HALF, HALF)
            return to_sibling(5 + 2 * p + part, grad_t.at[rows], grad_sib.at[rows])

        sib_branch = to_sibling(2, branch_own, branch_sib)

        for n in range(2):
            relayed(n).wait_recv()
            total = relay_in[n].astype(f32) + expert_ref[1 + n, n].astype(f32)
            relay_out[n] = total.astype(bf16)
            merged(n).start()

        gates = gates_ref[...]
        gdot = gdot_ref[...]
        logit_grad = gates * (gdot - jnp.sum(gates * gdot, axis=0, keepdims=True))
        high, rest = split_two(logit_grad)
        router_part = dot(high, routed_ref[...], ((1,), (0,)))
        router_part = router_part + dot(rest, routed_ref[...], ((1,), (0,)))
        routed_grad = dot(high, router_ref[...], ((0,), (0,)))
        routed_grad = routed_grad + dot(rest, router_ref[...], ((0,), (0,)))
        routed_grad = routed_grad + hgrad_ref[...]
        live = (
            r * tokens + lax.broadcasted_iota(jnp.int32, (tokens, 1), 0) < length_ref[0]
        ).astype(f32)
        middle = middle_ref[...]
        scale = lax.rsqrt(jnp.mean(middle * middle, axis=1, keepdims=True) + epsilon)
        rows = middle * scale
        moe_part = jnp.sum(routed_grad * rows, axis=0, keepdims=True)
        scaled = routed_grad * mgain_ref[...]
        inner = jnp.mean(scaled * rows, axis=1, keepdims=True)
        middle_grad = cot_ref[...].astype(f32) * live + scale * (scaled - rows * inner)
        hgrad_ref[...] = middle_grad
        branch_own[...] = middle_grad.astype(bf16)
        sib_branch.start()
        for j in range(8):
            part = slice(128 * j, 128 * j + 128)
            small_out[:, j, :] = router_part[:, part]
            small_out[:, 8 + j, :] = jnp.broadcast_to(moe_part[:, part], (GROUP, 128))

        def tiny(k):
            device, other = step_of(k, 1)
            return remote(small_out.at[other], small_in.at[me], sm_send.at[0], sm_recv.at[0], device)

        @pl.loop(1, GROUP)
        def _(k):
            tiny(k).start()

        small_in[me] = small_out[me]

        loads[0].wait()
        mg_t[...] = dot(weight(2 * D, D), branch_own[...], ((1,), (1,))).astype(bf16)

        mine = pl.ds(pl.multiple_of(r * HALF, HALF), HALF)

        def columns(p):
            return pl.ds(p * D, HALF), pl.ds(p * D + HALF, HALF)

        def first_step(p, d):
            left, right = columns(p)
            return (
                remote(
                    weight_part.at[lax.rem(z + d, 4), :, :, left],
                    rs_in.at[d, :, :, left],
                    rs_send.at[p],
                    rs_recv.at[p],
                    moved(0, d, r)[0],
                ),
                remote(
                    weight_part.at[:, lax.rem(x + d, 4), :, right],
                    rs_in.at[d, :, :, right],
                    rs_send.at[p],
                    rs_recv.at[p],
                    moved(d, 0, r)[0],
                ),
            )

        def second_step(p, d):
            left, right = columns(p)
            return (
                remote(
                    rs_out.at[lax.rem(x + d, 4), :, left],
                    rs_in2.at[d, :, left],
                    rs_send2.at[p],
                    rs_recv2.at[p],
                    moved(d, 0, r)[0],
                ),
                remote(
                    rs_out.at[lax.rem(z + d, 4), :, right],
                    rs_in2.at[d, :, right],
                    rs_send2.at[p],
                    rs_recv2.at[p],
                    moved(0, d, r)[0],
                ),
            )

        def across(p, n):
            cols = pl.ds(p * D, D)
            return remote(
                y_out.at[:, cols],
                y_parts.at[y, :, cols],
                ys_send.at[p],
                ys_recv.at[p],
                plane_shift(n)[0],
            )

        def sum_first(p, total):
            weight_part[:, :, :, p * D : p * D + D] = total.astype(bf16).reshape(4, 4, 32, D)

            @pl.loop(1, 4)
            def _(d):
                for copy in first_step(p, d):
                    copy.start()

        def sum_second(p):
            left, right = columns(p)

            done(rs_in.at[pl.ds(1, 3), :, :, pl.ds(p * D, D)], rs_recv.at[p])

            total = weight_part[z, :, :, left].astype(f32)
            other = weight_part[:, x, :, right].astype(f32)
            for d in range(1, 4):
                total = total + rs_in[d, :, :, left].astype(f32)
                other = other + rs_in[d, :, :, right].astype(f32)
            rs_out[:, :, left] = total.astype(bf16)
            rs_out[:, :, right] = other.astype(bf16)

            @pl.loop(1, 4)
            def _(d):
                for copy in second_step(p, d):
                    copy.start()

        def sum_third(p):
            left, right = columns(p)

            done(rs_in2.at[pl.ds(1, 3), :, pl.ds(p * D, D)], rs_recv2.at[p])

            total = rs_out[x, :, left].astype(f32)
            other = rs_out[z, :, right].astype(f32)
            for d in range(1, 4):
                total = total + rs_in2[d, :, left].astype(f32)
                other = other + rs_in2[d, :, right].astype(f32)
            y_out[:, left] = total.astype(bf16)
            y_out[:, right] = other.astype(bf16)
            y_parts[y, :, left] = total.astype(bf16)
            y_parts[y, :, right] = other.astype(bf16)
            for n in range(1, PLANES):
                across(p, n).start()

        sib_mixed.wait_recv()
        sib_branch.wait_recv()
        loads[1].wait()
        total = dot(mixed_ref[:, mine], branch_own[...], ((0,), (0,)))
        sum_first(2, total + dot(mixed_sib[...], branch_sib[...], ((0,), (0,))))

        key_live = lax.broadcasted_iota(jnp.int32, (2 * tokens, 1), 0) < length_ref[0]
        score_scale = HEAD ** (-0.5)
        here = pl.ds(pl.multiple_of(r * tokens, tokens), tokens)
        cosine, sine = cos_ref[:, here], sin_ref[:, here]
        first_core = r == 0

        def key_head(p, i):
            g = 4 * p + i
            head = pl.ds(pl.multiple_of(g * HEAD, HEAD), HEAD)
            keys, values = k_ref[head, :], v_ref[head, :]
            key_sum, value_sum = None, None
            for j in range(2):
                at = pl.ds(pl.multiple_of((2 * g + j) * HEAD, HEAD), HEAD)
                query, mixed_grad = q_ref[at, :], mg_t[at, :]
                scores = dot(keys, query, ((0,), (0,))) * score_scale
                scores = jnp.where(key_live, scores, NEG)
                probs = jnp.exp(scores - lse_ref[pl.ds(2 * g + j, 1), :])
                prob_grad = dot(values, mixed_grad, ((0,), (0,)))
                value_part = dot(mixed_grad, probs.astype(bf16), ((1,), (1,)))
                inner = jnp.sum(probs * prob_grad, axis=0, keepdims=True)
                score_grad = (probs * (prob_grad - inner)).astype(bf16)
                key_part = dot(query, score_grad, ((1,), (1,)))
                query_grad = dot(keys, score_grad, ((1,), (0,))) * score_scale
                to = pl.ds(pl.multiple_of(p * D + (2 * i + j) * HEAD, HEAD), HEAD)
                grad_t[to, :] = turned_back(query_grad, cosine, sine).astype(bf16)
                key_sum = key_part if key_sum is None else key_sum + key_part
                value_sum = value_part if value_sum is None else value_sum + value_part
            key_sum = key_sum * score_scale
            for n, part in enumerate((key_sum, value_sum)):
                to = pl.ds(pl.multiple_of(256 * n + i * HEAD, HEAD), HEAD)
                kv_own[p, to, :] = jnp.where(first_core, part[:, :tokens], part[:, tokens:])
                away = jnp.where(first_core, part[:, tokens:], part[:, :tokens])
                kv_out[p, to, :] = away.astype(bf16)

        def heads(p, first, last):
            @pl.loop(first, last)
            def _(i):
                key_head(p, i)

        def whole_keyval(p):
            sib_keyval(p).wait_recv()
            for i in range(4):
                rows = slice(HEAD * i, HEAD * i + HEAD)
                total = kv_own[p, rows, :] + kv_in[p, rows, :].astype(f32)
                to = p * D + HALF + HEAD * i
                grad_t[to : to + HEAD, :] = turned_back(total, cosine, sine).astype(bf16)
            total = kv_own[p, 256:512, :] + kv_in[p, 256:512, :].astype(f32)
            grad_t[p * D + HALF + 256 : p * D + D, :] = total.astype(bf16)
            sib_grads(p, 1).start()

        def projections(p):
            rows = slice(p * D, p * D + D)
            for part in range(2):
                sib_grads(p, part).wait_recv()
            total = dot(normed_ref[:, mine], grad_t[rows, :], ((0,), (1,)))
            sum_first(p, total + dot(normed_sib[...], grad_sib[rows, :], ((0,), (1,))))

        def inputs_part(p):
            return dot(grad_t[p * D : p * D + D, :], weight(p * D, D), ((0,), (1,)))

        for load in loads[2:5]:
            load.wait()
        heads(0, 0, 4)
        sib_keyval(0).start()
        sib_grads(0, 0).start()

        heads(1, 0, 4)
        sib_keyval(1).start()
        sib_grads(1, 0).start()
        for n in range(2):
            direct(n).wait_recv()
            merged(n).wait_recv()
        for n in range(2):
            total = expert_ref[3, n].astype(f32) + (y_in[0, n].astype(f32) + y_in[1, n].astype(f32))
            quarter_sum[n] = total.astype(bf16)
        quarter_out = pltpu.make_async_copy(quarter_sum, esum_hbm.at[y], load_sem.at[9])
        quarter_out.start()
        for n in range(2):
            handed(n).start()

        whole_keyval(0)
        for load in loads[5:]:
            load.wait()
        sib_normed.wait_recv()
        projections(0)
        done(all_slots(mid_hbm), c_recv.at[0])
        done(mid_hbm.at[0, 0], load_sem.at[8])
        results_in = pltpu.make_async_copy(mid_hbm, mid, load_sem.at[10])
        results_in.start()
        whole_keyval(1)
        normed_grad = inputs_part(0)
        projections(1)
        normed_grad = normed_grad + inputs_part(1)

        inputs = hidden_ref[...].astype(f32)
        scale = lax.rsqrt(jnp.mean(inputs * inputs, axis=1, keepdims=True) + epsilon)
        rows = inputs * scale
        attn_part = jnp.sum(normed_grad * rows, axis=0, keepdims=True)
        for j in range(8):
            gain_out[j : j + 1, :] = attn_part[:, 128 * j : 128 * j + 128]

        def gain(k):
            device, _ = step_of(k, 1)
            return remote(gain_out, gain_in.at[me], sm_send.at[3], sm_recv.at[3], device)

        @pl.loop(1, GROUP)
        def _(k):
            gain(k).start()

        gain_in[me] = gain_out[...]
        scaled = normed_grad * again_ref[...]
        inner = jnp.mean(scaled * rows, axis=1, keepdims=True)
        hgrad_ref[...] += scale * (scaled - rows * inner)

        sum_second(2)
        done(small_in.at[pl.ds(0, GROUP - 1)], sm_recv.at[0])

        def small_across(n):
            device, _ = plane_shift(n)
            return remote(
                small_y, small_y_in.at[y], sm_send.at[1], sm_recv.at[1], device
            )

        small_y[...] = jnp.sum(small_in[...], axis=0)
        small_y_in[y] = small_y[...]
        for n in range(1, PLANES):
            small_across(n).start()

        sum_second(0)
        results_in.wait()
        part_sems = part_send2, part_recv2
        fold_start(parts_out2, parts_in2, mid, None, posz_ref, posx_ref, part_sems)
        for n in range(2):
            handed(n).wait_recv()
            passed_on(n).start()

        done(small_y_in.at[pl.ds(0, 3)], sm_recv.at[1])
        totals = small_y_in[0] + small_y_in[1] + small_y_in[2] + small_y_in[3]
        mgain_out[...] = totals[8:16]
        router_all[me] = totals[0:8]

        def router_row(k):
            device, _ = step_of(k, 1)
            return remote(
                router_all.at[me], router_all.at[me], sm_send.at[2], sm_recv.at[2], device
            )

        @pl.loop(1, GROUP)
        def _(k):
            router_row(k).start()

        sum_second(1)
        fold_end(parts_out2, parts_in2, part_sems)
        sum_third(2)
        sum_third(0)

        done(gain_in.at[pl.ds(0, GROUP - 1)], sm_recv.at[3])

        gain_y[...] = jnp.sum(gain_in[...], axis=0)
        gain_y_in[y] = gain_y[...]

        def gain_across(n):
            device, _ = plane_shift(n)
            return remote(gain_y, gain_y_in.at[y], sm_send.at[4], sm_recv.at[4], device)

        for n in range(1, PLANES):
            gain_across(n).start()

        sum_third(1)

        mixture = folded(parts_in2, part_sems)
        hout_ref[...] = ((middle_ref[...] + mixture) * live).astype(bf16)

        done(gain_y_in.at[pl.ds(0, 3)], sm_recv.at[4])
        again_out[...] = (gain_y_in[0] + gain_y_in[1]) + (gain_y_in[2] + gain_y_in[3])

        done(router_all.at[pl.ds(0, GROUP - 1)], sm_recv.at[2])

        router_out[...] = router_all[...]

        done(all_slots(mid_hbm), c_send.at[0])
        done(parts_out2.at[pl.ds(0, 3)], part_send2.at[0])
        done(small_in.at[pl.ds(0, GROUP - 1)], sm_send.at[0])
        done(small_y_in.at[pl.ds(0, 3)], sm_send.at[1])
        done(router_all.at[pl.ds(0, GROUP - 1)], sm_send.at[2])
        done(gain_in.at[pl.ds(0, GROUP - 1)], sm_send.at[3])
        done(gain_y_in.at[pl.ds(0, 3)], sm_send.at[4])
        for p in range(3):
            done(rs_in.at[pl.ds(1, 3), :, :, pl.ds(p * D, D)], rs_send.at[p])
            done(rs_in2.at[pl.ds(1, 3), :, pl.ds(p * D, D)], rs_send2.at[p])
            done(y_parts.at[pl.ds(0, 3), :, pl.ds(p * D, D)], ys_recv.at[p])
            done(y_parts.at[pl.ds(0, 3), :, pl.ds(p * D, D)], ys_send.at[p])
        for n in range(2):
            for copy in (relayed(n), direct(n), merged(n), handed(n), passed_on(n)):
                copy.wait_send()
        for copy in (sib_normed, sib_mixed, sib_branch):
            copy.wait_send()
        for p in range(2):
            sib_keyval(p).wait_send()
            for part in range(2):
                sib_grads(p, part).wait_send()
        for n in range(2):
            passed_on(n).wait_recv()
        quarter_out.wait()
        own_out[...] = (y_parts[0].astype(f32) + y_parts[1].astype(f32)) + (
            y_parts[2].astype(f32) + y_parts[3].astype(f32)
        )

    pl.run_scoped(
        finish_phase,
        pltpu.VMEM((2, 4, 4, 32, 3 * D), bf16),
        pltpu.VMEM((D, tokens), bf16),
        pltpu.VMEM((HALF, 2 * tokens), bf16),
        pltpu.VMEM((HALF, 2 * tokens), bf16),
        pltpu.VMEM((tokens, D), bf16),
        pltpu.VMEM((tokens, D), bf16),
        pltpu.VMEM((tokens, D), bf16),
        pltpu.VMEM((4, tokens, D), bf16),
        pltpu.VMEM((2, 384, HALF), bf16),
        pltpu.VMEM((2, 384, HALF), bf16),
        pltpu.VMEM((tokens, D), bf16),
        pltpu.VMEM((D, tokens), bf16),
        pltpu.VMEM((2 * D, tokens), bf16),
        pltpu.VMEM((2, HALF, tokens), f32),
        pltpu.VMEM((2, HALF, tokens), bf16),
        pltpu.VMEM((4, 4, 32, 3 * D), bf16),
        pltpu.VMEM((4, 32, 3 * D), bf16),
        pltpu.VMEM((32, 3 * D), bf16),
        pltpu.VMEM((GROUP, 16, 128), f32),
        pltpu.VMEM((16, 128), f32),
        pltpu.VMEM((8, 128), f32),
        pltpu.VMEM((8, 128), f32),
    )


def rest(length, *arrays):
    tokens = TOKENS
    f32, bf16 = jnp.float32, jnp.bfloat16
    vmem = pl.BlockSpec(memory_space=pltpu.VMEM)
    hbm = pl.BlockSpec(memory_space=pl.ANY)
    shape = jax.ShapeDtypeStruct
    sems = pltpu.SemaphoreType.DMA
    scratch = [
        pltpu.VMEM((4, tokens, HALF), bf16),
        pltpu.VMEM((4, tokens, HALF), bf16),
        pltpu.VMEM((2, 4, 4, CAP, D), bf16),
        pltpu.VMEM((2, 4, 4, CAP, D), bf16),
        pltpu.VMEM((4, tokens, D), bf16),
        pltpu.VMEM((4, tokens, D), bf16),
        pltpu.VMEM((GROUP, 8, 128), f32),
        pltpu.VMEM((GROUP, 8, 128), f32),
        pltpu.VMEM((GROUP, 8, 128), f32),
        pltpu.VMEM((GROUP, 8, 128), f32),
        pltpu.VMEM((EXPERTS, tokens), f32),
        pltpu.VMEM((4, 2, 384, HALF), bf16),
        pltpu.VMEM((2, 384, HALF), bf16),
        pltpu.VMEM((2, 2, 384, HALF), bf16),
        pltpu.VMEM((tokens, D), bf16),
        pltpu.VMEM((tokens, HALF), bf16),
        pltpu.VMEM((tokens, HALF), bf16),
        pltpu.VMEM((2 * D, tokens), bf16),
        pltpu.VMEM((2, HALF, tokens), bf16),
        pltpu.VMEM((4, 4, 32, 3 * D), bf16),
        pltpu.VMEM((4, 32, 3 * D), bf16),
        pltpu.VMEM((PLANES, 32, 3 * D), bf16),
        pltpu.VMEM((GROUP, 16, 128), f32),
        pltpu.VMEM((PLANES, 16, 128), f32),
        pltpu.VMEM((GROUP, 8, 128), f32),
        pltpu.VMEM((PLANES, 8, 128), f32),
        pltpu.VMEM((GROUP, 8, 128), f32),
    ]
    for count in (11, 4, 4, 4, 4, 8, 1, 8, 1, 3, 2, 2, 1, 1, 1, 3, 10, 10, 9, 9, 3, 3, 3, 3, 3, 3, 5, 5):
        scratch += [sems((count,))]
    in_specs = [pl.BlockSpec(memory_space=pltpu.SMEM)] + [vmem] * len(arrays)
    for n in (6, 7, 8, 9, 13, 16, 17, 18, 19, 20, 21):
        in_specs[n] = hbm
    return pl.pallas_call(
        rest_kernel,
        out_shape=(
            shape((tokens, D), bf16),
            shape((tokens, D), f32),
            shape((8, 128), f32),
            shape((8, 128), f32),
            shape((GROUP, 8, 128), f32),
            shape((32, 3 * D), f32),
            shape((4, 2, 384, HALF), bf16),
            shape((2, 4, 4, CAP, D), bf16),
            shape((2, 4, 4, CAP, D), bf16),
        ),
        in_specs=in_specs,
        out_specs=[vmem] * 6 + [hbm] * 3,
        scratch_shapes=scratch,
        compiler_params=pltpu.CompilerParams(
            collective_id=2, has_side_effects=True, vmem_limit_bytes=62 << 20
        ),
        name="rest",
    )(length, *arrays)[:7]


def spread_kernel(
    hout_ref,
    hgrad_ref,
    own_ref,
    esum_ref,
    router_ref,
    again_ref,
    mgain_ref,
    hout_out,
    hgrad_out,
    q_out,
    k_out,
    v_out,
    o_out,
    gate_out,
    up_out,
    down_out,
    router_out,
    again_out,
    mgain_out,
):
    f32 = jnp.float32
    hout_out[...] = hout_ref[...]
    hgrad_out[...] = hgrad_ref[...]
    for n in range(2):
        for h in range(2):
            rows = slice(256 * n + 128 * h, 256 * n + 128 * h + 128)
            gate_out[0, rows, :] = esum_ref[n, h, 0:128, :].astype(f32)
            up_out[0, rows, :] = esum_ref[n, h, 128:256, :].astype(f32)
            rows = slice(128 * n + 64 * h, 128 * n + 64 * h + 64)
            down_out[0, rows, 0:HALF] = esum_ref[n, h, 256:320, :].astype(f32)
            down_out[0, rows, HALF:D] = esum_ref[n, h, 320:384, :].astype(f32)

    @pl.when(pl.program_id(0) == 0)
    def _():
        for p in range(2):
            q_out[:, p * HALF : p * HALF + HALF] = own_ref[:, p * D : p * D + HALF]
            k_out[:, p * 256 : p * 256 + 256] = own_ref[:, p * D + HALF : p * D + 768]
            v_out[:, p * 256 : p * 256 + 256] = own_ref[:, p * D + 768 : p * D + D]
        o_out[...] = own_ref[:, 2 * D : 3 * D]
        for j in range(8):
            router_out[:, 128 * j : 128 * j + 128] = router_ref[:, j, :]
        again_out[...] = again_ref[...]
        mgain_out[...] = mgain_ref[...]


def spread_out(*arrays):
    f32, bf16 = jnp.float32, jnp.bfloat16
    shape = jax.ShapeDtypeStruct

    def whole(*dims):
        return pl.BlockSpec(dims, lambda i: (0,) * len(dims))

    def rows(count, width):
        return pl.BlockSpec((count, width), lambda i: (i, 0))

    def expert_rows(count, width):
        return pl.BlockSpec((1, count, width), lambda i: (0, i, 0))

    return pl.pallas_call(
        spread_kernel,
        grid=(2,),
        out_shape=(
            shape((TOKENS, D), bf16),
            shape((TOKENS, D), f32),
            shape((32, D), f32),
            shape((32, HALF), f32),
            shape((32, HALF), f32),
            shape((32, D), f32),
            shape((1, D, HALF), f32),
            shape((1, D, HALF), f32),
            shape((1, HALF, D), f32),
            shape((EXPERTS, D), f32),
            shape((8, 128), f32),
            shape((8, 128), f32),
        ),
        in_specs=[
            rows(128, D),
            rows(128, D),
            whole(32, 3 * D),
            pl.BlockSpec((2, 2, 384, HALF), lambda i: (i, 0, 0, 0)),
            whole(GROUP, 8, 128),
            whole(8, 128),
            whole(8, 128),
        ],
        out_specs=[
            rows(128, D),
            rows(128, D),
            whole(32, D),
            whole(32, HALF),
            whole(32, HALF),
            whole(32, D),
            expert_rows(512, HALF),
            expert_rows(512, HALF),
            expert_rows(256, D),
            whole(EXPERTS, D),
            whole(8, 128),
            whole(8, 128),
        ],
        compiler_params=pltpu.CompilerParams(vmem_limit_bytes=60 << 20),
        name="spread_out",
    )(*arrays)


def on_device(
    hidden_in,
    cotangent,
    lengths,
    routes,
    priority,
    attn_gain,
    query_weight,
    key_weight,
    value_weight,
    output_weight,
    moe_gain,
    router,
    gate_weight,
    up_weight,
    down_weight,
):
    tok_count = hidden_in.shape[0]
    half_dim = HEAD // 2
    frequency = rotary_base ** (-np.arange(half_dim, dtype=np.float32) / half_dim)
    positions = np.arange(2 * tok_count, dtype=np.float32)
    angles = frequency.astype(np.float32)[:, None] * positions[None, :]
    cosine, sine = jnp.asarray(np.cos(angles)), jnp.asarray(np.sin(angles))
    router_t = router.T
    (
        weights,
        normed,
        queries,
        keys,
        values,
        log_total,
        mixed_rows,
        middle,
        routed,
        gates,
        pos,
        posz,
        posx,
        arrived_grad,
    ) = front(
        lengths,
        hidden_in,
        cotangent,
        routes.T,
        priority,
        attn_gain[None],
        moe_gain[None],
        query_weight,
        key_weight,
        value_weight,
        output_weight,
        router_t,
        cosine,
        sine,
    )
    summed = rest(
        lengths,
        routed,
        pos,
        posz,
        posx,
        gates,
        arrived_grad,
        gate_weight[0],
        up_weight[0],
        down_weight[0],
        router_t,
        middle,
        cotangent,
        hidden_in,
        attn_gain[None],
        moe_gain[None],
        normed,
        mixed_rows,
        weights,
        queries,
        keys,
        values,
        log_total,
        cosine,
        sine,
    )
    hidden_out, hidden_grad, attn_gain_sum, moe_gain_sum, router_sum, own_rows, expert_sum = summed
    (
        hidden_out,
        hidden_grad,
        query_grad,
        key_grad,
        value_grad,
        output_grad,
        gate_grad,
        up_grad,
        down_grad,
        router_grad,
        attn_gain_sum,
        moe_gain_sum,
    ) = spread_out(
        hidden_out, hidden_grad, own_rows, expert_sum, router_sum, attn_gain_sum, moe_gain_sum
    )
    return (
        hidden_out,
        hidden_grad,
        attn_gain_sum.reshape(D),
        query_grad,
        key_grad,
        value_grad,
        output_grad,
        moe_gain_sum.reshape(D),
        router_grad.T,
        gate_grad,
        up_grad,
        down_grad,
    )


def solution(mesh):
    return jax.shard_map(
        on_device,
        mesh=mesh,
        in_specs=(
            P(("dp", "col", "row"), None),
            P(("dp", "col", "row"), None),
            P(("dp", "col")),
            P(("dp", "col", "row"), None),
            P(("dp", "col", "row"), None),
            P(),
            P(("row", "col"), None),
            P(("row", "col"), None),
            P(("row", "col"), None),
            P(("row", "col"), None),
            P(),
            P(),
            P(("row", "col"), None, None),
            P(("row", "col"), None, None),
            P(("row", "col"), None, None),
        ),
        out_specs=(
            P(("dp", "col", "row"), None),
            P(("dp", "col", "row"), None),
            P(),
            P(("row", "col"), None),
            P(("row", "col"), None),
            P(("row", "col"), None),
            P(("row", "col"), None),
            P(),
            P(),
            P(("row", "col"), None, None),
            P(("row", "col"), None, None),
            P(("row", "col"), None, None),
        ),
        check_vma=False,
    )
```
